128 devices in a mesh: fsdp: 8 (over z, core), expert: 16 (over y, x).
Axes of the slice: x: 4, y: 4, z: 4, core: 2. Of those that a mesh axis runs over, the one named last changes fastest.
Arguments:
- tokens: bfloat16 [16, 1024, 1024], P('expert', 'fsdp'), may hold values from -6 to 6
- lengths: int32 [16, 4], P('expert'), may hold values from 1 to 960, 1024 in all within a row
- routes: int32 [16, 1024, 8], P('expert', 'fsdp'), may hold values from 0 to 31, all different within a row; in each aligned block of 128 rows (0 to 127, 128 to 255, ..., all dimensions but the last counted through in order) at most 48 rows name the same one
- first_gain: bfloat16 [1024], P('fsdp'), may hold values from 0.25 to 1.75
- query_weight: bfloat16 [1024, 1024], P('fsdp'), may hold values from -0.1875 to 0.1875
- key_weight: bfloat16 [1024, 512], P('fsdp'), may hold values from -0.1875 to 0.1875
- value_weight: bfloat16 [1024, 512], P('fsdp'), may hold values from -0.1875 to 0.1875
- output_weight: bfloat16 [1024, 1024], P('fsdp'), may hold values from -0.75 to 0.75
- query_gain: bfloat16 [64], P('fsdp'), may hold values from 0.25 to 1.75
- key_gain: bfloat16 [64], P('fsdp'), may hold values from 0.25 to 1.75
- second_gain: bfloat16 [1024], P('fsdp'), may hold values from 0.25 to 1.75
- router_weight: bfloat16 [1024, 32], P('fsdp'), may hold values from -0.09375 to 0.09375
- gate_weight: bfloat16 [32, 1024, 512], P('expert'), may hold values from -0.1875 to 0.1875
- up_weight: bfloat16 [32, 1024, 512], P('expert'), may hold values from -0.1875 to 0.1875
- down_weight: bfloat16 [32, 512, 1024], P('expert'), may hold values from -1 to 1
- cotangent: bfloat16 [16, 1024, 1024], P('expert', 'fsdp'), may hold values from -6 to 6
Outputs:
- layer_out: bfloat16 [16, 1024, 1024], P('expert', 'fsdp')
- tokens_grad: float32 [16, 1024, 1024], P('expert', 'fsdp')
- first_gain_grad: float32 [1024], P('fsdp')
- query_weight_grad: float32 [1024, 1024], P('fsdp')
- key_weight_grad: float32 [1024, 512], P('fsdp')
- value_weight_grad: float32 [1024, 512], P('fsdp')
- output_weight_grad: float32 [1024, 1024], P('fsdp')
- query_gain_grad: float32 [64], P('fsdp')
- key_gain_grad: float32 [64], P('fsdp')
- second_gain_grad: float32 [1024], P('fsdp')
- router_weight_grad: float32 [1024, 32], P('fsdp')
- gate_weight_grad: float32 [32, 1024, 512], P('expert')
- up_weight_grad: float32 [32, 1024, 512], P('expert')
- down_weight_grad: float32 [32, 512, 1024], P('expert')
The draws below stay inside these ranges and needn't reach their ends.
Inputs may be any that keep to these rules, and one draw needn't show every extreme that they name: `routes`: each row names 8 different experts. Among the rows of one device no expert is named more than 48 times, a bound that some block reaches. `lengths`: each row sums to 1024, and its largest entry is exactly 960.
All inputs are finite; a program needn't handle non-finite values.
Results may differ from the reference program's by a relative error of at most 0.025.
Values may be sent and summed in bfloat16 or wider, within the bound.
No kernel may reach another device: no remote copies, remote signals or barrier semaphores. Data moves between devices by JAX's collectives and lax.ppermute only.
A program may use at most 192 MiB of HBM per device.

```python
import math
import jax
import jax.numpy as jnp
import numpy as np
from jax import lax

D = 1024
HEADS = 16
KV_HEADS = 8
HEAD = 64
FF = 512
TOP = 8
TOK_DEV = 128
SEQS = 4
GROUPS = 16
GROUP_TOK = 1024
EXPERTS = 32
CAP = 48
LONGEST = 960


def steps_of(own_key, shape, cuts, low, largest):
    def one(dim, parts):
        heights = jax.random.uniform(jax.random.fold_in(jax.random.fold_in(own_key, 6), dim), (parts,), jnp.float32, low / len(cuts), largest / len(cuts))
        return jnp.repeat(jnp.exp(heights), shape[dim] // parts).reshape((-1,) + (1,) * (len(shape) - dim - 1))

    loudness = one(*cuts[0])
    for cut in cuts[1:]:
        loudness = loudness * one(*cut)
    return loudness


def length_profile(number_of, total, most, lean):
    loads = [(1 << 20) // math.isqrt(rank ** lean) + 1 for rank in range(2, number_of + 1)]
    spare, given = total - most - (number_of - 1), [1] * (number_of - 1)
    while spare > 0:
        candidates = [i for i in range(number_of - 1) if given[i] < most]
        mass, left = sum([loads[i] for i in candidates]), spare
        for i in candidates:
            addition = min(most - given[i], max(1, left * loads[i] // mass), spare)
            given[i] = given[i] + addition
            spare = spare - addition
    return np.array([most] + given)


def uneven(rng, amount, total, bound, lean):
    if amount == 2:
        one = jax.random.randint(rng, (), max(1, total - bound), min(bound, total - 1) + 1)
        return jnp.stack([one, total - one])
    tallies = jnp.asarray(length_profile(amount, total, bound, lean), jnp.int32)
    pairs = (amount - 1) // 2
    donor, taker = tallies[1:1 + 2 * pairs:2], tallies[2:2 + 2 * pairs:2]
    room = jnp.minimum(donor - 1, bound - taker)
    shifted = jax.random.randint(jax.random.fold_in(rng, 1), (pairs,), 0, 1 << 20) % (room + 1)
    tallies = tallies.at[1:1 + 2 * pairs:2].set(donor - shifted).at[2:2 + 2 * pairs:2].set(taker + shifted)
    return tallies[jax.random.permutation(jax.random.fold_in(rng, 2), amount)]


def deal_out(rng, own, number, rows, number_of, top, limit, skew):
    ranking = jax.random.permutation(rng, number_of)
    crowded, usual = portions_of(number_of, rows * top, limit, skew, True), portions_of(number_of, rows * top, limit, skew, False)
    places = jnp.arange(number_of)

    def named(tallies, offset_by):
        used = int((tallies > 0).sum())
        fixed = max(1, used // 4)
        shifted = fixed + (places - fixed + offset_by * (used - fixed)) % max(1, number_of - fixed)
        return jnp.zeros((number_of,), jnp.int32).at[ranking[jnp.where(places < fixed, places, shifted)]].set(jnp.asarray(tallies, jnp.int32))

    tallies = jnp.where(number % 4 == 0, named(crowded, number // 4), named(usual, number - number // 4 - 1))
    mixed = jax.random.permutation(jax.random.fold_in(own, 3), number_of)
    donor, taker = mixed[0:number_of // 2 * 2:2], mixed[1:number_of // 2 * 2:2]
    margin = jnp.minimum(tallies[donor] - 1, limit - tallies[taker]) // 2
    margin = jnp.where((donor == ranking[0]) | (taker == ranking[0]) | (tallies[taker] == 0), 0, jnp.maximum(margin, 0))
    shifted = jax.random.randint(jax.random.fold_in(own, 4), (number_of // 2,), 0, 1 << 20) % (margin + 1)
    tallies = tallies.at[donor].add(-shifted).at[taker].add(shifted)
    labels = jnp.searchsorted(jnp.cumsum(tallies), jnp.arange(rows * top), side="right").astype(jnp.int32)
    table = labels.reshape(top, rows).T
    table = table[jax.random.permutation(jax.random.fold_in(own, 1), rows)]
    offset_by = jax.random.randint(jax.random.fold_in(own, 2), (rows, 1), 0, top)
    return jnp.take_along_axis(table, (jnp.arange(top)[None, :] + offset_by) % top, axis=1)


def portions_of(number_of, total, most, lean, full):
    weights = [(1 << 20) // math.isqrt(grade ** lean) + 1 for grade in range(1, number_of + 1)]
    largest = most if full else min(most, max(-(-total // number_of), total * weights[0] // sum(weights)))
    least = 1 if total - largest >= number_of - 1 else 0
    counts, rest = [largest] + [least] * (number_of - 1), total - largest - least * (number_of - 1)
    while rest > 0:
        movable = [i for i in range(1, number_of) if counts[i] < largest] or [i for i in range(1, number_of) if counts[i] < most]
        mass, remaining = sum([weights[i] for i in movable]), rest
        for i in movable:
            extra = min(most - counts[i], max(1, remaining * weights[i] // mass), rest)
            counts[i] = counts[i] + extra
            rest = rest - extra
    return np.array(counts)


def centred(key, extent, scale, most, shards=(), held_as=jnp.bfloat16):
    values = jax.random.normal(key, extent, jnp.float32) * scale
    if len(shards) > 0:
        values = steps_of(key, extent, shards, -0.22, 0.18) * values
    return jnp.clip(values, min=-most, max=most).astype(held_as)


def setup_inputs(seed: int = 0) -> dict:
    streams_of = jax.random.split(jax.random.key(seed), 17)
    tokens = centred(streams_of[0], (GROUPS, GROUP_TOK, D), 1.0, 6.0, ((0, 16), (1, 8)))
    lengths = jax.vmap(lambda own: uneven(own, SEQS, GROUP_TOK, LONGEST, 2))(jax.random.split(streams_of[1], GROUPS)).reshape((GROUPS, SEQS)).astype(jnp.int32)
    routes_keys = jax.random.split(jax.random.fold_in(streams_of[2], 1), GROUPS * GROUP_TOK // TOK_DEV)
    routes_turns = jax.random.permutation(jax.random.fold_in(streams_of[2], 3), GROUPS * GROUP_TOK // TOK_DEV)
    routes = jax.vmap(lambda own, number: deal_out(jax.random.fold_in(streams_of[2], 2), own, number, TOK_DEV, EXPERTS, TOP, CAP, 1))(routes_keys, routes_turns).reshape((GROUPS, GROUP_TOK, TOP))
    first_gain = jnp.clip(1.0 + 0.15 * jax.random.normal(streams_of[3], (D,), jnp.float32), 0.25, 1.75).astype(jnp.bfloat16)
    query_weight = centred(streams_of[4], (D, HEADS * HEAD), D ** -0.5, 0.1875, ((0, 8),))
    key_weight = centred(streams_of[5], (D, KV_HEADS * HEAD), D ** -0.5, 0.1875, ((0, 8),))
    value_weight = centred(streams_of[6], (D, KV_HEADS * HEAD), D ** -0.5, 0.1875, ((0, 8),))
    output_weight = centred(streams_of[7], (HEADS * HEAD, D), (HEADS * HEAD // 16) ** -0.5, 0.75, ((0, 8),))
    query_gain = jnp.clip(1.0 + 0.15 * jax.random.normal(streams_of[8], (HEAD,), jnp.float32), 0.25, 1.75).astype(jnp.bfloat16)
    key_gain = jnp.clip(1.0 + 0.15 * jax.random.normal(streams_of[9], (HEAD,), jnp.float32), 0.25, 1.75).astype(jnp.bfloat16)
    second_gain = jnp.clip(1.0 + 0.15 * jax.random.normal(streams_of[10], (D,), jnp.float32), 0.25, 1.75).astype(jnp.bfloat16)
    router_weight = centred(streams_of[11], (D, EXPERTS), (4 * D) ** -0.5, 0.09375, ((0, 8),))
    gate_weight = centred(streams_of[12], (EXPERTS, D, FF), D ** -0.5, 0.1875, ((0, 16),))
    up_weight = centred(streams_of[13], (EXPERTS, D, FF), D ** -0.5, 0.1875, ((0, 16),))
    down_weight = centred(streams_of[14], (EXPERTS, FF, D), (FF // 16) ** -0.5, 1.0, ((0, 16),))
    cotangent = centred(streams_of[15], (GROUPS, GROUP_TOK, D), 1.0, 6.0, ((0, 16), (1, 8)))
    return dict(tokens=tokens, lengths=lengths, routes=routes, first_gain=first_gain, query_weight=query_weight, key_weight=key_weight, value_weight=value_weight, output_weight=output_weight, query_gain=query_gain, key_gain=key_gain, second_gain=second_gain, router_weight=router_weight, gate_weight=gate_weight, up_weight=up_weight, down_weight=down_weight, cotangent=cotangent)


EPSILON = 1e-06
ROPE_BASE = 10000.0
EXACT = lax.Precision.HIGHEST

@jax.custom_vjp
def low(v):
    return lax.optimization_barrier(v.astype(jnp.bfloat16)).astype(jnp.float32)

@jax.custom_vjp
def low_back(v):
    return v

def low_keep(v):
    return (low(v), None)

def low_pass(kept, grad):
    return (grad,)

def back_keep(v):
    return (v, None)

def back_low(kept, grad):
    return (low(grad),)
low.defvjp(low_keep, low_pass)
low_back.defvjp(back_keep, back_low)

def rms_norm(values, scales):
    return values * lax.rsqrt(lax.optimization_barrier(jnp.mean(values * values, axis=-1, keepdims=True)) + EPSILON) * scales

def product(left, right):
    return jnp.dot(left, right, precision=EXACT, preferred_element_type=jnp.float32)

def rotate(values, position):
    half_size = values.shape[-1] // 2
    frequency = ROPE_BASE ** (-jnp.arange(half_size, dtype=jnp.float32) * 2.0 / values.shape[-1])
    angles = position.astype(jnp.float32)[..., None] * frequency
    cosine = jnp.cos(angles)[..., None, :]
    sine = jnp.sin(angles)[..., None, :]
    lower_half = values[..., :half_size]
    upper_half = values[..., half_size:]
    return jnp.concatenate([lower_half * cosine - upper_half * sine, upper_half * cosine + lower_half * sine], axis=-1)

def seq_layout(lengths_row, count):
    seq_ends = jnp.cumsum(lengths_row).astype(jnp.int32)
    starts = (seq_ends - lengths_row).astype(jnp.int32)
    place_index = jnp.arange(count, dtype=jnp.int32)
    segment = lax.optimization_barrier(jnp.sum((place_index[:, None] >= seq_ends[None, :]).astype(jnp.int32), axis=1)).astype(jnp.int32)
    belongs = segment[:, None] == jnp.arange(seq_ends.shape[0], dtype=jnp.int32)[None, :]
    seq_begin = lax.optimization_barrier(jnp.sum(jnp.where(belongs, starts[None, :], 0), axis=1)).astype(jnp.int32)
    return (segment, (place_index - seq_begin).astype(jnp.int32))

def slot_tables(flat_routes, block, capacity, experts):
    slots, route_count = flat_routes.shape
    blocks = slots // block
    per_block = flat_routes.reshape(blocks, block * route_count)
    route_hits = (per_block[:, :, None] == jnp.arange(experts, dtype=jnp.int32)[None, None, :]).astype(jnp.int32)
    slot_rank = (lax.optimization_barrier(jnp.sum(jnp.cumsum(route_hits, axis=1).astype(jnp.int32) * route_hits, axis=2)) - 1).astype(jnp.int32)
    block_index = jnp.arange(blocks, dtype=jnp.int32)[:, None]
    slot_place = (per_block * (blocks * capacity) + block_index * capacity + slot_rank).reshape(-1).astype(jnp.int32)
    token_index = (jnp.arange(slots * route_count, dtype=jnp.int32) // route_count).astype(jnp.int32)
    slot_token = jnp.full((experts * blocks * capacity,), slots, jnp.int32).at[slot_place].set(token_index)
    return (slot_place, slot_token.reshape(experts, blocks * capacity))

def attend(pieces):
    queries, keys, values, segment, place_index = pieces
    count, head_count, head_size = queries.shape
    key_heads = keys.shape[1]
    grouped = queries.reshape(count, key_heads, head_count // key_heads, head_size)
    scores = jnp.einsum('ikrd,jkd->krij', grouped, keys, precision=EXACT) * head_size ** (-0.5)
    scores = low_back(scores)
    allowed = (segment[:, None] == segment[None, :]) & (place_index[None, :] <= place_index[:, None])
    scores = jnp.where(allowed, scores, -1e+30)
    row_max = lax.optimization_barrier(jnp.max(scores, axis=-1, keepdims=True))
    weights = jnp.exp(scores - row_max)
    probs = low(weights / lax.optimization_barrier(jnp.sum(weights, axis=-1, keepdims=True)))
    mixed_heads = jnp.einsum('krij,jkd->ikrd', probs, values, precision=EXACT)
    return mixed_heads.reshape(count, head_count * head_size)

def layer(tokens, first_gain, query_weight, key_weight, value_weight, output_weight, query_gain, key_gain, second_gain, router_weight, gate_weight, up_weight, down_weight, segment, place_index, position, routes, slot_place, slot_token):
    groups, count, model_width = tokens.shape
    head_count = query_weight.shape[1] // HEAD
    key_heads = key_weight.shape[1] // HEAD
    hidden_one = low(rms_norm(tokens, first_gain))
    query_pre = low_back(product(hidden_one, query_weight)).reshape(groups, count, head_count, HEAD)
    queries = low(rotate(rms_norm(query_pre, query_gain), position))
    key_pre = low_back(product(hidden_one, key_weight)).reshape(groups, count, key_heads, HEAD)
    keys = low(rotate(rms_norm(key_pre, key_gain), position))
    values = low(low_back(product(hidden_one, value_weight))).reshape(groups, count, key_heads, HEAD)
    mixed_heads = lax.map(jax.checkpoint(attend), (queries, keys, values, segment, place_index))
    mixed_heads = low(low_back(mixed_heads))
    branch = low_back(product(mixed_heads, output_weight))
    middle = tokens + branch
    hidden_two = low(rms_norm(middle, second_gain))
    logits = low_back(product(hidden_two, router_weight))
    probs = jax.nn.softmax(logits, axis=-1)
    picked = jnp.take_along_axis(probs, routes, axis=-1)
    gate_share = picked / lax.optimization_barrier(jnp.sum(picked, axis=-1, keepdims=True))
    flat_hidden = hidden_two.reshape(-1, model_width)
    padded = jnp.concatenate([flat_hidden, jnp.zeros((1, model_width), flat_hidden.dtype)], axis=0)

    def expert_rows(pieces):
        index_rows, gate_one, up_one, down_one = pieces
        arrived = padded[index_rows]
        gate_pre = low_back(product(arrived, gate_one))
        up_pre = low_back(product(arrived, up_one))
        active = low(jax.nn.silu(gate_pre) * up_pre)
        return low(low_back(product(active, down_one)))
    produced = lax.map(jax.checkpoint(expert_rows), (slot_token, gate_weight, up_weight, down_weight))
    per_slot = produced.reshape(-1, model_width)[slot_place].reshape(groups, count, routes.shape[-1], model_width)
    return middle + lax.optimization_barrier(jnp.sum(gate_share[..., None] * per_slot, axis=-2))

def reference(tokens, lengths, routes, first_gain, query_weight, key_weight, value_weight, output_weight, query_gain, key_gain, second_gain, router_weight, gate_weight, up_weight, down_weight, cotangent):
    groups, count, model_width = tokens.shape

    def layout_row(row):
        return seq_layout(row, count)
    segment, position = jax.vmap(layout_row)(lengths)
    place_index = jnp.broadcast_to(jnp.arange(count, dtype=jnp.int32), (groups, count))
    slot_place, slot_token = slot_tables(routes.reshape(-1, routes.shape[-1]), TOK_DEV, CAP, EXPERTS)
    floats = [item.astype(jnp.float32) for item in (tokens, first_gain, query_weight, key_weight, value_weight, output_weight, query_gain, key_gain, second_gain, router_weight, gate_weight, up_weight, down_weight)]

    def forward(*params):
        return layer(*params, segment, place_index, position, routes, slot_place, slot_token)
    result, pullback = jax.vjp(forward, *floats)
    grads = pullback(cotangent.astype(jnp.float32))
    return (result.astype(jnp.bfloat16), grads[0], grads[1], grads[2], grads[3], grads[4], grads[5], grads[6], grads[7], grads[8], grads[9], grads[10], grads[11], grads[12])
```

```python
import functools

import jax
import jax.numpy as jnp
from jax import lax
from jax.experimental import pallas as pl
from jax.experimental.pallas import tpu as pltpu
from jax.sharding import PartitionSpec as P

EPSILON = 1e-06
ROPE_BASE = 10000.0
HEAD = 64
TILE = 256
F32 = jnp.float32
BF16 = jnp.bfloat16
VMEM_BYTES = 56 * 1024 * 1024
VMEM = pl.BlockSpec(memory_space=pltpu.VMEM)
SMEM = pl.BlockSpec(memory_space=pltpu.SMEM)
CORE = 1
Z_STEPS = (2, 6, 4)
X_STEPS = (1, 3, 2)
Y_STEPS = (4, 12, 8)


def dot(left, right, dims=((1,), (0,))):
    return lax.dot_general(left, right, (dims, ((), ())), preferred_element_type=F32)


def params():
    return pltpu.CompilerParams(vmem_limit_bytes=VMEM_BYTES)


def shape(extent, dtype):
    return jax.ShapeDtypeStruct(extent, dtype)


def column_gain(small, lane):
    rows = small.reshape(8, -1, 128)[:, : HEAD // 8, :].reshape(HEAD, 128)
    return rows[:, lane : lane + 1]


def head_forward(pre, gain, cosine, sine):
    scale = lax.rsqrt(jnp.mean(pre * pre, axis=0, keepdims=True) + EPSILON)
    normed = pre * scale
    scaled = normed * gain
    a, b = scaled[: HEAD // 2], scaled[HEAD // 2 :]
    turned = jnp.concatenate([a * cosine - b * sine, b * cosine + a * sine], axis=0)
    return turned, normed, scale


def forward_kernel(me_ref, *refs, experts, q_heads):
    xs = refs[:8]
    arrived_ref, cos_ref, sin_ref, start_ref = refs[8:12]
    h1_ref, pre_ref, out_ref, inverse_ref, gains_ref, turned_ref = refs[12:]
    rows = xs[0].shape[0]
    q_columns = q_heads * HEAD
    columns = q_columns + 2 * HEAD
    width = xs[0].shape[1]
    total = rows * 8
    whole = arrived_ref[...].reshape(width, columns + 128)
    small = whole[:, columns:].astype(F32)
    small_rows = small.T
    gain_one = small_rows[experts : experts + 1]
    gains_ref[...] = small_rows[: experts + 8]
    turned_ref[...] = whole[:, :columns].astype(F32).T.astype(BF16)
    me = me_ref[0]
    for slot in range(8):
        x = xs[slot][...].astype(F32)
        scale = lax.rsqrt(jnp.mean(x * x, axis=1, keepdims=True) + EPSILON)
        h1_ref[slot] = (x * scale * gain_one).astype(BF16)
    for slot in range(8):
        block = dot(turned_ref[...], h1_ref[slot], ((1,), (1,)))
        place = pl.multiple_of((me ^ slot) * rows, rows)
        pre_ref[:, pl.ds(place, rows)] = block
    cosine, sine = cos_ref[...], sin_ref[...]
    gain_query = column_gain(small, experts + 2)
    gain_key = column_gain(small, experts + 3)
    key = head_forward(pre_ref[q_columns : q_columns + HEAD], gain_key, cosine, sine)[0]
    key = key.T.astype(BF16)
    value = pre_ref[q_columns + HEAD :].astype(BF16)
    inverse_ref[...] = jnp.zeros(inverse_ref.shape, F32)
    for head in range(q_heads):
        query = head_forward(pre_ref[head * HEAD : (head + 1) * HEAD], gain_query, cosine, sine)[0]
        query = query.astype(BF16) * jnp.array(HEAD ** (-0.5), BF16)
        for tile in range(total // TILE):
            low, high = tile * TILE, (tile + 1) * TILE
            scores = dot(key[:high], query[:, low:high])
            u = lax.broadcasted_iota(jnp.int32, (high, TILE), 0)
            t = lax.broadcasted_iota(jnp.int32, (high, TILE), 1) + low
            allowed = (u >= start_ref[:, low:high]) & (u <= t)
            powers = jnp.where(allowed, jnp.exp(scores), 0.0)
            inverse = 1.0 / jnp.sum(powers, axis=0, keepdims=True)
            probs = (powers * inverse).astype(BF16)
            mixed = dot(value[:, :high], probs).astype(BF16)
            inverse_ref[head : head + 1, low:high] = inverse
            for part in range(TILE // rows):
                out_ref[low // rows + part, head * HEAD : (head + 1) * HEAD] = mixed[
                    :, part * rows : (part + 1) * rows
                ]


def attention_forward(me, xs, arrived, cosine, sine, start, experts, q_heads):
    rows, width = xs[0].shape
    total = 8 * rows
    columns = arrived.shape[2] - 128
    return pl.pallas_call(
        functools.partial(forward_kernel, experts=experts, q_heads=q_heads),
        out_shape=(
            shape((8, rows, width), BF16),
            shape((columns, total), F32),
            shape((8, q_heads * HEAD, rows), BF16),
            shape((8, total), F32),
            shape((experts + 8, width), F32),
            shape((columns, width), BF16),
        ),
        in_specs=[SMEM] + [VMEM] * 12,
        out_specs=[VMEM] * 6,
        compiler_params=params(),
        name="attention_forward",
    )(me, *xs, arrived, cosine, sine, start)


def head_backward(grad, normed, scale, gain, cosine, sine):
    a, b = grad[: HEAD // 2], grad[HEAD // 2 :]
    unturned = jnp.concatenate([a * cosine + b * sine, b * cosine - a * sine], axis=0)
    gain_grad = jnp.sum(unturned * normed, axis=1, keepdims=True)
    inner = unturned * gain
    pre_grad = scale * (inner - normed * jnp.mean(inner * normed, axis=0, keepdims=True))
    return pre_grad, gain_grad


def backward_kernel(me_ref, *refs, experts, q_heads):
    das = refs[:8]
    arrived_ref, wo_ref, cos_ref, sin_ref, start_ref = refs[8:13]
    h1_ref, pre_ref, out_ref, inverse_ref, turned_ref, extra_ref = refs[13:19]
    first_ref, wo_grad_ref, keep_ref, send_ref = refs[19:23]
    da_ref, mixed_grad_ref, dkey_ref, dvalue_ref, low_ref, out_slots_ref = refs[23:]
    rows, width = das[0].shape
    q_columns = q_heads * HEAD
    columns = q_columns + 2 * HEAD
    total = rows * 8
    me = me_ref[0]
    for slot in range(8):
        da_ref[slot * rows : (slot + 1) * rows] = das[slot][...]
    for slot in range(8):
        block = me ^ slot
        place = pl.multiple_of(block * rows, rows)
        back = dot(wo_ref[...], das[slot][...], ((1,), (1,)))
        mixed_grad_ref[:, pl.ds(place, rows)] = back.astype(BF16)
        out_slots_ref[:, slot * rows : (slot + 1) * rows] = out_ref[block]
    wo_grad = dot(out_slots_ref[...], da_ref[...]).astype(BF16)
    for part in range(8):
        wo_grad_ref[part] = wo_grad[:, part * rows : (part + 1) * rows]

    small = arrived_ref[:, : HEAD // 8, columns:].astype(F32).reshape(HEAD, 128)
    gain_query = small[:, experts + 2 : experts + 3]
    gain_key = small[:, experts + 3 : experts + 4]
    cosine, sine = cos_ref[...], sin_ref[...]
    key_turned, key_normed, key_scale = head_forward(
        pre_ref[q_columns : q_columns + HEAD], gain_key, cosine, sine
    )
    key_low = key_turned.astype(BF16)
    key = key_turned.T.astype(BF16)
    value = pre_ref[q_columns + HEAD :].T.astype(BF16)
    dkey_ref[...] = jnp.zeros(dkey_ref.shape, F32)
    dvalue_ref[...] = jnp.zeros(dvalue_ref.shape, F32)
    gain_query_grad = jnp.zeros((HEAD, 1), F32)
    pieces = []
    for head in range(q_heads):
        span = slice(head * HEAD, (head + 1) * HEAD)
        turned, normed, scale = head_forward(pre_ref[span], gain_query, cosine, sine)
        query = turned.astype(BF16) * jnp.array(HEAD ** (-0.5), BF16)
        grads = []
        for tile in range(total // TILE):
            low, high = tile * TILE, (tile + 1) * TILE
            part = query[:, low:high]
            mixed_grad = mixed_grad_ref[span, low:high]
            scores = dot(key[:high], part)
            u = lax.broadcasted_iota(jnp.int32, (high, TILE), 0)
            t = lax.broadcasted_iota(jnp.int32, (high, TILE), 1) + low
            allowed = (u >= start_ref[:, low:high]) & (u <= t)
            probs = jnp.where(allowed, jnp.exp(scores) * inverse_ref[head : head + 1, low:high], 0.0)
            attend = dot(value[:high], mixed_grad)
            delta = jnp.sum(probs * attend, axis=0, keepdims=True)
            score_low = (probs * (attend - delta)).astype(BF16)
            grads.append(dot(key_low[:, :high], score_low))
            dkey_ref[:, :high] += dot(part, score_low, ((1,), (1,)))
            dvalue_ref[:, :high] += dot(mixed_grad, probs.astype(BF16), ((1,), (1,)))
        query_grad = jnp.concatenate(grads, axis=1) * HEAD ** (-0.5)
        pre_grad, gain_grad = head_backward(query_grad, normed, scale, gain_query, cosine, sine)
        gain_query_grad += gain_grad
        pieces.append(pre_grad)
    pre_grad, gain_key_grad = head_backward(
        dkey_ref[...], key_normed, key_scale, gain_key, cosine, sine
    )
    pieces += [pre_grad, dvalue_ref[...]]
    pre_grad = jnp.concatenate(pieces, axis=0)
    low_ref[...] = pre_grad.astype(BF16)
    low_rows = pre_grad.T.astype(BF16)
    slots_grad = []
    for slot in range(8):
        place = pl.multiple_of((me ^ slot) * rows, rows)
        slots_grad.append(low_ref[:, pl.ds(place, rows)])
    slots_grad = jnp.concatenate(slots_grad, axis=1)
    weights_grad = dot(slots_grad, h1_ref[...].reshape(total, width)).astype(BF16)
    extra = extra_ref[...]
    lane = lax.broadcasted_iota(jnp.int32, (HEAD, 128), 1)
    gains = jnp.where(lane == 0, gain_query_grad, jnp.where(lane == 1, gain_key_grad, 0.0))
    gains = gains.T[:2]
    step = HEAD // 8
    for part in range(8):
        span = slice(part * rows, (part + 1) * rows)
        first_ref[part, :columns] = weights_grad[:, span]
        mine = jnp.concatenate([gains[:, part * step : (part + 1) * step], jnp.zeros((2, rows - step), F32)], axis=1)
        whole = jnp.concatenate([extra[: experts + 1, span], mine, jnp.zeros((64 - experts - 3, rows), F32)], axis=0)
        first_ref[part, columns:] = whole.astype(BF16)
    turned = turned_ref[...]
    for slot in range(8):
        place = pl.multiple_of((me ^ slot) * rows, rows)
        low_rows_slot = slots_grad[:, slot * rows : (slot + 1) * rows].astype(F32).T.astype(BF16)
        part = dot(low_rows_slot, turned)
        if slot % 2 == 0:
            keep_ref[slot // 2] = part
        else:
            send_ref[slot // 2] = part.astype(BF16)


def attention_backward(me, das, arrived, wo, cosine, sine, start, h1, pre, out, inverse, turned, extra, experts, q_heads):
    rows, width = das[0].shape
    total = 8 * rows
    columns = pre.shape[0]
    q_columns = q_heads * HEAD
    return pl.pallas_call(
        functools.partial(backward_kernel, experts=experts, q_heads=q_heads),
        out_shape=(
            shape((8, columns + 64, rows), BF16),
            shape((8, q_columns, rows), BF16),
            shape((4, rows, width), F32),
            shape((4, rows, width), BF16),
        ),
        in_specs=[SMEM] + [VMEM] * 19,
        out_specs=[VMEM] * 4,
        scratch_shapes=[
            pltpu.VMEM((total, width), BF16),
            pltpu.VMEM((q_columns, total), BF16),
            pltpu.VMEM((HEAD, total), F32),
            pltpu.VMEM((HEAD, total), F32),
            pltpu.VMEM((columns, total), BF16),
            pltpu.VMEM((q_columns, total), BF16),
        ],
        compiler_params=params(),
        name="attention_backward",
    )(me, *das, arrived, wo, cosine, sine, start, h1, pre, out, inverse, turned, extra)


def middle_kernel(o_ref, wo_ref, x_ref, gains_ref, middle_ref, low_ref, high_ref, probs_ref, *, experts):
    rows, width = x_ref.shape
    mixed = o_ref[...].reshape(-1, rows).astype(F32).T.astype(BF16)
    middle = x_ref[...].astype(F32) + dot(mixed, wo_ref[...])
    middle_ref[...] = middle
    scale = lax.rsqrt(jnp.mean(middle * middle, axis=1, keepdims=True) + EPSILON)
    hidden = (middle * scale * gains_ref[experts + 1 : experts + 2]).astype(BF16)
    low_ref[...] = hidden[: rows // 2]
    high_ref[...] = hidden[rows // 2 :]
    probs_ref[...] = softmax_rows(dot(gains_ref[:experts].astype(BF16), hidden, ((1,), (1,))))


def softmax_rows(logits):
    powers = jnp.exp(logits - jnp.max(logits, axis=0, keepdims=True))
    return powers / jnp.sum(powers, axis=0, keepdims=True)


def middle_layer(o, wo, x, gains, experts):
    rows, width = x.shape
    return pl.pallas_call(
        functools.partial(middle_kernel, experts=experts),
        out_shape=(
            shape((rows, width), F32),
            shape((rows // 2, width), BF16),
            shape((rows // 2, width), BF16),
            shape((experts, rows), F32),
        ),
        in_specs=[VMEM] * 4,
        out_specs=[VMEM] * 4,
        compiler_params=params(),
        name="middle_layer",
    )(o, wo, x, gains)


def expert_kernel(owner_ref, *refs, experts, capacity):
    h_low, h_high, c_low, c_high = refs[:4], refs[4:8], refs[8:12], refs[12:16]
    gains_ref, gate_ref, up_ref, down_ref = refs[16:20]
    p_low, p_high = refs[20:24], refs[24:28]
    rows_h, rows_c, gate_out, up_out, active_out, weighted_out, deal_out, share_out = refs[28:36]
    back_ref, turn_ref, share_ref = refs[36:]
    per_owner = gate_ref.shape[0]
    width = gate_ref.shape[1]
    rows = 2 * h_low[0].shape[1]
    owner = owner_ref[0]
    router = gains_ref[:experts].astype(BF16)
    lanes = lax.broadcasted_iota(jnp.int32, (experts, 128), 1)
    subs = lax.broadcasted_iota(jnp.int32, (experts, 128), 0)
    eye = (lanes == subs).astype(BF16)
    before = (
        lax.broadcasted_iota(jnp.int32, (rows, rows), 0)
        <= lax.broadcasted_iota(jnp.int32, (rows, rows), 1)
    ).astype(BF16)
    mine_of = lax.broadcasted_iota(jnp.int32, (experts, rows), 0) - owner * per_owner
    slot = lax.broadcasted_iota(jnp.int32, (capacity, rows), 0).astype(F32) + 1.0
    for block in range(16):
        y, x = block // 4, block % 4
        h = jnp.concatenate([h_low[y][x], h_high[x][y]], axis=0)
        c = jnp.concatenate([c_low[y][x], c_high[x][y]], axis=0)
        mask = dot(eye, c[:, width:], ((1,), (1,)))
        ranks = dot(mask.astype(BF16), before)
        probs = softmax_rows(dot(router, h, ((1,), (1,)))) * mask
        share = probs / jnp.sum(probs, axis=0, keepdims=True)
        deals, shares = [], []
        for k in range(per_owner):
            mine = mine_of == k
            hit = jnp.sum(jnp.where(mine, mask, 0.0), axis=0, keepdims=True)
            rank = jnp.sum(jnp.where(mine, ranks, 0.0), axis=0, keepdims=True)
            part = jnp.sum(jnp.where(mine, share, 0.0), axis=0, keepdims=True)
            deal = jnp.where((rank == slot) & (hit > 0.5), 1.0, 0.0)
            deals.append(deal)
            span = slice(block * capacity, (block + 1) * capacity)
            column = jnp.sum(deal * part, axis=1, keepdims=True)
            share_ref[k, span] = jnp.broadcast_to(column, (capacity, 128))
        deal = jnp.concatenate(deals, axis=0)
        deal_low = deal.astype(BF16)
        padded = jnp.concatenate([deal, jnp.zeros((128 - deal.shape[0], rows), F32)], axis=0)
        turn_ref[block] = padded.T.astype(BF16)
        taken_h = dot(deal_low, h).astype(BF16)
        taken_c = dot(deal_low, c[:, :width]).astype(BF16)
        for k in range(per_owner):
            span = slice(block * capacity, (block + 1) * capacity)
            rows_h[k, span] = taken_h[k * capacity : (k + 1) * capacity]
            rows_c[k, span] = taken_c[k * capacity : (k + 1) * capacity]
    deal_out[...] = turn_ref[...]
    share_out[...] = share_ref[...]
    lane = lax.broadcasted_iota(jnp.int32, (TILE, 128), 1)
    for k in range(per_owner):
        for tile in range(16 * capacity // TILE):
            span = slice(tile * TILE, (tile + 1) * TILE)
            gate = dot(rows_h[k, span], gate_ref[k])
            up = dot(rows_h[k, span], up_ref[k])
            back = dot(rows_c[k, span], down_ref[k], ((1,), (1,)))
            sig = 1.0 / (1.0 + jnp.exp(-gate))
            silu = gate * sig
            active = silu * up
            active_low = active.astype(BF16)
            share = share_ref[k, span, :1]
            route_grad = jnp.sum(active_low.astype(F32) * back, axis=1, keepdims=True)
            grad = back * share
            gate_low = (grad * up * (sig + silu * (1.0 - sig))).astype(BF16)
            up_low = (grad * silu).astype(BF16)
            active_out[k, span] = active_low
            weighted_out[k, span] = (active * share).astype(BF16)
            gate_out[k, span] = gate_low
            up_out[k, span] = up_low
            total = dot(gate_low, gate_ref[k], ((1,), (1,))) + dot(up_low, up_ref[k], ((1,), (1,)))
            back_ref[k, span, :width] = total.astype(BF16)
            high = route_grad.astype(BF16).astype(F32)
            place = owner * per_owner + k
            spread = jnp.where(lane == place, high, 0.0)
            spread = jnp.where(lane == place + experts, route_grad - high, spread)
            back_ref[k, span, width:] = spread.astype(BF16)
    for block in range(16):
        y, x = block // 4, block % 4
        span = slice(block * capacity, (block + 1) * capacity)
        both = jnp.concatenate([back_ref[k, span] for k in range(per_owner)], axis=0)
        total = dot(turn_ref[block][:, : both.shape[0]], both).astype(BF16)
        p_low[y][x] = total[: rows // 2]
        p_high[x][y] = total[rows // 2 :]


def expert_layer(owner, h_low, h_high, c_low, c_high, gains, gate, up, down, experts, capacity):
    per_owner, width, hidden = gate.shape
    half = h_low[0].shape[1]
    count = 16 * capacity
    piece = shape((4, half, width + 128), BF16)
    return pl.pallas_call(
        functools.partial(expert_kernel, experts=experts, capacity=capacity),
        out_shape=[piece] * 8
        + [
            shape((per_owner, count, width), BF16),
            shape((per_owner, count, width), BF16),
        ]
        + [shape((per_owner, count, hidden), BF16)] * 4
        + [
            shape((16, 2 * half, 128), BF16),
            shape((per_owner, count, 128), F32),
        ],
        in_specs=[SMEM] + [VMEM] * 20,
        out_specs=[VMEM] * 16,
        scratch_shapes=[
            pltpu.VMEM((per_owner, count, width + 128), BF16),
            pltpu.VMEM((16, 2 * half, 128), BF16),
            pltpu.VMEM((per_owner, count, 128), F32),
        ],
        compiler_params=params(),
        name="expert_layer",
    )(owner, *h_low, *h_high, *c_low, *c_high, gains, gate, up, down)


def weights_kernel(rows_h, rows_c, gate_low, up_low, active, weighted, deal, share, down_ref, *outs, capacity):
    gate_grad, up_grad, down_grad = outs[:3]
    p_low, p_high = outs[3:7], outs[7:11]
    (out_ref,) = outs[11:]
    per_owner, count, width = rows_h.shape
    half = deal.shape[1] // 2
    first = ((0,), (0,))
    for k in range(per_owner):
        gate_grad[k] = dot(rows_h[k], gate_low[k], first).astype(BF16)
        up_grad[k] = dot(rows_h[k], up_low[k], first).astype(BF16)
        down_grad[k] = dot(weighted[k], rows_c[k], first).astype(BF16)
        for tile in range(count // TILE):
            span = slice(tile * TILE, (tile + 1) * TILE)
            produced = dot(active[k, span], down_ref[k]).astype(BF16).astype(F32)
            out_ref[k, span] = (produced * share[k, span, :1]).astype(BF16)
    for block in range(16):
        y, x = block // 4, block % 4
        span = slice(block * capacity, (block + 1) * capacity)
        both = jnp.concatenate([out_ref[k, span] for k in range(per_owner)], axis=0)
        total = dot(deal[block][:, : both.shape[0]], both).astype(BF16)
        p_low[y][x] = total[:half]
        p_high[x][y] = total[half:]


def expert_weights(rows_h, rows_c, gate_low, up_low, active, weighted, deal, share, down, capacity):
    per_owner, count, width = rows_h.shape
    hidden = gate_low.shape[2]
    half = deal.shape[1] // 2
    return pl.pallas_call(
        functools.partial(weights_kernel, capacity=capacity),
        out_shape=[
            shape((per_owner, width, hidden), BF16),
            shape((per_owner, width, hidden), BF16),
            shape((per_owner, hidden, width), BF16),
        ]
        + [shape((4, half, width), BF16)] * 8,
        in_specs=[VMEM] * 9,
        out_specs=[VMEM] * 11,
        scratch_shapes=[pltpu.VMEM((per_owner, count, width), BF16)],
        compiler_params=params(),
        name="expert_weights",
    )(rows_h, rows_c, gate_low, up_low, active, weighted, deal, share, down)


def fold_kernel(*refs):
    low, high = refs[:4], refs[4:8]
    outs = refs[8:]
    for part in range(4):
        for pieces, out in ((low, outs[part]), (high, outs[4 + part])):
            total = pieces[0][part].astype(F32)
            for piece in pieces[1:]:
                total = total + piece[part].astype(F32)
            out[...] = total.astype(out.dtype)


def fold(low, high):
    half, width = low[0].shape[1:]
    kinds = [F32, BF16, BF16, BF16] * 2
    return pl.pallas_call(
        fold_kernel,
        out_shape=[shape((half, width), kind) for kind in kinds],
        in_specs=[VMEM] * 8,
        out_specs=[VMEM] * 8,
        compiler_params=params(),
        name="fold",
    )(*low, *high)


def joined(low, high):
    sums = []
    for pieces in (low, high):
        total = pieces[0][...]
        for piece in pieces[1:]:
            total = total + piece[...].astype(F32)
        sums.append(total)
    return jnp.concatenate(sums, axis=0)


def output_kernel(*refs):
    middle_ref, out_ref = refs[8:]
    out_ref[...] = (middle_ref[...] + joined(refs[:4], refs[4:8])).astype(BF16)


def layer_output(low, high, middle):
    return pl.pallas_call(
        output_kernel,
        out_shape=shape(middle.shape, BF16),
        in_specs=[VMEM] * 9,
        out_specs=VMEM,
        compiler_params=params(),
        name="layer_output",
    )(*low, *high, middle)


def router_kernel(*refs, experts):
    middle_ref, probs_ref, routed_ref, gains_ref, c_ref, h_low, h_high = refs[8:15]
    grad_ref, send_ref, extra_ref = refs[15:]
    width = middle_ref.shape[1]
    rows = middle_ref.shape[0]
    returned = joined(refs[:4], refs[4:8])
    tail = returned[:, width:].T
    route_grad = tail[:experts] + tail[experts : 2 * experts]
    lanes = lax.broadcasted_iota(jnp.int32, (experts, 128), 1)
    subs = lax.broadcasted_iota(jnp.int32, (experts, 128), 0)
    mask = dot((lanes == subs).astype(BF16), routed_ref[...], ((1,), (1,)))
    probs = probs_ref[...]
    picked = probs * mask
    picked_sum = jnp.sum(picked, axis=0, keepdims=True)
    share = picked / picked_sum
    picked_grad = (route_grad - jnp.sum(route_grad * share, axis=0, keepdims=True)) / picked_sum
    prob_grad = mask * picked_grad
    logit_grad = probs * (prob_grad - jnp.sum(probs * prob_grad, axis=0, keepdims=True))
    logit_low = logit_grad.astype(BF16)
    hidden = jnp.concatenate([h_low[...], h_high[...]], axis=0)
    extra_ref[:experts] = dot(logit_low, hidden)
    logit_rows = jnp.concatenate([logit_grad, jnp.zeros((128 - experts, rows), F32)], axis=0).T
    router = gains_ref[:experts].astype(BF16)
    hidden_grad = returned[:, :width] + dot(logit_rows[:, :experts].astype(BF16), router)
    middle = middle_ref[...]
    scale = lax.rsqrt(jnp.mean(middle * middle, axis=1, keepdims=True) + EPSILON)
    normed = middle * scale
    extra_ref[experts : experts + 8] = jnp.broadcast_to(
        jnp.sum(hidden_grad * normed, axis=0, keepdims=True), (8, width)
    )
    inner = hidden_grad * gains_ref[experts + 1 : experts + 2]
    grad = c_ref[...].astype(F32) + scale * (
        inner - normed * jnp.mean(inner * normed, axis=1, keepdims=True)
    )
    grad_ref[...] = grad
    send_ref[...] = grad.astype(BF16)


def router_backward(low, high, middle, probs, routed, gains, c, h_low, h_high, experts):
    rows, width = middle.shape
    return pl.pallas_call(
        functools.partial(router_kernel, experts=experts),
        out_shape=(
            shape((rows, width), F32),
            shape((rows, width), BF16),
            shape((experts + 8, width), F32),
        ),
        in_specs=[VMEM] * 15,
        out_specs=[VMEM] * 3,
        compiler_params=params(),
        name="router_backward",
    )(*low, *high, middle, probs, routed, gains, c, h_low, h_high)


def pair_kernel(keep_ref, came_ref, *outs):
    for part in range(4):
        total = keep_ref[part] + came_ref[part].astype(F32)
        outs[part][...] = total.astype(outs[part].dtype)


def pair_sum(keep, came):
    rows, width = keep.shape[1:]
    return pl.pallas_call(
        pair_kernel,
        out_shape=[shape((rows, width), kind) for kind in (F32, BF16, BF16, BF16)],
        in_specs=[VMEM] * 2,
        out_specs=[VMEM] * 4,
        compiler_params=params(),
        name="pair_sum",
    )(keep, came)


def input_kernel(p0, p1, p2, p3, x_ref, gains_ref, middle_grad_ref, out_ref, *, experts):
    total = p0[...] + p1[...].astype(F32) + p2[...].astype(F32) + p3[...].astype(F32)
    x = x_ref[...].astype(F32)
    scale = lax.rsqrt(jnp.mean(x * x, axis=1, keepdims=True) + EPSILON)
    normed = x * scale
    inner = total * gains_ref[experts : experts + 1]
    out_ref[...] = middle_grad_ref[...] + scale * (
        inner - normed * jnp.mean(inner * normed, axis=1, keepdims=True)
    )


def input_grad(parts, x, gains, middle_grad, experts):
    return pl.pallas_call(
        functools.partial(input_kernel, experts=experts),
        out_shape=shape(middle_grad.shape, F32),
        in_specs=[VMEM] * 7,
        out_specs=VMEM,
        compiler_params=params(),
        name="input_grad",
    )(*parts, x, gains, middle_grad)


def sum_kernel(in_ref, out_ref):
    total = in_ref[0].astype(F32)
    for i in range(1, in_ref.shape[0]):
        total = total + in_ref[i].astype(F32)
    total = total.astype(BF16)
    for i in range(in_ref.shape[0]):
        out_ref[i] = total


def sum_all(pieces):
    return pl.pallas_call(
        sum_kernel,
        out_shape=shape(pieces.shape, BF16),
        in_specs=[VMEM],
        out_specs=VMEM,
        compiler_params=params(),
        name="sum_all",
    )(pieces)


def final_kernel(third_ref, wq_ref, wk_ref, wv_ref, gain_ref, *outs, experts, columns):
    query_ref, key_ref, value_ref, output_ref, one_ref, two_ref, gains_ref, router_ref = outs
    rows = third_ref.shape[2]
    tall = (columns + 64) // 2
    q_columns = query_ref.shape[1] // 8
    kv_columns = key_ref.shape[1] // 8
    extra = jnp.zeros((64, rows), F32)
    sums = jnp.zeros((rows, 1), F32)
    for source in range(8):
        block = jnp.concatenate(
            [third_ref[2 * source, :tall], third_ref[2 * source + 1, :tall]], axis=0
        ).astype(F32)
        turned = block[:columns].T
        query = turned[:, :q_columns]
        key = turned[:, q_columns : q_columns + kv_columns]
        value = turned[:, q_columns + kv_columns :]
        q_span = slice(source * q_columns, (source + 1) * q_columns)
        kv_span = slice(source * kv_columns, (source + 1) * kv_columns)
        query_ref[:, q_span] = query
        key_ref[:, kv_span] = key
        value_ref[:, kv_span] = value
        sums = sums + jnp.sum(query * wq_ref[:, q_span].astype(F32), axis=1, keepdims=True)
        sums = sums + jnp.sum(key * wk_ref[:, kv_span].astype(F32), axis=1, keepdims=True)
        sums = sums + jnp.sum(value * wv_ref[:, kv_span].astype(F32), axis=1, keepdims=True)
        extra = extra + block[columns:]
        for half in range(2):
            size = rows // 2
            output_ref[half * size : (half + 1) * size, source * rows : (source + 1) * rows] = (
                third_ref[2 * source + half, tall:].astype(F32)
            )
    one_ref[...] = jnp.broadcast_to(sums, (rows, 128)).T[:1] / gain_ref[...].astype(F32)
    two_ref[...] = extra[experts : experts + 1]
    gains_ref[...] = extra[experts + 1 : experts + 3]
    router_ref[...] = jnp.concatenate([extra, jnp.zeros((64, rows), F32)], axis=0).T[:, :experts]


def final_grads(third, wq, wk, wv, gain, experts, columns):
    rows = third.shape[2]
    return pl.pallas_call(
        functools.partial(final_kernel, experts=experts, columns=columns),
        out_shape=(
            shape(wq.shape, F32),
            shape(wk.shape, F32),
            shape(wv.shape, F32),
            shape((rows, 8 * rows), F32),
            shape((1, rows), F32),
            shape((1, rows), F32),
            shape((2, rows), F32),
            shape((rows, experts), F32),
        ),
        in_specs=[VMEM] * 5,
        out_specs=[VMEM] * 8,
        compiler_params=params(),
        name="final_grads",
    )(third, wq, wk, wv, gain)


def send(values, axis, flip):
    count = lax.axis_size(axis)
    return lax.ppermute(values, axis, [(i, i ^ flip) for i in range(count)])


def gather_fsdp(block):
    same = {0: block}
    for step in Z_STEPS:
        same[step] = send(block, "fsdp", step)
    slots = []
    for step in (0, 2, 4, 6):
        slots += [same[step], send(same[step], "fsdp", CORE)]
    return slots


def gather_expert(low, high):
    low_x = {s: send(low, "expert", s) for s in X_STEPS}
    high_y = {s: send(high, "expert", s) for s in Y_STEPS}
    low_x = jnp.concatenate([v[None] for v in (low, low_x[1], low_x[2], low_x[3])], axis=0)
    high_y = jnp.concatenate([v[None] for v in (high, high_y[4], high_y[8], high_y[12])], axis=0)
    low_xy = {s: send(low_x, "expert", s) for s in Y_STEPS}
    high_yx = {s: send(high_y, "expert", s) for s in X_STEPS}
    return (
        [low_x, low_xy[4], low_xy[8], low_xy[12]],
        [high_y, high_yx[1], high_yx[2], high_yx[3]],
    )


def scatter_expert(low, high):
    low = [low[0]] + [send(low[i], "expert", 4 * i) for i in (1, 2, 3)]
    high = [high[0]] + [send(high[i], "expert", i) for i in (1, 2, 3)]
    parts = fold(low, high)
    low = [parts[0]] + [send(parts[i], "expert", i) for i in (1, 2, 3)]
    high = [parts[4]] + [send(parts[4 + i], "expert", 4 * i) for i in (1, 2, 3)]
    return low, high


def shards(
    tokens,
    lengths,
    routes,
    first_gain,
    query_weight,
    key_weight,
    value_weight,
    output_weight,
    query_gain,
    key_gain,
    second_gain,
    router_weight,
    gate_weight,
    up_weight,
    down_weight,
    cotangent,
):
    own = tokens[0]
    upstream = cotangent[0]
    rows, width = own.shape
    fsdp = lax.axis_size("fsdp")
    owners = lax.axis_size("expert")
    me = lax.axis_index("fsdp").astype(jnp.int32).reshape(1)
    owner = lax.axis_index("expert").astype(jnp.int32).reshape(1)
    experts = router_weight.shape[1]
    capacity = 3 * rows * routes.shape[2] // (2 * experts)
    kv_columns = key_weight.shape[1] // fsdp
    q_columns = query_weight.shape[1] // fsdp
    columns = q_columns + 2 * kv_columns
    q_heads = q_columns // HEAD

    xs = gather_fsdp(own)
    head_gains = jnp.zeros((rows, 2), BF16)
    head_gains = jnp.concatenate(
        [
            jnp.concatenate([query_gain[:, None], key_gain[:, None]], axis=1),
            jnp.zeros((rows - query_gain.shape[0], 2), BF16),
        ],
        axis=0,
    )
    small = jnp.concatenate(
        [
            router_weight,
            first_gain[:, None],
            second_gain[:, None],
            head_gains,
            jnp.zeros((rows, 128 - experts - 4), BF16),
        ],
        axis=1,
    )
    outgoing = jnp.concatenate(
        [
            query_weight.reshape(rows, fsdp, q_columns),
            key_weight.reshape(rows, fsdp, kv_columns),
            value_weight.reshape(rows, fsdp, kv_columns),
            jnp.broadcast_to(small[:, None, :], (rows, fsdp, 128)),
        ],
        axis=2,
    ).transpose(1, 0, 2)
    arrived = lax.all_to_all(outgoing, "fsdp", 0, 0, tiled=True)
    whole_output = lax.all_gather(output_weight, "fsdp", axis=0, tiled=True)
    routed = jnp.sum(
        (routes[0][:, :, None] == jnp.arange(128, dtype=jnp.int32)).astype(F32), axis=1
    ).astype(BF16)
    dressed = jnp.concatenate([upstream, routed], axis=1)
    c_low, c_high = gather_expert(dressed[: rows // 2], dressed[rows // 2 :])

    ends = jnp.cumsum(lengths[0])
    place = jnp.arange(rows * fsdp, dtype=jnp.int32)
    start = jnp.max(jnp.where(ends[:, None] <= place[None, :], ends[:, None], 0), axis=0)
    position = (place - start).astype(F32)
    frequency = ROPE_BASE ** (-jnp.arange(HEAD // 2, dtype=F32) * 2.0 / HEAD)
    angles = frequency[:, None] * position[None, :]
    cosine, sine = jnp.cos(angles), jnp.sin(angles)
    start = start[None, :].astype(jnp.int32)

    h1, pre, mixed, inverse, gains, turned = attention_forward(
        me, xs, arrived, cosine, sine, start, experts, q_heads
    )
    mixed_own = lax.all_to_all(mixed, "fsdp", 0, 0, tiled=True)
    middle, own_low, own_high, probs = middle_layer(mixed_own, whole_output, own, gains, experts)
    h_low, h_high = gather_expert(own_low, own_high)
    made = expert_layer(
        owner, h_low, h_high, c_low, c_high, gains, gate_weight, up_weight, down_weight, experts, capacity
    )
    back_low, back_high = scatter_expert(made[:4], made[4:8])
    grads = expert_weights(*made[8:], down_weight, capacity)
    gate_sum, up_sum, down_sum = (lax.psum(grads[i], "fsdp").astype(F32) for i in range(3))
    out_low, out_high = scatter_expert(grads[3:7], grads[7:11])

    middle_grad, middle_low, extra = router_backward(
        back_low, back_high, middle, probs, routed, gains, upstream, own_low, own_high, experts
    )
    das = gather_fsdp(middle_low)
    first, output_grad, keep, give = attention_backward(
        me, das, arrived, output_weight, cosine, sine, start, h1, pre, mixed, inverse, turned, extra, experts, q_heads
    )
    came = send(give, "fsdp", CORE)
    parts = pair_sum(keep, came)
    parts = [parts[0]] + [send(parts[i], "fsdp", 2 * i) for i in (1, 2, 3)]
    first = lax.all_to_all(first, "fsdp", 0, 0, tiled=True)
    second = jnp.concatenate(
        [first.reshape(owners, -1, rows), output_grad.reshape(owners, -1, rows)], axis=1
    )
    second = sum_all(lax.all_to_all(second, "expert", 0, 0, tiled=True))
    third = lax.all_to_all(second, "expert", 0, 0, tiled=True)
    tokens_grad = input_grad(parts, own, gains, middle_grad, experts)
    layer_out = layer_output(out_low, out_high, middle)
    query_sum, key_sum, value_sum, output_sum, one_sum, two_sum, gain_sums, router_sum = final_grads(
        third, query_weight, key_weight, value_weight, first_gain[None], experts, columns
    )
    step = HEAD // fsdp
    return (
        layer_out[None],
        tokens_grad[None],
        one_sum[0],
        query_sum,
        key_sum,
        value_sum,
        output_sum,
        gain_sums[0, :step],
        gain_sums[1, :step],
        two_sum[0],
        router_sum,
        gate_sum,
        up_sum,
        down_sum,
    )


def solution(mesh):
    whole = P("expert", "fsdp", None)
    rows = P("fsdp", None)
    vector = P("fsdp")
    owned = P("expert", None, None)
    return jax.shard_map(
        shards,
        mesh=mesh,
        in_specs=(
            whole,
            P("expert", None),
            whole,
            vector,
            rows,
            rows,
            rows,
            rows,
            vector,
            vector,
            vector,
            rows,
            owned,
            owned,
            owned,
            whole,
        ),
        out_specs=(
            whole,
            whole,
            vector,
            rows,
            rows,
            rows,
            rows,
            vector,
            vector,
            vector,
            rows,
            owned,
            owned,
            owned,
        ),
        check_vma=False,
    )
```

```python
import functools

import jax
import jax.numpy as jnp
from jax import lax
from jax.experimental import pallas as pl
from jax.experimental.pallas import tpu as pltpu
from jax.sharding import PartitionSpec as P

EPSILON = 1e-06
ROPE_BASE = 10000.0
HEAD = 64
TILE = 256
F32 = jnp.float32
BF16 = jnp.bfloat16
VMEM = pl.BlockSpec(memory_space=pltpu.VMEM)
SMEM = pl.BlockSpec(memory_space=pltpu.SMEM)
ANY = pl.BlockSpec(memory_space=pl.ANY)
CORE = 1
Z_STEPS = (2, 6, 4)
X_STEPS = (1, 3, 2)
Y_STEPS = (4, 12, 8)


def dot(left, right, dims=((1,), (0,))):
    return lax.dot_general(left, right, (dims, ((), ())), preferred_element_type=F32)


def params(mib):
    return pltpu.CompilerParams(vmem_limit_bytes=mib * 1024 * 1024)


def cost(micros):
    return pl.CostEstimate(flops=0, bytes_accessed=int(micros * 3.6e6), transcendentals=0)


def shape(extent, dtype):
    return jax.ShapeDtypeStruct(extent, dtype)


def pack_kernel(wq_ref, wk_ref, wv_ref, router_ref, one_ref, two_ref, qg_ref, kg_ref, out_ref):
    rows, experts = router_ref.shape
    pairs = wk_ref.shape[1] // 128
    wide = wq_ref.shape[1] // 8
    narrow = wk_ref.shape[1] // 8
    router = jnp.concatenate([router_ref[...].astype(F32), jnp.zeros((rows, 128 - experts), F32)], axis=1)
    router = router.T[:experts]
    count = qg_ref.shape[1]
    heads = jnp.concatenate([qg_ref[...], kg_ref[...]], axis=0).astype(F32)
    heads = jnp.concatenate([heads, jnp.zeros((2, 128 - count), F32)], axis=1)
    heads = jnp.concatenate([heads, jnp.zeros((126, 128), F32)], axis=0).T[:count]
    small = jnp.concatenate(
        [router, one_ref[...].astype(F32), two_ref[...].astype(F32), jnp.zeros((6, 128), F32), heads], axis=0
    ).astype(BF16)
    for part in range(8):
        out_ref[part, :wide] = wq_ref[:, part * wide : (part + 1) * wide].astype(F32).T.astype(BF16)
        out_ref[part, wide + 2 * narrow :] = small
    for pair in range(pairs):
        span = slice(pair * 128, (pair + 1) * 128)
        for ref, place in ((wk_ref, wide), (wv_ref, wide + narrow)):
            turned = ref[:, span].astype(F32).T.astype(BF16)
            out_ref[2 * pair, place : place + narrow] = turned[:narrow]
            out_ref[2 * pair + 1, place : place + narrow] = turned[narrow:]


def pack_weights(wq, wk, wv, router, one, two, qg, kg):
    columns = (wq.shape[1] + wk.shape[1] + wv.shape[1]) // 8
    return pl.pallas_call(
        pack_kernel,
        out_shape=shape((8, columns + router.shape[1] + 16, wq.shape[0]), BF16),
        in_specs=[VMEM] * 8,
        out_specs=VMEM,
        compiler_params=params(8),
        cost_estimate=cost(2.5),
        name="pack_weights",
    )(wq, wk, wv, router, one, two, qg, kg)


def head_forward(pre, gain, cosine, sine):
    scale = lax.rsqrt(jnp.mean(pre * pre, axis=0, keepdims=True) + EPSILON)
    normed = pre * scale
    scaled = normed * gain
    a, b = scaled[: HEAD // 2], scaled[HEAD // 2 :]
    turned = jnp.concatenate([a * cosine - b * sine, b * cosine + a * sine], axis=0)
    return turned, normed, scale


def forward_kernel(me_ref, *refs, experts, q_heads):
    xs = refs[:8]
    arrived_ref, cos_ref, sin_ref, start_ref = refs[8:12]
    h1_ref, pre_ref, out_ref, inverse_ref, gains_ref, heads_ref, turned_ref = refs[-7:]
    rows = xs[0].shape[0]
    q_columns = q_heads * HEAD
    columns = q_columns + 2 * HEAD
    total = rows * 8
    for source in range(8):
        span = slice(source * rows, (source + 1) * rows)
        turned_ref[:, span] = arrived_ref[source, :columns]
        small = arrived_ref[source, columns:].astype(F32)
        gains_ref[:, span] = small[: experts + 8]
        heads_ref[source * 8 : (source + 1) * 8] = small[experts + 8 :]
    gain_one = gains_ref[experts : experts + 1]
    me = me_ref[0]
    for slot in range(8):
        x = xs[slot][...].astype(F32)
        scale = lax.rsqrt(jnp.mean(x * x, axis=1, keepdims=True) + EPSILON)
        h1_ref[slot] = (x * scale * gain_one).astype(BF16)
    for slot in range(8):
        block = dot(turned_ref[...], h1_ref[slot], ((1,), (1,)))
        place = pl.multiple_of((me ^ slot) * rows, rows)
        pre_ref[:, pl.ds(place, rows)] = block
    cosine, sine = cos_ref[...], sin_ref[...]
    gain_query, gain_key = heads_ref[:, :1], heads_ref[:, 1:2]
    key = head_forward(pre_ref[q_columns : q_columns + HEAD], gain_key, cosine, sine)[0]
    key = key.T.astype(BF16)
    value = pre_ref[q_columns + HEAD :].astype(BF16)
    inverse_ref[...] = jnp.zeros(inverse_ref.shape, F32)
    for head in range(q_heads):
        query = head_forward(pre_ref[head * HEAD : (head + 1) * HEAD], gain_query, cosine, sine)[0]
        query = query.astype(BF16) * jnp.array(HEAD ** (-0.5), BF16)
        for tile in range(total // TILE):
            low, high = tile * TILE, (tile + 1) * TILE
            scores = dot(key[:high], query[:, low:high])
            u = lax.broadcasted_iota(jnp.int32, (high, TILE), 0)
            t = lax.broadcasted_iota(jnp.int32, (high, TILE), 1) + low
            allowed = (u >= start_ref[:, low:high]) & (u <= t)
            powers = jnp.where(allowed, jnp.exp(scores), 0.0)
            inverse = 1.0 / jnp.sum(powers, axis=0, keepdims=True)
            probs = (powers * inverse).astype(BF16)
            mixed = dot(value[:, :high], probs).astype(BF16)
            inverse_ref[head : head + 1, low:high] = inverse
            for part in range(TILE // rows):
                out_ref[low // rows + part, head * HEAD : (head + 1) * HEAD] = mixed[
                    :, part * rows : (part + 1) * rows
                ]


def attention_forward(me, xs, arrived, cosine, sine, start, experts, q_heads, after=()):
    rows, width = xs[0].shape
    total = 8 * rows
    columns = (q_heads + 2) * HEAD
    return pl.pallas_call(
        functools.partial(forward_kernel, experts=experts, q_heads=q_heads),
        out_shape=(
            shape((8, rows, width), BF16),
            shape((columns, total), F32),
            shape((8, q_heads * HEAD, rows), BF16),
            shape((8, total), F32),
            shape((experts + 8, width), F32),
            shape((HEAD, 128), F32),
            shape((columns, width), BF16),
        ),
        in_specs=[SMEM] + [VMEM] * 12 + [ANY] * len(after),
        out_specs=[VMEM] * 7,
        compiler_params=params(18),
        cost_estimate=cost(8.5),
        name="attention_forward",
    )(me, *xs, arrived, cosine, sine, start, *after)


def head_backward(grad, normed, scale, gain, cosine, sine):
    a, b = grad[: HEAD // 2], grad[HEAD // 2 :]
    unturned = jnp.concatenate([a * cosine + b * sine, b * cosine - a * sine], axis=0)
    gain_grad = jnp.sum(unturned * normed, axis=1, keepdims=True)
    inner = unturned * gain
    pre_grad = scale * (inner - normed * jnp.mean(inner * normed, axis=0, keepdims=True))
    return pre_grad, gain_grad


def backward_kernel(me_ref, *refs, experts, q_heads):
    das = refs[:8]
    heads_ref, wo_ref, cos_ref, sin_ref, start_ref = refs[8:13]
    h1_ref, pre_ref, out_ref, inverse_ref, turned_ref, extra_ref = refs[13:19]
    first_ref, wo_grad_ref, keep_ref, send_ref = refs[-10:-6]
    da_ref, mixed_grad_ref, dkey_ref, dvalue_ref, low_ref, out_slots_ref = refs[-6:]
    rows, width = das[0].shape
    q_columns = q_heads * HEAD
    columns = q_columns + 2 * HEAD
    total = rows * 8
    me = me_ref[0]
    for slot in range(8):
        da_ref[slot * rows : (slot + 1) * rows] = das[slot][...]
    for slot in range(8):
        block = me ^ slot
        place = pl.multiple_of(block * rows, rows)
        back = dot(wo_ref[...], das[slot][...], ((1,), (1,)))
        mixed_grad_ref[:, pl.ds(place, rows)] = back.astype(BF16)
        out_slots_ref[:, slot * rows : (slot + 1) * rows] = out_ref[block]
    wo_grad = dot(out_slots_ref[...], da_ref[...]).astype(BF16)
    for part in range(8):
        wo_grad_ref[part] = wo_grad[:, part * rows : (part + 1) * rows]

    gain_query, gain_key = heads_ref[:, :1], heads_ref[:, 1:2]
    cosine, sine = cos_ref[...], sin_ref[...]
    key_turned, key_normed, key_scale = head_forward(
        pre_ref[q_columns : q_columns + HEAD], gain_key, cosine, sine
    )
    key_low = key_turned.astype(BF16)
    key = key_turned.T.astype(BF16)
    value = pre_ref[q_columns + HEAD :].T.astype(BF16)
    dkey_ref[...] = jnp.zeros(dkey_ref.shape, F32)
    dvalue_ref[...] = jnp.zeros(dvalue_ref.shape, F32)
    gain_query_grad = jnp.zeros((HEAD, 1), F32)
    pieces = []
    for head in range(q_heads):
        span = slice(head * HEAD, (head + 1) * HEAD)
        turned, normed, scale = head_forward(pre_ref[span], gain_query, cosine, sine)
        query = turned.astype(BF16) * jnp.array(HEAD ** (-0.5), BF16)
        grads = []
        for tile in range(total // TILE):
            low, high = tile * TILE, (tile + 1) * TILE
            part = query[:, low:high]
            mixed_grad = mixed_grad_ref[span, low:high]
            scores = dot(key[:high], part)
            u = lax.broadcasted_iota(jnp.int32, (high, TILE), 0)
            t = lax.broadcasted_iota(jnp.int32, (high, TILE), 1) + low
            allowed = (u >= start_ref[:, low:high]) & (u <= t)
            probs = jnp.where(allowed, jnp.exp(scores) * inverse_ref[head : head + 1, low:high], 0.0)
            attend = dot(value[:high], mixed_grad)
            delta = jnp.sum(probs * attend, axis=0, keepdims=True)
            score_low = (probs * (attend - delta)).astype(BF16)
            grads.append(dot(key_low[:, :high], score_low))
            dkey_ref[:, :high] += dot(part, score_low, ((1,), (1,)))
            dvalue_ref[:, :high] += dot(mixed_grad, probs.astype(BF16), ((1,), (1,)))
        query_grad = jnp.concatenate(grads, axis=1) * HEAD ** (-0.5)
        pre_grad, gain_grad = head_backward(query_grad, normed, scale, gain_query, cosine, sine)
        gain_query_grad += gain_grad
        pieces.append(pre_grad)
    pre_grad, gain_key_grad = head_backward(
        dkey_ref[...], key_normed, key_scale, gain_key, cosine, sine
    )
    pieces += [pre_grad, dvalue_ref[...]]
    pre_grad = jnp.concatenate(pieces, axis=0)
    low_ref[...] = pre_grad.astype(BF16)
    low_rows = pre_grad.T.astype(BF16)
    slots_grad = []
    for slot in range(8):
        place = pl.multiple_of((me ^ slot) * rows, rows)
        slots_grad.append(low_ref[:, pl.ds(place, rows)])
    slots_grad = jnp.concatenate(slots_grad, axis=1)
    weights_grad = dot(slots_grad, h1_ref[...].reshape(total, width)).astype(BF16)
    extra = extra_ref[...]
    lane = lax.broadcasted_iota(jnp.int32, (HEAD, 128), 1)
    gains = jnp.where(lane == 0, gain_query_grad, jnp.where(lane == 1, gain_key_grad, 0.0))
    gains = gains.T[:2]
    step = HEAD // 8
    for part in range(8):
        span = slice(part * rows, (part + 1) * rows)
        first_ref[part, :columns] = weights_grad[:, span]
        mine = jnp.concatenate([gains[:, part * step : (part + 1) * step], jnp.zeros((2, rows - step), F32)], axis=1)
        whole = jnp.concatenate([extra[: experts + 1, span], mine, jnp.zeros((64 - experts - 3, rows), F32)], axis=0)
        first_ref[part, columns:] = whole.astype(BF16)
    turned = turned_ref[...]
    for slot in range(8):
        place = pl.multiple_of((me ^ slot) * rows, rows)
        low_rows_slot = slots_grad[:, slot * rows : (slot + 1) * rows].astype(F32).T.astype(BF16)
        part = dot(low_rows_slot, turned)
        if slot % 2 == 0:
            keep_ref[slot // 2] = part
        else:
            send_ref[slot // 2] = part.astype(BF16)


def attention_backward(
    me, das, heads, wo, cosine, sine, start, h1, pre, out, inverse, turned, extra, experts, q_heads, after=()
):
    rows, width = das[0].shape
    total = 8 * rows
    columns = pre.shape[0]
    q_columns = q_heads * HEAD
    return pl.pallas_call(
        functools.partial(backward_kernel, experts=experts, q_heads=q_heads),
        out_shape=(
            shape((8, columns + 64, rows), BF16),
            shape((8, q_columns, rows), BF16),
            shape((4, rows, width), F32),
            shape((4, rows, width), BF16),
        ),
        in_specs=[SMEM] + [VMEM] * 19 + [ANY] * len(after),
        out_specs=[VMEM] * 4,
        scratch_shapes=[
            pltpu.VMEM((total, width), BF16),
            pltpu.VMEM((q_columns, total), BF16),
            pltpu.VMEM((HEAD, total), F32),
            pltpu.VMEM((HEAD, total), F32),
            pltpu.VMEM((columns, total), BF16),
            pltpu.VMEM((q_columns, total), BF16),
        ],
        compiler_params=params(28),
        cost_estimate=cost(13),
        name="attention_backward",
    )(me, *das, heads, wo, cosine, sine, start, h1, pre, out, inverse, turned, extra, *after)


def middle_kernel(o_ref, wo_ref, x_ref, gains_ref, *refs, experts):
    middle_ref, low_ref, high_ref, probs_ref = refs[-4:]
    rows, width = x_ref.shape
    mixed = o_ref[...].reshape(-1, rows).astype(F32).T.astype(BF16)
    middle = x_ref[...].astype(F32) + dot(mixed, wo_ref[...])
    middle_ref[...] = middle
    scale = lax.rsqrt(jnp.mean(middle * middle, axis=1, keepdims=True) + EPSILON)
    hidden = (middle * scale * gains_ref[experts + 1 : experts + 2]).astype(BF16)
    low_ref[...] = hidden[: rows // 2]
    high_ref[...] = hidden[rows // 2 :]
    probs_ref[...] = softmax_rows(dot(gains_ref[:experts].astype(BF16), hidden, ((1,), (1,))))


def softmax_rows(logits):
    powers = jnp.exp(logits - jnp.max(logits, axis=0, keepdims=True))
    return powers / jnp.sum(powers, axis=0, keepdims=True)


def middle_layer(o, wo, x, gains, experts, after=()):
    rows, width = x.shape
    return pl.pallas_call(
        functools.partial(middle_kernel, experts=experts),
        out_shape=(
            shape((rows, width), F32),
            shape((rows // 2, width), BF16),
            shape((rows // 2, width), BF16),
            shape((experts, rows), F32),
        ),
        in_specs=[VMEM] * 4 + [ANY] * len(after),
        out_specs=[VMEM] * 4,
        compiler_params=params(10),
        cost_estimate=cost(3),
        name="middle_layer",
    )(o, wo, x, gains, *after)


def expert_kernel(owner_ref, *refs, experts, capacity):
    sources, targets, scratch = refs[:20], refs[20:36], refs[36:]
    gains_ref, heavy = sources[16], sources[17:20]
    h_low, h_high, c_low, c_high = (scratch[i : i + 4] for i in (0, 4, 8, 12))
    gate_ref, up_ref, down_ref = scratch[16:19]
    p_low, p_high = scratch[19:23], scratch[23:27]
    rows_h, rows_c, gate_out, up_out, active_out, weighted_out, turn_ref, share_ref = scratch[27:35]
    back_ref, sems, out_sems = scratch[35:]
    loads = [
        pltpu.make_async_copy(source, target, sems.at[i])
        for i, (source, target) in enumerate(zip(sources[:16] + heavy, scratch[:19]))
    ]
    order = [0, 4, 8, 12, 5, 13, 6, 14, 7, 15, 1, 9, 2, 10, 3, 11, 16, 17, 18]
    for i in order:
        loads[i].start()
    stores = [
        pltpu.make_async_copy(source, target, out_sems.at[i])
        for i, (source, target) in enumerate(zip(scratch[19:35], targets))
    ]
    per_owner, width = gate_ref.shape[:2]
    rows = 2 * h_low[0].shape[1]
    owner = owner_ref[0]
    router = gains_ref[:experts].astype(BF16)
    lanes = lax.broadcasted_iota(jnp.int32, (experts, 128), 1)
    subs = lax.broadcasted_iota(jnp.int32, (experts, 128), 0)
    eye = (lanes == subs).astype(BF16)
    before = (
        lax.broadcasted_iota(jnp.int32, (rows, rows), 0)
        <= lax.broadcasted_iota(jnp.int32, (rows, rows), 1)
    ).astype(BF16)
    mine_of = lax.broadcasted_iota(jnp.int32, (experts, rows), 0) - owner * per_owner
    slot = lax.broadcasted_iota(jnp.int32, (capacity, rows), 0).astype(F32) + 1.0
    for block in range(16):
        y, x = block // 4, block % 4
        if x == 0:
            loads[y].wait()
            loads[8 + y].wait()
        if y == 0:
            loads[4 + x].wait()
            loads[12 + x].wait()
        h = jnp.concatenate([h_low[y][x], h_high[x][y]], axis=0)
        c = jnp.concatenate([c_low[y][x], c_high[x][y]], axis=0)
        mask = dot(eye, c[:, width:], ((1,), (1,)))
        ranks = dot(mask.astype(BF16), before)
        probs = softmax_rows(dot(router, h, ((1,), (1,)))) * mask
        share = probs / jnp.sum(probs, axis=0, keepdims=True)
        deals = []
        span = slice(block * capacity, (block + 1) * capacity)
        for k in range(per_owner):
            mine = mine_of == k
            hit = jnp.sum(jnp.where(mine, mask, 0.0), axis=0, keepdims=True)
            rank = jnp.sum(jnp.where(mine, ranks, 0.0), axis=0, keepdims=True)
            part = jnp.sum(jnp.where(mine, share, 0.0), axis=0, keepdims=True)
            deal = jnp.where((rank == slot) & (hit > 0.5), 1.0, 0.0)
            deals.append(deal)
            column = jnp.sum(deal * part, axis=1, keepdims=True)
            share_ref[k, span] = jnp.broadcast_to(column, (capacity, 128))
        deal = jnp.concatenate(deals, axis=0)
        padded = jnp.concatenate([deal, jnp.zeros((128 - deal.shape[0], rows), F32)], axis=0)
        turn_ref[block] = padded.T.astype(BF16)
        deal = deal.astype(BF16)
        taken_h = dot(deal, h).astype(BF16)
        taken_c = dot(deal, c[:, :width]).astype(BF16)
        for k in range(per_owner):
            rows_h[k, span] = taken_h[k * capacity : (k + 1) * capacity]
            rows_c[k, span] = taken_c[k * capacity : (k + 1) * capacity]
    for i in (8, 9, 14, 15):
        stores[i].start()
    for i in (16, 17, 18):
        loads[i].wait()
    lane = lax.broadcasted_iota(jnp.int32, (TILE, 128), 1)
    for k in range(per_owner):
        for tile in range(16 * capacity // TILE):
            span = slice(tile * TILE, (tile + 1) * TILE)
            gate = dot(rows_h[k, span], gate_ref[k])
            up = dot(rows_h[k, span], up_ref[k])
            back = dot(rows_c[k, span], down_ref[k], ((1,), (1,)))
            sig = 1.0 / (1.0 + jnp.exp(-gate))
            silu = gate * sig
            active = silu * up
            active_low = active.astype(BF16)
            share = share_ref[k, span, :1]
            route_grad = jnp.sum(active_low.astype(F32) * back, axis=1, keepdims=True)
            grad = back * share
            gate_low = (grad * up * (sig + silu * (1.0 - sig))).astype(BF16)
            up_low = (grad * silu).astype(BF16)
            active_out[k, span] = active_low
            weighted_out[k, span] = (active * share).astype(BF16)
            gate_out[k, span] = gate_low
            up_out[k, span] = up_low
            total = dot(gate_low, gate_ref[k], ((1,), (1,))) + dot(up_low, up_ref[k], ((1,), (1,)))
            back_ref[k, span, :width] = total.astype(BF16)
            high = route_grad.astype(BF16).astype(F32)
            place = owner * per_owner + k
            spread = jnp.where(lane == place, high, 0.0)
            spread = jnp.where(lane == place + experts, route_grad - high, spread)
            back_ref[k, span, width:] = spread.astype(BF16)
    for i in (10, 11, 12, 13):
        stores[i].start()
    for block in range(16):
        y, x = block // 4, block % 4
        span = slice(block * capacity, (block + 1) * capacity)
        both = jnp.concatenate([back_ref[k, span] for k in range(per_owner)], axis=0)
        total = dot(turn_ref[block][:, : both.shape[0]], both).astype(BF16)
        p_low[y][x] = total[: rows // 2]
        p_high[x][y] = total[rows // 2 :]
        if x == 3:
            stores[y].start()
        if y == 3:
            stores[4 + x].start()
    for store in stores:
        store.wait()


def expert_layer(owner, h_low, h_high, c_low, c_high, gains, gate, up, down, experts, capacity):
    per_owner, width, hidden = gate.shape
    half = h_low[0].shape[1]
    count = 16 * capacity
    piece = ((4, half, width + 128), BF16)
    wide = ((per_owner, count, width), BF16)
    narrow = ((per_owner, count, hidden), BF16)
    results = [piece] * 8 + [wide] * 2 + [narrow] * 4
    results += [((16, 2 * half, 128), BF16), ((per_owner, count, 128), F32)]
    operands = [*h_low, *h_high, *c_low, *c_high, gains, gate, up, down]
    held = [(value.shape, BF16) for i, value in enumerate(operands) if i != 16]
    held += results + [((per_owner, count, width + 128), BF16)]
    return pl.pallas_call(
        functools.partial(expert_kernel, experts=experts, capacity=capacity),
        out_shape=[shape(*result) for result in results],
        in_specs=[SMEM] + [ANY] * 16 + [VMEM] + [ANY] * 3,
        out_specs=[ANY] * 16,
        scratch_shapes=[pltpu.VMEM(*item) for item in held]
        + [pltpu.SemaphoreType.DMA((19,)), pltpu.SemaphoreType.DMA((16,))],
        compiler_params=params(44),
        cost_estimate=cost(18),
        name="expert_layer",
    )(owner, *operands)


def weights_kernel(rows_h, rows_c, gate_low, up_low, weighted, gate_grad, up_grad, down_grad):
    first = ((0,), (0,))
    for k in range(rows_h.shape[0]):
        gate_grad[k] = dot(rows_h[k], gate_low[k], first).astype(BF16)
        up_grad[k] = dot(rows_h[k], up_low[k], first).astype(BF16)
        down_grad[k] = dot(weighted[k], rows_c[k], first).astype(BF16)


def expert_weights(rows_h, rows_c, gate_low, up_low, weighted):
    per_owner, count, width = rows_h.shape
    hidden = gate_low.shape[2]
    return pl.pallas_call(
        weights_kernel,
        out_shape=[
            shape((per_owner, width, hidden), BF16),
            shape((per_owner, width, hidden), BF16),
            shape((per_owner, hidden, width), BF16),
        ],
        in_specs=[VMEM] * 5,
        out_specs=[VMEM] * 3,
        compiler_params=params(26),
        cost_estimate=cost(11),
        name="expert_weights",
    )(rows_h, rows_c, gate_low, up_low, weighted)


def outputs_kernel(active, deal, share, down_ref, *refs, capacity):
    p_low, p_high = refs[-9:-5], refs[-5:-1]
    out_ref = refs[-1]
    per_owner, count, hidden = active.shape
    half = deal.shape[1] // 2
    for k in range(per_owner):
        for tile in range(count // TILE):
            span = slice(tile * TILE, (tile + 1) * TILE)
            produced = dot(active[k, span], down_ref[k]).astype(BF16).astype(F32)
            out_ref[k, span] = (produced * share[k, span, :1]).astype(BF16)
    for block in range(16):
        y, x = block // 4, block % 4
        span = slice(block * capacity, (block + 1) * capacity)
        both = jnp.concatenate([out_ref[k, span] for k in range(per_owner)], axis=0)
        total = dot(deal[block][:, : both.shape[0]], both).astype(BF16)
        p_low[y][x] = total[:half]
        p_high[x][y] = total[half:]


def expert_outputs(active, deal, share, down, capacity, after=()):
    per_owner, count, hidden = active.shape
    width = down.shape[2]
    half = deal.shape[1] // 2
    return pl.pallas_call(
        functools.partial(outputs_kernel, capacity=capacity),
        out_shape=[shape((4, half, width), BF16)] * 8,
        in_specs=[VMEM] * 4 + [ANY] * len(after),
        out_specs=[VMEM] * 8,
        scratch_shapes=[pltpu.VMEM((per_owner, count, width), BF16)],
        compiler_params=params(18),
        cost_estimate=cost(7),
        name="expert_outputs",
    )(active, deal, share, down, *after)


def fold_kernel(*refs):
    low, high = refs[:4], refs[4:8]
    outs = refs[-8:]
    for part in range(4):
        for pieces, out in ((low, outs[part]), (high, outs[4 + part])):
            total = pieces[0][part].astype(F32)
            for piece in pieces[1:]:
                total = total + piece[part].astype(F32)
            out[...] = total.astype(out.dtype)


def fold(low, high, after=()):
    half, width = low[0].shape[1:]
    kinds = [F32, BF16, BF16, BF16] * 2
    return pl.pallas_call(
        fold_kernel,
        out_shape=[shape((half, width), kind) for kind in kinds],
        in_specs=[VMEM] * 8 + [ANY] * len(after),
        out_specs=[VMEM] * 8,
        compiler_params=params(10),
        cost_estimate=cost(3),
        name="fold",
    )(*low, *high, *after)


def joined(low, high):
    sums = []
    for pieces in (low, high):
        total = pieces[0][...]
        for piece in pieces[1:]:
            total = total + piece[...].astype(F32)
        sums.append(total)
    return jnp.concatenate(sums, axis=0)


def output_kernel(*refs):
    middle_ref, out_ref = refs[8:]
    out_ref[...] = (middle_ref[...] + joined(refs[:4], refs[4:8])).astype(BF16)


def layer_output(low, high, middle):
    return pl.pallas_call(
        output_kernel,
        out_shape=shape(middle.shape, BF16),
        in_specs=[VMEM] * 9,
        out_specs=VMEM,
        compiler_params=params(6),
        cost_estimate=cost(2.4),
        name="layer_output",
    )(*low, *high, middle)


def router_kernel(*refs, experts):
    middle_ref, probs_ref, routed_ref, gains_ref, c_ref, h_low, h_high = refs[8:15]
    grad_ref, send_ref, extra_ref = refs[15:]
    width = middle_ref.shape[1]
    rows = middle_ref.shape[0]
    returned = joined(refs[:4], refs[4:8])
    tail = returned[:, width:].T
    route_grad = tail[:experts] + tail[experts : 2 * experts]
    lanes = lax.broadcasted_iota(jnp.int32, (experts, 128), 1)
    subs = lax.broadcasted_iota(jnp.int32, (experts, 128), 0)
    mask = dot((lanes == subs).astype(BF16), routed_ref[...], ((1,), (1,)))
    probs = probs_ref[...]
    picked = probs * mask
    picked_sum = jnp.sum(picked, axis=0, keepdims=True)
    share = picked / picked_sum
    picked_grad = (route_grad - jnp.sum(route_grad * share, axis=0, keepdims=True)) / picked_sum
    prob_grad = mask * picked_grad
    logit_grad = probs * (prob_grad - jnp.sum(probs * prob_grad, axis=0, keepdims=True))
    logit_low = logit_grad.astype(BF16)
    hidden = jnp.concatenate([h_low[...], h_high[...]], axis=0)
    extra_ref[:experts] = dot(logit_low, hidden)
    logit_rows = jnp.concatenate([logit_grad, jnp.zeros((128 - experts, rows), F32)], axis=0).T
    router = gains_ref[:experts].astype(BF16)
    hidden_grad = returned[:, :width] + dot(logit_rows[:, :experts].astype(BF16), router)
    middle = middle_ref[...]
    scale = lax.rsqrt(jnp.mean(middle * middle, axis=1, keepdims=True) + EPSILON)
    normed = middle * scale
    extra_ref[experts : experts + 8] = jnp.broadcast_to(
        jnp.sum(hidden_grad * normed, axis=0, keepdims=True), (8, width)
    )
    inner = hidden_grad * gains_ref[experts + 1 : experts + 2]
    grad = c_ref[...].astype(F32) + scale * (
        inner - normed * jnp.mean(inner * normed, axis=1, keepdims=True)
    )
    grad_ref[...] = grad
    send_ref[...] = grad.astype(BF16)


def router_backward(low, high, middle, probs, routed, gains, c, h_low, h_high, experts):
    rows, width = middle.shape
    return pl.pallas_call(
        functools.partial(router_kernel, experts=experts),
        out_shape=(
            shape((rows, width), F32),
            shape((rows, width), BF16),
            shape((experts + 8, width), F32),
        ),
        in_specs=[VMEM] * 15,
        out_specs=[VMEM] * 3,
        compiler_params=params(10),
        cost_estimate=cost(3.5),
        name="router_backward",
    )(*low, *high, middle, probs, routed, gains, c, h_low, h_high)


def pair_kernel(keep_ref, came_ref, *outs):
    for part in range(4):
        total = keep_ref[part] + came_ref[part].astype(F32)
        outs[part][...] = total.astype(outs[part].dtype)


def pair_sum(keep, came):
    rows, width = keep.shape[1:]
    return pl.pallas_call(
        pair_kernel,
        out_shape=[shape((rows, width), kind) for kind in (F32, BF16, BF16, BF16)],
        in_specs=[VMEM] * 2,
        out_specs=[VMEM] * 4,
        compiler_params=params(8),
        cost_estimate=cost(2.5),
        name="pair_sum",
    )(keep, came)


def input_kernel(p0, p1, p2, p3, x_ref, gains_ref, middle_grad_ref, out_ref, *, experts):
    total = p0[...] + p1[...].astype(F32) + p2[...].astype(F32) + p3[...].astype(F32)
    x = x_ref[...].astype(F32)
    scale = lax.rsqrt(jnp.mean(x * x, axis=1, keepdims=True) + EPSILON)
    normed = x * scale
    inner = total * gains_ref[experts : experts + 1]
    out_ref[...] = middle_grad_ref[...] + scale * (
        inner - normed * jnp.mean(inner * normed, axis=1, keepdims=True)
    )


def input_grad(parts, x, gains, middle_grad, experts):
    return pl.pallas_call(
        functools.partial(input_kernel, experts=experts),
        out_shape=shape(middle_grad.shape, F32),
        in_specs=[VMEM] * 7,
        out_specs=VMEM,
        compiler_params=params(8),
        cost_estimate=cost(2.5),
        name="input_grad",
    )(*parts, x, gains, middle_grad)


def sum_kernel(in_ref, out_ref):
    total = in_ref[0].astype(F32)
    for i in range(1, in_ref.shape[0]):
        total = total + in_ref[i].astype(F32)
    total = total.astype(BF16)
    for i in range(in_ref.shape[0]):
        out_ref[i] = total


def sum_all(pieces):
    return pl.pallas_call(
        sum_kernel,
        out_shape=shape(pieces.shape, BF16),
        in_specs=[VMEM],
        out_specs=VMEM,
        compiler_params=params(8),
        cost_estimate=cost(2),
        name="sum_all",
    )(pieces)


def final_kernel(third_ref, wq_ref, wk_ref, wv_ref, gain_ref, *refs, experts, columns):
    outs = refs[-8:]
    query_ref, key_ref, value_ref, output_ref, one_ref, two_ref, gains_ref, router_ref = outs
    rows = third_ref.shape[2]
    tall = (columns + 64) // 2
    q_columns = query_ref.shape[1] // 8
    kv_columns = key_ref.shape[1] // 8
    extra = jnp.zeros((64, rows), F32)
    sums = jnp.zeros((rows, 1), F32)
    for source in range(8):
        block = jnp.concatenate(
            [third_ref[2 * source, :tall], third_ref[2 * source + 1, :tall]], axis=0
        ).astype(F32)
        turned = block[:columns].T
        query = turned[:, :q_columns]
        key = turned[:, q_columns : q_columns + kv_columns]
        value = turned[:, q_columns + kv_columns :]
        q_span = slice(source * q_columns, (source + 1) * q_columns)
        kv_span = slice(source * kv_columns, (source + 1) * kv_columns)
        query_ref[:, q_span] = query
        key_ref[:, kv_span] = key
        value_ref[:, kv_span] = value
        sums = sums + jnp.sum(query * wq_ref[:, q_span].astype(F32), axis=1, keepdims=True)
        sums = sums + jnp.sum(key * wk_ref[:, kv_span].astype(F32), axis=1, keepdims=True)
        sums = sums + jnp.sum(value * wv_ref[:, kv_span].astype(F32), axis=1, keepdims=True)
        extra = extra + block[columns:]
        for half in range(2):
            size = rows // 2
            output_ref[half * size : (half + 1) * size, source * rows : (source + 1) * rows] = (
                third_ref[2 * source + half, tall:].astype(F32)
            )
    one_ref[...] = jnp.broadcast_to(sums, (rows, 128)).T[:1] / gain_ref[...].astype(F32)
    two_ref[...] = extra[experts : experts + 1]
    gains_ref[...] = extra[experts + 1 : experts + 3]
    router_ref[...] = jnp.concatenate([extra, jnp.zeros((64, rows), F32)], axis=0).T[:, :experts]


def final_grads(third, wq, wk, wv, gain, experts, columns, after=()):
    rows = third.shape[2]
    return pl.pallas_call(
        functools.partial(final_kernel, experts=experts, columns=columns),
        out_shape=(
            shape(wq.shape, F32),
            shape(wk.shape, F32),
            shape(wv.shape, F32),
            shape((rows, 8 * rows), F32),
            shape((1, rows), F32),
            shape((1, rows), F32),
            shape((2, rows), F32),
            shape((rows, experts), F32),
        ),
        in_specs=[VMEM] * 5 + [ANY] * len(after),
        out_specs=[VMEM] * 8,
        compiler_params=params(10),
        cost_estimate=cost(5),
        name="final_grads",
    )(third, wq, wk, wv, gain, *after)


def send(values, axis, flip):
    count = lax.axis_size(axis)
    return lax.ppermute(values, axis, [(i, i ^ flip) for i in range(count)])


def gather_fsdp(block):
    same = {0: block}
    for step in Z_STEPS:
        same[step] = send(block, "fsdp", step)
    slots = []
    for step in (0, 2, 4, 6):
        slots += [same[step], send(same[step], "fsdp", CORE)]
    return slots


def gather_expert(low, high):
    low_x = {s: send(low, "expert", s) for s in X_STEPS}
    high_y = {s: send(high, "expert", s) for s in Y_STEPS}
    low_x = jnp.concatenate([v[None] for v in (low, low_x[1], low_x[2], low_x[3])], axis=0)
    high_y = jnp.concatenate([v[None] for v in (high, high_y[4], high_y[8], high_y[12])], axis=0)
    low_xy = {s: send(low_x, "expert", s) for s in Y_STEPS}
    high_yx = {s: send(high_y, "expert", s) for s in X_STEPS}
    return (
        [low_x, low_xy[4], low_xy[8], low_xy[12]],
        [high_y, high_yx[1], high_yx[2], high_yx[3]],
    )


def first_scatter(low, high):
    low = [low[0]] + [send(low[i], "expert", 4 * i) for i in (1, 2, 3)]
    high = [high[0]] + [send(high[i], "expert", i) for i in (1, 2, 3)]
    return low, high


def second_scatter(low, high, after=()):
    parts = fold(low, high, after)
    low = [parts[0]] + [send(parts[i], "expert", i) for i in (1, 2, 3)]
    high = [parts[4]] + [send(parts[4 + i], "expert", 4 * i) for i in (1, 2, 3)]
    return low, high


def scatter_expert(low, high, after=()):
    return second_scatter(*first_scatter(low, high), after)


def shards(
    tokens,
    lengths,
    routes,
    first_gain,
    query_weight,
    key_weight,
    value_weight,
    output_weight,
    query_gain,
    key_gain,
    second_gain,
    router_weight,
    gate_weight,
    up_weight,
    down_weight,
    cotangent,
):
    own = tokens[0]
    upstream = cotangent[0]
    rows, width = own.shape
    fsdp = lax.axis_size("fsdp")
    owners = lax.axis_size("expert")
    me = lax.axis_index("fsdp").astype(jnp.int32).reshape(1)
    owner = lax.axis_index("expert").astype(jnp.int32).reshape(1)
    experts = router_weight.shape[1]
    capacity = 3 * rows * routes.shape[2] // (2 * experts)
    kv_columns = key_weight.shape[1] // fsdp
    q_columns = query_weight.shape[1] // fsdp
    columns = q_columns + 2 * kv_columns
    q_heads = q_columns // HEAD

    xs = gather_fsdp(own)
    outgoing = pack_weights(
        query_weight,
        key_weight,
        value_weight,
        router_weight,
        first_gain[None],
        second_gain[None],
        query_gain[None],
        key_gain[None],
    )
    arrived = lax.all_to_all(outgoing, "fsdp", 0, 0, tiled=True)
    whole_output = lax.all_gather(output_weight, "fsdp", axis=0, tiled=True)
    routed = jnp.sum(
        (routes[0][:, :, None] == jnp.arange(128, dtype=jnp.int32)).astype(F32), axis=1
    ).astype(BF16)
    dressed = jnp.concatenate([upstream, routed], axis=1)
    c_low, c_high = gather_expert(dressed[: rows // 2], dressed[rows // 2 :])

    ends = jnp.cumsum(lengths[0])
    place = jnp.arange(rows * fsdp, dtype=jnp.int32)
    start = jnp.max(jnp.where(ends[:, None] <= place[None, :], ends[:, None], 0), axis=0)
    position = (place - start).astype(F32)
    frequency = ROPE_BASE ** (-jnp.arange(HEAD // 2, dtype=F32) * 2.0 / HEAD)
    angles = frequency[:, None] * position[None, :]
    cosine, sine = jnp.cos(angles), jnp.sin(angles)
    start = start[None, :].astype(jnp.int32)

    h1, pre, mixed, inverse, gains, heads, turned = attention_forward(
        me, xs, arrived, cosine, sine, start, experts, q_heads, after=(c_low[0], c_high[0])
    )
    mixed_own = lax.all_to_all(mixed, "fsdp", 0, 0, tiled=True)
    middle, own_low, own_high, probs = middle_layer(
        mixed_own, whole_output, own, gains, experts, after=c_low[1:] + c_high[1:]
    )
    h_low, h_high = gather_expert(own_low, own_high)
    made = expert_layer(
        owner, h_low, h_high, c_low, c_high, gains, gate_weight, up_weight, down_weight, experts, capacity
    )
    rows_h, rows_c, gate_low, up_low, active, weighted, deal, share = made[8:]
    grads = expert_weights(rows_h, rows_c, gate_low, up_low, weighted)
    gate_sum, up_sum, down_sum = (lax.psum(grad, "fsdp").astype(F32) for grad in grads)
    back_low, back_high = scatter_expert(made[:4], made[4:8], after=(grads[0],))

    middle_grad, middle_low, extra = router_backward(
        back_low, back_high, middle, probs, routed, gains, upstream, own_low, own_high, experts
    )
    das = gather_fsdp(middle_low)
    outs = expert_outputs(active, deal, share, down_weight, capacity, after=(middle_low,))
    out_low, out_high = first_scatter(outs[:4], outs[4:])
    first, output_grad, keep, give = attention_backward(
        me,
        das,
        heads,
        output_weight,
        cosine,
        sine,
        start,
        h1,
        pre,
        mixed,
        inverse,
        turned,
        extra,
        experts,
        q_heads,
        after=out_low[1:] + out_high[1:],
    )
    out_low, out_high = second_scatter(out_low, out_high)
    came = send(give, "fsdp", CORE)
    parts = pair_sum(keep, came)
    parts = [parts[0]] + [send(parts[i], "fsdp", 2 * i) for i in (1, 2, 3)]
    first = lax.all_to_all(first, "fsdp", 0, 0, tiled=True)
    second = jnp.concatenate(
        [first.reshape(owners, -1, rows), output_grad.reshape(owners, -1, rows)], axis=1
    )
    second = sum_all(lax.all_to_all(second, "expert", 0, 0, tiled=True))
    third = lax.all_to_all(second, "expert", 0, 0, tiled=True)
    tokens_grad = input_grad(parts, own, gains, middle_grad, experts)
    layer_out = layer_output(out_low, out_high, middle)
    query_sum, key_sum, value_sum, output_sum, one_sum, two_sum, gain_sums, router_sum = final_grads(
        third,
        query_weight,
        key_weight,
        value_weight,
        first_gain[None],
        experts,
        columns,
        after=(gate_sum, up_sum, down_sum),
    )
    step = HEAD // fsdp
    return (
        layer_out[None],
        tokens_grad[None],
        one_sum[0],
        query_sum,
        key_sum,
        value_sum,
        output_sum,
        gain_sums[0, :step],
        gain_sums[1, :step],
        two_sum[0],
        router_sum,
        gate_sum,
        up_sum,
        down_sum,
    )


def solution(mesh):
    whole = P("expert", "fsdp", None)
    rows = P("fsdp", None)
    vector = P("fsdp")
    owned = P("expert", None, None)
    return jax.shard_map(
        shards,
        mesh=mesh,
        in_specs=(
            whole,
            P("expert", None),
            whole,
            vector,
            rows,
            rows,
            rows,
            rows,
            vector,
            vector,
            vector,
            rows,
            owned,
            owned,
            owned,
            whole,
        ),
        out_specs=(
            whole,
            whole,
            vector,
            rows,
            rows,
            rows,
            rows,
            vector,
            vector,
            vector,
            rows,
            owned,
            owned,
            owned,
        ),
        check_vma=False,
    )
```

```python
import functools

import jax
import jax.numpy as jnp
from jax import lax
from jax.experimental import pallas as pl
from jax.experimental.pallas import tpu as pltpu
from jax.sharding import PartitionSpec as P

EPSILON = 1e-06
ROPE_BASE = 10000.0
HEAD = 64
TILE = 256
F32 = jnp.float32
BF16 = jnp.bfloat16
VMEM = pl.BlockSpec(memory_space=pltpu.VMEM)
SMEM = pl.BlockSpec(memory_space=pltpu.SMEM)
ANY = pl.BlockSpec(memory_space=pl.ANY)
CUBE = (1, 4, 3, 12)


def dot(left, right, dims=((1,), (0,))):
    return lax.dot_general(left, right, (dims, ((), ())), preferred_element_type=F32)


def shape(extent, dtype):
    return jax.ShapeDtypeStruct(extent, dtype)


def kernel_call(body, name, mib, micros, operands, results, specs=None, after=(), scratch=(), out_specs=None):
    specs = specs or [VMEM] * len(operands)
    return pl.pallas_call(
        body,
        out_shape=[shape(*result) for result in results],
        in_specs=specs + [ANY] * len(after),
        out_specs=out_specs or [VMEM] * len(results),
        scratch_shapes=list(scratch),
        compiler_params=pltpu.CompilerParams(vmem_limit_bytes=mib * 1024 * 1024),
        cost_estimate=pl.CostEstimate(flops=0, bytes_accessed=int(micros * 3.6e6), transcendentals=0),
        name=name,
    )(*operands, *after)


def lane_blocks(value):
    return jnp.concatenate([value[:, i : i + 128] for i in range(0, value.shape[1], 128)], axis=0)


def joined_lanes(value, count):
    rows = value.shape[0] // count
    return jnp.concatenate([value[i * rows : (i + 1) * rows] for i in range(count)], axis=1)


def softmax_rows(logits):
    powers = jnp.exp(logits - jnp.max(logits, axis=0, keepdims=True))
    return powers / jnp.sum(powers, axis=0, keepdims=True)


def head_forward(pre, gain, cosine, sine):
    scale = lax.rsqrt(jnp.mean(pre * pre, axis=0, keepdims=True) + EPSILON)
    normed = pre * scale
    scaled = normed * gain
    a, b = scaled[: HEAD // 2], scaled[HEAD // 2 :]
    turned = jnp.concatenate([a * cosine - b * sine, b * cosine + a * sine], axis=0)
    return turned, normed, scale


def head_backward(grad, normed, scale, gain, cosine, sine):
    a, b = grad[: HEAD // 2], grad[HEAD // 2 :]
    unturned = jnp.concatenate([a * cosine + b * sine, b * cosine - a * sine], axis=0)
    gain_grad = jnp.sum(unturned * normed, axis=1, keepdims=True)
    inner = unturned * gain
    pre_grad = scale * (inner - normed * jnp.mean(inner * normed, axis=0, keepdims=True))
    return pre_grad, gain_grad


def pack_kernel(me_ref, x_ref, wq_ref, wk_ref, wv_ref, router_ref, one_ref, two_ref, qg_ref, kg_ref, *outs):
    own_ref, sends, parts_ref = outs[0], outs[1:4], outs[4]
    rows, experts = router_ref.shape
    wide = wq_ref.shape[1] // 8
    narrow = wk_ref.shape[1] // 8
    router = jnp.concatenate([router_ref[...].astype(F32), jnp.zeros((rows, 128 - experts), F32)], axis=1)
    count = qg_ref.shape[1]
    heads = jnp.concatenate([qg_ref[...], kg_ref[...]], axis=0).astype(F32)
    heads = jnp.concatenate([heads, jnp.zeros((2, 128 - count), F32)], axis=1)
    heads = jnp.concatenate([heads, jnp.zeros((126, 128), F32)], axis=0).T[:count]
    small = jnp.concatenate(
        [
            router.T[:experts],
            one_ref[...].astype(F32),
            two_ref[...].astype(F32),
            jnp.zeros((6, 128), F32),
            heads,
        ],
        axis=0,
    ).astype(BF16)
    for part in range(8):
        parts_ref[part, :wide] = wq_ref[:, part * wide : (part + 1) * wide].astype(F32).T.astype(BF16)
        parts_ref[part, wide + 2 * narrow :] = small
    for pair in range(4):
        span = slice(pair * 128, (pair + 1) * 128)
        for ref, place in ((wk_ref, wide), (wv_ref, wide + narrow)):
            turned = ref[:, span].astype(F32).T.astype(BF16)
            parts_ref[2 * pair, place : place + narrow] = turned[:narrow]
            parts_ref[2 * pair + 1, place : place + narrow] = turned[narrow:]
    me = me_ref[0]
    tall = parts_ref.shape[1]
    blocks = lane_blocks(x_ref[...])
    base = blocks.shape[0]
    own_ref[:tall] = parts_ref[me]
    own_ref[tall:] = parts_ref[me ^ 1]
    for flip in range(1, 4):
        sends[flip - 1][:base] = blocks
        sends[flip - 1][base : base + tall] = parts_ref[me ^ (2 * flip)]
        sends[flip - 1][base + tall :] = parts_ref[me ^ (2 * flip + 1)]


def pack_weights(me, x, wq, wk, wv, router, one, two, qg, kg):
    tall = (wq.shape[1] + wk.shape[1] + wv.shape[1]) // 8 + router.shape[1] + 16
    base = x.shape[0] * 8
    return kernel_call(
        pack_kernel,
        "pack_weights",
        12,
        2.0,
        [me, x, wq, wk, wv, router, one, two, qg, kg],
        [((2 * tall, 128), BF16)] + [((base + 2 * tall, 128), BF16)] * 3,
        specs=[SMEM] + [VMEM] * 9,
        scratch=[pltpu.VMEM((8, tall, 128), BF16)],
    )


def relay_kernel(x_ref, own_ref, *refs):
    came, out_ref = refs[:3], refs[3]
    tall = own_ref.shape[0] // 2
    base = came[0].shape[0] - 2 * tall
    out_ref[0, :base] = lane_blocks(x_ref[...])
    out_ref[0, base:] = own_ref[tall:]
    for flip in range(1, 4):
        out_ref[flip, :base] = came[flip - 1][:base]
        out_ref[flip, base:] = came[flip - 1][base + tall :]


def relay(x, own, came):
    tall = own.shape[0] // 2
    base = came[0].shape[0] - 2 * tall
    return kernel_call(
        relay_kernel, "relay", 8, 1.5, [x, own, *came], [((4, base + tall, 128), BF16)]
    )[0]


def forward_kernel(me_ref, x_ref, own_ref, *refs, experts, q_heads):
    came, other_ref = refs[:3], refs[3]
    cos_ref, sin_ref, start_ref = refs[4:7]
    h1_ref, pre_ref, keep_ref, give_ref, inverse_ref, gains_ref, heads_ref, turned_ref, out_ref = refs[-9:]
    rows, width = x_ref.shape
    q_columns = q_heads * HEAD
    columns = q_columns + 2 * HEAD
    total = rows * 8
    tall = own_ref.shape[0] // 2
    base = 8 * rows
    me = me_ref[0]
    for slot in range(8):
        flip = slot // 2
        if slot % 2:
            piece = other_ref[flip, base:]
        elif flip:
            piece = came[flip - 1][base : base + tall]
        else:
            piece = own_ref[:tall]
        span = pl.ds(pl.multiple_of((me ^ slot) * rows, rows), rows)
        turned_ref[:, span] = piece[:columns]
        small = piece[columns:].astype(F32)
        gains_ref[:, span] = small[: experts + 8]
        heads_ref[pl.ds(pl.multiple_of((me ^ slot) * 8, 8), 8)] = small[experts + 8 :]
    gain_one = gains_ref[experts : experts + 1]
    for slot in range(8):
        flip = slot // 2
        if slot % 2:
            x = joined_lanes(other_ref[flip, :base], 8)
        elif flip:
            x = joined_lanes(came[flip - 1][:base], 8)
        else:
            x = x_ref[...]
        x = x.astype(F32)
        scale = lax.rsqrt(jnp.mean(x * x, axis=1, keepdims=True) + EPSILON)
        h1_ref[slot] = (x * scale * gain_one).astype(BF16)
    for slot in range(8):
        block = dot(turned_ref[...], h1_ref[slot], ((1,), (1,)))
        place = pl.multiple_of((me ^ slot) * rows, rows)
        pre_ref[:, pl.ds(place, rows)] = block
    cosine, sine = cos_ref[...], sin_ref[...]
    gain_query, gain_key = heads_ref[:, :1], heads_ref[:, 1:2]
    key = head_forward(pre_ref[q_columns : q_columns + HEAD], gain_key, cosine, sine)[0]
    key = key.T.astype(BF16)
    value = pre_ref[q_columns + HEAD :].astype(BF16)
    inverse_ref[...] = jnp.zeros(inverse_ref.shape, F32)
    for head in range(q_heads):
        query = head_forward(pre_ref[head * HEAD : (head + 1) * HEAD], gain_query, cosine, sine)[0]
        query = query.astype(BF16) * jnp.array(HEAD ** (-0.5), BF16)
        for tile in range(total // TILE):
            low, high = tile * TILE, (tile + 1) * TILE
            scores = dot(key[:high], query[:, low:high])
            u = lax.broadcasted_iota(jnp.int32, (high, TILE), 0)
            t = lax.broadcasted_iota(jnp.int32, (high, TILE), 1) + low
            allowed = (u >= start_ref[:, low:high]) & (u <= t)
            powers = jnp.where(allowed, jnp.exp(scores), 0.0)
            inverse = 1.0 / jnp.sum(powers, axis=0, keepdims=True)
            probs = (powers * inverse).astype(BF16)
            mixed = dot(value[:, :high], probs).astype(BF16)
            inverse_ref[head : head + 1, low:high] = inverse
            for part in range(TILE // rows):
                out_ref[low // rows + part, head * HEAD : (head + 1) * HEAD] = mixed[
                    :, part * rows : (part + 1) * rows
                ]
    for slot in range(8):
        (give_ref if slot % 2 else keep_ref)[slot // 2] = out_ref[me ^ slot]


def attention_forward(me, x, own, came, other, cosine, sine, start, experts, q_heads):
    rows, width = x.shape
    total = 8 * rows
    columns = (q_heads + 2) * HEAD
    q_columns = q_heads * HEAD
    return kernel_call(
        functools.partial(forward_kernel, experts=experts, q_heads=q_heads),
        "attention_forward",
        20,
        7.0,
        [me, x, own, *came, other, cosine, sine, start],
        [
            ((8, rows, width), BF16),
            ((columns, total), F32),
            ((4, q_columns, rows), BF16),
            ((4, q_columns, rows), BF16),
            ((8, total), F32),
            ((experts + 8, width), F32),
            ((HEAD, 128), F32),
            ((columns, width), BF16),
        ],
        specs=[SMEM] + [VMEM] * 9,
        scratch=[pltpu.VMEM((8, q_columns, rows), BF16)],
    )


def merge_kernel(keep_ref, came_ref, *outs):
    for flip in range(1, 4):
        outs[flip - 1][0] = keep_ref[flip]
        outs[flip - 1][1] = came_ref[flip]


def merge(keep, came):
    extent = ((2,) + keep.shape[1:], BF16)
    return kernel_call(merge_kernel, "merge", 4, 0.6, [keep, came], [extent] * 3)


def middle_kernel(x_ref, keep_ref, other_ref, *refs, experts):
    came, wo_ref, wo_came, wo_other_ref, gains_ref = refs[:3], refs[3], refs[4:7], refs[7], refs[8]
    middle_ref, probs_ref = refs[9:11]
    parts = refs[11:15]
    mixed_ref, whole_ref = refs[15:]
    rows, width = x_ref.shape
    for slot in range(8):
        flip, core = slot // 2, slot % 2
        if flip:
            piece = came[flip - 1][core]
        else:
            piece = (other_ref if core else keep_ref)[0]
        span = slice(slot * 128, (slot + 1) * 128)
        mixed_ref[:, span] = piece.astype(F32).T.astype(BF16)
        if core:
            whole_ref[span] = wo_other_ref[flip]
        else:
            whole_ref[span] = (wo_came[flip - 1] if flip else wo_ref)[...]
    middle = x_ref[...].astype(F32) + dot(mixed_ref[...], whole_ref[...])
    middle_ref[...] = middle
    scale = lax.rsqrt(jnp.mean(middle * middle, axis=1, keepdims=True) + EPSILON)
    hidden = (middle * scale * gains_ref[experts + 1 : experts + 2]).astype(BF16)
    size = rows // 4
    for k in range(4):
        parts[k][...] = hidden[k * size : (k + 1) * size]
    probs_ref[...] = softmax_rows(dot(gains_ref[:experts].astype(BF16), hidden, ((1,), (1,))))


def middle_layer(x, keep, other, came, wo, wo_came, wo_other, gains, experts):
    rows, width = x.shape
    return kernel_call(
        functools.partial(middle_kernel, experts=experts),
        "middle_layer",
        12,
        2.0,
        [x, keep, other, *came, wo, *wo_came, wo_other, gains],
        [((rows, width), F32), ((experts, rows), F32)] + [((rows // 4, width), BF16)] * 4,
        scratch=[pltpu.VMEM((rows, width), BF16), pltpu.VMEM((width, width), BF16)],
    )


def stack_kernel(*refs):
    for mine, came, out in zip(refs[:4], refs[4:8], refs[-4:]):
        half = mine.shape[0]
        out[:half] = mine[...]
        out[half:] = came[...]


def stack(mine, came, after=()):
    results = [((2 * v.shape[0],) + v.shape[1:], BF16) for v in mine]
    return kernel_call(stack_kernel, "stack", 8, 0.8, [*mine, *came], results, after=after)


def row_kernel(*refs):
    for i, ref in enumerate(refs[:-1]):
        refs[-1][i] = ref[...]


def row(pieces, name):
    return kernel_call(row_kernel, name, 4, 0.8, pieces, [((len(pieces),) + pieces[0].shape, BF16)])[0]


def slot_index(part, offset):
    for index in range(16):
        reached = 0
        for step in range(4):
            if index >> step & 1:
                reached ^= CUBE[(part + step) % 4]
        if reached == offset:
            return index
    raise ValueError(offset)


def backward_kernel(me_ref, own_da_ref, *refs, experts, q_heads):
    came, other_ref = refs[:3], refs[3]
    heads_ref, wo_ref, cos_ref, sin_ref, start_ref = refs[4:9]
    h1_ref, pre_ref, mixed_keep, mixed_give, inverse_ref, turned_ref, extra_ref = refs[9:16]
    first_ref, wo_grad_ref, keep_ref, send_ref = refs[-11:-7]
    da_ref, mixed_grad_ref, dkey_ref, dvalue_ref, low_ref, out_slots_ref, grad_ref = refs[-7:]
    rows, width = own_da_ref.shape
    q_columns = q_heads * HEAD
    columns = q_columns + 2 * HEAD
    total = rows * 8
    me = me_ref[0]
    for slot in range(8):
        flip, core = slot // 2, slot % 2
        if core:
            piece = other_ref[flip]
        else:
            piece = (came[flip - 1] if flip else own_da_ref)[...]
        span = slice(slot * rows, (slot + 1) * rows)
        da_ref[span] = piece
        place = pl.multiple_of((me ^ slot) * rows, rows)
        mixed_grad_ref[:, pl.ds(place, rows)] = dot(wo_ref[...], piece, ((1,), (1,))).astype(BF16)
        out_slots_ref[:, span] = (mixed_give if core else mixed_keep)[flip]
    wo_grad = dot(out_slots_ref[...], da_ref[...]).astype(BF16)
    wo_grad_ref[...] = lane_blocks(wo_grad)
    gain_query, gain_key = heads_ref[:, :1], heads_ref[:, 1:2]
    cosine, sine = cos_ref[...], sin_ref[...]
    key_turned, key_normed, key_scale = head_forward(
        pre_ref[q_columns : q_columns + HEAD], gain_key, cosine, sine
    )
    key_low = key_turned.astype(BF16)
    key = key_turned.T.astype(BF16)
    value = pre_ref[q_columns + HEAD :].T.astype(BF16)
    dkey_ref[...] = jnp.zeros(dkey_ref.shape, F32)
    dvalue_ref[...] = jnp.zeros(dvalue_ref.shape, F32)
    gain_query_grad = jnp.zeros((HEAD, 1), F32)
    pieces = []
    for head in range(q_heads):
        span = slice(head * HEAD, (head + 1) * HEAD)
        turned, normed, scale = head_forward(pre_ref[span], gain_query, cosine, sine)
        query = turned.astype(BF16) * jnp.array(HEAD ** (-0.5), BF16)
        grads = []
        for tile in range(total // TILE):
            low, high = tile * TILE, (tile + 1) * TILE
            part = query[:, low:high]
            mixed_grad = mixed_grad_ref[span, low:high]
            scores = dot(key[:high], part)
            u = lax.broadcasted_iota(jnp.int32, (high, TILE), 0)
            t = lax.broadcasted_iota(jnp.int32, (high, TILE), 1) + low
            allowed = (u >= start_ref[:, low:high]) & (u <= t)
            probs = jnp.where(allowed, jnp.exp(scores) * inverse_ref[head : head + 1, low:high], 0.0)
            attend = dot(value[:high], mixed_grad)
            delta = jnp.sum(probs * attend, axis=0, keepdims=True)
            score_low = (probs * (attend - delta)).astype(BF16)
            grads.append(dot(key_low[:, :high], score_low))
            dkey_ref[:, :high] += dot(part, score_low, ((1,), (1,)))
            dvalue_ref[:, :high] += dot(mixed_grad, probs.astype(BF16), ((1,), (1,)))
        query_grad = jnp.concatenate(grads, axis=1) * HEAD ** (-0.5)
        pre_grad, gain_grad = head_backward(query_grad, normed, scale, gain_query, cosine, sine)
        gain_query_grad += gain_grad
        pieces.append(pre_grad)
    pre_grad, gain_key_grad = head_backward(
        dkey_ref[...], key_normed, key_scale, gain_key, cosine, sine
    )
    pieces += [pre_grad, dvalue_ref[...]]
    pre_grad = jnp.concatenate(pieces, axis=0)
    low_ref[...] = pre_grad.astype(BF16)
    slots_grad = []
    for slot in range(8):
        place = pl.multiple_of((me ^ slot) * rows, rows)
        slots_grad.append(low_ref[:, pl.ds(place, rows)])
    slots_grad = jnp.concatenate(slots_grad, axis=1)
    grad_ref[:columns] = dot(slots_grad, h1_ref[...].reshape(total, width))
    extra = extra_ref[...]
    lane = lax.broadcasted_iota(jnp.int32, (HEAD, 128), 1)
    gains = jnp.where(lane == 0, gain_query_grad, jnp.where(lane == 1, gain_key_grad, 0.0))
    gains = gains.T[:2]
    step = HEAD // 8
    grad_ref[columns:] = jnp.zeros((64, width), F32)
    grad_ref[columns : columns + experts + 1] = extra[: experts + 1]
    for part in range(8):
        grad_ref[columns + experts + 1 : columns + experts + 3, part * rows : part * rows + step] = gains[
            :, part * step : (part + 1) * step
        ]
    turned = turned_ref[...]
    base = 8 * rows
    for slot in range(8):
        place = pl.multiple_of((me ^ slot) * rows, rows)
        first = grad_ref[:, pl.ds(place, rows)].astype(BF16)
        low_rows_slot = slots_grad[:, slot * rows : (slot + 1) * rows].astype(F32).T.astype(BF16)
        part = dot(low_rows_slot, turned)
        if slot % 2:
            send_ref[slot // 2, :base] = lane_blocks(part.astype(BF16))
            send_ref[slot // 2, base:] = first
        else:
            keep_ref[slot // 2] = part
            first_ref[slot // 2] = first


def attention_backward(
    me, da, came, other, heads, wo, cosine, sine, start, h1, pre, keep, give, inverse, turned, extra, experts, q_heads, after=()
):
    rows, width = da.shape
    total = 8 * rows
    columns = pre.shape[0]
    q_columns = q_heads * HEAD
    return kernel_call(
        functools.partial(backward_kernel, experts=experts, q_heads=q_heads),
        "attention_backward",
        30,
        9.0,
        [me, da, *came, other, heads, wo, cosine, sine, start, h1, pre, keep, give, inverse, turned, extra],
        [
            ((4, columns + 64, 128), BF16),
            ((8 * q_columns, 128), BF16),
            ((4, rows, width), F32),
            ((4, 8 * rows + columns + 64, 128), BF16),
        ],
        specs=[SMEM] + [VMEM] * 17,
        after=after,
        scratch=[
            pltpu.VMEM((total, width), BF16),
            pltpu.VMEM((q_columns, total), BF16),
            pltpu.VMEM((HEAD, total), F32),
            pltpu.VMEM((HEAD, total), F32),
            pltpu.VMEM((columns, total), BF16),
            pltpu.VMEM((q_columns, total), BF16),
            pltpu.VMEM((columns + 64, width), F32),
        ],
    )


def deal_kernel(owner_ref, c_ref, down_ref, *refs, experts, capacity):
    outs, scratch = refs[:6], refs[6:]
    mask_ref, deal_ref, turn_ref, rows_c, back_ref = outs[:5]
    tick_ref = outs[5]
    c_scratch, down_scratch, sems = scratch
    owner = owner_ref[0]
    per_owner, hidden, width = down_ref.shape
    rows = c_ref.shape[1]
    loads = [
        pltpu.make_async_copy(c_ref.at[owner ^ i], c_scratch.at[i], sems.at[i]) for i in range(16)
    ]
    loads.append(pltpu.make_async_copy(down_ref, down_scratch, sems.at[16]))
    for load in loads:
        load.start()
    tick_ref[...] = jnp.zeros(tick_ref.shape, F32)
    lanes = lax.broadcasted_iota(jnp.int32, (experts, 128), 1)
    subs = lax.broadcasted_iota(jnp.int32, (experts, 128), 0)
    eye = (lanes == subs).astype(BF16)
    before = (
        lax.broadcasted_iota(jnp.int32, (rows, rows), 0)
        <= lax.broadcasted_iota(jnp.int32, (rows, rows), 1)
    ).astype(BF16)
    mine_of = lax.broadcasted_iota(jnp.int32, (experts, rows), 0) - owner * per_owner
    slot = lax.broadcasted_iota(jnp.int32, (capacity, rows), 0).astype(F32) + 1.0
    for block in range(16):
        loads[block].wait()
        c = c_scratch[block]
        mask = dot(eye, c[:, width:], ((1,), (1,)))
        mask_ref[block] = mask
        ranks = dot(mask.astype(BF16), before)
        deals = []
        for k in range(per_owner):
            mine = mine_of == k
            hit = jnp.sum(jnp.where(mine, mask, 0.0), axis=0, keepdims=True)
            rank = jnp.sum(jnp.where(mine, ranks, 0.0), axis=0, keepdims=True)
            deals.append(jnp.where((rank == slot) & (hit > 0.5), 1.0, 0.0))
        deal = jnp.concatenate(deals + [jnp.zeros((128 - per_owner * capacity, rows), F32)], axis=0)
        turn_ref[block] = deal.T.astype(BF16)
        deal = deal.astype(BF16)
        deal_ref[block] = deal
        taken = dot(deal[: per_owner * capacity], c[:, :width]).astype(BF16)
        for k in range(per_owner):
            rows_c[k, block * capacity : (block + 1) * capacity] = taken[k * capacity : (k + 1) * capacity]
    loads[16].wait()
    for k in range(per_owner):
        for tile in range(16 * capacity // TILE):
            span = slice(tile * TILE, (tile + 1) * TILE)
            back_ref[k, span] = dot(rows_c[k, span], down_scratch[k], ((1,), (1,)))


def deal_rows(owner, c, down, experts, capacity):
    per_owner, hidden, width = down.shape
    rows = c.shape[1]
    count = 16 * capacity
    return kernel_call(
        functools.partial(deal_kernel, experts=experts, capacity=capacity),
        "deal_rows",
        28,
        10.0,
        [owner, c, down],
        [
            ((16, experts, rows), F32),
            ((16, 128, rows), BF16),
            ((16, rows, 128), BF16),
            ((per_owner, count, width), BF16),
            ((per_owner, count, hidden), F32),
            ((8, 128), F32),
        ],
        specs=[SMEM, ANY, ANY],
        scratch=[
            pltpu.VMEM(c.shape, BF16),
            pltpu.VMEM(down.shape, BF16),
            pltpu.SemaphoreType.DMA((17,)),
        ],
    )


def expert_kernel(owner_ref, *refs, experts, capacity):
    hs = refs[:4]
    gains_ref, mask_ref, deal_ref, turn_ref, back_in, gate_in, up_in = refs[4:11]
    keeps, gives = refs[11:15], refs[15:19]
    targets = refs[19:25]
    gate_ref, up_ref, back_ref, rows_h, gate_out, up_out, active_out, weighted_out, share_ref = refs[25:34]
    rows_back, sems, out_sems = refs[34:]
    per_owner, width = gate_ref.shape[:2]
    loads = [
        pltpu.make_async_copy(gate_in, gate_ref, sems.at[0]),
        pltpu.make_async_copy(up_in, up_ref, sems.at[1]),
        pltpu.make_async_copy(back_in, back_ref, sems.at[2]),
    ]
    for load in loads:
        load.start()
    stores = [
        pltpu.make_async_copy(source, target, out_sems.at[i])
        for i, (source, target) in enumerate(
            zip((rows_h, gate_out, up_out, active_out, weighted_out, share_ref), targets)
        )
    ]
    quarter = hs[0].shape[1]
    rows = 4 * quarter
    owner = owner_ref[0]
    router = gains_ref[:experts].astype(BF16)
    mine_of = lax.broadcasted_iota(jnp.int32, (experts, rows), 0) - owner * per_owner
    both = per_owner * capacity
    for block in range(16):
        h = jnp.concatenate([hs[k][slot_index(k, block)] for k in range(4)], axis=0)
        probs = softmax_rows(dot(router, h, ((1,), (1,)))) * mask_ref[block]
        share = probs / jnp.sum(probs, axis=0, keepdims=True)
        deal = deal_ref[block]
        taken = dot(deal[:both], h).astype(BF16)
        span = slice(block * capacity, (block + 1) * capacity)
        for k in range(per_owner):
            part = jnp.sum(jnp.where(mine_of == k, share, 0.0), axis=0, keepdims=True)
            spot = slice(k * capacity, (k + 1) * capacity)
            column = jnp.sum(deal[spot].astype(F32) * part, axis=1, keepdims=True)
            share_ref[k, span] = jnp.broadcast_to(column, (capacity, 128))
            rows_h[k, span] = taken[spot]
    stores[0].start()
    stores[5].start()
    for load in loads:
        load.wait()
    lane = lax.broadcasted_iota(jnp.int32, (TILE, 128), 1)
    for k in range(per_owner):
        for tile in range(16 * capacity // TILE):
            span = slice(tile * TILE, (tile + 1) * TILE)
            gate = dot(rows_h[k, span], gate_ref[k])
            up = dot(rows_h[k, span], up_ref[k])
            back = back_ref[k, span]
            sig = 1.0 / (1.0 + jnp.exp(-gate))
            silu = gate * sig
            active = silu * up
            active_low = active.astype(BF16)
            share = share_ref[k, span, :1]
            route_grad = jnp.sum(active_low.astype(F32) * back, axis=1, keepdims=True)
            grad = back * share
            gate_low = (grad * up * (sig + silu * (1.0 - sig))).astype(BF16)
            up_low = (grad * silu).astype(BF16)
            active_out[k, span] = active_low
            weighted_out[k, span] = (active * share).astype(BF16)
            gate_out[k, span] = gate_low
            up_out[k, span] = up_low
            total = dot(gate_low, gate_ref[k], ((1,), (1,))) + dot(up_low, up_ref[k], ((1,), (1,)))
            rows_back[k, span, :width] = total.astype(BF16)
            high = route_grad.astype(BF16).astype(F32)
            place = owner * per_owner + k
            spread = jnp.where(lane == place, high, 0.0)
            spread = jnp.where(lane == place + experts, route_grad - high, spread)
            rows_back[k, span, width:] = spread.astype(BF16)
    for i in (1, 2, 3, 4):
        stores[i].start()
    for block in range(16):
        span = slice(block * capacity, (block + 1) * capacity)
        total = dot(
            turn_ref[block][:, :both],
            jnp.concatenate([rows_back[k, span] for k in range(per_owner)], axis=0),
        ).astype(BF16)
        deliver(total, block, keeps, gives)
    for store in stores:
        store.wait()


def deliver(total, block, keeps, gives):
    quarter = total.shape[0] // 4
    for k in range(4):
        index = slot_index(k, block)
        target = gives[k] if index >= 8 else keeps[k]
        target[index % 8] = total[k * quarter : (k + 1) * quarter]


def expert_layer(owner, hs, gains, mask, deal, turn, back, gate, up, experts, capacity):
    per_owner, width, hidden = gate.shape
    quarter = hs[0].shape[1]
    count = 16 * capacity
    piece = ((8, quarter, width + 128), BF16)
    narrow = ((per_owner, count, hidden), BF16)
    saved = [((per_owner, count, width), BF16)] + [narrow] * 4 + [((per_owner, count, 128), F32)]
    held = [(gate.shape, BF16), (up.shape, BF16), (back.shape, F32)] + saved
    held += [((per_owner, count, width + 128), BF16)]
    return kernel_call(
        functools.partial(expert_kernel, experts=experts, capacity=capacity),
        "expert_layer",
        44,
        16.0,
        [owner, *hs, gains, mask, deal, turn, back, gate, up],
        [piece] * 8 + saved,
        specs=[SMEM] + [VMEM] * 8 + [ANY] * 3,
        out_specs=[VMEM] * 8 + [ANY] * 6,
        scratch=[pltpu.VMEM(*item) for item in held]
        + [pltpu.SemaphoreType.DMA((3,)), pltpu.SemaphoreType.DMA((6,))],
    )


def weights_kernel(rows_h, rows_c, gate_low, up_low, weighted, gate_grad, up_grad, down_grad, tick_ref):
    first = ((0,), (0,))
    tick_ref[...] = jnp.zeros(tick_ref.shape, F32)
    for k in range(rows_h.shape[0]):
        gate_grad[k] = dot(rows_h[k], gate_low[k], first).astype(BF16)
        up_grad[k] = dot(rows_h[k], up_low[k], first).astype(BF16)
        down_grad[k] = dot(weighted[k], rows_c[k], first).astype(BF16)


def expert_weights(rows_h, rows_c, gate_low, up_low, weighted):
    per_owner, count, width = rows_h.shape
    hidden = gate_low.shape[2]
    return kernel_call(
        weights_kernel,
        "expert_weights",
        26,
        8.0,
        [rows_h, rows_c, gate_low, up_low, weighted],
        [((per_owner, width, hidden), BF16)] * 2
        + [((per_owner, hidden, width), BF16), ((8, 128), F32)],
    )


def outputs_kernel(active, turn, share, down_ref, *refs, capacity):
    keeps, gives, tick_ref, out_ref = refs[-10:-6], refs[-6:-2], refs[-2], refs[-1]
    tick_ref[...] = jnp.zeros(tick_ref.shape, F32)
    per_owner, count, hidden = active.shape
    for k in range(per_owner):
        for tile in range(count // TILE):
            span = slice(tile * TILE, (tile + 1) * TILE)
            produced = dot(active[k, span], down_ref[k]).astype(BF16).astype(F32)
            out_ref[k, span] = (produced * share[k, span, :1]).astype(BF16)
    for block in range(16):
        span = slice(block * capacity, (block + 1) * capacity)
        both = jnp.concatenate([out_ref[k, span] for k in range(per_owner)], axis=0)
        total = dot(turn[block][:, : both.shape[0]], both).astype(BF16)
        deliver(total, block, keeps, gives)


def expert_outputs(active, turn, share, down, capacity, after=()):
    per_owner, count, hidden = active.shape
    width = down.shape[2]
    quarter = turn.shape[1] // 4
    return kernel_call(
        functools.partial(outputs_kernel, capacity=capacity),
        "expert_outputs",
        18,
        5.0,
        [active, turn, share, down],
        [((8, quarter, width), BF16)] * 8 + [((8, 128), F32)],
        after=after,
        scratch=[pltpu.VMEM((per_owner, count, width), BF16)],
    )


def halve_kernel(*refs):
    mine, came, keeps, gives = refs[:4], refs[4:8], refs[-9:-5], refs[-5:-1]
    refs[-1][...] = jnp.zeros(refs[-1].shape, F32)
    for k in range(4):
        half = keeps[k].shape[0]
        total = mine[k][...].astype(F32) + came[k][...].astype(F32)
        keeps[k][...] = total[:half]
        gives[k][...] = total[half:].astype(BF16)


def halve(mine, came, name, after=()):
    blocks, quarter, width = mine[0].shape
    half = (blocks // 2, quarter, width)
    results = [(half, F32)] * 4 + [(half, BF16)] * 4 + [((8, 128), F32)]
    return kernel_call(halve_kernel, name, 14, 1.0, [*mine, *came], results, after=after)


def landed(refs):
    return jnp.concatenate(
        [mine[0] + came[0].astype(F32) for mine, came in zip(refs[:4], refs[4:8])], axis=0
    )


def output_kernel(*refs):
    middle_ref, out_ref = refs[8:]
    out_ref[...] = (middle_ref[...] + landed(refs[:8])).astype(BF16)


def layer_output(mine, came, middle):
    return kernel_call(
        output_kernel, "layer_output", 6, 1.0, [*mine, *came, middle], [(middle.shape, BF16)]
    )[0]


def router_kernel(*refs, experts):
    middle_ref, probs_ref, routed_ref, gains_ref, c_ref = refs[8:13]
    parts = refs[13:17]
    grad_ref, send_ref, extra_ref = refs[17:]
    rows, width = middle_ref.shape
    returned = landed(refs[:8])
    tail = returned[:, width:].T
    route_grad = tail[:experts] + tail[experts : 2 * experts]
    lanes = lax.broadcasted_iota(jnp.int32, (experts, 128), 1)
    subs = lax.broadcasted_iota(jnp.int32, (experts, 128), 0)
    mask = dot((lanes == subs).astype(BF16), routed_ref[...], ((1,), (1,)))
    probs = probs_ref[...]
    picked = probs * mask
    picked_sum = jnp.sum(picked, axis=0, keepdims=True)
    share = picked / picked_sum
    picked_grad = (route_grad - jnp.sum(route_grad * share, axis=0, keepdims=True)) / picked_sum
    prob_grad = mask * picked_grad
    logit_grad = probs * (prob_grad - jnp.sum(probs * prob_grad, axis=0, keepdims=True))
    logit_low = logit_grad.astype(BF16)
    hidden = jnp.concatenate([part[...] for part in parts], axis=0)
    extra_ref[:experts] = dot(logit_low, hidden)
    logit_rows = jnp.concatenate([logit_grad, jnp.zeros((128 - experts, rows), F32)], axis=0).T
    router = gains_ref[:experts].astype(BF16)
    hidden_grad = returned[:, :width] + dot(logit_rows[:, :experts].astype(BF16), router)
    middle = middle_ref[...]
    scale = lax.rsqrt(jnp.mean(middle * middle, axis=1, keepdims=True) + EPSILON)
    normed = middle * scale
    extra_ref[experts : experts + 8] = jnp.broadcast_to(
        jnp.sum(hidden_grad * normed, axis=0, keepdims=True), (8, width)
    )
    inner = hidden_grad * gains_ref[experts + 1 : experts + 2]
    grad = c_ref[...].astype(F32) + scale * (
        inner - normed * jnp.mean(inner * normed, axis=1, keepdims=True)
    )
    grad_ref[...] = grad
    send_ref[...] = grad.astype(BF16)


def router_backward(mine, came, middle, probs, routed, gains, c, parts, experts):
    rows, width = middle.shape
    return kernel_call(
        functools.partial(router_kernel, experts=experts),
        "router_backward",
        10,
        1.5,
        [*mine, *came, middle, probs, routed, gains, c, *parts],
        [((rows, width), F32), ((rows, width), BF16), ((experts + 8, width), F32)],
    )


def pair_kernel(keep_ref, first_ref, other_ref, *refs):
    total_ref, own_ref, *sends = refs[-5:]
    rows, width = keep_ref.shape[1:]
    base = 8 * rows
    tall = first_ref.shape[1]
    for flip in range(4):
        total = keep_ref[flip] + joined_lanes(other_ref[flip, :base].astype(F32), 8)
        if flip:
            out = sends[flip - 1]
            out[:base] = lane_blocks(total.astype(BF16))
            out[base : base + tall] = first_ref[flip]
            out[base + tall :] = other_ref[flip, base:]
        else:
            total_ref[...] = total
            own_ref[:tall] = first_ref[0]
            own_ref[tall:] = other_ref[0, base:]


def pair_sum(keep, first, other, after=()):
    rows, width = keep.shape[1:]
    tall = first.shape[1]
    return kernel_call(
        pair_kernel,
        "pair_sum",
        12,
        1.5,
        [keep, first, other],
        [((rows, width), F32), ((2 * tall, 128), BF16)] + [((8 * rows + 2 * tall, 128), BF16)] * 3,
        after=after,
    )


def input_kernel(total_ref, *refs, experts):
    came = refs[:3]
    x_ref, gains_ref, middle_grad_ref, out_ref = refs[3:]
    rows, width = x_ref.shape
    total = total_ref[...]
    for piece in came:
        total = total + joined_lanes(piece[: 8 * rows].astype(F32), 8)
    x = x_ref[...].astype(F32)
    scale = lax.rsqrt(jnp.mean(x * x, axis=1, keepdims=True) + EPSILON)
    normed = x * scale
    inner = total * gains_ref[experts : experts + 1]
    out_ref[...] = middle_grad_ref[...] + scale * (
        inner - normed * jnp.mean(inner * normed, axis=1, keepdims=True)
    )


def input_grad(total, came, x, gains, middle_grad, experts):
    return kernel_call(
        functools.partial(input_kernel, experts=experts),
        "input_grad",
        8,
        1.5,
        [total, *came, x, gains, middle_grad],
        [(middle_grad.shape, F32)],
    )[0]


def spread_kernel(own_ref, *refs):
    came, output_ref, out_ref = refs[:3], refs[3], refs[4]
    refs[5][...] = jnp.zeros(refs[5].shape, F32)
    tall = own_ref.shape[0] // 2
    half = tall // 2
    base = came[0].shape[0] - 2 * tall
    size = output_ref.shape[0] // 16
    for piece in range(16):
        flip, place = piece // 4, piece % 4 * half
        source = came[flip - 1][base + place : base + place + half] if flip else own_ref[place : place + half]
        out_ref[piece, :half] = source
        out_ref[piece, half:] = output_ref[piece * size : (piece + 1) * size]


def spread(own, came, output):
    half = own.shape[0] // 4
    return kernel_call(
        spread_kernel,
        "spread",
        6,
        0.8,
        [own, *came, output],
        [((16, half + output.shape[0] // 16, 128), BF16), ((8, 128), F32)],
    )


def sum_kernel(in_ref, *refs):
    out_ref = refs[-1]
    total = in_ref[0].astype(F32)
    for i in range(1, in_ref.shape[0]):
        total = total + in_ref[i].astype(F32)
    total = total.astype(BF16)
    for i in range(in_ref.shape[0]):
        out_ref[i] = total


def sum_all(pieces, after=()):
    return kernel_call(sum_kernel, "sum_all", 6, 1.2, [pieces], [(pieces.shape, BF16)], after=after)[0]


def final_kernel(me_ref, third_ref, wq_ref, wk_ref, wv_ref, gain_ref, *outs, experts, columns):
    query_ref, key_ref, value_ref, output_ref, one_ref, two_ref, gains_ref, router_ref = outs
    rows = third_ref.shape[2]
    tall = (columns + 64) // 2
    q_columns = query_ref.shape[1] // 8
    kv_columns = key_ref.shape[1] // 8
    me = me_ref[0]
    odd = me & 1
    extra = jnp.zeros((64, rows), F32)
    sums = jnp.zeros((rows, 1), F32)
    for flip in range(4):
        pair = []
        for slot in (2 * flip, 2 * flip + 1):
            block = jnp.concatenate(
                [third_ref[2 * slot, :tall], third_ref[2 * slot + 1, :tall]], axis=0
            ).astype(F32)
            turned = block[:columns].T
            span = pl.ds(pl.multiple_of((me ^ slot) * q_columns, q_columns), q_columns)
            query = turned[:, :q_columns]
            query_ref[:, span] = query
            sums = sums + jnp.sum(query * wq_ref[:, span].astype(F32), axis=1, keepdims=True)
            pair.append(turned[:, q_columns:])
            extra = extra + block[columns:]
            for half in range(2):
                size = rows // 2
                output_ref[half * size : (half + 1) * size, slot * rows : (slot + 1) * rows] = third_ref[
                    2 * slot + half, tall:
                ].astype(F32)
        span = pl.ds(pl.multiple_of((me ^ (2 * flip)) // 2 * 2 * kv_columns, 128), 2 * kv_columns)
        first = jnp.where(odd == 1, pair[1], pair[0])
        second = jnp.where(odd == 1, pair[0], pair[1])
        key = jnp.concatenate([first[:, :kv_columns], second[:, :kv_columns]], axis=1)
        value = jnp.concatenate([first[:, kv_columns:], second[:, kv_columns:]], axis=1)
        key_ref[:, span] = key
        value_ref[:, span] = value
        sums = sums + jnp.sum(key * wk_ref[:, span].astype(F32), axis=1, keepdims=True)
        sums = sums + jnp.sum(value * wv_ref[:, span].astype(F32), axis=1, keepdims=True)
    one_ref[...] = jnp.broadcast_to(sums, (rows, 128)).T[:1] / gain_ref[...].astype(F32)
    two_ref[...] = extra[experts : experts + 1]
    gains_ref[...] = extra[experts + 1 : experts + 3]
    router_ref[...] = jnp.concatenate([extra, jnp.zeros((64, rows), F32)], axis=0).T[:, :experts]


def final_grads(me, third, wq, wk, wv, gain, experts, columns):
    rows = third.shape[2]
    return kernel_call(
        functools.partial(final_kernel, experts=experts, columns=columns),
        "final_grads",
        10,
        4.0,
        [me, third, wq, wk, wv, gain],
        [
            (wq.shape, F32),
            (wk.shape, F32),
            (wv.shape, F32),
            ((rows, 8 * rows), F32),
            ((1, rows), F32),
            ((1, rows), F32),
            ((2, rows), F32),
            ((rows, experts), F32),
        ],
        specs=[SMEM] + [VMEM] * 5,
    )


def send(values, axis, flip):
    count = lax.axis_size(axis)
    return lax.ppermute(values, axis, [(i, i ^ flip) for i in range(count)])


def along_z(values):
    if not isinstance(values, (list, tuple)):
        values = [values] * 3
    return [send(value, "fsdp", 2 * (i + 1)) for i, value in enumerate(values)]


def gather_fsdp(block, name):
    came = along_z(block)
    return came, send(row([block, *came], name), "fsdp", 1)


def gather_expert(parts, after=()):
    parts = [part[None] for part in parts]
    for step in range(4):
        came = [send(parts[k], "expert", CUBE[(k + step) % 4]) for k in range(4)]
        parts = stack(parts, came, after if step == 3 else ())
    return parts


def scatter_step(give, step):
    return [send(give[k], "expert", CUBE[(k + step) % 4]) for k in range(4)]


def scatter_expert(mine, give, name, after=()):
    for step in (3, 2, 1):
        halves = halve(mine, scatter_step(give, step), name, after if step == 3 else ())
        mine, give = halves[:4], halves[4:8]
    return mine, scatter_step(give, 0)


def shards(
    tokens,
    lengths,
    routes,
    first_gain,
    query_weight,
    key_weight,
    value_weight,
    output_weight,
    query_gain,
    key_gain,
    second_gain,
    router_weight,
    gate_weight,
    up_weight,
    down_weight,
    cotangent,
):
    own = tokens[0]
    upstream = cotangent[0]
    rows, width = own.shape
    fsdp = lax.axis_size("fsdp")
    owners = lax.axis_size("expert")
    me = lax.axis_index("fsdp").astype(jnp.int32).reshape(1)
    owner = lax.axis_index("expert").astype(jnp.int32).reshape(1)
    experts = router_weight.shape[1]
    capacity = 3 * rows * routes.shape[2] // (2 * experts)
    kv_columns = key_weight.shape[1] // fsdp
    q_columns = query_weight.shape[1] // fsdp
    columns = q_columns + 2 * kv_columns
    q_heads = q_columns // HEAD

    packed = pack_weights(
        me,
        own,
        query_weight,
        key_weight,
        value_weight,
        router_weight,
        first_gain[None],
        second_gain[None],
        query_gain[None],
        key_gain[None],
    )
    x_came = along_z(packed[1:])
    x_other = send(relay(own, packed[0], x_came), "fsdp", 1)
    routed = jnp.sum(
        (routes[0][:, :, None] == jnp.arange(128, dtype=jnp.int32)).astype(F32), axis=1
    ).astype(BF16)
    c_all = lax.all_gather(jnp.concatenate([upstream, routed], axis=1), "expert", axis=0)
    wo_came, wo_other = gather_fsdp(output_weight, "row_output")

    ends = jnp.cumsum(lengths[0])
    place = jnp.arange(rows * fsdp, dtype=jnp.int32)
    start = jnp.max(jnp.where(ends[:, None] <= place[None, :], ends[:, None], 0), axis=0)
    position = (place - start).astype(F32)
    frequency = ROPE_BASE ** (-jnp.arange(HEAD // 2, dtype=F32) * 2.0 / HEAD)
    angles = frequency[:, None] * position[None, :]
    cosine, sine = jnp.cos(angles), jnp.sin(angles)
    start = start[None, :].astype(jnp.int32)

    h1, pre, keep, give, inverse, gains, heads, turned = attention_forward(
        me, own, packed[0], x_came, x_other, cosine, sine, start, experts, q_heads
    )
    other = send(give, "fsdp", 1)
    mixed_came = along_z(merge(keep, other))
    made = middle_layer(own, keep, other, mixed_came, output_weight, wo_came, wo_other, gains, experts)
    middle, probs, own_parts = made[0], made[1], made[2:]
    mask, deal, turn, rows_c, back, tick = deal_rows(owner, c_all, down_weight, experts, capacity)
    hs = gather_expert(own_parts, after=(tick,))
    made = expert_layer(
        owner, hs, gains, mask, deal, turn, back, gate_weight, up_weight, experts, capacity
    )
    rows_h, gate_low, up_low, active, weighted, share = made[8:]
    *grads, tick = expert_weights(rows_h, rows_c, gate_low, up_low, weighted)
    sums = [lax.psum(grad, "fsdp") for grad in grads]
    gate_sum, up_sum, down_sum = (value.astype(F32) for value in sums)
    mine, came = scatter_expert(made[:4], made[4:8], "halve", after=(tick,))

    middle_grad, middle_low, extra = router_backward(
        mine, came, middle, probs, routed, gains, upstream, own_parts, experts
    )
    da_came, da_other = gather_fsdp(middle_low, "row_middle")
    outs = expert_outputs(active, turn, share, down_weight, capacity, after=(extra,))
    first, output_grad, dh_keep, dh_give = attention_backward(
        me,
        middle_low,
        da_came,
        da_other,
        heads,
        output_weight,
        cosine,
        sine,
        start,
        h1,
        pre,
        keep,
        give,
        inverse,
        turned,
        extra,
        experts,
        q_heads,
        after=(outs[8],),
    )
    halves = halve(outs[:4], scatter_step(outs[4:8], 3), "halve_output")
    dh_total, first_own, *dh_sends = pair_sum(
        dh_keep, first, send(dh_give, "fsdp", 1), after=(halves[8],)
    )
    dh_came = along_z(dh_sends)
    second, tick = spread(first_own, dh_came, output_grad)
    for step in (2, 1):
        halves = halve(halves[:4], scatter_step(halves[4:8], step), "halve_output", after=(tick,))
    out_mine, out_came = halves[:4], scatter_step(halves[4:8], 0)
    second = lax.all_to_all(second, "expert", 0, 0, tiled=True)
    second = sum_all(second, after=(sums[0][0, :8, :128],))
    third = lax.all_to_all(second, "expert", 0, 0, tiled=True)
    tokens_grad = input_grad(dh_total, dh_came, own, gains, middle_grad, experts)
    layer_out = layer_output(out_mine, out_came, middle)
    query_sum, key_sum, value_sum, output_sum, one_sum, two_sum, gain_sums, router_sum = final_grads(
        me, third, query_weight, key_weight, value_weight, first_gain[None], experts, columns
    )
    step = HEAD // fsdp
    return (
        layer_out[None],
        tokens_grad[None],
        one_sum[0],
        query_sum,
        key_sum,
        value_sum,
        output_sum,
        gain_sums[0, :step],
        gain_sums[1, :step],
        two_sum[0],
        router_sum,
        gate_sum,
        up_sum,
        down_sum,
    )


def solution(mesh):
    whole = P("expert", "fsdp", None)
    rows = P("fsdp", None)
    vector = P("fsdp")
    owned = P("expert", None, None)
    return jax.shard_map(
        shards,
        mesh=mesh,
        in_specs=(
            whole,
            P("expert", None),
            whole,
            vector,
            rows,
            rows,
            rows,
            rows,
            vector,
            vector,
            vector,
            rows,
            owned,
            owned,
            owned,
            whole,
        ),
        out_specs=(
            whole,
            whole,
            vector,
            rows,
            rows,
            rows,
            rows,
            vector,
            vector,
            vector,
            rows,
            owned,
            owned,
            owned,
        ),
        check_vma=False,
    )
```

```python
import functools

import jax
import jax.numpy as jnp
from jax import lax
from jax.experimental import pallas as pl
from jax.experimental.pallas import tpu as pltpu
from jax.sharding import PartitionSpec as P

EPSILON = 1e-06
ROPE_BASE = 10000.0
HEAD = 64
TILE = 256
F32 = jnp.float32
BF16 = jnp.bfloat16
VMEM = pl.BlockSpec(memory_space=pltpu.VMEM)
SMEM = pl.BlockSpec(memory_space=pltpu.SMEM)
ANY = pl.BlockSpec(memory_space=pl.ANY)
HBM = pl.BlockSpec(memory_space=pltpu.HBM)


def dot(left, right, dims=((1,), (0,))):
    return lax.dot_general(left, right, (dims, ((), ())), preferred_element_type=F32)


def shape(extent, dtype):
    return jax.ShapeDtypeStruct(extent, dtype)


def kernel_call(
    body,
    name,
    mib,
    micros,
    operands,
    results,
    specs=None,
    out_specs=None,
    after=(),
    scratch=(),
    held=(),
    late=(),
    stored=(),
):
    specs = list(specs or [VMEM] * len(operands))
    out_specs = list(out_specs or [VMEM] * len(results))
    scratch = list(scratch)
    held = tuple(held) + tuple(late)
    for i in held:
        specs[i] = HBM
    for i in stored:
        out_specs[i] = HBM
    staged = [pltpu.VMEM(operands[i].shape, operands[i].dtype) for i in held]
    staged += [pltpu.VMEM(*results[i]) for i in stored]
    sems = [pltpu.SemaphoreType.DMA((max(len(held), 1),)), pltpu.SemaphoreType.DMA((max(len(stored), 1),))]
    n, a, r, s = len(operands), len(after), len(results), len(scratch)

    def wrapped(*refs):
        ins, outs = list(refs[:n]), list(refs[n + a : n + a + r])
        own = refs[n + a + r : n + a + r + s]
        stages, (load_sem, store_sem) = refs[n + a + r + s : -2], refs[-2:]
        loads = {}
        for k, i in enumerate(held):
            loads[i] = pltpu.make_async_copy(ins[i], stages[k], load_sem.at[k])
            loads[i].start()
            ins[i] = stages[k]
        stores = []
        for k, i in enumerate(stored):
            stores.append(pltpu.make_async_copy(stages[len(held) + k], outs[i], store_sem.at[k]))
            outs[i] = stages[len(held) + k]
        for i in held:
            if i not in late:
                loads[i].wait()
        if late:
            body(*ins, *outs, *own, wait=lambda i: loads[i].wait())
        else:
            body(*ins, *outs, *own)
        for store in stores:
            store.start()
        for store in stores:
            store.wait()

    return pl.pallas_call(
        wrapped,
        out_shape=[shape(*result) for result in results],
        in_specs=specs + [ANY] * a,
        out_specs=out_specs,
        scratch_shapes=scratch + staged + sems,
        compiler_params=pltpu.CompilerParams(vmem_limit_bytes=mib * 1024 * 1024),
        cost_estimate=pl.CostEstimate(flops=0, bytes_accessed=int(micros * 3.6e6), transcendentals=0),
        name=name,
    )(*operands, *after)


def lane_blocks(value):
    return jnp.concatenate([value[:, i : i + 128] for i in range(0, value.shape[1], 128)], axis=0)


def joined_lanes(value, count):
    rows = value.shape[0] // count
    return jnp.concatenate([value[i * rows : (i + 1) * rows] for i in range(count)], axis=1)


def softmax_rows(logits):
    powers = jnp.exp(logits - jnp.max(logits, axis=0, keepdims=True))
    return powers / jnp.sum(powers, axis=0, keepdims=True)


def head_forward(pre, gain, cosine, sine):
    scale = lax.rsqrt(jnp.mean(pre * pre, axis=0, keepdims=True) + EPSILON)
    normed = pre * scale
    scaled = normed * gain
    a, b = scaled[: HEAD // 2], scaled[HEAD // 2 :]
    turned = jnp.concatenate([a * cosine - b * sine, b * cosine + a * sine], axis=0)
    return turned, normed, scale


def head_backward(grad, normed, scale, gain, cosine, sine):
    a, b = grad[: HEAD // 2], grad[HEAD // 2 :]
    unturned = jnp.concatenate([a * cosine + b * sine, b * cosine - a * sine], axis=0)
    gain_grad = jnp.sum(unturned * normed, axis=1, keepdims=True)
    inner = unturned * gain
    pre_grad = scale * (inner - normed * jnp.mean(inner * normed, axis=0, keepdims=True))
    return pre_grad, gain_grad


def prepare_kernel(routes_ref, c_ref, dressed_ref, mask_ref, deal_ref, turn_ref, whole_ref, *, experts, capacity):
    rows, width = c_ref.shape
    lanes = lax.broadcasted_iota(jnp.int32, (rows, 128), 1)
    routed = jnp.zeros((rows, 128), F32)
    for route in range(routes_ref.shape[1]):
        routed = routed + jnp.where(routes_ref[:, route : route + 1] == lanes, 1.0, 0.0)
    dressed_ref[:, :width] = c_ref[...]
    dressed_ref[:, width:] = routed.astype(BF16)
    mask = routed.T[:experts]
    mask_ref[...] = mask
    ranks = dot(mask.astype(BF16), earlier(rows))
    slot = lax.broadcasted_iota(jnp.int32, (capacity, rows), 0).astype(F32) + 1.0
    for expert in range(experts):
        one = slice(expert, expert + 1)
        whole_ref[expert * capacity : (expert + 1) * capacity] = jnp.where(
            (ranks[one] == slot) & (mask[one] > 0.5), 1.0, 0.0
        )
    deal_ref[...] = whole_ref[...].astype(BF16)
    for part in range(0, experts * capacity, 128):
        turn_ref[:, part : part + 128] = whole_ref[part : part + 128].T.astype(BF16)


def earlier(rows):
    return (
        lax.broadcasted_iota(jnp.int32, (rows, rows), 0)
        <= lax.broadcasted_iota(jnp.int32, (rows, rows), 1)
    ).astype(BF16)


def prepare(routes, c, experts, capacity):
    rows, width = c.shape
    slots = experts * capacity
    return kernel_call(
        functools.partial(prepare_kernel, experts=experts, capacity=capacity),
        "prepare",
        10,
        2.0,
        [routes, c],
        [((rows, width + 128), BF16), ((experts, rows), F32), ((slots, rows), BF16), ((rows, slots), BF16)],
        scratch=[pltpu.VMEM((slots, rows), F32)],
        held=(0, 1),
        stored=(0, 1, 2, 3),
    )


def pack_kernel(me_ref, x_ref, wq_ref, wk_ref, wv_ref, router_ref, one_ref, two_ref, qg_ref, kg_ref, *outs):
    own_ref, sends, parts_ref = outs[0], outs[1:4], outs[4]
    rows, experts = router_ref.shape
    wide = wq_ref.shape[1] // 8
    narrow = wk_ref.shape[1] // 8
    router = jnp.concatenate([router_ref[...].astype(F32), jnp.zeros((rows, 128 - experts), F32)], axis=1)
    count = qg_ref.shape[1]
    heads = jnp.concatenate([qg_ref[...], kg_ref[...]], axis=0).astype(F32)
    heads = jnp.concatenate([heads, jnp.zeros((2, 128 - count), F32)], axis=1)
    heads = jnp.concatenate([heads, jnp.zeros((126, 128), F32)], axis=0).T[:count]
    small = jnp.concatenate(
        [
            router.T[:experts],
            one_ref[...].astype(F32),
            two_ref[...].astype(F32),
            jnp.zeros((6, 128), F32),
            heads,
        ],
        axis=0,
    ).astype(BF16)
    for part in range(8):
        parts_ref[part, :wide] = wq_ref[:, part * wide : (part + 1) * wide].astype(F32).T.astype(BF16)
        parts_ref[part, wide + 2 * narrow :] = small
    for pair in range(4):
        span = slice(pair * 128, (pair + 1) * 128)
        for ref, place in ((wk_ref, wide), (wv_ref, wide + narrow)):
            turned = ref[:, span].astype(F32).T.astype(BF16)
            parts_ref[2 * pair, place : place + narrow] = turned[:narrow]
            parts_ref[2 * pair + 1, place : place + narrow] = turned[narrow:]
    me = me_ref[0]
    tall = parts_ref.shape[1]
    blocks = lane_blocks(x_ref[...])
    base = blocks.shape[0]
    own_ref[:tall] = parts_ref[me]
    own_ref[tall:] = parts_ref[me ^ 1]
    for flip in range(1, 4):
        sends[flip - 1][:base] = blocks
        sends[flip - 1][base : base + tall] = parts_ref[me ^ (2 * flip)]
        sends[flip - 1][base + tall :] = parts_ref[me ^ (2 * flip + 1)]


def pack_weights(me, x, wq, wk, wv, router, one, two, qg, kg):
    tall = (wq.shape[1] + wk.shape[1] + wv.shape[1]) // 8 + router.shape[1] + 16
    base = x.shape[0] * 8
    return kernel_call(
        pack_kernel,
        "pack_weights",
        16,
        2.0,
        [me, x, wq, wk, wv, router, one, two, qg, kg],
        [((2 * tall, 128), BF16)] + [((base + 2 * tall, 128), BF16)] * 3,
        specs=[SMEM] + [VMEM] * 9,
        scratch=[pltpu.VMEM((8, tall, 128), BF16)],
        held=range(1, 10),
    )


def relay_kernel(x_ref, own_ref, *refs):
    came, out_ref = refs[:3], refs[3]
    tall = own_ref.shape[0] // 2
    base = came[0].shape[0] - 2 * tall
    out_ref[0, :base] = lane_blocks(x_ref[...])
    out_ref[0, base:] = own_ref[tall:]
    for flip in range(1, 4):
        out_ref[flip, :base] = came[flip - 1][:base]
        out_ref[flip, base:] = came[flip - 1][base + tall :]


def relay(x, own, came, after=()):
    tall = own.shape[0] // 2
    base = came[0].shape[0] - 2 * tall
    return kernel_call(
        relay_kernel, "relay", 8, 1.5, [x, own, *came], [((4, base + tall, 128), BF16)], after=after, held=(0,)
    )[0]


def forward_kernel(me_ref, x_ref, own_ref, *refs, experts, q_heads):
    came, other_ref = refs[:3], refs[3]
    cos_ref, sin_ref, start_ref = refs[4:7]
    h1_ref, pre_ref, keep_ref, give_ref, inverse_ref, gains_ref, heads_ref, turned_ref, out_ref = refs[-9:]
    rows, width = x_ref.shape
    q_columns = q_heads * HEAD
    columns = q_columns + 2 * HEAD
    total = rows * 8
    tall = own_ref.shape[0] // 2
    base = 8 * rows
    me = me_ref[0]
    for slot in range(8):
        flip = slot // 2
        if slot % 2:
            piece = other_ref[flip, base:]
        elif flip:
            piece = came[flip - 1][base : base + tall]
        else:
            piece = own_ref[:tall]
        span = pl.ds(pl.multiple_of((me ^ slot) * rows, rows), rows)
        turned_ref[:, span] = piece[:columns]
        small = piece[columns:].astype(F32)
        gains_ref[:, span] = small[: experts + 8]
        heads_ref[pl.ds(pl.multiple_of((me ^ slot) * 8, 8), 8)] = small[experts + 8 :]
    gain_one = gains_ref[experts : experts + 1]
    for slot in range(8):
        flip = slot // 2
        if slot % 2:
            x = joined_lanes(other_ref[flip, :base], 8)
        elif flip:
            x = joined_lanes(came[flip - 1][:base], 8)
        else:
            x = x_ref[...]
        x = x.astype(F32)
        scale = lax.rsqrt(jnp.mean(x * x, axis=1, keepdims=True) + EPSILON)
        h1_ref[slot] = (x * scale * gain_one).astype(BF16)
    for slot in range(8):
        block = dot(turned_ref[...], h1_ref[slot], ((1,), (1,)))
        place = pl.multiple_of((me ^ slot) * rows, rows)
        pre_ref[:, pl.ds(place, rows)] = block
    cosine, sine = cos_ref[...], sin_ref[...]
    gain_query, gain_key = heads_ref[:, :1], heads_ref[:, 1:2]
    key = head_forward(pre_ref[q_columns : q_columns + HEAD], gain_key, cosine, sine)[0]
    key = key.T.astype(BF16)
    value = pre_ref[q_columns + HEAD :].astype(BF16)
    inverse_ref[...] = jnp.zeros(inverse_ref.shape, F32)
    for head in range(q_heads):
        query = head_forward(pre_ref[head * HEAD : (head + 1) * HEAD], gain_query, cosine, sine)[0]
        query = query.astype(BF16) * jnp.array(HEAD ** (-0.5), BF16)
        for tile in range(total // TILE):
            low, high = tile * TILE, (tile + 1) * TILE
            scores = dot(key[:high], query[:, low:high])
            u = lax.broadcasted_iota(jnp.int32, (high, TILE), 0)
            t = lax.broadcasted_iota(jnp.int32, (high, TILE), 1) + low
            allowed = (u >= start_ref[:, low:high]) & (u <= t)
            powers = jnp.where(allowed, jnp.exp(scores), 0.0)
            inverse = 1.0 / jnp.sum(powers, axis=0, keepdims=True)
            probs = (powers * inverse).astype(BF16)
            mixed = dot(value[:, :high], probs).astype(BF16)
            inverse_ref[head : head + 1, low:high] = inverse
            for part in range(TILE // rows):
                out_ref[low // rows + part, head * HEAD : (head + 1) * HEAD] = mixed[
                    :, part * rows : (part + 1) * rows
                ]
    for slot in range(8):
        (give_ref if slot % 2 else keep_ref)[slot // 2] = out_ref[me ^ slot]


def attention_forward(me, x, own, came, other, cosine, sine, start, experts, q_heads):
    rows, width = x.shape
    total = 8 * rows
    columns = (q_heads + 2) * HEAD
    q_columns = q_heads * HEAD
    return kernel_call(
        functools.partial(forward_kernel, experts=experts, q_heads=q_heads),
        "attention_forward",
        24,
        7.0,
        [me, x, own, *came, other, cosine, sine, start],
        [
            ((8, rows, width), BF16),
            ((columns, total), F32),
            ((4, q_columns, rows), BF16),
            ((4, q_columns, rows), BF16),
            ((8, total), F32),
            ((experts + 8, width), F32),
            ((HEAD, 128), F32),
            ((columns, width), BF16),
            ((8, q_columns, rows), BF16),
        ],
        specs=[SMEM] + [VMEM] * 9,
        held=(1,),
        stored=(0, 1, 4, 6, 7, 8),
    )


def merge_kernel(keep_ref, came_ref, *outs):
    for flip in range(1, 4):
        outs[flip - 1][0] = keep_ref[flip]
        outs[flip - 1][1] = came_ref[flip]


def merge(keep, came):
    extent = ((2,) + keep.shape[1:], BF16)
    return kernel_call(merge_kernel, "merge", 4, 0.6, [keep, came], [extent] * 3)


def middle_kernel(x_ref, keep_ref, other_ref, *refs, experts):
    came, wo_ref, wo_came, wo_other_ref, gains_ref, deal_ref = refs[:3], refs[3], refs[4:7], refs[7], refs[8], refs[9]
    middle_ref, probs_ref, hidden_ref, sent_ref, mixed_ref, whole_ref = refs[10:]
    rows, width = x_ref.shape
    for slot in range(8):
        flip, core = slot // 2, slot % 2
        if flip:
            piece = came[flip - 1][core]
        else:
            piece = (other_ref if core else keep_ref)[0]
        span = slice(slot * 128, (slot + 1) * 128)
        mixed_ref[:, span] = piece.astype(F32).T.astype(BF16)
        if core:
            whole_ref[span] = wo_other_ref[flip]
        else:
            whole_ref[span] = (wo_came[flip - 1] if flip else wo_ref)[...]
    middle = x_ref[...].astype(F32) + dot(mixed_ref[...], whole_ref[...])
    middle_ref[...] = middle
    scale = lax.rsqrt(jnp.mean(middle * middle, axis=1, keepdims=True) + EPSILON)
    hidden = (middle * scale * gains_ref[experts + 1 : experts + 2]).astype(BF16)
    hidden_ref[...] = hidden
    probs_ref[...] = softmax_rows(dot(gains_ref[:experts].astype(BF16), hidden, ((1,), (1,))))
    owners, per_owner, capacity, _ = sent_ref.shape
    size = 4 * per_owner * capacity
    for part in range(owners // 4):
        taken = dot(deal_ref[part * size : (part + 1) * size], hidden).astype(BF16)
        sent_ref[4 * part : 4 * part + 4] = taken.reshape(4, per_owner, capacity, width)


def middle_layer(x, keep, other, came, wo, wo_came, wo_other, gains, deal, experts, owners):
    rows, width = x.shape
    per_owner = experts // owners
    capacity = deal.shape[0] // experts
    return kernel_call(
        functools.partial(middle_kernel, experts=experts),
        "middle_layer",
        22,
        3.0,
        [x, keep, other, *came, wo, *wo_came, wo_other, gains, deal],
        [
            ((rows, width), F32),
            ((experts, rows), F32),
            ((rows, width), BF16),
            ((owners, per_owner, capacity, width), BF16),
        ],
        scratch=[pltpu.VMEM((rows, width), BF16), pltpu.VMEM((width, width), BF16)],
        held=(0, 6, 12),
        stored=(0, 2),
    )


def row_kernel(*refs):
    for i, ref in enumerate(refs[:-1]):
        refs[-1][i] = ref[...]


def row(pieces, name, after=()):
    return kernel_call(
        row_kernel, name, 6, 0.8, pieces, [((len(pieces),) + pieces[0].shape, BF16)], after=after
    )[0]


def backward_kernel(me_ref, own_da_ref, *refs, experts, q_heads, wait):
    came, other_ref = refs[:3], refs[3]
    heads_ref, wo_ref, cos_ref, sin_ref, start_ref = refs[4:9]
    h1_ref, pre_ref, mixed_ref, inverse_ref, turned_ref, extra_ref = refs[9:15]
    first_ref, wo_grad_ref, keep_ref, send_ref = refs[-11:-7]
    da_ref, mixed_grad_ref, dkey_ref, dvalue_ref, low_ref, out_slots_ref, grad_ref = refs[-7:]
    rows, width = own_da_ref.shape
    q_columns = q_heads * HEAD
    columns = q_columns + 2 * HEAD
    total = rows * 8
    me = me_ref[0]
    for slot in range(8):
        flip, core = slot // 2, slot % 2
        if core:
            piece = other_ref[flip]
        else:
            piece = (came[flip - 1] if flip else own_da_ref)[...]
        span = slice(slot * rows, (slot + 1) * rows)
        da_ref[span] = piece
        place = pl.multiple_of((me ^ slot) * rows, rows)
        mixed_grad_ref[:, pl.ds(place, rows)] = dot(wo_ref[...], piece, ((1,), (1,))).astype(BF16)
    wait(13)
    for slot in range(8):
        out_slots_ref[:, slot * rows : (slot + 1) * rows] = mixed_ref[me ^ slot]
    wo_grad = dot(out_slots_ref[...], da_ref[...]).astype(BF16)
    wo_grad_ref[...] = lane_blocks(wo_grad)
    wait(12)
    wait(14)
    gain_query, gain_key = heads_ref[:, :1], heads_ref[:, 1:2]
    cosine, sine = cos_ref[...], sin_ref[...]
    key_turned, key_normed, key_scale = head_forward(
        pre_ref[q_columns : q_columns + HEAD], gain_key, cosine, sine
    )
    key_low = key_turned.astype(BF16)
    key = key_turned.T.astype(BF16)
    value = pre_ref[q_columns + HEAD :].T.astype(BF16)
    dkey_ref[...] = jnp.zeros(dkey_ref.shape, F32)
    dvalue_ref[...] = jnp.zeros(dvalue_ref.shape, F32)
    gain_query_grad = jnp.zeros((HEAD, 1), F32)
    pieces = []
    for head in range(q_heads):
        span = slice(head * HEAD, (head + 1) * HEAD)
        turned, normed, scale = head_forward(pre_ref[span], gain_query, cosine, sine)
        query = turned.astype(BF16) * jnp.array(HEAD ** (-0.5), BF16)
        grads = []
        for tile in range(total // TILE):
            low, high = tile * TILE, (tile + 1) * TILE
            part = query[:, low:high]
            mixed_grad = mixed_grad_ref[span, low:high]
            scores = dot(key[:high], part)
            u = lax.broadcasted_iota(jnp.int32, (high, TILE), 0)
            t = lax.broadcasted_iota(jnp.int32, (high, TILE), 1) + low
            allowed = (u >= start_ref[:, low:high]) & (u <= t)
            probs = jnp.where(allowed, jnp.exp(scores) * inverse_ref[head : head + 1, low:high], 0.0)
            attend = dot(value[:high], mixed_grad)
            delta = jnp.sum(probs * attend, axis=0, keepdims=True)
            score_low = (probs * (attend - delta)).astype(BF16)
            grads.append(dot(key_low[:, :high], score_low))
            dkey_ref[:, :high] += dot(part, score_low, ((1,), (1,)))
            dvalue_ref[:, :high] += dot(mixed_grad, probs.astype(BF16), ((1,), (1,)))
        query_grad = jnp.concatenate(grads, axis=1) * HEAD ** (-0.5)
        pre_grad, gain_grad = head_backward(query_grad, normed, scale, gain_query, cosine, sine)
        gain_query_grad += gain_grad
        pieces.append(pre_grad)
    pre_grad, gain_key_grad = head_backward(
        dkey_ref[...], key_normed, key_scale, gain_key, cosine, sine
    )
    pieces += [pre_grad, dvalue_ref[...]]
    pre_grad = jnp.concatenate(pieces, axis=0)
    low_ref[...] = pre_grad.astype(BF16)
    slots_grad = []
    for slot in range(8):
        place = pl.multiple_of((me ^ slot) * rows, rows)
        slots_grad.append(low_ref[:, pl.ds(place, rows)])
    slots_grad = jnp.concatenate(slots_grad, axis=1)
    wait(11)
    wait(15)
    grad_ref[:columns] = dot(slots_grad, h1_ref[...].reshape(total, width))
    extra = extra_ref[...]
    lane = lax.broadcasted_iota(jnp.int32, (HEAD, 128), 1)
    gains = jnp.where(lane == 0, gain_query_grad, jnp.where(lane == 1, gain_key_grad, 0.0))
    gains = gains.T[:2]
    step = HEAD // 8
    grad_ref[columns:] = jnp.zeros((64, width), F32)
    grad_ref[columns : columns + experts + 1] = extra[: experts + 1]
    for part in range(8):
        grad_ref[columns + experts + 1 : columns + experts + 3, part * rows : part * rows + step] = gains[
            :, part * step : (part + 1) * step
        ]
    turned = turned_ref[...]
    base = 8 * rows
    for slot in range(8):
        place = pl.multiple_of((me ^ slot) * rows, rows)
        first = grad_ref[:, pl.ds(place, rows)].astype(BF16)
        low_rows_slot = slots_grad[:, slot * rows : (slot + 1) * rows].astype(F32).T.astype(BF16)
        part = dot(low_rows_slot, turned)
        if slot % 2:
            send_ref[slot // 2, :base] = lane_blocks(part.astype(BF16))
            send_ref[slot // 2, base:] = first
        else:
            keep_ref[slot // 2] = part
            first_ref[slot // 2] = first


def attention_backward(
    me, da, came, other, heads, wo, cosine, sine, start, h1, pre, mixed, inverse, turned, extra, experts, q_heads
):
    rows, width = da.shape
    total = 8 * rows
    columns = pre.shape[0]
    q_columns = q_heads * HEAD
    return kernel_call(
        functools.partial(backward_kernel, experts=experts, q_heads=q_heads),
        "attention_backward",
        30,
        0.5,
        [me, da, *came, other, heads, wo, cosine, sine, start, h1, pre, mixed, inverse, turned, extra],
        [
            ((4, columns + 64, 128), BF16),
            ((8 * q_columns, 128), BF16),
            ((4, rows, width), F32),
            ((4, 8 * rows + columns + 64, 128), BF16),
        ],
        specs=[SMEM] + [VMEM] * 16,
        held=(6, 7),
        late=(11, 12, 13, 14, 15),
        scratch=[
            pltpu.VMEM((total, width), BF16),
            pltpu.VMEM((q_columns, total), BF16),
            pltpu.VMEM((HEAD, total), F32),
            pltpu.VMEM((HEAD, total), F32),
            pltpu.VMEM((columns, total), BF16),
            pltpu.VMEM((q_columns, total), BF16),
            pltpu.VMEM((columns + 64, width), F32),
        ],
    )


def deal_kernel(owner_ref, c_ref, down_ref, rows_c, mask_ref, back_ref, c_scratch, sems, *, experts, capacity):
    owner = owner_ref[0]
    per_owner, hidden, width = down_ref.shape
    rows = c_ref.shape[1]
    loads = [pltpu.make_async_copy(c_ref.at[i], c_scratch.at[i], sems.at[i]) for i in range(16)]
    for load in loads:
        load.start()
    lanes = lax.broadcasted_iota(jnp.int32, (experts, 128), 1)
    subs = lax.broadcasted_iota(jnp.int32, (experts, 128), 0)
    eye = (lanes == subs).astype(BF16)
    before = earlier(rows)
    mine_of = lax.broadcasted_iota(jnp.int32, (experts, rows), 0) - owner * per_owner
    slot = lax.broadcasted_iota(jnp.int32, (capacity, rows), 0).astype(F32) + 1.0
    for block in range(16):
        loads[block].wait()
        c = c_scratch[block]
        mask = dot(eye, c[:, width:], ((1,), (1,)))
        ranks = dot(mask.astype(BF16), before)
        deals = []
        for k in range(per_owner):
            mine = mine_of == k
            hit = jnp.sum(jnp.where(mine, mask, 0.0), axis=0, keepdims=True)
            rank = jnp.sum(jnp.where(mine, ranks, 0.0), axis=0, keepdims=True)
            deals.append(jnp.where((rank == slot) & (hit > 0.5), 1.0, 0.0))
        taken = dot(jnp.concatenate(deals, axis=0).astype(BF16), c).astype(BF16)
        span = slice(block * capacity, (block + 1) * capacity)
        for k in range(per_owner):
            spot = slice(k * capacity, (k + 1) * capacity)
            rows_c[k, span] = taken[spot, :width]
            mask_ref[k, span] = taken[spot, width:]
    for k in range(per_owner):
        for tile in range(16 * capacity // TILE):
            span = slice(tile * TILE, (tile + 1) * TILE)
            back_ref[k, span] = dot(rows_c[k, span], down_ref[k], ((1,), (1,)))


def deal_rows(owner, c, down, experts, capacity):
    per_owner, hidden, width = down.shape
    count = 16 * capacity
    return kernel_call(
        functools.partial(deal_kernel, experts=experts, capacity=capacity),
        "deal_rows",
        28,
        12.0,
        [owner, c, down],
        [
            ((per_owner, count, width), BF16),
            ((per_owner, count, 128), BF16),
            ((per_owner, count, hidden), F32),
        ],
        specs=[SMEM, HBM, HBM],
        scratch=[pltpu.VMEM(c.shape, BF16), pltpu.SemaphoreType.DMA((16,))],
        held=(2,),
        stored=(0, 1, 2),
    )


def expert_kernel(
    owner_ref,
    h_ref,
    gains_ref,
    mask_ref,
    back_in,
    gate_ref,
    up_ref,
    rows_back,
    gate_out,
    up_out,
    active_out,
    weighted_out,
    share_ref,
    *,
    experts,
    wait,
):
    owners, per_owner, capacity, width = h_ref.shape
    owner = owner_ref[0]
    router = jnp.concatenate([gains_ref[:experts], jnp.zeros((128 - experts, width), F32)], axis=0)
    router = router.astype(BF16)
    group = 8
    size = group * capacity
    lane = lax.broadcasted_iota(jnp.int32, (size, 128), 1)
    for i in (5, 6, 3, 4):
        wait(i)
    for k in range(per_owner):
        place = owner * per_owner + k
        for part in range(owners // group):
            blocks = slice(part * group, (part + 1) * group)
            span = slice(part * size, (part + 1) * size)
            h = h_ref[blocks, k].reshape(size, width)
            gate = dot(h, gate_ref[k])
            up = dot(h, up_ref[k])
            logits = dot(h, router, ((1,), (1,)))
            chosen = mask_ref[k, span] > 0.5
            top = jnp.max(jnp.where(chosen, logits, -1e30), axis=1, keepdims=True)
            powers = jnp.where(chosen, jnp.exp(logits - top), 0.0)
            total = jnp.sum(powers, axis=1, keepdims=True)
            share = jnp.sum(jnp.where(lane == place, powers, 0.0), axis=1, keepdims=True)
            share = share / jnp.where(total > 0.0, total, 1.0)
            share_ref[k, span] = jnp.broadcast_to(share, (size, 128))
            back = back_in[k, span]
            sig = 1.0 / (1.0 + jnp.exp(-gate))
            silu = gate * sig
            active = silu * up
            active_low = active.astype(BF16)
            route_grad = jnp.sum(active_low.astype(F32) * back, axis=1, keepdims=True)
            grad = back * share
            gate_low = (grad * up * (sig + silu * (1.0 - sig))).astype(BF16)
            up_low = (grad * silu).astype(BF16)
            active_out[k, span] = active_low
            weighted_out[k, span] = (active * share).astype(BF16)
            gate_out[k, span] = gate_low
            up_out[k, span] = up_low
            rows = dot(gate_low, gate_ref[k], ((1,), (1,))) + dot(up_low, up_ref[k], ((1,), (1,)))
            high = route_grad.astype(BF16).astype(F32)
            spread_out = jnp.where(lane == place, high, 0.0)
            spread_out = jnp.where(lane == place + experts, route_grad - high, spread_out)
            whole = jnp.concatenate([rows.astype(BF16), spread_out.astype(BF16)], axis=1)
            rows_back[blocks, k] = whole.reshape(group, capacity, width + 128)


def expert_layer(owner, h, gains, mask, back, gate, up, experts):
    per_owner, width, hidden = gate.shape
    owners, _, capacity, _ = h.shape
    count = owners * capacity
    narrow = ((per_owner, count, hidden), BF16)
    return kernel_call(
        functools.partial(expert_kernel, experts=experts),
        "expert_layer",
        40,
        14.0,
        [owner, h, gains, mask, back, gate, up],
        [((owners, per_owner, capacity, width + 128), BF16)] + [narrow] * 4 + [((per_owner, count, 128), F32)],
        specs=[SMEM] + [VMEM] * 6,
        late=(5, 6, 3, 4),
        stored=(1, 2, 3, 4, 5),
    )


def weights_kernel(h_ref, rows_c, gate_low, up_low, weighted, gate_grad, up_grad, down_grad, tick_ref):
    tick_ref[...] = jnp.zeros(tick_ref.shape, F32)
    first = ((0,), (0,))
    owners, per_owner, capacity, width = h_ref.shape
    for k in range(per_owner):
        rows_h = h_ref[:, k].reshape(owners * capacity, width)
        gate_grad[k] = dot(rows_h, gate_low[k], first).astype(BF16)
        up_grad[k] = dot(rows_h, up_low[k], first).astype(BF16)
        down_grad[k] = dot(weighted[k], rows_c[k], first).astype(BF16)


def expert_weights(h, rows_c, gate_low, up_low, weighted):
    per_owner, count, width = rows_c.shape
    hidden = gate_low.shape[2]
    return kernel_call(
        weights_kernel,
        "expert_weights",
        32,
        9.0,
        [h, rows_c, gate_low, up_low, weighted],
        [((per_owner, width, hidden), BF16)] * 2 + [((per_owner, hidden, width), BF16), ((8, 128), F32)],
        held=(1, 2, 3, 4),
        stored=(0, 1, 2),
    )


def outputs_kernel(active, share, down_ref, sent_ref, tick_ref):
    tick_ref[...] = jnp.zeros(tick_ref.shape, F32)
    per_owner, count, hidden = active.shape
    owners, _, capacity, width = sent_ref.shape
    group = 8
    size = group * capacity
    for k in range(per_owner):
        for part in range(owners // group):
            span = slice(part * size, (part + 1) * size)
            produced = dot(active[k, span], down_ref[k]).astype(BF16).astype(F32)
            produced = (produced * share[k, span, :1]).astype(BF16)
            sent_ref[part * group : (part + 1) * group, k] = produced.reshape(group, capacity, width)


def expert_outputs(active, share, down, owners, after=()):
    per_owner, count, hidden = active.shape
    width = down.shape[2]
    return kernel_call(
        outputs_kernel,
        "expert_outputs",
        18,
        5.0,
        [active, share, down],
        [((owners, per_owner, count // owners, width), BF16), ((8, 128), F32)],
        after=after,
        held=(0, 1, 2),
    )


def output_kernel(rows_ref, turn_ref, middle_ref, out_ref, tick_ref):
    slots = turn_ref.shape[1]
    total = dot(turn_ref[...], rows_ref[...].reshape(slots, rows_ref.shape[3]))
    out_ref[...] = (middle_ref[...] + total).astype(BF16)
    tick_ref[...] = jnp.zeros(tick_ref.shape, F32)


def layer_output(rows, turn, middle):
    return kernel_call(
        output_kernel,
        "layer_output",
        14,
        0.3,
        [rows, turn, middle],
        [(middle.shape, BF16), ((8, 128), F32)],
        held=(1, 2),
        stored=(0,),
    )


def router_kernel(rows_ref, turn_ref, middle_ref, probs_ref, mask_ref, gains_ref, c_ref, hidden_ref, *refs, experts):
    grad_ref, send_ref, extra_ref = refs
    rows, width = middle_ref.shape
    returned = dot(turn_ref[...], rows_ref[...].reshape(turn_ref.shape[1], width + 128))
    tail = returned[:, width:].T
    route_grad = tail[:experts] + tail[experts : 2 * experts]
    mask = mask_ref[...]
    probs = probs_ref[...]
    picked = probs * mask
    picked_sum = jnp.sum(picked, axis=0, keepdims=True)
    share = picked / picked_sum
    picked_grad = (route_grad - jnp.sum(route_grad * share, axis=0, keepdims=True)) / picked_sum
    prob_grad = mask * picked_grad
    logit_grad = probs * (prob_grad - jnp.sum(probs * prob_grad, axis=0, keepdims=True))
    extra_ref[:experts] = dot(logit_grad.astype(BF16), hidden_ref[...])
    logit_rows = jnp.concatenate([logit_grad, jnp.zeros((128 - experts, rows), F32)], axis=0).T
    router = gains_ref[:experts].astype(BF16)
    hidden_grad = returned[:, :width] + dot(logit_rows[:, :experts].astype(BF16), router)
    middle = middle_ref[...]
    scale = lax.rsqrt(jnp.mean(middle * middle, axis=1, keepdims=True) + EPSILON)
    normed = middle * scale
    extra_ref[experts : experts + 8] = jnp.broadcast_to(
        jnp.sum(hidden_grad * normed, axis=0, keepdims=True), (8, width)
    )
    inner = hidden_grad * gains_ref[experts + 1 : experts + 2]
    grad = c_ref[...].astype(F32) + scale * (
        inner - normed * jnp.mean(inner * normed, axis=1, keepdims=True)
    )
    grad_ref[...] = grad
    send_ref[...] = grad.astype(BF16)


def router_backward(rows_back, turn, middle, probs, mask, gains, c, hidden, experts, after=()):
    rows, width = middle.shape
    return kernel_call(
        functools.partial(router_kernel, experts=experts),
        "router_backward",
        16,
        0.5,
        [rows_back, turn, middle, probs, mask, gains, c, hidden],
        [((rows, width), F32), ((rows, width), BF16), ((experts + 8, width), F32)],
        after=after,
        held=(1, 2, 4, 6, 7),
        stored=(0,),
    )


def pair_kernel(keep_ref, first_ref, other_ref, *refs):
    total_ref, own_ref, *sends = refs[-5:]
    rows, width = keep_ref.shape[1:]
    base = 8 * rows
    tall = first_ref.shape[1]
    for flip in range(4):
        total = keep_ref[flip] + joined_lanes(other_ref[flip, :base].astype(F32), 8)
        if flip:
            out = sends[flip - 1]
            out[:base] = lane_blocks(total.astype(BF16))
            out[base : base + tall] = first_ref[flip]
            out[base + tall :] = other_ref[flip, base:]
        else:
            total_ref[...] = total
            own_ref[:tall] = first_ref[0]
            own_ref[tall:] = other_ref[0, base:]


def pair_sum(keep, first, other, after=()):
    rows, width = keep.shape[1:]
    tall = first.shape[1]
    return kernel_call(
        pair_kernel,
        "pair_sum",
        12,
        0.2,
        [keep, first, other],
        [((rows, width), F32), ((2 * tall, 128), BF16)] + [((8 * rows + 2 * tall, 128), BF16)] * 3,
        after=after,
    )


def input_kernel(total_ref, *refs, experts):
    came = refs[:3]
    x_ref, gains_ref, middle_grad_ref, out_ref = refs[3:]
    rows, width = x_ref.shape
    total = total_ref[...]
    for piece in came:
        total = total + joined_lanes(piece[: 8 * rows].astype(F32), 8)
    x = x_ref[...].astype(F32)
    scale = lax.rsqrt(jnp.mean(x * x, axis=1, keepdims=True) + EPSILON)
    normed = x * scale
    inner = total * gains_ref[experts : experts + 1]
    out_ref[...] = middle_grad_ref[...] + scale * (
        inner - normed * jnp.mean(inner * normed, axis=1, keepdims=True)
    )


def input_grad(total, came, x, gains, middle_grad, experts):
    return kernel_call(
        functools.partial(input_kernel, experts=experts),
        "input_grad",
        8,
        0.2,
        [total, *came, x, gains, middle_grad],
        [(middle_grad.shape, F32)],
        held=(4, 6),
        stored=(0,),
    )[0]


def spread_kernel(own_ref, *refs):
    came, output_ref, out_ref = refs[:3], refs[3], refs[4]
    tall = own_ref.shape[0] // 2
    half = tall // 2
    base = came[0].shape[0] - 2 * tall
    size = output_ref.shape[0] // 16
    for piece in range(16):
        flip, place = piece // 4, piece % 4 * half
        source = came[flip - 1][base + place : base + place + half] if flip else own_ref[place : place + half]
        out_ref[piece, :half] = source
        out_ref[piece, half:] = output_ref[piece * size : (piece + 1) * size]


def spread(own, came, output, after=()):
    half = own.shape[0] // 4
    return kernel_call(
        spread_kernel,
        "spread",
        6,
        0.1,
        [own, *came, output],
        [((16, half + output.shape[0] // 16, 128), BF16)],
        after=after,
    )[0]


def sum_kernel(in_ref, out_ref):
    total = in_ref[0].astype(F32)
    for i in range(1, in_ref.shape[0]):
        total = total + in_ref[i].astype(F32)
    total = total.astype(BF16)
    for i in range(in_ref.shape[0]):
        out_ref[i] = total


def sum_all(pieces, after=()):
    return kernel_call(sum_kernel, "sum_all", 6, 0.1, [pieces], [(pieces.shape, BF16)], after=after)[0]


def final_kernel(me_ref, third_ref, wq_ref, wk_ref, wv_ref, gain_ref, *outs, experts, columns):
    query_ref, key_ref, value_ref, output_ref, one_ref, two_ref, gains_ref, router_ref = outs
    rows = third_ref.shape[2]
    tall = (columns + 64) // 2
    q_columns = query_ref.shape[1] // 8
    kv_columns = key_ref.shape[1] // 8
    me = me_ref[0]
    odd = me & 1
    extra = jnp.zeros((64, rows), F32)
    sums = jnp.zeros((rows, 1), F32)
    for flip in range(4):
        pair = []
        for slot in (2 * flip, 2 * flip + 1):
            block = jnp.concatenate(
                [third_ref[2 * slot, :tall], third_ref[2 * slot + 1, :tall]], axis=0
            ).astype(F32)
            turned = block[:columns].T
            span = pl.ds(pl.multiple_of((me ^ slot) * q_columns, q_columns), q_columns)
            query = turned[:, :q_columns]
            query_ref[:, span] = query
            sums = sums + jnp.sum(query * wq_ref[:, span].astype(F32), axis=1, keepdims=True)
            pair.append(turned[:, q_columns:])
            extra = extra + block[columns:]
            for half in range(2):
                size = rows // 2
                output_ref[half * size : (half + 1) * size, slot * rows : (slot + 1) * rows] = third_ref[
                    2 * slot + half, tall:
                ].astype(F32)
        span = pl.ds(pl.multiple_of((me ^ (2 * flip)) // 2 * 2 * kv_columns, 128), 2 * kv_columns)
        first = jnp.where(odd == 1, pair[1], pair[0])
        second = jnp.where(odd == 1, pair[0], pair[1])
        key = jnp.concatenate([first[:, :kv_columns], second[:, :kv_columns]], axis=1)
        value = jnp.concatenate([first[:, kv_columns:], second[:, kv_columns:]], axis=1)
        key_ref[:, span] = key
        value_ref[:, span] = value
        sums = sums + jnp.sum(key * wk_ref[:, span].astype(F32), axis=1, keepdims=True)
        sums = sums + jnp.sum(value * wv_ref[:, span].astype(F32), axis=1, keepdims=True)
    one_ref[...] = jnp.broadcast_to(sums, (rows, 128)).T[:1] / gain_ref[...].astype(F32)
    two_ref[...] = extra[experts : experts + 1]
    gains_ref[...] = extra[experts + 1 : experts + 3]
    router_ref[...] = jnp.concatenate([extra, jnp.zeros((64, rows), F32)], axis=0).T[:, :experts]


def final_grads(me, third, wq, wk, wv, gain, experts, columns):
    rows = third.shape[2]
    return kernel_call(
        functools.partial(final_kernel, experts=experts, columns=columns),
        "final_grads",
        10,
        0.2,
        [me, third, wq, wk, wv, gain],
        [
            (wq.shape, F32),
            (wk.shape, F32),
            (wv.shape, F32),
            ((rows, 8 * rows), F32),
            ((1, rows), F32),
            ((1, rows), F32),
            ((2, rows), F32),
            ((rows, experts), F32),
        ],
        specs=[SMEM] + [VMEM] * 5,
        held=(2, 3, 4, 5),
    )


def send(values, axis, flip):
    count = lax.axis_size(axis)
    return lax.ppermute(values, axis, [(i, i ^ flip) for i in range(count)])


def along_z(values):
    if not isinstance(values, (list, tuple)):
        values = [values] * 3
    return [send(value, "fsdp", 2 * (i + 1)) for i, value in enumerate(values)]


def gather_fsdp(block, name, after=()):
    came = along_z(block)
    return came, send(row([block, *came], name, after), "fsdp", 1)


def exchange(rows):
    return lax.all_to_all(rows, "expert", 0, 0, tiled=True)


def shards(
    tokens,
    lengths,
    routes,
    first_gain,
    query_weight,
    key_weight,
    value_weight,
    output_weight,
    query_gain,
    key_gain,
    second_gain,
    router_weight,
    gate_weight,
    up_weight,
    down_weight,
    cotangent,
):
    own = tokens[0]
    upstream = cotangent[0]
    rows, width = own.shape
    fsdp = lax.axis_size("fsdp")
    owners = lax.axis_size("expert")
    me = lax.axis_index("fsdp").astype(jnp.int32).reshape(1)
    owner = lax.axis_index("expert").astype(jnp.int32).reshape(1)
    experts = router_weight.shape[1]
    capacity = 3 * rows * routes.shape[2] // (2 * experts)
    kv_columns = key_weight.shape[1] // fsdp
    q_columns = query_weight.shape[1] // fsdp
    columns = q_columns + 2 * kv_columns
    q_heads = q_columns // HEAD

    packed = pack_weights(
        me,
        own,
        query_weight,
        key_weight,
        value_weight,
        router_weight,
        first_gain[None],
        second_gain[None],
        query_gain[None],
        key_gain[None],
    )
    x_came = along_z(packed[1:])
    dressed, mask, deal, turn = prepare(routes[0], upstream, experts, capacity)
    x_other = send(relay(own, packed[0], x_came, after=(mask,)), "fsdp", 1)
    c_all = lax.all_gather(dressed, "expert", axis=0)

    ends = jnp.cumsum(lengths[0])
    place = jnp.arange(rows * fsdp, dtype=jnp.int32)
    start = jnp.max(jnp.where(ends[:, None] <= place[None, :], ends[:, None], 0), axis=0)
    position = (place - start).astype(F32)
    frequency = ROPE_BASE ** (-jnp.arange(HEAD // 2, dtype=F32) * 2.0 / HEAD)
    angles = frequency[:, None] * position[None, :]
    cosine, sine = jnp.cos(angles), jnp.sin(angles)
    start = start[None, :].astype(jnp.int32)

    h1, pre, keep, give, inverse, gains, heads, turned, mixed = attention_forward(
        me, own, packed[0], x_came, x_other, cosine, sine, start, experts, q_heads
    )
    wo_came, wo_other = gather_fsdp(output_weight, "row_output", after=(heads,))
    other = send(give, "fsdp", 1)
    mixed_came = along_z(merge(keep, other))
    middle, probs, hidden, sent = middle_layer(
        own, keep, other, mixed_came, output_weight, wo_came, wo_other, gains, deal, experts, owners
    )
    h_rows = exchange(sent)
    rows_c, row_mask, back = deal_rows(owner, c_all, down_weight, experts, capacity)
    rows_back, gate_low, up_low, active, weighted, share = expert_layer(
        owner, h_rows, gains, row_mask, back, gate_weight, up_weight, experts
    )
    came_back = exchange(rows_back)
    *grads, tick = expert_weights(h_rows, rows_c, gate_low, up_low, weighted)
    sums = [lax.psum(grad, "fsdp") for grad in grads]
    gate_sum, up_sum, down_sum = (value.astype(F32) for value in sums)

    middle_grad, middle_low, extra = router_backward(
        came_back, turn, middle, probs, mask, gains, upstream, hidden, experts, after=(tick,)
    )
    da_came, da_other = gather_fsdp(middle_low, "row_middle")
    sent, _ = expert_outputs(active, share, down_weight, owners, after=(extra,))
    layer_out, tick = layer_output(exchange(sent), turn, middle)
    first, output_grad, dh_keep, dh_give = attention_backward(
        me,
        middle_low,
        da_came,
        da_other,
        heads,
        output_weight,
        cosine,
        sine,
        start,
        h1,
        pre,
        mixed,
        inverse,
        turned,
        extra,
        experts,
        q_heads,
    )
    dh_total, first_own, *dh_sends = pair_sum(dh_keep, first, send(dh_give, "fsdp", 1))
    dh_came = along_z(dh_sends)
    second = spread(first_own, dh_came, output_grad, after=(tick, sums[0][0, :8, :128]))
    third = exchange(sum_all(exchange(second)))
    tokens_grad = input_grad(dh_total, dh_came, own, gains, middle_grad, experts)
    query_sum, key_sum, value_sum, output_sum, one_sum, two_sum, gain_sums, router_sum = final_grads(
        me, third, query_weight, key_weight, value_weight, first_gain[None], experts, columns
    )
    step = HEAD // fsdp
    return (
        layer_out[None],
        tokens_grad[None],
        one_sum[0],
        query_sum,
        key_sum,
        value_sum,
        output_sum,
        gain_sums[0, :step],
        gain_sums[1, :step],
        two_sum[0],
        router_sum,
        gate_sum,
        up_sum,
        down_sum,
    )


def solution(mesh):
    whole = P("expert", "fsdp", None)
    rows = P("fsdp", None)
    vector = P("fsdp")
    owned = P("expert", None, None)
    return jax.shard_map(
        shards,
        mesh=mesh,
        in_specs=(
            whole,
            P("expert", None),
            whole,
            vector,
            rows,
            rows,
            rows,
            rows,
            vector,
            vector,
            vector,
            rows,
            owned,
            owned,
            owned,
            whole,
        ),
        out_specs=(
            whole,
            whole,
            vector,
            rows,
            rows,
            rows,
            rows,
            vector,
            vector,
            vector,
            rows,
            owned,
            owned,
            owned,
        ),
        check_vma=False,
    )
```

```python
import functools

import jax
import jax.numpy as jnp
from jax import lax
from jax.experimental import pallas as pl
from jax.experimental.pallas import tpu as pltpu
from jax.sharding import PartitionSpec as P

EPSILON = 1e-06
ROPE_BASE = 10000.0
HEAD = 64
TILE = 256
F32 = jnp.float32
BF16 = jnp.bfloat16
VMEM = pl.BlockSpec(memory_space=pltpu.VMEM)
SMEM = pl.BlockSpec(memory_space=pltpu.SMEM)
ANY = pl.BlockSpec(memory_space=pl.ANY)
HBM = pl.BlockSpec(memory_space=pltpu.HBM)


def dot(left, right, dims=((1,), (0,))):
    return lax.dot_general(left, right, (dims, ((), ())), preferred_element_type=F32)


def shape(extent, dtype):
    return jax.ShapeDtypeStruct(extent, dtype)


def kernel_call(
    body, name, micros, operands, results, smem=0, hbm=(), out_hbm=(), after=(), scratch=(), held=(), late=(), stored=()
):
    held = tuple(held) + tuple(late)
    n, a, r, s = len(operands), len(after), len(results), len(scratch)
    specs = [SMEM if i < smem else HBM if i in held or i in hbm else VMEM for i in range(n)]
    out_specs = [HBM if i in stored or i in out_hbm else VMEM for i in range(r)]
    staged = [pltpu.VMEM(operands[i].shape, operands[i].dtype) for i in held]
    staged += [pltpu.VMEM(*results[i]) for i in stored]
    sems = [pltpu.SemaphoreType.DMA((max(len(held), 1),)), pltpu.SemaphoreType.DMA((max(len(stored), 1),))]

    def wrapped(*refs):
        ins, outs = list(refs[:n]), list(refs[n + a : n + a + r])
        own = refs[n + a + r : n + a + r + s]
        stages, (load_sem, store_sem) = refs[n + a + r + s : -2], refs[-2:]
        loads, stores, begun = {}, {}, []
        for k, i in enumerate(held):
            loads[i] = pltpu.make_async_copy(ins[i], stages[k], load_sem.at[k])
            loads[i].start()
            ins[i] = stages[k]
        for k, i in enumerate(stored):
            stores[i] = pltpu.make_async_copy(stages[len(held) + k], outs[i], store_sem.at[k])
            outs[i] = stages[len(held) + k]
        for i in held:
            if i not in late:
                loads[i].wait()

        def store(*which):
            for i in which:
                stores[i].start()
                begun.append(i)

        extra = {}
        if late:
            extra["wait"] = lambda i: loads[i].wait()
        if stored:
            extra["store"] = store
        body(*ins, *outs, *own, **extra)
        store(*[i for i in stored if i not in begun])
        for i in stored:
            stores[i].wait()

    return pl.pallas_call(
        wrapped,
        out_shape=[shape(*result) for result in results],
        in_specs=specs + [ANY] * a,
        out_specs=out_specs,
        scratch_shapes=list(scratch) + staged + sems,
        compiler_params=pltpu.CompilerParams(vmem_limit_bytes=63 * 1024 * 1024),
        cost_estimate=pl.CostEstimate(flops=0, bytes_accessed=int(micros * 3.6e6), transcendentals=0),
        name=name,
    )(*operands, *after)


def lane_blocks(value):
    return jnp.concatenate([value[:, i : i + 128] for i in range(0, value.shape[1], 128)], axis=0)


def joined_lanes(value, count):
    rows = value.shape[0] // count
    return jnp.concatenate([value[i * rows : (i + 1) * rows] for i in range(count)], axis=1)


def softmax_rows(logits):
    powers = jnp.exp(logits - jnp.max(logits, axis=0, keepdims=True))
    return powers / jnp.sum(powers, axis=0, keepdims=True)


def head_forward(pre, gain, cosine, sine):
    scale = lax.rsqrt(jnp.mean(pre * pre, axis=0, keepdims=True) + EPSILON)
    normed = pre * scale
    scaled = normed * gain
    a, b = scaled[: HEAD // 2], scaled[HEAD // 2 :]
    turned = jnp.concatenate([a * cosine - b * sine, b * cosine + a * sine], axis=0)
    return turned, normed, scale


def head_backward(grad, normed, scale, gain, cosine, sine):
    a, b = grad[: HEAD // 2], grad[HEAD // 2 :]
    unturned = jnp.concatenate([a * cosine + b * sine, b * cosine - a * sine], axis=0)
    gain_grad = jnp.sum(unturned * normed, axis=1, keepdims=True)
    inner = unturned * gain
    pre_grad = scale * (inner - normed * jnp.mean(inner * normed, axis=0, keepdims=True))
    return pre_grad, gain_grad


def prepare_kernel(
    routes_ref, c_ref, dressed_ref, mask_ref, deal_ref, turn_ref, whole_ref, *, experts, capacity, store
):
    rows, width = c_ref.shape
    subs = lax.broadcasted_iota(jnp.int32, (128, rows), 0)
    routed = jnp.zeros((128, rows), F32)
    for route in range(routes_ref.shape[0]):
        routed = routed + jnp.where(routes_ref[route : route + 1] == subs, 1.0, 0.0)
    dressed_ref[:, :width] = c_ref[...]
    dressed_ref[:, width:] = routed.T.astype(BF16)
    store(0)
    mask = routed[:experts]
    mask_ref[...] = mask
    ranks = dot(mask.astype(BF16), earlier(rows))
    slot = lax.broadcasted_iota(jnp.int32, (capacity, rows), 0).astype(F32) + 1.0
    for expert in range(experts):
        one = slice(expert, expert + 1)
        whole_ref[expert * capacity : (expert + 1) * capacity] = jnp.where(
            (ranks[one] == slot) & (mask[one] > 0.5), 1.0, 0.0
        )
    deal_ref[...] = whole_ref[...].astype(BF16)
    for part in range(0, experts * capacity, 128):
        turn_ref[:, part : part + 128] = whole_ref[part : part + 128].T.astype(BF16)


def earlier(rows):
    return (
        lax.broadcasted_iota(jnp.int32, (rows, rows), 0)
        <= lax.broadcasted_iota(jnp.int32, (rows, rows), 1)
    ).astype(BF16)


def prepare(routes, c, experts, capacity):
    rows, width = c.shape
    slots = experts * capacity
    return kernel_call(
        functools.partial(prepare_kernel, experts=experts, capacity=capacity),
        "prepare",
        2.0,
        [routes, c],
        [((rows, width + 128), BF16), ((experts, rows), F32), ((slots, rows), BF16), ((rows, slots), BF16)],
        scratch=[pltpu.VMEM((slots, rows), F32)],
        held=(0, 1),
        stored=(0, 1, 2, 3),
    )


def pack_kernel(me_ref, x_ref, wq_ref, wk_ref, wv_ref, router_ref, one_ref, two_ref, qg_ref, kg_ref, *outs):
    own_ref, sends, parts_ref = outs[0], outs[1:4], outs[4]
    experts, rows = router_ref.shape
    wide = wq_ref.shape[1] // 8
    narrow = wk_ref.shape[1] // 8
    count = qg_ref.shape[1]
    heads = jnp.concatenate([qg_ref[...], kg_ref[...]], axis=0).astype(F32)
    heads = jnp.concatenate([heads, jnp.zeros((2, 128 - count), F32)], axis=1)
    heads = jnp.concatenate([heads, jnp.zeros((126, 128), F32)], axis=0).T[:count]
    small = jnp.concatenate(
        [
            router_ref[...].astype(F32),
            one_ref[...].astype(F32),
            two_ref[...].astype(F32),
            jnp.zeros((6, 128), F32),
            heads,
        ],
        axis=0,
    ).astype(BF16)
    for part in range(8):
        parts_ref[part, :wide] = wq_ref[:, part * wide : (part + 1) * wide].astype(F32).T.astype(BF16)
        parts_ref[part, wide + 2 * narrow :] = small
    for pair in range(4):
        span = slice(pair * 128, (pair + 1) * 128)
        for ref, place in ((wk_ref, wide), (wv_ref, wide + narrow)):
            turned = ref[:, span].astype(F32).T.astype(BF16)
            parts_ref[2 * pair, place : place + narrow] = turned[:narrow]
            parts_ref[2 * pair + 1, place : place + narrow] = turned[narrow:]
    me = me_ref[0]
    tall = parts_ref.shape[1]
    blocks = lane_blocks(x_ref[...])
    base = blocks.shape[0]
    own_ref[:tall] = parts_ref[me]
    own_ref[tall:] = parts_ref[me ^ 1]
    for flip in range(1, 4):
        sends[flip - 1][:base] = blocks
        sends[flip - 1][base : base + tall] = parts_ref[me ^ (2 * flip)]
        sends[flip - 1][base + tall :] = parts_ref[me ^ (2 * flip + 1)]


def pack_weights(me, x, wq, wk, wv, router, one, two, qg, kg):
    tall = (wq.shape[1] + wk.shape[1] + wv.shape[1]) // 8 + router.shape[0] + 16
    base = x.shape[0] * 8
    return kernel_call(
        pack_kernel,
        "pack_weights",
        2.0,
        [me, x, wq, wk, wv, router, one, two, qg, kg],
        [((2 * tall, 128), BF16)] + [((base + 2 * tall, 128), BF16)] * 3,
        smem=1,
        scratch=[pltpu.VMEM((8, tall, 128), BF16)],
        held=range(1, 10),
    )


def relay_kernel(x_ref, own_ref, *refs):
    came, out_ref = refs[:3], refs[3]
    tall = own_ref.shape[0] // 2
    base = came[0].shape[0] - 2 * tall
    out_ref[0, :base] = lane_blocks(x_ref[...])
    out_ref[0, base:] = own_ref[tall:]
    for flip in range(1, 4):
        out_ref[flip, :base] = came[flip - 1][:base]
        out_ref[flip, base:] = came[flip - 1][base + tall :]


def relay(x, own, came, after=()):
    tall = own.shape[0] // 2
    base = came[0].shape[0] - 2 * tall
    return kernel_call(
        relay_kernel, "relay", 1.5, [x, own, *came], [((4, base + tall, 128), BF16)], after=after, held=(0,)
    )[0]


def forward_kernel(me_ref, x_ref, own_ref, *refs, experts, q_heads, store):
    came, other_ref = refs[:3], refs[3]
    cos_ref, sin_ref, start_ref = refs[4:7]
    h1_ref, pre_ref, keep_ref, give_ref, inverse_ref, gains_ref, heads_ref, turned_ref, out_ref = refs[-9:]
    rows, width = x_ref.shape
    q_columns = q_heads * HEAD
    columns = q_columns + 2 * HEAD
    total = rows * 8
    tall = own_ref.shape[0] // 2
    base = 8 * rows
    me = me_ref[0]
    for slot in range(8):
        flip = slot // 2
        if slot % 2:
            piece = other_ref[flip, base:]
        elif flip:
            piece = came[flip - 1][base : base + tall]
        else:
            piece = own_ref[:tall]
        span = pl.ds(pl.multiple_of((me ^ slot) * rows, rows), rows)
        turned_ref[:, span] = piece[:columns]
        small = piece[columns:].astype(F32)
        gains_ref[:, span] = small[: experts + 8]
        heads_ref[pl.ds(pl.multiple_of((me ^ slot) * 8, 8), 8)] = small[experts + 8 :]
    gain_one = gains_ref[experts : experts + 1]
    for slot in range(8):
        flip = slot // 2
        if slot % 2:
            x = joined_lanes(other_ref[flip, :base], 8)
        elif flip:
            x = joined_lanes(came[flip - 1][:base], 8)
        else:
            x = x_ref[...]
        x = x.astype(F32)
        scale = lax.rsqrt(jnp.mean(x * x, axis=1, keepdims=True) + EPSILON)
        h1_ref[slot] = (x * scale * gain_one).astype(BF16)
    store(0, 6, 7)
    for slot in range(8):
        block = dot(turned_ref[...], h1_ref[slot], ((1,), (1,)))
        place = pl.multiple_of((me ^ slot) * rows, rows)
        pre_ref[:, pl.ds(place, rows)] = block
    store(1)
    cosine, sine = cos_ref[...], sin_ref[...]
    gain_query, gain_key = heads_ref[:, :1], heads_ref[:, 1:2]
    key = head_forward(pre_ref[q_columns : q_columns + HEAD], gain_key, cosine, sine)[0]
    key = key.T.astype(BF16)
    value = pre_ref[q_columns + HEAD :].astype(BF16)
    inverse_ref[...] = jnp.zeros(inverse_ref.shape, F32)
    for head in range(q_heads):
        query = head_forward(pre_ref[head * HEAD : (head + 1) * HEAD], gain_query, cosine, sine)[0]
        query = query.astype(BF16) * jnp.array(HEAD ** (-0.5), BF16)
        for tile in range(total // TILE):
            low, high = tile * TILE, (tile + 1) * TILE
            scores = dot(key[:high], query[:, low:high])
            u = lax.broadcasted_iota(jnp.int32, (high, TILE), 0)
            t = lax.broadcasted_iota(jnp.int32, (high, TILE), 1) + low
            allowed = (u >= start_ref[:, low:high]) & (u <= t)
            powers = jnp.where(allowed, jnp.exp(scores), 0.0)
            inverse = 1.0 / jnp.sum(powers, axis=0, keepdims=True)
            probs = (powers * inverse).astype(BF16)
            mixed = dot(value[:, :high], probs).astype(BF16)
            inverse_ref[head : head + 1, low:high] = inverse
            for part in range(TILE // rows):
                out_ref[low // rows + part, head * HEAD : (head + 1) * HEAD] = mixed[
                    :, part * rows : (part + 1) * rows
                ]
    for slot in range(8):
        (give_ref if slot % 2 else keep_ref)[slot // 2] = out_ref[me ^ slot]


def attention_forward(me, x, own, came, other, cosine, sine, start, experts, q_heads):
    rows, width = x.shape
    total = 8 * rows
    columns = (q_heads + 2) * HEAD
    q_columns = q_heads * HEAD
    return kernel_call(
        functools.partial(forward_kernel, experts=experts, q_heads=q_heads),
        "attention_forward",
        7.0,
        [me, x, own, *came, other, cosine, sine, start],
        [
            ((8, rows, width), BF16),
            ((columns, total), F32),
            ((4, q_columns, rows), BF16),
            ((4, q_columns, rows), BF16),
            ((8, total), F32),
            ((experts + 8, width), F32),
            ((HEAD, 128), F32),
            ((columns, width), BF16),
            ((8, q_columns, rows), BF16),
        ],
        smem=1,
        held=(1,),
        stored=(0, 1, 4, 6, 7, 8),
    )


def merge_kernel(keep_ref, came_ref, *outs):
    for flip in range(1, 4):
        outs[flip - 1][0] = keep_ref[flip]
        outs[flip - 1][1] = came_ref[flip]


def merge(keep, came):
    extent = ((2,) + keep.shape[1:], BF16)
    return kernel_call(merge_kernel, "merge", 0.6, [keep, came], [extent] * 3)


def middle_kernel(x_ref, keep_ref, other_ref, *refs, experts, wait, store):
    came, wo_ref, wo_came, wo_other_ref, gains_ref, deal_ref = refs[:3], refs[3], refs[4:7], refs[7], refs[8], refs[9]
    middle_ref, probs_ref, hidden_ref, sent_ref, mixed_ref, whole_ref, out_ref, out_sem = refs[10:]
    rows, width = x_ref.shape
    for slot in range(8):
        flip, core = slot // 2, slot % 2
        if flip:
            piece = came[flip - 1][core]
        else:
            piece = (other_ref if core else keep_ref)[0]
        span = slice(slot * 128, (slot + 1) * 128)
        mixed_ref[:, span] = piece.astype(F32).T.astype(BF16)
        if core:
            whole_ref[span] = wo_other_ref[flip]
        else:
            whole_ref[span] = (wo_came[flip - 1] if flip else wo_ref)[...]
    middle = x_ref[...].astype(F32) + dot(mixed_ref[...], whole_ref[...])
    middle_ref[...] = middle
    scale = lax.rsqrt(jnp.mean(middle * middle, axis=1, keepdims=True) + EPSILON)
    hidden = (middle * scale * gains_ref[experts + 1 : experts + 2]).astype(BF16)
    hidden_ref[...] = hidden
    probs_ref[...] = softmax_rows(dot(gains_ref[:experts].astype(BF16), hidden, ((1,), (1,))))
    store(0, 2)
    owners, per_owner, capacity, _ = sent_ref.shape
    group = owners // 4
    size = group * per_owner * capacity
    copies = []
    wait(12)
    for part in range(4):
        taken = dot(deal_ref[part * size : (part + 1) * size], hidden).astype(BF16)
        blocks = slice(group * part, group * (part + 1))
        out_ref[blocks] = taken.reshape(group, per_owner, capacity, width)
        copies.append(pltpu.make_async_copy(out_ref.at[blocks], sent_ref.at[blocks], out_sem.at[part]))
        copies[-1].start()
    for copy in copies:
        copy.wait()


def middle_layer(x, keep, other, came, wo, wo_came, wo_other, gains, deal, experts, owners):
    rows, width = x.shape
    per_owner = experts // owners
    capacity = deal.shape[0] // experts
    sent = ((owners, per_owner, capacity, width), BF16)
    return kernel_call(
        functools.partial(middle_kernel, experts=experts),
        "middle_layer",
        3.0,
        [x, keep, other, *came, wo, *wo_came, wo_other, gains, deal],
        [((rows, width), F32), ((experts, rows), F32), ((rows, width), BF16), sent],
        out_hbm=(3,),
        scratch=[
            pltpu.VMEM((rows, width), BF16),
            pltpu.VMEM((width, width), BF16),
            pltpu.VMEM(*sent),
            pltpu.SemaphoreType.DMA((4,)),
        ],
        held=(0, 6),
        late=(12,),
        stored=(0, 2),
    )


def row_kernel(*refs):
    for i, ref in enumerate(refs[:-1]):
        refs[-1][i] = ref[...]


def row(pieces, name, after=()):
    return kernel_call(
        row_kernel, name, 0.8, pieces, [((len(pieces),) + pieces[0].shape, BF16)], after=after
    )[0]


def backward_kernel(me_ref, own_da_ref, *refs, experts, q_heads, wait):
    came, other_ref = refs[:3], refs[3]
    heads_ref, wo_ref, cos_ref, sin_ref, start_ref = refs[4:9]
    h1_ref, pre_ref, mixed_ref, inverse_ref, turned_ref, extra_ref = refs[9:15]
    first_ref, keep_ref, send_ref = refs[-10:-7]
    da_ref, mixed_grad_ref, dkey_ref, dvalue_ref, low_ref, out_slots_ref, grad_ref = refs[-7:]
    rows, width = own_da_ref.shape
    q_columns = q_heads * HEAD
    columns = q_columns + 2 * HEAD
    total = rows * 8
    me = me_ref[0]
    for slot in range(8):
        flip, core = slot // 2, slot % 2
        if core:
            piece = other_ref[flip]
        else:
            piece = (came[flip - 1] if flip else own_da_ref)[...]
        span = slice(slot * rows, (slot + 1) * rows)
        da_ref[span] = piece
        place = pl.multiple_of((me ^ slot) * rows, rows)
        mixed_grad_ref[:, pl.ds(place, rows)] = dot(wo_ref[...], piece, ((1,), (1,))).astype(BF16)
    wait(13)
    for slot in range(8):
        out_slots_ref[:, slot * rows : (slot + 1) * rows] = mixed_ref[me ^ slot]
    wo_grad = dot(out_slots_ref[...], da_ref[...]).astype(BF16)
    wo_grad = lane_blocks(wo_grad)
    wait(12)
    wait(14)
    gain_query, gain_key = heads_ref[:, :1], heads_ref[:, 1:2]
    cosine, sine = cos_ref[...], sin_ref[...]
    key_turned, key_normed, key_scale = head_forward(
        pre_ref[q_columns : q_columns + HEAD], gain_key, cosine, sine
    )
    key_low = key_turned.astype(BF16)
    key = key_turned.T.astype(BF16)
    value = pre_ref[q_columns + HEAD :].T.astype(BF16)
    dkey_ref[...] = jnp.zeros(dkey_ref.shape, F32)
    dvalue_ref[...] = jnp.zeros(dvalue_ref.shape, F32)
    gain_query_grad = jnp.zeros((HEAD, 1), F32)
    pieces = []
    for head in range(q_heads):
        span = slice(head * HEAD, (head + 1) * HEAD)
        turned, normed, scale = head_forward(pre_ref[span], gain_query, cosine, sine)
        query = turned.astype(BF16) * jnp.array(HEAD ** (-0.5), BF16)
        grads = []
        for tile in range(total // TILE):
            low, high = tile * TILE, (tile + 1) * TILE
            part = query[:, low:high]
            mixed_grad = mixed_grad_ref[span, low:high]
            scores = dot(key[:high], part)
            u = lax.broadcasted_iota(jnp.int32, (high, TILE), 0)
            t = lax.broadcasted_iota(jnp.int32, (high, TILE), 1) + low
            allowed = (u >= start_ref[:, low:high]) & (u <= t)
            probs = jnp.where(allowed, jnp.exp(scores) * inverse_ref[head : head + 1, low:high], 0.0)
            attend = dot(value[:high], mixed_grad)
            delta = jnp.sum(probs * attend, axis=0, keepdims=True)
            score_low = (probs * (attend - delta)).astype(BF16)
            grads.append(dot(key_low[:, :high], score_low))
            dkey_ref[:, :high] += dot(part, score_low, ((1,), (1,)))
            dvalue_ref[:, :high] += dot(mixed_grad, probs.astype(BF16), ((1,), (1,)))
        query_grad = jnp.concatenate(grads, axis=1) * HEAD ** (-0.5)
        pre_grad, gain_grad = head_backward(query_grad, normed, scale, gain_query, cosine, sine)
        gain_query_grad += gain_grad
        pieces.append(pre_grad)
    pre_grad, gain_key_grad = head_backward(
        dkey_ref[...], key_normed, key_scale, gain_key, cosine, sine
    )
    pieces += [pre_grad, dvalue_ref[...]]
    pre_grad = jnp.concatenate(pieces, axis=0)
    low_ref[...] = pre_grad.astype(BF16)
    slots_grad = []
    for slot in range(8):
        place = pl.multiple_of((me ^ slot) * rows, rows)
        slots_grad.append(low_ref[:, pl.ds(place, rows)])
    slots_grad = jnp.concatenate(slots_grad, axis=1)
    wait(11)
    wait(15)
    grad_ref[:columns] = dot(slots_grad, h1_ref[...].reshape(total, width))
    extra = extra_ref[...]
    lane = lax.broadcasted_iota(jnp.int32, (HEAD, 128), 1)
    gains = jnp.where(lane == 0, gain_query_grad, jnp.where(lane == 1, gain_key_grad, 0.0))
    gains = gains.T[:2]
    step = HEAD // 8
    grad_ref[columns:] = jnp.zeros((64, width), F32)
    grad_ref[columns : columns + experts + 1] = extra[: experts + 1]
    for part in range(8):
        grad_ref[columns + experts + 1 : columns + experts + 3, part * rows : part * rows + step] = gains[
            :, part * step : (part + 1) * step
        ]
    for piece in range(16):
        spare = []
        place = columns + piece * SPARE
        for part in range(8):
            span = slice(part * rows, (part + 1) * rows)
            block = grad_ref[piece * PIECE : (piece + 1) * PIECE, span]
            first_ref[piece, part * PIECE : (part + 1) * PIECE] = block.astype(BF16)
            spare.append(grad_ref[place : place + SPARE, span])
        spare.append(jnp.zeros((2 * PIECE - 8 * SPARE, 128), F32))
        first_ref[piece, 8 * PIECE : 10 * PIECE] = jnp.concatenate(spare, axis=0).astype(BF16)
        first_ref[piece, 10 * PIECE :] = wo_grad[piece * SLICE : (piece + 1) * SLICE]
    turned = turned_ref[...]
    for slot in range(8):
        low_rows_slot = slots_grad[:, slot * rows : (slot + 1) * rows].astype(F32).T.astype(BF16)
        part = dot(low_rows_slot, turned)
        if slot % 2:
            send_ref[slot // 2] = part.astype(BF16)
        else:
            keep_ref[slot // 2] = part


def attention_backward(
    me, da, came, other, heads, wo, cosine, sine, start, h1, pre, mixed, inverse, turned, extra, experts, q_heads, after=()
):
    rows, width = da.shape
    total = 8 * rows
    columns = pre.shape[0]
    q_columns = q_heads * HEAD
    return kernel_call(
        functools.partial(backward_kernel, experts=experts, q_heads=q_heads),
        "attention_backward",
        12,
        [me, da, *came, other, heads, wo, cosine, sine, start, h1, pre, mixed, inverse, turned, extra],
        [
            ((16, 10 * PIECE + SLICE, 128), BF16),
            ((4, rows, width), F32),
            ((4, rows, width), BF16),
        ],
        smem=1,
        after=after,
        held=(6, 7),
        late=(11, 12, 13, 14, 15),
        scratch=[
            pltpu.VMEM((total, width), BF16),
            pltpu.VMEM((q_columns, total), BF16),
            pltpu.VMEM((HEAD, total), F32),
            pltpu.VMEM((HEAD, total), F32),
            pltpu.VMEM((columns, total), BF16),
            pltpu.VMEM((q_columns, total), BF16),
            pltpu.VMEM((columns + 64, width), F32),
        ],
    )


def deal_kernel(owner_ref, c_ref, down_ref, rows_c, mask_ref, back_ref, c_scratch, sems, *, experts, capacity, wait, store):
    owner = owner_ref[0]
    per_owner, hidden, width = down_ref.shape
    rows = c_ref.shape[1]
    loads = [pltpu.make_async_copy(c_ref.at[i], c_scratch.at[i], sems.at[i]) for i in range(16)]
    for load in loads:
        load.start()
    lanes = lax.broadcasted_iota(jnp.int32, (experts, 128), 1)
    subs = lax.broadcasted_iota(jnp.int32, (experts, 128), 0)
    eye = (lanes == subs).astype(BF16)
    before = earlier(rows)
    mine_of = lax.broadcasted_iota(jnp.int32, (experts, rows), 0) - owner * per_owner
    slot = lax.broadcasted_iota(jnp.int32, (capacity, rows), 0).astype(F32) + 1.0
    for block in range(16):
        loads[block].wait()
        c = c_scratch[block]
        mask = dot(eye, c[:, width:], ((1,), (1,)))
        ranks = dot(mask.astype(BF16), before)
        deals = []
        for k in range(per_owner):
            mine = mine_of == k
            hit = jnp.sum(jnp.where(mine, mask, 0.0), axis=0, keepdims=True)
            rank = jnp.sum(jnp.where(mine, ranks, 0.0), axis=0, keepdims=True)
            deals.append(jnp.where((rank == slot) & (hit > 0.5), 1.0, 0.0))
        taken = dot(jnp.concatenate(deals, axis=0).astype(BF16), c).astype(BF16)
        span = slice(block * capacity, (block + 1) * capacity)
        for k in range(per_owner):
            spot = slice(k * capacity, (k + 1) * capacity)
            rows_c[k, span] = taken[spot, :width]
            mask_ref[k, span] = taken[spot, width:]
    store(0, 1)
    wait(2)
    for k in range(per_owner):
        for tile in range(16 * capacity // TILE):
            span = slice(tile * TILE, (tile + 1) * TILE)
            back_ref[k, span] = dot(rows_c[k, span], down_ref[k], ((1,), (1,)))


def deal_rows(owner, c, down, experts, capacity):
    per_owner, hidden, width = down.shape
    count = 16 * capacity
    return kernel_call(
        functools.partial(deal_kernel, experts=experts, capacity=capacity),
        "deal_rows",
        12.0,
        [owner, c, down],
        [
            ((per_owner, count, width), BF16),
            ((per_owner, count, 128), BF16),
            ((per_owner, count, hidden), F32),
        ],
        smem=1,
        hbm=(1,),
        scratch=[pltpu.VMEM(c.shape, BF16), pltpu.SemaphoreType.DMA((16,))],
        late=(2,),
        stored=(0, 1, 2),
    )


def expert_kernel(
    owner_ref,
    h_hbm,
    gains_ref,
    mask_ref,
    back_hbm,
    gate_hbm,
    up_hbm,
    rows_hbm,
    gate_out,
    up_out,
    active_out,
    weighted_out,
    share_ref,
    h_ref,
    back_in,
    gate_ref,
    up_ref,
    rows_back,
    load_sem,
    store_sem,
    *,
    experts,
    store,
):
    owners, per_owner, capacity, width = h_hbm.shape
    group = 8
    parts = owners // group
    size = group * capacity
    loads = {}
    for k in range(per_owner):
        for part in range(parts):
            blocks = slice(part * group, (part + 1) * group)
            spot = (k * parts + part) * 4
            loads[k, part] = [
                pltpu.make_async_copy(h_hbm.at[blocks, k], h_ref.at[blocks, k], load_sem.at[spot]),
                pltpu.make_async_copy(
                    back_hbm.at[k, part * size : (part + 1) * size],
                    back_in.at[k, part * size : (part + 1) * size],
                    load_sem.at[spot + 1],
                ),
            ]
            if part == 0:
                loads[k, part] += [
                    pltpu.make_async_copy(gate_hbm.at[k], gate_ref.at[k], load_sem.at[spot + 2]),
                    pltpu.make_async_copy(up_hbm.at[k], up_ref.at[k], load_sem.at[spot + 3]),
                ]
            for load in loads[k, part]:
                load.start()
    owner = owner_ref[0]
    router = jnp.concatenate([gains_ref[:experts], jnp.zeros((128 - experts, width), F32)], axis=0)
    router = router.astype(BF16)
    lane = lax.broadcasted_iota(jnp.int32, (size, 128), 1)
    copies = []
    for k in range(per_owner):
        place = owner * per_owner + k
        for part in range(parts):
            blocks = slice(part * group, (part + 1) * group)
            span = slice(part * size, (part + 1) * size)
            for load in loads[k, part]:
                load.wait()
            h = h_ref[blocks, k].reshape(size, width)
            gate = dot(h, gate_ref[k])
            up = dot(h, up_ref[k])
            logits = dot(h, router, ((1,), (1,)))
            chosen = mask_ref[k, span] > 0.5
            top = jnp.max(jnp.where(chosen, logits, -1e30), axis=1, keepdims=True)
            powers = jnp.where(chosen, jnp.exp(logits - top), 0.0)
            total = jnp.sum(powers, axis=1, keepdims=True)
            share = jnp.sum(jnp.where(lane == place, powers, 0.0), axis=1, keepdims=True)
            share = share / jnp.where(total > 0.0, total, 1.0)
            share_ref[k, span] = jnp.broadcast_to(share, (size, 128))
            back = back_in[k, span]
            sig = 1.0 / (1.0 + jnp.exp(-gate))
            silu = gate * sig
            active = silu * up
            active_low = active.astype(BF16)
            route_grad = jnp.sum(active_low.astype(F32) * back, axis=1, keepdims=True)
            grad = back * share
            gate_low = (grad * up * (sig + silu * (1.0 - sig))).astype(BF16)
            up_low = (grad * silu).astype(BF16)
            active_out[k, span] = active_low
            weighted_out[k, span] = (active * share).astype(BF16)
            gate_out[k, span] = gate_low
            up_out[k, span] = up_low
            rows = dot(gate_low, gate_ref[k], ((1,), (1,))) + dot(up_low, up_ref[k], ((1,), (1,)))
            high = route_grad.astype(BF16).astype(F32)
            spread_out = jnp.where(lane == place, high, 0.0)
            spread_out = jnp.where(lane == place + experts, route_grad - high, spread_out)
            whole = jnp.concatenate([rows.astype(BF16), spread_out.astype(BF16)], axis=1)
            rows_back[blocks, k] = whole.reshape(group, capacity, width + 128)
            copies.append(
                pltpu.make_async_copy(
                    rows_back.at[blocks, k], rows_hbm.at[blocks, k], store_sem.at[k * parts + part]
                )
            )
            copies[-1].start()
    store(1, 2, 3, 4, 5)
    for copy in copies:
        copy.wait()


def expert_layer(owner, h, gains, mask, back, gate, up, experts):
    per_owner, width, hidden = gate.shape
    owners, _, capacity, _ = h.shape
    count = owners * capacity
    narrow = ((per_owner, count, hidden), BF16)
    rows_back = ((owners, per_owner, capacity, width + 128), BF16)
    pieces = per_owner * (owners // 8)
    return kernel_call(
        functools.partial(expert_kernel, experts=experts),
        "expert_layer",
        14.0,
        [owner, h, gains, mask, back, gate, up],
        [rows_back] + [narrow] * 4 + [((per_owner, count, 128), F32)],
        smem=1,
        hbm=(1, 4, 5, 6),
        out_hbm=(0,),
        scratch=[pltpu.VMEM(value.shape, value.dtype) for value in (h, back, gate, up)]
        + [pltpu.VMEM(*rows_back), pltpu.SemaphoreType.DMA((4 * pieces,)), pltpu.SemaphoreType.DMA((pieces,))],
        stored=(1, 2, 3, 4, 5),
    )


def weights_kernel(h_ref, rows_c, gate_low, up_low, weighted, out_ref, tick_ref, *, wait, store):
    tick_ref[...] = jnp.zeros(tick_ref.shape, F32)
    first = ((0,), (0,))
    owners, per_owner, capacity, width = h_ref.shape
    hidden = gate_low.shape[2]
    half = width // 2
    for i in (0, 2, 3):
        wait(i)
    for k in range(per_owner):
        rows_h = h_ref[:, k].reshape(owners * capacity, width)
        for place, low in ((k, gate_low), (per_owner + k, up_low)):
            total = dot(rows_h, low[k], first).astype(BF16)
            out_ref[place, :, :hidden] = total[:half]
            out_ref[place, :, hidden:] = total[half:]
        if k == 0:
            wait(1)
            wait(4)
        out_ref[2 * per_owner + k] = dot(weighted[k], rows_c[k], first).astype(BF16)


def expert_weights(h, rows_c, gate_low, up_low, weighted):
    per_owner, count, width = rows_c.shape
    hidden = gate_low.shape[2]
    return kernel_call(
        weights_kernel,
        "expert_weights",
        0.1,
        [h, rows_c, gate_low, up_low, weighted],
        [((3 * per_owner, hidden, width), BF16), ((8, 128), F32)],
        late=(0, 1, 2, 3, 4),
        stored=(0,),
    )


def widen_kernel(low_ref, gate_ref, up_ref, down_ref):
    step = pl.program_id(0)
    hidden = gate_ref.shape[2]
    value = low_ref[0].astype(F32)
    half = value.shape[0]
    for place, ref in ((0, gate_ref), (1, up_ref)):

        @pl.when(step // 2 == place)
        def _():
            ref[0, :half] = value[:, :hidden]
            ref[0, half:] = value[:, hidden:]

    @pl.when(step // 2 == 2)
    def _():
        down_ref[0] = value


def widen(low):
    count, hidden, width = low.shape
    per_owner = count // 3

    def spot(place):
        return lambda i: (jnp.clip(i - place * per_owner, 0, per_owner - 1), 0, 0)

    return pl.pallas_call(
        widen_kernel,
        grid=(count,),
        out_shape=[shape((per_owner, width, hidden), F32)] * 2 + [shape((per_owner, hidden, width), F32)],
        in_specs=[pl.BlockSpec((1, hidden, width), lambda i: (i, 0, 0))],
        out_specs=[
            pl.BlockSpec((1, width, hidden), spot(0)),
            pl.BlockSpec((1, width, hidden), spot(1)),
            pl.BlockSpec((1, hidden, width), spot(2)),
        ],
        compiler_params=pltpu.CompilerParams(vmem_limit_bytes=63 * 1024 * 1024),
        cost_estimate=pl.CostEstimate(flops=0, bytes_accessed=24_000_000, transcendentals=0),
        name="widen",
    )(low)


def outputs_kernel(active, share, down_ref, sent_ref, tick_ref, out_ref, out_sem, *, wait):
    tick_ref[...] = jnp.zeros(tick_ref.shape, F32)
    per_owner, count, hidden = active.shape
    owners, _, capacity, width = sent_ref.shape
    group = 8
    size = group * capacity
    copies = []
    for i in range(3):
        wait(i)
    for k in range(per_owner):
        for part in range(owners // group):
            span = slice(part * size, (part + 1) * size)
            blocks = slice(part * group, (part + 1) * group)
            produced = dot(active[k, span], down_ref[k]).astype(BF16).astype(F32)
            produced = (produced * share[k, span, :1]).astype(BF16)
            out_ref[blocks, k] = produced.reshape(group, capacity, width)
            copies.append(
                pltpu.make_async_copy(
                    out_ref.at[blocks, k], sent_ref.at[blocks, k], out_sem.at[k * (owners // group) + part]
                )
            )
            copies[-1].start()
    for copy in copies:
        copy.wait()


def expert_outputs(active, share, down, owners, after=()):
    per_owner, count, hidden = active.shape
    width = down.shape[2]
    sent = ((owners, per_owner, count // owners, width), BF16)
    return kernel_call(
        outputs_kernel,
        "expert_outputs",
        0.1,
        [active, share, down],
        [sent, ((8, 128), F32)],
        out_hbm=(0,),
        after=after,
        scratch=[pltpu.VMEM(*sent), pltpu.SemaphoreType.DMA((per_owner * (owners // 8),))],
        late=(0, 1, 2),
    )


def combined(rows_hbm, rows_ref, sems, turn_ref, ready):
    owners, per_owner, capacity, wide = rows_hbm.shape
    group = owners // 4
    size = group * per_owner * capacity
    loads = []
    for part in range(4):
        blocks = slice(part * group, (part + 1) * group)
        loads.append(pltpu.make_async_copy(rows_hbm.at[blocks], rows_ref.at[blocks], sems.at[part]))
        loads[-1].start()
    ready()
    total = None
    for part in range(4):
        loads[part].wait()
        rows = rows_ref[part * group : (part + 1) * group].reshape(size, wide)
        one = dot(turn_ref[:, part * size : (part + 1) * size], rows)
        total = one if total is None else total + one
    return total


def output_kernel(rows_hbm, turn_ref, middle_ref, out_ref, tick_ref, rows_ref, sems, *, wait, store):
    tick_ref[...] = jnp.zeros(tick_ref.shape, F32)
    total = combined(rows_hbm, rows_ref, sems, turn_ref, lambda: wait(1))
    wait(2)
    out_ref[...] = (middle_ref[...] + total).astype(BF16)


def layer_output(rows, turn, middle):
    return kernel_call(
        output_kernel,
        "layer_output",
        3,
        [rows, turn, middle],
        [(middle.shape, BF16), ((8, 128), F32)],
        hbm=(0,),
        scratch=[pltpu.VMEM(rows.shape, BF16), pltpu.SemaphoreType.DMA((4,))],
        late=(1, 2),
        stored=(0,),
    )


def router_kernel(
    rows_hbm,
    turn_ref,
    middle_ref,
    probs_ref,
    mask_ref,
    gains_ref,
    c_ref,
    hidden_ref,
    grad_ref,
    send_ref,
    extra_ref,
    rows_ref,
    sems,
    *,
    experts,
    wait,
    store,
):
    rows, width = middle_ref.shape
    returned = combined(rows_hbm, rows_ref, sems, turn_ref, lambda: wait(1))
    for i in (2, 4, 6, 7):
        wait(i)
    tail = returned[:, width:].T
    route_grad = tail[:experts] + tail[experts : 2 * experts]
    mask = mask_ref[...]
    probs = probs_ref[...]
    picked = probs * mask
    picked_sum = jnp.sum(picked, axis=0, keepdims=True)
    share = picked / picked_sum
    picked_grad = (route_grad - jnp.sum(route_grad * share, axis=0, keepdims=True)) / picked_sum
    prob_grad = mask * picked_grad
    logit_grad = probs * (prob_grad - jnp.sum(probs * prob_grad, axis=0, keepdims=True))
    extra_ref[:experts] = dot(logit_grad.astype(BF16), hidden_ref[...])
    logit_rows = jnp.concatenate([logit_grad, jnp.zeros((128 - experts, rows), F32)], axis=0).T
    router = gains_ref[:experts].astype(BF16)
    hidden_grad = returned[:, :width] + dot(logit_rows[:, :experts].astype(BF16), router)
    middle = middle_ref[...]
    scale = lax.rsqrt(jnp.mean(middle * middle, axis=1, keepdims=True) + EPSILON)
    normed = middle * scale
    extra_ref[experts : experts + 8] = jnp.broadcast_to(
        jnp.sum(hidden_grad * normed, axis=0, keepdims=True), (8, width)
    )
    inner = hidden_grad * gains_ref[experts + 1 : experts + 2]
    grad = c_ref[...].astype(F32) + scale * (
        inner - normed * jnp.mean(inner * normed, axis=1, keepdims=True)
    )
    grad_ref[...] = grad
    send_ref[...] = grad.astype(BF16)


def router_backward(rows_back, turn, middle, probs, mask, gains, c, hidden, experts, after=()):
    rows, width = middle.shape
    return kernel_call(
        functools.partial(router_kernel, experts=experts),
        "router_backward",
        5,
        [rows_back, turn, middle, probs, mask, gains, c, hidden],
        [((rows, width), F32), ((rows, width), BF16), ((experts + 8, width), F32)],
        hbm=(0,),
        after=after,
        scratch=[pltpu.VMEM(rows_back.shape, BF16), pltpu.SemaphoreType.DMA((4,))],
        late=(1, 2, 4, 6, 7),
        stored=(0,),
    )


def pair_kernel(keep_ref, other_ref, total_ref, *sends):
    for flip in range(4):
        total = keep_ref[flip] + other_ref[flip].astype(F32)
        if flip:
            sends[flip - 1][...] = total.astype(BF16)
        else:
            total_ref[...] = total


def pair_sum(keep, other):
    rows, width = keep.shape[1:]
    return kernel_call(
        pair_kernel, "pair_sum", 1.2, [keep, other], [((rows, width), F32)] + [((rows, width), BF16)] * 3
    )


def input_kernel(total_ref, *refs, experts, store):
    came = refs[:3]
    x_ref, gains_ref, middle_grad_ref, out_ref = refs[3:]
    total = total_ref[...]
    for piece in came:
        total = total + piece[...].astype(F32)
    x = x_ref[...].astype(F32)
    scale = lax.rsqrt(jnp.mean(x * x, axis=1, keepdims=True) + EPSILON)
    normed = x * scale
    inner = total * gains_ref[experts : experts + 1]
    out_ref[...] = middle_grad_ref[...] + scale * (
        inner - normed * jnp.mean(inner * normed, axis=1, keepdims=True)
    )


def input_grad(total, came, x, gains, middle_grad, experts):
    return kernel_call(
        functools.partial(input_kernel, experts=experts),
        "input_grad",
        2,
        [total, *came, x, gains, middle_grad],
        [(middle_grad.shape, F32)],
        held=(4, 6),
        stored=(0,),
    )[0]


PIECE, SPARE, SLICE = 16, 3, 64


def pass_kernel(in_ref, out_ref):
    out_ref[...] = in_ref[...]


def passed(value, after):
    return kernel_call(pass_kernel, "passed", 0.5, [value], [(value.shape, value.dtype)], after=after)[0]


def shares_kernel(pieces_ref, out_ref, rest_ref):
    total = pieces_ref[0].astype(F32)
    for i in range(1, pieces_ref.shape[0]):
        total = total + pieces_ref[i].astype(F32)
    base = 8 * PIECE
    fill = jnp.zeros((PIECE - SPARE, 128), F32)
    for part in range(8):
        out_ref[part, :PIECE] = total[part * PIECE : (part + 1) * PIECE].astype(BF16)
        spare = total[base + part * SPARE : base + (part + 1) * SPARE]
        out_ref[part, PIECE:] = jnp.concatenate([spare, fill], axis=0).astype(BF16)
    rest_ref[...] = total[base + 2 * PIECE :].astype(BF16)


def shares_sum(pieces, after=()):
    return kernel_call(
        shares_kernel,
        "shares_sum",
        0.1,
        [pieces],
        [((8, 2 * PIECE, 128), BF16), ((SLICE, 128), BF16)],
        after=after,
    )


def whole_kernel(came_ref, rest_ref, out_ref):
    spare = came_ref[0, PIECE:].astype(F32)
    for i in range(1, 8):
        spare = spare + came_ref[i, PIECE:].astype(F32)
    rows = [came_ref[i, :PIECE] for i in range(8)] + [spare.astype(BF16), rest_ref[...]]
    rows = jnp.concatenate(rows, axis=0)
    for i in range(16):
        out_ref[i] = rows


def whole_pieces(came, rest):
    return kernel_call(
        whole_kernel, "whole_pieces", 0.1, [came, rest], [((16, 9 * PIECE + SLICE, 128), BF16)]
    )[0]


def final_kernel(pieces_ref, wq_ref, wk_ref, wv_ref, gain_ref, *outs, experts):
    query_ref, key_ref, value_ref, output_ref, one_ref, two_ref, gains_ref, router_ref = outs
    rows = pieces_ref.shape[2]
    q_columns = query_ref.shape[1] // 8
    kv_columns = key_ref.shape[1] // 8
    sums = jnp.zeros((rows, 1), F32)
    base = 8 * PIECE
    for pair in range(4):
        keys, values = [], []
        for source in (2 * pair, 2 * pair + 1):
            block = [pieces_ref[i, source * PIECE : (source + 1) * PIECE] for i in range(16)]
            turned = jnp.concatenate(block, axis=0).astype(F32).T
            span = slice(source * q_columns, (source + 1) * q_columns)
            query = turned[:, :q_columns]
            query_ref[:, span] = query
            sums = sums + jnp.sum(query * wq_ref[:, span].astype(F32), axis=1, keepdims=True)
            keys.append(turned[:, q_columns : q_columns + kv_columns])
            values.append(turned[:, q_columns + kv_columns :])
        span = slice(2 * pair * kv_columns, 2 * (pair + 1) * kv_columns)
        for parts, ref, weight in ((keys, key_ref, wk_ref), (values, value_ref, wv_ref)):
            both = jnp.concatenate(parts, axis=1)
            ref[:, span] = both
            sums = sums + jnp.sum(both * weight[:, span].astype(F32), axis=1, keepdims=True)
    for i in range(16):
        half = i % 2 * SLICE
        output_ref[half : half + SLICE, i // 2 * rows : (i // 2 + 1) * rows] = pieces_ref[
            i, base + PIECE :
        ].astype(F32)
    spare = pieces_ref[:, base : base + PIECE].astype(F32)
    spare = jnp.concatenate([spare[i, :SPARE] for i in range(16)], axis=0)
    one_ref[...] = jnp.broadcast_to(sums, (rows, 128)).T[:1] / gain_ref[...].astype(F32)
    two_ref[...] = spare[experts : experts + 1]
    gains_ref[...] = spare[experts + 1 : experts + 3]
    router_ref[...] = spare[:experts]


def final_grads(pieces, wq, wk, wv, gain, experts):
    rows = pieces.shape[2]
    return kernel_call(
        functools.partial(final_kernel, experts=experts),
        "final_grads",
        0.2,
        [pieces, wq, wk, wv, gain],
        [
            (wq.shape, F32),
            (wk.shape, F32),
            (wv.shape, F32),
            ((rows, 8 * rows), F32),
            ((1, rows), F32),
            ((1, rows), F32),
            ((2, rows), F32),
            ((experts, rows), F32),
        ],
        held=(1, 2, 3, 4),
    )


def send(values, axis, flip):
    count = lax.axis_size(axis)
    return lax.ppermute(values, axis, [(i, i ^ flip) for i in range(count)])


def along_z(values):
    if not isinstance(values, (list, tuple)):
        values = [values] * 3
    return [send(value, "fsdp", 2 * (i + 1)) for i, value in enumerate(values)]


def gather_fsdp(block, name, after=()):
    came = along_z(block)
    return came, send(row([block, *came], name, after), "fsdp", 1)


def exchange(rows):
    return lax.all_to_all(rows, "expert", 0, 0, tiled=True)


def shards(
    tokens,
    lengths,
    routes,
    first_gain,
    query_weight,
    key_weight,
    value_weight,
    output_weight,
    query_gain,
    key_gain,
    second_gain,
    router_weight,
    gate_weight,
    up_weight,
    down_weight,
    cotangent,
):
    own = tokens[0]
    upstream = cotangent[0]
    rows, width = own.shape
    fsdp = lax.axis_size("fsdp")
    owners = lax.axis_size("expert")
    me = lax.axis_index("fsdp").astype(jnp.int32).reshape(1)
    owner = lax.axis_index("expert").astype(jnp.int32).reshape(1)
    experts = router_weight.shape[1]
    capacity = 3 * rows * routes.shape[2] // (2 * experts)
    kv_columns = key_weight.shape[1] // fsdp
    q_columns = query_weight.shape[1] // fsdp
    columns = q_columns + 2 * kv_columns
    q_heads = q_columns // HEAD

    packed = pack_weights(
        me,
        own,
        query_weight,
        key_weight,
        value_weight,
        router_weight.T,
        first_gain[None],
        second_gain[None],
        query_gain[None],
        key_gain[None],
    )
    x_came = along_z(packed[1:])
    dressed, mask, deal, turn = prepare(routes[0].T, upstream, experts, capacity)
    x_other = send(relay(own, packed[0], x_came, after=(mask,)), "fsdp", 1)
    c_all = lax.all_gather(dressed, "expert", axis=0)

    ends = jnp.cumsum(lengths[0])
    place = jnp.arange(rows * fsdp, dtype=jnp.int32)
    start = jnp.max(jnp.where(ends[:, None] <= place[None, :], ends[:, None], 0), axis=0)
    position = (place - start).astype(F32)
    frequency = ROPE_BASE ** (-jnp.arange(HEAD // 2, dtype=F32) * 2.0 / HEAD)
    angles = frequency[:, None] * position[None, :]
    cosine, sine = jnp.cos(angles), jnp.sin(angles)
    start = start[None, :].astype(jnp.int32)

    h1, pre, keep, give, inverse, gains, heads, turned, mixed = attention_forward(
        me, own, packed[0], x_came, x_other, cosine, sine, start, experts, q_heads
    )
    wo_came, wo_other = gather_fsdp(output_weight, "row_output", after=(heads,))
    other = send(give, "fsdp", 1)
    mixed_came = along_z(merge(keep, other))
    middle, probs, hidden, sent = middle_layer(
        own, keep, other, mixed_came, output_weight, wo_came, wo_other, gains, deal, experts, owners
    )
    h_rows = exchange(sent)
    rows_c, row_mask, back = deal_rows(owner, c_all, down_weight, experts, capacity)
    rows_back, gate_low, up_low, active, weighted, share = expert_layer(
        owner, h_rows, gains, row_mask, back, gate_weight, up_weight, experts
    )
    came_back = exchange(rows_back)
    grads, tick = expert_weights(h_rows, rows_c, gate_low, up_low, weighted)
    grads = lax.psum(grads, "fsdp")
    gate_sum, up_sum, down_sum = widen(grads)
    sent, tick = expert_outputs(active, share, down_weight, owners, after=(tick,))

    middle_grad, middle_low, extra = router_backward(
        came_back, turn, middle, probs, mask, gains, upstream, hidden, experts, after=(tick,)
    )
    da_came, da_other = gather_fsdp(middle_low, "row_middle")
    out_rows = exchange(sent)
    layer_out, _ = layer_output(out_rows, turn, middle)
    first, dh_keep, dh_give = attention_backward(
        me,
        middle_low,
        da_came,
        da_other,
        heads,
        output_weight,
        cosine,
        sine,
        start,
        h1,
        pre,
        mixed,
        inverse,
        turned,
        extra,
        experts,
        q_heads,
    )
    dh_total, *dh_sends = pair_sum(dh_keep, send(dh_give, "fsdp", 1))
    dh_came = along_z(dh_sends)
    tokens_grad = input_grad(dh_total, dh_came, own, gains, middle_grad, experts)
    first = passed(first, after=(out_rows, grads[0, :8, :128]))
    parted, rest = shares_sum(exchange(first))
    parted = lax.all_to_all(parted, "fsdp", 0, 0, tiled=True)
    pieces = exchange(whole_pieces(parted, rest))
    query_sum, key_sum, value_sum, output_sum, one_sum, two_sum, gain_sums, router_sum = final_grads(
        pieces, query_weight, key_weight, value_weight, first_gain[None], experts
    )
    step = HEAD // fsdp
    return (
        layer_out[None],
        tokens_grad[None],
        one_sum[0],
        query_sum,
        key_sum,
        value_sum,
        output_sum,
        gain_sums[0, :step],
        gain_sums[1, :step],
        two_sum[0],
        router_sum.T,
        gate_sum,
        up_sum,
        down_sum,
    )


def solution(mesh):
    whole = P("expert", "fsdp", None)
    rows = P("fsdp", None)
    vector = P("fsdp")
    owned = P("expert", None, None)
    return jax.shard_map(
        shards,
        mesh=mesh,
        in_specs=(
            whole,
            P("expert", None),
            whole,
            vector,
            rows,
            rows,
            rows,
            rows,
            vector,
            vector,
            vector,
            rows,
            owned,
            owned,
            owned,
            whole,
        ),
        out_specs=(
            whole,
            whole,
            vector,
            rows,
            rows,
            rows,
            rows,
            vector,
            vector,
            vector,
            rows,
            owned,
            owned,
            owned,
        ),
        check_vma=False,
    )
```

```python
import functools

import jax
import jax.numpy as jnp
from jax import lax
from jax.experimental import pallas as pl
from jax.experimental.pallas import tpu as pltpu
from jax.sharding import PartitionSpec as P

EPSILON = 1e-06
ROPE_BASE = 10000.0
HEAD = 64
TILE = 256
F32 = jnp.float32
BF16 = jnp.bfloat16
VMEM = pl.BlockSpec(memory_space=pltpu.VMEM)
SMEM = pl.BlockSpec(memory_space=pltpu.SMEM)
ANY = pl.BlockSpec(memory_space=pl.ANY)
HBM = pl.BlockSpec(memory_space=pltpu.HBM)


def dot(left, right, dims=((1,), (0,))):
    return lax.dot_general(left, right, (dims, ((), ())), preferred_element_type=F32)


def shape(extent, dtype):
    return jax.ShapeDtypeStruct(extent, dtype)


def kernel_call(
    body, name, micros, operands, results, smem=0, hbm=(), out_hbm=(), after=(), scratch=(), held=(), late=(), stored=(), mib=63
):
    held = tuple(held) + tuple(late)
    n, a, r, s = len(operands), len(after), len(results), len(scratch)
    specs = [SMEM if i < smem else HBM if i in held or i in hbm else VMEM for i in range(n)]
    out_specs = [HBM if i in stored or i in out_hbm else VMEM for i in range(r)]
    staged = [pltpu.VMEM(operands[i].shape, operands[i].dtype) for i in held]
    staged += [pltpu.VMEM(*results[i]) for i in stored]
    sems = [pltpu.SemaphoreType.DMA((max(len(held), 1),)), pltpu.SemaphoreType.DMA((max(len(stored), 1),))]

    def wrapped(*refs):
        ins, outs = list(refs[:n]), list(refs[n + a : n + a + r])
        own = refs[n + a + r : n + a + r + s]
        stages, (load_sem, store_sem) = refs[n + a + r + s : -2], refs[-2:]
        loads, stores, begun = {}, {}, []
        for k, i in enumerate(held):
            loads[i] = pltpu.make_async_copy(ins[i], stages[k], load_sem.at[k])
            loads[i].start()
            ins[i] = stages[k]
        for k, i in enumerate(stored):
            stores[i] = pltpu.make_async_copy(stages[len(held) + k], outs[i], store_sem.at[k])
            outs[i] = stages[len(held) + k]
        for i in held:
            if i not in late:
                loads[i].wait()

        def store(*which):
            for i in which:
                stores[i].start()
                begun.append(i)

        extra = {}
        if late:
            extra["wait"] = lambda i: loads[i].wait()
        if stored:
            extra["store"] = store
        body(*ins, *outs, *own, **extra)
        store(*[i for i in stored if i not in begun])
        for i in stored:
            stores[i].wait()

    return pl.pallas_call(
        wrapped,
        out_shape=[shape(*result) for result in results],
        in_specs=specs + [ANY] * a,
        out_specs=out_specs,
        scratch_shapes=list(scratch) + staged + sems,
        compiler_params=pltpu.CompilerParams(vmem_limit_bytes=mib * 1024 * 1024),
        cost_estimate=pl.CostEstimate(flops=0, bytes_accessed=int(micros * 3.6e6), transcendentals=0),
        name=name,
    )(*operands, *after)


def move_call(moves, name, micros, operands, results, count, after=()):
    def body(*refs):
        pairs = moves(*refs[:-1])
        assert len(pairs) == count
        copies = [pltpu.make_async_copy(*pair, refs[-1].at[i]) for i, pair in enumerate(pairs)]
        for copy in copies:
            copy.start()
        for copy in copies:
            copy.wait()

    return kernel_call(
        body,
        name,
        micros,
        operands,
        results,
        hbm=range(len(operands)),
        out_hbm=range(len(results)),
        after=after,
        scratch=[pltpu.SemaphoreType.DMA((count,))],
    )


def lane_blocks(value):
    return jnp.concatenate([value[:, i : i + 128] for i in range(0, value.shape[1], 128)], axis=0)


def joined_lanes(value, count):
    rows = value.shape[0] // count
    return jnp.concatenate([value[i * rows : (i + 1) * rows] for i in range(count)], axis=1)


def softmax_rows(logits):
    powers = jnp.exp(logits - jnp.max(logits, axis=0, keepdims=True))
    return powers / jnp.sum(powers, axis=0, keepdims=True)


def head_forward(pre, gain, cosine, sine):
    scale = lax.rsqrt(jnp.mean(pre * pre, axis=0, keepdims=True) + EPSILON)
    normed = pre * scale
    scaled = normed * gain
    a, b = scaled[: HEAD // 2], scaled[HEAD // 2 :]
    turned = jnp.concatenate([a * cosine - b * sine, b * cosine + a * sine], axis=0)
    return turned, normed, scale


def head_backward(grad, normed, scale, gain, cosine, sine):
    a, b = grad[: HEAD // 2], grad[HEAD // 2 :]
    unturned = jnp.concatenate([a * cosine + b * sine, b * cosine - a * sine], axis=0)
    gain_grad = jnp.sum(unturned * normed, axis=1, keepdims=True)
    inner = unturned * gain
    pre_grad = scale * (inner - normed * jnp.mean(inner * normed, axis=0, keepdims=True))
    return pre_grad, gain_grad


def prepare_kernel(
    routes_ref, c_ref, dressed_ref, mask_ref, deal_ref, turn_ref, whole_ref, *, experts, capacity, store
):
    rows, width = c_ref.shape
    subs = lax.broadcasted_iota(jnp.int32, (128, rows), 0)
    routed = jnp.zeros((128, rows), F32)
    for route in range(routes_ref.shape[0]):
        routed = routed + jnp.where(routes_ref[route : route + 1] == subs, 1.0, 0.0)
    dressed_ref[:, :width] = c_ref[...]
    dressed_ref[:, width:] = routed.T.astype(BF16)
    store(0)
    mask = routed[:experts]
    mask_ref[...] = mask
    ranks = dot(mask.astype(BF16), earlier(rows))
    slot = lax.broadcasted_iota(jnp.int32, (capacity, rows), 0).astype(F32) + 1.0
    for expert in range(experts):
        one = slice(expert, expert + 1)
        whole_ref[expert * capacity : (expert + 1) * capacity] = jnp.where(
            (ranks[one] == slot) & (mask[one] > 0.5), 1.0, 0.0
        )
    deal_ref[...] = whole_ref[...].astype(BF16)
    for part in range(0, experts * capacity, 128):
        turn_ref[:, part : part + 128] = whole_ref[part : part + 128].T.astype(BF16)


def earlier(rows):
    return (
        lax.broadcasted_iota(jnp.int32, (rows, rows), 0)
        <= lax.broadcasted_iota(jnp.int32, (rows, rows), 1)
    ).astype(BF16)


def prepare(routes, c, experts, capacity, after=()):
    rows, width = c.shape
    slots = experts * capacity
    return kernel_call(
        functools.partial(prepare_kernel, experts=experts, capacity=capacity),
        "prepare",
        2.0,
        [routes, c],
        [((rows, width + 128), BF16), ((experts, rows), F32), ((slots, rows), BF16), ((rows, slots), BF16)],
        after=after,
        scratch=[pltpu.VMEM((slots, rows), F32)],
        held=(0, 1),
        stored=(0, 1, 2, 3),
    )


def pack_kernel(me_ref, x_ref, wq_ref, wk_ref, wv_ref, router_ref, one_ref, two_ref, qg_ref, kg_ref, *outs):
    own_ref, sends, parts_ref = outs[0], outs[1:4], outs[4]
    experts, rows = router_ref.shape
    wide = wq_ref.shape[1] // 8
    narrow = wk_ref.shape[1] // 8
    count = qg_ref.shape[1]
    heads = jnp.concatenate([qg_ref[...], kg_ref[...]], axis=0).astype(F32)
    heads = jnp.concatenate([heads, jnp.zeros((2, 128 - count), F32)], axis=1)
    heads = jnp.concatenate([heads, jnp.zeros((126, 128), F32)], axis=0).T[:count]
    small = jnp.concatenate(
        [
            router_ref[...].astype(F32),
            one_ref[...].astype(F32),
            two_ref[...].astype(F32),
            jnp.zeros((6, 128), F32),
            heads,
        ],
        axis=0,
    ).astype(BF16)
    for part in range(8):
        parts_ref[part, :wide] = wq_ref[:, part * wide : (part + 1) * wide].astype(F32).T.astype(BF16)
        parts_ref[part, wide + 2 * narrow :] = small
    for pair in range(4):
        span = slice(pair * 128, (pair + 1) * 128)
        for ref, place in ((wk_ref, wide), (wv_ref, wide + narrow)):
            turned = ref[:, span].astype(F32).T.astype(BF16)
            parts_ref[2 * pair, place : place + narrow] = turned[:narrow]
            parts_ref[2 * pair + 1, place : place + narrow] = turned[narrow:]
    me = me_ref[0]
    tall = parts_ref.shape[1]
    blocks = lane_blocks(x_ref[...])
    base = blocks.shape[0]
    own_ref[:tall] = parts_ref[me]
    own_ref[tall:] = parts_ref[me ^ 1]
    for flip in range(1, 4):
        sends[flip - 1][:base] = blocks
        sends[flip - 1][base : base + tall] = parts_ref[me ^ (2 * flip)]
        sends[flip - 1][base + tall :] = parts_ref[me ^ (2 * flip + 1)]


def pack_weights(me, x, wq, wk, wv, router, one, two, qg, kg):
    tall = (wq.shape[1] + wk.shape[1] + wv.shape[1]) // 8 + router.shape[0] + 16
    base = x.shape[0] * 8
    return kernel_call(
        pack_kernel,
        "pack_weights",
        2.0,
        [me, x, wq, wk, wv, router, one, two, qg, kg],
        [((2 * tall, 128), BF16)] + [((base + 2 * tall, 128), BF16)] * 3,
        smem=1,
        scratch=[pltpu.VMEM((8, tall, 128), BF16)],
        held=range(1, 10),
    )


def relay(x, own, came):
    tall = own.shape[0] // 2
    base = came[0].shape[0] - 2 * tall
    rows, blocks = x.shape[0], x.shape[1] // 128

    def moves(x_ref, own_ref, *refs):
        out = refs[3]
        pairs = [
            (x_ref.at[:, i * 128 : (i + 1) * 128], out.at[0, i * rows : (i + 1) * rows]) for i in range(blocks)
        ]
        pairs.append((own_ref.at[tall:], out.at[0, base:]))
        for flip in range(1, 4):
            pairs.append((refs[flip - 1].at[:base], out.at[flip, :base]))
            pairs.append((refs[flip - 1].at[base + tall :], out.at[flip, base:]))
        return pairs

    return move_call(moves, "relay", 2.0, [x, own, *came], [((4, base + tall, 128), BF16)], blocks + 7)[0]


def forward_kernel(me_ref, x_ref, own_ref, *refs, experts, q_heads, store):
    came, other_ref = refs[:3], refs[3]
    cos_ref, sin_ref, start_ref = refs[4:7]
    h1_ref, pre_ref, keep_ref, give_ref, inverse_ref, gains_ref, heads_ref, turned_ref, out_ref = refs[-9:]
    rows, width = x_ref.shape
    q_columns = q_heads * HEAD
    columns = q_columns + 2 * HEAD
    total = rows * 8
    tall = own_ref.shape[0] // 2
    base = 8 * rows
    me = me_ref[0]
    for slot in range(8):
        flip = slot // 2
        if slot % 2:
            piece = other_ref[flip, base:]
        elif flip:
            piece = came[flip - 1][base : base + tall]
        else:
            piece = own_ref[:tall]
        span = pl.ds(pl.multiple_of((me ^ slot) * rows, rows), rows)
        turned_ref[:, span] = piece[:columns]
        small = piece[columns:].astype(F32)
        gains_ref[:, span] = small[: experts + 8]
        heads_ref[pl.ds(pl.multiple_of((me ^ slot) * 8, 8), 8)] = small[experts + 8 :]
    gain_one = gains_ref[experts : experts + 1]
    for slot in range(8):
        flip = slot // 2
        if slot % 2:
            x = joined_lanes(other_ref[flip, :base], 8)
        elif flip:
            x = joined_lanes(came[flip - 1][:base], 8)
        else:
            x = x_ref[...]
        x = x.astype(F32)
        scale = lax.rsqrt(jnp.mean(x * x, axis=1, keepdims=True) + EPSILON)
        h1_ref[slot] = (x * scale * gain_one).astype(BF16)
    store(0, 6, 7)
    for slot in range(8):
        block = dot(turned_ref[...], h1_ref[slot], ((1,), (1,)))
        place = pl.multiple_of((me ^ slot) * rows, rows)
        pre_ref[:, pl.ds(place, rows)] = block
    store(1)
    cosine, sine = cos_ref[...], sin_ref[...]
    gain_query, gain_key = heads_ref[:, :1], heads_ref[:, 1:2]
    key = head_forward(pre_ref[q_columns : q_columns + HEAD], gain_key, cosine, sine)[0]
    key = key.T.astype(BF16)
    value = pre_ref[q_columns + HEAD :].astype(BF16)
    inverse_ref[...] = jnp.zeros(inverse_ref.shape, F32)
    for head in range(q_heads):
        query = head_forward(pre_ref[head * HEAD : (head + 1) * HEAD], gain_query, cosine, sine)[0]
        query = query.astype(BF16) * jnp.array(HEAD ** (-0.5), BF16)
        for tile in range(total // TILE):
            low, high = tile * TILE, (tile + 1) * TILE
            scores = dot(key[:high], query[:, low:high])
            u = lax.broadcasted_iota(jnp.int32, (high, TILE), 0)
            t = lax.broadcasted_iota(jnp.int32, (high, TILE), 1) + low
            allowed = (u >= start_ref[:, low:high]) & (u <= t)
            powers = jnp.where(allowed, jnp.exp(scores), 0.0)
            inverse = 1.0 / jnp.sum(powers, axis=0, keepdims=True)
            probs = (powers * inverse).astype(BF16)
            mixed = dot(value[:, :high], probs).astype(BF16)
            inverse_ref[head : head + 1, low:high] = inverse
            for part in range(TILE // rows):
                out_ref[low // rows + part, head * HEAD : (head + 1) * HEAD] = mixed[
                    :, part * rows : (part + 1) * rows
                ]
    for slot in range(8):
        (give_ref if slot % 2 else keep_ref)[slot // 2] = out_ref[me ^ slot]


def attention_forward(me, x, own, came, other, cosine, sine, start, experts, q_heads):
    rows, width = x.shape
    total = 8 * rows
    columns = (q_heads + 2) * HEAD
    q_columns = q_heads * HEAD
    return kernel_call(
        functools.partial(forward_kernel, experts=experts, q_heads=q_heads),
        "attention_forward",
        7.0,
        [me, x, own, *came, other, cosine, sine, start],
        [
            ((8, rows, width), BF16),
            ((columns, total), F32),
            ((4, q_columns, rows), BF16),
            ((4, q_columns, rows), BF16),
            ((8, total), F32),
            ((experts + 8, width), F32),
            ((HEAD, 128), F32),
            ((columns, width), BF16),
            ((8, q_columns, rows), BF16),
        ],
        smem=1,
        held=(1,),
        stored=(0, 1, 4, 6, 7, 8),
    )


def merge(keep, came, wo, wo_came):
    def moves(keep_ref, came_ref, *refs):
        weights, outs, stacked = refs[:4], refs[4:7], refs[7]
        pairs = [(weight, stacked.at[i]) for i, weight in enumerate(weights)]
        for flip in range(1, 4):
            pairs.append((keep_ref.at[flip], outs[flip - 1].at[0]))
            pairs.append((came_ref.at[flip], outs[flip - 1].at[1]))
        return pairs

    extent = ((2,) + keep.shape[1:], BF16)
    results = [extent] * 3 + [((4,) + wo.shape, BF16)]
    *sends, stacked = move_call(moves, "merge", 1.0, [keep, came, wo, *wo_came], results, 10)
    return sends, stacked


def middle_kernel(x_ref, keep_ref, other_ref, *refs, experts, wait, store):
    came, wo_ref, wo_came, wo_other_ref, gains_ref, deal_ref = refs[:3], refs[3], refs[4:7], refs[7], refs[8], refs[9]
    middle_ref, probs_ref, hidden_ref, sent_ref, mixed_ref, whole_ref, out_ref, out_sem = refs[10:]
    rows, width = x_ref.shape
    for slot in range(8):
        flip, core = slot // 2, slot % 2
        if flip:
            piece = came[flip - 1][core]
        else:
            piece = (other_ref if core else keep_ref)[0]
        span = slice(slot * 128, (slot + 1) * 128)
        mixed_ref[:, span] = piece.astype(F32).T.astype(BF16)
    for i in (6, 7, 8, 9, 10):
        wait(i)
    for slot in range(8):
        flip = slot // 2
        span = slice(slot * 128, (slot + 1) * 128)
        if slot % 2:
            whole_ref[span] = wo_other_ref[flip]
        else:
            whole_ref[span] = (wo_came[flip - 1] if flip else wo_ref)[...]
    wait(0)
    middle = x_ref[...].astype(F32) + dot(mixed_ref[...], whole_ref[...])
    middle_ref[...] = middle
    scale = lax.rsqrt(jnp.mean(middle * middle, axis=1, keepdims=True) + EPSILON)
    hidden = (middle * scale * gains_ref[experts + 1 : experts + 2]).astype(BF16)
    hidden_ref[...] = hidden
    probs_ref[...] = softmax_rows(dot(gains_ref[:experts].astype(BF16), hidden, ((1,), (1,))))
    store(0, 2)
    owners, per_owner, capacity, _ = sent_ref.shape
    group = owners // 4
    size = group * per_owner * capacity
    copies = []
    wait(12)
    for part in range(4):
        taken = dot(deal_ref[part * size : (part + 1) * size], hidden).astype(BF16)
        blocks = slice(group * part, group * (part + 1))
        out_ref[blocks] = taken.reshape(group, per_owner, capacity, width)
        copies.append(pltpu.make_async_copy(out_ref.at[blocks], sent_ref.at[blocks], out_sem.at[part]))
        copies[-1].start()
    for copy in copies:
        copy.wait()


def middle_layer(x, keep, other, came, wo, wo_came, wo_other, gains, deal, experts, owners):
    rows, width = x.shape
    per_owner = experts // owners
    capacity = deal.shape[0] // experts
    sent = ((owners, per_owner, capacity, width), BF16)
    return kernel_call(
        functools.partial(middle_kernel, experts=experts),
        "middle_layer",
        3.0,
        [x, keep, other, *came, wo, *wo_came, wo_other, gains, deal],
        [((rows, width), F32), ((experts, rows), F32), ((rows, width), BF16), sent],
        out_hbm=(3,),
        scratch=[
            pltpu.VMEM((rows, width), BF16),
            pltpu.VMEM((width, width), BF16),
            pltpu.VMEM(*sent),
            pltpu.SemaphoreType.DMA((4,)),
        ],
        late=(6, 7, 8, 9, 10, 0, 12),
        stored=(0, 2),
    )


def row(pieces, name):
    def moves(*refs):
        return [(ref, refs[-1].at[i]) for i, ref in enumerate(refs[:-1])]

    return move_call(moves, name, 1.0, pieces, [((len(pieces),) + pieces[0].shape, BF16)], len(pieces))[0]


def backward_kernel(me_ref, own_da_ref, *refs, experts, q_heads, wait):
    came, other_ref = refs[:3], refs[3]
    heads_ref, wo_ref, cos_ref, sin_ref, start_ref = refs[4:9]
    h1_ref, pre_ref, mixed_ref, inverse_ref, turned_ref, extra_ref = refs[9:15]
    first_ref, keep_ref, send_ref = refs[-10:-7]
    da_ref, mixed_grad_ref, dkey_ref, dvalue_ref, low_ref, out_slots_ref, grad_ref = refs[-7:]
    rows, width = own_da_ref.shape
    q_columns = q_heads * HEAD
    columns = q_columns + 2 * HEAD
    total = rows * 8
    me = me_ref[0]
    for slot in range(8):
        flip, core = slot // 2, slot % 2
        if core:
            piece = other_ref[flip]
        else:
            piece = (came[flip - 1] if flip else own_da_ref)[...]
        span = slice(slot * rows, (slot + 1) * rows)
        da_ref[span] = piece
        place = pl.multiple_of((me ^ slot) * rows, rows)
        mixed_grad_ref[:, pl.ds(place, rows)] = dot(wo_ref[...], piece, ((1,), (1,))).astype(BF16)
    wait(13)
    for slot in range(8):
        out_slots_ref[:, slot * rows : (slot + 1) * rows] = mixed_ref[me ^ slot]
    wo_grad = dot(out_slots_ref[...], da_ref[...]).astype(BF16)
    wo_grad = lane_blocks(wo_grad)
    wait(12)
    wait(14)
    gain_query, gain_key = heads_ref[:, :1], heads_ref[:, 1:2]
    cosine, sine = cos_ref[...], sin_ref[...]
    key_turned, key_normed, key_scale = head_forward(
        pre_ref[q_columns : q_columns + HEAD], gain_key, cosine, sine
    )
    key_low = key_turned.astype(BF16)
    key = key_turned.T.astype(BF16)
    value = pre_ref[q_columns + HEAD :].T.astype(BF16)
    dkey_ref[...] = jnp.zeros(dkey_ref.shape, F32)
    dvalue_ref[...] = jnp.zeros(dvalue_ref.shape, F32)
    gain_query_grad = jnp.zeros((HEAD, 1), F32)
    pieces = []
    for head in range(q_heads):
        span = slice(head * HEAD, (head + 1) * HEAD)
        turned, normed, scale = head_forward(pre_ref[span], gain_query, cosine, sine)
        query = turned.astype(BF16) * jnp.array(HEAD ** (-0.5), BF16)
        grads = []
        for tile in range(total // TILE):
            low, high = tile * TILE, (tile + 1) * TILE
            part = query[:, low:high]
            mixed_grad = mixed_grad_ref[span, low:high]
            scores = dot(key[:high], part)
            u = lax.broadcasted_iota(jnp.int32, (high, TILE), 0)
            t = lax.broadcasted_iota(jnp.int32, (high, TILE), 1) + low
            allowed = (u >= start_ref[:, low:high]) & (u <= t)
            probs = jnp.where(allowed, jnp.exp(scores) * inverse_ref[head : head + 1, low:high], 0.0)
            attend = dot(value[:high], mixed_grad)
            delta = jnp.sum(probs * attend, axis=0, keepdims=True)
            score_low = (probs * (attend - delta)).astype(BF16)
            grads.append(dot(key_low[:, :high], score_low))
            dkey_ref[:, :high] += dot(part, score_low, ((1,), (1,)))
            dvalue_ref[:, :high] += dot(mixed_grad, probs.astype(BF16), ((1,), (1,)))
        query_grad = jnp.concatenate(grads, axis=1) * HEAD ** (-0.5)
        pre_grad, gain_grad = head_backward(query_grad, normed, scale, gain_query, cosine, sine)
        gain_query_grad += gain_grad
        pieces.append(pre_grad)
    pre_grad, gain_key_grad = head_backward(
        dkey_ref[...], key_normed, key_scale, gain_key, cosine, sine
    )
    pieces += [pre_grad, dvalue_ref[...]]
    pre_grad = jnp.concatenate(pieces, axis=0)
    low_ref[...] = pre_grad.astype(BF16)
    slots_grad = []
    for slot in range(8):
        place = pl.multiple_of((me ^ slot) * rows, rows)
        slots_grad.append(low_ref[:, pl.ds(place, rows)])
    slots_grad = jnp.concatenate(slots_grad, axis=1)
    wait(11)
    wait(15)
    grad_ref[:columns] = dot(slots_grad, h1_ref[...].reshape(total, width))
    extra = extra_ref[...]
    lane = lax.broadcasted_iota(jnp.int32, (HEAD, 128), 1)
    gains = jnp.where(lane == 0, gain_query_grad, jnp.where(lane == 1, gain_key_grad, 0.0))
    gains = gains.T[:2]
    step = HEAD // 8
    grad_ref[columns:] = jnp.zeros((64, width), F32)
    grad_ref[columns : columns + experts + 1] = extra[: experts + 1]
    for part in range(8):
        grad_ref[columns + experts + 1 : columns + experts + 3, part * rows : part * rows + step] = gains[
            :, part * step : (part + 1) * step
        ]
    for piece in range(16):
        spare = []
        place = columns + piece * SPARE
        for part in range(8):
            span = slice(part * rows, (part + 1) * rows)
            block = grad_ref[piece * PIECE : (piece + 1) * PIECE, span]
            first_ref[piece, part * PIECE : (part + 1) * PIECE] = block.astype(BF16)
            spare.append(grad_ref[place : place + SPARE, span])
        spare.append(jnp.zeros((2 * PIECE - 8 * SPARE, 128), F32))
        first_ref[piece, 8 * PIECE : 10 * PIECE] = jnp.concatenate(spare, axis=0).astype(BF16)
        first_ref[piece, 10 * PIECE :] = wo_grad[piece * SLICE : (piece + 1) * SLICE]
    turned = turned_ref[...]
    for slot in range(8):
        low_rows_slot = slots_grad[:, slot * rows : (slot + 1) * rows].astype(F32).T.astype(BF16)
        part = dot(low_rows_slot, turned)
        if slot % 2:
            send_ref[slot // 2] = part.astype(BF16)
        else:
            keep_ref[slot // 2] = part


def attention_backward(
    me, da, came, other, heads, wo, cosine, sine, start, h1, pre, mixed, inverse, turned, extra, experts, q_heads, after=()
):
    rows, width = da.shape
    total = 8 * rows
    columns = pre.shape[0]
    q_columns = q_heads * HEAD
    return kernel_call(
        functools.partial(backward_kernel, experts=experts, q_heads=q_heads),
        "attention_backward",
        12,
        [me, da, *came, other, heads, wo, cosine, sine, start, h1, pre, mixed, inverse, turned, extra],
        [
            ((16, 10 * PIECE + SLICE, 128), BF16),
            ((4, rows, width), F32),
            ((4, rows, width), BF16),
        ],
        smem=1,
        after=after,
        held=(6, 7),
        late=(11, 12, 13, 14, 15),
        scratch=[
            pltpu.VMEM((total, width), BF16),
            pltpu.VMEM((q_columns, total), BF16),
            pltpu.VMEM((HEAD, total), F32),
            pltpu.VMEM((HEAD, total), F32),
            pltpu.VMEM((columns, total), BF16),
            pltpu.VMEM((q_columns, total), BF16),
            pltpu.VMEM((columns + 64, width), F32),
        ],
    )


def deal_kernel(owner_ref, c_ref, down_ref, rows_c, mask_ref, back_ref, c_scratch, sems, *, experts, capacity, wait, store):
    owner = owner_ref[0]
    per_owner, hidden, width = down_ref.shape
    rows = c_ref.shape[1]
    loads = [pltpu.make_async_copy(c_ref.at[i], c_scratch.at[i], sems.at[i]) for i in range(16)]
    for load in loads:
        load.start()
    lanes = lax.broadcasted_iota(jnp.int32, (experts, 128), 1)
    subs = lax.broadcasted_iota(jnp.int32, (experts, 128), 0)
    eye = (lanes == subs).astype(BF16)
    before = earlier(rows)
    mine_of = lax.broadcasted_iota(jnp.int32, (experts, rows), 0) - owner * per_owner
    slot = lax.broadcasted_iota(jnp.int32, (capacity, rows), 0).astype(F32) + 1.0
    for block in range(16):
        loads[block].wait()
        c = c_scratch[block]
        mask = dot(eye, c[:, width:], ((1,), (1,)))
        ranks = dot(mask.astype(BF16), before)
        deals = []
        for k in range(per_owner):
            mine = mine_of == k
            hit = jnp.sum(jnp.where(mine, mask, 0.0), axis=0, keepdims=True)
            rank = jnp.sum(jnp.where(mine, ranks, 0.0), axis=0, keepdims=True)
            deals.append(jnp.where((rank == slot) & (hit > 0.5), 1.0, 0.0))
        taken = dot(jnp.concatenate(deals, axis=0).astype(BF16), c).astype(BF16)
        span = slice(block * capacity, (block + 1) * capacity)
        for k in range(per_owner):
            spot = slice(k * capacity, (k + 1) * capacity)
            rows_c[k, span] = taken[spot, :width]
            mask_ref[k, span] = taken[spot, width:]
    store(0, 1)
    wait(2)
    for k in range(per_owner):
        for tile in range(16 * capacity // TILE):
            span = slice(tile * TILE, (tile + 1) * TILE)
            back_ref[k, span] = dot(rows_c[k, span], down_ref[k], ((1,), (1,)))


def deal_rows(owner, c, down, experts, capacity):
    per_owner, hidden, width = down.shape
    count = 16 * capacity
    return kernel_call(
        functools.partial(deal_kernel, experts=experts, capacity=capacity),
        "deal_rows",
        12.0,
        [owner, c, down],
        [
            ((per_owner, count, width), BF16),
            ((per_owner, count, 128), BF16),
            ((per_owner, count, hidden), F32),
        ],
        smem=1,
        hbm=(1,),
        scratch=[pltpu.VMEM(c.shape, BF16), pltpu.SemaphoreType.DMA((16,))],
        late=(2,),
        stored=(0, 1, 2),
    )


def expert_kernel(
    owner_ref,
    h_hbm,
    gains_ref,
    mask_ref,
    back_hbm,
    gate_hbm,
    up_hbm,
    rows_hbm,
    gate_out,
    up_out,
    active_out,
    weighted_out,
    share_ref,
    h_ref,
    back_in,
    gate_ref,
    up_ref,
    rows_back,
    load_sem,
    store_sem,
    *,
    experts,
    store,
):
    owners, per_owner, capacity, width = h_hbm.shape
    group = 8
    parts = owners // group
    size = group * capacity
    loads = {}
    for k in range(per_owner):
        for part in range(parts):
            blocks = slice(part * group, (part + 1) * group)
            spot = (k * parts + part) * 4
            loads[k, part] = [
                pltpu.make_async_copy(h_hbm.at[blocks, k], h_ref.at[blocks, k], load_sem.at[spot]),
                pltpu.make_async_copy(
                    back_hbm.at[k, part * size : (part + 1) * size],
                    back_in.at[k, part * size : (part + 1) * size],
                    load_sem.at[spot + 1],
                ),
            ]
            if part == 0:
                loads[k, part] += [
                    pltpu.make_async_copy(gate_hbm.at[k], gate_ref.at[k], load_sem.at[spot + 2]),
                    pltpu.make_async_copy(up_hbm.at[k], up_ref.at[k], load_sem.at[spot + 3]),
                ]
            for load in loads[k, part]:
                load.start()
    owner = owner_ref[0]
    router = jnp.concatenate([gains_ref[:experts], jnp.zeros((128 - experts, width), F32)], axis=0)
    router = router.astype(BF16)
    lane = lax.broadcasted_iota(jnp.int32, (size, 128), 1)
    copies = []
    for k in range(per_owner):
        place = owner * per_owner + k
        for part in range(parts):
            blocks = slice(part * group, (part + 1) * group)
            span = slice(part * size, (part + 1) * size)
            for load in loads[k, part]:
                load.wait()
            h = h_ref[blocks, k].reshape(size, width)
            gate = dot(h, gate_ref[k])
            up = dot(h, up_ref[k])
            logits = dot(h, router, ((1,), (1,)))
            chosen = mask_ref[k, span] > 0.5
            top = jnp.max(jnp.where(chosen, logits, -1e30), axis=1, keepdims=True)
            powers = jnp.where(chosen, jnp.exp(logits - top), 0.0)
            total = jnp.sum(powers, axis=1, keepdims=True)
            share = jnp.sum(jnp.where(lane == place, powers, 0.0), axis=1, keepdims=True)
            share = share / jnp.where(total > 0.0, total, 1.0)
            share_ref[k, span] = jnp.broadcast_to(share, (size, 128))
            back = back_in[k, span]
            sig = 1.0 / (1.0 + jnp.exp(-gate))
            silu = gate * sig
            active = silu * up
            active_low = active.astype(BF16)
            route_grad = jnp.sum(active_low.astype(F32) * back, axis=1, keepdims=True)
            grad = back * share
            gate_low = (grad * up * (sig + silu * (1.0 - sig))).astype(BF16)
            up_low = (grad * silu).astype(BF16)
            active_out[k, span] = active_low
            weighted_out[k, span] = (active * share).astype(BF16)
            gate_out[k, span] = gate_low
            up_out[k, span] = up_low
            rows = dot(gate_low, gate_ref[k], ((1,), (1,))) + dot(up_low, up_ref[k], ((1,), (1,)))
            high = route_grad.astype(BF16).astype(F32)
            spread_out = jnp.where(lane == place, high, 0.0)
            spread_out = jnp.where(lane == place + experts, route_grad - high, spread_out)
            whole = jnp.concatenate([rows.astype(BF16), spread_out.astype(BF16)], axis=1)
            rows_back[blocks, k] = whole.reshape(group, capacity, width + 128)
            copies.append(
                pltpu.make_async_copy(
                    rows_back.at[blocks, k], rows_hbm.at[blocks, k], store_sem.at[k * parts + part]
                )
            )
            copies[-1].start()
    store(1, 2, 3, 4, 5)
    for copy in copies:
        copy.wait()


def expert_layer(owner, h, gains, mask, back, gate, up, experts):
    per_owner, width, hidden = gate.shape
    owners, _, capacity, _ = h.shape
    count = owners * capacity
    narrow = ((per_owner, count, hidden), BF16)
    rows_back = ((owners, per_owner, capacity, width + 128), BF16)
    pieces = per_owner * (owners // 8)
    return kernel_call(
        functools.partial(expert_kernel, experts=experts),
        "expert_layer",
        14.0,
        [owner, h, gains, mask, back, gate, up],
        [rows_back] + [narrow] * 4 + [((per_owner, count, 128), F32)],
        smem=1,
        hbm=(1, 4, 5, 6),
        out_hbm=(0,),
        scratch=[pltpu.VMEM(value.shape, value.dtype) for value in (h, back, gate, up)]
        + [pltpu.VMEM(*rows_back), pltpu.SemaphoreType.DMA((4 * pieces,)), pltpu.SemaphoreType.DMA((pieces,))],
        stored=(1, 2, 3, 4, 5),
    )


def weights_kernel(h_ref, rows_c, gate_low, up_low, weighted, out_ref, tick_ref, *, wait, store):
    tick_ref[...] = jnp.zeros(tick_ref.shape, F32)
    first = ((0,), (0,))
    owners, per_owner, capacity, width = h_ref.shape
    hidden = gate_low.shape[2]
    half = width // 2
    for i in (0, 2, 3):
        wait(i)
    for k in range(per_owner):
        rows_h = h_ref[:, k].reshape(owners * capacity, width)
        for place, low in ((k, gate_low), (per_owner + k, up_low)):
            total = dot(rows_h, low[k], first).astype(BF16)
            out_ref[place, :, :hidden] = total[:half]
            out_ref[place, :, hidden:] = total[half:]
        if k == 0:
            wait(1)
            wait(4)
        out_ref[2 * per_owner + k] = dot(weighted[k], rows_c[k], first).astype(BF16)


def expert_weights(h, rows_c, gate_low, up_low, weighted):
    per_owner, count, width = rows_c.shape
    hidden = gate_low.shape[2]
    return kernel_call(
        weights_kernel,
        "expert_weights",
        0.1,
        [h, rows_c, gate_low, up_low, weighted],
        [((3 * per_owner, hidden, width), BF16), ((8, 128), F32)],
        late=(0, 1, 2, 3, 4),
        stored=(0,),
    )


def widen_kernel(low_ref, gate_ref, up_ref, down_ref):
    step = pl.program_id(0)
    hidden = gate_ref.shape[2]
    value = low_ref[0].astype(F32)
    half = value.shape[0]
    for place, ref in ((0, gate_ref), (1, up_ref)):

        @pl.when(step // 2 == place)
        def _():
            ref[0, :half] = value[:, :hidden]
            ref[0, half:] = value[:, hidden:]

    @pl.when(step // 2 == 2)
    def _():
        down_ref[0] = value


def widen(low):
    count, hidden, width = low.shape
    per_owner = count // 3

    def spot(place):
        return lambda i: (jnp.clip(i - place * per_owner, 0, per_owner - 1), 0, 0)

    return pl.pallas_call(
        widen_kernel,
        grid=(count,),
        out_shape=[shape((per_owner, width, hidden), F32)] * 2 + [shape((per_owner, hidden, width), F32)],
        in_specs=[pl.BlockSpec((1, hidden, width), lambda i: (i, 0, 0))],
        out_specs=[
            pl.BlockSpec((1, width, hidden), spot(0)),
            pl.BlockSpec((1, width, hidden), spot(1)),
            pl.BlockSpec((1, hidden, width), spot(2)),
        ],
        compiler_params=pltpu.CompilerParams(vmem_limit_bytes=63 * 1024 * 1024),
        cost_estimate=pl.CostEstimate(flops=0, bytes_accessed=24_000_000, transcendentals=0),
        name="widen",
    )(low)


def outputs_kernel(active, share, down_ref, sent_ref, tick_ref, out_ref, out_sem, *, wait):
    tick_ref[...] = jnp.zeros(tick_ref.shape, F32)
    per_owner, count, hidden = active.shape
    owners, _, capacity, width = sent_ref.shape
    group = 8
    size = group * capacity
    copies = []
    for i in range(3):
        wait(i)
    for k in range(per_owner):
        for part in range(owners // group):
            span = slice(part * size, (part + 1) * size)
            blocks = slice(part * group, (part + 1) * group)
            produced = dot(active[k, span], down_ref[k]).astype(BF16).astype(F32)
            produced = (produced * share[k, span, :1]).astype(BF16)
            out_ref[blocks, k] = produced.reshape(group, capacity, width)
            copies.append(
                pltpu.make_async_copy(
                    out_ref.at[blocks, k], sent_ref.at[blocks, k], out_sem.at[k * (owners // group) + part]
                )
            )
            copies[-1].start()
    for copy in copies:
        copy.wait()


def expert_outputs(active, share, down, owners, after=()):
    per_owner, count, hidden = active.shape
    width = down.shape[2]
    sent = ((owners, per_owner, count // owners, width), BF16)
    return kernel_call(
        outputs_kernel,
        "expert_outputs",
        0.1,
        [active, share, down],
        [sent, ((8, 128), F32)],
        out_hbm=(0,),
        after=after,
        scratch=[pltpu.VMEM(*sent), pltpu.SemaphoreType.DMA((per_owner * (owners // 8),))],
        late=(0, 1, 2),
    )


def combined(rows_hbm, rows_ref, sems, turn_ref, ready):
    owners, per_owner, capacity, wide = rows_hbm.shape
    group = owners // 4
    size = group * per_owner * capacity
    loads = []
    for part in range(4):
        blocks = slice(part * group, (part + 1) * group)
        loads.append(pltpu.make_async_copy(rows_hbm.at[blocks], rows_ref.at[blocks], sems.at[part]))
        loads[-1].start()
    ready()
    total = None
    for part in range(4):
        loads[part].wait()
        rows = rows_ref[part * group : (part + 1) * group].reshape(size, wide)
        one = dot(turn_ref[:, part * size : (part + 1) * size], rows)
        total = one if total is None else total + one
    return total


def output_kernel(rows_hbm, turn_ref, middle_ref, out_ref, tick_ref, rows_ref, sems, *, wait, store):
    tick_ref[...] = jnp.zeros(tick_ref.shape, F32)
    total = combined(rows_hbm, rows_ref, sems, turn_ref, lambda: wait(1))
    wait(2)
    out_ref[...] = (middle_ref[...] + total).astype(BF16)


def layer_output(rows, turn, middle):
    return kernel_call(
        output_kernel,
        "layer_output",
        3,
        [rows, turn, middle],
        [(middle.shape, BF16), ((8, 128), F32)],
        hbm=(0,),
        scratch=[pltpu.VMEM(rows.shape, BF16), pltpu.SemaphoreType.DMA((4,))],
        late=(1, 2),
        stored=(0,),
    )


def router_kernel(
    rows_hbm,
    turn_ref,
    middle_ref,
    probs_ref,
    mask_ref,
    gains_ref,
    c_ref,
    hidden_ref,
    grad_ref,
    send_ref,
    extra_ref,
    rows_ref,
    sems,
    *,
    experts,
    wait,
    store,
):
    rows, width = middle_ref.shape
    returned = combined(rows_hbm, rows_ref, sems, turn_ref, lambda: wait(1))
    for i in (2, 4, 6, 7):
        wait(i)
    tail = returned[:, width:].T
    route_grad = tail[:experts] + tail[experts : 2 * experts]
    mask = mask_ref[...]
    probs = probs_ref[...]
    picked = probs * mask
    picked_sum = jnp.sum(picked, axis=0, keepdims=True)
    share = picked / picked_sum
    picked_grad = (route_grad - jnp.sum(route_grad * share, axis=0, keepdims=True)) / picked_sum
    prob_grad = mask * picked_grad
    logit_grad = probs * (prob_grad - jnp.sum(probs * prob_grad, axis=0, keepdims=True))
    extra_ref[:experts] = dot(logit_grad.astype(BF16), hidden_ref[...])
    logit_rows = jnp.concatenate([logit_grad, jnp.zeros((128 - experts, rows), F32)], axis=0).T
    router = gains_ref[:experts].astype(BF16)
    hidden_grad = returned[:, :width] + dot(logit_rows[:, :experts].astype(BF16), router)
    middle = middle_ref[...]
    scale = lax.rsqrt(jnp.mean(middle * middle, axis=1, keepdims=True) + EPSILON)
    normed = middle * scale
    extra_ref[experts : experts + 8] = jnp.broadcast_to(
        jnp.sum(hidden_grad * normed, axis=0, keepdims=True), (8, width)
    )
    inner = hidden_grad * gains_ref[experts + 1 : experts + 2]
    grad = c_ref[...].astype(F32) + scale * (
        inner - normed * jnp.mean(inner * normed, axis=1, keepdims=True)
    )
    grad_ref[...] = grad
    send_ref[...] = grad.astype(BF16)


def router_backward(rows_back, turn, middle, probs, mask, gains, c, hidden, experts, after=()):
    rows, width = middle.shape
    return kernel_call(
        functools.partial(router_kernel, experts=experts),
        "router_backward",
        5,
        [rows_back, turn, middle, probs, mask, gains, c, hidden],
        [((rows, width), F32), ((rows, width), BF16), ((experts + 8, width), F32)],
        hbm=(0,),
        after=after,
        scratch=[pltpu.VMEM(rows_back.shape, BF16), pltpu.SemaphoreType.DMA((4,))],
        late=(1, 2, 4, 6, 7),
        stored=(0,),
    )


def pair_kernel(keep_ref, other_ref, total_ref, *sends):
    for flip in range(4):
        total = keep_ref[flip] + other_ref[flip].astype(F32)
        if flip:
            sends[flip - 1][...] = total.astype(BF16)
        else:
            total_ref[...] = total


def pair_sum(keep, other):
    rows, width = keep.shape[1:]
    return kernel_call(
        pair_kernel, "pair_sum", 1.2, [keep, other], [((rows, width), F32)] + [((rows, width), BF16)] * 3
    )


def input_kernel(total_ref, *refs, experts, store):
    came = refs[:3]
    x_ref, gains_ref, middle_grad_ref, out_ref = refs[3:]
    total = total_ref[...]
    for piece in came:
        total = total + piece[...].astype(F32)
    x = x_ref[...].astype(F32)
    scale = lax.rsqrt(jnp.mean(x * x, axis=1, keepdims=True) + EPSILON)
    normed = x * scale
    inner = total * gains_ref[experts : experts + 1]
    out_ref[...] = middle_grad_ref[...] + scale * (
        inner - normed * jnp.mean(inner * normed, axis=1, keepdims=True)
    )


def input_grad(total, came, x, gains, middle_grad, experts):
    return kernel_call(
        functools.partial(input_kernel, experts=experts),
        "input_grad",
        2,
        [total, *came, x, gains, middle_grad],
        [(middle_grad.shape, F32)],
        held=(4, 6),
        stored=(0,),
    )[0]


PIECE, SPARE, SLICE = 16, 3, 64


def passed(value, after):
    return move_call(
        lambda source, out: [(source, out)], "passed", 0.5, [value], [(value.shape, value.dtype)], 1, after
    )[0]


def shares_kernel(pieces_ref, out_ref, rest_ref):
    total = pieces_ref[0].astype(F32)
    for i in range(1, pieces_ref.shape[0]):
        total = total + pieces_ref[i].astype(F32)
    base = 8 * PIECE
    fill = jnp.zeros((PIECE - SPARE, 128), F32)
    for part in range(8):
        out_ref[part, :PIECE] = total[part * PIECE : (part + 1) * PIECE].astype(BF16)
        spare = total[base + part * SPARE : base + (part + 1) * SPARE]
        out_ref[part, PIECE:] = jnp.concatenate([spare, fill], axis=0).astype(BF16)
    rest_ref[...] = total[base + 2 * PIECE :].astype(BF16)


def shares_sum(pieces, after=()):
    return kernel_call(
        shares_kernel,
        "shares_sum",
        0.1,
        [pieces],
        [((8, 2 * PIECE, 128), BF16), ((SLICE, 128), BF16)],
        after=after,
    )


def whole_kernel(came_ref, rest_ref, out_ref):
    spare = came_ref[0, PIECE:].astype(F32)
    for i in range(1, 8):
        spare = spare + came_ref[i, PIECE:].astype(F32)
    rows = [came_ref[i, :PIECE] for i in range(8)] + [spare.astype(BF16), rest_ref[...]]
    rows = jnp.concatenate(rows, axis=0)
    for i in range(16):
        out_ref[i] = rows


def whole_pieces(came, rest, after=()):
    return kernel_call(
        whole_kernel,
        "whole_pieces",
        0.1,
        [came, rest],
        [((16, 9 * PIECE + SLICE, 128), BF16)],
        after=after,
    )[0]


def final_kernel(pieces_ref, wq_ref, wk_ref, wv_ref, gain_ref, *outs, experts):
    query_ref, key_ref, value_ref, output_ref, one_ref, two_ref, gains_ref, router_ref = outs
    rows = pieces_ref.shape[2]
    q_columns = query_ref.shape[1] // 8
    kv_columns = key_ref.shape[1] // 8
    sums = jnp.zeros((rows, 1), F32)
    base = 8 * PIECE
    for pair in range(4):
        keys, values = [], []
        for source in (2 * pair, 2 * pair + 1):
            block = [pieces_ref[i, source * PIECE : (source + 1) * PIECE] for i in range(16)]
            turned = jnp.concatenate(block, axis=0).astype(F32).T
            span = slice(source * q_columns, (source + 1) * q_columns)
            query = turned[:, :q_columns]
            query_ref[:, span] = query
            sums = sums + jnp.sum(query * wq_ref[:, span].astype(F32), axis=1, keepdims=True)
            keys.append(turned[:, q_columns : q_columns + kv_columns])
            values.append(turned[:, q_columns + kv_columns :])
        span = slice(2 * pair * kv_columns, 2 * (pair + 1) * kv_columns)
        for parts, ref, weight in ((keys, key_ref, wk_ref), (values, value_ref, wv_ref)):
            both = jnp.concatenate(parts, axis=1)
            ref[:, span] = both
            sums = sums + jnp.sum(both * weight[:, span].astype(F32), axis=1, keepdims=True)
    for i in range(16):
        half = i % 2 * SLICE
        output_ref[half : half + SLICE, i // 2 * rows : (i // 2 + 1) * rows] = pieces_ref[
            i, base + PIECE :
        ].astype(F32)
    spare = pieces_ref[:, base : base + PIECE].astype(F32)
    spare = jnp.concatenate([spare[i, :SPARE] for i in range(16)], axis=0)
    one_ref[...] = jnp.broadcast_to(sums, (rows, 128)).T[:1] / gain_ref[...].astype(F32)
    two_ref[...] = spare[experts : experts + 1]
    gains_ref[...] = spare[experts + 1 : experts + 3]
    router_ref[...] = spare[:experts]


def final_grads(pieces, wq, wk, wv, gain, experts):
    rows = pieces.shape[2]
    return kernel_call(
        functools.partial(final_kernel, experts=experts),
        "final_grads",
        0.2,
        [pieces, wq, wk, wv, gain],
        [
            (wq.shape, F32),
            (wk.shape, F32),
            (wv.shape, F32),
            ((rows, 8 * rows), F32),
            ((1, rows), F32),
            ((1, rows), F32),
            ((2, rows), F32),
            ((experts, rows), F32),
        ],
        held=(1, 2, 3, 4),
    )


def send(values, axis, flip):
    count = lax.axis_size(axis)
    return lax.ppermute(values, axis, [(i, i ^ flip) for i in range(count)])


def along_z(values):
    if not isinstance(values, (list, tuple)):
        values = [values] * 3
    return [send(value, "fsdp", 2 * (i + 1)) for i, value in enumerate(values)]


def gather_fsdp(block, name):
    came = along_z(block)
    return came, send(row([block, *came], name), "fsdp", 1)


def exchange(rows):
    return lax.all_to_all(rows, "expert", 0, 0, tiled=True)


def shards(
    tokens,
    lengths,
    routes,
    first_gain,
    query_weight,
    key_weight,
    value_weight,
    output_weight,
    query_gain,
    key_gain,
    second_gain,
    router_weight,
    gate_weight,
    up_weight,
    down_weight,
    cotangent,
):
    own = tokens[0]
    upstream = cotangent[0]
    rows, width = own.shape
    fsdp = lax.axis_size("fsdp")
    owners = lax.axis_size("expert")
    me = lax.axis_index("fsdp").astype(jnp.int32).reshape(1)
    owner = lax.axis_index("expert").astype(jnp.int32).reshape(1)
    experts = router_weight.shape[1]
    capacity = 3 * rows * routes.shape[2] // (2 * experts)
    kv_columns = key_weight.shape[1] // fsdp
    q_columns = query_weight.shape[1] // fsdp
    columns = q_columns + 2 * kv_columns
    q_heads = q_columns // HEAD

    packed = pack_weights(
        me,
        own,
        query_weight,
        key_weight,
        value_weight,
        router_weight.T,
        first_gain[None],
        second_gain[None],
        query_gain[None],
        key_gain[None],
    )
    x_came = along_z(packed[1:])
    dressed, mask, deal, turn = prepare(routes[0].T, upstream, experts, capacity)
    x_other = send(relay(own, packed[0], x_came), "fsdp", 1)
    c_all = lax.all_gather(dressed, "expert", axis=0)
    wo_came = along_z(output_weight)

    ends = jnp.cumsum(lengths[0])
    place = jnp.arange(rows * fsdp, dtype=jnp.int32)
    start = jnp.max(jnp.where(ends[:, None] <= place[None, :], ends[:, None], 0), axis=0)
    position = (place - start).astype(F32)
    frequency = ROPE_BASE ** (-jnp.arange(HEAD // 2, dtype=F32) * 2.0 / HEAD)
    angles = frequency[:, None] * position[None, :]
    cosine, sine = jnp.cos(angles), jnp.sin(angles)
    start = start[None, :].astype(jnp.int32)

    h1, pre, keep, give, inverse, gains, heads, turned, mixed = attention_forward(
        me, own, packed[0], x_came, x_other, cosine, sine, start, experts, q_heads
    )
    other = send(give, "fsdp", 1)
    mixed_sends, wo_stack = merge(keep, other, output_weight, wo_came)
    mixed_came = along_z(mixed_sends)
    wo_other = send(wo_stack, "fsdp", 1)
    middle, probs, hidden, sent = middle_layer(
        own, keep, other, mixed_came, output_weight, wo_came, wo_other, gains, deal, experts, owners
    )
    h_rows = exchange(sent)
    rows_c, row_mask, back = deal_rows(owner, c_all, down_weight, experts, capacity)
    rows_back, gate_low, up_low, active, weighted, share = expert_layer(
        owner, h_rows, gains, row_mask, back, gate_weight, up_weight, experts
    )
    came_back = exchange(rows_back)
    grads, tick = expert_weights(h_rows, rows_c, gate_low, up_low, weighted)
    grads = lax.psum(grads, "fsdp")
    gate_sum, up_sum, down_sum = widen(grads)
    sent, tick = expert_outputs(active, share, down_weight, owners, after=(tick,))

    middle_grad, middle_low, extra = router_backward(
        came_back, turn, middle, probs, mask, gains, upstream, hidden, experts, after=(tick,)
    )
    da_came, da_other = gather_fsdp(middle_low, "row_middle")
    out_rows = exchange(sent)
    layer_out, _ = layer_output(out_rows, turn, middle)
    first, dh_keep, dh_give = attention_backward(
        me,
        middle_low,
        da_came,
        da_other,
        heads,
        output_weight,
        cosine,
        sine,
        start,
        h1,
        pre,
        mixed,
        inverse,
        turned,
        extra,
        experts,
        q_heads,
    )
    dh_total, *dh_sends = pair_sum(dh_keep, send(dh_give, "fsdp", 1))
    dh_came = along_z(dh_sends)
    tokens_grad = input_grad(dh_total, dh_came, own, gains, middle_grad, experts)
    first = passed(first, after=(out_rows, grads))
    parted, rest = shares_sum(exchange(first), after=(dh_total,))
    parted = lax.all_to_all(parted, "fsdp", 0, 0, tiled=True)
    pieces = exchange(whole_pieces(parted, rest, after=(layer_out,)))
    query_sum, key_sum, value_sum, output_sum, one_sum, two_sum, gain_sums, router_sum = final_grads(
        pieces, query_weight, key_weight, value_weight, first_gain[None], experts
    )
    step = HEAD // fsdp
    return (
        layer_out[None],
        tokens_grad[None],
        one_sum[0],
        query_sum,
        key_sum,
        value_sum,
        output_sum,
        gain_sums[0, :step],
        gain_sums[1, :step],
        two_sum[0],
        router_sum.T,
        gate_sum,
        up_sum,
        down_sum,
    )


def solution(mesh):
    whole = P("expert", "fsdp", None)
    rows = P("fsdp", None)
    vector = P("fsdp")
    owned = P("expert", None, None)
    return jax.shard_map(
        shards,
        mesh=mesh,
        in_specs=(
            whole,
            P("expert", None),
            whole,
            vector,
            rows,
            rows,
            rows,
            rows,
            vector,
            vector,
            vector,
            rows,
            owned,
            owned,
            owned,
            whole,
        ),
        out_specs=(
            whole,
            whole,
            vector,
            rows,
            rows,
            rows,
            rows,
            vector,
            vector,
            vector,
            rows,
            owned,
            owned,
            owned,
        ),
        check_vma=False,
    )
```

```python
import functools

import jax
import jax.numpy as jnp
from jax import lax
from jax.experimental import pallas as pl
from jax.experimental.pallas import tpu as pltpu
from jax.sharding import PartitionSpec as P

EPSILON = 1e-06
ROPE_BASE = 10000.0
HEAD = 64
TILE = 256
F32 = jnp.float32
BF16 = jnp.bfloat16
VMEM = pl.BlockSpec(memory_space=pltpu.VMEM)
SMEM = pl.BlockSpec(memory_space=pltpu.SMEM)
ANY = pl.BlockSpec(memory_space=pl.ANY)
HBM = pl.BlockSpec(memory_space=pltpu.HBM)


def dot(left, right, dims=((1,), (0,))):
    return lax.dot_general(left, right, (dims, ((), ())), preferred_element_type=F32)


def shape(extent, dtype):
    return jax.ShapeDtypeStruct(extent, dtype)


def kernel_call(
    body, name, micros, operands, results, smem=0, hbm=(), out_hbm=(), after=(), scratch=(), held=(), late=(), stored=(), mib=63
):
    held = tuple(held) + tuple(late)
    n, a, r, s = len(operands), len(after), len(results), len(scratch)
    specs = [SMEM if i < smem else HBM if i in held or i in hbm else VMEM for i in range(n)]
    out_specs = [HBM if i in stored or i in out_hbm else VMEM for i in range(r)]
    staged = [pltpu.VMEM(operands[i].shape, operands[i].dtype) for i in held]
    staged += [pltpu.VMEM(*results[i]) for i in stored]
    sems = [pltpu.SemaphoreType.DMA((max(len(held), 1),)), pltpu.SemaphoreType.DMA((max(len(stored), 1),))]

    def wrapped(*refs):
        ins, outs = list(refs[:n]), list(refs[n + a : n + a + r])
        own = refs[n + a + r : n + a + r + s]
        stages, (load_sem, store_sem) = refs[n + a + r + s : -2], refs[-2:]
        loads, stores, begun = {}, {}, []
        for k, i in enumerate(held):
            loads[i] = pltpu.make_async_copy(ins[i], stages[k], load_sem.at[k])
            loads[i].start()
            ins[i] = stages[k]
        for k, i in enumerate(stored):
            stores[i] = pltpu.make_async_copy(stages[len(held) + k], outs[i], store_sem.at[k])
            outs[i] = stages[len(held) + k]
        for i in held:
            if i not in late:
                loads[i].wait()

        def store(*which):
            for i in which:
                stores[i].start()
                begun.append(i)

        extra = {}
        if late:
            extra["wait"] = lambda i: loads[i].wait()
        if stored:
            extra["store"] = store
        body(*ins, *outs, *own, **extra)
        store(*[i for i in stored if i not in begun])
        for i in stored:
            stores[i].wait()

    return pl.pallas_call(
        wrapped,
        out_shape=[shape(*result) for result in results],
        in_specs=specs + [ANY] * a,
        out_specs=out_specs,
        scratch_shapes=list(scratch) + staged + sems,
        compiler_params=pltpu.CompilerParams(vmem_limit_bytes=mib * 1024 * 1024),
        cost_estimate=pl.CostEstimate(flops=0, bytes_accessed=int(micros * 3.6e6), transcendentals=0),
        name=name,
    )(*operands, *after)


def move_call(moves, name, micros, operands, results, after=(), mib=10):
    def body(*refs):
        for source, target in moves(*refs):
            target[...] = source[...]

    return kernel_call(body, name, micros, operands, results, after=after, mib=mib)


def lane_blocks(value):
    return jnp.concatenate([value[:, i : i + 128] for i in range(0, value.shape[1], 128)], axis=0)


def joined_lanes(value, count):
    rows = value.shape[0] // count
    return jnp.concatenate([value[i * rows : (i + 1) * rows] for i in range(count)], axis=1)


def softmax_rows(logits):
    powers = jnp.exp(logits - jnp.max(logits, axis=0, keepdims=True))
    return powers / jnp.sum(powers, axis=0, keepdims=True)


def head_forward(pre, gain, cosine, sine):
    scale = lax.rsqrt(jnp.mean(pre * pre, axis=0, keepdims=True) + EPSILON)
    normed = pre * scale
    scaled = normed * gain
    a, b = scaled[: HEAD // 2], scaled[HEAD // 2 :]
    turned = jnp.concatenate([a * cosine - b * sine, b * cosine + a * sine], axis=0)
    return turned, normed, scale


def head_backward(grad, normed, scale, gain, cosine, sine):
    a, b = grad[: HEAD // 2], grad[HEAD // 2 :]
    unturned = jnp.concatenate([a * cosine + b * sine, b * cosine - a * sine], axis=0)
    gain_grad = jnp.sum(unturned * normed, axis=1, keepdims=True)
    inner = unturned * gain
    pre_grad = scale * (inner - normed * jnp.mean(inner * normed, axis=0, keepdims=True))
    return pre_grad, gain_grad


def slots_kernel(mask_ref, deal_ref, turn_ref, whole_ref, *, capacity, store):
    experts, rows = mask_ref.shape
    mask = mask_ref[...]
    ranks = dot(mask.astype(BF16), earlier(rows))
    slot = lax.broadcasted_iota(jnp.int32, (capacity, rows), 0).astype(F32) + 1.0
    for expert in range(experts):
        one = slice(expert, expert + 1)
        whole_ref[expert * capacity : (expert + 1) * capacity] = jnp.where(
            (ranks[one] == slot) & (mask[one] > 0.5), 1.0, 0.0
        )
    deal_ref[...] = whole_ref[...].astype(BF16)
    store(0)
    for part in range(0, experts * capacity, 128):
        turn_ref[:, part : part + 128] = whole_ref[part : part + 128].T.astype(BF16)


def slot_tables(mask, capacity):
    experts, rows = mask.shape
    slots = experts * capacity
    return kernel_call(
        functools.partial(slots_kernel, capacity=capacity),
        "slot_tables",
        2.0,
        [mask],
        [((slots, rows), BF16), ((rows, slots), BF16)],
        scratch=[pltpu.VMEM((slots, rows), F32)],
        stored=(0, 1),
    )


def earlier(rows):
    return (
        lax.broadcasted_iota(jnp.int32, (rows, rows), 0)
        <= lax.broadcasted_iota(jnp.int32, (rows, rows), 1)
    ).astype(BF16)


def pack_kernel(
    me_ref, x_ref, wq_ref, wk_ref, wv_ref, router_ref, one_ref, two_ref, qg_ref, kg_ref, routes_ref, c_ref, *outs, wait, store
):
    own_ref, sends, dressed_ref, mask_ref, parts_ref = outs[0], outs[1:4], outs[4], outs[5], outs[6]
    experts, rows = router_ref.shape
    wide = wq_ref.shape[1] // 8
    narrow = wk_ref.shape[1] // 8
    count = qg_ref.shape[1]
    heads = jnp.concatenate([qg_ref[...], kg_ref[...]], axis=0).astype(F32)
    heads = jnp.concatenate([heads, jnp.zeros((2, 128 - count), F32)], axis=1)
    heads = jnp.concatenate([heads, jnp.zeros((126, 128), F32)], axis=0).T[:count]
    small = jnp.concatenate(
        [
            router_ref[...].astype(F32),
            one_ref[...].astype(F32),
            two_ref[...].astype(F32),
            jnp.zeros((6, 128), F32),
            heads,
        ],
        axis=0,
    ).astype(BF16)
    for part in range(8):
        parts_ref[part, :wide] = wq_ref[:, part * wide : (part + 1) * wide].astype(F32).T.astype(BF16)
        parts_ref[part, wide + 2 * narrow :] = small
    for pair in range(4):
        span = slice(pair * 128, (pair + 1) * 128)
        for ref, place in ((wk_ref, wide), (wv_ref, wide + narrow)):
            turned = ref[:, span].astype(F32).T.astype(BF16)
            parts_ref[2 * pair, place : place + narrow] = turned[:narrow]
            parts_ref[2 * pair + 1, place : place + narrow] = turned[narrow:]
    me = me_ref[0]
    tall = parts_ref.shape[1]
    blocks = lane_blocks(x_ref[...])
    base = blocks.shape[0]
    own_ref[:tall] = parts_ref[me]
    own_ref[tall:] = parts_ref[me ^ 1]
    for flip in range(1, 4):
        sends[flip - 1][:base] = blocks
        sends[flip - 1][base : base + tall] = parts_ref[me ^ (2 * flip)]
        sends[flip - 1][base + tall :] = parts_ref[me ^ (2 * flip + 1)]
    store(0, 1, 2, 3)
    wait(10)
    wait(11)
    width = c_ref.shape[1]
    subs = lax.broadcasted_iota(jnp.int32, (128, rows), 0)
    routed = jnp.zeros((128, rows), F32)
    for route in range(routes_ref.shape[0]):
        routed = routed + jnp.where(routes_ref[route : route + 1] == subs, 1.0, 0.0)
    dressed_ref[:, :width] = c_ref[...]
    dressed_ref[:, width:] = routed.T.astype(BF16)
    mask_ref[...] = routed[:experts]


def pack_weights(me, x, wq, wk, wv, router, one, two, qg, kg, routes, c):
    experts = router.shape[0]
    tall = (wq.shape[1] + wk.shape[1] + wv.shape[1]) // 8 + experts + 16
    rows, width = x.shape
    base = rows * 8
    own, first, second, third, dressed, mask = kernel_call(
        pack_kernel,
        "pack_weights",
        2.5,
        [me, x, wq, wk, wv, router, one, two, qg, kg, routes, c],
        [((2 * tall, 128), BF16)]
        + [((base + 2 * tall, 128), BF16)] * 3
        + [((rows, width + 128), BF16), ((experts, rows), F32)],
        smem=1,
        scratch=[pltpu.VMEM((8, tall, 128), BF16)],
        held=range(1, 10),
        late=(10, 11),
        stored=(0, 1, 2, 3, 4, 5),
    )
    return own, [first, second, third], dressed, mask


def relay(x, own, came):
    tall = own.shape[0] // 2
    base = came[0].shape[0] - 2 * tall
    rows, blocks = x.shape[0], x.shape[1] // 128

    def body(x_ref, own_ref, *refs):
        out_ref = refs[3]
        out_ref[0, :base] = lane_blocks(x_ref[...])
        out_ref[0, base:] = own_ref[tall:]
        for flip in range(1, 4):
            out_ref[flip, :base] = refs[flip - 1][:base]
            out_ref[flip, base:] = refs[flip - 1][base + tall :]

    return kernel_call(
        body, "relay", 1.5, [x, own, *came], [((4, base + tall, 128), BF16)], held=(0, 1), mib=10
    )[0]


def forward_kernel(me_ref, x_ref, own_ref, *refs, experts, q_heads, store):
    came, other_ref = refs[:3], refs[3]
    cos_ref, sin_ref, start_ref = refs[4:7]
    h1_ref, pre_ref, keep_ref, give_ref, inverse_ref, gains_ref, heads_ref, turned_ref, out_ref = refs[-9:]
    rows, width = x_ref.shape
    q_columns = q_heads * HEAD
    columns = q_columns + 2 * HEAD
    total = rows * 8
    tall = own_ref.shape[0] // 2
    base = 8 * rows
    me = me_ref[0]
    for slot in range(8):
        flip = slot // 2
        if slot % 2:
            piece = other_ref[flip, base:]
        elif flip:
            piece = came[flip - 1][base : base + tall]
        else:
            piece = own_ref[:tall]
        span = pl.ds(pl.multiple_of((me ^ slot) * rows, rows), rows)
        turned_ref[:, span] = piece[:columns]
        small = piece[columns:].astype(F32)
        gains_ref[:, span] = small[: experts + 8]
        heads_ref[pl.ds(pl.multiple_of((me ^ slot) * 8, 8), 8)] = small[experts + 8 :]
    gain_one = gains_ref[experts : experts + 1]
    for slot in range(8):
        flip = slot // 2
        if slot % 2:
            x = joined_lanes(other_ref[flip, :base], 8)
        elif flip:
            x = joined_lanes(came[flip - 1][:base], 8)
        else:
            x = x_ref[...]
        x = x.astype(F32)
        scale = lax.rsqrt(jnp.mean(x * x, axis=1, keepdims=True) + EPSILON)
        h1_ref[slot] = (x * scale * gain_one).astype(BF16)
    store(0, 6, 7)
    for slot in range(8):
        block = dot(turned_ref[...], h1_ref[slot], ((1,), (1,)))
        place = pl.multiple_of((me ^ slot) * rows, rows)
        pre_ref[:, pl.ds(place, rows)] = block
    store(1)
    cosine, sine = cos_ref[...], sin_ref[...]
    gain_query, gain_key = heads_ref[:, :1], heads_ref[:, 1:2]
    key = head_forward(pre_ref[q_columns : q_columns + HEAD], gain_key, cosine, sine)[0]
    key = key.T.astype(BF16)
    value = pre_ref[q_columns + HEAD :].astype(BF16)
    inverse_ref[...] = jnp.zeros(inverse_ref.shape, F32)
    for head in range(q_heads):
        query = head_forward(pre_ref[head * HEAD : (head + 1) * HEAD], gain_query, cosine, sine)[0]
        query = query.astype(BF16) * jnp.array(HEAD ** (-0.5), BF16)
        for tile in range(total // TILE):
            low, high = tile * TILE, (tile + 1) * TILE
            scores = dot(key[:high], query[:, low:high])
            u = lax.broadcasted_iota(jnp.int32, (high, TILE), 0)
            t = lax.broadcasted_iota(jnp.int32, (high, TILE), 1) + low
            allowed = (u >= start_ref[:, low:high]) & (u <= t)
            powers = jnp.where(allowed, jnp.exp(scores), 0.0)
            inverse = 1.0 / jnp.sum(powers, axis=0, keepdims=True)
            probs = (powers * inverse).astype(BF16)
            mixed = dot(value[:, :high], probs).astype(BF16)
            inverse_ref[head : head + 1, low:high] = inverse
            for part in range(TILE // rows):
                out_ref[low // rows + part, head * HEAD : (head + 1) * HEAD] = mixed[
                    :, part * rows : (part + 1) * rows
                ]
    for slot in range(8):
        (give_ref if slot % 2 else keep_ref)[slot // 2] = out_ref[me ^ slot]


def attention_forward(me, x, own, came, other, cosine, sine, start, experts, q_heads, after=()):
    rows, width = x.shape
    total = 8 * rows
    columns = (q_heads + 2) * HEAD
    q_columns = q_heads * HEAD
    return kernel_call(
        functools.partial(forward_kernel, experts=experts, q_heads=q_heads),
        "attention_forward",
        7.0,
        [me, x, own, *came, other, cosine, sine, start],
        [
            ((8, rows, width), BF16),
            ((columns, total), F32),
            ((4, q_columns, rows), BF16),
            ((4, q_columns, rows), BF16),
            ((8, total), F32),
            ((experts + 8, width), F32),
            ((HEAD, 128), F32),
            ((columns, width), BF16),
            ((8, q_columns, rows), BF16),
        ],
        smem=1,
        after=after,
        held=(1,),
        stored=(0, 1, 4, 6, 7, 8),
    )


def merge(keep, came, wo, wo_came):
    def moves(keep_ref, came_ref, *refs):
        weights, outs, stacked = refs[:4], refs[4:7], refs[7]
        pairs = [(weight, stacked.at[i]) for i, weight in enumerate(weights)]
        for flip in range(1, 4):
            pairs.append((keep_ref.at[flip], outs[flip - 1].at[0]))
            pairs.append((came_ref.at[flip], outs[flip - 1].at[1]))
        return pairs

    extent = ((2,) + keep.shape[1:], BF16)
    results = [extent] * 3 + [((4,) + wo.shape, BF16)]
    *sends, stacked = move_call(moves, "merge", 1.0, [keep, came, wo, *wo_came], results)
    return sends, stacked


def middle_kernel(x_ref, keep_ref, other_ref, *refs, experts, wait, store):
    came, wo_ref, wo_came, wo_other_ref, gains_ref, deal_ref = refs[:3], refs[3], refs[4:7], refs[7], refs[8], refs[9]
    middle_ref, probs_ref, hidden_ref, sent_ref, mixed_ref, whole_ref, out_ref, out_sem = refs[10:]
    rows, width = x_ref.shape
    for slot in range(8):
        flip, core = slot // 2, slot % 2
        if flip:
            piece = came[flip - 1][core]
        else:
            piece = (other_ref if core else keep_ref)[0]
        span = slice(slot * 128, (slot + 1) * 128)
        mixed_ref[:, span] = piece.astype(F32).T.astype(BF16)
    for i in (6, 7, 8, 9, 10):
        wait(i)
    for slot in range(8):
        flip = slot // 2
        span = slice(slot * 128, (slot + 1) * 128)
        if slot % 2:
            whole_ref[span] = wo_other_ref[flip]
        else:
            whole_ref[span] = (wo_came[flip - 1] if flip else wo_ref)[...]
    wait(0)
    middle = x_ref[...].astype(F32) + dot(mixed_ref[...], whole_ref[...])
    middle_ref[...] = middle
    scale = lax.rsqrt(jnp.mean(middle * middle, axis=1, keepdims=True) + EPSILON)
    hidden = (middle * scale * gains_ref[experts + 1 : experts + 2]).astype(BF16)
    hidden_ref[...] = hidden
    probs_ref[...] = softmax_rows(dot(gains_ref[:experts].astype(BF16), hidden, ((1,), (1,))))
    store(0, 2)
    owners, per_owner, capacity, _ = sent_ref.shape
    group = owners // 4
    size = group * per_owner * capacity
    copies = []
    wait(12)
    for part in range(4):
        taken = dot(deal_ref[part * size : (part + 1) * size], hidden).astype(BF16)
        blocks = slice(group * part, group * (part + 1))
        out_ref[blocks] = taken.reshape(group, per_owner, capacity, width)
        copies.append(pltpu.make_async_copy(out_ref.at[blocks], sent_ref.at[blocks], out_sem.at[part]))
        copies[-1].start()
    for copy in copies:
        copy.wait()


def middle_layer(x, keep, other, came, wo, wo_came, wo_other, gains, deal, experts, owners):
    rows, width = x.shape
    per_owner = experts // owners
    capacity = deal.shape[0] // experts
    sent = ((owners, per_owner, capacity, width), BF16)
    return kernel_call(
        functools.partial(middle_kernel, experts=experts),
        "middle_layer",
        3.0,
        [x, keep, other, *came, wo, *wo_came, wo_other, gains, deal],
        [((rows, width), F32), ((experts, rows), F32), ((rows, width), BF16), sent],
        out_hbm=(3,),
        scratch=[
            pltpu.VMEM((rows, width), BF16),
            pltpu.VMEM((width, width), BF16),
            pltpu.VMEM(*sent),
            pltpu.SemaphoreType.DMA((4,)),
        ],
        late=(6, 7, 8, 9, 10, 0, 12),
        stored=(0, 2),
    )


def row(pieces, name):
    def moves(*refs):
        return [(ref, refs[-1].at[i]) for i, ref in enumerate(refs[:-1])]

    return move_call(moves, name, 1.0, pieces, [((len(pieces),) + pieces[0].shape, BF16)])[0]


def backward_kernel(me_ref, own_da_ref, *refs, experts, q_heads, wait):
    came, other_ref = refs[:3], refs[3]
    heads_ref, wo_ref, cos_ref, sin_ref, start_ref = refs[4:9]
    h1_ref, pre_ref, mixed_ref, inverse_ref, turned_ref, extra_ref = refs[9:15]
    first_ref, keep_ref, send_ref = refs[-10:-7]
    da_ref, mixed_grad_ref, dkey_ref, dvalue_ref, low_ref, out_slots_ref, grad_ref = refs[-7:]
    rows, width = own_da_ref.shape
    q_columns = q_heads * HEAD
    columns = q_columns + 2 * HEAD
    total = rows * 8
    me = me_ref[0]
    for slot in range(8):
        flip, core = slot // 2, slot % 2
        if core:
            piece = other_ref[flip]
        else:
            piece = (came[flip - 1] if flip else own_da_ref)[...]
        span = slice(slot * rows, (slot + 1) * rows)
        da_ref[span] = piece
        place = pl.multiple_of((me ^ slot) * rows, rows)
        mixed_grad_ref[:, pl.ds(place, rows)] = dot(wo_ref[...], piece, ((1,), (1,))).astype(BF16)
    wait(13)
    for slot in range(8):
        out_slots_ref[:, slot * rows : (slot + 1) * rows] = mixed_ref[me ^ slot]
    wo_grad = dot(out_slots_ref[...], da_ref[...]).astype(BF16)
    wo_grad = lane_blocks(wo_grad)
    wait(12)
    wait(14)
    gain_query, gain_key = heads_ref[:, :1], heads_ref[:, 1:2]
    cosine, sine = cos_ref[...], sin_ref[...]
    key_turned, key_normed, key_scale = head_forward(
        pre_ref[q_columns : q_columns + HEAD], gain_key, cosine, sine
    )
    key_low = key_turned.astype(BF16)
    key = key_turned.T.astype(BF16)
    value = pre_ref[q_columns + HEAD :].T.astype(BF16)
    dkey_ref[...] = jnp.zeros(dkey_ref.shape, F32)
    dvalue_ref[...] = jnp.zeros(dvalue_ref.shape, F32)
    gain_query_grad = jnp.zeros((HEAD, 1), F32)
    pieces = []
    for head in range(q_heads):
        span = slice(head * HEAD, (head + 1) * HEAD)
        turned, normed, scale = head_forward(pre_ref[span], gain_query, cosine, sine)
        query = turned.astype(BF16) * jnp.array(HEAD ** (-0.5), BF16)
        grads = []
        for tile in range(total // TILE):
            low, high = tile * TILE, (tile + 1) * TILE
            part = query[:, low:high]
            mixed_grad = mixed_grad_ref[span, low:high]
            scores = dot(key[:high], part)
            u = lax.broadcasted_iota(jnp.int32, (high, TILE), 0)
            t = lax.broadcasted_iota(jnp.int32, (high, TILE), 1) + low
            allowed = (u >= start_ref[:, low:high]) & (u <= t)
            probs = jnp.where(allowed, jnp.exp(scores) * inverse_ref[head : head + 1, low:high], 0.0)
            attend = dot(value[:high], mixed_grad)
            delta = jnp.sum(probs * attend, axis=0, keepdims=True)
            score_low = (probs * (attend - delta)).astype(BF16)
            grads.append(dot(key_low[:, :high], score_low))
            dkey_ref[:, :high] += dot(part, score_low, ((1,), (1,)))
            dvalue_ref[:, :high] += dot(mixed_grad, probs.astype(BF16), ((1,), (1,)))
        query_grad = jnp.concatenate(grads, axis=1) * HEAD ** (-0.5)
        pre_grad, gain_grad = head_backward(query_grad, normed, scale, gain_query, cosine, sine)
        gain_query_grad += gain_grad
        pieces.append(pre_grad)
    pre_grad, gain_key_grad = head_backward(
        dkey_ref[...], key_normed, key_scale, gain_key, cosine, sine
    )
    pieces += [pre_grad, dvalue_ref[...]]
    pre_grad = jnp.concatenate(pieces, axis=0)
    low_ref[...] = pre_grad.astype(BF16)
    slots_grad = []
    for slot in range(8):
        place = pl.multiple_of((me ^ slot) * rows, rows)
        slots_grad.append(low_ref[:, pl.ds(place, rows)])
    slots_grad = jnp.concatenate(slots_grad, axis=1)
    wait(11)
    wait(15)
    grad_ref[:columns] = dot(slots_grad, h1_ref[...].reshape(total, width))
    extra = extra_ref[...]
    lane = lax.broadcasted_iota(jnp.int32, (HEAD, 128), 1)
    gains = jnp.where(lane == 0, gain_query_grad, jnp.where(lane == 1, gain_key_grad, 0.0))
    gains = gains.T[:2]
    step = HEAD // 8
    grad_ref[columns:] = jnp.zeros((64, width), F32)
    grad_ref[columns : columns + experts + 1] = extra[: experts + 1]
    for part in range(8):
        grad_ref[columns + experts + 1 : columns + experts + 3, part * rows : part * rows + step] = gains[
            :, part * step : (part + 1) * step
        ]
    for piece in range(16):
        spare = []
        place = columns + piece * SPARE
        for part in range(8):
            span = slice(part * rows, (part + 1) * rows)
            block = grad_ref[piece * PIECE : (piece + 1) * PIECE, span]
            first_ref[piece, part * PIECE : (part + 1) * PIECE] = block.astype(BF16)
            spare.append(grad_ref[place : place + SPARE, span])
        spare.append(jnp.zeros((2 * PIECE - 8 * SPARE, 128), F32))
        first_ref[piece, 8 * PIECE : 10 * PIECE] = jnp.concatenate(spare, axis=0).astype(BF16)
        first_ref[piece, 10 * PIECE :] = wo_grad[piece * SLICE : (piece + 1) * SLICE]
    turned = turned_ref[...]
    for slot in range(8):
        low_rows_slot = slots_grad[:, slot * rows : (slot + 1) * rows].astype(F32).T.astype(BF16)
        part = dot(low_rows_slot, turned)
        if slot % 2:
            send_ref[slot // 2] = part.astype(BF16)
        else:
            keep_ref[slot // 2] = part


def attention_backward(
    me, da, came, other, heads, wo, cosine, sine, start, h1, pre, mixed, inverse, turned, extra, experts, q_heads, after=()
):
    rows, width = da.shape
    total = 8 * rows
    columns = pre.shape[0]
    q_columns = q_heads * HEAD
    return kernel_call(
        functools.partial(backward_kernel, experts=experts, q_heads=q_heads),
        "attention_backward",
        12,
        [me, da, *came, other, heads, wo, cosine, sine, start, h1, pre, mixed, inverse, turned, extra],
        [
            ((16, 10 * PIECE + SLICE, 128), BF16),
            ((4, rows, width), F32),
            ((4, rows, width), BF16),
        ],
        smem=1,
        after=after,
        held=(6, 7),
        late=(11, 12, 13, 14, 15),
        scratch=[
            pltpu.VMEM((total, width), BF16),
            pltpu.VMEM((q_columns, total), BF16),
            pltpu.VMEM((HEAD, total), F32),
            pltpu.VMEM((HEAD, total), F32),
            pltpu.VMEM((columns, total), BF16),
            pltpu.VMEM((q_columns, total), BF16),
            pltpu.VMEM((columns + 64, width), F32),
        ],
    )


def deal_kernel(owner_ref, c_ref, down_ref, rows_c, mask_ref, back_ref, c_scratch, sems, *, experts, capacity, wait, store):
    owner = owner_ref[0]
    per_owner, hidden, width = down_ref.shape
    rows = c_ref.shape[1]
    loads = [pltpu.make_async_copy(c_ref.at[i], c_scratch.at[i], sems.at[i]) for i in range(16)]
    for load in loads:
        load.start()
    lanes = lax.broadcasted_iota(jnp.int32, (experts, 128), 1)
    subs = lax.broadcasted_iota(jnp.int32, (experts, 128), 0)
    eye = (lanes == subs).astype(BF16)
    before = earlier(rows)
    mine_of = lax.broadcasted_iota(jnp.int32, (experts, rows), 0) - owner * per_owner
    slot = lax.broadcasted_iota(jnp.int32, (capacity, rows), 0).astype(F32) + 1.0
    for block in range(16):
        loads[block].wait()
        c = c_scratch[block]
        mask = dot(eye, c[:, width:], ((1,), (1,)))
        ranks = dot(mask.astype(BF16), before)
        deals = []
        for k in range(per_owner):
            mine = mine_of == k
            hit = jnp.sum(jnp.where(mine, mask, 0.0), axis=0, keepdims=True)
            rank = jnp.sum(jnp.where(mine, ranks, 0.0), axis=0, keepdims=True)
            deals.append(jnp.where((rank == slot) & (hit > 0.5), 1.0, 0.0))
        taken = dot(jnp.concatenate(deals, axis=0).astype(BF16), c).astype(BF16)
        span = slice(block * capacity, (block + 1) * capacity)
        for k in range(per_owner):
            spot = slice(k * capacity, (k + 1) * capacity)
            rows_c[k, span] = taken[spot, :width]
            mask_ref[k, span] = taken[spot, width:]
    store(0, 1)
    wait(2)
    for k in range(per_owner):
        for tile in range(16 * capacity // TILE):
            span = slice(tile * TILE, (tile + 1) * TILE)
            back_ref[k, span] = dot(rows_c[k, span], down_ref[k], ((1,), (1,)))


def deal_rows(owner, c, down, experts, capacity):
    per_owner, hidden, width = down.shape
    count = 16 * capacity
    return kernel_call(
        functools.partial(deal_kernel, experts=experts, capacity=capacity),
        "deal_rows",
        12.0,
        [owner, c, down],
        [
            ((per_owner, count, width), BF16),
            ((per_owner, count, 128), BF16),
            ((per_owner, count, hidden), F32),
        ],
        smem=1,
        hbm=(1,),
        scratch=[pltpu.VMEM(c.shape, BF16), pltpu.SemaphoreType.DMA((16,))],
        late=(2,),
        stored=(0, 1, 2),
    )


def expert_kernel(
    owner_ref,
    h_hbm,
    gains_ref,
    mask_ref,
    back_hbm,
    gate_hbm,
    up_hbm,
    rows_hbm,
    gate_out,
    up_out,
    active_out,
    weighted_out,
    share_ref,
    h_ref,
    back_in,
    gate_ref,
    up_ref,
    rows_back,
    load_sem,
    store_sem,
    *,
    experts,
    store,
):
    owners, per_owner, capacity, width = h_hbm.shape
    group = 8
    parts = owners // group
    size = group * capacity
    loads = {}
    for k in range(per_owner):
        for part in range(parts):
            blocks = slice(part * group, (part + 1) * group)
            spot = (k * parts + part) * 4
            loads[k, part] = [
                pltpu.make_async_copy(h_hbm.at[blocks, k], h_ref.at[blocks, k], load_sem.at[spot]),
                pltpu.make_async_copy(
                    back_hbm.at[k, part * size : (part + 1) * size],
                    back_in.at[k, part * size : (part + 1) * size],
                    load_sem.at[spot + 1],
                ),
            ]
            if part == 0:
                loads[k, part] += [
                    pltpu.make_async_copy(gate_hbm.at[k], gate_ref.at[k], load_sem.at[spot + 2]),
                    pltpu.make_async_copy(up_hbm.at[k], up_ref.at[k], load_sem.at[spot + 3]),
                ]
            for load in loads[k, part]:
                load.start()
    owner = owner_ref[0]
    router = jnp.concatenate([gains_ref[:experts], jnp.zeros((128 - experts, width), F32)], axis=0)
    router = router.astype(BF16)
    lane = lax.broadcasted_iota(jnp.int32, (size, 128), 1)
    copies = []
    for k in range(per_owner):
        place = owner * per_owner + k
        for part in range(parts):
            blocks = slice(part * group, (part + 1) * group)
            span = slice(part * size, (part + 1) * size)
            for load in loads[k, part]:
                load.wait()
            h = h_ref[blocks, k].reshape(size, width)
            gate = dot(h, gate_ref[k])
            up = dot(h, up_ref[k])
            logits = dot(h, router, ((1,), (1,)))
            chosen = mask_ref[k, span] > 0.5
            top = jnp.max(jnp.where(chosen, logits, -1e30), axis=1, keepdims=True)
            powers = jnp.where(chosen, jnp.exp(logits - top), 0.0)
            total = jnp.sum(powers, axis=1, keepdims=True)
            share = jnp.sum(jnp.where(lane == place, powers, 0.0), axis=1, keepdims=True)
            share = share / jnp.where(total > 0.0, total, 1.0)
            share_ref[k, span] = jnp.broadcast_to(share, (size, 128))
            back = back_in[k, span]
            sig = 1.0 / (1.0 + jnp.exp(-gate))
            silu = gate * sig
            active = silu * up
            active_low = active.astype(BF16)
            route_grad = jnp.sum(active_low.astype(F32) * back, axis=1, keepdims=True)
            grad = back * share
            gate_low = (grad * up * (sig + silu * (1.0 - sig))).astype(BF16)
            up_low = (grad * silu).astype(BF16)
            active_out[k, span] = active_low
            weighted_out[k, span] = (active * share).astype(BF16)
            gate_out[k, span] = gate_low
            up_out[k, span] = up_low
            rows = dot(gate_low, gate_ref[k], ((1,), (1,))) + dot(up_low, up_ref[k], ((1,), (1,)))
            high = route_grad.astype(BF16).astype(F32)
            spread_out = jnp.where(lane == place, high, 0.0)
            spread_out = jnp.where(lane == place + experts, route_grad - high, spread_out)
            whole = jnp.concatenate([rows.astype(BF16), spread_out.astype(BF16)], axis=1)
            rows_back[blocks, k] = whole.reshape(group, capacity, width + 128)
            copies.append(
                pltpu.make_async_copy(
                    rows_back.at[blocks, k], rows_hbm.at[blocks, k], store_sem.at[k * parts + part]
                )
            )
            copies[-1].start()
    store(1, 2, 3, 4, 5)
    for copy in copies:
        copy.wait()


def expert_layer(owner, h, gains, mask, back, gate, up, experts):
    per_owner, width, hidden = gate.shape
    owners, _, capacity, _ = h.shape
    count = owners * capacity
    narrow = ((per_owner, count, hidden), BF16)
    rows_back = ((owners, per_owner, capacity, width + 128), BF16)
    pieces = per_owner * (owners // 8)
    return kernel_call(
        functools.partial(expert_kernel, experts=experts),
        "expert_layer",
        14.0,
        [owner, h, gains, mask, back, gate, up],
        [rows_back] + [narrow] * 4 + [((per_owner, count, 128), F32)],
        smem=1,
        hbm=(1, 4, 5, 6),
        out_hbm=(0,),
        scratch=[pltpu.VMEM(value.shape, value.dtype) for value in (h, back, gate, up)]
        + [pltpu.VMEM(*rows_back), pltpu.SemaphoreType.DMA((4 * pieces,)), pltpu.SemaphoreType.DMA((pieces,))],
        stored=(1, 2, 3, 4, 5),
    )


def weights_kernel(h_ref, rows_c, gate_low, up_low, weighted, out_ref, tick_ref, *, wait, store):
    tick_ref[...] = jnp.zeros(tick_ref.shape, F32)
    first = ((0,), (0,))
    owners, per_owner, capacity, width = h_ref.shape
    hidden = gate_low.shape[2]
    half = width // 2
    for i in (0, 2, 3):
        wait(i)
    for k in range(per_owner):
        rows_h = h_ref[:, k].reshape(owners * capacity, width)
        for place, low in ((k, gate_low), (per_owner + k, up_low)):
            total = dot(rows_h, low[k], first).astype(BF16)
            out_ref[place, :, :hidden] = total[:half]
            out_ref[place, :, hidden:] = total[half:]
        if k == 0:
            wait(1)
            wait(4)
        out_ref[2 * per_owner + k] = dot(weighted[k], rows_c[k], first).astype(BF16)


def expert_weights(h, rows_c, gate_low, up_low, weighted):
    per_owner, count, width = rows_c.shape
    hidden = gate_low.shape[2]
    return kernel_call(
        weights_kernel,
        "expert_weights",
        0.1,
        [h, rows_c, gate_low, up_low, weighted],
        [((3 * per_owner, hidden, width), BF16), ((8, 128), F32)],
        late=(0, 1, 2, 3, 4),
        stored=(0,),
    )


def widen_kernel(low_ref, gate_ref, up_ref, down_ref):
    step = pl.program_id(0)
    hidden = gate_ref.shape[2]
    value = low_ref[0].astype(F32)
    half = value.shape[0]
    for place, ref in ((0, gate_ref), (1, up_ref)):

        @pl.when(step // 2 == place)
        def _():
            ref[0, :half] = value[:, :hidden]
            ref[0, half:] = value[:, hidden:]

    @pl.when(step // 2 == 2)
    def _():
        down_ref[0] = value


def widen(low):
    count, hidden, width = low.shape
    per_owner = count // 3

    def spot(place):
        return lambda i: (jnp.clip(i - place * per_owner, 0, per_owner - 1), 0, 0)

    return pl.pallas_call(
        widen_kernel,
        grid=(count,),
        out_shape=[shape((per_owner, width, hidden), F32)] * 2 + [shape((per_owner, hidden, width), F32)],
        in_specs=[pl.BlockSpec((1, hidden, width), lambda i: (i, 0, 0))],
        out_specs=[
            pl.BlockSpec((1, width, hidden), spot(0)),
            pl.BlockSpec((1, width, hidden), spot(1)),
            pl.BlockSpec((1, hidden, width), spot(2)),
        ],
        compiler_params=pltpu.CompilerParams(vmem_limit_bytes=63 * 1024 * 1024),
        cost_estimate=pl.CostEstimate(flops=0, bytes_accessed=24_000_000, transcendentals=0),
        name="widen",
    )(low)


def outputs_kernel(active, share, down_ref, sent_ref, tick_ref, out_ref, out_sem, *, wait):
    tick_ref[...] = jnp.zeros(tick_ref.shape, F32)
    per_owner, count, hidden = active.shape
    owners, _, capacity, width = sent_ref.shape
    group = 8
    size = group * capacity
    copies = []
    for i in range(3):
        wait(i)
    for k in range(per_owner):
        for part in range(owners // group):
            span = slice(part * size, (part + 1) * size)
            blocks = slice(part * group, (part + 1) * group)
            produced = dot(active[k, span], down_ref[k]).astype(BF16).astype(F32)
            produced = (produced * share[k, span, :1]).astype(BF16)
            out_ref[blocks, k] = produced.reshape(group, capacity, width)
            copies.append(
                pltpu.make_async_copy(
                    out_ref.at[blocks, k], sent_ref.at[blocks, k], out_sem.at[k * (owners // group) + part]
                )
            )
            copies[-1].start()
    for copy in copies:
        copy.wait()


def expert_outputs(active, share, down, owners, after=()):
    per_owner, count, hidden = active.shape
    width = down.shape[2]
    sent = ((owners, per_owner, count // owners, width), BF16)
    return kernel_call(
        outputs_kernel,
        "expert_outputs",
        0.1,
        [active, share, down],
        [sent, ((8, 128), F32)],
        out_hbm=(0,),
        after=after,
        scratch=[pltpu.VMEM(*sent), pltpu.SemaphoreType.DMA((per_owner * (owners // 8),))],
        late=(0, 1, 2),
    )


def combined(rows_hbm, rows_ref, sems, turn_ref, ready):
    owners, per_owner, capacity, wide = rows_hbm.shape
    group = owners // 4
    size = group * per_owner * capacity
    loads = []
    for part in range(4):
        blocks = slice(part * group, (part + 1) * group)
        loads.append(pltpu.make_async_copy(rows_hbm.at[blocks], rows_ref.at[blocks], sems.at[part]))
        loads[-1].start()
    ready()
    total = None
    for part in range(4):
        loads[part].wait()
        rows = rows_ref[part * group : (part + 1) * group].reshape(size, wide)
        one = dot(turn_ref[:, part * size : (part + 1) * size], rows)
        total = one if total is None else total + one
    return total


def output_kernel(rows_hbm, turn_ref, middle_ref, out_ref, tick_ref, rows_ref, sems, *, wait, store):
    tick_ref[...] = jnp.zeros(tick_ref.shape, F32)
    total = combined(rows_hbm, rows_ref, sems, turn_ref, lambda: wait(1))
    wait(2)
    out_ref[...] = (middle_ref[...] + total).astype(BF16)


def layer_output(rows, turn, middle):
    return kernel_call(
        output_kernel,
        "layer_output",
        3,
        [rows, turn, middle],
        [(middle.shape, BF16), ((8, 128), F32)],
        hbm=(0,),
        scratch=[pltpu.VMEM(rows.shape, BF16), pltpu.SemaphoreType.DMA((4,))],
        late=(1, 2),
        stored=(0,),
    )


def router_kernel(
    rows_hbm,
    turn_ref,
    middle_ref,
    probs_ref,
    mask_ref,
    gains_ref,
    c_ref,
    hidden_ref,
    grad_ref,
    send_ref,
    extra_ref,
    rows_ref,
    sems,
    *,
    experts,
    wait,
    store,
):
    rows, width = middle_ref.shape
    returned = combined(rows_hbm, rows_ref, sems, turn_ref, lambda: wait(1))
    for i in (2, 4, 6, 7):
        wait(i)
    tail = returned[:, width:].T
    route_grad = tail[:experts] + tail[experts : 2 * experts]
    mask = mask_ref[...]
    probs = probs_ref[...]
    picked = probs * mask
    picked_sum = jnp.sum(picked, axis=0, keepdims=True)
    share = picked / picked_sum
    picked_grad = (route_grad - jnp.sum(route_grad * share, axis=0, keepdims=True)) / picked_sum
    prob_grad = mask * picked_grad
    logit_grad = probs * (prob_grad - jnp.sum(probs * prob_grad, axis=0, keepdims=True))
    extra_ref[:experts] = dot(logit_grad.astype(BF16), hidden_ref[...])
    logit_rows = jnp.concatenate([logit_grad, jnp.zeros((128 - experts, rows), F32)], axis=0).T
    router = gains_ref[:experts].astype(BF16)
    hidden_grad = returned[:, :width] + dot(logit_rows[:, :experts].astype(BF16), router)
    middle = middle_ref[...]
    scale = lax.rsqrt(jnp.mean(middle * middle, axis=1, keepdims=True) + EPSILON)
    normed = middle * scale
    extra_ref[experts : experts + 8] = jnp.broadcast_to(
        jnp.sum(hidden_grad * normed, axis=0, keepdims=True), (8, width)
    )
    inner = hidden_grad * gains_ref[experts + 1 : experts + 2]
    grad = c_ref[...].astype(F32) + scale * (
        inner - normed * jnp.mean(inner * normed, axis=1, keepdims=True)
    )
    grad_ref[...] = grad
    send_ref[...] = grad.astype(BF16)


def router_backward(rows_back, turn, middle, probs, mask, gains, c, hidden, experts, after=()):
    rows, width = middle.shape
    return kernel_call(
        functools.partial(router_kernel, experts=experts),
        "router_backward",
        5,
        [rows_back, turn, middle, probs, mask, gains, c, hidden],
        [((rows, width), F32), ((rows, width), BF16), ((experts + 8, width), F32)],
        hbm=(0,),
        after=after,
        scratch=[pltpu.VMEM(rows_back.shape, BF16), pltpu.SemaphoreType.DMA((4,))],
        late=(1, 2, 4, 6, 7),
        stored=(0,),
    )


def pair_kernel(keep_ref, other_ref, total_ref, *sends):
    for flip in range(4):
        total = keep_ref[flip] + other_ref[flip].astype(F32)
        if flip:
            sends[flip - 1][...] = total.astype(BF16)
        else:
            total_ref[...] = total


def pair_sum(keep, other):
    rows, width = keep.shape[1:]
    return kernel_call(
        pair_kernel, "pair_sum", 1.2, [keep, other], [((rows, width), F32)] + [((rows, width), BF16)] * 3
    )


def input_kernel(total_ref, *refs, experts, store):
    came = refs[:3]
    x_ref, gains_ref, middle_grad_ref, out_ref = refs[3:]
    total = total_ref[...]
    for piece in came:
        total = total + piece[...].astype(F32)
    x = x_ref[...].astype(F32)
    scale = lax.rsqrt(jnp.mean(x * x, axis=1, keepdims=True) + EPSILON)
    normed = x * scale
    inner = total * gains_ref[experts : experts + 1]
    out_ref[...] = middle_grad_ref[...] + scale * (
        inner - normed * jnp.mean(inner * normed, axis=1, keepdims=True)
    )


def input_grad(total, came, x, gains, middle_grad, experts):
    return kernel_call(
        functools.partial(input_kernel, experts=experts),
        "input_grad",
        2,
        [total, *came, x, gains, middle_grad],
        [(middle_grad.shape, F32)],
        held=(4, 6),
        stored=(0,),
    )[0]


PIECE, SPARE, SLICE = 16, 3, 64


def passed(value, after):
    results = [(value.shape, value.dtype)]
    return move_call(lambda *refs: [refs], "passed", 0.5, [value], results, after, 63)[0]


def shares_kernel(pieces_ref, out_ref, rest_ref):
    total = pieces_ref[0].astype(F32)
    for i in range(1, pieces_ref.shape[0]):
        total = total + pieces_ref[i].astype(F32)
    base = 8 * PIECE
    fill = jnp.zeros((PIECE - SPARE, 128), F32)
    for part in range(8):
        out_ref[part, :PIECE] = total[part * PIECE : (part + 1) * PIECE].astype(BF16)
        spare = total[base + part * SPARE : base + (part + 1) * SPARE]
        out_ref[part, PIECE:] = jnp.concatenate([spare, fill], axis=0).astype(BF16)
    rest_ref[...] = total[base + 2 * PIECE :].astype(BF16)


def shares_sum(pieces, after=()):
    return kernel_call(
        shares_kernel,
        "shares_sum",
        0.1,
        [pieces],
        [((8, 2 * PIECE, 128), BF16), ((SLICE, 128), BF16)],
        after=after,
    )


def whole_kernel(came_ref, rest_ref, out_ref):
    spare = came_ref[0, PIECE:].astype(F32)
    for i in range(1, 8):
        spare = spare + came_ref[i, PIECE:].astype(F32)
    rows = [came_ref[i, :PIECE] for i in range(8)] + [spare.astype(BF16), rest_ref[...]]
    rows = jnp.concatenate(rows, axis=0)
    for i in range(16):
        out_ref[i] = rows


def whole_pieces(came, rest, after=()):
    return kernel_call(
        whole_kernel,
        "whole_pieces",
        0.1,
        [came, rest],
        [((16, 9 * PIECE + SLICE, 128), BF16)],
        after=after,
    )[0]


def final_kernel(pieces_ref, wq_ref, wk_ref, wv_ref, gain_ref, *outs, experts):
    query_ref, key_ref, value_ref, output_ref, one_ref, two_ref, gains_ref, router_ref = outs
    rows = pieces_ref.shape[2]
    q_columns = query_ref.shape[1] // 8
    kv_columns = key_ref.shape[1] // 8
    sums = jnp.zeros((rows, 1), F32)
    base = 8 * PIECE
    for pair in range(4):
        keys, values = [], []
        for source in (2 * pair, 2 * pair + 1):
            block = [pieces_ref[i, source * PIECE : (source + 1) * PIECE] for i in range(16)]
            turned = jnp.concatenate(block, axis=0).astype(F32).T
            span = slice(source * q_columns, (source + 1) * q_columns)
            query = turned[:, :q_columns]
            query_ref[:, span] = query
            sums = sums + jnp.sum(query * wq_ref[:, span].astype(F32), axis=1, keepdims=True)
            keys.append(turned[:, q_columns : q_columns + kv_columns])
            values.append(turned[:, q_columns + kv_columns :])
        span = slice(2 * pair * kv_columns, 2 * (pair + 1) * kv_columns)
        for parts, ref, weight in ((keys, key_ref, wk_ref), (values, value_ref, wv_ref)):
            both = jnp.concatenate(parts, axis=1)
            ref[:, span] = both
            sums = sums + jnp.sum(both * weight[:, span].astype(F32), axis=1, keepdims=True)
    for i in range(16):
        half = i % 2 * SLICE
        output_ref[half : half + SLICE, i // 2 * rows : (i // 2 + 1) * rows] = pieces_ref[
            i, base + PIECE :
        ].astype(F32)
    spare = pieces_ref[:, base : base + PIECE].astype(F32)
    spare = jnp.concatenate([spare[i, :SPARE] for i in range(16)], axis=0)
    one_ref[...] = jnp.broadcast_to(sums, (rows, 128)).T[:1] / gain_ref[...].astype(F32)
    two_ref[...] = spare[experts : experts + 1]
    gains_ref[...] = spare[experts + 1 : experts + 3]
    router_ref[...] = spare[:experts]


def final_grads(pieces, wq, wk, wv, gain, experts):
    rows = pieces.shape[2]
    return kernel_call(
        functools.partial(final_kernel, experts=experts),
        "final_grads",
        0.2,
        [pieces, wq, wk, wv, gain],
        [
            (wq.shape, F32),
            (wk.shape, F32),
            (wv.shape, F32),
            ((rows, 8 * rows), F32),
            ((1, rows), F32),
            ((1, rows), F32),
            ((2, rows), F32),
            ((experts, rows), F32),
        ],
        held=(1, 2, 3, 4),
    )


def send(values, axis, flip):
    count = lax.axis_size(axis)
    return lax.ppermute(values, axis, [(i, i ^ flip) for i in range(count)])


def along_z(values):
    if not isinstance(values, (list, tuple)):
        values = [values] * 3
    return [send(value, "fsdp", 2 * (i + 1)) for i, value in enumerate(values)]


def gather_fsdp(block, name):
    came = along_z(block)
    return came, send(row([block, *came], name), "fsdp", 1)


def exchange(rows):
    return lax.all_to_all(rows, "expert", 0, 0, tiled=True)


def shards(
    tokens,
    lengths,
    routes,
    first_gain,
    query_weight,
    key_weight,
    value_weight,
    output_weight,
    query_gain,
    key_gain,
    second_gain,
    router_weight,
    gate_weight,
    up_weight,
    down_weight,
    cotangent,
):
    own = tokens[0]
    upstream = cotangent[0]
    rows, width = own.shape
    fsdp = lax.axis_size("fsdp")
    owners = lax.axis_size("expert")
    me = lax.axis_index("fsdp").astype(jnp.int32).reshape(1)
    owner = lax.axis_index("expert").astype(jnp.int32).reshape(1)
    experts = router_weight.shape[1]
    capacity = 3 * rows * routes.shape[2] // (2 * experts)
    kv_columns = key_weight.shape[1] // fsdp
    q_columns = query_weight.shape[1] // fsdp
    columns = q_columns + 2 * kv_columns
    q_heads = q_columns // HEAD

    packed, x_sends, dressed, mask = pack_weights(
        me,
        own,
        query_weight,
        key_weight,
        value_weight,
        router_weight.T,
        first_gain[None],
        second_gain[None],
        query_gain[None],
        key_gain[None],
        routes[0].T,
        upstream,
    )
    x_came = along_z(x_sends)
    x_other = send(relay(own, packed, x_came), "fsdp", 1)
    deal, turn = slot_tables(mask, capacity)
    c_all = lax.all_gather(dressed, "expert", axis=0)
    wo_came = along_z(output_weight)

    ends = jnp.cumsum(lengths[0])
    place = jnp.arange(rows * fsdp, dtype=jnp.int32)
    start = jnp.max(jnp.where(ends[:, None] <= place[None, :], ends[:, None], 0), axis=0)
    position = (place - start).astype(F32)
    frequency = ROPE_BASE ** (-jnp.arange(HEAD // 2, dtype=F32) * 2.0 / HEAD)
    angles = frequency[:, None] * position[None, :]
    cosine, sine = jnp.cos(angles), jnp.sin(angles)
    start = start[None, :].astype(jnp.int32)

    h1, pre, keep, give, inverse, gains, heads, turned, mixed = attention_forward(
        me, own, packed, x_came, x_other, cosine, sine, start, experts, q_heads, after=(deal,)
    )
    other = send(give, "fsdp", 1)
    mixed_sends, wo_stack = merge(keep, other, output_weight, wo_came)
    mixed_came = along_z(mixed_sends)
    wo_other = send(wo_stack, "fsdp", 1)
    middle, probs, hidden, sent = middle_layer(
        own, keep, other, mixed_came, output_weight, wo_came, wo_other, gains, deal, experts, owners
    )
    h_rows = exchange(sent)
    rows_c, row_mask, back = deal_rows(owner, c_all, down_weight, experts, capacity)
    rows_back, gate_low, up_low, active, weighted, share = expert_layer(
        owner, h_rows, gains, row_mask, back, gate_weight, up_weight, experts
    )
    came_back = exchange(rows_back)
    grads, tick = expert_weights(h_rows, rows_c, gate_low, up_low, weighted)
    grads = lax.psum(grads, "fsdp")
    gate_sum, up_sum, down_sum = widen(grads)
    sent, tick = expert_outputs(active, share, down_weight, owners, after=(tick,))

    middle_grad, middle_low, extra = router_backward(
        came_back, turn, middle, probs, mask, gains, upstream, hidden, experts, after=(tick,)
    )
    da_came, da_other = gather_fsdp(middle_low, "row_middle")
    out_rows = exchange(sent)
    layer_out, _ = layer_output(out_rows, turn, middle)
    first, dh_keep, dh_give = attention_backward(
        me,
        middle_low,
        da_came,
        da_other,
        heads,
        output_weight,
        cosine,
        sine,
        start,
        h1,
        pre,
        mixed,
        inverse,
        turned,
        extra,
        experts,
        q_heads,
    )
    dh_total, *dh_sends = pair_sum(dh_keep, send(dh_give, "fsdp", 1))
    dh_came = along_z(dh_sends)
    tokens_grad = input_grad(dh_total, dh_came, own, gains, middle_grad, experts)
    first = passed(first, after=(out_rows, grads))
    parted, rest = shares_sum(exchange(first), after=(tokens_grad,))
    parted = lax.all_to_all(parted, "fsdp", 0, 0, tiled=True)
    pieces = exchange(whole_pieces(parted, rest, after=(layer_out,)))
    query_sum, key_sum, value_sum, output_sum, one_sum, two_sum, gain_sums, router_sum = final_grads(
        pieces, query_weight, key_weight, value_weight, first_gain[None], experts
    )
    step = HEAD // fsdp
    return (
        layer_out[None],
        tokens_grad[None],
        one_sum[0],
        query_sum,
        key_sum,
        value_sum,
        output_sum,
        gain_sums[0, :step],
        gain_sums[1, :step],
        two_sum[0],
        router_sum.T,
        gate_sum,
        up_sum,
        down_sum,
    )


def solution(mesh):
    whole = P("expert", "fsdp", None)
    rows = P("fsdp", None)
    vector = P("fsdp")
    owned = P("expert", None, None)
    return jax.shard_map(
        shards,
        mesh=mesh,
        in_specs=(
            whole,
            P("expert", None),
            whole,
            vector,
            rows,
            rows,
            rows,
            rows,
            vector,
            vector,
            vector,
            rows,
            owned,
            owned,
            owned,
            whole,
        ),
        out_specs=(
            whole,
            whole,
            vector,
            rows,
            rows,
            rows,
            rows,
            vector,
            vector,
            vector,
            rows,
            owned,
            owned,
            owned,
        ),
        check_vma=False,
    )
```

```python
import functools

import jax
import jax.numpy as jnp
from jax import lax
from jax.experimental import pallas as pl
from jax.experimental.pallas import tpu as pltpu
from jax.sharding import PartitionSpec as P

EPSILON = 1e-06
ROPE_BASE = 10000.0
HEAD = 64
TILE = 256
F32 = jnp.float32
BF16 = jnp.bfloat16
VMEM = pl.BlockSpec(memory_space=pltpu.VMEM)
SMEM = pl.BlockSpec(memory_space=pltpu.SMEM)
ANY = pl.BlockSpec(memory_space=pl.ANY)
HBM = pl.BlockSpec(memory_space=pltpu.HBM)


def dot(left, right, dims=((1,), (0,))):
    return lax.dot_general(left, right, (dims, ((), ())), preferred_element_type=F32)


def shape(extent, dtype):
    return jax.ShapeDtypeStruct(extent, dtype)


def kernel_call(
    body, name, micros, operands, results, smem=0, hbm=(), out_hbm=(), after=(), scratch=(), held=(), late=(), stored=(), mib=63
):
    held = tuple(held) + tuple(late)
    n, a, r, s = len(operands), len(after), len(results), len(scratch)
    specs = [SMEM if i < smem else HBM if i in held or i in hbm else VMEM for i in range(n)]
    out_specs = [HBM if i in stored or i in out_hbm else VMEM for i in range(r)]
    staged = [pltpu.VMEM(operands[i].shape, operands[i].dtype) for i in held]
    staged += [pltpu.VMEM(*results[i]) for i in stored]
    sems = [pltpu.SemaphoreType.DMA((max(len(held), 1),)), pltpu.SemaphoreType.DMA((max(len(stored), 1),))]

    def wrapped(*refs):
        ins, outs = list(refs[:n]), list(refs[n + a : n + a + r])
        own = refs[n + a + r : n + a + r + s]
        stages, (load_sem, store_sem) = refs[n + a + r + s : -2], refs[-2:]
        loads, stores, begun = {}, {}, []
        for k, i in enumerate(held):
            loads[i] = pltpu.make_async_copy(ins[i], stages[k], load_sem.at[k])
            loads[i].start()
            ins[i] = stages[k]
        for k, i in enumerate(stored):
            stores[i] = pltpu.make_async_copy(stages[len(held) + k], outs[i], store_sem.at[k])
            outs[i] = stages[len(held) + k]
        for i in held:
            if i not in late:
                loads[i].wait()

        def store(*which):
            for i in which:
                stores[i].start()
                begun.append(i)

        extra = {}
        if late:
            extra["wait"] = lambda i: loads[i].wait()
        if stored:
            extra["store"] = store
        body(*ins, *outs, *own, **extra)
        store(*[i for i in stored if i not in begun])
        for i in stored:
            stores[i].wait()

    return pl.pallas_call(
        wrapped,
        out_shape=[shape(*result) for result in results],
        in_specs=specs + [ANY] * a,
        out_specs=out_specs,
        scratch_shapes=list(scratch) + staged + sems,
        compiler_params=pltpu.CompilerParams(vmem_limit_bytes=mib * 1024 * 1024),
        cost_estimate=pl.CostEstimate(flops=0, bytes_accessed=int(micros * 3.6e6), transcendentals=0),
        name=name,
    )(*operands, *after)


def move_call(moves, name, micros, operands, results, after=(), mib=10):
    def body(*refs):
        for source, target in moves(*refs):
            target[...] = source[...]

    return kernel_call(body, name, micros, operands, results, after=after, mib=mib)


def lane_blocks(value):
    return jnp.concatenate([value[:, i : i + 128] for i in range(0, value.shape[1], 128)], axis=0)


def joined_lanes(value, count):
    rows = value.shape[0] // count
    return jnp.concatenate([value[i * rows : (i + 1) * rows] for i in range(count)], axis=1)


def softmax_rows(logits):
    powers = jnp.exp(logits - jnp.max(logits, axis=0, keepdims=True))
    return powers / jnp.sum(powers, axis=0, keepdims=True)


def head_forward(pre, gain, cosine, sine):
    scale = lax.rsqrt(jnp.mean(pre * pre, axis=0, keepdims=True) + EPSILON)
    normed = pre * scale
    scaled = normed * gain
    a, b = scaled[: HEAD // 2], scaled[HEAD // 2 :]
    turned = jnp.concatenate([a * cosine - b * sine, b * cosine + a * sine], axis=0)
    return turned, normed, scale


def head_backward(grad, normed, scale, gain, cosine, sine):
    a, b = grad[: HEAD // 2], grad[HEAD // 2 :]
    unturned = jnp.concatenate([a * cosine + b * sine, b * cosine - a * sine], axis=0)
    gain_grad = jnp.sum(unturned * normed, axis=1, keepdims=True)
    inner = unturned * gain
    pre_grad = scale * (inner - normed * jnp.mean(inner * normed, axis=0, keepdims=True))
    return pre_grad, gain_grad


def slots_kernel(mask_ref, deal_ref, turn_ref, whole_ref, *, capacity, store):
    experts, rows = mask_ref.shape
    mask = mask_ref[...]
    ranks = dot(mask.astype(BF16), earlier(rows))
    slot = lax.broadcasted_iota(jnp.int32, (capacity, rows), 0).astype(F32) + 1.0
    for expert in range(experts):
        one = slice(expert, expert + 1)
        whole_ref[expert * capacity : (expert + 1) * capacity] = jnp.where(
            (ranks[one] == slot) & (mask[one] > 0.5), 1.0, 0.0
        )
    deal_ref[...] = whole_ref[...].astype(BF16)
    store(0)
    for part in range(0, experts * capacity, 128):
        turn_ref[:, part : part + 128] = whole_ref[part : part + 128].T.astype(BF16)


def slot_tables(mask, capacity):
    experts, rows = mask.shape
    slots = experts * capacity
    return kernel_call(
        functools.partial(slots_kernel, capacity=capacity),
        "slot_tables",
        2.0,
        [mask],
        [((slots, rows), BF16), ((rows, slots), BF16)],
        scratch=[pltpu.VMEM((slots, rows), F32)],
        stored=(0, 1),
    )


def earlier(rows):
    return (
        lax.broadcasted_iota(jnp.int32, (rows, rows), 0)
        <= lax.broadcasted_iota(jnp.int32, (rows, rows), 1)
    ).astype(BF16)


def pack_kernel(
    me_ref, x_ref, wq_ref, wk_ref, wv_ref, router_ref, one_ref, two_ref, qg_ref, kg_ref, routes_ref, c_ref, *outs, wait, store
):
    own_ref, sends, dressed_ref, mask_ref, other_ref, parts_ref = outs[0], outs[1:4], *outs[4:]
    experts, rows = router_ref.shape
    wide = wq_ref.shape[1] // 8
    narrow = wk_ref.shape[1] // 8
    count = qg_ref.shape[1]
    heads = jnp.concatenate([qg_ref[...], kg_ref[...]], axis=0).astype(F32)
    heads = jnp.concatenate([heads, jnp.zeros((2, 128 - count), F32)], axis=1)
    heads = jnp.concatenate([heads, jnp.zeros((126, 128), F32)], axis=0).T[:count]
    small = jnp.concatenate(
        [
            router_ref[...].astype(F32),
            one_ref[...].astype(F32),
            two_ref[...].astype(F32),
            jnp.zeros((6, 128), F32),
            heads,
        ],
        axis=0,
    ).astype(BF16)
    for part in range(8):
        parts_ref[part, :wide] = wq_ref[:, part * wide : (part + 1) * wide].astype(F32).T.astype(BF16)
        parts_ref[part, wide + 2 * narrow :] = small
    for pair in range(4):
        span = slice(pair * 128, (pair + 1) * 128)
        for ref, place in ((wk_ref, wide), (wv_ref, wide + narrow)):
            turned = ref[:, span].astype(F32).T.astype(BF16)
            parts_ref[2 * pair, place : place + narrow] = turned[:narrow]
            parts_ref[2 * pair + 1, place : place + narrow] = turned[narrow:]
    me = me_ref[0]
    tall = parts_ref.shape[1]
    blocks = lane_blocks(x_ref[...])
    base = blocks.shape[0]
    own_ref[...] = parts_ref[me]
    other_ref[...] = parts_ref[me ^ 1]
    for flip in range(1, 4):
        sends[flip - 1][:base] = blocks
        sends[flip - 1][base : base + tall] = parts_ref[me ^ (2 * flip)]
        sends[flip - 1][base + tall :] = parts_ref[me ^ (2 * flip + 1)]
    store(1, 2, 3, 6, 0)
    wait(10)
    wait(11)
    width = c_ref.shape[1]
    subs = lax.broadcasted_iota(jnp.int32, (128, rows), 0)
    routed = jnp.zeros((128, rows), F32)
    for route in range(routes_ref.shape[0]):
        routed = routed + jnp.where(routes_ref[route : route + 1] == subs, 1.0, 0.0)
    dressed_ref[:, :width] = c_ref[...]
    dressed_ref[:, width:] = routed.T.astype(BF16)
    mask_ref[...] = routed[:experts]


def pack_weights(me, x, wq, wk, wv, router, one, two, qg, kg, routes, c):
    experts = router.shape[0]
    tall = (wq.shape[1] + wk.shape[1] + wv.shape[1]) // 8 + experts + 16
    rows, width = x.shape
    base = rows * 8
    own, first, second, third, dressed, mask, other = kernel_call(
        pack_kernel,
        "pack_weights",
        2.5,
        [me, x, wq, wk, wv, router, one, two, qg, kg, routes, c],
        [((tall, 128), BF16)]
        + [((base + 2 * tall, 128), BF16)] * 3
        + [((rows, width + 128), BF16), ((experts, rows), F32), ((tall, 128), BF16)],
        smem=1,
        scratch=[pltpu.VMEM((8, tall, 128), BF16)],
        held=range(1, 10),
        late=(10, 11),
        stored=(0, 1, 2, 3, 4, 5, 6),
    )
    return (own, other), [first, second, third], dressed, mask


def relay(came, base, after):
    tall = (came[0].shape[0] - base) // 2

    def moves(*refs):
        pairs = []
        for flip, ref in enumerate(refs[:3]):
            pairs.append((ref.at[:base], refs[3].at[flip, :base]))
            pairs.append((ref.at[base + tall :], refs[3].at[flip, base:]))
        return pairs

    return move_call(moves, "relay", 1.5, came, [((3, base + tall, 128), BF16)], after)[0]


def forward_kernel(me_ref, x_ref, own_ref, *refs, experts, q_heads, store):
    came, other_x, other_w, other_ref = refs[:3], refs[3], refs[4], refs[5]
    cos_ref, sin_ref, start_ref = refs[6:9]
    h1_ref, pre_ref, keep_ref, give_ref, inverse_ref, gains_ref, heads_ref, turned_ref, out_ref = refs[-9:]
    rows, width = x_ref.shape
    q_columns = q_heads * HEAD
    columns = q_columns + 2 * HEAD
    total = rows * 8
    tall = own_ref.shape[0]
    base = 8 * rows
    me = me_ref[0]
    for slot in range(8):
        flip = slot // 2
        if slot % 2:
            piece = other_ref[flip - 1, base:] if flip else other_w[...]
        elif flip:
            piece = came[flip - 1][base : base + tall]
        else:
            piece = own_ref[...]
        span = pl.ds(pl.multiple_of((me ^ slot) * rows, rows), rows)
        turned_ref[:, span] = piece[:columns]
        small = piece[columns:].astype(F32)
        gains_ref[:, span] = small[: experts + 8]
        heads_ref[pl.ds(pl.multiple_of((me ^ slot) * 8, 8), 8)] = small[experts + 8 :]
    gain_one = gains_ref[experts : experts + 1]
    for slot in range(8):
        flip = slot // 2
        if slot % 2:
            x = joined_lanes(other_ref[flip - 1, :base], 8) if flip else other_x[...]
        elif flip:
            x = joined_lanes(came[flip - 1][:base], 8)
        else:
            x = x_ref[...]
        x = x.astype(F32)
        scale = lax.rsqrt(jnp.mean(x * x, axis=1, keepdims=True) + EPSILON)
        h1_ref[slot] = (x * scale * gain_one).astype(BF16)
    store(0, 6, 7)
    for slot in range(8):
        block = dot(turned_ref[...], h1_ref[slot], ((1,), (1,)))
        place = pl.multiple_of((me ^ slot) * rows, rows)
        pre_ref[:, pl.ds(place, rows)] = block
    store(1)
    cosine, sine = cos_ref[...], sin_ref[...]
    gain_query, gain_key = heads_ref[:, :1], heads_ref[:, 1:2]
    key = head_forward(pre_ref[q_columns : q_columns + HEAD], gain_key, cosine, sine)[0]
    key = key.T.astype(BF16)
    value = pre_ref[q_columns + HEAD :].astype(BF16)
    inverse_ref[...] = jnp.zeros(inverse_ref.shape, F32)
    for head in range(q_heads):
        query = head_forward(pre_ref[head * HEAD : (head + 1) * HEAD], gain_query, cosine, sine)[0]
        query = query.astype(BF16) * jnp.array(HEAD ** (-0.5), BF16)
        for tile in range(total // TILE):
            low, high = tile * TILE, (tile + 1) * TILE
            scores = dot(key[:high], query[:, low:high])
            u = lax.broadcasted_iota(jnp.int32, (high, TILE), 0)
            t = lax.broadcasted_iota(jnp.int32, (high, TILE), 1) + low
            allowed = (u >= start_ref[:, low:high]) & (u <= t)
            powers = jnp.where(allowed, jnp.exp(scores), 0.0)
            inverse = 1.0 / jnp.sum(powers, axis=0, keepdims=True)
            probs = (powers * inverse).astype(BF16)
            mixed = dot(value[:, :high], probs).astype(BF16)
            inverse_ref[head : head + 1, low:high] = inverse
            for part in range(TILE // rows):
                out_ref[low // rows + part, head * HEAD : (head + 1) * HEAD] = mixed[
                    :, part * rows : (part + 1) * rows
                ]
    for slot in range(8):
        (give_ref if slot % 2 else keep_ref)[slot // 2] = out_ref[me ^ slot]


def attention_forward(me, x, own, came, other, cosine, sine, start, experts, q_heads, after=()):
    rows, width = x.shape
    total = 8 * rows
    columns = (q_heads + 2) * HEAD
    q_columns = q_heads * HEAD
    return kernel_call(
        functools.partial(forward_kernel, experts=experts, q_heads=q_heads),
        "attention_forward",
        7.0,
        [me, x, own, *came, *other, cosine, sine, start],
        [
            ((8, rows, width), BF16),
            ((columns, total), F32),
            ((4, q_columns, rows), BF16),
            ((4, q_columns, rows), BF16),
            ((8, total), F32),
            ((experts + 8, width), F32),
            ((HEAD, 128), F32),
            ((columns, width), BF16),
            ((8, q_columns, rows), BF16),
        ],
        smem=1,
        after=after,
        held=(1,),
        stored=(0, 1, 4, 6, 7, 8),
    )


def merge(keep, came, wo, wo_came):
    def moves(keep_ref, came_ref, *refs):
        weights, outs, stacked = refs[:4], refs[4:7], refs[7]
        pairs = [(weight, stacked.at[i]) for i, weight in enumerate(weights)]
        for flip in range(1, 4):
            pairs.append((keep_ref.at[flip], outs[flip - 1].at[0]))
            pairs.append((came_ref.at[flip], outs[flip - 1].at[1]))
        return pairs

    extent = ((2,) + keep.shape[1:], BF16)
    results = [extent] * 3 + [((4,) + wo.shape, BF16)]
    *sends, stacked = move_call(moves, "merge", 1.0, [keep, came, wo, *wo_came], results)
    return sends, stacked


def middle_kernel(x_ref, keep_ref, other_ref, *refs, experts, wait, store):
    came, wo_ref, wo_came, wo_other_ref, gains_ref, deal_ref = refs[:3], refs[3], refs[4:7], refs[7], refs[8], refs[9]
    middle_ref, probs_ref, hidden_ref, sent_ref, mixed_ref, whole_ref, out_ref, out_sem = refs[10:]
    rows, width = x_ref.shape
    for slot in range(8):
        flip, core = slot // 2, slot % 2
        if flip:
            piece = came[flip - 1][core]
        else:
            piece = (other_ref if core else keep_ref)[0]
        span = slice(slot * 128, (slot + 1) * 128)
        mixed_ref[:, span] = piece.astype(F32).T.astype(BF16)
    for i in (6, 7, 8, 9, 10):
        wait(i)
    for slot in range(8):
        flip = slot // 2
        span = slice(slot * 128, (slot + 1) * 128)
        if slot % 2:
            whole_ref[span] = wo_other_ref[flip]
        else:
            whole_ref[span] = (wo_came[flip - 1] if flip else wo_ref)[...]
    wait(0)
    middle = x_ref[...].astype(F32) + dot(mixed_ref[...], whole_ref[...])
    middle_ref[...] = middle
    scale = lax.rsqrt(jnp.mean(middle * middle, axis=1, keepdims=True) + EPSILON)
    hidden = (middle * scale * gains_ref[experts + 1 : experts + 2]).astype(BF16)
    hidden_ref[...] = hidden
    probs_ref[...] = softmax_rows(dot(gains_ref[:experts].astype(BF16), hidden, ((1,), (1,))))
    store(0, 2)
    owners, per_owner, capacity, _ = sent_ref.shape
    group = owners // 4
    size = group * per_owner * capacity
    copies = []
    wait(12)
    for part in range(4):
        taken = dot(deal_ref[part * size : (part + 1) * size], hidden).astype(BF16)
        blocks = slice(group * part, group * (part + 1))
        out_ref[blocks] = taken.reshape(group, per_owner, capacity, width)
        copies.append(pltpu.make_async_copy(out_ref.at[blocks], sent_ref.at[blocks], out_sem.at[part]))
        copies[-1].start()
    for copy in copies:
        copy.wait()


def middle_layer(x, keep, other, came, wo, wo_came, wo_other, gains, deal, experts, owners):
    rows, width = x.shape
    per_owner = experts // owners
    capacity = deal.shape[0] // experts
    sent = ((owners, per_owner, capacity, width), BF16)
    return kernel_call(
        functools.partial(middle_kernel, experts=experts),
        "middle_layer",
        3.0,
        [x, keep, other, *came, wo, *wo_came, wo_other, gains, deal],
        [((rows, width), F32), ((experts, rows), F32), ((rows, width), BF16), sent],
        out_hbm=(3,),
        scratch=[
            pltpu.VMEM((rows, width), BF16),
            pltpu.VMEM((width, width), BF16),
            pltpu.VMEM(*sent),
            pltpu.SemaphoreType.DMA((4,)),
        ],
        late=(6, 7, 8, 9, 10, 0, 12),
        stored=(0, 2),
    )


def row(pieces, name):
    def moves(*refs):
        return [(ref, refs[-1].at[i]) for i, ref in enumerate(refs[:-1])]

    return move_call(moves, name, 1.0, pieces, [((len(pieces),) + pieces[0].shape, BF16)])[0]


def backward_kernel(me_ref, own_da_ref, *refs, experts, q_heads, wait):
    came, other_ref = refs[:3], refs[3]
    heads_ref, wo_ref, cos_ref, sin_ref, start_ref = refs[4:9]
    h1_ref, pre_ref, mixed_ref, inverse_ref, turned_ref, extra_ref = refs[9:15]
    first_ref, keep_ref, send_ref = refs[-10:-7]
    da_ref, mixed_grad_ref, dkey_ref, dvalue_ref, low_ref, out_slots_ref, grad_ref = refs[-7:]
    rows, width = own_da_ref.shape
    q_columns = q_heads * HEAD
    columns = q_columns + 2 * HEAD
    total = rows * 8
    me = me_ref[0]
    for slot in range(8):
        flip, core = slot // 2, slot % 2
        if core:
            piece = other_ref[flip]
        else:
            piece = (came[flip - 1] if flip else own_da_ref)[...]
        span = slice(slot * rows, (slot + 1) * rows)
        da_ref[span] = piece
        place = pl.multiple_of((me ^ slot) * rows, rows)
        mixed_grad_ref[:, pl.ds(place, rows)] = dot(wo_ref[...], piece, ((1,), (1,))).astype(BF16)
    wait(13)
    for slot in range(8):
        out_slots_ref[:, slot * rows : (slot + 1) * rows] = mixed_ref[me ^ slot]
    wo_grad = dot(out_slots_ref[...], da_ref[...]).astype(BF16)
    wo_grad = lane_blocks(wo_grad)
    wait(12)
    wait(14)
    gain_query, gain_key = heads_ref[:, :1], heads_ref[:, 1:2]
    cosine, sine = cos_ref[...], sin_ref[...]
    key_turned, key_normed, key_scale = head_forward(
        pre_ref[q_columns : q_columns + HEAD], gain_key, cosine, sine
    )
    key_low = key_turned.astype(BF16)
    key = key_turned.T.astype(BF16)
    value = pre_ref[q_columns + HEAD :].T.astype(BF16)
    dkey_ref[...] = jnp.zeros(dkey_ref.shape, F32)
    dvalue_ref[...] = jnp.zeros(dvalue_ref.shape, F32)
    gain_query_grad = jnp.zeros((HEAD, 1), F32)
    pieces = []
    for head in range(q_heads):
        span = slice(head * HEAD, (head + 1) * HEAD)
        turned, normed, scale = head_forward(pre_ref[span], gain_query, cosine, sine)
        query = turned.astype(BF16) * jnp.array(HEAD ** (-0.5), BF16)
        grads = []
        for tile in range(total // TILE):
            low, high = tile * TILE, (tile + 1) * TILE
            part = query[:, low:high]
            mixed_grad = mixed_grad_ref[span, low:high]
            scores = dot(key[:high], part)
            u = lax.broadcasted_iota(jnp.int32, (high, TILE), 0)
            t = lax.broadcasted_iota(jnp.int32, (high, TILE), 1) + low
            allowed = (u >= start_ref[:, low:high]) & (u <= t)
            probs = jnp.where(allowed, jnp.exp(scores) * inverse_ref[head : head + 1, low:high], 0.0)
            attend = dot(value[:high], mixed_grad)
            delta = jnp.sum(probs * attend, axis=0, keepdims=True)
            score_low = (probs * (attend - delta)).astype(BF16)
            grads.append(dot(key_low[:, :high], score_low))
            dkey_ref[:, :high] += dot(part, score_low, ((1,), (1,)))
            dvalue_ref[:, :high] += dot(mixed_grad, probs.astype(BF16), ((1,), (1,)))
        query_grad = jnp.concatenate(grads, axis=1) * HEAD ** (-0.5)
        pre_grad, gain_grad = head_backward(query_grad, normed, scale, gain_query, cosine, sine)
        gain_query_grad += gain_grad
        pieces.append(pre_grad)
    pre_grad, gain_key_grad = head_backward(
        dkey_ref[...], key_normed, key_scale, gain_key, cosine, sine
    )
    pieces += [pre_grad, dvalue_ref[...]]
    pre_grad = jnp.concatenate(pieces, axis=0)
    low_ref[...] = pre_grad.astype(BF16)
    slots_grad = []
    for slot in range(8):
        place = pl.multiple_of((me ^ slot) * rows, rows)
        slots_grad.append(low_ref[:, pl.ds(place, rows)])
    slots_grad = jnp.concatenate(slots_grad, axis=1)
    wait(11)
    wait(15)
    grad_ref[:columns] = dot(slots_grad, h1_ref[...].reshape(total, width))
    extra = extra_ref[...]
    lane = lax.broadcasted_iota(jnp.int32, (HEAD, 128), 1)
    gains = jnp.where(lane == 0, gain_query_grad, jnp.where(lane == 1, gain_key_grad, 0.0))
    gains = gains.T[:2]
    step = HEAD // 8
    grad_ref[columns:] = jnp.zeros((64, width), F32)
    grad_ref[columns : columns + experts + 1] = extra[: experts + 1]
    for part in range(8):
        grad_ref[columns + experts + 1 : columns + experts + 3, part * rows : part * rows + step] = gains[
            :, part * step : (part + 1) * step
        ]
    for piece in range(16):
        spare = []
        place = columns + piece * SPARE
        for part in range(8):
            span = slice(part * rows, (part + 1) * rows)
            block = grad_ref[piece * PIECE : (piece + 1) * PIECE, span]
            first_ref[piece, part * PIECE : (part + 1) * PIECE] = block.astype(BF16)
            spare.append(grad_ref[place : place + SPARE, span])
        spare.append(jnp.zeros((2 * PIECE - 8 * SPARE, 128), F32))
        first_ref[piece, 8 * PIECE : 10 * PIECE] = jnp.concatenate(spare, axis=0).astype(BF16)
        first_ref[piece, 10 * PIECE :] = wo_grad[piece * SLICE : (piece + 1) * SLICE]
    turned = turned_ref[...]
    for slot in range(8):
        low_rows_slot = slots_grad[:, slot * rows : (slot + 1) * rows].astype(F32).T.astype(BF16)
        part = dot(low_rows_slot, turned)
        if slot % 2:
            send_ref[slot // 2] = part.astype(BF16)
        else:
            keep_ref[slot // 2] = part


def attention_backward(
    me, da, came, other, heads, wo, cosine, sine, start, h1, pre, mixed, inverse, turned, extra, experts, q_heads, after=()
):
    rows, width = da.shape
    total = 8 * rows
    columns = pre.shape[0]
    q_columns = q_heads * HEAD
    return kernel_call(
        functools.partial(backward_kernel, experts=experts, q_heads=q_heads),
        "attention_backward",
        12,
        [me, da, *came, other, heads, wo, cosine, sine, start, h1, pre, mixed, inverse, turned, extra],
        [
            ((16, 10 * PIECE + SLICE, 128), BF16),
            ((4, rows, width), F32),
            ((4, rows, width), BF16),
        ],
        smem=1,
        after=after,
        held=(6, 7),
        late=(11, 12, 13, 14, 15),
        scratch=[
            pltpu.VMEM((total, width), BF16),
            pltpu.VMEM((q_columns, total), BF16),
            pltpu.VMEM((HEAD, total), F32),
            pltpu.VMEM((HEAD, total), F32),
            pltpu.VMEM((columns, total), BF16),
            pltpu.VMEM((q_columns, total), BF16),
            pltpu.VMEM((columns + 64, width), F32),
        ],
    )


def deal_kernel(owner_ref, c_ref, down_ref, rows_c, mask_ref, back_ref, c_scratch, sems, *, experts, capacity, wait, store):
    owner = owner_ref[0]
    per_owner, hidden, width = down_ref.shape
    rows = c_ref.shape[1]
    loads = [pltpu.make_async_copy(c_ref.at[i], c_scratch.at[i], sems.at[i]) for i in range(16)]
    for load in loads:
        load.start()
    lanes = lax.broadcasted_iota(jnp.int32, (experts, 128), 1)
    subs = lax.broadcasted_iota(jnp.int32, (experts, 128), 0)
    eye = (lanes == subs).astype(BF16)
    before = earlier(rows)
    mine_of = lax.broadcasted_iota(jnp.int32, (experts, rows), 0) - owner * per_owner
    slot = lax.broadcasted_iota(jnp.int32, (capacity, rows), 0).astype(F32) + 1.0
    for block in range(16):
        loads[block].wait()
        c = c_scratch[block]
        mask = dot(eye, c[:, width:], ((1,), (1,)))
        ranks = dot(mask.astype(BF16), before)
        deals = []
        for k in range(per_owner):
            mine = mine_of == k
            hit = jnp.sum(jnp.where(mine, mask, 0.0), axis=0, keepdims=True)
            rank = jnp.sum(jnp.where(mine, ranks, 0.0), axis=0, keepdims=True)
            deals.append(jnp.where((rank == slot) & (hit > 0.5), 1.0, 0.0))
        taken = dot(jnp.concatenate(deals, axis=0).astype(BF16), c).astype(BF16)
        span = slice(block * capacity, (block + 1) * capacity)
        for k in range(per_owner):
            spot = slice(k * capacity, (k + 1) * capacity)
            rows_c[k, span] = taken[spot, :width]
            mask_ref[k, span] = taken[spot, width:]
    store(0, 1)
    wait(2)
    for k in range(per_owner):
        for tile in range(16 * capacity // TILE):
            span = slice(tile * TILE, (tile + 1) * TILE)
            back_ref[k, span] = dot(rows_c[k, span], down_ref[k], ((1,), (1,)))


def deal_rows(owner, c, down, experts, capacity):
    per_owner, hidden, width = down.shape
    count = 16 * capacity
    return kernel_call(
        functools.partial(deal_kernel, experts=experts, capacity=capacity),
        "deal_rows",
        12.0,
        [owner, c, down],
        [
            ((per_owner, count, width), BF16),
            ((per_owner, count, 128), BF16),
            ((per_owner, count, hidden), F32),
        ],
        smem=1,
        hbm=(1,),
        scratch=[pltpu.VMEM(c.shape, BF16), pltpu.SemaphoreType.DMA((16,))],
        late=(2,),
        stored=(0, 1, 2),
    )


def expert_kernel(
    owner_ref,
    h_hbm,
    gains_ref,
    mask_ref,
    back_hbm,
    gate_hbm,
    up_hbm,
    rows_hbm,
    gate_out,
    up_out,
    active_out,
    weighted_out,
    share_ref,
    h_ref,
    back_in,
    gate_ref,
    up_ref,
    rows_back,
    load_sem,
    store_sem,
    *,
    experts,
    store,
):
    owners, per_owner, capacity, width = h_hbm.shape
    group = 8
    parts = owners // group
    size = group * capacity
    loads = {}
    for k in range(per_owner):
        for part in range(parts):
            blocks = slice(part * group, (part + 1) * group)
            spot = (k * parts + part) * 4
            loads[k, part] = [
                pltpu.make_async_copy(h_hbm.at[blocks, k], h_ref.at[blocks, k], load_sem.at[spot]),
                pltpu.make_async_copy(
                    back_hbm.at[k, part * size : (part + 1) * size],
                    back_in.at[k, part * size : (part + 1) * size],
                    load_sem.at[spot + 1],
                ),
            ]
            if part == 0:
                loads[k, part] += [
                    pltpu.make_async_copy(gate_hbm.at[k], gate_ref.at[k], load_sem.at[spot + 2]),
                    pltpu.make_async_copy(up_hbm.at[k], up_ref.at[k], load_sem.at[spot + 3]),
                ]
            for load in loads[k, part]:
                load.start()
    owner = owner_ref[0]
    router = jnp.concatenate([gains_ref[:experts], jnp.zeros((128 - experts, width), F32)], axis=0)
    router = router.astype(BF16)
    lane = lax.broadcasted_iota(jnp.int32, (size, 128), 1)
    copies = []
    for k in range(per_owner):
        place = owner * per_owner + k
        for part in range(parts):
            blocks = slice(part * group, (part + 1) * group)
            span = slice(part * size, (part + 1) * size)
            for load in loads[k, part]:
                load.wait()
            h = h_ref[blocks, k].reshape(size, width)
            gate = dot(h, gate_ref[k])
            up = dot(h, up_ref[k])
            logits = dot(h, router, ((1,), (1,)))
            chosen = mask_ref[k, span] > 0.5
            top = jnp.max(jnp.where(chosen, logits, -1e30), axis=1, keepdims=True)
            powers = jnp.where(chosen, jnp.exp(logits - top), 0.0)
            total = jnp.sum(powers, axis=1, keepdims=True)
            share = jnp.sum(jnp.where(lane == place, powers, 0.0), axis=1, keepdims=True)
            share = share / jnp.where(total > 0.0, total, 1.0)
            share_ref[k, span] = jnp.broadcast_to(share, (size, 128))
            back = back_in[k, span]
            sig = 1.0 / (1.0 + jnp.exp(-gate))
            silu = gate * sig
            active = silu * up
            active_low = active.astype(BF16)
            route_grad = jnp.sum(active_low.astype(F32) * back, axis=1, keepdims=True)
            grad = back * share
            gate_low = (grad * up * (sig + silu * (1.0 - sig))).astype(BF16)
            up_low = (grad * silu).astype(BF16)
            active_out[k, span] = active_low
            weighted_out[k, span] = (active * share).astype(BF16)
            gate_out[k, span] = gate_low
            up_out[k, span] = up_low
            rows = dot(gate_low, gate_ref[k], ((1,), (1,))) + dot(up_low, up_ref[k], ((1,), (1,)))
            high = route_grad.astype(BF16).astype(F32)
            spread_out = jnp.where(lane == place, high, 0.0)
            spread_out = jnp.where(lane == place + experts, route_grad - high, spread_out)
            whole = jnp.concatenate([rows.astype(BF16), spread_out.astype(BF16)], axis=1)
            rows_back[blocks, k] = whole.reshape(group, capacity, width + 128)
            copies.append(
                pltpu.make_async_copy(
                    rows_back.at[blocks, k], rows_hbm.at[blocks, k], store_sem.at[k * parts + part]
                )
            )
            copies[-1].start()
    store(1, 2, 3, 4, 5)
    for copy in copies:
        copy.wait()


def expert_layer(owner, h, gains, mask, back, gate, up, experts):
    per_owner, width, hidden = gate.shape
    owners, _, capacity, _ = h.shape
    count = owners * capacity
    narrow = ((per_owner, count, hidden), BF16)
    rows_back = ((owners, per_owner, capacity, width + 128), BF16)
    pieces = per_owner * (owners // 8)
    return kernel_call(
        functools.partial(expert_kernel, experts=experts),
        "expert_layer",
        14.0,
        [owner, h, gains, mask, back, gate, up],
        [rows_back] + [narrow] * 4 + [((per_owner, count, 128), F32)],
        smem=1,
        hbm=(1, 4, 5, 6),
        out_hbm=(0,),
        scratch=[pltpu.VMEM(value.shape, value.dtype) for value in (h, back, gate, up)]
        + [pltpu.VMEM(*rows_back), pltpu.SemaphoreType.DMA((4 * pieces,)), pltpu.SemaphoreType.DMA((pieces,))],
        stored=(1, 2, 3, 4, 5),
    )


def weights_kernel(
    h_hbm, rows_c, gate_low, up_low, weighted, out_hbm, tick_ref, h_ref, out_ref, load_sem, store_sem, *, wait
):
    tick_ref[...] = jnp.zeros(tick_ref.shape, F32)
    first = ((0,), (0,))
    owners, per_owner, capacity, width = h_hbm.shape
    hidden = gate_low.shape[2]
    half = width // 2
    loads = [
        pltpu.make_async_copy(h_hbm.at[:, k], h_ref.at[:, k], load_sem.at[k]) for k in range(per_owner)
    ]
    for load in loads:
        load.start()
    stores = []

    def keep(place):
        stores.append(pltpu.make_async_copy(out_ref.at[place], out_hbm.at[place], store_sem.at[place]))
        stores[-1].start()

    wait(2)
    for k in range(per_owner):
        loads[k].wait()
        rows_h = h_ref[:, k].reshape(owners * capacity, width)
        for place, low in ((k, gate_low), (per_owner + k, up_low)):
            if k == 0 and place:
                wait(3)
            total = dot(rows_h, low[k], first).astype(BF16)
            out_ref[place, :, :hidden] = total[:half]
            out_ref[place, :, hidden:] = total[half:]
            keep(place)
        if k == 0:
            wait(4)
            wait(1)
        place = 2 * per_owner + k
        out_ref[place] = dot(weighted[k], rows_c[k], first).astype(BF16)
        keep(place)
    for store in stores:
        store.wait()


def expert_weights(h, rows_c, gate_low, up_low, weighted):
    per_owner, count, width = rows_c.shape
    hidden = gate_low.shape[2]
    out = ((3 * per_owner, hidden, width), BF16)
    return kernel_call(
        weights_kernel,
        "expert_weights",
        0.1,
        [h, rows_c, gate_low, up_low, weighted],
        [out, ((8, 128), F32)],
        hbm=(0,),
        out_hbm=(0,),
        scratch=[
            pltpu.VMEM(h.shape, BF16),
            pltpu.VMEM(*out),
            pltpu.SemaphoreType.DMA((per_owner,)),
            pltpu.SemaphoreType.DMA((3 * per_owner,)),
        ],
        late=(2, 3, 4, 1),
    )


def widen_kernel(low_ref, gate_ref, up_ref, down_ref):
    step = pl.program_id(0)
    hidden = gate_ref.shape[2]
    value = low_ref[0].astype(F32)
    half = value.shape[0]
    for place, ref in ((0, gate_ref), (1, up_ref)):

        @pl.when(step // 2 == place)
        def _():
            ref[0, :half] = value[:, :hidden]
            ref[0, half:] = value[:, hidden:]

    @pl.when(step // 2 == 2)
    def _():
        down_ref[0] = value


def widen(low):
    count, hidden, width = low.shape
    per_owner = count // 3

    def spot(place):
        return lambda i: (jnp.clip(i - place * per_owner, 0, per_owner - 1), 0, 0)

    return pl.pallas_call(
        widen_kernel,
        grid=(count,),
        out_shape=[shape((per_owner, width, hidden), F32)] * 2 + [shape((per_owner, hidden, width), F32)],
        in_specs=[pl.BlockSpec((1, hidden, width), lambda i: (i, 0, 0))],
        out_specs=[
            pl.BlockSpec((1, width, hidden), spot(0)),
            pl.BlockSpec((1, width, hidden), spot(1)),
            pl.BlockSpec((1, hidden, width), spot(2)),
        ],
        compiler_params=pltpu.CompilerParams(vmem_limit_bytes=63 * 1024 * 1024),
        cost_estimate=pl.CostEstimate(flops=0, bytes_accessed=24_000_000, transcendentals=0),
        name="widen",
    )(low)


def outputs_kernel(active, share, down_ref, sent_ref, tick_ref, out_ref, out_sem, *, wait):
    tick_ref[...] = jnp.zeros(tick_ref.shape, F32)
    per_owner, count, hidden = active.shape
    owners, _, capacity, width = sent_ref.shape
    group = 8
    size = group * capacity
    copies = []
    for i in range(3):
        wait(i)
    for k in range(per_owner):
        for part in range(owners // group):
            span = slice(part * size, (part + 1) * size)
            blocks = slice(part * group, (part + 1) * group)
            produced = dot(active[k, span], down_ref[k]).astype(BF16).astype(F32)
            produced = (produced * share[k, span, :1]).astype(BF16)
            out_ref[blocks, k] = produced.reshape(group, capacity, width)
            copies.append(
                pltpu.make_async_copy(
                    out_ref.at[blocks, k], sent_ref.at[blocks, k], out_sem.at[k * (owners // group) + part]
                )
            )
            copies[-1].start()
    for copy in copies:
        copy.wait()


def expert_outputs(active, share, down, owners, after=()):
    per_owner, count, hidden = active.shape
    width = down.shape[2]
    sent = ((owners, per_owner, count // owners, width), BF16)
    return kernel_call(
        outputs_kernel,
        "expert_outputs",
        0.1,
        [active, share, down],
        [sent, ((8, 128), F32)],
        out_hbm=(0,),
        after=after,
        scratch=[pltpu.VMEM(*sent), pltpu.SemaphoreType.DMA((per_owner * (owners // 8),))],
        late=(0, 1, 2),
    )


def combined(rows_hbm, rows_ref, sems, turn_ref, ready):
    owners, per_owner, capacity, wide = rows_hbm.shape
    group = owners // 4
    size = group * per_owner * capacity
    loads = []
    for part in range(4):
        blocks = slice(part * group, (part + 1) * group)
        loads.append(pltpu.make_async_copy(rows_hbm.at[blocks], rows_ref.at[blocks], sems.at[part]))
        loads[-1].start()
    ready()
    total = None
    for part in range(4):
        loads[part].wait()
        rows = rows_ref[part * group : (part + 1) * group].reshape(size, wide)
        one = dot(turn_ref[:, part * size : (part + 1) * size], rows)
        total = one if total is None else total + one
    return total


def output_kernel(rows_hbm, turn_ref, middle_ref, out_ref, tick_ref, rows_ref, sems, *, wait, store):
    tick_ref[...] = jnp.zeros(tick_ref.shape, F32)
    total = combined(rows_hbm, rows_ref, sems, turn_ref, lambda: wait(1))
    wait(2)
    out_ref[...] = (middle_ref[...] + total).astype(BF16)


def layer_output(rows, turn, middle):
    return kernel_call(
        output_kernel,
        "layer_output",
        3,
        [rows, turn, middle],
        [(middle.shape, BF16), ((8, 128), F32)],
        hbm=(0,),
        scratch=[pltpu.VMEM(rows.shape, BF16), pltpu.SemaphoreType.DMA((4,))],
        late=(1, 2),
        stored=(0,),
    )


def router_kernel(
    rows_hbm,
    turn_ref,
    middle_ref,
    probs_ref,
    mask_ref,
    gains_ref,
    c_ref,
    hidden_ref,
    grad_ref,
    send_ref,
    extra_ref,
    rows_ref,
    sems,
    *,
    experts,
    wait,
    store,
):
    rows, width = middle_ref.shape
    returned = combined(rows_hbm, rows_ref, sems, turn_ref, lambda: wait(1))
    for i in (2, 4, 6, 7):
        wait(i)
    tail = returned[:, width:].T
    route_grad = tail[:experts] + tail[experts : 2 * experts]
    mask = mask_ref[...]
    probs = probs_ref[...]
    picked = probs * mask
    picked_sum = jnp.sum(picked, axis=0, keepdims=True)
    share = picked / picked_sum
    picked_grad = (route_grad - jnp.sum(route_grad * share, axis=0, keepdims=True)) / picked_sum
    prob_grad = mask * picked_grad
    logit_grad = probs * (prob_grad - jnp.sum(probs * prob_grad, axis=0, keepdims=True))
    extra_ref[:experts] = dot(logit_grad.astype(BF16), hidden_ref[...])
    logit_rows = jnp.concatenate([logit_grad, jnp.zeros((128 - experts, rows), F32)], axis=0).T
    router = gains_ref[:experts].astype(BF16)
    hidden_grad = returned[:, :width] + dot(logit_rows[:, :experts].astype(BF16), router)
    middle = middle_ref[...]
    scale = lax.rsqrt(jnp.mean(middle * middle, axis=1, keepdims=True) + EPSILON)
    normed = middle * scale
    extra_ref[experts : experts + 8] = jnp.broadcast_to(
        jnp.sum(hidden_grad * normed, axis=0, keepdims=True), (8, width)
    )
    inner = hidden_grad * gains_ref[experts + 1 : experts + 2]
    grad = c_ref[...].astype(F32) + scale * (
        inner - normed * jnp.mean(inner * normed, axis=1, keepdims=True)
    )
    grad_ref[...] = grad
    send_ref[...] = grad.astype(BF16)


def router_backward(rows_back, turn, middle, probs, mask, gains, c, hidden, experts, after=()):
    rows, width = middle.shape
    return kernel_call(
        functools.partial(router_kernel, experts=experts),
        "router_backward",
        5,
        [rows_back, turn, middle, probs, mask, gains, c, hidden],
        [((rows, width), F32), ((rows, width), BF16), ((experts + 8, width), F32)],
        hbm=(0,),
        after=after,
        scratch=[pltpu.VMEM(rows_back.shape, BF16), pltpu.SemaphoreType.DMA((4,))],
        late=(1, 2, 4, 6, 7),
        stored=(0,),
    )


def pair_kernel(keep_ref, other_ref, total_ref, *sends):
    for flip in range(4):
        total = keep_ref[flip] + other_ref[flip].astype(F32)
        if flip:
            sends[flip - 1][...] = total.astype(BF16)
        else:
            total_ref[...] = total


def pair_sum(keep, other):
    rows, width = keep.shape[1:]
    return kernel_call(
        pair_kernel, "pair_sum", 1.2, [keep, other], [((rows, width), F32)] + [((rows, width), BF16)] * 3
    )


def input_kernel(total_ref, *refs, experts, store):
    came = refs[:3]
    x_ref, gains_ref, middle_grad_ref, out_ref = refs[3:]
    total = total_ref[...]
    for piece in came:
        total = total + piece[...].astype(F32)
    x = x_ref[...].astype(F32)
    scale = lax.rsqrt(jnp.mean(x * x, axis=1, keepdims=True) + EPSILON)
    normed = x * scale
    inner = total * gains_ref[experts : experts + 1]
    out_ref[...] = middle_grad_ref[...] + scale * (
        inner - normed * jnp.mean(inner * normed, axis=1, keepdims=True)
    )


def input_grad(total, came, x, gains, middle_grad, experts):
    return kernel_call(
        functools.partial(input_kernel, experts=experts),
        "input_grad",
        2,
        [total, *came, x, gains, middle_grad],
        [(middle_grad.shape, F32)],
        held=(4, 6),
        stored=(0,),
    )[0]


PIECE, SPARE, SLICE = 16, 3, 64


def passed(value, after):
    results = [(value.shape, value.dtype)]
    return move_call(lambda *refs: [refs], "passed", 0.5, [value], results, after, 63)[0]


def shares_kernel(pieces_ref, out_ref, rest_ref):
    total = pieces_ref[0].astype(F32)
    for i in range(1, pieces_ref.shape[0]):
        total = total + pieces_ref[i].astype(F32)
    base = 8 * PIECE
    fill = jnp.zeros((PIECE - SPARE, 128), F32)
    for part in range(8):
        out_ref[part, :PIECE] = total[part * PIECE : (part + 1) * PIECE].astype(BF16)
        spare = total[base + part * SPARE : base + (part + 1) * SPARE]
        out_ref[part, PIECE:] = jnp.concatenate([spare, fill], axis=0).astype(BF16)
    rest_ref[...] = total[base + 2 * PIECE :].astype(BF16)


def shares_sum(pieces, after=()):
    return kernel_call(
        shares_kernel,
        "shares_sum",
        0.1,
        [pieces],
        [((8, 2 * PIECE, 128), BF16), ((SLICE, 128), BF16)],
        after=after,
    )


def whole_kernel(came_ref, rest_ref, out_ref):
    spare = came_ref[0, PIECE:].astype(F32)
    for i in range(1, 8):
        spare = spare + came_ref[i, PIECE:].astype(F32)
    rows = [came_ref[i, :PIECE] for i in range(8)] + [spare.astype(BF16), rest_ref[...]]
    rows = jnp.concatenate(rows, axis=0)
    for i in range(16):
        out_ref[i] = rows


def whole_pieces(came, rest, after=()):
    return kernel_call(
        whole_kernel,
        "whole_pieces",
        0.1,
        [came, rest],
        [((16, 9 * PIECE + SLICE, 128), BF16)],
        after=after,
    )[0]


def final_kernel(pieces_ref, wq_ref, wk_ref, wv_ref, gain_ref, *outs, experts):
    query_ref, key_ref, value_ref, output_ref, one_ref, two_ref, qg_ref, kg_ref, router_ref = outs
    rows = pieces_ref.shape[2]
    q_columns = query_ref.shape[1] // 8
    kv_columns = key_ref.shape[1] // 8
    sums = jnp.zeros((rows, 1), F32)
    base = 8 * PIECE
    for pair in range(4):
        keys, values = [], []
        for source in (2 * pair, 2 * pair + 1):
            block = [pieces_ref[i, source * PIECE : (source + 1) * PIECE] for i in range(16)]
            turned = jnp.concatenate(block, axis=0).astype(F32).T
            span = slice(source * q_columns, (source + 1) * q_columns)
            query = turned[:, :q_columns]
            query_ref[:, span] = query
            sums = sums + jnp.sum(query * wq_ref[:, span].astype(F32), axis=1, keepdims=True)
            keys.append(turned[:, q_columns : q_columns + kv_columns])
            values.append(turned[:, q_columns + kv_columns :])
        span = slice(2 * pair * kv_columns, 2 * (pair + 1) * kv_columns)
        for parts, ref, weight in ((keys, key_ref, wk_ref), (values, value_ref, wv_ref)):
            both = jnp.concatenate(parts, axis=1)
            ref[:, span] = both
            sums = sums + jnp.sum(both * weight[:, span].astype(F32), axis=1, keepdims=True)
    for i in range(16):
        half = i % 2 * SLICE
        output_ref[half : half + SLICE, i // 2 * rows : (i // 2 + 1) * rows] = pieces_ref[
            i, base + PIECE :
        ].astype(F32)
    spare = pieces_ref[:, base : base + PIECE].astype(F32)
    spare = jnp.concatenate([spare[i, :SPARE] for i in range(16)], axis=0)
    one_ref[...] = jnp.broadcast_to(sums, (rows, 128)).T[:1] / gain_ref[...].astype(F32)
    two_ref[...] = spare[experts : experts + 1]
    step = qg_ref.shape[1]
    qg_ref[...] = spare[experts + 1 : experts + 2, :step]
    kg_ref[...] = spare[experts + 2 : experts + 3, :step]
    router_ref[...] = spare[:experts]


def final_grads(pieces, wq, wk, wv, gain, experts):
    rows = pieces.shape[2]
    return kernel_call(
        functools.partial(final_kernel, experts=experts),
        "final_grads",
        0.2,
        [pieces, wq, wk, wv, gain],
        [
            (wq.shape, F32),
            (wk.shape, F32),
            (wv.shape, F32),
            ((rows, 8 * rows), F32),
            ((1, rows), F32),
            ((1, rows), F32),
            ((1, HEAD // 8), F32),
            ((1, HEAD // 8), F32),
            ((experts, rows), F32),
        ],
        held=(1, 2, 3, 4),
    )


def send(values, axis, flip):
    count = lax.axis_size(axis)
    return lax.ppermute(values, axis, [(i, i ^ flip) for i in range(count)])


def along_z(values):
    if not isinstance(values, (list, tuple)):
        values = [values] * 3
    return [send(value, "fsdp", 2 * (i + 1)) for i, value in enumerate(values)]


def gather_fsdp(block, name):
    came = along_z(block)
    return came, send(row([block, *came], name), "fsdp", 1)


def exchange(rows):
    return lax.all_to_all(rows, "expert", 0, 0, tiled=True)


def shards(
    tokens,
    lengths,
    routes,
    first_gain,
    query_weight,
    key_weight,
    value_weight,
    output_weight,
    query_gain,
    key_gain,
    second_gain,
    router_weight,
    gate_weight,
    up_weight,
    down_weight,
    cotangent,
):
    own = tokens[0]
    upstream = cotangent[0]
    rows, width = own.shape
    fsdp = lax.axis_size("fsdp")
    owners = lax.axis_size("expert")
    me = lax.axis_index("fsdp").astype(jnp.int32).reshape(1)
    owner = lax.axis_index("expert").astype(jnp.int32).reshape(1)
    experts = router_weight.shape[1]
    capacity = 3 * rows * routes.shape[2] // (2 * experts)
    kv_columns = key_weight.shape[1] // fsdp
    q_columns = query_weight.shape[1] // fsdp
    columns = q_columns + 2 * kv_columns
    q_heads = q_columns // HEAD

    packed, x_sends, dressed, mask = pack_weights(
        me,
        own,
        query_weight,
        key_weight,
        value_weight,
        router_weight.T,
        first_gain[None],
        second_gain[None],
        query_gain[None],
        key_gain[None],
        routes[0].T,
        upstream,
    )
    x_came = along_z(x_sends)
    x_other = [send(own, "fsdp", 1), send(packed[1], "fsdp", 1)]
    x_other.append(send(relay(x_came, rows * fsdp, after=tuple(x_other)), "fsdp", 1))
    deal, turn = slot_tables(mask, capacity)
    c_all = lax.all_gather(dressed, "expert", axis=0)
    wo_came = along_z(output_weight)

    ends = jnp.cumsum(lengths[0])
    place = jnp.arange(rows * fsdp, dtype=jnp.int32)
    start = jnp.max(jnp.where(ends[:, None] <= place[None, :], ends[:, None], 0), axis=0)
    position = (place - start).astype(F32)
    frequency = ROPE_BASE ** (-jnp.arange(HEAD // 2, dtype=F32) * 2.0 / HEAD)
    angles = frequency[:, None] * position[None, :]
    cosine, sine = jnp.cos(angles), jnp.sin(angles)
    start = start[None, :].astype(jnp.int32)

    h1, pre, keep, give, inverse, gains, heads, turned, mixed = attention_forward(
        me, own, packed[0], x_came, x_other, cosine, sine, start, experts, q_heads, after=(deal,)
    )
    other = send(give, "fsdp", 1)
    mixed_sends, wo_stack = merge(keep, other, output_weight, wo_came)
    mixed_came = along_z(mixed_sends)
    wo_other = send(wo_stack, "fsdp", 1)
    middle, probs, hidden, sent = middle_layer(
        own, keep, other, mixed_came, output_weight, wo_came, wo_other, gains, deal, experts, owners
    )
    h_rows = exchange(sent)
    rows_c, row_mask, back = deal_rows(owner, c_all, down_weight, experts, capacity)
    rows_back, gate_low, up_low, active, weighted, share = expert_layer(
        owner, h_rows, gains, row_mask, back, gate_weight, up_weight, experts
    )
    came_back = exchange(rows_back)
    grads, tick = expert_weights(h_rows, rows_c, gate_low, up_low, weighted)
    grads = lax.psum(grads, "fsdp")
    gate_sum, up_sum, down_sum = widen(grads)
    sent, tick = expert_outputs(active, share, down_weight, owners, after=(tick,))

    middle_grad, middle_low, extra = router_backward(
        came_back, turn, middle, probs, mask, gains, upstream, hidden, experts, after=(tick,)
    )
    da_came, da_other = gather_fsdp(middle_low, "row_middle")
    out_rows = exchange(sent)
    layer_out, _ = layer_output(out_rows, turn, middle)
    first, dh_keep, dh_give = attention_backward(
        me,
        middle_low,
        da_came,
        da_other,
        heads,
        output_weight,
        cosine,
        sine,
        start,
        h1,
        pre,
        mixed,
        inverse,
        turned,
        extra,
        experts,
        q_heads,
    )
    dh_total, *dh_sends = pair_sum(dh_keep, send(dh_give, "fsdp", 1))
    dh_came = along_z(dh_sends)
    tokens_grad = input_grad(dh_total, dh_came, own, gains, middle_grad, experts)
    first = passed(first, after=(out_rows, grads))
    parted, rest = shares_sum(exchange(first), after=(dh_total,))
    parted = lax.all_to_all(parted, "fsdp", 0, 0, tiled=True)
    pieces = exchange(whole_pieces(parted, rest, after=(layer_out,)))
    query_sum, key_sum, value_sum, output_sum, one_sum, two_sum, *gain_sums, router_sum = final_grads(
        pieces, query_weight, key_weight, value_weight, first_gain[None], experts
    )
    return (
        layer_out[None],
        tokens_grad[None],
        one_sum[0],
        query_sum,
        key_sum,
        value_sum,
        output_sum,
        gain_sums[0][0],
        gain_sums[1][0],
        two_sum[0],
        router_sum.T,
        gate_sum,
        up_sum,
        down_sum,
    )


def solution(mesh):
    whole = P("expert", "fsdp", None)
    rows = P("fsdp", None)
    vector = P("fsdp")
    owned = P("expert", None, None)
    return jax.shard_map(
        shards,
        mesh=mesh,
        in_specs=(
            whole,
            P("expert", None),
            whole,
            vector,
            rows,
            rows,
            rows,
            rows,
            vector,
            vector,
            vector,
            rows,
            owned,
            owned,
            owned,
            whole,
        ),
        out_specs=(
            whole,
            whole,
            vector,
            rows,
            rows,
            rows,
            rows,
            vector,
            vector,
            vector,
            rows,
            owned,
            owned,
            owned,
        ),
        check_vma=False,
    )
```

```python
import functools

import jax
import jax.numpy as jnp
from jax import lax
from jax.experimental import pallas as pl
from jax.experimental.pallas import tpu as pltpu
from jax.sharding import PartitionSpec as P

EPSILON = 1e-06
ROPE_BASE = 10000.0
HEAD = 64
TILE = 256
F32 = jnp.float32
BF16 = jnp.bfloat16
VMEM = pl.BlockSpec(memory_space=pltpu.VMEM)
SMEM = pl.BlockSpec(memory_space=pltpu.SMEM)
ANY = pl.BlockSpec(memory_space=pl.ANY)
HBM = pl.BlockSpec(memory_space=pltpu.HBM)


def dot(left, right, dims=((1,), (0,))):
    return lax.dot_general(left, right, (dims, ((), ())), preferred_element_type=F32)


def shape(extent, dtype):
    return jax.ShapeDtypeStruct(extent, dtype)


def kernel_call(
    body, name, micros, operands, results, smem=0, hbm=(), out_hbm=(), after=(), scratch=(), held=(), late=(), stored=(), mib=63
):
    held = tuple(held) + tuple(late)
    n, a, r, s = len(operands), len(after), len(results), len(scratch)
    specs = [SMEM if i < smem else HBM if i in held or i in hbm else VMEM for i in range(n)]
    out_specs = [HBM if i in stored or i in out_hbm else VMEM for i in range(r)]
    staged = [pltpu.VMEM(operands[i].shape, operands[i].dtype) for i in held]
    staged += [pltpu.VMEM(*results[i]) for i in stored]
    sems = [pltpu.SemaphoreType.DMA((max(len(held), 1),)), pltpu.SemaphoreType.DMA((max(len(stored), 1),))]

    def wrapped(*refs):
        ins, outs = list(refs[:n]), list(refs[n + a : n + a + r])
        own = refs[n + a + r : n + a + r + s]
        stages, (load_sem, store_sem) = refs[n + a + r + s : -2], refs[-2:]
        loads, stores, begun = {}, {}, []
        for k, i in enumerate(held):
            loads[i] = pltpu.make_async_copy(ins[i], stages[k], load_sem.at[k])
            loads[i].start()
            ins[i] = stages[k]
        for k, i in enumerate(stored):
            stores[i] = pltpu.make_async_copy(stages[len(held) + k], outs[i], store_sem.at[k])
            outs[i] = stages[len(held) + k]
        for i in held:
            if i not in late:
                loads[i].wait()

        def store(*which):
            for i in which:
                stores[i].start()
                begun.append(i)

        extra = {}
        if late:
            extra["wait"] = lambda i: loads[i].wait()
        if stored:
            extra["store"] = store
        body(*ins, *outs, *own, **extra)
        store(*[i for i in stored if i not in begun])
        for i in stored:
            stores[i].wait()

    return pl.pallas_call(
        wrapped,
        out_shape=[shape(*result) for result in results],
        in_specs=specs + [ANY] * a,
        out_specs=out_specs,
        scratch_shapes=list(scratch) + staged + sems,
        compiler_params=pltpu.CompilerParams(vmem_limit_bytes=mib * 1024 * 1024),
        cost_estimate=pl.CostEstimate(flops=0, bytes_accessed=int(micros * 3.6e6), transcendentals=0),
        name=name,
    )(*operands, *after)


def move_call(moves, name, micros, operands, results, after=(), mib=10):
    def body(*refs):
        for source, target in moves(*refs):
            target[...] = source[...]

    return kernel_call(body, name, micros, operands, results, after=after, mib=mib)


def lane_blocks(value):
    return jnp.concatenate([value[:, i : i + 128] for i in range(0, value.shape[1], 128)], axis=0)


def joined_lanes(value, count):
    rows = value.shape[0] // count
    return jnp.concatenate([value[i * rows : (i + 1) * rows] for i in range(count)], axis=1)


def softmax_rows(logits):
    powers = jnp.exp(logits - jnp.max(logits, axis=0, keepdims=True))
    return powers / jnp.sum(powers, axis=0, keepdims=True)


def head_forward(pre, gain, cosine, sine):
    scale = lax.rsqrt(jnp.mean(pre * pre, axis=0, keepdims=True) + EPSILON)
    normed = pre * scale
    scaled = normed * gain
    a, b = scaled[: HEAD // 2], scaled[HEAD // 2 :]
    turned = jnp.concatenate([a * cosine - b * sine, b * cosine + a * sine], axis=0)
    return turned, normed, scale


def head_backward(grad, normed, scale, gain, cosine, sine):
    a, b = grad[: HEAD // 2], grad[HEAD // 2 :]
    unturned = jnp.concatenate([a * cosine + b * sine, b * cosine - a * sine], axis=0)
    gain_grad = jnp.sum(unturned * normed, axis=1, keepdims=True)
    inner = unturned * gain
    pre_grad = scale * (inner - normed * jnp.mean(inner * normed, axis=0, keepdims=True))
    return pre_grad, gain_grad


def slots_kernel(mask_ref, deal_ref, turn_ref, whole_ref, *, capacity, store):
    experts, rows = mask_ref.shape
    mask = mask_ref[...]
    ranks = dot(mask.astype(BF16), earlier(rows))
    slot = lax.broadcasted_iota(jnp.int32, (capacity, rows), 0).astype(F32) + 1.0
    for expert in range(experts):
        one = slice(expert, expert + 1)
        whole_ref[expert * capacity : (expert + 1) * capacity] = jnp.where(
            (ranks[one] == slot) & (mask[one] > 0.5), 1.0, 0.0
        )
    deal_ref[...] = whole_ref[...].astype(BF16)
    store(0)
    for part in range(0, experts * capacity, 128):
        turn_ref[:, part : part + 128] = whole_ref[part : part + 128].T.astype(BF16)


def slot_tables(mask, capacity):
    experts, rows = mask.shape
    slots = experts * capacity
    return kernel_call(
        functools.partial(slots_kernel, capacity=capacity),
        "slot_tables",
        2.0,
        [mask],
        [((slots, rows), BF16), ((rows, slots), BF16)],
        scratch=[pltpu.VMEM((slots, rows), F32)],
        stored=(0, 1),
    )


def earlier(rows):
    return (
        lax.broadcasted_iota(jnp.int32, (rows, rows), 0)
        <= lax.broadcasted_iota(jnp.int32, (rows, rows), 1)
    ).astype(BF16)


def pack_kernel(
    me_ref, x_ref, wq_ref, wk_ref, wv_ref, router_ref, one_ref, two_ref, qg_ref, kg_ref, routes_ref, c_ref, *outs, wait, store
):
    own_ref, sends, dressed_ref, mask_ref, other_ref, parts_ref = outs[0], outs[1:4], *outs[4:]
    experts, rows = router_ref.shape
    wide = wq_ref.shape[1] // 8
    narrow = wk_ref.shape[1] // 8
    count = qg_ref.shape[1]
    heads = jnp.concatenate([qg_ref[...], kg_ref[...]], axis=0).astype(F32)
    heads = jnp.concatenate([heads, jnp.zeros((2, 128 - count), F32)], axis=1)
    heads = jnp.concatenate([heads, jnp.zeros((126, 128), F32)], axis=0).T[:count]
    small = jnp.concatenate(
        [
            router_ref[...].astype(F32),
            one_ref[...].astype(F32),
            two_ref[...].astype(F32),
            jnp.zeros((6, 128), F32),
            heads,
        ],
        axis=0,
    ).astype(BF16)
    for part in range(8):
        parts_ref[part, :wide] = wq_ref[:, part * wide : (part + 1) * wide].astype(F32).T.astype(BF16)
        parts_ref[part, wide + 2 * narrow :] = small
    for pair in range(4):
        span = slice(pair * 128, (pair + 1) * 128)
        for ref, place in ((wk_ref, wide), (wv_ref, wide + narrow)):
            turned = ref[:, span].astype(F32).T.astype(BF16)
            parts_ref[2 * pair, place : place + narrow] = turned[:narrow]
            parts_ref[2 * pair + 1, place : place + narrow] = turned[narrow:]
    me = me_ref[0]
    tall = parts_ref.shape[1]
    blocks = lane_blocks(x_ref[...])
    base = blocks.shape[0]
    own_ref[...] = parts_ref[me]
    other_ref[...] = parts_ref[me ^ 1]
    for flip in range(1, 4):
        sends[flip - 1][:base] = blocks
        sends[flip - 1][base : base + tall] = parts_ref[me ^ (2 * flip)]
        sends[flip - 1][base + tall :] = parts_ref[me ^ (2 * flip + 1)]
    store(1, 2, 3, 6, 0)
    wait(10)
    wait(11)
    width = c_ref.shape[1]
    subs = lax.broadcasted_iota(jnp.int32, (128, rows), 0)
    routed = jnp.zeros((128, rows), F32)
    for route in range(routes_ref.shape[0]):
        routed = routed + jnp.where(routes_ref[route : route + 1] == subs, 1.0, 0.0)
    dressed_ref[:, :width] = c_ref[...]
    dressed_ref[:, width:] = routed.T.astype(BF16)
    mask_ref[...] = routed[:experts]


def pack_weights(me, x, wq, wk, wv, router, one, two, qg, kg, routes, c):
    experts = router.shape[0]
    tall = (wq.shape[1] + wk.shape[1] + wv.shape[1]) // 8 + experts + 16
    rows, width = x.shape
    base = rows * 8
    own, first, second, third, dressed, mask, other = kernel_call(
        pack_kernel,
        "pack_weights",
        2.5,
        [me, x, wq, wk, wv, router, one, two, qg, kg, routes, c],
        [((tall, 128), BF16)]
        + [((base + 2 * tall, 128), BF16)] * 3
        + [((rows, width + 128), BF16), ((experts, rows), F32), ((tall, 128), BF16)],
        smem=1,
        scratch=[pltpu.VMEM((8, tall, 128), BF16)],
        held=range(1, 10),
        late=(10, 11),
        stored=(0, 1, 2, 3, 4, 5, 6),
    )
    return (own, other), [first, second, third], dressed, mask


def relay(came, base, after):
    tall = (came[0].shape[0] - base) // 2

    def moves(*refs):
        pairs = []
        for flip, ref in enumerate(refs[:3]):
            pairs.append((ref.at[:base], refs[3].at[flip, :base]))
            pairs.append((ref.at[base + tall :], refs[3].at[flip, base:]))
        return pairs

    return move_call(moves, "relay", 1.5, came, [((3, base + tall, 128), BF16)], after)[0]


def forward_kernel(me_ref, x_ref, own_ref, *refs, experts, q_heads, store):
    came, other_x, other_w, other_ref = refs[:3], refs[3], refs[4], refs[5]
    cos_ref, sin_ref, start_ref = refs[6:9]
    h1_ref, pre_ref, keep_ref, give_ref, inverse_ref, gains_ref, heads_ref, turned_ref, out_ref = refs[-9:]
    rows, width = x_ref.shape
    q_columns = q_heads * HEAD
    columns = q_columns + 2 * HEAD
    total = rows * 8
    tall = own_ref.shape[0]
    base = 8 * rows
    me = me_ref[0]
    for slot in range(8):
        flip = slot // 2
        if slot % 2:
            piece = other_ref[flip - 1, base:] if flip else other_w[...]
        elif flip:
            piece = came[flip - 1][base : base + tall]
        else:
            piece = own_ref[...]
        span = pl.ds(pl.multiple_of((me ^ slot) * rows, rows), rows)
        turned_ref[:, span] = piece[:columns]
        small = piece[columns:].astype(F32)
        gains_ref[:, span] = small[: experts + 8]
        heads_ref[pl.ds(pl.multiple_of((me ^ slot) * 8, 8), 8)] = small[experts + 8 :]
    gain_one = gains_ref[experts : experts + 1]
    for slot in range(8):
        flip = slot // 2
        if slot % 2:
            x = joined_lanes(other_ref[flip - 1, :base], 8) if flip else other_x[...]
        elif flip:
            x = joined_lanes(came[flip - 1][:base], 8)
        else:
            x = x_ref[...]
        x = x.astype(F32)
        scale = lax.rsqrt(jnp.mean(x * x, axis=1, keepdims=True) + EPSILON)
        h1_ref[slot] = (x * scale * gain_one).astype(BF16)
    store(0, 6, 7)
    for slot in range(8):
        block = dot(turned_ref[...], h1_ref[slot], ((1,), (1,)))
        place = pl.multiple_of((me ^ slot) * rows, rows)
        pre_ref[:, pl.ds(place, rows)] = block
    store(1)
    cosine, sine = cos_ref[...], sin_ref[...]
    gain_query, gain_key = heads_ref[:, :1], heads_ref[:, 1:2]
    key = head_forward(pre_ref[q_columns : q_columns + HEAD], gain_key, cosine, sine)[0]
    key = key.T.astype(BF16)
    value = pre_ref[q_columns + HEAD :].astype(BF16)
    inverse_ref[...] = jnp.zeros(inverse_ref.shape, F32)
    for head in range(q_heads):
        query = head_forward(pre_ref[head * HEAD : (head + 1) * HEAD], gain_query, cosine, sine)[0]
        query = query.astype(BF16) * jnp.array(HEAD ** (-0.5), BF16)
        for tile in range(total // TILE):
            low, high = tile * TILE, (tile + 1) * TILE
            scores = dot(key[:high], query[:, low:high])
            u = lax.broadcasted_iota(jnp.int32, (high, TILE), 0)
            t = lax.broadcasted_iota(jnp.int32, (high, TILE), 1) + low
            allowed = (u >= start_ref[:, low:high]) & (u <= t)
            powers = jnp.where(allowed, jnp.exp(scores), 0.0)
            inverse = 1.0 / jnp.sum(powers, axis=0, keepdims=True)
            probs = (powers * inverse).astype(BF16)
            mixed = dot(value[:, :high], probs).astype(BF16)
            inverse_ref[head : head + 1, low:high] = inverse
            for part in range(TILE // rows):
                out_ref[low // rows + part, head * HEAD : (head + 1) * HEAD] = mixed[
                    :, part * rows : (part + 1) * rows
                ]
    for slot in range(8):
        (give_ref if slot % 2 else keep_ref)[slot // 2] = out_ref[me ^ slot]


def attention_forward(me, x, own, came, other, cosine, sine, start, experts, q_heads, after=()):
    rows, width = x.shape
    total = 8 * rows
    columns = (q_heads + 2) * HEAD
    q_columns = q_heads * HEAD
    return kernel_call(
        functools.partial(forward_kernel, experts=experts, q_heads=q_heads),
        "attention_forward",
        7.0,
        [me, x, own, *came, *other, cosine, sine, start],
        [
            ((8, rows, width), BF16),
            ((columns, total), F32),
            ((4, q_columns, rows), BF16),
            ((4, q_columns, rows), BF16),
            ((8, total), F32),
            ((experts + 8, width), F32),
            ((HEAD, 128), F32),
            ((columns, width), BF16),
            ((8, q_columns, rows), BF16),
        ],
        smem=1,
        after=after,
        held=(1,),
        stored=(0, 1, 4, 6, 7, 8),
    )


def merge(keep, came, wo, wo_came):
    def moves(keep_ref, came_ref, *refs):
        weights, outs, stacked = refs[:4], refs[4:7], refs[7]
        pairs = [(weight, stacked.at[i]) for i, weight in enumerate(weights)]
        for flip in range(1, 4):
            pairs.append((keep_ref.at[flip], outs[flip - 1].at[0]))
            pairs.append((came_ref.at[flip], outs[flip - 1].at[1]))
        return pairs

    extent = ((2,) + keep.shape[1:], BF16)
    results = [extent] * 3 + [((4,) + wo.shape, BF16)]
    *sends, stacked = move_call(moves, "merge", 1.0, [keep, came, wo, *wo_came], results)
    return sends, stacked


def middle_kernel(x_ref, keep_ref, other_ref, *refs, experts, wait, store):
    came, wo_ref, wo_came, wo_other_ref, gains_ref, deal_ref = refs[:3], refs[3], refs[4:7], refs[7], refs[8], refs[9]
    middle_ref, probs_ref, hidden_ref, sent_ref, mixed_ref, whole_ref, out_ref, out_sem = refs[10:]
    rows, width = x_ref.shape
    for slot in range(8):
        flip, core = slot // 2, slot % 2
        if flip:
            piece = came[flip - 1][core]
        else:
            piece = (other_ref if core else keep_ref)[0]
        span = slice(slot * 128, (slot + 1) * 128)
        mixed_ref[:, span] = piece.astype(F32).T.astype(BF16)
    for i in (6, 7, 8, 9, 10):
        wait(i)
    for slot in range(8):
        flip = slot // 2
        span = slice(slot * 128, (slot + 1) * 128)
        if slot % 2:
            whole_ref[span] = wo_other_ref[flip]
        else:
            whole_ref[span] = (wo_came[flip - 1] if flip else wo_ref)[...]
    wait(0)
    middle = x_ref[...].astype(F32) + dot(mixed_ref[...], whole_ref[...])
    middle_ref[...] = middle
    scale = lax.rsqrt(jnp.mean(middle * middle, axis=1, keepdims=True) + EPSILON)
    hidden = (middle * scale * gains_ref[experts + 1 : experts + 2]).astype(BF16)
    hidden_ref[...] = hidden
    probs_ref[...] = softmax_rows(dot(gains_ref[:experts].astype(BF16), hidden, ((1,), (1,))))
    store(0, 2)
    owners, per_owner, capacity, _ = sent_ref.shape
    group = owners // 4
    size = group * per_owner * capacity
    copies = []
    wait(12)
    for part in range(4):
        taken = dot(deal_ref[part * size : (part + 1) * size], hidden).astype(BF16)
        blocks = slice(group * part, group * (part + 1))
        out_ref[blocks] = taken.reshape(group, per_owner, capacity, width)
        copies.append(pltpu.make_async_copy(out_ref.at[blocks], sent_ref.at[blocks], out_sem.at[part]))
        copies[-1].start()
    for copy in copies:
        copy.wait()


def middle_layer(x, keep, other, came, wo, wo_came, wo_other, gains, deal, experts, owners):
    rows, width = x.shape
    per_owner = experts // owners
    capacity = deal.shape[0] // experts
    sent = ((owners, per_owner, capacity, width), BF16)
    return kernel_call(
        functools.partial(middle_kernel, experts=experts),
        "middle_layer",
        3.0,
        [x, keep, other, *came, wo, *wo_came, wo_other, gains, deal],
        [((rows, width), F32), ((experts, rows), F32), ((rows, width), BF16), sent],
        out_hbm=(3,),
        scratch=[
            pltpu.VMEM((rows, width), BF16),
            pltpu.VMEM((width, width), BF16),
            pltpu.VMEM(*sent),
            pltpu.SemaphoreType.DMA((4,)),
        ],
        late=(6, 7, 8, 9, 10, 0, 12),
        stored=(0, 2),
    )


def row(pieces, name):
    def moves(*refs):
        return [(ref, refs[-1].at[i]) for i, ref in enumerate(refs[:-1])]

    return move_call(moves, name, 1.0, pieces, [((len(pieces),) + pieces[0].shape, BF16)])[0]


def backward_kernel(me_ref, own_da_ref, *refs, experts, q_heads, wait):
    came, other_ref = refs[:3], refs[3]
    heads_ref, wo_ref, cos_ref, sin_ref, start_ref = refs[4:9]
    h1_ref, pre_ref, mixed_ref, inverse_ref, turned_ref, extra_ref = refs[9:15]
    first_ref, keep_ref, send_ref = refs[-10:-7]
    da_ref, mixed_grad_ref, dkey_ref, dvalue_ref, low_ref, out_slots_ref, grad_ref = refs[-7:]
    rows, width = own_da_ref.shape
    q_columns = q_heads * HEAD
    columns = q_columns + 2 * HEAD
    total = rows * 8
    me = me_ref[0]
    for slot in range(8):
        flip, core = slot // 2, slot % 2
        if core:
            piece = other_ref[flip]
        else:
            piece = (came[flip - 1] if flip else own_da_ref)[...]
        span = slice(slot * rows, (slot + 1) * rows)
        da_ref[span] = piece
        place = pl.multiple_of((me ^ slot) * rows, rows)
        mixed_grad_ref[:, pl.ds(place, rows)] = dot(wo_ref[...], piece, ((1,), (1,))).astype(BF16)
    wait(13)
    for slot in range(8):
        out_slots_ref[:, slot * rows : (slot + 1) * rows] = mixed_ref[me ^ slot]
    wo_grad = dot(out_slots_ref[...], da_ref[...]).astype(BF16)
    wo_grad = lane_blocks(wo_grad)
    wait(12)
    wait(14)
    gain_query, gain_key = heads_ref[:, :1], heads_ref[:, 1:2]
    cosine, sine = cos_ref[...], sin_ref[...]
    key_turned, key_normed, key_scale = head_forward(
        pre_ref[q_columns : q_columns + HEAD], gain_key, cosine, sine
    )
    key_low = key_turned.astype(BF16)
    key = key_turned.T.astype(BF16)
    value = pre_ref[q_columns + HEAD :].T.astype(BF16)
    dkey_ref[...] = jnp.zeros(dkey_ref.shape, F32)
    dvalue_ref[...] = jnp.zeros(dvalue_ref.shape, F32)
    gain_query_grad = jnp.zeros((HEAD, 1), F32)
    pieces = []
    for head in range(q_heads):
        span = slice(head * HEAD, (head + 1) * HEAD)
        turned, normed, scale = head_forward(pre_ref[span], gain_query, cosine, sine)
        query = turned.astype(BF16) * jnp.array(HEAD ** (-0.5), BF16)
        grads = []
        for tile in range(total // TILE):
            low, high = tile * TILE, (tile + 1) * TILE
            part = query[:, low:high]
            mixed_grad = mixed_grad_ref[span, low:high]
            scores = dot(key[:high], part)
            u = lax.broadcasted_iota(jnp.int32, (high, TILE), 0)
            t = lax.broadcasted_iota(jnp.int32, (high, TILE), 1) + low
            allowed = (u >= start_ref[:, low:high]) & (u <= t)
            probs = jnp.where(allowed, jnp.exp(scores) * inverse_ref[head : head + 1, low:high], 0.0)
            attend = dot(value[:high], mixed_grad)
            delta = jnp.sum(probs * attend, axis=0, keepdims=True)
            score_low = (probs * (attend - delta)).astype(BF16)
            grads.append(dot(key_low[:, :high], score_low))
            dkey_ref[:, :high] += dot(part, score_low, ((1,), (1,)))
            dvalue_ref[:, :high] += dot(mixed_grad, probs.astype(BF16), ((1,), (1,)))
        query_grad = jnp.concatenate(grads, axis=1) * HEAD ** (-0.5)
        pre_grad, gain_grad = head_backward(query_grad, normed, scale, gain_query, cosine, sine)
        gain_query_grad += gain_grad
        pieces.append(pre_grad)
    pre_grad, gain_key_grad = head_backward(
        dkey_ref[...], key_normed, key_scale, gain_key, cosine, sine
    )
    pieces += [pre_grad, dvalue_ref[...]]
    pre_grad = jnp.concatenate(pieces, axis=0)
    low_ref[...] = pre_grad.astype(BF16)
    slots_grad = []
    for slot in range(8):
        place = pl.multiple_of((me ^ slot) * rows, rows)
        slots_grad.append(low_ref[:, pl.ds(place, rows)])
    slots_grad = jnp.concatenate(slots_grad, axis=1)
    wait(11)
    wait(15)
    grad_ref[:columns] = dot(slots_grad, h1_ref[...].reshape(total, width))
    extra = extra_ref[...]
    lane = lax.broadcasted_iota(jnp.int32, (HEAD, 128), 1)
    gains = jnp.where(lane == 0, gain_query_grad, jnp.where(lane == 1, gain_key_grad, 0.0))
    gains = gains.T[:2]
    step = HEAD // 8
    grad_ref[columns:] = jnp.zeros((64, width), F32)
    grad_ref[columns : columns + experts + 1] = extra[: experts + 1]
    for part in range(8):
        grad_ref[columns + experts + 1 : columns + experts + 3, part * rows : part * rows + step] = gains[
            :, part * step : (part + 1) * step
        ]
    for piece in range(16):
        spare = []
        place = columns + piece * SPARE
        for part in range(8):
            span = slice(part * rows, (part + 1) * rows)
            block = grad_ref[piece * PIECE : (piece + 1) * PIECE, span]
            first_ref[piece, part * PIECE : (part + 1) * PIECE] = block.astype(BF16)
            spare.append(grad_ref[place : place + SPARE, span])
        spare.append(jnp.zeros((2 * PIECE - 8 * SPARE, 128), F32))
        first_ref[piece, 8 * PIECE : 10 * PIECE] = jnp.concatenate(spare, axis=0).astype(BF16)
        first_ref[piece, 10 * PIECE :] = wo_grad[piece * SLICE : (piece + 1) * SLICE]
    turned = turned_ref[...]
    for slot in range(8):
        low_rows_slot = slots_grad[:, slot * rows : (slot + 1) * rows].astype(F32).T.astype(BF16)
        part = dot(low_rows_slot, turned)
        if slot % 2:
            send_ref[slot // 2] = part.astype(BF16)
        else:
            keep_ref[slot // 2] = part


def attention_backward(
    me, da, came, other, heads, wo, cosine, sine, start, h1, pre, mixed, inverse, turned, extra, experts, q_heads, after=()
):
    rows, width = da.shape
    total = 8 * rows
    columns = pre.shape[0]
    q_columns = q_heads * HEAD
    return kernel_call(
        functools.partial(backward_kernel, experts=experts, q_heads=q_heads),
        "attention_backward",
        12,
        [me, da, *came, other, heads, wo, cosine, sine, start, h1, pre, mixed, inverse, turned, extra],
        [
            ((16, 10 * PIECE + SLICE, 128), BF16),
            ((4, rows, width), F32),
            ((4, rows, width), BF16),
        ],
        smem=1,
        after=after,
        held=(6, 7),
        late=(11, 12, 13, 14, 15),
        scratch=[
            pltpu.VMEM((total, width), BF16),
            pltpu.VMEM((q_columns, total), BF16),
            pltpu.VMEM((HEAD, total), F32),
            pltpu.VMEM((HEAD, total), F32),
            pltpu.VMEM((columns, total), BF16),
            pltpu.VMEM((q_columns, total), BF16),
            pltpu.VMEM((columns + 64, width), F32),
        ],
    )


def deal_kernel(owner_ref, c_ref, down_ref, rows_c, mask_ref, back_ref, c_scratch, sems, *, experts, capacity, wait, store):
    owner = owner_ref[0]
    per_owner, hidden, width = down_ref.shape
    rows = c_ref.shape[1]
    loads = [pltpu.make_async_copy(c_ref.at[i], c_scratch.at[i], sems.at[i]) for i in range(16)]
    for load in loads:
        load.start()
    lanes = lax.broadcasted_iota(jnp.int32, (experts, 128), 1)
    subs = lax.broadcasted_iota(jnp.int32, (experts, 128), 0)
    eye = (lanes == subs).astype(BF16)
    before = earlier(rows)
    mine_of = lax.broadcasted_iota(jnp.int32, (experts, rows), 0) - owner * per_owner
    slot = lax.broadcasted_iota(jnp.int32, (capacity, rows), 0).astype(F32) + 1.0
    for block in range(16):
        loads[block].wait()
        c = c_scratch[block]
        mask = dot(eye, c[:, width:], ((1,), (1,)))
        ranks = dot(mask.astype(BF16), before)
        deals = []
        for k in range(per_owner):
            mine = mine_of == k
            hit = jnp.sum(jnp.where(mine, mask, 0.0), axis=0, keepdims=True)
            rank = jnp.sum(jnp.where(mine, ranks, 0.0), axis=0, keepdims=True)
            deals.append(jnp.where((rank == slot) & (hit > 0.5), 1.0, 0.0))
        taken = dot(jnp.concatenate(deals, axis=0).astype(BF16), c).astype(BF16)
        span = slice(block * capacity, (block + 1) * capacity)
        for k in range(per_owner):
            spot = slice(k * capacity, (k + 1) * capacity)
            rows_c[k, span] = taken[spot, :width]
            mask_ref[k, span] = taken[spot, width:]
    store(0, 1)
    wait(2)
    for k in range(per_owner):
        for tile in range(16 * capacity // TILE):
            span = slice(tile * TILE, (tile + 1) * TILE)
            back_ref[k, span] = dot(rows_c[k, span], down_ref[k], ((1,), (1,)))


def deal_rows(owner, c, down, experts, capacity):
    per_owner, hidden, width = down.shape
    count = 16 * capacity
    return kernel_call(
        functools.partial(deal_kernel, experts=experts, capacity=capacity),
        "deal_rows",
        12.0,
        [owner, c, down],
        [
            ((per_owner, count, width), BF16),
            ((per_owner, count, 128), BF16),
            ((per_owner, count, hidden), F32),
        ],
        smem=1,
        hbm=(1,),
        scratch=[pltpu.VMEM(c.shape, BF16), pltpu.SemaphoreType.DMA((16,))],
        late=(2,),
        stored=(0, 1, 2),
    )


def expert_kernel(
    owner_ref,
    h_hbm,
    gains_ref,
    mask_ref,
    back_hbm,
    gate_hbm,
    up_hbm,
    rows_hbm,
    gate_out,
    up_out,
    active_out,
    weighted_out,
    share_ref,
    h_ref,
    back_in,
    gate_ref,
    up_ref,
    rows_back,
    load_sem,
    store_sem,
    *,
    experts,
    store,
):
    owners, per_owner, capacity, width = h_hbm.shape
    group = 8
    parts = owners // group
    size = group * capacity
    loads = {}
    for k in range(per_owner):
        for part in range(parts):
            blocks = slice(part * group, (part + 1) * group)
            spot = (k * parts + part) * 4
            loads[k, part] = [
                pltpu.make_async_copy(h_hbm.at[blocks, k], h_ref.at[blocks, k], load_sem.at[spot]),
                pltpu.make_async_copy(
                    back_hbm.at[k, part * size : (part + 1) * size],
                    back_in.at[k, part * size : (part + 1) * size],
                    load_sem.at[spot + 1],
                ),
            ]
            if part == 0:
                loads[k, part] += [
                    pltpu.make_async_copy(gate_hbm.at[k], gate_ref.at[k], load_sem.at[spot + 2]),
                    pltpu.make_async_copy(up_hbm.at[k], up_ref.at[k], load_sem.at[spot + 3]),
                ]
            for load in loads[k, part]:
                load.start()
    owner = owner_ref[0]
    router = jnp.concatenate([gains_ref[:experts], jnp.zeros((128 - experts, width), F32)], axis=0)
    router = router.astype(BF16)
    lane = lax.broadcasted_iota(jnp.int32, (size, 128), 1)
    copies = []
    for k in range(per_owner):
        place = owner * per_owner + k
        for part in range(parts):
            blocks = slice(part * group, (part + 1) * group)
            span = slice(part * size, (part + 1) * size)
            for load in loads[k, part]:
                load.wait()
            h = h_ref[blocks, k].reshape(size, width)
            gate = dot(h, gate_ref[k])
            up = dot(h, up_ref[k])
            logits = dot(h, router, ((1,), (1,)))
            chosen = mask_ref[k, span] > 0.5
            top = jnp.max(jnp.where(chosen, logits, -1e30), axis=1, keepdims=True)
            powers = jnp.where(chosen, jnp.exp(logits - top), 0.0)
            total = jnp.sum(powers, axis=1, keepdims=True)
            share = jnp.sum(jnp.where(lane == place, powers, 0.0), axis=1, keepdims=True)
            share = share / jnp.where(total > 0.0, total, 1.0)
            share_ref[k, span] = jnp.broadcast_to(share, (size, 128))
            back = back_in[k, span]
            sig = 1.0 / (1.0 + jnp.exp(-gate))
            silu = gate * sig
            active = silu * up
            active_low = active.astype(BF16)
            route_grad = jnp.sum(active_low.astype(F32) * back, axis=1, keepdims=True)
            grad = back * share
            gate_low = (grad * up * (sig + silu * (1.0 - sig))).astype(BF16)
            up_low = (grad * silu).astype(BF16)
            active_out[k, span] = active_low
            weighted_out[k, span] = (active * share).astype(BF16)
            gate_out[k, span] = gate_low
            up_out[k, span] = up_low
            rows = dot(gate_low, gate_ref[k], ((1,), (1,))) + dot(up_low, up_ref[k], ((1,), (1,)))
            high = route_grad.astype(BF16).astype(F32)
            spread_out = jnp.where(lane == place, high, 0.0)
            spread_out = jnp.where(lane == place + experts, route_grad - high, spread_out)
            whole = jnp.concatenate([rows.astype(BF16), spread_out.astype(BF16)], axis=1)
            rows_back[blocks, k] = whole.reshape(group, capacity, width + 128)
            copies.append(
                pltpu.make_async_copy(
                    rows_back.at[blocks, k], rows_hbm.at[blocks, k], store_sem.at[k * parts + part]
                )
            )
            copies[-1].start()
    store(1, 2, 3, 4, 5)
    for copy in copies:
        copy.wait()


def expert_layer(owner, h, gains, mask, back, gate, up, experts):
    per_owner, width, hidden = gate.shape
    owners, _, capacity, _ = h.shape
    count = owners * capacity
    narrow = ((per_owner, count, hidden), BF16)
    rows_back = ((owners, per_owner, capacity, width + 128), BF16)
    pieces = per_owner * (owners // 8)
    return kernel_call(
        functools.partial(expert_kernel, experts=experts),
        "expert_layer",
        14.0,
        [owner, h, gains, mask, back, gate, up],
        [rows_back] + [narrow] * 4 + [((per_owner, count, 128), F32)],
        smem=1,
        hbm=(1, 4, 5, 6),
        out_hbm=(0,),
        scratch=[pltpu.VMEM(value.shape, value.dtype) for value in (h, back, gate, up)]
        + [pltpu.VMEM(*rows_back), pltpu.SemaphoreType.DMA((4 * pieces,)), pltpu.SemaphoreType.DMA((pieces,))],
        stored=(1, 2, 3, 4, 5),
    )


def weights_kernel(
    h_hbm, rows_c, gate_low, up_low, weighted, out_hbm, tick_ref, h_ref, out_ref, load_sem, store_sem, *, wait
):
    tick_ref[...] = jnp.zeros(tick_ref.shape, F32)
    first = ((0,), (0,))
    owners, per_owner, capacity, width = h_hbm.shape
    hidden = gate_low.shape[2]
    half = width // 2
    loads = [
        pltpu.make_async_copy(h_hbm.at[:, k], h_ref.at[:, k], load_sem.at[k]) for k in range(per_owner)
    ]
    for load in loads:
        load.start()
    stores = []

    def keep(place):
        stores.append(pltpu.make_async_copy(out_ref.at[place], out_hbm.at[place], store_sem.at[place]))
        stores[-1].start()

    wait(2)
    for k in range(per_owner):
        loads[k].wait()
        rows_h = h_ref[:, k].reshape(owners * capacity, width)
        for place, low in ((k, gate_low), (per_owner + k, up_low)):
            if k == 0 and place:
                wait(3)
            total = dot(rows_h, low[k], first).astype(BF16)
            out_ref[place, :, :hidden] = total[:half]
            out_ref[place, :, hidden:] = total[half:]
            keep(place)
        if k == 0:
            wait(4)
            wait(1)
        place = 2 * per_owner + k
        out_ref[place] = dot(weighted[k], rows_c[k], first).astype(BF16)
        keep(place)
    for store in stores:
        store.wait()


def expert_weights(h, rows_c, gate_low, up_low, weighted):
    per_owner, count, width = rows_c.shape
    hidden = gate_low.shape[2]
    out = ((3 * per_owner, hidden, width), BF16)
    return kernel_call(
        weights_kernel,
        "expert_weights",
        0.1,
        [h, rows_c, gate_low, up_low, weighted],
        [out, ((8, 128), F32)],
        hbm=(0,),
        out_hbm=(0,),
        scratch=[
            pltpu.VMEM(h.shape, BF16),
            pltpu.VMEM(*out),
            pltpu.SemaphoreType.DMA((per_owner,)),
            pltpu.SemaphoreType.DMA((3 * per_owner,)),
        ],
        late=(2, 3, 4, 1),
    )


def widen_kernel(low_ref, gate_ref, up_ref, down_ref):
    step = pl.program_id(0)
    hidden = gate_ref.shape[2]
    value = low_ref[0].astype(F32)
    half = value.shape[0]
    for place, ref in ((0, gate_ref), (1, up_ref)):

        @pl.when(step // 2 == place)
        def _():
            ref[0, :half] = value[:, :hidden]
            ref[0, half:] = value[:, hidden:]

    @pl.when(step // 2 == 2)
    def _():
        down_ref[0] = value


def widen(low):
    count, hidden, width = low.shape
    per_owner = count // 3

    def spot(place):
        return lambda i: (jnp.clip(i - place * per_owner, 0, per_owner - 1), 0, 0)

    return pl.pallas_call(
        widen_kernel,
        grid=(count,),
        out_shape=[shape((per_owner, width, hidden), F32)] * 2 + [shape((per_owner, hidden, width), F32)],
        in_specs=[pl.BlockSpec((1, hidden, width), lambda i: (i, 0, 0))],
        out_specs=[
            pl.BlockSpec((1, width, hidden), spot(0)),
            pl.BlockSpec((1, width, hidden), spot(1)),
            pl.BlockSpec((1, hidden, width), spot(2)),
        ],
        compiler_params=pltpu.CompilerParams(vmem_limit_bytes=63 * 1024 * 1024),
        cost_estimate=pl.CostEstimate(flops=0, bytes_accessed=24_000_000, transcendentals=0),
        name="widen",
    )(low)


def outputs_kernel(active, share, down_ref, sent_ref, tick_ref, out_ref, out_sem, *, wait):
    tick_ref[...] = jnp.zeros(tick_ref.shape, F32)
    per_owner, count, hidden = active.shape
    owners, _, capacity, width = sent_ref.shape
    group = 8
    size = group * capacity
    copies = []
    for i in range(3):
        wait(i)
    for k in range(per_owner):
        for part in range(owners // group):
            span = slice(part * size, (part + 1) * size)
            blocks = slice(part * group, (part + 1) * group)
            produced = dot(active[k, span], down_ref[k]).astype(BF16).astype(F32)
            produced = (produced * share[k, span, :1]).astype(BF16)
            out_ref[blocks, k] = produced.reshape(group, capacity, width)
            copies.append(
                pltpu.make_async_copy(
                    out_ref.at[blocks, k], sent_ref.at[blocks, k], out_sem.at[k * (owners // group) + part]
                )
            )
            copies[-1].start()
    for copy in copies:
        copy.wait()


def expert_outputs(active, share, down, owners, after=()):
    per_owner, count, hidden = active.shape
    width = down.shape[2]
    sent = ((owners, per_owner, count // owners, width), BF16)
    return kernel_call(
        outputs_kernel,
        "expert_outputs",
        0.1,
        [active, share, down],
        [sent, ((8, 128), F32)],
        out_hbm=(0,),
        after=after,
        scratch=[pltpu.VMEM(*sent), pltpu.SemaphoreType.DMA((per_owner * (owners // 8),))],
        late=(0, 1, 2),
    )


def combined(rows_hbm, rows_ref, sems, turn_ref, ready):
    owners, per_owner, capacity, wide = rows_hbm.shape
    group = owners // 4
    size = group * per_owner * capacity
    loads = []
    for part in range(4):
        blocks = slice(part * group, (part + 1) * group)
        loads.append(pltpu.make_async_copy(rows_hbm.at[blocks], rows_ref.at[blocks], sems.at[part]))
        loads[-1].start()
    ready()
    total = None
    for part in range(4):
        loads[part].wait()
        rows = rows_ref[part * group : (part + 1) * group].reshape(size, wide)
        one = dot(turn_ref[:, part * size : (part + 1) * size], rows)
        total = one if total is None else total + one
    return total


def output_kernel(rows_hbm, turn_ref, middle_ref, out_ref, tick_ref, rows_ref, sems, *, wait, store):
    tick_ref[...] = jnp.zeros(tick_ref.shape, F32)
    total = combined(rows_hbm, rows_ref, sems, turn_ref, lambda: wait(1))
    wait(2)
    out_ref[...] = (middle_ref[...] + total).astype(BF16)


def layer_output(rows, turn, middle):
    return kernel_call(
        output_kernel,
        "layer_output",
        3,
        [rows, turn, middle],
        [(middle.shape, BF16), ((8, 128), F32)],
        hbm=(0,),
        scratch=[pltpu.VMEM(rows.shape, BF16), pltpu.SemaphoreType.DMA((4,))],
        late=(1, 2),
        stored=(0,),
    )


def router_kernel(
    rows_hbm,
    turn_ref,
    middle_ref,
    probs_ref,
    mask_ref,
    gains_ref,
    c_ref,
    hidden_ref,
    grad_ref,
    send_ref,
    extra_ref,
    rows_ref,
    sems,
    *,
    experts,
    wait,
    store,
):
    rows, width = middle_ref.shape
    returned = combined(rows_hbm, rows_ref, sems, turn_ref, lambda: wait(1))
    for i in (2, 4, 6, 7):
        wait(i)
    tail = returned[:, width:].T
    route_grad = tail[:experts] + tail[experts : 2 * experts]
    mask = mask_ref[...]
    probs = probs_ref[...]
    picked = probs * mask
    picked_sum = jnp.sum(picked, axis=0, keepdims=True)
    share = picked / picked_sum
    picked_grad = (route_grad - jnp.sum(route_grad * share, axis=0, keepdims=True)) / picked_sum
    prob_grad = mask * picked_grad
    logit_grad = probs * (prob_grad - jnp.sum(probs * prob_grad, axis=0, keepdims=True))
    extra_ref[:experts] = dot(logit_grad.astype(BF16), hidden_ref[...])
    logit_rows = jnp.concatenate([logit_grad, jnp.zeros((128 - experts, rows), F32)], axis=0).T
    router = gains_ref[:experts].astype(BF16)
    hidden_grad = returned[:, :width] + dot(logit_rows[:, :experts].astype(BF16), router)
    middle = middle_ref[...]
    scale = lax.rsqrt(jnp.mean(middle * middle, axis=1, keepdims=True) + EPSILON)
    normed = middle * scale
    extra_ref[experts : experts + 8] = jnp.broadcast_to(
        jnp.sum(hidden_grad * normed, axis=0, keepdims=True), (8, width)
    )
    inner = hidden_grad * gains_ref[experts + 1 : experts + 2]
    grad = c_ref[...].astype(F32) + scale * (
        inner - normed * jnp.mean(inner * normed, axis=1, keepdims=True)
    )
    grad_ref[...] = grad
    send_ref[...] = grad.astype(BF16)


def router_backward(rows_back, turn, middle, probs, mask, gains, c, hidden, experts, after=()):
    rows, width = middle.shape
    return kernel_call(
        functools.partial(router_kernel, experts=experts),
        "router_backward",
        5,
        [rows_back, turn, middle, probs, mask, gains, c, hidden],
        [((rows, width), F32), ((rows, width), BF16), ((experts + 8, width), F32)],
        hbm=(0,),
        after=after,
        scratch=[pltpu.VMEM(rows_back.shape, BF16), pltpu.SemaphoreType.DMA((4,))],
        late=(1, 2, 4, 6, 7),
        stored=(0,),
    )


def pair_kernel(keep_ref, other_ref, total_ref, *sends):
    for flip in range(4):
        total = keep_ref[flip] + other_ref[flip].astype(F32)
        if flip:
            sends[flip - 1][...] = total.astype(BF16)
        else:
            total_ref[...] = total


def pair_sum(keep, other):
    rows, width = keep.shape[1:]
    return kernel_call(
        pair_kernel, "pair_sum", 1.2, [keep, other], [((rows, width), F32)] + [((rows, width), BF16)] * 3
    )


def input_kernel(total_ref, *refs, experts, store):
    came = refs[:3]
    x_ref, gains_ref, middle_grad_ref, out_ref = refs[3:]
    total = total_ref[...]
    for piece in came:
        total = total + piece[...].astype(F32)
    x = x_ref[...].astype(F32)
    scale = lax.rsqrt(jnp.mean(x * x, axis=1, keepdims=True) + EPSILON)
    normed = x * scale
    inner = total * gains_ref[experts : experts + 1]
    out_ref[...] = middle_grad_ref[...] + scale * (
        inner - normed * jnp.mean(inner * normed, axis=1, keepdims=True)
    )


def input_grad(total, came, x, gains, middle_grad, experts):
    return kernel_call(
        functools.partial(input_kernel, experts=experts),
        "input_grad",
        2,
        [total, *came, x, gains, middle_grad],
        [(middle_grad.shape, F32)],
        held=(4, 6),
        stored=(0,),
    )[0]


PIECE, SPARE, SLICE = 16, 3, 64


def passed(value, after):
    results = [(value.shape, value.dtype)]
    return move_call(lambda *refs: [refs], "passed", 0.5, [value], results, after, 63)[0]


def shares_kernel(pieces_ref, out_ref, rest_ref):
    total = pieces_ref[0].astype(F32)
    for i in range(1, pieces_ref.shape[0]):
        total = total + pieces_ref[i].astype(F32)
    base = 8 * PIECE
    fill = jnp.zeros((PIECE - SPARE, 128), F32)
    for part in range(8):
        out_ref[part, :PIECE] = total[part * PIECE : (part + 1) * PIECE].astype(BF16)
        spare = total[base + part * SPARE : base + (part + 1) * SPARE]
        out_ref[part, PIECE:] = jnp.concatenate([spare, fill], axis=0).astype(BF16)
    rest_ref[...] = total[base + 2 * PIECE :].astype(BF16)


def shares_sum(pieces, after=()):
    return kernel_call(
        shares_kernel,
        "shares_sum",
        0.1,
        [pieces],
        [((8, 2 * PIECE, 128), BF16), ((SLICE, 128), BF16)],
        after=after,
    )


def whole_kernel(came_ref, rest_ref, out_ref):
    spare = came_ref[0, PIECE:].astype(F32)
    for i in range(1, 8):
        spare = spare + came_ref[i, PIECE:].astype(F32)
    rows = [came_ref[i, :PIECE] for i in range(8)] + [spare.astype(BF16), rest_ref[...]]
    rows = jnp.concatenate(rows, axis=0)
    for i in range(16):
        out_ref[i] = rows


def whole_pieces(came, rest, after=()):
    return kernel_call(
        whole_kernel,
        "whole_pieces",
        0.1,
        [came, rest],
        [((16, 9 * PIECE + SLICE, 128), BF16)],
        after=after,
    )[0]


def final_kernel(pieces_ref, wq_ref, wk_ref, wv_ref, gain_ref, *outs, experts):
    query_ref, key_ref, value_ref, output_ref, one_ref, two_ref, qg_ref, kg_ref, router_ref = outs
    rows = pieces_ref.shape[2]
    q_columns = query_ref.shape[1] // 8
    kv_columns = key_ref.shape[1] // 8
    sums = jnp.zeros((rows, 1), F32)
    base = 8 * PIECE
    for pair in range(4):
        keys, values = [], []
        for source in (2 * pair, 2 * pair + 1):
            block = [pieces_ref[i, source * PIECE : (source + 1) * PIECE] for i in range(16)]
            turned = jnp.concatenate(block, axis=0).astype(F32).T
            span = slice(source * q_columns, (source + 1) * q_columns)
            query = turned[:, :q_columns]
            query_ref[:, span] = query
            sums = sums + jnp.sum(query * wq_ref[:, span].astype(F32), axis=1, keepdims=True)
            keys.append(turned[:, q_columns : q_columns + kv_columns])
            values.append(turned[:, q_columns + kv_columns :])
        span = slice(2 * pair * kv_columns, 2 * (pair + 1) * kv_columns)
        for parts, ref, weight in ((keys, key_ref, wk_ref), (values, value_ref, wv_ref)):
            both = jnp.concatenate(parts, axis=1)
            ref[:, span] = both
            sums = sums + jnp.sum(both * weight[:, span].astype(F32), axis=1, keepdims=True)
    for i in range(16):
        half = i % 2 * SLICE
        output_ref[half : half + SLICE, i // 2 * rows : (i // 2 + 1) * rows] = pieces_ref[
            i, base + PIECE :
        ].astype(F32)
    spare = pieces_ref[:, base : base + PIECE].astype(F32)
    spare = jnp.concatenate([spare[i, :SPARE] for i in range(16)], axis=0)
    one_ref[...] = jnp.broadcast_to(sums, (rows, 128)).T[:1] / gain_ref[...].astype(F32)
    two_ref[...] = spare[experts : experts + 1]
    step = qg_ref.shape[1]
    qg_ref[...] = spare[experts + 1 : experts + 2, :step]
    kg_ref[...] = spare[experts + 2 : experts + 3, :step]
    router_ref[...] = spare[:experts]


def final_grads(pieces, wq, wk, wv, gain, experts):
    rows = pieces.shape[2]
    return kernel_call(
        functools.partial(final_kernel, experts=experts),
        "final_grads",
        0.2,
        [pieces, wq, wk, wv, gain],
        [
            (wq.shape, F32),
            (wk.shape, F32),
            (wv.shape, F32),
            ((rows, 8 * rows), F32),
            ((1, rows), F32),
            ((1, rows), F32),
            ((1, HEAD // 8), F32),
            ((1, HEAD // 8), F32),
            ((experts, rows), F32),
        ],
        held=(1, 2, 3, 4),
    )


def send(values, axis, flip):
    count = lax.axis_size(axis)
    return lax.ppermute(values, axis, [(i, i ^ flip) for i in range(count)])


def along_z(values):
    if not isinstance(values, (list, tuple)):
        values = [values] * 3
    return [send(value, "fsdp", 2 * (i + 1)) for i, value in enumerate(values)]


def gather_fsdp(block, name):
    came = along_z(block)
    return came, send(row([block, *came], name), "fsdp", 1)


def exchange(rows):
    return lax.all_to_all(rows, "expert", 0, 0, tiled=True)


def shards(
    tokens,
    lengths,
    routes,
    first_gain,
    query_weight,
    key_weight,
    value_weight,
    output_weight,
    query_gain,
    key_gain,
    second_gain,
    router_weight,
    gate_weight,
    up_weight,
    down_weight,
    cotangent,
):
    own = tokens[0]
    upstream = cotangent[0]
    rows, width = own.shape
    fsdp = lax.axis_size("fsdp")
    owners = lax.axis_size("expert")
    me = lax.axis_index("fsdp").astype(jnp.int32).reshape(1)
    owner = lax.axis_index("expert").astype(jnp.int32).reshape(1)
    experts = router_weight.shape[1]
    capacity = 3 * rows * routes.shape[2] // (2 * experts)
    kv_columns = key_weight.shape[1] // fsdp
    q_columns = query_weight.shape[1] // fsdp
    columns = q_columns + 2 * kv_columns
    q_heads = q_columns // HEAD

    ends = jnp.cumsum(lengths[0])
    place = jnp.arange(rows * fsdp, dtype=jnp.int32)
    start = jnp.max(jnp.where(ends[:, None] <= place[None, :], ends[:, None], 0), axis=0)
    position = (place - start).astype(F32)
    frequency = ROPE_BASE ** (-jnp.arange(HEAD // 2, dtype=F32) * 2.0 / HEAD)
    angles = frequency[:, None] * position[None, :]
    cosine, sine = jnp.cos(angles), jnp.sin(angles)
    start = start[None, :].astype(jnp.int32)

    packed, x_sends, dressed, mask = pack_weights(
        me,
        own,
        query_weight,
        key_weight,
        value_weight,
        router_weight.T,
        first_gain[None],
        second_gain[None],
        query_gain[None],
        key_gain[None],
        routes[0].T,
        upstream,
    )
    x_came = along_z(x_sends)
    x_other = [send(own, "fsdp", 1), send(packed[1], "fsdp", 1)]
    deal, turn = slot_tables(mask, capacity)
    ready = (*x_other, deal, cosine, sine, start)
    x_other.append(send(relay(x_came, rows * fsdp, after=ready), "fsdp", 1))
    c_all = lax.all_gather(dressed, "expert", axis=0)
    wo_came = along_z(output_weight)

    h1, pre, keep, give, inverse, gains, heads, turned, mixed = attention_forward(
        me, own, packed[0], x_came, x_other, cosine, sine, start, experts, q_heads
    )
    other = send(give, "fsdp", 1)
    mixed_sends, wo_stack = merge(keep, other, output_weight, wo_came)
    mixed_came = along_z(mixed_sends)
    wo_other = send(wo_stack, "fsdp", 1)
    middle, probs, hidden, sent = middle_layer(
        own, keep, other, mixed_came, output_weight, wo_came, wo_other, gains, deal, experts, owners
    )
    h_rows = exchange(sent)
    rows_c, row_mask, back = deal_rows(owner, c_all, down_weight, experts, capacity)
    rows_back, gate_low, up_low, active, weighted, share = expert_layer(
        owner, h_rows, gains, row_mask, back, gate_weight, up_weight, experts
    )
    came_back = exchange(rows_back)
    grads, tick = expert_weights(h_rows, rows_c, gate_low, up_low, weighted)
    grads = lax.psum(grads, "fsdp")
    gate_sum, up_sum, down_sum = widen(grads)
    sent, tick = expert_outputs(active, share, down_weight, owners, after=(tick,))

    middle_grad, middle_low, extra = router_backward(
        came_back, turn, middle, probs, mask, gains, upstream, hidden, experts, after=(tick,)
    )
    da_came, da_other = gather_fsdp(middle_low, "row_middle")
    out_rows = exchange(sent)
    layer_out, _ = layer_output(out_rows, turn, middle)
    first, dh_keep, dh_give = attention_backward(
        me,
        middle_low,
        da_came,
        da_other,
        heads,
        output_weight,
        cosine,
        sine,
        start,
        h1,
        pre,
        mixed,
        inverse,
        turned,
        extra,
        experts,
        q_heads,
    )
    dh_total, *dh_sends = pair_sum(dh_keep, send(dh_give, "fsdp", 1))
    dh_came = along_z(dh_sends)
    tokens_grad = input_grad(dh_total, dh_came, own, gains, middle_grad, experts)
    first = passed(first, after=(out_rows, grads))
    parted, rest = shares_sum(exchange(first), after=(dh_total, down_sum))
    parted = lax.all_to_all(parted, "fsdp", 0, 0, tiled=True)
    pieces = exchange(whole_pieces(parted, rest, after=(layer_out,)))
    query_sum, key_sum, value_sum, output_sum, one_sum, two_sum, *gain_sums, router_sum = final_grads(
        pieces, query_weight, key_weight, value_weight, first_gain[None], experts
    )
    return (
        layer_out[None],
        tokens_grad[None],
        one_sum[0],
        query_sum,
        key_sum,
        value_sum,
        output_sum,
        gain_sums[0][0],
        gain_sums[1][0],
        two_sum[0],
        router_sum.T,
        gate_sum,
        up_sum,
        down_sum,
    )


def solution(mesh):
    whole = P("expert", "fsdp", None)
    rows = P("fsdp", None)
    vector = P("fsdp")
    owned = P("expert", None, None)
    return jax.shard_map(
        shards,
        mesh=mesh,
        in_specs=(
            whole,
            P("expert", None),
            whole,
            vector,
            rows,
            rows,
            rows,
            rows,
            vector,
            vector,
            vector,
            rows,
            owned,
            owned,
            owned,
            whole,
        ),
        out_specs=(
            whole,
            whole,
            vector,
            rows,
            rows,
            rows,
            rows,
            vector,
            vector,
            vector,
            rows,
            owned,
            owned,
            owned,
        ),
        check_vma=False,
    )
```

```python
import functools

import jax
import jax.numpy as jnp
from jax import lax
from jax.experimental import pallas as pl
from jax.experimental.pallas import tpu as pltpu
from jax.sharding import PartitionSpec as P

EPSILON = 1e-06
ROPE_BASE = 10000.0
HEAD = 64
TILE = 256
F32 = jnp.float32
BF16 = jnp.bfloat16
VMEM = pl.BlockSpec(memory_space=pltpu.VMEM)
SMEM = pl.BlockSpec(memory_space=pltpu.SMEM)
ANY = pl.BlockSpec(memory_space=pl.ANY)
HBM = pl.BlockSpec(memory_space=pltpu.HBM)


def dot(left, right, dims=((1,), (0,))):
    return lax.dot_general(left, right, (dims, ((), ())), preferred_element_type=F32)


def shape(extent, dtype):
    return jax.ShapeDtypeStruct(extent, dtype)


def kernel_call(
    body, name, micros, operands, results, smem=0, hbm=(), out_hbm=(), after=(), scratch=(), held=(), late=(), stored=(), mib=63
):
    held = tuple(held) + tuple(late)
    n, a, r, s = len(operands), len(after), len(results), len(scratch)
    specs = [SMEM if i < smem else HBM if i in held or i in hbm else VMEM for i in range(n)]
    out_specs = [HBM if i in stored or i in out_hbm else VMEM for i in range(r)]
    staged = [pltpu.VMEM(operands[i].shape, operands[i].dtype) for i in held]
    staged += [pltpu.VMEM(*results[i]) for i in stored]
    sems = [pltpu.SemaphoreType.DMA((max(len(held), 1),)), pltpu.SemaphoreType.DMA((max(len(stored), 1),))]

    def wrapped(*refs):
        ins, outs = list(refs[:n]), list(refs[n + a : n + a + r])
        own = refs[n + a + r : n + a + r + s]
        stages, (load_sem, store_sem) = refs[n + a + r + s : -2], refs[-2:]
        loads, stores, begun = {}, {}, []
        for k, i in enumerate(held):
            loads[i] = pltpu.make_async_copy(ins[i], stages[k], load_sem.at[k])
            loads[i].start()
            ins[i] = stages[k]
        for k, i in enumerate(stored):
            stores[i] = pltpu.make_async_copy(stages[len(held) + k], outs[i], store_sem.at[k])
            outs[i] = stages[len(held) + k]
        for i in held:
            if i not in late:
                loads[i].wait()

        def store(*which):
            for i in which:
                stores[i].start()
                begun.append(i)

        extra = {}
        if late:
            extra["wait"] = lambda i: loads[i].wait()
        if stored:
            extra["store"] = store
        body(*ins, *outs, *own, **extra)
        store(*[i for i in stored if i not in begun])
        for i in stored:
            stores[i].wait()

    return pl.pallas_call(
        wrapped,
        out_shape=[shape(*result) for result in results],
        in_specs=specs + [ANY] * a,
        out_specs=out_specs,
        scratch_shapes=list(scratch) + staged + sems,
        compiler_params=pltpu.CompilerParams(vmem_limit_bytes=mib * 1024 * 1024),
        cost_estimate=pl.CostEstimate(flops=0, bytes_accessed=int(micros * 3.6e6), transcendentals=0),
        name=name,
    )(*operands, *after)


def move_call(moves, name, micros, operands, results, after=(), mib=10):
    def body(*refs):
        for source, target in moves(*refs):
            target[...] = source[...]

    return kernel_call(body, name, micros, operands, results, after=after, mib=mib)


def lane_blocks(value):
    return jnp.concatenate([value[:, i : i + 128] for i in range(0, value.shape[1], 128)], axis=0)


def joined_lanes(value, count):
    rows = value.shape[0] // count
    return jnp.concatenate([value[i * rows : (i + 1) * rows] for i in range(count)], axis=1)


def softmax_rows(logits):
    powers = jnp.exp(logits - jnp.max(logits, axis=0, keepdims=True))
    return powers / jnp.sum(powers, axis=0, keepdims=True)


def head_forward(pre, gain, cosine, sine):
    scale = lax.rsqrt(jnp.mean(pre * pre, axis=0, keepdims=True) + EPSILON)
    normed = pre * scale
    scaled = normed * gain
    a, b = scaled[: HEAD // 2], scaled[HEAD // 2 :]
    turned = jnp.concatenate([a * cosine - b * sine, b * cosine + a * sine], axis=0)
    return turned, normed, scale


def head_backward(grad, normed, scale, gain, cosine, sine):
    a, b = grad[: HEAD // 2], grad[HEAD // 2 :]
    unturned = jnp.concatenate([a * cosine + b * sine, b * cosine - a * sine], axis=0)
    gain_grad = jnp.sum(unturned * normed, axis=1, keepdims=True)
    inner = unturned * gain
    pre_grad = scale * (inner - normed * jnp.mean(inner * normed, axis=0, keepdims=True))
    return pre_grad, gain_grad


def slots_kernel(mask_ref, deal_ref, turn_ref, whole_ref, *, capacity, owners, store):
    experts, rows = mask_ref.shape
    mask = mask_ref[...]
    ranks = dot(mask.astype(BF16), earlier(rows))
    slot = lax.broadcasted_iota(jnp.int32, (capacity, rows), 0).astype(F32) + 1.0
    for expert in range(experts):
        one = slice(expert, expert + 1)
        per_owner = experts // owners
        place = (expert % per_owner * owners + expert // per_owner) * capacity
        whole_ref[place : place + capacity] = jnp.where((ranks[one] == slot) & (mask[one] > 0.5), 1.0, 0.0)
    deal_ref[...] = whole_ref[...].astype(BF16)
    store(0)
    for part in range(0, experts * capacity, 128):
        turn_ref[:, part : part + 128] = whole_ref[part : part + 128].T.astype(BF16)


def slot_tables(mask, capacity, owners):
    experts, rows = mask.shape
    slots = experts * capacity
    return kernel_call(
        functools.partial(slots_kernel, capacity=capacity, owners=owners),
        "slot_tables",
        2.0,
        [mask],
        [((slots, rows), BF16), ((rows, slots), BF16)],
        scratch=[pltpu.VMEM((slots, rows), F32)],
        stored=(0, 1),
    )


def earlier(rows):
    return (
        lax.broadcasted_iota(jnp.int32, (rows, rows), 0)
        <= lax.broadcasted_iota(jnp.int32, (rows, rows), 1)
    ).astype(BF16)


def pack_kernel(
    me_ref, x_ref, wq_ref, wk_ref, wv_ref, router_ref, one_ref, two_ref, qg_ref, kg_ref, routes_ref, c_ref, *outs, wait, store
):
    own_ref, sends, dressed_ref, mask_ref, other_ref, parts_ref = outs[0], outs[1:4], *outs[4:]
    experts, rows = router_ref.shape
    wide = wq_ref.shape[1] // 8
    narrow = wk_ref.shape[1] // 8
    count = qg_ref.shape[1]
    heads = jnp.concatenate([qg_ref[...], kg_ref[...]], axis=0).astype(F32)
    heads = jnp.concatenate([heads, jnp.zeros((2, 128 - count), F32)], axis=1)
    heads = jnp.concatenate([heads, jnp.zeros((126, 128), F32)], axis=0).T[:count]
    small = jnp.concatenate(
        [
            router_ref[...].astype(F32),
            one_ref[...].astype(F32),
            two_ref[...].astype(F32),
            jnp.zeros((6, 128), F32),
            heads,
        ],
        axis=0,
    ).astype(BF16)
    for part in range(8):
        parts_ref[part, :wide] = wq_ref[:, part * wide : (part + 1) * wide].astype(F32).T.astype(BF16)
        parts_ref[part, wide + 2 * narrow :] = small
    for pair in range(4):
        span = slice(pair * 128, (pair + 1) * 128)
        for ref, place in ((wk_ref, wide), (wv_ref, wide + narrow)):
            turned = ref[:, span].astype(F32).T.astype(BF16)
            parts_ref[2 * pair, place : place + narrow] = turned[:narrow]
            parts_ref[2 * pair + 1, place : place + narrow] = turned[narrow:]
    me = me_ref[0]
    tall = parts_ref.shape[1]
    blocks = lane_blocks(x_ref[...])
    base = blocks.shape[0]
    own_ref[...] = parts_ref[me]
    other_ref[...] = parts_ref[me ^ 1]
    for flip in range(1, 4):
        sends[flip - 1][:base] = blocks
        sends[flip - 1][base : base + tall] = parts_ref[me ^ (2 * flip)]
        sends[flip - 1][base + tall :] = parts_ref[me ^ (2 * flip + 1)]
    store(1, 2, 3, 6, 0)
    wait(10)
    wait(11)
    width = c_ref.shape[1]
    subs = lax.broadcasted_iota(jnp.int32, (128, rows), 0)
    routed = jnp.zeros((128, rows), F32)
    for route in range(routes_ref.shape[0]):
        routed = routed + jnp.where(routes_ref[route : route + 1] == subs, 1.0, 0.0)
    dressed_ref[:, :width] = c_ref[...]
    dressed_ref[:, width:] = routed.T.astype(BF16)
    mask_ref[...] = routed[:experts]


def pack_weights(me, x, wq, wk, wv, router, one, two, qg, kg, routes, c):
    experts = router.shape[0]
    tall = (wq.shape[1] + wk.shape[1] + wv.shape[1]) // 8 + experts + 16
    rows, width = x.shape
    base = rows * 8
    own, first, second, third, dressed, mask, other = kernel_call(
        pack_kernel,
        "pack_weights",
        2.5,
        [me, x, wq, wk, wv, router, one, two, qg, kg, routes, c],
        [((tall, 128), BF16)]
        + [((base + 2 * tall, 128), BF16)] * 3
        + [((rows, width + 128), BF16), ((experts, rows), F32), ((tall, 128), BF16)],
        smem=1,
        scratch=[pltpu.VMEM((8, tall, 128), BF16)],
        held=range(1, 10),
        late=(10, 11),
        stored=(0, 1, 2, 3, 4, 5, 6),
    )
    return (own, other), [first, second, third], dressed, mask


def relay(came, base, after):
    tall = (came[0].shape[0] - base) // 2

    def moves(*refs):
        pairs = []
        for flip, ref in enumerate(refs[:3]):
            pairs.append((ref.at[:base], refs[3].at[flip, :base]))
            pairs.append((ref.at[base + tall :], refs[3].at[flip, base:]))
        return pairs

    return move_call(moves, "relay", 1.5, came, [((3, base + tall, 128), BF16)], after)[0]


def forward_kernel(me_ref, x_ref, own_ref, *refs, experts, q_heads, store):
    came, other_x, other_w, other_ref = refs[:3], refs[3], refs[4], refs[5]
    cos_ref, sin_ref, start_ref = refs[6:9]
    h1_ref, pre_ref, keep_ref, give_ref, inverse_ref, gains_ref, heads_ref, turned_ref, out_ref = refs[-9:]
    rows, width = x_ref.shape
    q_columns = q_heads * HEAD
    columns = q_columns + 2 * HEAD
    total = rows * 8
    tall = own_ref.shape[0]
    base = 8 * rows
    me = me_ref[0]
    for slot in range(8):
        flip = slot // 2
        if slot % 2:
            piece = other_ref[flip - 1, base:] if flip else other_w[...]
        elif flip:
            piece = came[flip - 1][base : base + tall]
        else:
            piece = own_ref[...]
        span = pl.ds(pl.multiple_of((me ^ slot) * rows, rows), rows)
        turned_ref[:, span] = piece[:columns]
        small = piece[columns:].astype(F32)
        gains_ref[:, span] = small[: experts + 8]
        heads_ref[pl.ds(pl.multiple_of((me ^ slot) * 8, 8), 8)] = small[experts + 8 :]
    gain_one = gains_ref[experts : experts + 1]
    for slot in range(8):
        flip = slot // 2
        if slot % 2:
            x = joined_lanes(other_ref[flip - 1, :base], 8) if flip else other_x[...]
        elif flip:
            x = joined_lanes(came[flip - 1][:base], 8)
        else:
            x = x_ref[...]
        x = x.astype(F32)
        scale = lax.rsqrt(jnp.mean(x * x, axis=1, keepdims=True) + EPSILON)
        h1_ref[slot] = (x * scale * gain_one).astype(BF16)
    store(0, 6, 7)
    for slot in range(8):
        block = dot(turned_ref[...], h1_ref[slot], ((1,), (1,)))
        place = pl.multiple_of((me ^ slot) * rows, rows)
        pre_ref[:, pl.ds(place, rows)] = block
    store(1)
    cosine, sine = cos_ref[...], sin_ref[...]
    gain_query, gain_key = heads_ref[:, :1], heads_ref[:, 1:2]
    key = head_forward(pre_ref[q_columns : q_columns + HEAD], gain_key, cosine, sine)[0]
    key = key.T.astype(BF16)
    value = pre_ref[q_columns + HEAD :].astype(BF16)
    inverse_ref[...] = jnp.zeros(inverse_ref.shape, F32)
    for head in range(q_heads):
        query = head_forward(pre_ref[head * HEAD : (head + 1) * HEAD], gain_query, cosine, sine)[0]
        query = query.astype(BF16) * jnp.array(HEAD ** (-0.5), BF16)
        for tile in range(total // TILE):
            low, high = tile * TILE, (tile + 1) * TILE
            scores = dot(key[:high], query[:, low:high])
            u = lax.broadcasted_iota(jnp.int32, (high, TILE), 0)
            t = lax.broadcasted_iota(jnp.int32, (high, TILE), 1) + low
            allowed = (u >= start_ref[:, low:high]) & (u <= t)
            powers = jnp.where(allowed, jnp.exp(scores), 0.0)
            inverse = 1.0 / jnp.sum(powers, axis=0, keepdims=True)
            probs = (powers * inverse).astype(BF16)
            mixed = dot(value[:, :high], probs).astype(BF16)
            inverse_ref[head : head + 1, low:high] = inverse
            for part in range(TILE // rows):
                out_ref[low // rows + part, head * HEAD : (head + 1) * HEAD] = mixed[
                    :, part * rows : (part + 1) * rows
                ]
    for slot in range(8):
        (give_ref if slot % 2 else keep_ref)[slot // 2] = out_ref[me ^ slot]


def attention_forward(me, x, own, came, other, cosine, sine, start, experts, q_heads, after=()):
    rows, width = x.shape
    total = 8 * rows
    columns = (q_heads + 2) * HEAD
    q_columns = q_heads * HEAD
    return kernel_call(
        functools.partial(forward_kernel, experts=experts, q_heads=q_heads),
        "attention_forward",
        7.0,
        [me, x, own, *came, *other, cosine, sine, start],
        [
            ((8, rows, width), BF16),
            ((columns, total), F32),
            ((4, q_columns, rows), BF16),
            ((4, q_columns, rows), BF16),
            ((8, total), F32),
            ((experts + 8, width), F32),
            ((HEAD, 128), F32),
            ((columns, width), BF16),
            ((8, q_columns, rows), BF16),
        ],
        smem=1,
        after=after,
        held=(1,),
        stored=(0, 1, 4, 6, 7, 8),
    )


def merge(keep, came, wo, wo_came):
    def moves(keep_ref, came_ref, *refs):
        weights, outs, stacked = refs[:4], refs[4:7], refs[7]
        pairs = [(weight, stacked.at[i]) for i, weight in enumerate(weights)]
        for flip in range(1, 4):
            pairs.append((keep_ref.at[flip], outs[flip - 1].at[0]))
            pairs.append((came_ref.at[flip], outs[flip - 1].at[1]))
        return pairs

    extent = ((2,) + keep.shape[1:], BF16)
    results = [extent] * 3 + [((4,) + wo.shape, BF16)]
    *sends, stacked = move_call(moves, "merge", 1.0, [keep, came, wo, *wo_came], results)
    return sends, stacked


def middle_kernel(x_ref, keep_ref, other_ref, *refs, experts, wait, store):
    came, wo_ref, wo_came, wo_other_ref, gains_ref, deal_ref = refs[:3], refs[3], refs[4:7], refs[7], refs[8], refs[9]
    middle_ref, probs_ref, hidden_ref, *sent, mixed_ref, whole_ref, out_ref, out_sem = refs[10:]
    rows, width = x_ref.shape
    for slot in range(8):
        flip, core = slot // 2, slot % 2
        if flip:
            piece = came[flip - 1][core]
        else:
            piece = (other_ref if core else keep_ref)[0]
        span = slice(slot * 128, (slot + 1) * 128)
        mixed_ref[:, span] = piece.astype(F32).T.astype(BF16)
    for i in (6, 7, 8, 9, 10):
        wait(i)
    for slot in range(8):
        flip = slot // 2
        span = slice(slot * 128, (slot + 1) * 128)
        if slot % 2:
            whole_ref[span] = wo_other_ref[flip]
        else:
            whole_ref[span] = (wo_came[flip - 1] if flip else wo_ref)[...]
    wait(0)
    middle = x_ref[...].astype(F32) + dot(mixed_ref[...], whole_ref[...])
    middle_ref[...] = middle
    scale = lax.rsqrt(jnp.mean(middle * middle, axis=1, keepdims=True) + EPSILON)
    hidden = (middle * scale * gains_ref[experts + 1 : experts + 2]).astype(BF16)
    hidden_ref[...] = hidden
    probs_ref[...] = softmax_rows(dot(gains_ref[:experts].astype(BF16), hidden, ((1,), (1,))))
    store(0, 2)
    owners, capacity, _ = sent[0].shape
    group = owners // 2
    size = group * capacity
    copies = []
    wait(12)
    for k, target in enumerate(sent):
        for part in range(2):
            place = (2 * k + part) * size
            taken = dot(deal_ref[place : place + size], hidden).astype(BF16)
            blocks = slice(group * part, group * (part + 1))
            out_ref[k, blocks] = taken.reshape(group, capacity, width)
            copies.append(
                pltpu.make_async_copy(out_ref.at[k, blocks], target.at[blocks], out_sem.at[2 * k + part])
            )
            copies[-1].start()
    for copy in copies:
        copy.wait()


def middle_layer(x, keep, other, came, wo, wo_came, wo_other, gains, deal, experts, owners):
    rows, width = x.shape
    per_owner = experts // owners
    capacity = deal.shape[0] // experts
    sent = ((owners, capacity, width), BF16)
    return kernel_call(
        functools.partial(middle_kernel, experts=experts),
        "middle_layer",
        3.0,
        [x, keep, other, *came, wo, *wo_came, wo_other, gains, deal],
        [((rows, width), F32), ((experts, rows), F32), ((rows, width), BF16)] + [sent] * per_owner,
        out_hbm=range(3, 3 + per_owner),
        scratch=[
            pltpu.VMEM((rows, width), BF16),
            pltpu.VMEM((width, width), BF16),
            pltpu.VMEM((per_owner, *sent[0]), BF16),
            pltpu.SemaphoreType.DMA((2 * per_owner,)),
        ],
        late=(6, 7, 8, 9, 10, 0, 12),
        stored=(0, 2),
    )


def row(pieces, name, after=()):
    def moves(*refs):
        return [(ref, refs[-1].at[i]) for i, ref in enumerate(refs[:-1])]

    return move_call(moves, name, 1.0, pieces, [((len(pieces),) + pieces[0].shape, BF16)], after)[0]


def backward_kernel(me_ref, own_da_ref, *refs, experts, q_heads, wait):
    came, other_ref = refs[:3], refs[3]
    heads_ref, wo_ref, cos_ref, sin_ref, start_ref = refs[4:9]
    h1_ref, pre_ref, mixed_ref, inverse_ref, turned_ref, extra_ref = refs[9:15]
    first_ref, keep_ref, send_ref = refs[-10:-7]
    da_ref, mixed_grad_ref, dkey_ref, dvalue_ref, low_ref, out_slots_ref, grad_ref = refs[-7:]
    rows, width = own_da_ref.shape
    q_columns = q_heads * HEAD
    columns = q_columns + 2 * HEAD
    total = rows * 8
    me = me_ref[0]
    for slot in range(8):
        flip, core = slot // 2, slot % 2
        if core:
            piece = other_ref[flip]
        else:
            piece = (came[flip - 1] if flip else own_da_ref)[...]
        span = slice(slot * rows, (slot + 1) * rows)
        da_ref[span] = piece
        place = pl.multiple_of((me ^ slot) * rows, rows)
        mixed_grad_ref[:, pl.ds(place, rows)] = dot(wo_ref[...], piece, ((1,), (1,))).astype(BF16)
    wait(13)
    for slot in range(8):
        out_slots_ref[:, slot * rows : (slot + 1) * rows] = mixed_ref[me ^ slot]
    wo_grad = dot(out_slots_ref[...], da_ref[...]).astype(BF16)
    wo_grad = lane_blocks(wo_grad)
    wait(12)
    wait(14)
    gain_query, gain_key = heads_ref[:, :1], heads_ref[:, 1:2]
    cosine, sine = cos_ref[...], sin_ref[...]
    key_turned, key_normed, key_scale = head_forward(
        pre_ref[q_columns : q_columns + HEAD], gain_key, cosine, sine
    )
    key_low = key_turned.astype(BF16)
    key = key_turned.T.astype(BF16)
    value = pre_ref[q_columns + HEAD :].T.astype(BF16)
    dkey_ref[...] = jnp.zeros(dkey_ref.shape, F32)
    dvalue_ref[...] = jnp.zeros(dvalue_ref.shape, F32)
    gain_query_grad = jnp.zeros((HEAD, 1), F32)
    pieces = []
    for head in range(q_heads):
        span = slice(head * HEAD, (head + 1) * HEAD)
        turned, normed, scale = head_forward(pre_ref[span], gain_query, cosine, sine)
        query = turned.astype(BF16) * jnp.array(HEAD ** (-0.5), BF16)
        grads = []
        for tile in range(total // TILE):
            low, high = tile * TILE, (tile + 1) * TILE
            part = query[:, low:high]
            mixed_grad = mixed_grad_ref[span, low:high]
            scores = dot(key[:high], part)
            u = lax.broadcasted_iota(jnp.int32, (high, TILE), 0)
            t = lax.broadcasted_iota(jnp.int32, (high, TILE), 1) + low
            allowed = (u >= start_ref[:, low:high]) & (u <= t)
            probs = jnp.where(allowed, jnp.exp(scores) * inverse_ref[head : head + 1, low:high], 0.0)
            attend = dot(value[:high], mixed_grad)
            delta = jnp.sum(probs * attend, axis=0, keepdims=True)
            score_low = (probs * (attend - delta)).astype(BF16)
            grads.append(dot(key_low[:, :high], score_low))
            dkey_ref[:, :high] += dot(part, score_low, ((1,), (1,)))
            dvalue_ref[:, :high] += dot(mixed_grad, probs.astype(BF16), ((1,), (1,)))
        query_grad = jnp.concatenate(grads, axis=1) * HEAD ** (-0.5)
        pre_grad, gain_grad = head_backward(query_grad, normed, scale, gain_query, cosine, sine)
        gain_query_grad += gain_grad
        pieces.append(pre_grad)
    pre_grad, gain_key_grad = head_backward(
        dkey_ref[...], key_normed, key_scale, gain_key, cosine, sine
    )
    pieces += [pre_grad, dvalue_ref[...]]
    pre_grad = jnp.concatenate(pieces, axis=0)
    low_ref[...] = pre_grad.astype(BF16)
    slots_grad = []
    for slot in range(8):
        place = pl.multiple_of((me ^ slot) * rows, rows)
        slots_grad.append(low_ref[:, pl.ds(place, rows)])
    slots_grad = jnp.concatenate(slots_grad, axis=1)
    wait(11)
    wait(15)
    grad_ref[:columns] = dot(slots_grad, h1_ref[...].reshape(total, width))
    extra = extra_ref[...]
    lane = lax.broadcasted_iota(jnp.int32, (HEAD, 128), 1)
    gains = jnp.where(lane == 0, gain_query_grad, jnp.where(lane == 1, gain_key_grad, 0.0))
    gains = gains.T[:2]
    step = HEAD // 8
    grad_ref[columns:] = jnp.zeros((64, width), F32)
    grad_ref[columns : columns + experts + 1] = extra[: experts + 1]
    for part in range(8):
        grad_ref[columns + experts + 1 : columns + experts + 3, part * rows : part * rows + step] = gains[
            :, part * step : (part + 1) * step
        ]
    for piece in range(16):
        spare = []
        place = columns + piece * SPARE
        for part in range(8):
            span = slice(part * rows, (part + 1) * rows)
            block = grad_ref[piece * PIECE : (piece + 1) * PIECE, span]
            first_ref[piece, part * PIECE : (part + 1) * PIECE] = block.astype(BF16)
            spare.append(grad_ref[place : place + SPARE, span])
        spare.append(jnp.zeros((2 * PIECE - 8 * SPARE, 128), F32))
        first_ref[piece, 8 * PIECE : 10 * PIECE] = jnp.concatenate(spare, axis=0).astype(BF16)
        first_ref[piece, 10 * PIECE :] = wo_grad[piece * SLICE : (piece + 1) * SLICE]
    turned = turned_ref[...]
    for slot in range(8):
        low_rows_slot = slots_grad[:, slot * rows : (slot + 1) * rows].astype(F32).T.astype(BF16)
        part = dot(low_rows_slot, turned)
        if slot % 2:
            send_ref[slot // 2] = part.astype(BF16)
        else:
            keep_ref[slot // 2] = part


def attention_backward(
    me, da, came, other, heads, wo, cosine, sine, start, h1, pre, mixed, inverse, turned, extra, experts, q_heads, after=()
):
    rows, width = da.shape
    total = 8 * rows
    columns = pre.shape[0]
    q_columns = q_heads * HEAD
    return kernel_call(
        functools.partial(backward_kernel, experts=experts, q_heads=q_heads),
        "attention_backward",
        12,
        [me, da, *came, other, heads, wo, cosine, sine, start, h1, pre, mixed, inverse, turned, extra],
        [
            ((16, 10 * PIECE + SLICE, 128), BF16),
            ((4, rows, width), F32),
            ((4, rows, width), BF16),
        ],
        smem=1,
        after=after,
        held=(6, 7),
        late=(11, 12, 13, 14, 15),
        scratch=[
            pltpu.VMEM((total, width), BF16),
            pltpu.VMEM((q_columns, total), BF16),
            pltpu.VMEM((HEAD, total), F32),
            pltpu.VMEM((HEAD, total), F32),
            pltpu.VMEM((columns, total), BF16),
            pltpu.VMEM((q_columns, total), BF16),
            pltpu.VMEM((columns + 64, width), F32),
        ],
    )


def deal_kernel(owner_ref, c_ref, down_ref, rows_c, mask_ref, back_ref, c_scratch, sems, *, experts, capacity, wait, store):
    owner = owner_ref[0]
    per_owner, hidden, width = down_ref.shape
    rows = c_ref.shape[1]
    loads = [pltpu.make_async_copy(c_ref.at[i], c_scratch.at[i], sems.at[i]) for i in range(16)]
    for load in loads:
        load.start()
    lanes = lax.broadcasted_iota(jnp.int32, (experts, 128), 1)
    subs = lax.broadcasted_iota(jnp.int32, (experts, 128), 0)
    eye = (lanes == subs).astype(BF16)
    before = earlier(rows)
    mine_of = lax.broadcasted_iota(jnp.int32, (experts, rows), 0) - owner * per_owner
    slot = lax.broadcasted_iota(jnp.int32, (capacity, rows), 0).astype(F32) + 1.0
    for block in range(16):
        loads[block].wait()
        c = c_scratch[block]
        mask = dot(eye, c[:, width:], ((1,), (1,)))
        ranks = dot(mask.astype(BF16), before)
        deals = []
        for k in range(per_owner):
            mine = mine_of == k
            hit = jnp.sum(jnp.where(mine, mask, 0.0), axis=0, keepdims=True)
            rank = jnp.sum(jnp.where(mine, ranks, 0.0), axis=0, keepdims=True)
            deals.append(jnp.where((rank == slot) & (hit > 0.5), 1.0, 0.0))
        taken = dot(jnp.concatenate(deals, axis=0).astype(BF16), c).astype(BF16)
        span = slice(block * capacity, (block + 1) * capacity)
        for k in range(per_owner):
            spot = slice(k * capacity, (k + 1) * capacity)
            rows_c[k, span] = taken[spot, :width]
            mask_ref[k, span] = taken[spot, width:]
    store(0, 1)
    wait(2)
    for k in range(per_owner):
        for tile in range(16 * capacity // TILE):
            span = slice(tile * TILE, (tile + 1) * TILE)
            back_ref[k, span] = dot(rows_c[k, span], down_ref[k], ((1,), (1,)))


def deal_rows(owner, c, down, experts, capacity):
    per_owner, hidden, width = down.shape
    count = 16 * capacity
    return kernel_call(
        functools.partial(deal_kernel, experts=experts, capacity=capacity),
        "deal_rows",
        12.0,
        [owner, c, down],
        [
            ((per_owner, count, width), BF16),
            ((per_owner, count, 128), BF16),
            ((per_owner, count, hidden), F32),
        ],
        smem=1,
        hbm=(1,),
        scratch=[pltpu.VMEM(c.shape, BF16), pltpu.SemaphoreType.DMA((16,))],
        late=(2,),
        stored=(0, 1, 2),
    )


def expert_kernel(
    owner_ref,
    h_hbm,
    gains_ref,
    mask_hbm,
    back_hbm,
    gate_hbm,
    up_hbm,
    rows_hbm,
    gate_out,
    up_out,
    active_out,
    weighted_out,
    share_ref,
    h_ref,
    mask_ref,
    back_in,
    gate_ref,
    up_ref,
    rows_back,
    gate_sum,
    up_sum,
    logit_sum,
    spread_ref,
    load_sem,
    store_sem,
    *,
    experts,
    k,
    store,
):
    owners, capacity, width = h_hbm.shape
    group = owners // 2
    size = group * capacity
    pairs = [
        (h_hbm.at[:group], h_ref.at[:group]),
        (gate_hbm.at[k], gate_ref),
        (up_hbm.at[k], up_ref),
        (mask_hbm.at[k], mask_ref),
        (back_hbm.at[k], back_in),
        (h_hbm.at[group:], h_ref.at[group:]),
    ]
    loads = [pltpu.make_async_copy(*pair, load_sem.at[i]) for i, pair in enumerate(pairs)]
    for load in loads:
        load.start()
    place = owner_ref[0] * (experts // owners) + k
    router = jnp.concatenate([gains_ref[:experts], jnp.zeros((128 - experts, width), F32)], axis=0)
    router = router.astype(BF16)
    lane = lax.broadcasted_iota(jnp.int32, (capacity, 128), 1)

    def begin(part):
        h = h_ref[part * group : (part + 1) * group].reshape(size, width)
        gate_sum[part] = dot(h, gate_ref[...])
        up_sum[part] = dot(h, up_ref[...])
        logit_sum[part] = dot(h, router, ((1,), (1,)))

    for load in loads[:3]:
        load.wait()
    begin(0)
    for load in loads[3:]:
        load.wait()
    begin(1)
    copies = []
    for part in range(2):
        blocks = slice(part * group, (part + 1) * group)
        for spot in range(0, size, capacity):
            here = slice(part * size + spot, part * size + spot + capacity)
            near = slice(spot, spot + capacity)
            logits = logit_sum[part, near]
            chosen = mask_ref[here] > 0.5
            top = jnp.max(jnp.where(chosen, logits, -1e30), axis=1, keepdims=True)
            powers = jnp.where(chosen, jnp.exp(logits - top), 0.0)
            total = jnp.sum(powers, axis=1, keepdims=True)
            share = jnp.sum(jnp.where(lane == place, powers, 0.0), axis=1, keepdims=True)
            share = share / jnp.where(total > 0.0, total, 1.0)
            share_ref[here] = jnp.broadcast_to(share, (capacity, 128))
            gate, up, back = gate_sum[part, near], up_sum[part, near], back_in[here]
            sig = 1.0 / (1.0 + jnp.exp(-gate))
            silu = gate * sig
            active = silu * up
            active_low = active.astype(BF16)
            route_grad = jnp.sum(active_low.astype(F32) * back, axis=1, keepdims=True)
            grad = back * share
            gate_out[here] = (grad * up * (sig + silu * (1.0 - sig))).astype(BF16)
            up_out[here] = (grad * silu).astype(BF16)
            active_out[here] = active_low
            weighted_out[here] = (active * share).astype(BF16)
            high = route_grad.astype(BF16).astype(F32)
            spread_out = jnp.where(lane == place, high, 0.0)
            spread_out = jnp.where(lane == place + experts, route_grad - high, spread_out)
            spread_ref[near] = spread_out.astype(BF16)
        span = slice(part * size, (part + 1) * size)
        rows = dot(gate_out[span], gate_ref[...], ((1,), (1,))) + dot(up_out[span], up_ref[...], ((1,), (1,)))
        rows_back[blocks, :, :width] = rows.astype(BF16).reshape(group, capacity, width)
        rows_back[blocks, :, width:] = spread_ref[...].reshape(group, capacity, 128)
        copies.append(pltpu.make_async_copy(rows_back.at[blocks], rows_hbm.at[blocks], store_sem.at[part]))
        copies[-1].start()
    store(1, 2, 3, 4, 5)
    for copy in copies:
        copy.wait()


def expert_layer(owner, h, gains, mask, back, gate, up, experts, k, after=()):
    per_owner, width, hidden = gate.shape
    owners, capacity, _ = h.shape
    count = owners * capacity
    narrow = ((count, hidden), BF16)
    rows_back = ((owners, capacity, width + 128), BF16)
    half = count // 2
    return kernel_call(
        functools.partial(expert_kernel, experts=experts, k=k),
        "expert_layer",
        8.0,
        [owner, h, gains, mask, back, gate, up],
        [rows_back] + [narrow] * 4 + [((count, 128), F32)],
        smem=1,
        hbm=(1, 3, 4, 5, 6),
        out_hbm=(0,),
        after=after,
        scratch=[
            pltpu.VMEM(h.shape, BF16),
            pltpu.VMEM((count, 128), BF16),
            pltpu.VMEM((count, hidden), F32),
            pltpu.VMEM((width, hidden), BF16),
            pltpu.VMEM((width, hidden), BF16),
            pltpu.VMEM(*rows_back),
            pltpu.VMEM((2, half, hidden), F32),
            pltpu.VMEM((2, half, hidden), F32),
            pltpu.VMEM((2, half, 128), F32),
            pltpu.VMEM((half, 128), BF16),
            pltpu.SemaphoreType.DMA((6,)),
            pltpu.SemaphoreType.DMA((2,)),
        ],
        stored=(1, 2, 3, 4, 5),
    )


def weights_kernel(
    h_ref, rows_hbm, gate_low, up_low, weighted, out_hbm, tick_ref, rows_c, out_ref, load_sem, store_sem, *, k, wait
):
    tick_ref[...] = jnp.zeros(tick_ref.shape, F32)
    first = ((0,), (0,))
    owners, capacity, width = h_ref.shape
    hidden = gate_low.shape[1]
    half = width // 2
    load = pltpu.make_async_copy(rows_hbm.at[k], rows_c, load_sem.at[0])
    load.start()
    stores = []

    def keep(place):
        stores.append(pltpu.make_async_copy(out_ref.at[place], out_hbm.at[place], store_sem.at[place]))
        stores[-1].start()

    wait(0)
    rows_h = h_ref[...].reshape(owners * capacity, width)
    for place, low in ((0, gate_low), (1, up_low)):
        wait(2 + place)
        total = dot(rows_h, low[...], first).astype(BF16)
        out_ref[place, :, :hidden] = total[:half]
        out_ref[place, :, hidden:] = total[half:]
        keep(place)
    wait(4)
    load.wait()
    out_ref[2] = dot(weighted[...], rows_c[...], first).astype(BF16)
    keep(2)
    for store in stores:
        store.wait()


def expert_weights(h, rows_c, gate_low, up_low, weighted, k, after=()):
    per_owner, count, width = rows_c.shape
    hidden = gate_low.shape[1]
    out = ((3, hidden, width), BF16)
    return kernel_call(
        functools.partial(weights_kernel, k=k),
        "expert_weights",
        0.1,
        [h, rows_c, gate_low, up_low, weighted],
        [out, ((8, 128), F32)],
        hbm=(1,),
        out_hbm=(0,),
        after=after,
        scratch=[
            pltpu.VMEM((count, width), BF16),
            pltpu.VMEM(*out),
            pltpu.SemaphoreType.DMA((1,)),
            pltpu.SemaphoreType.DMA((3,)),
        ],
        late=(0, 2, 3, 4),
    )


def widen_kernel(first_ref, second_ref, gate_ref, up_ref, down_ref):
    step = pl.program_id(0)
    hidden = gate_ref.shape[2]
    half = first_ref.shape[1]
    for place, ref in enumerate((gate_ref, up_ref, down_ref)):
        for k, low_ref in enumerate((first_ref, second_ref)):

            @pl.when(step == 2 * place + k)
            def _():
                if place < 2:
                    ref[0, :half] = low_ref[0, :, :hidden].astype(F32)
                    ref[0, half:] = low_ref[0, :, hidden:].astype(F32)
                else:
                    ref[0] = low_ref[0].astype(F32)


def widen(first, second):
    count, hidden, width = first.shape

    def spot(place):
        return lambda i: (jnp.clip(i - 2 * place, 0, 1), 0, 0)

    return pl.pallas_call(
        widen_kernel,
        grid=(2 * count,),
        out_shape=[shape((2, width, hidden), F32)] * 2 + [shape((2, hidden, width), F32)],
        in_specs=[pl.BlockSpec((1, hidden, width), lambda i: (i // 2, 0, 0))] * 2,
        out_specs=[
            pl.BlockSpec((1, width, hidden), spot(0)),
            pl.BlockSpec((1, width, hidden), spot(1)),
            pl.BlockSpec((1, hidden, width), spot(2)),
        ],
        compiler_params=pltpu.CompilerParams(vmem_limit_bytes=63 * 1024 * 1024),
        cost_estimate=pl.CostEstimate(flops=0, bytes_accessed=24_000_000, transcendentals=0),
        name="widen",
    )(first, second)


def outputs_kernel(active_0, active_1, share_0, share_1, down_ref, sent_ref, tick_ref, out_ref, out_sem, *, wait):
    tick_ref[...] = jnp.zeros(tick_ref.shape, F32)
    owners, per_owner, capacity, width = sent_ref.shape
    group = owners // 2
    size = group * capacity
    copies = []
    wait(4)
    for k, (active, share) in enumerate(((active_0, share_0), (active_1, share_1))):
        wait(k)
        wait(2 + k)
        for part in range(2):
            span = slice(part * size, (part + 1) * size)
            blocks = slice(part * group, (part + 1) * group)
            produced = dot(active[span], down_ref[k]).astype(BF16).astype(F32)
            produced = (produced * share[span, :1]).astype(BF16)
            out_ref[blocks, k] = produced.reshape(group, capacity, width)
            copies.append(
                pltpu.make_async_copy(out_ref.at[blocks, k], sent_ref.at[blocks, k], out_sem.at[2 * k + part])
            )
            copies[-1].start()
    for copy in copies:
        copy.wait()


def expert_outputs(actives, shares, down, owners, after=()):
    count, hidden = actives[0].shape
    width = down.shape[2]
    sent = ((owners, 2, count // owners, width), BF16)
    return kernel_call(
        outputs_kernel,
        "expert_outputs",
        0.1,
        [*actives, *shares, down],
        [sent, ((8, 128), F32)],
        out_hbm=(0,),
        after=after,
        scratch=[pltpu.VMEM(*sent), pltpu.SemaphoreType.DMA((4,))],
        late=(0, 1, 2, 3, 4),
    )


def combined(pieces, sems, turn_ref, ready):
    loads = [pltpu.make_async_copy(*piece, sems.at[i]) for i, piece in enumerate(pieces)]
    for load in loads:
        load.start()
    ready()
    total, place = None, 0
    for load, (_, rows_ref) in zip(loads, pieces):
        load.wait()
        rows = rows_ref[...]
        rows = rows.reshape(rows.shape[0] * rows.shape[1], rows.shape[2])
        one = dot(turn_ref[:, place : place + rows.shape[0]], rows)
        place += rows.shape[0]
        total = one if total is None else total + one
    return total


def output_kernel(rows_hbm, turn_ref, middle_ref, out_ref, tick_ref, rows_ref, sems, *, wait, store):
    tick_ref[...] = jnp.zeros(tick_ref.shape, F32)
    half = rows_hbm.shape[0] // 2
    pieces = [
        (rows_hbm.at[part : part + half, k], rows_ref.at[part : part + half, k])
        for k in range(rows_hbm.shape[1])
        for part in (0, half)
    ]
    total = combined(pieces, sems, turn_ref, lambda: wait(1))
    wait(2)
    out_ref[...] = (middle_ref[...] + total).astype(BF16)


def layer_output(rows, turn, middle):
    return kernel_call(
        output_kernel,
        "layer_output",
        3,
        [rows, turn, middle],
        [(middle.shape, BF16), ((8, 128), F32)],
        hbm=(0,),
        scratch=[pltpu.VMEM(rows.shape, BF16), pltpu.SemaphoreType.DMA((4,))],
        late=(1, 2),
        stored=(0,),
    )


def router_kernel(
    first_hbm,
    second_hbm,
    turn_ref,
    middle_ref,
    probs_ref,
    mask_ref,
    gains_ref,
    c_ref,
    hidden_ref,
    grad_ref,
    send_ref,
    extra_ref,
    first_rows,
    second_rows,
    sems,
    *,
    experts,
    wait,
    store,
):
    rows, width = middle_ref.shape
    half = first_hbm.shape[0] // 2
    pieces = [
        (source.at[part : part + half], target.at[part : part + half])
        for source, target in ((first_hbm, first_rows), (second_hbm, second_rows))
        for part in (0, half)
    ]
    returned = combined(pieces, sems, turn_ref, lambda: wait(2))
    for i in (3, 5, 7, 8):
        wait(i)
    tail = returned[:, width:].T
    route_grad = tail[:experts] + tail[experts : 2 * experts]
    mask = mask_ref[...]
    probs = probs_ref[...]
    picked = probs * mask
    picked_sum = jnp.sum(picked, axis=0, keepdims=True)
    share = picked / picked_sum
    picked_grad = (route_grad - jnp.sum(route_grad * share, axis=0, keepdims=True)) / picked_sum
    prob_grad = mask * picked_grad
    logit_grad = probs * (prob_grad - jnp.sum(probs * prob_grad, axis=0, keepdims=True))
    extra_ref[:experts] = dot(logit_grad.astype(BF16), hidden_ref[...])
    logit_rows = jnp.concatenate([logit_grad, jnp.zeros((128 - experts, rows), F32)], axis=0).T
    router = gains_ref[:experts].astype(BF16)
    hidden_grad = returned[:, :width] + dot(logit_rows[:, :experts].astype(BF16), router)
    middle = middle_ref[...]
    scale = lax.rsqrt(jnp.mean(middle * middle, axis=1, keepdims=True) + EPSILON)
    normed = middle * scale
    extra_ref[experts : experts + 8] = jnp.broadcast_to(
        jnp.sum(hidden_grad * normed, axis=0, keepdims=True), (8, width)
    )
    inner = hidden_grad * gains_ref[experts + 1 : experts + 2]
    grad = c_ref[...].astype(F32) + scale * (
        inner - normed * jnp.mean(inner * normed, axis=1, keepdims=True)
    )
    grad_ref[...] = grad
    send_ref[...] = grad.astype(BF16)


def router_backward(first, second, turn, middle, probs, mask, gains, c, hidden, experts, after=()):
    rows, width = middle.shape
    return kernel_call(
        functools.partial(router_kernel, experts=experts),
        "router_backward",
        0.1,
        [first, second, turn, middle, probs, mask, gains, c, hidden],
        [((rows, width), F32), ((rows, width), BF16), ((experts + 8, width), F32)],
        hbm=(0, 1),
        after=after,
        scratch=[pltpu.VMEM(first.shape, BF16), pltpu.VMEM(first.shape, BF16), pltpu.SemaphoreType.DMA((4,))],
        late=(2, 3, 5, 7, 8),
        stored=(0,),
    )


def pair_kernel(keep_ref, other_ref, total_ref, *sends):
    for flip in range(4):
        total = keep_ref[flip] + other_ref[flip].astype(F32)
        if flip:
            sends[flip - 1][...] = total.astype(BF16)
        else:
            total_ref[...] = total


def pair_sum(keep, other):
    rows, width = keep.shape[1:]
    return kernel_call(
        pair_kernel, "pair_sum", 1.2, [keep, other], [((rows, width), F32)] + [((rows, width), BF16)] * 3
    )


def input_kernel(total_ref, *refs, experts, store):
    came = refs[:3]
    x_ref, gains_ref, middle_grad_ref, out_ref = refs[3:]
    total = total_ref[...]
    for piece in came:
        total = total + piece[...].astype(F32)
    x = x_ref[...].astype(F32)
    scale = lax.rsqrt(jnp.mean(x * x, axis=1, keepdims=True) + EPSILON)
    normed = x * scale
    inner = total * gains_ref[experts : experts + 1]
    out_ref[...] = middle_grad_ref[...] + scale * (
        inner - normed * jnp.mean(inner * normed, axis=1, keepdims=True)
    )


def input_grad(total, came, x, gains, middle_grad, experts):
    return kernel_call(
        functools.partial(input_kernel, experts=experts),
        "input_grad",
        2,
        [total, *came, x, gains, middle_grad],
        [(middle_grad.shape, F32)],
        held=(4, 6),
        stored=(0,),
    )[0]


PIECE, SPARE, SLICE = 16, 3, 64


def passed(value, after):
    results = [(value.shape, value.dtype)]
    return move_call(lambda *refs: [refs], "passed", 0.5, [value], results, after, 63)[0]


def shares_kernel(pieces_ref, out_ref, rest_ref):
    total = pieces_ref[0].astype(F32)
    for i in range(1, pieces_ref.shape[0]):
        total = total + pieces_ref[i].astype(F32)
    base = 8 * PIECE
    fill = jnp.zeros((PIECE - SPARE, 128), F32)
    for part in range(8):
        out_ref[part, :PIECE] = total[part * PIECE : (part + 1) * PIECE].astype(BF16)
        spare = total[base + part * SPARE : base + (part + 1) * SPARE]
        out_ref[part, PIECE:] = jnp.concatenate([spare, fill], axis=0).astype(BF16)
    rest_ref[...] = total[base + 2 * PIECE :].astype(BF16)


def shares_sum(pieces, after=()):
    return kernel_call(
        shares_kernel,
        "shares_sum",
        0.1,
        [pieces],
        [((8, 2 * PIECE, 128), BF16), ((SLICE, 128), BF16)],
        after=after,
    )


def whole_kernel(came_ref, rest_ref, out_ref):
    spare = came_ref[0, PIECE:].astype(F32)
    for i in range(1, 8):
        spare = spare + came_ref[i, PIECE:].astype(F32)
    rows = [came_ref[i, :PIECE] for i in range(8)] + [spare.astype(BF16), rest_ref[...]]
    rows = jnp.concatenate(rows, axis=0)
    for i in range(16):
        out_ref[i] = rows


def whole_pieces(came, rest, after=()):
    return kernel_call(
        whole_kernel,
        "whole_pieces",
        0.1,
        [came, rest],
        [((16, 9 * PIECE + SLICE, 128), BF16)],
        after=after,
    )[0]


def final_kernel(pieces_ref, wq_ref, wk_ref, wv_ref, gain_ref, *outs, experts):
    query_ref, key_ref, value_ref, output_ref, one_ref, two_ref, qg_ref, kg_ref, router_ref = outs
    rows = pieces_ref.shape[2]
    q_columns = query_ref.shape[1] // 8
    kv_columns = key_ref.shape[1] // 8
    sums = jnp.zeros((rows, 1), F32)
    base = 8 * PIECE
    for pair in range(4):
        keys, values = [], []
        for source in (2 * pair, 2 * pair + 1):
            block = [pieces_ref[i, source * PIECE : (source + 1) * PIECE] for i in range(16)]
            turned = jnp.concatenate(block, axis=0).astype(F32).T
            span = slice(source * q_columns, (source + 1) * q_columns)
            query = turned[:, :q_columns]
            query_ref[:, span] = query
            sums = sums + jnp.sum(query * wq_ref[:, span].astype(F32), axis=1, keepdims=True)
            keys.append(turned[:, q_columns : q_columns + kv_columns])
            values.append(turned[:, q_columns + kv_columns :])
        span = slice(2 * pair * kv_columns, 2 * (pair + 1) * kv_columns)
        for parts, ref, weight in ((keys, key_ref, wk_ref), (values, value_ref, wv_ref)):
            both = jnp.concatenate(parts, axis=1)
            ref[:, span] = both
            sums = sums + jnp.sum(both * weight[:, span].astype(F32), axis=1, keepdims=True)
    for i in range(16):
        half = i % 2 * SLICE
        output_ref[half : half + SLICE, i // 2 * rows : (i // 2 + 1) * rows] = pieces_ref[
            i, base + PIECE :
        ].astype(F32)
    spare = pieces_ref[:, base : base + PIECE].astype(F32)
    spare = jnp.concatenate([spare[i, :SPARE] for i in range(16)], axis=0)
    one_ref[...] = jnp.broadcast_to(sums, (rows, 128)).T[:1] / gain_ref[...].astype(F32)
    two_ref[...] = spare[experts : experts + 1]
    step = qg_ref.shape[1]
    qg_ref[...] = spare[experts + 1 : experts + 2, :step]
    kg_ref[...] = spare[experts + 2 : experts + 3, :step]
    router_ref[...] = spare[:experts]


def final_grads(pieces, wq, wk, wv, gain, experts):
    rows = pieces.shape[2]
    return kernel_call(
        functools.partial(final_kernel, experts=experts),
        "final_grads",
        0.2,
        [pieces, wq, wk, wv, gain],
        [
            (wq.shape, F32),
            (wk.shape, F32),
            (wv.shape, F32),
            ((rows, 8 * rows), F32),
            ((1, rows), F32),
            ((1, rows), F32),
            ((1, HEAD // 8), F32),
            ((1, HEAD // 8), F32),
            ((experts, rows), F32),
        ],
        held=(1, 2, 3, 4),
    )


def send(values, axis, flip):
    count = lax.axis_size(axis)
    return lax.ppermute(values, axis, [(i, i ^ flip) for i in range(count)])


def along_z(values):
    if not isinstance(values, (list, tuple)):
        values = [values] * 3
    return [send(value, "fsdp", 2 * (i + 1)) for i, value in enumerate(values)]


def gather_fsdp(block, name, after=()):
    came = along_z(block)
    return came, send(row([block, *came], name, after), "fsdp", 1)


def exchange(rows):
    return lax.all_to_all(rows, "expert", 0, 0, tiled=True)


def shards(
    tokens,
    lengths,
    routes,
    first_gain,
    query_weight,
    key_weight,
    value_weight,
    output_weight,
    query_gain,
    key_gain,
    second_gain,
    router_weight,
    gate_weight,
    up_weight,
    down_weight,
    cotangent,
):
    own = tokens[0]
    upstream = cotangent[0]
    rows, width = own.shape
    fsdp = lax.axis_size("fsdp")
    owners = lax.axis_size("expert")
    me = lax.axis_index("fsdp").astype(jnp.int32).reshape(1)
    owner = lax.axis_index("expert").astype(jnp.int32).reshape(1)
    experts = router_weight.shape[1]
    capacity = 3 * rows * routes.shape[2] // (2 * experts)
    kv_columns = key_weight.shape[1] // fsdp
    q_columns = query_weight.shape[1] // fsdp
    columns = q_columns + 2 * kv_columns
    q_heads = q_columns // HEAD

    ends = jnp.cumsum(lengths[0])
    place = jnp.arange(rows * fsdp, dtype=jnp.int32)
    start = jnp.max(jnp.where(ends[:, None] <= place[None, :], ends[:, None], 0), axis=0)
    position = (place - start).astype(F32)
    frequency = ROPE_BASE ** (-jnp.arange(HEAD // 2, dtype=F32) * 2.0 / HEAD)
    angles = frequency[:, None] * position[None, :]
    cosine, sine = jnp.cos(angles), jnp.sin(angles)
    start = start[None, :].astype(jnp.int32)

    packed, x_sends, dressed, mask = pack_weights(
        me,
        own,
        query_weight,
        key_weight,
        value_weight,
        router_weight.T,
        first_gain[None],
        second_gain[None],
        query_gain[None],
        key_gain[None],
        routes[0].T,
        upstream,
    )
    x_came = along_z(x_sends)
    x_other = [send(own, "fsdp", 1), send(packed[1], "fsdp", 1)]
    deal, turn = slot_tables(mask, capacity, owners)
    ready = (*x_other, deal, cosine, sine, start)
    x_other.append(send(relay(x_came, rows * fsdp, after=ready), "fsdp", 1))
    c_all = lax.all_gather(dressed, "expert", axis=0)
    wo_came = along_z(output_weight)

    h1, pre, keep, give, inverse, gains, heads, turned, mixed = attention_forward(
        me, own, packed[0], x_came, x_other, cosine, sine, start, experts, q_heads
    )
    other = send(give, "fsdp", 1)
    mixed_sends, wo_stack = merge(keep, other, output_weight, wo_came)
    mixed_came = along_z(mixed_sends)
    wo_other = send(wo_stack, "fsdp", 1)
    middle, probs, hidden, *sends = middle_layer(
        own, keep, other, mixed_came, output_weight, wo_came, wo_other, gains, deal, experts, owners
    )
    h_rows = [exchange(sent) for sent in sends]
    rows_c, row_mask, back = deal_rows(owner, c_all, down_weight, experts, capacity)
    came_back, actives, shares, grads, tick = [], [], [], [], ()
    for k, h in enumerate(h_rows):
        rows_back, gate_low, up_low, active, weighted, share = expert_layer(
            owner, h, gains, row_mask, back, gate_weight, up_weight, experts, k, after=tick
        )
        came_back.append(exchange(rows_back))
        actives.append(active)
        shares.append(share)
        grad, tick = expert_weights(h, rows_c, gate_low, up_low, weighted, k, after=grads[-1:])
        grads.append(lax.psum(grad, "fsdp"))
        tick = (tick,)
    gate_sum, up_sum, down_sum = widen(*grads)
    sent, _ = expert_outputs(actives, shares, down_weight, owners)

    middle_grad, middle_low, extra = router_backward(
        *came_back, turn, middle, probs, mask, gains, upstream, hidden, experts
    )
    da_came, da_other = gather_fsdp(middle_low, "row_middle", after=tick)
    out_rows = exchange(sent)
    layer_out, _ = layer_output(out_rows, turn, middle)
    first, dh_keep, dh_give = attention_backward(
        me,
        middle_low,
        da_came,
        da_other,
        heads,
        output_weight,
        cosine,
        sine,
        start,
        h1,
        pre,
        mixed,
        inverse,
        turned,
        extra,
        experts,
        q_heads,
    )
    dh_total, *dh_sends = pair_sum(dh_keep, send(dh_give, "fsdp", 1))
    dh_came = along_z(dh_sends)
    tokens_grad = input_grad(dh_total, dh_came, own, gains, middle_grad, experts)
    first = passed(first, after=(out_rows,))
    parted, rest = shares_sum(exchange(first), after=(*dh_came, grads[1]))
    parted = lax.all_to_all(parted, "fsdp", 0, 0, tiled=True)
    pieces = exchange(whole_pieces(parted, rest, after=(layer_out, tokens_grad)))
    query_sum, key_sum, value_sum, output_sum, one_sum, two_sum, *gain_sums, router_sum = final_grads(
        pieces, query_weight, key_weight, value_weight, first_gain[None], experts
    )
    return (
        layer_out[None],
        tokens_grad[None],
        one_sum[0],
        query_sum,
        key_sum,
        value_sum,
        output_sum,
        gain_sums[0][0],
        gain_sums[1][0],
        two_sum[0],
        router_sum.T,
        gate_sum,
        up_sum,
        down_sum,
    )


def solution(mesh):
    whole = P("expert", "fsdp", None)
    rows = P("fsdp", None)
    vector = P("fsdp")
    owned = P("expert", None, None)
    return jax.shard_map(
        shards,
        mesh=mesh,
        in_specs=(
            whole,
            P("expert", None),
            whole,
            vector,
            rows,
            rows,
            rows,
            rows,
            vector,
            vector,
            vector,
            rows,
            owned,
            owned,
            owned,
            whole,
        ),
        out_specs=(
            whole,
            whole,
            vector,
            rows,
            rows,
            rows,
            rows,
            vector,
            vector,
            vector,
            rows,
            owned,
            owned,
            owned,
        ),
        check_vma=False,
    )
```

```python
import functools

import jax
import jax.numpy as jnp
from jax import lax
from jax.experimental import pallas as pl
from jax.experimental.pallas import tpu as pltpu
from jax.sharding import PartitionSpec as P

EPSILON = 1e-06
ROPE_BASE = 10000.0
HEAD = 64
TILE = 256
F32 = jnp.float32
BF16 = jnp.bfloat16
VMEM = pl.BlockSpec(memory_space=pltpu.VMEM)
SMEM = pl.BlockSpec(memory_space=pltpu.SMEM)
ANY = pl.BlockSpec(memory_space=pl.ANY)
HBM = pl.BlockSpec(memory_space=pltpu.HBM)


def dot(left, right, dims=((1,), (0,))):
    return lax.dot_general(left, right, (dims, ((), ())), preferred_element_type=F32)


def shape(extent, dtype):
    return jax.ShapeDtypeStruct(extent, dtype)


def kernel_call(
    body, name, micros, operands, results, smem=0, hbm=(), out_hbm=(), after=(), scratch=(), held=(), late=(), stored=(), mib=61
):
    held = tuple(held) + tuple(late)
    n, a, r, s = len(operands), len(after), len(results), len(scratch)
    specs = [SMEM if i < smem else HBM if i in held or i in hbm else VMEM for i in range(n)]
    out_specs = [HBM if i in stored or i in out_hbm else VMEM for i in range(r)]
    staged = [pltpu.VMEM(operands[i].shape, operands[i].dtype) for i in held]
    staged += [pltpu.VMEM(*results[i]) for i in stored]
    sems = [pltpu.SemaphoreType.DMA((max(len(held), 1),)), pltpu.SemaphoreType.DMA((max(len(stored), 1),))]

    def wrapped(*refs):
        ins, outs = list(refs[:n]), list(refs[n + a : n + a + r])
        own = refs[n + a + r : n + a + r + s]
        stages, (load_sem, store_sem) = refs[n + a + r + s : -2], refs[-2:]
        loads, stores, begun = {}, {}, []
        for k, i in enumerate(held):
            loads[i] = pltpu.make_async_copy(ins[i], stages[k], load_sem.at[k])
            loads[i].start()
            ins[i] = stages[k]
        for k, i in enumerate(stored):
            stores[i] = pltpu.make_async_copy(stages[len(held) + k], outs[i], store_sem.at[k])
            outs[i] = stages[len(held) + k]
        for i in held:
            if i not in late:
                loads[i].wait()

        def store(*which):
            for i in which:
                stores[i].start()
                begun.append(i)

        extra = {}
        if late:
            extra["wait"] = lambda i: loads[i].wait()
        if stored:
            extra["store"] = store
        body(*ins, *outs, *own, **extra)
        store(*[i for i in stored if i not in begun])
        for i in stored:
            stores[i].wait()

    return pl.pallas_call(
        wrapped,
        out_shape=[shape(*result) for result in results],
        in_specs=specs + [ANY] * a,
        out_specs=out_specs,
        scratch_shapes=list(scratch) + staged + sems,
        compiler_params=pltpu.CompilerParams(vmem_limit_bytes=mib * 1024 * 1024),
        cost_estimate=pl.CostEstimate(flops=0, bytes_accessed=int(micros * 3.6e6), transcendentals=0),
        name=name,
    )(*operands, *after)


def move_call(moves, name, micros, operands, results, after=(), mib=10):
    def body(*refs):
        for source, target in moves(*refs):
            target[...] = source[...]

    return kernel_call(body, name, micros, operands, results, after=after, mib=mib)


def lane_blocks(value):
    return jnp.concatenate([value[:, i : i + 128] for i in range(0, value.shape[1], 128)], axis=0)


def joined_lanes(value, count):
    rows = value.shape[0] // count
    return jnp.concatenate([value[i * rows : (i + 1) * rows] for i in range(count)], axis=1)


def softmax_rows(logits):
    powers = jnp.exp(logits - jnp.max(logits, axis=0, keepdims=True))
    return powers / jnp.sum(powers, axis=0, keepdims=True)


def head_forward(pre, gain, cosine, sine):
    scale = lax.rsqrt(jnp.mean(pre * pre, axis=0, keepdims=True) + EPSILON)
    normed = pre * scale
    scaled = normed * gain
    a, b = scaled[: HEAD // 2], scaled[HEAD // 2 :]
    turned = jnp.concatenate([a * cosine - b * sine, b * cosine + a * sine], axis=0)
    return turned, normed, scale


def head_backward(grad, normed, scale, gain, cosine, sine):
    a, b = grad[: HEAD // 2], grad[HEAD // 2 :]
    unturned = jnp.concatenate([a * cosine + b * sine, b * cosine - a * sine], axis=0)
    gain_grad = jnp.sum(unturned * normed, axis=1, keepdims=True)
    inner = unturned * gain
    pre_grad = scale * (inner - normed * jnp.mean(inner * normed, axis=0, keepdims=True))
    return pre_grad, gain_grad


def slots_kernel(mask_ref, deal_ref, turn_ref, tick_ref, whole_ref, *, capacity, store):
    tick_ref[...] = jnp.zeros(tick_ref.shape, F32)
    experts, rows = mask_ref.shape
    mask = mask_ref[...]
    ranks = dot(mask.astype(BF16), earlier(rows))
    slot = lax.broadcasted_iota(jnp.int32, (capacity, rows), 0).astype(F32) + 1.0
    for expert in range(experts):
        one = slice(expert, expert + 1)
        whole_ref[expert * capacity : (expert + 1) * capacity] = jnp.where(
            (ranks[one] == slot) & (mask[one] > 0.5), 1.0, 0.0
        )
    deal_ref[...] = whole_ref[...].astype(BF16)
    store(0)
    for part in range(0, experts * capacity, 128):
        turn_ref[:, part : part + 128] = whole_ref[part : part + 128].T.astype(BF16)


def slot_tables(mask, capacity):
    experts, rows = mask.shape
    slots = experts * capacity
    return kernel_call(
        functools.partial(slots_kernel, capacity=capacity),
        "slot_tables",
        2.0,
        [mask],
        [((slots, rows), BF16), ((rows, slots), BF16), ((8, 128), F32)],
        scratch=[pltpu.VMEM((slots, rows), F32)],
        stored=(0, 1),
    )


def earlier(rows):
    return (
        lax.broadcasted_iota(jnp.int32, (rows, rows), 0)
        <= lax.broadcasted_iota(jnp.int32, (rows, rows), 1)
    ).astype(BF16)


def pack_kernel(
    me_ref, x_ref, wq_ref, wk_ref, wv_ref, router_ref, one_ref, two_ref, qg_ref, kg_ref, routes_ref, c_ref, *outs, wait, store
):
    own_ref, sends, dressed_ref, mask_ref, other_ref, parts_ref = outs[0], outs[1:4], *outs[4:]
    experts, rows = router_ref.shape
    wide = wq_ref.shape[1] // 8
    narrow = wk_ref.shape[1] // 8
    count = qg_ref.shape[1]
    heads = jnp.concatenate([qg_ref[...], kg_ref[...]], axis=0).astype(F32)
    heads = jnp.concatenate([heads, jnp.zeros((2, 128 - count), F32)], axis=1)
    heads = jnp.concatenate([heads, jnp.zeros((126, 128), F32)], axis=0).T[:count]
    small = jnp.concatenate(
        [
            router_ref[...].astype(F32),
            one_ref[...].astype(F32),
            two_ref[...].astype(F32),
            jnp.zeros((6, 128), F32),
            heads,
        ],
        axis=0,
    ).astype(BF16)
    for part in range(8):
        parts_ref[part, :wide] = wq_ref[:, part * wide : (part + 1) * wide].astype(F32).T.astype(BF16)
        parts_ref[part, wide + 2 * narrow :] = small
    for pair in range(4):
        span = slice(pair * 128, (pair + 1) * 128)
        for ref, place in ((wk_ref, wide), (wv_ref, wide + narrow)):
            turned = ref[:, span].astype(F32).T.astype(BF16)
            parts_ref[2 * pair, place : place + narrow] = turned[:narrow]
            parts_ref[2 * pair + 1, place : place + narrow] = turned[narrow:]
    me = me_ref[0]
    tall = parts_ref.shape[1]
    blocks = lane_blocks(x_ref[...])
    base = blocks.shape[0]
    own_ref[...] = parts_ref[me]
    other_ref[...] = parts_ref[me ^ 1]
    for flip in range(1, 4):
        sends[flip - 1][:base] = blocks
        sends[flip - 1][base : base + tall] = parts_ref[me ^ (2 * flip)]
        sends[flip - 1][base + tall :] = parts_ref[me ^ (2 * flip + 1)]
    store(1, 2, 3, 6, 0)
    wait(10)
    wait(11)
    width = c_ref.shape[1]
    subs = lax.broadcasted_iota(jnp.int32, (128, rows), 0)
    routed = jnp.zeros((128, rows), F32)
    for route in range(routes_ref.shape[0]):
        routed = routed + jnp.where(routes_ref[route : route + 1] == subs, 1.0, 0.0)
    dressed_ref[:, :width] = c_ref[...]
    dressed_ref[:, width:] = routed.T.astype(BF16)
    mask_ref[...] = routed[:experts]


def pack_weights(me, x, wq, wk, wv, router, one, two, qg, kg, routes, c):
    experts = router.shape[0]
    tall = (wq.shape[1] + wk.shape[1] + wv.shape[1]) // 8 + experts + 16
    rows, width = x.shape
    base = rows * 8
    own, first, second, third, dressed, mask, other = kernel_call(
        pack_kernel,
        "pack_weights",
        2.5,
        [me, x, wq, wk, wv, router, one, two, qg, kg, routes, c],
        [((tall, 128), BF16)]
        + [((base + 2 * tall, 128), BF16)] * 3
        + [((rows, width + 128), BF16), ((experts, rows), F32), ((tall, 128), BF16)],
        smem=1,
        scratch=[pltpu.VMEM((8, tall, 128), BF16)],
        held=range(1, 10),
        late=(10, 11),
        stored=(0, 1, 2, 3, 4, 5, 6),
    )
    return (own, other), [first, second, third], dressed, mask


def relay(came, base, after):
    tall = (came[0].shape[0] - base) // 2

    def moves(*refs):
        pairs = []
        for flip, ref in enumerate(refs[:3]):
            pairs.append((ref.at[:base], refs[3].at[flip, :base]))
            pairs.append((ref.at[base + tall :], refs[3].at[flip, base:]))
        return pairs

    return move_call(moves, "relay", 1.5, came, [((3, base + tall, 128), BF16)], after)[0]


def forward_kernel(me_ref, x_ref, own_ref, *refs, experts, q_heads, store):
    came, other_x, other_w, other_ref = refs[:3], refs[3], refs[4], refs[5]
    cos_ref, sin_ref, start_ref = refs[6:9]
    h1_ref, pre_ref, keep_ref, give_ref, inverse_ref, gains_ref, heads_ref, turned_ref, out_ref = refs[-9:]
    rows, width = x_ref.shape
    q_columns = q_heads * HEAD
    columns = q_columns + 2 * HEAD
    total = rows * 8
    tall = own_ref.shape[0]
    base = 8 * rows
    me = me_ref[0]
    for slot in range(8):
        flip = slot // 2
        if slot % 2:
            piece = other_ref[flip - 1, base:] if flip else other_w[...]
        elif flip:
            piece = came[flip - 1][base : base + tall]
        else:
            piece = own_ref[...]
        span = pl.ds(pl.multiple_of((me ^ slot) * rows, rows), rows)
        turned_ref[:, span] = piece[:columns]
        small = piece[columns:].astype(F32)
        gains_ref[:, span] = small[: experts + 8]
        heads_ref[pl.ds(pl.multiple_of((me ^ slot) * 8, 8), 8)] = small[experts + 8 :]
    gain_one = gains_ref[experts : experts + 1]
    for slot in range(8):
        flip = slot // 2
        if slot % 2:
            x = joined_lanes(other_ref[flip - 1, :base], 8) if flip else other_x[...]
        elif flip:
            x = joined_lanes(came[flip - 1][:base], 8)
        else:
            x = x_ref[...]
        x = x.astype(F32)
        scale = lax.rsqrt(jnp.mean(x * x, axis=1, keepdims=True) + EPSILON)
        h1_ref[slot] = (x * scale * gain_one).astype(BF16)
    store(0, 6, 7)
    for slot in range(8):
        block = dot(turned_ref[...], h1_ref[slot], ((1,), (1,)))
        place = pl.multiple_of((me ^ slot) * rows, rows)
        pre_ref[:, pl.ds(place, rows)] = block
    store(1)
    cosine, sine = cos_ref[...], sin_ref[...]
    gain_query, gain_key = heads_ref[:, :1], heads_ref[:, 1:2]
    key = head_forward(pre_ref[q_columns : q_columns + HEAD], gain_key, cosine, sine)[0]
    key = key.T.astype(BF16)
    value = pre_ref[q_columns + HEAD :].astype(BF16)
    inverse_ref[...] = jnp.zeros(inverse_ref.shape, F32)
    for head in range(q_heads):
        query = head_forward(pre_ref[head * HEAD : (head + 1) * HEAD], gain_query, cosine, sine)[0]
        query = query.astype(BF16) * jnp.array(HEAD ** (-0.5), BF16)
        for tile in range(total // TILE):
            low, high = tile * TILE, (tile + 1) * TILE
            scores = dot(key[:high], query[:, low:high])
            u = lax.broadcasted_iota(jnp.int32, (high, TILE), 0)
            t = lax.broadcasted_iota(jnp.int32, (high, TILE), 1) + low
            allowed = (u >= start_ref[:, low:high]) & (u <= t)
            powers = jnp.where(allowed, jnp.exp(scores), 0.0)
            inverse = 1.0 / jnp.sum(powers, axis=0, keepdims=True)
            probs = (powers * inverse).astype(BF16)
            mixed = dot(value[:, :high], probs).astype(BF16)
            inverse_ref[head : head + 1, low:high] = inverse
            for part in range(TILE // rows):
                out_ref[low // rows + part, head * HEAD : (head + 1) * HEAD] = mixed[
                    :, part * rows : (part + 1) * rows
                ]
    for slot in range(8):
        (give_ref if slot % 2 else keep_ref)[slot // 2] = out_ref[me ^ slot]


def attention_forward(me, x, own, came, other, cosine, sine, start, experts, q_heads, after=()):
    rows, width = x.shape
    total = 8 * rows
    columns = (q_heads + 2) * HEAD
    q_columns = q_heads * HEAD
    return kernel_call(
        functools.partial(forward_kernel, experts=experts, q_heads=q_heads),
        "attention_forward",
        7.0,
        [me, x, own, *came, *other, cosine, sine, start],
        [
            ((8, rows, width), BF16),
            ((columns, total), F32),
            ((4, q_columns, rows), BF16),
            ((4, q_columns, rows), BF16),
            ((8, total), F32),
            ((experts + 8, width), F32),
            ((HEAD, 128), F32),
            ((columns, width), BF16),
            ((8, q_columns, rows), BF16),
        ],
        smem=1,
        after=after,
        held=(1,),
        stored=(0, 1, 4, 6, 7, 8),
    )


def merge(keep, came, wo, wo_came):
    def moves(keep_ref, came_ref, *refs):
        weights, outs, stacked = refs[:4], refs[4:7], refs[7]
        pairs = [(weight, stacked.at[i]) for i, weight in enumerate(weights)]
        for flip in range(1, 4):
            pairs.append((keep_ref.at[flip], outs[flip - 1].at[0]))
            pairs.append((came_ref.at[flip], outs[flip - 1].at[1]))
        return pairs

    extent = ((2,) + keep.shape[1:], BF16)
    results = [extent] * 3 + [((4,) + wo.shape, BF16)]
    *sends, stacked = move_call(moves, "merge", 1.0, [keep, came, wo, *wo_came], results, mib=61)
    return sends, stacked


def middle_kernel(x_ref, keep_ref, other_ref, *refs, experts, wait, store):
    came, wo_ref, wo_came, wo_other_ref, gains_ref, deal_ref = refs[:3], refs[3], refs[4:7], refs[7], refs[8], refs[9]
    middle_ref, probs_ref, hidden_ref, sent_ref, mixed_ref, whole_ref, out_ref, out_sem = refs[10:]
    rows, width = x_ref.shape
    for slot in range(8):
        flip, core = slot // 2, slot % 2
        if flip:
            piece = came[flip - 1][core]
        else:
            piece = (other_ref if core else keep_ref)[0]
        span = slice(slot * 128, (slot + 1) * 128)
        mixed_ref[:, span] = piece.astype(F32).T.astype(BF16)
    for i in (6, 7, 8, 9, 10):
        wait(i)
    for slot in range(8):
        flip = slot // 2
        span = slice(slot * 128, (slot + 1) * 128)
        if slot % 2:
            whole_ref[span] = wo_other_ref[flip]
        else:
            whole_ref[span] = (wo_came[flip - 1] if flip else wo_ref)[...]
    wait(0)
    middle = x_ref[...].astype(F32) + dot(mixed_ref[...], whole_ref[...])
    middle_ref[...] = middle
    scale = lax.rsqrt(jnp.mean(middle * middle, axis=1, keepdims=True) + EPSILON)
    hidden = (middle * scale * gains_ref[experts + 1 : experts + 2]).astype(BF16)
    hidden_ref[...] = hidden
    probs_ref[...] = softmax_rows(dot(gains_ref[:experts].astype(BF16), hidden, ((1,), (1,))))
    store(0, 2)
    owners, per_owner, capacity, _ = sent_ref.shape
    group = owners // 4
    size = group * per_owner * capacity
    copies = []
    wait(12)
    for part in range(4):
        taken = dot(deal_ref[part * size : (part + 1) * size], hidden).astype(BF16)
        blocks = slice(group * part, group * (part + 1))
        out_ref[blocks] = taken.reshape(group, per_owner, capacity, width)
        copies.append(pltpu.make_async_copy(out_ref.at[blocks], sent_ref.at[blocks], out_sem.at[part]))
        copies[-1].start()
    for copy in copies:
        copy.wait()


def middle_layer(x, keep, other, came, wo, wo_came, wo_other, gains, deal, experts, owners):
    rows, width = x.shape
    per_owner = experts // owners
    capacity = deal.shape[0] // experts
    sent = ((owners, per_owner, capacity, width), BF16)
    return kernel_call(
        functools.partial(middle_kernel, experts=experts),
        "middle_layer",
        3.0,
        [x, keep, other, *came, wo, *wo_came, wo_other, gains, deal],
        [((rows, width), F32), ((experts, rows), F32), ((rows, width), BF16), sent],
        out_hbm=(3,),
        scratch=[
            pltpu.VMEM((rows, width), BF16),
            pltpu.VMEM((width, width), BF16),
            pltpu.VMEM(*sent),
            pltpu.SemaphoreType.DMA((4,)),
        ],
        late=(6, 7, 8, 9, 10, 0, 12),
        stored=(0, 2),
    )


def row(pieces, name):
    def moves(*refs):
        return [(ref, refs[-1].at[i]) for i, ref in enumerate(refs[:-1])]

    return move_call(moves, name, 1.0, pieces, [((len(pieces),) + pieces[0].shape, BF16)])[0]


def backward_kernel(me_ref, own_da_ref, *refs, experts, q_heads, wait):
    came, other_ref = refs[:3], refs[3]
    heads_ref, wo_ref, cos_ref, sin_ref, start_ref = refs[4:9]
    h1_ref, pre_ref, mixed_ref, inverse_ref, turned_ref, extra_ref = refs[9:15]
    first_ref, keep_ref, send_ref = refs[-10:-7]
    da_ref, mixed_grad_ref, dkey_ref, dvalue_ref, low_ref, out_slots_ref, grad_ref = refs[-7:]
    rows, width = own_da_ref.shape
    q_columns = q_heads * HEAD
    columns = q_columns + 2 * HEAD
    total = rows * 8
    me = me_ref[0]
    for slot in range(8):
        flip, core = slot // 2, slot % 2
        if core:
            piece = other_ref[flip]
        else:
            piece = (came[flip - 1] if flip else own_da_ref)[...]
        span = slice(slot * rows, (slot + 1) * rows)
        da_ref[span] = piece
        place = pl.multiple_of((me ^ slot) * rows, rows)
        mixed_grad_ref[:, pl.ds(place, rows)] = dot(wo_ref[...], piece, ((1,), (1,))).astype(BF16)
    wait(13)
    for slot in range(8):
        out_slots_ref[:, slot * rows : (slot + 1) * rows] = mixed_ref[me ^ slot]
    wo_grad = dot(out_slots_ref[...], da_ref[...]).astype(BF16)
    wo_grad = lane_blocks(wo_grad)
    wait(12)
    wait(14)
    gain_query, gain_key = heads_ref[:, :1], heads_ref[:, 1:2]
    cosine, sine = cos_ref[...], sin_ref[...]
    key_turned, key_normed, key_scale = head_forward(
        pre_ref[q_columns : q_columns + HEAD], gain_key, cosine, sine
    )
    key_low = key_turned.astype(BF16)
    key = key_turned.T.astype(BF16)
    value = pre_ref[q_columns + HEAD :].T.astype(BF16)
    dkey_ref[...] = jnp.zeros(dkey_ref.shape, F32)
    dvalue_ref[...] = jnp.zeros(dvalue_ref.shape, F32)
    gain_query_grad = jnp.zeros((HEAD, 1), F32)
    pieces = []
    for head in range(q_heads):
        span = slice(head * HEAD, (head + 1) * HEAD)
        turned, normed, scale = head_forward(pre_ref[span], gain_query, cosine, sine)
        query = turned.astype(BF16) * jnp.array(HEAD ** (-0.5), BF16)
        grads = []
        for tile in range(total // TILE):
            low, high = tile * TILE, (tile + 1) * TILE
            part = query[:, low:high]
            mixed_grad = mixed_grad_ref[span, low:high]
            scores = dot(key[:high], part)
            u = lax.broadcasted_iota(jnp.int32, (high, TILE), 0)
            t = lax.broadcasted_iota(jnp.int32, (high, TILE), 1) + low
            allowed = (u >= start_ref[:, low:high]) & (u <= t)
            probs = jnp.where(allowed, jnp.exp(scores) * inverse_ref[head : head + 1, low:high], 0.0)
            attend = dot(value[:high], mixed_grad)
            delta = jnp.sum(probs * attend, axis=0, keepdims=True)
            score_low = (probs * (attend - delta)).astype(BF16)
            grads.append(dot(key_low[:, :high], score_low))
            dkey_ref[:, :high] += dot(part, score_low, ((1,), (1,)))
            dvalue_ref[:, :high] += dot(mixed_grad, probs.astype(BF16), ((1,), (1,)))
        query_grad = jnp.concatenate(grads, axis=1) * HEAD ** (-0.5)
        pre_grad, gain_grad = head_backward(query_grad, normed, scale, gain_query, cosine, sine)
        gain_query_grad += gain_grad
        pieces.append(pre_grad)
    pre_grad, gain_key_grad = head_backward(
        dkey_ref[...], key_normed, key_scale, gain_key, cosine, sine
    )
    pieces += [pre_grad, dvalue_ref[...]]
    pre_grad = jnp.concatenate(pieces, axis=0)
    low_ref[...] = pre_grad.astype(BF16)
    slots_grad = []
    for slot in range(8):
        place = pl.multiple_of((me ^ slot) * rows, rows)
        slots_grad.append(low_ref[:, pl.ds(place, rows)])
    slots_grad = jnp.concatenate(slots_grad, axis=1)
    wait(11)
    wait(15)
    grad_ref[:columns] = dot(slots_grad, h1_ref[...].reshape(total, width))
    extra = extra_ref[...]
    lane = lax.broadcasted_iota(jnp.int32, (HEAD, 128), 1)
    gains = jnp.where(lane == 0, gain_query_grad, jnp.where(lane == 1, gain_key_grad, 0.0))
    gains = gains.T[:2]
    step = HEAD // 8
    grad_ref[columns:] = jnp.zeros((64, width), F32)
    grad_ref[columns : columns + experts + 1] = extra[: experts + 1]
    for part in range(8):
        grad_ref[columns + experts + 1 : columns + experts + 3, part * rows : part * rows + step] = gains[
            :, part * step : (part + 1) * step
        ]
    for piece in range(16):
        spare = []
        place = columns + piece * SPARE
        for part in range(8):
            span = slice(part * rows, (part + 1) * rows)
            block = grad_ref[piece * PIECE : (piece + 1) * PIECE, span]
            first_ref[piece, part * PIECE : (part + 1) * PIECE] = block.astype(BF16)
            spare.append(grad_ref[place : place + SPARE, span])
        spare.append(jnp.zeros((2 * PIECE - 8 * SPARE, 128), F32))
        first_ref[piece, 8 * PIECE : 10 * PIECE] = jnp.concatenate(spare, axis=0).astype(BF16)
        first_ref[piece, 10 * PIECE :] = wo_grad[piece * SLICE : (piece + 1) * SLICE]
    turned = turned_ref[...]
    for slot in range(8):
        low_rows_slot = slots_grad[:, slot * rows : (slot + 1) * rows].astype(F32).T.astype(BF16)
        part = dot(low_rows_slot, turned)
        if slot % 2:
            send_ref[slot // 2] = part.astype(BF16)
        else:
            keep_ref[slot // 2] = part


def attention_backward(
    me, da, came, other, heads, wo, cosine, sine, start, h1, pre, mixed, inverse, turned, extra, experts, q_heads, after=()
):
    rows, width = da.shape
    total = 8 * rows
    columns = pre.shape[0]
    q_columns = q_heads * HEAD
    return kernel_call(
        functools.partial(backward_kernel, experts=experts, q_heads=q_heads),
        "attention_backward",
        12,
        [me, da, *came, other, heads, wo, cosine, sine, start, h1, pre, mixed, inverse, turned, extra],
        [
            ((16, 10 * PIECE + SLICE, 128), BF16),
            ((4, rows, width), F32),
            ((4, rows, width), BF16),
        ],
        smem=1,
        after=after,
        held=(6, 7),
        late=(11, 12, 13, 14, 15),
        scratch=[
            pltpu.VMEM((total, width), BF16),
            pltpu.VMEM((q_columns, total), BF16),
            pltpu.VMEM((HEAD, total), F32),
            pltpu.VMEM((HEAD, total), F32),
            pltpu.VMEM((columns, total), BF16),
            pltpu.VMEM((q_columns, total), BF16),
            pltpu.VMEM((columns + 64, width), F32),
        ],
    )


def deal_kernel(owner_ref, c_ref, down_ref, rows_c, mask_ref, back_ref, c_scratch, sems, *, experts, capacity, wait, store):
    owner = owner_ref[0]
    per_owner, hidden, width = down_ref.shape
    rows = c_ref.shape[1]
    loads = [pltpu.make_async_copy(c_ref.at[i], c_scratch.at[i], sems.at[i]) for i in range(16)]
    for load in loads:
        load.start()
    lanes = lax.broadcasted_iota(jnp.int32, (experts, 128), 1)
    subs = lax.broadcasted_iota(jnp.int32, (experts, 128), 0)
    eye = (lanes == subs).astype(BF16)
    before = earlier(rows)
    mine_of = lax.broadcasted_iota(jnp.int32, (experts, rows), 0) - owner * per_owner
    slot = lax.broadcasted_iota(jnp.int32, (capacity, rows), 0).astype(F32) + 1.0
    for block in range(16):
        loads[block].wait()
        c = c_scratch[block]
        mask = dot(eye, c[:, width:], ((1,), (1,)))
        ranks = dot(mask.astype(BF16), before)
        deals = []
        for k in range(per_owner):
            mine = mine_of == k
            hit = jnp.sum(jnp.where(mine, mask, 0.0), axis=0, keepdims=True)
            rank = jnp.sum(jnp.where(mine, ranks, 0.0), axis=0, keepdims=True)
            deals.append(jnp.where((rank == slot) & (hit > 0.5), 1.0, 0.0))
        taken = dot(jnp.concatenate(deals, axis=0).astype(BF16), c).astype(BF16)
        span = slice(block * capacity, (block + 1) * capacity)
        for k in range(per_owner):
            spot = slice(k * capacity, (k + 1) * capacity)
            rows_c[k, span] = taken[spot, :width]
            mask_ref[k, span] = taken[spot, width:]
    store(0, 1)
    wait(2)
    for k in range(per_owner):
        for tile in range(16 * capacity // TILE):
            span = slice(tile * TILE, (tile + 1) * TILE)
            back_ref[k, span] = dot(rows_c[k, span], down_ref[k], ((1,), (1,)))


def deal_rows(owner, c, down, experts, capacity):
    per_owner, hidden, width = down.shape
    count = 16 * capacity
    return kernel_call(
        functools.partial(deal_kernel, experts=experts, capacity=capacity),
        "deal_rows",
        12.0,
        [owner, c, down],
        [
            ((per_owner, count, width), BF16),
            ((per_owner, count, 128), BF16),
            ((per_owner, count, hidden), F32),
        ],
        smem=1,
        hbm=(1,),
        scratch=[pltpu.VMEM(c.shape, BF16), pltpu.SemaphoreType.DMA((16,))],
        late=(2,),
        stored=(0, 1, 2),
    )


def expert_kernel(
    owner_ref,
    h_hbm,
    gains_ref,
    mask_ref,
    back_hbm,
    gate_hbm,
    up_hbm,
    rows_hbm,
    gate_out,
    up_out,
    active_out,
    weighted_out,
    share_ref,
    h_ref,
    back_in,
    gate_ref,
    up_ref,
    rows_back,
    gate_sum,
    up_sum,
    logit_sum,
    spread_ref,
    load_sem,
    store_sem,
    *,
    experts,
    store,
):
    owners, per_owner, capacity, width = h_hbm.shape
    group = 8
    parts = owners // group
    size = group * capacity
    loads = {}
    for k in range(per_owner):
        for part in range(parts):
            blocks = slice(part * group, (part + 1) * group)
            spot = (k * parts + part) * 4
            loads[k, part] = [
                pltpu.make_async_copy(h_hbm.at[blocks, k], h_ref.at[blocks, k], load_sem.at[spot]),
                pltpu.make_async_copy(
                    back_hbm.at[k, part * size : (part + 1) * size],
                    back_in.at[k, part * size : (part + 1) * size],
                    load_sem.at[spot + 1],
                ),
            ]
            if part == 0:
                loads[k, part] += [
                    pltpu.make_async_copy(gate_hbm.at[k], gate_ref.at[k], load_sem.at[spot + 2]),
                    pltpu.make_async_copy(up_hbm.at[k], up_ref.at[k], load_sem.at[spot + 3]),
                ]
            for load in loads[k, part]:
                load.start()
    owner = owner_ref[0]
    router = jnp.concatenate([gains_ref[:experts], jnp.zeros((128 - experts, width), F32)], axis=0)
    router = router.astype(BF16)
    lane = lax.broadcasted_iota(jnp.int32, (size, 128), 1)
    copies = []
    chunk = capacity
    lane = lane[:chunk]
    order = [(k, part) for k in range(per_owner) for part in range(parts)]

    def begin(i):
        k, part = order[i]
        blocks = slice(part * group, (part + 1) * group)
        for load in loads[k, part]:
            load.wait()
        h = h_ref[blocks, k].reshape(size, width)
        gate_sum[i % 2] = dot(h, gate_ref[k])
        up_sum[i % 2] = dot(h, up_ref[k])
        logit_sum[i % 2] = dot(h, router, ((1,), (1,)))

    begin(0)
    for i, (k, part) in enumerate(order):
        if i + 1 < len(order):
            begin(i + 1)
        place = owner * per_owner + k
        blocks = slice(part * group, (part + 1) * group)
        span = slice(part * size, (part + 1) * size)
        for spot in range(0, size, chunk):
            here = slice(part * size + spot, part * size + spot + chunk)
            near = slice(spot, spot + chunk)
            logits = logit_sum[i % 2, near]
            chosen = mask_ref[k, here] > 0.5
            top = jnp.max(jnp.where(chosen, logits, -1e30), axis=1, keepdims=True)
            powers = jnp.where(chosen, jnp.exp(logits - top), 0.0)
            total = jnp.sum(powers, axis=1, keepdims=True)
            share = jnp.sum(jnp.where(lane == place, powers, 0.0), axis=1, keepdims=True)
            share = share / jnp.where(total > 0.0, total, 1.0)
            share_ref[k, here] = jnp.broadcast_to(share, (chunk, 128))
            gate, up, back = gate_sum[i % 2, near], up_sum[i % 2, near], back_in[k, here]
            sig = 1.0 / (1.0 + jnp.exp(-gate))
            silu = gate * sig
            active = silu * up
            active_low = active.astype(BF16)
            route_grad = jnp.sum(active_low.astype(F32) * back, axis=1, keepdims=True)
            grad = back * share
            gate_out[k, here] = (grad * up * (sig + silu * (1.0 - sig))).astype(BF16)
            up_out[k, here] = (grad * silu).astype(BF16)
            active_out[k, here] = active_low
            weighted_out[k, here] = (active * share).astype(BF16)
            high = route_grad.astype(BF16).astype(F32)
            spread_out = jnp.where(lane == place, high, 0.0)
            spread_out = jnp.where(lane == place + experts, route_grad - high, spread_out)
            spread_ref[near] = spread_out.astype(BF16)
        rows = dot(gate_out[k, span], gate_ref[k], ((1,), (1,))) + dot(up_out[k, span], up_ref[k], ((1,), (1,)))
        rows_back[blocks, k, :, :width] = rows.astype(BF16).reshape(group, capacity, width)
        rows_back[blocks, k, :, width:] = spread_ref[...].reshape(group, capacity, 128)
        copies.append(
            pltpu.make_async_copy(rows_back.at[blocks, k], rows_hbm.at[blocks, k], store_sem.at[k * parts + part])
        )
        copies[-1].start()
    store(1, 2, 3, 4, 5)
    for copy in copies:
        copy.wait()


def expert_layer(owner, h, gains, mask, back, gate, up, experts):
    per_owner, width, hidden = gate.shape
    owners, _, capacity, _ = h.shape
    count = owners * capacity
    narrow = ((per_owner, count, hidden), BF16)
    rows_back = ((owners, per_owner, capacity, width + 128), BF16)
    pieces = per_owner * (owners // 8)
    return kernel_call(
        functools.partial(expert_kernel, experts=experts),
        "expert_layer",
        14.0,
        [owner, h, gains, mask, back, gate, up],
        [rows_back] + [narrow] * 4 + [((per_owner, count, 128), F32)],
        smem=1,
        hbm=(1, 4, 5, 6),
        out_hbm=(0,),
        scratch=[pltpu.VMEM(value.shape, value.dtype) for value in (h, back, gate, up)]
        + [pltpu.VMEM(*rows_back)]
        + [pltpu.VMEM((2, 8 * capacity, n), F32) for n in (hidden, hidden, 128)]
        + [pltpu.VMEM((8 * capacity, 128), BF16)]
        + [pltpu.SemaphoreType.DMA((4 * pieces,)), pltpu.SemaphoreType.DMA((pieces,))],
        stored=(1, 2, 3, 4, 5),
    )


def weights_kernel(
    h_hbm, rows_c, gate_low, up_low, weighted, out_hbm, tick_ref, h_ref, out_ref, load_sem, store_sem, *, wait
):
    tick_ref[...] = jnp.zeros(tick_ref.shape, F32)
    first = ((0,), (0,))
    owners, per_owner, capacity, width = h_hbm.shape
    hidden = gate_low.shape[2]
    half = width // 2
    loads = [
        pltpu.make_async_copy(h_hbm.at[:, k], h_ref.at[:, k], load_sem.at[k]) for k in range(per_owner)
    ]
    for load in loads:
        load.start()
    stores = []

    def keep(place):
        stores.append(pltpu.make_async_copy(out_ref.at[place], out_hbm.at[place], store_sem.at[place]))
        stores[-1].start()

    wait(2)
    for k in range(per_owner):
        loads[k].wait()
        rows_h = h_ref[:, k].reshape(owners * capacity, width)
        for place, low in ((k, gate_low), (per_owner + k, up_low)):
            if k == 0 and place:
                wait(3)
            total = dot(rows_h, low[k], first).astype(BF16)
            out_ref[place, :, :hidden] = total[:half]
            out_ref[place, :, hidden:] = total[half:]
            keep(place)
        if k == 0:
            wait(4)
            wait(1)
        place = 2 * per_owner + k
        out_ref[place] = dot(weighted[k], rows_c[k], first).astype(BF16)
        keep(place)
    for store in stores:
        store.wait()


def expert_weights(h, rows_c, gate_low, up_low, weighted):
    per_owner, count, width = rows_c.shape
    hidden = gate_low.shape[2]
    out = ((3 * per_owner, hidden, width), BF16)
    return kernel_call(
        weights_kernel,
        "expert_weights",
        0.1,
        [h, rows_c, gate_low, up_low, weighted],
        [out, ((8, 128), F32)],
        hbm=(0,),
        out_hbm=(0,),
        scratch=[
            pltpu.VMEM(h.shape, BF16),
            pltpu.VMEM(*out),
            pltpu.SemaphoreType.DMA((per_owner,)),
            pltpu.SemaphoreType.DMA((3 * per_owner,)),
        ],
        late=(2, 3, 4, 1),
    )


def widen_kernel(low_ref, gate_ref, up_ref, down_ref):
    step = pl.program_id(0)
    hidden = gate_ref.shape[2]
    value = low_ref[0].astype(F32)
    half = value.shape[0]
    for place, ref in ((0, gate_ref), (1, up_ref)):

        @pl.when(step // 2 == place)
        def _():
            ref[0, :half] = value[:, :hidden]
            ref[0, half:] = value[:, hidden:]

    @pl.when(step // 2 == 2)
    def _():
        down_ref[0] = value


def widen(low):
    count, hidden, width = low.shape
    per_owner = count // 3

    def spot(place):
        return lambda i: (jnp.clip(i - place * per_owner, 0, per_owner - 1), 0, 0)

    return pl.pallas_call(
        widen_kernel,
        grid=(count,),
        out_shape=[shape((per_owner, width, hidden), F32)] * 2 + [shape((per_owner, hidden, width), F32)],
        in_specs=[pl.BlockSpec((1, hidden, width), lambda i: (i, 0, 0))],
        out_specs=[
            pl.BlockSpec((1, width, hidden), spot(0)),
            pl.BlockSpec((1, width, hidden), spot(1)),
            pl.BlockSpec((1, hidden, width), spot(2)),
        ],
        compiler_params=pltpu.CompilerParams(vmem_limit_bytes=63 * 1024 * 1024),
        cost_estimate=pl.CostEstimate(flops=0, bytes_accessed=24_000_000, transcendentals=0),
        name="widen",
    )(low)


def outputs_kernel(active, share, down_ref, sent_ref, tick_ref, out_ref, out_sem, *, wait):
    tick_ref[...] = jnp.zeros(tick_ref.shape, F32)
    per_owner, count, hidden = active.shape
    owners, _, capacity, width = sent_ref.shape
    group = 8
    size = group * capacity
    copies = []
    for i in range(3):
        wait(i)
    for k in range(per_owner):
        for part in range(owners // group):
            span = slice(part * size, (part + 1) * size)
            blocks = slice(part * group, (part + 1) * group)
            produced = dot(active[k, span], down_ref[k]).astype(BF16).astype(F32)
            produced = (produced * share[k, span, :1]).astype(BF16)
            out_ref[blocks, k] = produced.reshape(group, capacity, width)
            copies.append(
                pltpu.make_async_copy(
                    out_ref.at[blocks, k], sent_ref.at[blocks, k], out_sem.at[k * (owners // group) + part]
                )
            )
            copies[-1].start()
    for copy in copies:
        copy.wait()


def expert_outputs(active, share, down, owners, after=()):
    per_owner, count, hidden = active.shape
    width = down.shape[2]
    sent = ((owners, per_owner, count // owners, width), BF16)
    return kernel_call(
        outputs_kernel,
        "expert_outputs",
        0.1,
        [active, share, down],
        [sent, ((8, 128), F32)],
        out_hbm=(0,),
        after=after,
        scratch=[pltpu.VMEM(*sent), pltpu.SemaphoreType.DMA((per_owner * (owners // 8),))],
        late=(0, 1, 2),
    )


def combined(rows_hbm, rows_ref, sems, turn_ref, ready):
    owners, per_owner, capacity, wide = rows_hbm.shape
    group = owners // 4
    size = group * per_owner * capacity
    loads = []
    for part in range(4):
        blocks = slice(part * group, (part + 1) * group)
        loads.append(pltpu.make_async_copy(rows_hbm.at[blocks], rows_ref.at[blocks], sems.at[part]))
        loads[-1].start()
    ready()
    total = None
    for part in range(4):
        loads[part].wait()
        rows = rows_ref[part * group : (part + 1) * group].reshape(size, wide)
        one = dot(turn_ref[:, part * size : (part + 1) * size], rows)
        total = one if total is None else total + one
    return total


def output_kernel(rows_hbm, turn_ref, middle_ref, out_ref, tick_ref, rows_ref, sems, *, wait, store):
    tick_ref[...] = jnp.zeros(tick_ref.shape, F32)
    total = combined(rows_hbm, rows_ref, sems, turn_ref, lambda: wait(1))
    wait(2)
    out_ref[...] = (middle_ref[...] + total).astype(BF16)


def layer_output(rows, turn, middle):
    return kernel_call(
        output_kernel,
        "layer_output",
        3,
        [rows, turn, middle],
        [(middle.shape, BF16), ((8, 128), F32)],
        hbm=(0,),
        scratch=[pltpu.VMEM(rows.shape, BF16), pltpu.SemaphoreType.DMA((4,))],
        late=(1, 2),
        stored=(0,),
    )


def router_kernel(
    rows_hbm,
    turn_ref,
    middle_ref,
    probs_ref,
    mask_ref,
    gains_ref,
    c_ref,
    hidden_ref,
    grad_ref,
    send_ref,
    extra_ref,
    rows_ref,
    sems,
    *,
    experts,
    wait,
    store,
):
    rows, width = middle_ref.shape
    returned = combined(rows_hbm, rows_ref, sems, turn_ref, lambda: wait(1))
    for i in (2, 4, 6, 7):
        wait(i)
    tail = returned[:, width:].T
    route_grad = tail[:experts] + tail[experts : 2 * experts]
    mask = mask_ref[...]
    probs = probs_ref[...]
    picked = probs * mask
    picked_sum = jnp.sum(picked, axis=0, keepdims=True)
    share = picked / picked_sum
    picked_grad = (route_grad - jnp.sum(route_grad * share, axis=0, keepdims=True)) / picked_sum
    prob_grad = mask * picked_grad
    logit_grad = probs * (prob_grad - jnp.sum(probs * prob_grad, axis=0, keepdims=True))
    extra_ref[:experts] = dot(logit_grad.astype(BF16), hidden_ref[...])
    logit_rows = jnp.concatenate([logit_grad, jnp.zeros((128 - experts, rows), F32)], axis=0).T
    router = gains_ref[:experts].astype(BF16)
    hidden_grad = returned[:, :width] + dot(logit_rows[:, :experts].astype(BF16), router)
    middle = middle_ref[...]
    scale = lax.rsqrt(jnp.mean(middle * middle, axis=1, keepdims=True) + EPSILON)
    normed = middle * scale
    extra_ref[experts : experts + 8] = jnp.broadcast_to(
        jnp.sum(hidden_grad * normed, axis=0, keepdims=True), (8, width)
    )
    inner = hidden_grad * gains_ref[experts + 1 : experts + 2]
    grad = c_ref[...].astype(F32) + scale * (
        inner - normed * jnp.mean(inner * normed, axis=1, keepdims=True)
    )
    grad_ref[...] = grad
    send_ref[...] = grad.astype(BF16)


def router_backward(rows_back, turn, middle, probs, mask, gains, c, hidden, experts, after=()):
    rows, width = middle.shape
    return kernel_call(
        functools.partial(router_kernel, experts=experts),
        "router_backward",
        5,
        [rows_back, turn, middle, probs, mask, gains, c, hidden],
        [((rows, width), F32), ((rows, width), BF16), ((experts + 8, width), F32)],
        hbm=(0,),
        after=after,
        scratch=[pltpu.VMEM(rows_back.shape, BF16), pltpu.SemaphoreType.DMA((4,))],
        late=(1, 2, 4, 6, 7),
        stored=(0,),
    )


def pair_kernel(keep_ref, other_ref, total_ref, *sends):
    for flip in range(4):
        total = keep_ref[flip] + other_ref[flip].astype(F32)
        if flip:
            sends[flip - 1][...] = total.astype(BF16)
        else:
            total_ref[...] = total


def pair_sum(keep, other):
    rows, width = keep.shape[1:]
    return kernel_call(
        pair_kernel, "pair_sum", 1.2, [keep, other], [((rows, width), F32)] + [((rows, width), BF16)] * 3
    )


def input_kernel(total_ref, *refs, experts, store):
    came = refs[:3]
    x_ref, gains_ref, middle_grad_ref, out_ref = refs[3:]
    total = total_ref[...]
    for piece in came:
        total = total + piece[...].astype(F32)
    x = x_ref[...].astype(F32)
    scale = lax.rsqrt(jnp.mean(x * x, axis=1, keepdims=True) + EPSILON)
    normed = x * scale
    inner = total * gains_ref[experts : experts + 1]
    out_ref[...] = middle_grad_ref[...] + scale * (
        inner - normed * jnp.mean(inner * normed, axis=1, keepdims=True)
    )


def input_grad(total, came, x, gains, middle_grad, experts):
    return kernel_call(
        functools.partial(input_kernel, experts=experts),
        "input_grad",
        2,
        [total, *came, x, gains, middle_grad],
        [(middle_grad.shape, F32)],
        held=(4, 6),
        stored=(0,),
    )[0]


PIECE, SPARE, SLICE = 16, 3, 64


def passed(value, after):
    results = [(value.shape, value.dtype)]
    return move_call(lambda *refs: [refs], "passed", 0.5, [value], results, after, 63)[0]


def shares_kernel(pieces_ref, out_ref, rest_ref):
    total = pieces_ref[0].astype(F32)
    for i in range(1, pieces_ref.shape[0]):
        total = total + pieces_ref[i].astype(F32)
    base = 8 * PIECE
    fill = jnp.zeros((PIECE - SPARE, 128), F32)
    for part in range(8):
        out_ref[part, :PIECE] = total[part * PIECE : (part + 1) * PIECE].astype(BF16)
        spare = total[base + part * SPARE : base + (part + 1) * SPARE]
        out_ref[part, PIECE:] = jnp.concatenate([spare, fill], axis=0).astype(BF16)
    rest_ref[...] = total[base + 2 * PIECE :].astype(BF16)


def shares_sum(pieces, after=()):
    return kernel_call(
        shares_kernel,
        "shares_sum",
        0.1,
        [pieces],
        [((8, 2 * PIECE, 128), BF16), ((SLICE, 128), BF16)],
        after=after,
    )


def whole_kernel(came_ref, rest_ref, out_ref):
    spare = came_ref[0, PIECE:].astype(F32)
    for i in range(1, 8):
        spare = spare + came_ref[i, PIECE:].astype(F32)
    rows = [came_ref[i, :PIECE] for i in range(8)] + [spare.astype(BF16), rest_ref[...]]
    rows = jnp.concatenate(rows, axis=0)
    for i in range(16):
        out_ref[i] = rows


def whole_pieces(came, rest, after=()):
    return kernel_call(
        whole_kernel,
        "whole_pieces",
        0.1,
        [came, rest],
        [((16, 9 * PIECE + SLICE, 128), BF16)],
        after=after,
    )[0]


def final_kernel(pieces_ref, wq_ref, wk_ref, wv_ref, gain_ref, *outs, experts):
    query_ref, key_ref, value_ref, output_ref, one_ref, two_ref, qg_ref, kg_ref, router_ref = outs
    rows = pieces_ref.shape[2]
    q_columns = query_ref.shape[1] // 8
    kv_columns = key_ref.shape[1] // 8
    sums = jnp.zeros((rows, 1), F32)
    base = 8 * PIECE
    for pair in range(4):
        keys, values = [], []
        for source in (2 * pair, 2 * pair + 1):
            block = [pieces_ref[i, source * PIECE : (source + 1) * PIECE] for i in range(16)]
            turned = jnp.concatenate(block, axis=0).astype(F32).T
            span = slice(source * q_columns, (source + 1) * q_columns)
            query = turned[:, :q_columns]
            query_ref[:, span] = query
            sums = sums + jnp.sum(query * wq_ref[:, span].astype(F32), axis=1, keepdims=True)
            keys.append(turned[:, q_columns : q_columns + kv_columns])
            values.append(turned[:, q_columns + kv_columns :])
        span = slice(2 * pair * kv_columns, 2 * (pair + 1) * kv_columns)
        for parts, ref, weight in ((keys, key_ref, wk_ref), (values, value_ref, wv_ref)):
            both = jnp.concatenate(parts, axis=1)
            ref[:, span] = both
            sums = sums + jnp.sum(both * weight[:, span].astype(F32), axis=1, keepdims=True)
    for i in range(16):
        half = i % 2 * SLICE
        output_ref[half : half + SLICE, i // 2 * rows : (i // 2 + 1) * rows] = pieces_ref[
            i, base + PIECE :
        ].astype(F32)
    spare = pieces_ref[:, base : base + PIECE].astype(F32)
    spare = jnp.concatenate([spare[i, :SPARE] for i in range(16)], axis=0)
    one_ref[...] = jnp.broadcast_to(sums, (rows, 128)).T[:1] / gain_ref[...].astype(F32)
    two_ref[...] = spare[experts : experts + 1]
    step = qg_ref.shape[1]
    qg_ref[...] = spare[experts + 1 : experts + 2, :step]
    kg_ref[...] = spare[experts + 2 : experts + 3, :step]
    router_ref[...] = spare[:experts]


def final_grads(pieces, wq, wk, wv, gain, experts):
    rows = pieces.shape[2]
    return kernel_call(
        functools.partial(final_kernel, experts=experts),
        "final_grads",
        0.2,
        [pieces, wq, wk, wv, gain],
        [
            (wq.shape, F32),
            (wk.shape, F32),
            (wv.shape, F32),
            ((rows, 8 * rows), F32),
            ((1, rows), F32),
            ((1, rows), F32),
            ((1, HEAD // 8), F32),
            ((1, HEAD // 8), F32),
            ((experts, rows), F32),
        ],
        held=(1, 2, 3, 4),
    )


def send(values, axis, flip):
    count = lax.axis_size(axis)
    return lax.ppermute(values, axis, [(i, i ^ flip) for i in range(count)])


def along_z(values):
    if not isinstance(values, (list, tuple)):
        values = [values] * 3
    return [send(value, "fsdp", 2 * (i + 1)) for i, value in enumerate(values)]


def gather_fsdp(block, name):
    came = along_z(block)
    return came, send(row([block, *came], name), "fsdp", 1)


def exchange(rows):
    return lax.all_to_all(rows, "expert", 0, 0, tiled=True)


def shards(
    tokens,
    lengths,
    routes,
    first_gain,
    query_weight,
    key_weight,
    value_weight,
    output_weight,
    query_gain,
    key_gain,
    second_gain,
    router_weight,
    gate_weight,
    up_weight,
    down_weight,
    cotangent,
):
    own = tokens[0]
    upstream = cotangent[0]
    rows, width = own.shape
    fsdp = lax.axis_size("fsdp")
    owners = lax.axis_size("expert")
    me = lax.axis_index("fsdp").astype(jnp.int32).reshape(1)
    owner = lax.axis_index("expert").astype(jnp.int32).reshape(1)
    experts = router_weight.shape[1]
    capacity = 3 * rows * routes.shape[2] // (2 * experts)
    kv_columns = key_weight.shape[1] // fsdp
    q_columns = query_weight.shape[1] // fsdp
    columns = q_columns + 2 * kv_columns
    q_heads = q_columns // HEAD

    ends = jnp.cumsum(lengths[0])
    place = jnp.arange(rows * fsdp, dtype=jnp.int32)
    start = jnp.max(jnp.where(ends[:, None] <= place[None, :], ends[:, None], 0), axis=0)
    position = (place - start).astype(F32)
    frequency = ROPE_BASE ** (-jnp.arange(HEAD // 2, dtype=F32) * 2.0 / HEAD)
    angles = frequency[:, None] * position[None, :]
    cosine, sine = jnp.cos(angles), jnp.sin(angles)
    start = start[None, :].astype(jnp.int32)

    packed, x_sends, dressed, mask = pack_weights(
        me,
        own,
        query_weight,
        key_weight,
        value_weight,
        router_weight.T,
        first_gain[None],
        second_gain[None],
        query_gain[None],
        key_gain[None],
        routes[0].T,
        upstream,
    )
    x_came = along_z(x_sends)
    x_other = [send(own, "fsdp", 1), send(packed[1], "fsdp", 1)]
    deal, turn, tick = slot_tables(mask, capacity)
    ready = (*x_other, tick, cosine, sine, start)
    x_other.append(send(relay(x_came, rows * fsdp, after=ready), "fsdp", 1))
    c_all = lax.all_gather(dressed, "expert", axis=0)
    wo_came = along_z(output_weight)

    h1, pre, keep, give, inverse, gains, heads, turned, mixed = attention_forward(
        me, own, packed[0], x_came, x_other, cosine, sine, start, experts, q_heads
    )
    other = send(give, "fsdp", 1)
    mixed_sends, wo_stack = merge(keep, other, output_weight, wo_came)
    mixed_came = along_z(mixed_sends)
    wo_other = send(wo_stack, "fsdp", 1)
    middle, probs, hidden, sent = middle_layer(
        own, keep, other, mixed_came, output_weight, wo_came, wo_other, gains, deal, experts, owners
    )
    h_rows = exchange(sent)
    rows_c, row_mask, back = deal_rows(owner, c_all, down_weight, experts, capacity)
    rows_back, gate_low, up_low, active, weighted, share = expert_layer(
        owner, h_rows, gains, row_mask, back, gate_weight, up_weight, experts
    )
    came_back = exchange(rows_back)
    grads, tick = expert_weights(h_rows, rows_c, gate_low, up_low, weighted)
    grads = lax.psum(grads, "fsdp")
    gate_sum, up_sum, down_sum = widen(grads)
    sent, tick = expert_outputs(active, share, down_weight, owners, after=(tick,))

    middle_grad, middle_low, extra = router_backward(
        came_back, turn, middle, probs, mask, gains, upstream, hidden, experts, after=(tick,)
    )
    da_came, da_other = gather_fsdp(middle_low, "row_middle")
    out_rows = exchange(sent)
    layer_out, _ = layer_output(out_rows, turn, middle)
    first, dh_keep, dh_give = attention_backward(
        me,
        middle_low,
        da_came,
        da_other,
        heads,
        output_weight,
        cosine,
        sine,
        start,
        h1,
        pre,
        mixed,
        inverse,
        turned,
        extra,
        experts,
        q_heads,
    )
    dh_total, *dh_sends = pair_sum(dh_keep, send(dh_give, "fsdp", 1))
    dh_came = along_z(dh_sends)
    tokens_grad = input_grad(dh_total, dh_came, own, gains, middle_grad, experts)
    first = passed(first, after=(out_rows, grads))
    parted, rest = shares_sum(exchange(first), after=(*dh_came, down_sum))
    parted = lax.all_to_all(parted, "fsdp", 0, 0, tiled=True)
    pieces = exchange(whole_pieces(parted, rest, after=(layer_out, tokens_grad)))
    query_sum, key_sum, value_sum, output_sum, one_sum, two_sum, *gain_sums, router_sum = final_grads(
        pieces, query_weight, key_weight, value_weight, first_gain[None], experts
    )
    return (
        layer_out[None],
        tokens_grad[None],
        one_sum[0],
        query_sum,
        key_sum,
        value_sum,
        output_sum,
        gain_sums[0][0],
        gain_sums[1][0],
        two_sum[0],
        router_sum.T,
        gate_sum,
        up_sum,
        down_sum,
    )


def solution(mesh):
    whole = P("expert", "fsdp", None)
    rows = P("fsdp", None)
    vector = P("fsdp")
    owned = P("expert", None, None)
    return jax.shard_map(
        shards,
        mesh=mesh,
        in_specs=(
            whole,
            P("expert", None),
            whole,
            vector,
            rows,
            rows,
            rows,
            rows,
            vector,
            vector,
            vector,
            rows,
            owned,
            owned,
            owned,
            whole,
        ),
        out_specs=(
            whole,
            whole,
            vector,
            rows,
            rows,
            rows,
            rows,
            vector,
            vector,
            vector,
            rows,
            owned,
            owned,
            owned,
        ),
        check_vma=False,
    )
```

```python
import functools

import jax
import jax.numpy as jnp
from jax import lax
from jax.experimental import pallas as pl
from jax.experimental.pallas import tpu as pltpu
from jax.sharding import PartitionSpec as P

EPSILON = 1e-06
ROPE_BASE = 10000.0
HEAD = 64
TILE = 256
F32 = jnp.float32
BF16 = jnp.bfloat16
VMEM = pl.BlockSpec(memory_space=pltpu.VMEM)
SMEM = pl.BlockSpec(memory_space=pltpu.SMEM)
ANY = pl.BlockSpec(memory_space=pl.ANY)
HBM = pl.BlockSpec(memory_space=pltpu.HBM)


def dot(left, right, dims=((1,), (0,))):
    return lax.dot_general(left, right, (dims, ((), ())), preferred_element_type=F32)


def shape(extent, dtype):
    return jax.ShapeDtypeStruct(extent, dtype)


def kernel_call(
    body, name, micros, operands, results, smem=0, hbm=(), out_hbm=(), after=(), scratch=(), held=(), late=(), stored=(), mib=63
):
    held = tuple(held) + tuple(late)
    n, a, r, s = len(operands), len(after), len(results), len(scratch)
    specs = [SMEM if i < smem else HBM if i in held or i in hbm else VMEM for i in range(n)]
    out_specs = [HBM if i in stored or i in out_hbm else VMEM for i in range(r)]
    staged = [pltpu.VMEM(operands[i].shape, operands[i].dtype) for i in held]
    staged += [pltpu.VMEM(*results[i]) for i in stored]
    sems = [pltpu.SemaphoreType.DMA((max(len(held), 1),)), pltpu.SemaphoreType.DMA((max(len(stored), 1),))]

    def wrapped(*refs):
        ins, outs = list(refs[:n]), list(refs[n + a : n + a + r])
        own = refs[n + a + r : n + a + r + s]
        stages, (load_sem, store_sem) = refs[n + a + r + s : -2], refs[-2:]
        loads, stores, begun = {}, {}, []
        for k, i in enumerate(held):
            loads[i] = pltpu.make_async_copy(ins[i], stages[k], load_sem.at[k])
            loads[i].start()
            ins[i] = stages[k]
        for k, i in enumerate(stored):
            stores[i] = pltpu.make_async_copy(stages[len(held) + k], outs[i], store_sem.at[k])
            outs[i] = stages[len(held) + k]
        for i in held:
            if i not in late:
                loads[i].wait()

        def store(*which):
            for i in which:
                stores[i].start()
                begun.append(i)

        extra = {}
        if late:
            extra["wait"] = lambda i: loads[i].wait()
        if stored:
            extra["store"] = store
        body(*ins, *outs, *own, **extra)
        store(*[i for i in stored if i not in begun])
        for i in stored:
            stores[i].wait()

    return pl.pallas_call(
        wrapped,
        out_shape=[shape(*result) for result in results],
        in_specs=specs + [ANY] * a,
        out_specs=out_specs,
        scratch_shapes=list(scratch) + staged + sems,
        compiler_params=pltpu.CompilerParams(vmem_limit_bytes=mib * 1024 * 1024),
        cost_estimate=pl.CostEstimate(flops=0, bytes_accessed=int(micros * 3.6e6), transcendentals=0),
        name=name,
    )(*operands, *after)


def move_call(moves, name, micros, operands, results, after=(), mib=10):
    def body(*refs):
        for source, target in moves(*refs):
            target[...] = source[...]

    return kernel_call(body, name, micros, operands, results, after=after, mib=mib)


def lane_blocks(value):
    return jnp.concatenate([value[:, i : i + 128] for i in range(0, value.shape[1], 128)], axis=0)


def joined_lanes(value, count):
    rows = value.shape[0] // count
    return jnp.concatenate([value[i * rows : (i + 1) * rows] for i in range(count)], axis=1)


def softmax_rows(logits):
    powers = jnp.exp(logits - jnp.max(logits, axis=0, keepdims=True))
    return powers / jnp.sum(powers, axis=0, keepdims=True)


def head_forward(pre, gain, cosine, sine):
    scale = lax.rsqrt(jnp.mean(pre * pre, axis=0, keepdims=True) + EPSILON)
    normed = pre * scale
    scaled = normed * gain
    a, b = scaled[: HEAD // 2], scaled[HEAD // 2 :]
    turned = jnp.concatenate([a * cosine - b * sine, b * cosine + a * sine], axis=0)
    return turned, normed, scale


def head_backward(grad, normed, scale, gain, cosine, sine):
    a, b = grad[: HEAD // 2], grad[HEAD // 2 :]
    unturned = jnp.concatenate([a * cosine + b * sine, b * cosine - a * sine], axis=0)
    gain_grad = jnp.sum(unturned * normed, axis=1, keepdims=True)
    inner = unturned * gain
    pre_grad = scale * (inner - normed * jnp.mean(inner * normed, axis=0, keepdims=True))
    return pre_grad, gain_grad


def slots_kernel(mask_ref, deal_ref, turn_ref, tick_ref, whole_ref, *, capacity, store):
    tick_ref[...] = jnp.zeros(tick_ref.shape, F32)
    experts, rows = mask_ref.shape
    mask = mask_ref[...]
    ranks = dot(mask.astype(BF16), earlier(rows))
    slot = lax.broadcasted_iota(jnp.int32, (capacity, rows), 0).astype(F32) + 1.0
    for expert in range(experts):
        one = slice(expert, expert + 1)
        whole_ref[expert * capacity : (expert + 1) * capacity] = jnp.where(
            (ranks[one] == slot) & (mask[one] > 0.5), 1.0, 0.0
        )
    deal_ref[...] = whole_ref[...].astype(BF16)
    store(0)
    for part in range(0, experts * capacity, 128):
        turn_ref[:, part : part + 128] = whole_ref[part : part + 128].T.astype(BF16)


def slot_tables(mask, capacity):
    experts, rows = mask.shape
    slots = experts * capacity
    return kernel_call(
        functools.partial(slots_kernel, capacity=capacity),
        "slot_tables",
        2.0,
        [mask],
        [((slots, rows), BF16), ((rows, slots), BF16), ((8, 128), F32)],
        scratch=[pltpu.VMEM((slots, rows), F32)],
        stored=(0, 1),
    )


def earlier(rows):
    return (
        lax.broadcasted_iota(jnp.int32, (rows, rows), 0)
        <= lax.broadcasted_iota(jnp.int32, (rows, rows), 1)
    ).astype(BF16)


def pack_kernel(
    me_ref, x_ref, wq_ref, wk_ref, wv_ref, router_ref, one_ref, two_ref, qg_ref, kg_ref, routes_ref, c_ref, *outs, wait, store
):
    own_ref, sends, dressed_ref, mask_ref, other_ref, parts_ref = outs[0], outs[1:4], *outs[4:]
    experts, rows = router_ref.shape
    wide = wq_ref.shape[1] // 8
    narrow = wk_ref.shape[1] // 8
    count = qg_ref.shape[1]
    heads = jnp.concatenate([qg_ref[...], kg_ref[...]], axis=0).astype(F32)
    heads = jnp.concatenate([heads, jnp.zeros((2, 128 - count), F32)], axis=1)
    heads = jnp.concatenate([heads, jnp.zeros((126, 128), F32)], axis=0).T[:count]
    small = jnp.concatenate(
        [
            router_ref[...].astype(F32),
            one_ref[...].astype(F32),
            two_ref[...].astype(F32),
            jnp.zeros((6, 128), F32),
            heads,
        ],
        axis=0,
    ).astype(BF16)
    for part in range(8):
        parts_ref[part, :wide] = wq_ref[:, part * wide : (part + 1) * wide].astype(F32).T.astype(BF16)
        parts_ref[part, wide + 2 * narrow :] = small
    for pair in range(4):
        span = slice(pair * 128, (pair + 1) * 128)
        for ref, place in ((wk_ref, wide), (wv_ref, wide + narrow)):
            turned = ref[:, span].astype(F32).T.astype(BF16)
            parts_ref[2 * pair, place : place + narrow] = turned[:narrow]
            parts_ref[2 * pair + 1, place : place + narrow] = turned[narrow:]
    me = me_ref[0]
    tall = parts_ref.shape[1]
    blocks = lane_blocks(x_ref[...])
    base = blocks.shape[0]
    own_ref[...] = parts_ref[me]
    other_ref[...] = parts_ref[me ^ 1]
    for flip in range(1, 4):
        sends[flip - 1][:base] = blocks
        sends[flip - 1][base : base + tall] = parts_ref[me ^ (2 * flip)]
        sends[flip - 1][base + tall :] = parts_ref[me ^ (2 * flip + 1)]
    store(1, 2, 3, 6, 0)
    wait(10)
    wait(11)
    width = c_ref.shape[1]
    subs = lax.broadcasted_iota(jnp.int32, (128, rows), 0)
    routed = jnp.zeros((128, rows), F32)
    for route in range(routes_ref.shape[0]):
        routed = routed + jnp.where(routes_ref[route : route + 1] == subs, 1.0, 0.0)
    dressed_ref[:, :width] = c_ref[...]
    dressed_ref[:, width:] = routed.T.astype(BF16)
    mask_ref[...] = routed[:experts]


def pack_weights(me, x, wq, wk, wv, router, one, two, qg, kg, routes, c):
    experts = router.shape[0]
    tall = (wq.shape[1] + wk.shape[1] + wv.shape[1]) // 8 + experts + 16
    rows, width = x.shape
    base = rows * 8
    own, first, second, third, dressed, mask, other = kernel_call(
        pack_kernel,
        "pack_weights",
        2.5,
        [me, x, wq, wk, wv, router, one, two, qg, kg, routes, c],
        [((tall, 128), BF16)]
        + [((base + 2 * tall, 128), BF16)] * 3
        + [((rows, width + 128), BF16), ((experts, rows), F32), ((tall, 128), BF16)],
        smem=1,
        scratch=[pltpu.VMEM((8, tall, 128), BF16)],
        held=range(1, 10),
        late=(10, 11),
        stored=(0, 1, 2, 3, 4, 5, 6),
    )
    return (own, other), [first, second, third], dressed, mask


def relay(came, base, after):
    tall = (came[0].shape[0] - base) // 2

    def moves(*refs):
        pairs = []
        for flip, ref in enumerate(refs[:3]):
            pairs.append((ref.at[:base], refs[3].at[flip, :base]))
            pairs.append((ref.at[base + tall :], refs[3].at[flip, base:]))
        return pairs

    return move_call(moves, "relay", 1.5, came, [((3, base + tall, 128), BF16)], after)[0]


def forward_kernel(me_ref, x_ref, own_ref, *refs, experts, q_heads, store):
    came, other_x, other_w, other_ref = refs[:3], refs[3], refs[4], refs[5]
    cos_ref, sin_ref, start_ref = refs[6:9]
    h1_ref, pre_ref, keep_ref, give_ref, inverse_ref, gains_ref, heads_ref, turned_ref, out_ref = refs[-9:]
    rows, width = x_ref.shape
    q_columns = q_heads * HEAD
    columns = q_columns + 2 * HEAD
    total = rows * 8
    tall = own_ref.shape[0]
    base = 8 * rows
    me = me_ref[0]
    for slot in range(8):
        flip = slot // 2
        if slot % 2:
            piece = other_ref[flip - 1, base:] if flip else other_w[...]
        elif flip:
            piece = came[flip - 1][base : base + tall]
        else:
            piece = own_ref[...]
        span = pl.ds(pl.multiple_of((me ^ slot) * rows, rows), rows)
        turned_ref[:, span] = piece[:columns]
        small = piece[columns:].astype(F32)
        gains_ref[:, span] = small[: experts + 8]
        heads_ref[pl.ds(pl.multiple_of((me ^ slot) * 8, 8), 8)] = small[experts + 8 :]
    gain_one = gains_ref[experts : experts + 1]
    for slot in range(8):
        flip = slot // 2
        if slot % 2:
            x = joined_lanes(other_ref[flip - 1, :base], 8) if flip else other_x[...]
        elif flip:
            x = joined_lanes(came[flip - 1][:base], 8)
        else:
            x = x_ref[...]
        x = x.astype(F32)
        scale = lax.rsqrt(jnp.mean(x * x, axis=1, keepdims=True) + EPSILON)
        h1_ref[slot] = (x * scale * gain_one).astype(BF16)
    store(0, 6, 7)
    for slot in range(8):
        block = dot(turned_ref[...], h1_ref[slot], ((1,), (1,)))
        place = pl.multiple_of((me ^ slot) * rows, rows)
        pre_ref[:, pl.ds(place, rows)] = block
    store(1)
    cosine, sine = cos_ref[...], sin_ref[...]
    gain_query, gain_key = heads_ref[:, :1], heads_ref[:, 1:2]
    key = head_forward(pre_ref[q_columns : q_columns + HEAD], gain_key, cosine, sine)[0]
    key = key.T.astype(BF16)
    value = pre_ref[q_columns + HEAD :].astype(BF16)
    inverse_ref[...] = jnp.zeros(inverse_ref.shape, F32)
    for head in range(q_heads):
        query = head_forward(pre_ref[head * HEAD : (head + 1) * HEAD], gain_query, cosine, sine)[0]
        query = query.astype(BF16) * jnp.array(HEAD ** (-0.5), BF16)
        for tile in range(total // TILE):
            low, high = tile * TILE, (tile + 1) * TILE
            scores = dot(key[:high], query[:, low:high])
            u = lax.broadcasted_iota(jnp.int32, (high, TILE), 0)
            t = lax.broadcasted_iota(jnp.int32, (high, TILE), 1) + low
            allowed = (u >= start_ref[:, low:high]) & (u <= t)
            powers = jnp.where(allowed, jnp.exp(scores), 0.0)
            inverse = 1.0 / jnp.sum(powers, axis=0, keepdims=True)
            probs = (powers * inverse).astype(BF16)
            mixed = dot(value[:, :high], probs).astype(BF16)
            inverse_ref[head : head + 1, low:high] = inverse
            for part in range(TILE // rows):
                out_ref[low // rows + part, head * HEAD : (head + 1) * HEAD] = mixed[
                    :, part * rows : (part + 1) * rows
                ]
    for slot in range(8):
        (give_ref if slot % 2 else keep_ref)[slot // 2] = out_ref[me ^ slot]


def attention_forward(me, x, own, came, other, cosine, sine, start, experts, q_heads, after=()):
    rows, width = x.shape
    total = 8 * rows
    columns = (q_heads + 2) * HEAD
    q_columns = q_heads * HEAD
    return kernel_call(
        functools.partial(forward_kernel, experts=experts, q_heads=q_heads),
        "attention_forward",
        7.0,
        [me, x, own, *came, *other, cosine, sine, start],
        [
            ((8, rows, width), BF16),
            ((columns, total), F32),
            ((4, q_columns, rows), BF16),
            ((4, q_columns, rows), BF16),
            ((8, total), F32),
            ((experts + 8, width), F32),
            ((HEAD, 128), F32),
            ((columns, width), BF16),
            ((8, q_columns, rows), BF16),
        ],
        smem=1,
        after=after,
        held=(1,),
        stored=(0, 1, 4, 6, 7, 8),
    )


def merge(keep, came, wo, wo_came):
    def moves(keep_ref, came_ref, *refs):
        weights, outs, stacked = refs[:4], refs[4:7], refs[7]
        pairs = [(weight, stacked.at[i]) for i, weight in enumerate(weights)]
        for flip in range(1, 4):
            pairs.append((keep_ref.at[flip], outs[flip - 1].at[0]))
            pairs.append((came_ref.at[flip], outs[flip - 1].at[1]))
        return pairs

    extent = ((2,) + keep.shape[1:], BF16)
    results = [extent] * 3 + [((4,) + wo.shape, BF16)]
    *sends, stacked = move_call(moves, "merge", 1.0, [keep, came, wo, *wo_came], results)
    return sends, stacked


def middle_kernel(x_ref, keep_ref, other_ref, *refs, experts, wait, store):
    came, wo_ref, wo_came, wo_other_ref, gains_ref, deal_ref = refs[:3], refs[3], refs[4:7], refs[7], refs[8], refs[9]
    middle_ref, probs_ref, hidden_ref, sent_ref, mixed_ref, whole_ref, out_ref, out_sem = refs[10:]
    rows, width = x_ref.shape
    for slot in range(8):
        flip, core = slot // 2, slot % 2
        if flip:
            piece = came[flip - 1][core]
        else:
            piece = (other_ref if core else keep_ref)[0]
        span = slice(slot * 128, (slot + 1) * 128)
        mixed_ref[:, span] = piece.astype(F32).T.astype(BF16)
    for i in (6, 7, 8, 9, 10):
        wait(i)
    for slot in range(8):
        flip = slot // 2
        span = slice(slot * 128, (slot + 1) * 128)
        if slot % 2:
            whole_ref[span] = wo_other_ref[flip]
        else:
            whole_ref[span] = (wo_came[flip - 1] if flip else wo_ref)[...]
    wait(0)
    middle = x_ref[...].astype(F32) + dot(mixed_ref[...], whole_ref[...])
    middle_ref[...] = middle
    scale = lax.rsqrt(jnp.mean(middle * middle, axis=1, keepdims=True) + EPSILON)
    hidden = (middle * scale * gains_ref[experts + 1 : experts + 2]).astype(BF16)
    hidden_ref[...] = hidden
    probs_ref[...] = softmax_rows(dot(gains_ref[:experts].astype(BF16), hidden, ((1,), (1,))))
    store(0, 2)
    owners, per_owner, capacity, _ = sent_ref.shape
    group = owners // 4
    size = group * per_owner * capacity
    copies = []
    wait(12)
    for part in range(4):
        taken = dot(deal_ref[part * size : (part + 1) * size], hidden).astype(BF16)
        blocks = slice(group * part, group * (part + 1))
        out_ref[blocks] = taken.reshape(group, per_owner, capacity, width)
        copies.append(pltpu.make_async_copy(out_ref.at[blocks], sent_ref.at[blocks], out_sem.at[part]))
        copies[-1].start()
    for copy in copies:
        copy.wait()


def middle_layer(x, keep, other, came, wo, wo_came, wo_other, gains, deal, experts, owners):
    rows, width = x.shape
    per_owner = experts // owners
    capacity = deal.shape[0] // experts
    sent = ((owners, per_owner, capacity, width), BF16)
    return kernel_call(
        functools.partial(middle_kernel, experts=experts),
        "middle_layer",
        3.0,
        [x, keep, other, *came, wo, *wo_came, wo_other, gains, deal],
        [((rows, width), F32), ((experts, rows), F32), ((rows, width), BF16), sent],
        out_hbm=(3,),
        scratch=[
            pltpu.VMEM((rows, width), BF16),
            pltpu.VMEM((width, width), BF16),
            pltpu.VMEM(*sent),
            pltpu.SemaphoreType.DMA((4,)),
        ],
        late=(6, 7, 8, 9, 10, 0, 12),
        stored=(0, 2),
    )


def row(pieces, name):
    def moves(*refs):
        return [(ref, refs[-1].at[i]) for i, ref in enumerate(refs[:-1])]

    return move_call(moves, name, 1.0, pieces, [((len(pieces),) + pieces[0].shape, BF16)])[0]


def backward_kernel(me_ref, own_da_ref, *refs, experts, q_heads, wait):
    came, other_ref = refs[:3], refs[3]
    heads_ref, wo_ref, cos_ref, sin_ref, start_ref = refs[4:9]
    h1_ref, pre_ref, mixed_ref, inverse_ref, turned_ref, extra_ref = refs[9:15]
    first_ref, keep_ref, send_ref = refs[-10:-7]
    da_ref, mixed_grad_ref, dkey_ref, dvalue_ref, low_ref, out_slots_ref, grad_ref = refs[-7:]
    rows, width = own_da_ref.shape
    q_columns = q_heads * HEAD
    columns = q_columns + 2 * HEAD
    total = rows * 8
    me = me_ref[0]
    for slot in range(8):
        flip, core = slot // 2, slot % 2
        if core:
            piece = other_ref[flip]
        else:
            piece = (came[flip - 1] if flip else own_da_ref)[...]
        span = slice(slot * rows, (slot + 1) * rows)
        da_ref[span] = piece
        place = pl.multiple_of((me ^ slot) * rows, rows)
        mixed_grad_ref[:, pl.ds(place, rows)] = dot(wo_ref[...], piece, ((1,), (1,))).astype(BF16)
    wait(13)
    for slot in range(8):
        out_slots_ref[:, slot * rows : (slot + 1) * rows] = mixed_ref[me ^ slot]
    wo_grad = dot(out_slots_ref[...], da_ref[...]).astype(BF16)
    wo_grad = lane_blocks(wo_grad)
    wait(12)
    wait(14)
    gain_query, gain_key = heads_ref[:, :1], heads_ref[:, 1:2]
    cosine, sine = cos_ref[...], sin_ref[...]
    key_turned, key_normed, key_scale = head_forward(
        pre_ref[q_columns : q_columns + HEAD], gain_key, cosine, sine
    )
    key_low = key_turned.astype(BF16)
    key = key_turned.T.astype(BF16)
    value = pre_ref[q_columns + HEAD :].T.astype(BF16)
    dkey_ref[...] = jnp.zeros(dkey_ref.shape, F32)
    dvalue_ref[...] = jnp.zeros(dvalue_ref.shape, F32)
    gain_query_grad = jnp.zeros((HEAD, 1), F32)
    pieces = []
    for head in range(q_heads):
        span = slice(head * HEAD, (head + 1) * HEAD)
        turned, normed, scale = head_forward(pre_ref[span], gain_query, cosine, sine)
        query = turned.astype(BF16) * jnp.array(HEAD ** (-0.5), BF16)
        grads = []
        for tile in range(total // TILE):
            low, high = tile * TILE, (tile + 1) * TILE
            part = query[:, low:high]
            mixed_grad = mixed_grad_ref[span, low:high]
            scores = dot(key[:high], part)
            u = lax.broadcasted_iota(jnp.int32, (high, TILE), 0)
            t = lax.broadcasted_iota(jnp.int32, (high, TILE), 1) + low
            allowed = (u >= start_ref[:, low:high]) & (u <= t)
            probs = jnp.where(allowed, jnp.exp(scores) * inverse_ref[head : head + 1, low:high], 0.0)
            attend = dot(value[:high], mixed_grad)
            delta = jnp.sum(probs * attend, axis=0, keepdims=True)
            score_low = (probs * (attend - delta)).astype(BF16)
            grads.append(dot(key_low[:, :high], score_low))
            dkey_ref[:, :high] += dot(part, score_low, ((1,), (1,)))
            dvalue_ref[:, :high] += dot(mixed_grad, probs.astype(BF16), ((1,), (1,)))
        query_grad = jnp.concatenate(grads, axis=1) * HEAD ** (-0.5)
        pre_grad, gain_grad = head_backward(query_grad, normed, scale, gain_query, cosine, sine)
        gain_query_grad += gain_grad
        pieces.append(pre_grad)
    pre_grad, gain_key_grad = head_backward(
        dkey_ref[...], key_normed, key_scale, gain_key, cosine, sine
    )
    pieces += [pre_grad, dvalue_ref[...]]
    pre_grad = jnp.concatenate(pieces, axis=0)
    low_ref[...] = pre_grad.astype(BF16)
    slots_grad = []
    for slot in range(8):
        place = pl.multiple_of((me ^ slot) * rows, rows)
        slots_grad.append(low_ref[:, pl.ds(place, rows)])
    slots_grad = jnp.concatenate(slots_grad, axis=1)
    wait(11)
    wait(15)
    grad_ref[:columns] = dot(slots_grad, h1_ref[...].reshape(total, width))
    extra = extra_ref[...]
    lane = lax.broadcasted_iota(jnp.int32, (HEAD, 128), 1)
    gains = jnp.where(lane == 0, gain_query_grad, jnp.where(lane == 1, gain_key_grad, 0.0))
    gains = gains.T[:2]
    step = HEAD // 8
    grad_ref[columns:] = jnp.zeros((64, width), F32)
    grad_ref[columns : columns + experts + 1] = extra[: experts + 1]
    for part in range(8):
        grad_ref[columns + experts + 1 : columns + experts + 3, part * rows : part * rows + step] = gains[
            :, part * step : (part + 1) * step
        ]
    for piece in range(16):
        spare = []
        place = columns + piece * SPARE
        for part in range(8):
            span = slice(part * rows, (part + 1) * rows)
            block = grad_ref[piece * PIECE : (piece + 1) * PIECE, span]
            first_ref[piece, part * PIECE : (part + 1) * PIECE] = block.astype(BF16)
            spare.append(grad_ref[place : place + SPARE, span])
        spare.append(jnp.zeros((2 * PIECE - 8 * SPARE, 128), F32))
        first_ref[piece, 8 * PIECE : 10 * PIECE] = jnp.concatenate(spare, axis=0).astype(BF16)
        first_ref[piece, 10 * PIECE :] = wo_grad[piece * SLICE : (piece + 1) * SLICE]
    turned = turned_ref[...]
    for slot in range(8):
        low_rows_slot = slots_grad[:, slot * rows : (slot + 1) * rows].astype(F32).T.astype(BF16)
        part = dot(low_rows_slot, turned)
        if slot % 2:
            send_ref[slot // 2] = part.astype(BF16)
        else:
            keep_ref[slot // 2] = part


def attention_backward(
    me, da, came, other, heads, wo, cosine, sine, start, h1, pre, mixed, inverse, turned, extra, experts, q_heads, after=()
):
    rows, width = da.shape
    total = 8 * rows
    columns = pre.shape[0]
    q_columns = q_heads * HEAD
    return kernel_call(
        functools.partial(backward_kernel, experts=experts, q_heads=q_heads),
        "attention_backward",
        12,
        [me, da, *came, other, heads, wo, cosine, sine, start, h1, pre, mixed, inverse, turned, extra],
        [
            ((16, 10 * PIECE + SLICE, 128), BF16),
            ((4, rows, width), F32),
            ((4, rows, width), BF16),
        ],
        smem=1,
        after=after,
        held=(6, 7),
        late=(11, 12, 13, 14, 15),
        scratch=[
            pltpu.VMEM((total, width), BF16),
            pltpu.VMEM((q_columns, total), BF16),
            pltpu.VMEM((HEAD, total), F32),
            pltpu.VMEM((HEAD, total), F32),
            pltpu.VMEM((columns, total), BF16),
            pltpu.VMEM((q_columns, total), BF16),
            pltpu.VMEM((columns + 64, width), F32),
        ],
    )


def deal_kernel(owner_ref, c_ref, down_ref, rows_c, mask_ref, back_ref, c_scratch, sems, *, experts, capacity, wait, store):
    owner = owner_ref[0]
    per_owner, hidden, width = down_ref.shape
    rows = c_ref.shape[1]
    loads = [pltpu.make_async_copy(c_ref.at[i], c_scratch.at[i], sems.at[i]) for i in range(16)]
    for load in loads:
        load.start()
    lanes = lax.broadcasted_iota(jnp.int32, (experts, 128), 1)
    subs = lax.broadcasted_iota(jnp.int32, (experts, 128), 0)
    eye = (lanes == subs).astype(BF16)
    before = earlier(rows)
    mine_of = lax.broadcasted_iota(jnp.int32, (experts, rows), 0) - owner * per_owner
    slot = lax.broadcasted_iota(jnp.int32, (capacity, rows), 0).astype(F32) + 1.0
    for block in range(16):
        loads[block].wait()
        c = c_scratch[block]
        mask = dot(eye, c[:, width:], ((1,), (1,)))
        ranks = dot(mask.astype(BF16), before)
        deals = []
        for k in range(per_owner):
            mine = mine_of == k
            hit = jnp.sum(jnp.where(mine, mask, 0.0), axis=0, keepdims=True)
            rank = jnp.sum(jnp.where(mine, ranks, 0.0), axis=0, keepdims=True)
            deals.append(jnp.where((rank == slot) & (hit > 0.5), 1.0, 0.0))
        taken = dot(jnp.concatenate(deals, axis=0).astype(BF16), c).astype(BF16)
        span = slice(block * capacity, (block + 1) * capacity)
        for k in range(per_owner):
            spot = slice(k * capacity, (k + 1) * capacity)
            rows_c[k, span] = taken[spot, :width]
            mask_ref[k, span] = taken[spot, width:]
    store(0, 1)
    wait(2)
    for k in range(per_owner):
        for tile in range(16 * capacity // TILE):
            span = slice(tile * TILE, (tile + 1) * TILE)
            back_ref[k, span] = dot(rows_c[k, span], down_ref[k], ((1,), (1,)))


def deal_rows(owner, c, down, experts, capacity):
    per_owner, hidden, width = down.shape
    count = 16 * capacity
    return kernel_call(
        functools.partial(deal_kernel, experts=experts, capacity=capacity),
        "deal_rows",
        12.0,
        [owner, c, down],
        [
            ((per_owner, count, width), BF16),
            ((per_owner, count, 128), BF16),
            ((per_owner, count, hidden), F32),
        ],
        smem=1,
        hbm=(1,),
        scratch=[pltpu.VMEM(c.shape, BF16), pltpu.SemaphoreType.DMA((16,))],
        late=(2,),
        stored=(0, 1, 2),
    )


def expert_kernel(
    owner_ref,
    h_hbm,
    gains_ref,
    mask_ref,
    back_hbm,
    gate_hbm,
    up_hbm,
    rows_hbm,
    gate_out,
    up_out,
    active_out,
    weighted_out,
    share_ref,
    h_ref,
    back_in,
    gate_ref,
    up_ref,
    rows_back,
    gate_sum,
    up_sum,
    logit_sum,
    spread_ref,
    load_sem,
    store_sem,
    *,
    experts,
    store,
):
    owners, per_owner, capacity, width = h_hbm.shape
    group = 8
    parts = owners // group
    size = group * capacity
    loads = {}
    for k in range(per_owner):
        for part in range(parts):
            blocks = slice(part * group, (part + 1) * group)
            spot = (k * parts + part) * 4
            loads[k, part] = [
                pltpu.make_async_copy(h_hbm.at[blocks, k], h_ref.at[blocks, k], load_sem.at[spot]),
                pltpu.make_async_copy(
                    back_hbm.at[k, part * size : (part + 1) * size],
                    back_in.at[k, part * size : (part + 1) * size],
                    load_sem.at[spot + 1],
                ),
            ]
            if part == 0:
                loads[k, part] += [
                    pltpu.make_async_copy(gate_hbm.at[k], gate_ref.at[k], load_sem.at[spot + 2]),
                    pltpu.make_async_copy(up_hbm.at[k], up_ref.at[k], load_sem.at[spot + 3]),
                ]
            for load in loads[k, part]:
                load.start()
    owner = owner_ref[0]
    router = jnp.concatenate([gains_ref[:experts], jnp.zeros((128 - experts, width), F32)], axis=0)
    router = router.astype(BF16)
    lane = lax.broadcasted_iota(jnp.int32, (size, 128), 1)
    copies = []
    chunk = capacity
    lane = lane[:chunk]
    order = [(k, part) for k in range(per_owner) for part in range(parts)]

    def begin(i):
        k, part = order[i]
        blocks = slice(part * group, (part + 1) * group)
        for load in loads[k, part]:
            load.wait()
        h = h_ref[blocks, k].reshape(size, width)
        gate_sum[i % 2] = dot(h, gate_ref[k])
        up_sum[i % 2] = dot(h, up_ref[k])
        logit_sum[i % 2] = dot(h, router, ((1,), (1,)))

    begin(0)
    for i, (k, part) in enumerate(order):
        if i + 1 < len(order):
            begin(i + 1)
        place = owner * per_owner + k
        blocks = slice(part * group, (part + 1) * group)
        span = slice(part * size, (part + 1) * size)
        for spot in range(0, size, chunk):
            here = slice(part * size + spot, part * size + spot + chunk)
            near = slice(spot, spot + chunk)
            logits = logit_sum[i % 2, near]
            chosen = mask_ref[k, here] > 0.5
            top = jnp.max(jnp.where(chosen, logits, -1e30), axis=1, keepdims=True)
            powers = jnp.where(chosen, jnp.exp(logits - top), 0.0)
            total = jnp.sum(powers, axis=1, keepdims=True)
            share = jnp.sum(jnp.where(lane == place, powers, 0.0), axis=1, keepdims=True)
            share = share / jnp.where(total > 0.0, total, 1.0)
            share_ref[k, here] = jnp.broadcast_to(share, (chunk, 128))
            gate, up, back = gate_sum[i % 2, near], up_sum[i % 2, near], back_in[k, here]
            sig = 1.0 / (1.0 + jnp.exp(-gate))
            silu = gate * sig
            active = silu * up
            active_low = active.astype(BF16)
            route_grad = jnp.sum(active_low.astype(F32) * back, axis=1, keepdims=True)
            grad = back * share
            gate_out[k, here] = (grad * up * (sig + silu * (1.0 - sig))).astype(BF16)
            up_out[k, here] = (grad * silu).astype(BF16)
            active_out[k, here] = active_low
            weighted_out[k, here] = (active * share).astype(BF16)
            high = route_grad.astype(BF16).astype(F32)
            spread_out = jnp.where(lane == place, high, 0.0)
            spread_out = jnp.where(lane == place + experts, route_grad - high, spread_out)
            spread_ref[near] = spread_out.astype(BF16)
        rows = dot(gate_out[k, span], gate_ref[k], ((1,), (1,))) + dot(up_out[k, span], up_ref[k], ((1,), (1,)))
        rows_back[blocks, k, :, :width] = rows.astype(BF16).reshape(group, capacity, width)
        rows_back[blocks, k, :, width:] = spread_ref[...].reshape(group, capacity, 128)
        copies.append(
            pltpu.make_async_copy(rows_back.at[blocks, k], rows_hbm.at[blocks, k], store_sem.at[k * parts + part])
        )
        copies[-1].start()
    store(1, 2, 3, 4, 5)
    for copy in copies:
        copy.wait()


def expert_layer(owner, h, gains, mask, back, gate, up, experts):
    per_owner, width, hidden = gate.shape
    owners, _, capacity, _ = h.shape
    count = owners * capacity
    narrow = ((per_owner, count, hidden), BF16)
    rows_back = ((owners, per_owner, capacity, width + 128), BF16)
    pieces = per_owner * (owners // 8)
    return kernel_call(
        functools.partial(expert_kernel, experts=experts),
        "expert_layer",
        14.0,
        [owner, h, gains, mask, back, gate, up],
        [rows_back] + [narrow] * 4 + [((per_owner, count, 128), F32)],
        smem=1,
        hbm=(1, 4, 5, 6),
        out_hbm=(0,),
        scratch=[pltpu.VMEM(value.shape, value.dtype) for value in (h, back, gate, up)]
        + [pltpu.VMEM(*rows_back)]
        + [pltpu.VMEM((2, 8 * capacity, n), F32) for n in (hidden, hidden, 128)]
        + [pltpu.VMEM((8 * capacity, 128), BF16)]
        + [pltpu.SemaphoreType.DMA((4 * pieces,)), pltpu.SemaphoreType.DMA((pieces,))],
        stored=(1, 2, 3, 4, 5),
    )


def weights_kernel(
    h_hbm, rows_c, gate_low, up_low, weighted, out_hbm, tick_ref, h_ref, out_ref, load_sem, store_sem, *, wait
):
    tick_ref[...] = jnp.zeros(tick_ref.shape, F32)
    first = ((0,), (0,))
    owners, per_owner, capacity, width = h_hbm.shape
    hidden = gate_low.shape[2]
    half = width // 2
    loads = [
        pltpu.make_async_copy(h_hbm.at[:, k], h_ref.at[:, k], load_sem.at[k]) for k in range(per_owner)
    ]
    for load in loads:
        load.start()
    stores = []

    def keep(place):
        stores.append(pltpu.make_async_copy(out_ref.at[place], out_hbm.at[place], store_sem.at[place]))
        stores[-1].start()

    wait(2)
    for k in range(per_owner):
        loads[k].wait()
        rows_h = h_ref[:, k].reshape(owners * capacity, width)
        for place, low in ((k, gate_low), (per_owner + k, up_low)):
            if k == 0 and place:
                wait(3)
            total = dot(rows_h, low[k], first).astype(BF16)
            out_ref[place, :, :hidden] = total[:half]
            out_ref[place, :, hidden:] = total[half:]
            keep(place)
        if k == 0:
            wait(4)
            wait(1)
        place = 2 * per_owner + k
        out_ref[place] = dot(weighted[k], rows_c[k], first).astype(BF16)
        keep(place)
    for store in stores:
        store.wait()


def expert_weights(h, rows_c, gate_low, up_low, weighted):
    per_owner, count, width = rows_c.shape
    hidden = gate_low.shape[2]
    out = ((3 * per_owner, hidden, width), BF16)
    return kernel_call(
        weights_kernel,
        "expert_weights",
        0.1,
        [h, rows_c, gate_low, up_low, weighted],
        [out, ((8, 128), F32)],
        hbm=(0,),
        out_hbm=(0,),
        scratch=[
            pltpu.VMEM(h.shape, BF16),
            pltpu.VMEM(*out),
            pltpu.SemaphoreType.DMA((per_owner,)),
            pltpu.SemaphoreType.DMA((3 * per_owner,)),
        ],
        late=(2, 3, 4, 1),
    )


def widen_kernel(low_ref, gate_ref, up_ref, down_ref):
    step = pl.program_id(0)
    hidden = gate_ref.shape[2]
    value = low_ref[0].astype(F32)
    half = value.shape[0]
    for place, ref in ((0, gate_ref), (1, up_ref)):

        @pl.when(step // 2 == place)
        def _():
            ref[0, :half] = value[:, :hidden]
            ref[0, half:] = value[:, hidden:]

    @pl.when(step // 2 == 2)
    def _():
        down_ref[0] = value


def widen(low):
    count, hidden, width = low.shape
    per_owner = count // 3

    def spot(place):
        return lambda i: (jnp.clip(i - place * per_owner, 0, per_owner - 1), 0, 0)

    return pl.pallas_call(
        widen_kernel,
        grid=(count,),
        out_shape=[shape((per_owner, width, hidden), F32)] * 2 + [shape((per_owner, hidden, width), F32)],
        in_specs=[pl.BlockSpec((1, hidden, width), lambda i: (i, 0, 0))],
        out_specs=[
            pl.BlockSpec((1, width, hidden), spot(0)),
            pl.BlockSpec((1, width, hidden), spot(1)),
            pl.BlockSpec((1, hidden, width), spot(2)),
        ],
        compiler_params=pltpu.CompilerParams(vmem_limit_bytes=63 * 1024 * 1024),
        cost_estimate=pl.CostEstimate(flops=0, bytes_accessed=24_000_000, transcendentals=0),
        name="widen",
    )(low)


def outputs_kernel(active, share, down_ref, sent_ref, tick_ref, out_ref, out_sem, *, wait):
    tick_ref[...] = jnp.zeros(tick_ref.shape, F32)
    per_owner, count, hidden = active.shape
    owners, _, capacity, width = sent_ref.shape
    group = 8
    size = group * capacity
    copies = []
    for i in range(3):
        wait(i)
    for k in range(per_owner):
        for part in range(owners // group):
            span = slice(part * size, (part + 1) * size)
            blocks = slice(part * group, (part + 1) * group)
            produced = dot(active[k, span], down_ref[k]).astype(BF16).astype(F32)
            produced = (produced * share[k, span, :1]).astype(BF16)
            out_ref[blocks, k] = produced.reshape(group, capacity, width)
            copies.append(
                pltpu.make_async_copy(
                    out_ref.at[blocks, k], sent_ref.at[blocks, k], out_sem.at[k * (owners // group) + part]
                )
            )
            copies[-1].start()
    for copy in copies:
        copy.wait()


def expert_outputs(active, share, down, owners, after=()):
    per_owner, count, hidden = active.shape
    width = down.shape[2]
    sent = ((owners, per_owner, count // owners, width), BF16)
    return kernel_call(
        outputs_kernel,
        "expert_outputs",
        0.1,
        [active, share, down],
        [sent, ((8, 128), F32)],
        out_hbm=(0,),
        after=after,
        scratch=[pltpu.VMEM(*sent), pltpu.SemaphoreType.DMA((per_owner * (owners // 8),))],
        late=(0, 1, 2),
    )


def combined(rows_hbm, rows_ref, sems, turn_ref, ready):
    owners, per_owner, capacity, wide = rows_hbm.shape
    group = owners // 4
    size = group * per_owner * capacity
    loads = []
    for part in range(4):
        blocks = slice(part * group, (part + 1) * group)
        loads.append(pltpu.make_async_copy(rows_hbm.at[blocks], rows_ref.at[blocks], sems.at[part]))
        loads[-1].start()
    ready()
    total = None
    for part in range(4):
        loads[part].wait()
        rows = rows_ref[part * group : (part + 1) * group].reshape(size, wide)
        one = dot(turn_ref[:, part * size : (part + 1) * size], rows)
        total = one if total is None else total + one
    return total


def output_kernel(rows_hbm, turn_ref, middle_ref, out_ref, tick_ref, rows_ref, sems, *, wait, store):
    tick_ref[...] = jnp.zeros(tick_ref.shape, F32)
    total = combined(rows_hbm, rows_ref, sems, turn_ref, lambda: wait(1))
    wait(2)
    out_ref[...] = (middle_ref[...] + total).astype(BF16)


def layer_output(rows, turn, middle):
    return kernel_call(
        output_kernel,
        "layer_output",
        3,
        [rows, turn, middle],
        [(middle.shape, BF16), ((8, 128), F32)],
        hbm=(0,),
        scratch=[pltpu.VMEM(rows.shape, BF16), pltpu.SemaphoreType.DMA((4,))],
        late=(1, 2),
        stored=(0,),
    )


def router_kernel(
    rows_hbm,
    turn_ref,
    middle_ref,
    probs_ref,
    mask_ref,
    gains_ref,
    c_ref,
    hidden_ref,
    grad_ref,
    send_ref,
    extra_ref,
    rows_ref,
    sems,
    *,
    experts,
    wait,
    store,
):
    rows, width = middle_ref.shape
    returned = combined(rows_hbm, rows_ref, sems, turn_ref, lambda: wait(1))
    for i in (2, 4, 6, 7):
        wait(i)
    tail = returned[:, width:].T
    route_grad = tail[:experts] + tail[experts : 2 * experts]
    mask = mask_ref[...]
    probs = probs_ref[...]
    picked = probs * mask
    picked_sum = jnp.sum(picked, axis=0, keepdims=True)
    share = picked / picked_sum
    picked_grad = (route_grad - jnp.sum(route_grad * share, axis=0, keepdims=True)) / picked_sum
    prob_grad = mask * picked_grad
    logit_grad = probs * (prob_grad - jnp.sum(probs * prob_grad, axis=0, keepdims=True))
    extra_ref[:experts] = dot(logit_grad.astype(BF16), hidden_ref[...])
    logit_rows = jnp.concatenate([logit_grad, jnp.zeros((128 - experts, rows), F32)], axis=0).T
    router = gains_ref[:experts].astype(BF16)
    hidden_grad = returned[:, :width] + dot(logit_rows[:, :experts].astype(BF16), router)
    middle = middle_ref[...]
    scale = lax.rsqrt(jnp.mean(middle * middle, axis=1, keepdims=True) + EPSILON)
    normed = middle * scale
    extra_ref[experts : experts + 8] = jnp.broadcast_to(
        jnp.sum(hidden_grad * normed, axis=0, keepdims=True), (8, width)
    )
    inner = hidden_grad * gains_ref[experts + 1 : experts + 2]
    grad = c_ref[...].astype(F32) + scale * (
        inner - normed * jnp.mean(inner * normed, axis=1, keepdims=True)
    )
    grad_ref[...] = grad
    send_ref[...] = grad.astype(BF16)


def router_backward(rows_back, turn, middle, probs, mask, gains, c, hidden, experts, after=()):
    rows, width = middle.shape
    return kernel_call(
        functools.partial(router_kernel, experts=experts),
        "router_backward",
        5,
        [rows_back, turn, middle, probs, mask, gains, c, hidden],
        [((rows, width), F32), ((rows, width), BF16), ((experts + 8, width), F32)],
        hbm=(0,),
        after=after,
        scratch=[pltpu.VMEM(rows_back.shape, BF16), pltpu.SemaphoreType.DMA((4,))],
        late=(1, 2, 4, 6, 7),
        stored=(0,),
    )


def pair_kernel(keep_ref, other_ref, total_ref, *sends):
    for flip in range(4):
        total = keep_ref[flip] + other_ref[flip].astype(F32)
        if flip:
            sends[flip - 1][...] = total.astype(BF16)
        else:
            total_ref[...] = total


def pair_sum(keep, other):
    rows, width = keep.shape[1:]
    return kernel_call(
        pair_kernel, "pair_sum", 1.2, [keep, other], [((rows, width), F32)] + [((rows, width), BF16)] * 3
    )


def input_kernel(total_ref, *refs, experts, store):
    came = refs[:3]
    x_ref, gains_ref, middle_grad_ref, out_ref = refs[3:]
    total = total_ref[...]
    for piece in came:
        total = total + piece[...].astype(F32)
    x = x_ref[...].astype(F32)
    scale = lax.rsqrt(jnp.mean(x * x, axis=1, keepdims=True) + EPSILON)
    normed = x * scale
    inner = total * gains_ref[experts : experts + 1]
    out_ref[...] = middle_grad_ref[...] + scale * (
        inner - normed * jnp.mean(inner * normed, axis=1, keepdims=True)
    )


def input_grad(total, came, x, gains, middle_grad, experts):
    return kernel_call(
        functools.partial(input_kernel, experts=experts),
        "input_grad",
        2,
        [total, *came, x, gains, middle_grad],
        [(middle_grad.shape, F32)],
        held=(4, 6),
        stored=(0,),
    )[0]


PIECE, SPARE, SLICE = 16, 3, 64


def passed(value, after):
    results = [(value.shape, value.dtype)]
    return move_call(lambda *refs: [refs], "passed", 0.5, [value], results, after, 63)[0]


def shares_kernel(pieces_ref, out_ref, rest_ref):
    total = pieces_ref[0].astype(F32)
    for i in range(1, pieces_ref.shape[0]):
        total = total + pieces_ref[i].astype(F32)
    base = 8 * PIECE
    fill = jnp.zeros((PIECE - SPARE, 128), F32)
    for part in range(8):
        out_ref[part, :PIECE] = total[part * PIECE : (part + 1) * PIECE].astype(BF16)
        spare = total[base + part * SPARE : base + (part + 1) * SPARE]
        out_ref[part, PIECE:] = jnp.concatenate([spare, fill], axis=0).astype(BF16)
    rest_ref[...] = total[base + 2 * PIECE :].astype(BF16)


def shares_sum(pieces, after=()):
    return kernel_call(
        shares_kernel,
        "shares_sum",
        0.1,
        [pieces],
        [((8, 2 * PIECE, 128), BF16), ((SLICE, 128), BF16)],
        after=after,
    )


def whole_kernel(came_ref, rest_ref, out_ref):
    spare = came_ref[0, PIECE:].astype(F32)
    for i in range(1, 8):
        spare = spare + came_ref[i, PIECE:].astype(F32)
    rows = [came_ref[i, :PIECE] for i in range(8)] + [spare.astype(BF16), rest_ref[...]]
    rows = jnp.concatenate(rows, axis=0)
    for i in range(16):
        out_ref[i] = rows


def whole_pieces(came, rest, after=()):
    return kernel_call(
        whole_kernel,
        "whole_pieces",
        0.1,
        [came, rest],
        [((16, 9 * PIECE + SLICE, 128), BF16)],
        after=after,
    )[0]


def final_kernel(pieces_ref, wq_ref, wk_ref, wv_ref, gain_ref, *outs, experts):
    query_ref, key_ref, value_ref, output_ref, one_ref, two_ref, qg_ref, kg_ref, router_ref = outs
    rows = pieces_ref.shape[2]
    q_columns = query_ref.shape[1] // 8
    kv_columns = key_ref.shape[1] // 8
    sums = jnp.zeros((rows, 1), F32)
    base = 8 * PIECE
    for pair in range(4):
        keys, values = [], []
        for source in (2 * pair, 2 * pair + 1):
            block = [pieces_ref[i, source * PIECE : (source + 1) * PIECE] for i in range(16)]
            turned = jnp.concatenate(block, axis=0).astype(F32).T
            span = slice(source * q_columns, (source + 1) * q_columns)
            query = turned[:, :q_columns]
            query_ref[:, span] = query
            sums = sums + jnp.sum(query * wq_ref[:, span].astype(F32), axis=1, keepdims=True)
            keys.append(turned[:, q_columns : q_columns + kv_columns])
            values.append(turned[:, q_columns + kv_columns :])
        span = slice(2 * pair * kv_columns, 2 * (pair + 1) * kv_columns)
        for parts, ref, weight in ((keys, key_ref, wk_ref), (values, value_ref, wv_ref)):
            both = jnp.concatenate(parts, axis=1)
            ref[:, span] = both
            sums = sums + jnp.sum(both * weight[:, span].astype(F32), axis=1, keepdims=True)
    for i in range(16):
        half = i % 2 * SLICE
        output_ref[half : half + SLICE, i // 2 * rows : (i // 2 + 1) * rows] = pieces_ref[
            i, base + PIECE :
        ].astype(F32)
    spare = pieces_ref[:, base : base + PIECE].astype(F32)
    spare = jnp.concatenate([spare[i, :SPARE] for i in range(16)], axis=0)
    one_ref[...] = jnp.broadcast_to(sums, (rows, 128)).T[:1] / gain_ref[...].astype(F32)
    two_ref[...] = spare[experts : experts + 1]
    step = qg_ref.shape[1]
    qg_ref[...] = spare[experts + 1 : experts + 2, :step]
    kg_ref[...] = spare[experts + 2 : experts + 3, :step]
    router_ref[...] = spare[:experts]


def final_grads(pieces, wq, wk, wv, gain, experts):
    rows = pieces.shape[2]
    return kernel_call(
        functools.partial(final_kernel, experts=experts),
        "final_grads",
        0.2,
        [pieces, wq, wk, wv, gain],
        [
            (wq.shape, F32),
            (wk.shape, F32),
            (wv.shape, F32),
            ((rows, 8 * rows), F32),
            ((1, rows), F32),
            ((1, rows), F32),
            ((1, HEAD // 8), F32),
            ((1, HEAD // 8), F32),
            ((experts, rows), F32),
        ],
        held=(1, 2, 3, 4),
    )


def send(values, axis, flip):
    count = lax.axis_size(axis)
    return lax.ppermute(values, axis, [(i, i ^ flip) for i in range(count)])


def along_z(values):
    if not isinstance(values, (list, tuple)):
        values = [values] * 3
    return [send(value, "fsdp", 2 * (i + 1)) for i, value in enumerate(values)]


def gather_fsdp(block, name):
    came = along_z(block)
    return came, send(row([block, *came], name), "fsdp", 1)


def exchange(rows):
    return lax.all_to_all(rows, "expert", 0, 0, tiled=True)


def shards(
    tokens,
    lengths,
    routes,
    first_gain,
    query_weight,
    key_weight,
    value_weight,
    output_weight,
    query_gain,
    key_gain,
    second_gain,
    router_weight,
    gate_weight,
    up_weight,
    down_weight,
    cotangent,
):
    own = tokens[0]
    upstream = cotangent[0]
    rows, width = own.shape
    fsdp = lax.axis_size("fsdp")
    owners = lax.axis_size("expert")
    me = lax.axis_index("fsdp").astype(jnp.int32).reshape(1)
    owner = lax.axis_index("expert").astype(jnp.int32).reshape(1)
    experts = router_weight.shape[1]
    capacity = 3 * rows * routes.shape[2] // (2 * experts)
    kv_columns = key_weight.shape[1] // fsdp
    q_columns = query_weight.shape[1] // fsdp
    columns = q_columns + 2 * kv_columns
    q_heads = q_columns // HEAD

    ends = jnp.cumsum(lengths[0])
    place = jnp.arange(rows * fsdp, dtype=jnp.int32)
    start = jnp.max(jnp.where(ends[:, None] <= place[None, :], ends[:, None], 0), axis=0)
    position = (place - start).astype(F32)
    frequency = ROPE_BASE ** (-jnp.arange(HEAD // 2, dtype=F32) * 2.0 / HEAD)
    angles = frequency[:, None] * position[None, :]
    cosine, sine = jnp.cos(angles), jnp.sin(angles)
    start = start[None, :].astype(jnp.int32)

    packed, x_sends, dressed, mask = pack_weights(
        me,
        own,
        query_weight,
        key_weight,
        value_weight,
        router_weight.T,
        first_gain[None],
        second_gain[None],
        query_gain[None],
        key_gain[None],
        routes[0].T,
        upstream,
    )
    x_came = along_z(x_sends)
    x_other = [send(own, "fsdp", 1), send(packed[1], "fsdp", 1)]
    deal, turn, tick = slot_tables(mask, capacity)
    ready = (*x_other, tick, cosine, sine, start)
    x_other.append(send(relay(x_came, rows * fsdp, after=ready), "fsdp", 1))
    c_all = lax.all_gather(dressed, "expert", axis=0)
    wo_came = along_z(output_weight)

    h1, pre, keep, give, inverse, gains, heads, turned, mixed = attention_forward(
        me, own, packed[0], x_came, x_other, cosine, sine, start, experts, q_heads
    )
    other = send(give, "fsdp", 1)
    mixed_sends, wo_stack = merge(keep, other, output_weight, wo_came)
    mixed_came = along_z(mixed_sends)
    wo_other = send(wo_stack, "fsdp", 1)
    middle, probs, hidden, sent = middle_layer(
        own, keep, other, mixed_came, output_weight, wo_came, wo_other, gains, deal, experts, owners
    )
    h_rows = exchange(sent)
    rows_c, row_mask, back = deal_rows(owner, c_all, down_weight, experts, capacity)
    rows_back, gate_low, up_low, active, weighted, share = expert_layer(
        owner, h_rows, gains, row_mask, back, gate_weight, up_weight, experts
    )
    came_back = exchange(rows_back)
    grads, tick = expert_weights(h_rows, rows_c, gate_low, up_low, weighted)
    grads = lax.psum(grads, "fsdp")
    gate_sum, up_sum, down_sum = widen(grads)
    sent, tick = expert_outputs(active, share, down_weight, owners, after=(tick,))

    middle_grad, middle_low, extra = router_backward(
        came_back, turn, middle, probs, mask, gains, upstream, hidden, experts, after=(tick,)
    )
    da_came, da_other = gather_fsdp(middle_low, "row_middle")
    out_rows = exchange(sent)
    layer_out, _ = layer_output(out_rows, turn, middle)
    first, dh_keep, dh_give = attention_backward(
        me,
        middle_low,
        da_came,
        da_other,
        heads,
        output_weight,
        cosine,
        sine,
        start,
        h1,
        pre,
        mixed,
        inverse,
        turned,
        extra,
        experts,
        q_heads,
    )
    dh_total, *dh_sends = pair_sum(dh_keep, send(dh_give, "fsdp", 1))
    dh_came = along_z(dh_sends)
    tokens_grad = input_grad(dh_total, dh_came, own, gains, middle_grad, experts)
    first = passed(first, after=(out_rows, grads))
    parted, rest = shares_sum(exchange(first), after=(*dh_came, down_sum))
    parted = lax.all_to_all(parted, "fsdp", 0, 0, tiled=True)
    pieces = exchange(whole_pieces(parted, rest, after=(layer_out, tokens_grad)))
    query_sum, key_sum, value_sum, output_sum, one_sum, two_sum, *gain_sums, router_sum = final_grads(
        pieces, query_weight, key_weight, value_weight, first_gain[None], experts
    )
    return (
        layer_out[None],
        tokens_grad[None],
        one_sum[0],
        query_sum,
        key_sum,
        value_sum,
        output_sum,
        gain_sums[0][0],
        gain_sums[1][0],
        two_sum[0],
        router_sum.T,
        gate_sum,
        up_sum,
        down_sum,
    )


def solution(mesh):
    whole = P("expert", "fsdp", None)
    rows = P("fsdp", None)
    vector = P("fsdp")
    owned = P("expert", None, None)
    return jax.shard_map(
        shards,
        mesh=mesh,
        in_specs=(
            whole,
            P("expert", None),
            whole,
            vector,
            rows,
            rows,
            rows,
            rows,
            vector,
            vector,
            vector,
            rows,
            owned,
            owned,
            owned,
            whole,
        ),
        out_specs=(
            whole,
            whole,
            vector,
            rows,
            rows,
            rows,
            rows,
            vector,
            vector,
            vector,
            rows,
            owned,
            owned,
            owned,
        ),
        check_vma=False,
    )
```

```python
import functools

import jax
import jax.numpy as jnp
from jax import lax
from jax.experimental import pallas as pl
from jax.experimental.pallas import tpu as pltpu
from jax.sharding import PartitionSpec as P

EPSILON = 1e-06
ROPE_BASE = 10000.0
HEAD = 64
TILE = 256
F32 = jnp.float32
BF16 = jnp.bfloat16
VMEM = pl.BlockSpec(memory_space=pltpu.VMEM)
SMEM = pl.BlockSpec(memory_space=pltpu.SMEM)
ANY = pl.BlockSpec(memory_space=pl.ANY)
HBM = pl.BlockSpec(memory_space=pltpu.HBM)


def dot(left, right, dims=((1,), (0,))):
    return lax.dot_general(left, right, (dims, ((), ())), preferred_element_type=F32)


def shape(extent, dtype):
    return jax.ShapeDtypeStruct(extent, dtype)


def kernel_call(
    body, name, micros, operands, results, smem=0, hbm=(), out_hbm=(), after=(), scratch=(), held=(), late=(), stored=(), mib=63
):
    held = tuple(held) + tuple(late)
    n, a, r, s = len(operands), len(after), len(results), len(scratch)
    specs = [SMEM if i < smem else HBM if i in held or i in hbm else VMEM for i in range(n)]
    out_specs = [HBM if i in stored or i in out_hbm else VMEM for i in range(r)]
    staged = [pltpu.VMEM(operands[i].shape, operands[i].dtype) for i in held]
    staged += [pltpu.VMEM(*results[i]) for i in stored]
    sems = [pltpu.SemaphoreType.DMA((max(len(held), 1),)), pltpu.SemaphoreType.DMA((max(len(stored), 1),))]

    def wrapped(*refs):
        ins, outs = list(refs[:n]), list(refs[n + a : n + a + r])
        own = refs[n + a + r : n + a + r + s]
        stages, (load_sem, store_sem) = refs[n + a + r + s : -2], refs[-2:]
        loads, stores, begun = {}, {}, []
        for k, i in enumerate(held):
            loads[i] = pltpu.make_async_copy(ins[i], stages[k], load_sem.at[k])
            loads[i].start()
            ins[i] = stages[k]
        for k, i in enumerate(stored):
            stores[i] = pltpu.make_async_copy(stages[len(held) + k], outs[i], store_sem.at[k])
            outs[i] = stages[len(held) + k]
        for i in held:
            if i not in late:
                loads[i].wait()

        def store(*which):
            for i in which:
                stores[i].start()
                begun.append(i)

        extra = {}
        if late:
            extra["wait"] = lambda i: loads[i].wait()
        if stored:
            extra["store"] = store
        body(*ins, *outs, *own, **extra)
        store(*[i for i in stored if i not in begun])
        for i in stored:
            stores[i].wait()

    return pl.pallas_call(
        wrapped,
        out_shape=[shape(*result) for result in results],
        in_specs=specs + [ANY] * a,
        out_specs=out_specs,
        scratch_shapes=list(scratch) + staged + sems,
        compiler_params=pltpu.CompilerParams(vmem_limit_bytes=mib * 1024 * 1024),
        cost_estimate=pl.CostEstimate(flops=0, bytes_accessed=int(micros * 3.6e6), transcendentals=0),
        name=name,
    )(*operands, *after)


def move_call(moves, name, micros, operands, results, after=(), mib=10):
    def body(*refs):
        for source, target in moves(*refs):
            target[...] = source[...]

    return kernel_call(body, name, micros, operands, results, after=after, mib=mib)


def lane_blocks(value):
    return jnp.concatenate([value[:, i : i + 128] for i in range(0, value.shape[1], 128)], axis=0)


def joined_lanes(value, count):
    rows = value.shape[0] // count
    return jnp.concatenate([value[i * rows : (i + 1) * rows] for i in range(count)], axis=1)


def softmax_rows(logits):
    powers = jnp.exp(logits - jnp.max(logits, axis=0, keepdims=True))
    return powers / jnp.sum(powers, axis=0, keepdims=True)


def head_forward(pre, gain, cosine, sine):
    scale = lax.rsqrt(jnp.mean(pre * pre, axis=0, keepdims=True) + EPSILON)
    normed = pre * scale
    scaled = normed * gain
    a, b = scaled[: HEAD // 2], scaled[HEAD // 2 :]
    turned = jnp.concatenate([a * cosine - b * sine, b * cosine + a * sine], axis=0)
    return turned, normed, scale


def head_backward(grad, normed, scale, gain, cosine, sine):
    a, b = grad[: HEAD // 2], grad[HEAD // 2 :]
    unturned = jnp.concatenate([a * cosine + b * sine, b * cosine - a * sine], axis=0)
    gain_grad = jnp.sum(unturned * normed, axis=1, keepdims=True)
    inner = unturned * gain
    pre_grad = scale * (inner - normed * jnp.mean(inner * normed, axis=0, keepdims=True))
    return pre_grad, gain_grad


def slots_kernel(mask_ref, deal_ref, turn_ref, whole_ref, *, capacity, store):
    experts, rows = mask_ref.shape
    mask = mask_ref[...]
    ranks = dot(mask.astype(BF16), earlier(rows))
    slot = lax.broadcasted_iota(jnp.int32, (capacity, rows), 0).astype(F32) + 1.0
    for expert in range(experts):
        one = slice(expert, expert + 1)
        whole_ref[expert * capacity : (expert + 1) * capacity] = jnp.where(
            (ranks[one] == slot) & (mask[one] > 0.5), 1.0, 0.0
        )
    deal_ref[...] = whole_ref[...].astype(BF16)
    store(0)
    for part in range(0, experts * capacity, 128):
        turn_ref[:, part : part + 128] = whole_ref[part : part + 128].T.astype(BF16)


def slot_tables(mask, capacity):
    experts, rows = mask.shape
    slots = experts * capacity
    return kernel_call(
        functools.partial(slots_kernel, capacity=capacity),
        "slot_tables",
        2.0,
        [mask],
        [((slots, rows), BF16), ((rows, slots), BF16)],
        scratch=[pltpu.VMEM((slots, rows), F32)],
        stored=(0, 1),
    )


def earlier(rows):
    return (
        lax.broadcasted_iota(jnp.int32, (rows, rows), 0)
        <= lax.broadcasted_iota(jnp.int32, (rows, rows), 1)
    ).astype(BF16)


def pack_kernel(
    me_ref, x_ref, wq_ref, wk_ref, wv_ref, router_ref, one_ref, two_ref, qg_ref, kg_ref, routes_ref, c_ref, *outs, wait, store
):
    own_ref, sends, dressed_ref, mask_ref, other_ref, parts_ref = outs[0], outs[1:4], *outs[4:]
    experts, rows = router_ref.shape
    wide = wq_ref.shape[1] // 8
    narrow = wk_ref.shape[1] // 8
    count = qg_ref.shape[1]
    heads = jnp.concatenate([qg_ref[...], kg_ref[...]], axis=0).astype(F32)
    heads = jnp.concatenate([heads, jnp.zeros((2, 128 - count), F32)], axis=1)
    heads = jnp.concatenate([heads, jnp.zeros((126, 128), F32)], axis=0).T[:count]
    small = jnp.concatenate(
        [
            router_ref[...].astype(F32),
            one_ref[...].astype(F32),
            two_ref[...].astype(F32),
            jnp.zeros((6, 128), F32),
            heads,
        ],
        axis=0,
    ).astype(BF16)
    for part in range(8):
        parts_ref[part, :wide] = wq_ref[:, part * wide : (part + 1) * wide].astype(F32).T.astype(BF16)
        parts_ref[part, wide + 2 * narrow :] = small
    for pair in range(4):
        span = slice(pair * 128, (pair + 1) * 128)
        for ref, place in ((wk_ref, wide), (wv_ref, wide + narrow)):
            turned = ref[:, span].astype(F32).T.astype(BF16)
            parts_ref[2 * pair, place : place + narrow] = turned[:narrow]
            parts_ref[2 * pair + 1, place : place + narrow] = turned[narrow:]
    me = me_ref[0]
    tall = parts_ref.shape[1]
    blocks = lane_blocks(x_ref[...])
    base = blocks.shape[0]
    own_ref[...] = parts_ref[me]
    other_ref[...] = parts_ref[me ^ 1]
    for flip in range(1, 4):
        sends[flip - 1][:base] = blocks
        sends[flip - 1][base : base + tall] = parts_ref[me ^ (2 * flip)]
        sends[flip - 1][base + tall :] = parts_ref[me ^ (2 * flip + 1)]
    store(1, 2, 3, 6, 0)
    wait(10)
    wait(11)
    width = c_ref.shape[1]
    subs = lax.broadcasted_iota(jnp.int32, (128, rows), 0)
    routed = jnp.zeros((128, rows), F32)
    for route in range(routes_ref.shape[0]):
        routed = routed + jnp.where(routes_ref[route : route + 1] == subs, 1.0, 0.0)
    dressed_ref[:, :width] = c_ref[...]
    dressed_ref[:, width:] = routed.T.astype(BF16)
    mask_ref[...] = routed[:experts]


def pack_weights(me, x, wq, wk, wv, router, one, two, qg, kg, routes, c):
    experts = router.shape[0]
    tall = (wq.shape[1] + wk.shape[1] + wv.shape[1]) // 8 + experts + 16
    rows, width = x.shape
    base = rows * 8
    own, first, second, third, dressed, mask, other = kernel_call(
        pack_kernel,
        "pack_weights",
        2.5,
        [me, x, wq, wk, wv, router, one, two, qg, kg, routes, c],
        [((tall, 128), BF16)]
        + [((base + 2 * tall, 128), BF16)] * 3
        + [((rows, width + 128), BF16), ((experts, rows), F32), ((tall, 128), BF16)],
        smem=1,
        scratch=[pltpu.VMEM((8, tall, 128), BF16)],
        held=range(1, 10),
        late=(10, 11),
        stored=(0, 1, 2, 3, 4, 5, 6),
    )
    return (own, other), [first, second, third], dressed, mask


def relay(came, base, after):
    tall = (came[0].shape[0] - base) // 2

    def moves(*refs):
        pairs = []
        for flip, ref in enumerate(refs[:3]):
            pairs.append((ref.at[:base], refs[3].at[flip, :base]))
            pairs.append((ref.at[base + tall :], refs[3].at[flip, base:]))
        return pairs

    return move_call(moves, "relay", 1.5, came, [((3, base + tall, 128), BF16)], after)[0]


def forward_kernel(me_ref, x_ref, own_ref, *refs, experts, q_heads, store):
    came, other_x, other_w, other_ref = refs[:3], refs[3], refs[4], refs[5]
    cos_ref, sin_ref, start_ref = refs[6:9]
    h1_ref, pre_ref, keep_ref, give_ref, inverse_ref, gains_ref, heads_ref, turned_ref, out_ref = refs[-9:]
    rows, width = x_ref.shape
    q_columns = q_heads * HEAD
    columns = q_columns + 2 * HEAD
    total = rows * 8
    tall = own_ref.shape[0]
    base = 8 * rows
    me = me_ref[0]
    for slot in range(8):
        flip = slot // 2
        if slot % 2:
            piece = other_ref[flip - 1, base:] if flip else other_w[...]
        elif flip:
            piece = came[flip - 1][base : base + tall]
        else:
            piece = own_ref[...]
        span = pl.ds(pl.multiple_of((me ^ slot) * rows, rows), rows)
        turned_ref[:, span] = piece[:columns]
        small = piece[columns:].astype(F32)
        gains_ref[:, span] = small[: experts + 8]
        heads_ref[pl.ds(pl.multiple_of((me ^ slot) * 8, 8), 8)] = small[experts + 8 :]
    gain_one = gains_ref[experts : experts + 1]
    for slot in range(8):
        flip = slot // 2
        if slot % 2:
            x = joined_lanes(other_ref[flip - 1, :base], 8) if flip else other_x[...]
        elif flip:
            x = joined_lanes(came[flip - 1][:base], 8)
        else:
            x = x_ref[...]
        x = x.astype(F32)
        scale = lax.rsqrt(jnp.mean(x * x, axis=1, keepdims=True) + EPSILON)
        h1_ref[slot] = (x * scale * gain_one).astype(BF16)
    store(0, 6, 7)
    for slot in range(8):
        block = dot(turned_ref[...], h1_ref[slot], ((1,), (1,)))
        place = pl.multiple_of((me ^ slot) * rows, rows)
        pre_ref[:, pl.ds(place, rows)] = block
    store(1)
    cosine, sine = cos_ref[...], sin_ref[...]
    gain_query, gain_key = heads_ref[:, :1], heads_ref[:, 1:2]
    key = head_forward(pre_ref[q_columns : q_columns + HEAD], gain_key, cosine, sine)[0]
    key = key.T.astype(BF16)
    value = pre_ref[q_columns + HEAD :].astype(BF16)
    inverse_ref[...] = jnp.zeros(inverse_ref.shape, F32)
    for head in range(q_heads):
        query = head_forward(pre_ref[head * HEAD : (head + 1) * HEAD], gain_query, cosine, sine)[0]
        query = query.astype(BF16) * jnp.array(HEAD ** (-0.5), BF16)
        for tile in range(total // TILE):
            low, high = tile * TILE, (tile + 1) * TILE
            scores = dot(key[:high], query[:, low:high])
            u = lax.broadcasted_iota(jnp.int32, (high, TILE), 0)
            t = lax.broadcasted_iota(jnp.int32, (high, TILE), 1) + low
            allowed = (u >= start_ref[:, low:high]) & (u <= t)
            powers = jnp.where(allowed, jnp.exp(scores), 0.0)
            inverse = 1.0 / jnp.sum(powers, axis=0, keepdims=True)
            probs = (powers * inverse).astype(BF16)
            mixed = dot(value[:, :high], probs).astype(BF16)
            inverse_ref[head : head + 1, low:high] = inverse
            for part in range(TILE // rows):
                out_ref[low // rows + part, head * HEAD : (head + 1) * HEAD] = mixed[
                    :, part * rows : (part + 1) * rows
                ]
    for slot in range(8):
        (give_ref if slot % 2 else keep_ref)[slot // 2] = out_ref[me ^ slot]


def attention_forward(me, x, own, came, other, cosine, sine, start, experts, q_heads, after=()):
    rows, width = x.shape
    total = 8 * rows
    columns = (q_heads + 2) * HEAD
    q_columns = q_heads * HEAD
    return kernel_call(
        functools.partial(forward_kernel, experts=experts, q_heads=q_heads),
        "attention_forward",
        7.0,
        [me, x, own, *came, *other, cosine, sine, start],
        [
            ((8, rows, width), BF16),
            ((columns, total), F32),
            ((4, q_columns, rows), BF16),
            ((4, q_columns, rows), BF16),
            ((8, total), F32),
            ((experts + 8, width), F32),
            ((HEAD, 128), F32),
            ((columns, width), BF16),
            ((8, q_columns, rows), BF16),
        ],
        smem=1,
        after=after,
        held=(1,),
        stored=(0, 1, 4, 6, 7, 8),
    )


def merge(keep, came, wo, wo_came):
    def moves(keep_ref, came_ref, *refs):
        weights, outs, stacked = refs[:4], refs[4:7], refs[7]
        pairs = [(weight, stacked.at[i]) for i, weight in enumerate(weights)]
        for flip in range(1, 4):
            pairs.append((keep_ref.at[flip], outs[flip - 1].at[0]))
            pairs.append((came_ref.at[flip], outs[flip - 1].at[1]))
        return pairs

    extent = ((2,) + keep.shape[1:], BF16)
    results = [extent] * 3 + [((4,) + wo.shape, BF16)]
    *sends, stacked = move_call(moves, "merge", 1.0, [keep, came, wo, *wo_came], results)
    return sends, stacked


def middle_kernel(x_ref, keep_ref, other_ref, *refs, experts, wait, store):
    came, wo_ref, wo_came, wo_other_ref, gains_ref, deal_ref = refs[:3], refs[3], refs[4:7], refs[7], refs[8], refs[9]
    middle_ref, probs_ref, hidden_ref, sent_ref, mixed_ref, whole_ref, out_ref, out_sem = refs[10:]
    rows, width = x_ref.shape
    for slot in range(8):
        flip, core = slot // 2, slot % 2
        if flip:
            piece = came[flip - 1][core]
        else:
            piece = (other_ref if core else keep_ref)[0]
        span = slice(slot * 128, (slot + 1) * 128)
        mixed_ref[:, span] = piece.astype(F32).T.astype(BF16)
    for i in (6, 7, 8, 9, 10):
        wait(i)
    for slot in range(8):
        flip = slot // 2
        span = slice(slot * 128, (slot + 1) * 128)
        if slot % 2:
            whole_ref[span] = wo_other_ref[flip]
        else:
            whole_ref[span] = (wo_came[flip - 1] if flip else wo_ref)[...]
    wait(0)
    middle = x_ref[...].astype(F32) + dot(mixed_ref[...], whole_ref[...])
    middle_ref[...] = middle
    scale = lax.rsqrt(jnp.mean(middle * middle, axis=1, keepdims=True) + EPSILON)
    hidden = (middle * scale * gains_ref[experts + 1 : experts + 2]).astype(BF16)
    hidden_ref[...] = hidden
    probs_ref[...] = softmax_rows(dot(gains_ref[:experts].astype(BF16), hidden, ((1,), (1,))))
    store(0, 2)
    owners, per_owner, capacity, _ = sent_ref.shape
    group = owners // 4
    size = group * per_owner * capacity
    copies = []
    wait(12)
    for part in range(4):
        taken = dot(deal_ref[part * size : (part + 1) * size], hidden).astype(BF16)
        blocks = slice(group * part, group * (part + 1))
        out_ref[blocks] = taken.reshape(group, per_owner, capacity, width)
        copies.append(pltpu.make_async_copy(out_ref.at[blocks], sent_ref.at[blocks], out_sem.at[part]))
        copies[-1].start()
    for copy in copies:
        copy.wait()


def middle_layer(x, keep, other, came, wo, wo_came, wo_other, gains, deal, experts, owners):
    rows, width = x.shape
    per_owner = experts // owners
    capacity = deal.shape[0] // experts
    sent = ((owners, per_owner, capacity, width), BF16)
    return kernel_call(
        functools.partial(middle_kernel, experts=experts),
        "middle_layer",
        3.0,
        [x, keep, other, *came, wo, *wo_came, wo_other, gains, deal],
        [((rows, width), F32), ((experts, rows), F32), ((rows, width), BF16), sent],
        out_hbm=(3,),
        scratch=[
            pltpu.VMEM((rows, width), BF16),
            pltpu.VMEM((width, width), BF16),
            pltpu.VMEM(*sent),
            pltpu.SemaphoreType.DMA((4,)),
        ],
        late=(6, 7, 8, 9, 10, 0, 12),
        stored=(0, 2),
    )


def row(pieces, name):
    def moves(*refs):
        return [(ref, refs[-1].at[i]) for i, ref in enumerate(refs[:-1])]

    return move_call(moves, name, 1.0, pieces, [((len(pieces),) + pieces[0].shape, BF16)])[0]


def backward_kernel(me_ref, own_da_ref, *refs, experts, q_heads, wait):
    came, other_ref = refs[:3], refs[3]
    heads_ref, wo_ref, cos_ref, sin_ref, start_ref = refs[4:9]
    h1_ref, pre_ref, mixed_ref, inverse_ref, turned_ref, extra_ref = refs[9:15]
    first_ref, keep_ref, send_ref = refs[-10:-7]
    da_ref, mixed_grad_ref, dkey_ref, dvalue_ref, low_ref, out_slots_ref, grad_ref = refs[-7:]
    rows, width = own_da_ref.shape
    q_columns = q_heads * HEAD
    columns = q_columns + 2 * HEAD
    total = rows * 8
    me = me_ref[0]
    for slot in range(8):
        flip, core = slot // 2, slot % 2
        if core:
            piece = other_ref[flip]
        else:
            piece = (came[flip - 1] if flip else own_da_ref)[...]
        span = slice(slot * rows, (slot + 1) * rows)
        da_ref[span] = piece
        place = pl.multiple_of((me ^ slot) * rows, rows)
        mixed_grad_ref[:, pl.ds(place, rows)] = dot(wo_ref[...], piece, ((1,), (1,))).astype(BF16)
    wait(13)
    for slot in range(8):
        out_slots_ref[:, slot * rows : (slot + 1) * rows] = mixed_ref[me ^ slot]
    wo_grad = dot(out_slots_ref[...], da_ref[...]).astype(BF16)
    wo_grad = lane_blocks(wo_grad)
    wait(12)
    wait(14)
    gain_query, gain_key = heads_ref[:, :1], heads_ref[:, 1:2]
    cosine, sine = cos_ref[...], sin_ref[...]
    key_turned, key_normed, key_scale = head_forward(
        pre_ref[q_columns : q_columns + HEAD], gain_key, cosine, sine
    )
    key_low = key_turned.astype(BF16)
    key = key_turned.T.astype(BF16)
    value = pre_ref[q_columns + HEAD :].T.astype(BF16)
    dkey_ref[...] = jnp.zeros(dkey_ref.shape, F32)
    dvalue_ref[...] = jnp.zeros(dvalue_ref.shape, F32)
    gain_query_grad = jnp.zeros((HEAD, 1), F32)
    pieces = []
    for head in range(q_heads):
        span = slice(head * HEAD, (head + 1) * HEAD)
        turned, normed, scale = head_forward(pre_ref[span], gain_query, cosine, sine)
        query = turned.astype(BF16) * jnp.array(HEAD ** (-0.5), BF16)
        grads = []
        for tile in range(total // TILE):
            low, high = tile * TILE, (tile + 1) * TILE
            part = query[:, low:high]
            mixed_grad = mixed_grad_ref[span, low:high]
            scores = dot(key[:high], part)
            u = lax.broadcasted_iota(jnp.int32, (high, TILE), 0)
            t = lax.broadcasted_iota(jnp.int32, (high, TILE), 1) + low
            allowed = (u >= start_ref[:, low:high]) & (u <= t)
            probs = jnp.where(allowed, jnp.exp(scores) * inverse_ref[head : head + 1, low:high], 0.0)
            attend = dot(value[:high], mixed_grad)
            delta = jnp.sum(probs * attend, axis=0, keepdims=True)
            score_low = (probs * (attend - delta)).astype(BF16)
            grads.append(dot(key_low[:, :high], score_low))
            dkey_ref[:, :high] += dot(part, score_low, ((1,), (1,)))
            dvalue_ref[:, :high] += dot(mixed_grad, probs.astype(BF16), ((1,), (1,)))
        query_grad = jnp.concatenate(grads, axis=1) * HEAD ** (-0.5)
        pre_grad, gain_grad = head_backward(query_grad, normed, scale, gain_query, cosine, sine)
        gain_query_grad += gain_grad
        pieces.append(pre_grad)
    pre_grad, gain_key_grad = head_backward(
        dkey_ref[...], key_normed, key_scale, gain_key, cosine, sine
    )
    pieces += [pre_grad, dvalue_ref[...]]
    pre_grad = jnp.concatenate(pieces, axis=0)
    low_ref[...] = pre_grad.astype(BF16)
    slots_grad = []
    for slot in range(8):
        place = pl.multiple_of((me ^ slot) * rows, rows)
        slots_grad.append(low_ref[:, pl.ds(place, rows)])
    slots_grad = jnp.concatenate(slots_grad, axis=1)
    wait(11)
    wait(15)
    grad_ref[:columns] = dot(slots_grad, h1_ref[...].reshape(total, width))
    extra = extra_ref[...]
    lane = lax.broadcasted_iota(jnp.int32, (HEAD, 128), 1)
    gains = jnp.where(lane == 0, gain_query_grad, jnp.where(lane == 1, gain_key_grad, 0.0))
    gains = gains.T[:2]
    step = HEAD // 8
    grad_ref[columns:] = jnp.zeros((64, width), F32)
    grad_ref[columns : columns + experts + 1] = extra[: experts + 1]
    for part in range(8):
        grad_ref[columns + experts + 1 : columns + experts + 3, part * rows : part * rows + step] = gains[
            :, part * step : (part + 1) * step
        ]
    for piece in range(16):
        spare = []
        place = columns + piece * SPARE
        for part in range(8):
            span = slice(part * rows, (part + 1) * rows)
            block = grad_ref[piece * PIECE : (piece + 1) * PIECE, span]
            first_ref[piece, part * PIECE : (part + 1) * PIECE] = block.astype(BF16)
            spare.append(grad_ref[place : place + SPARE, span])
        spare.append(jnp.zeros((2 * PIECE - 8 * SPARE, 128), F32))
        first_ref[piece, 8 * PIECE : 10 * PIECE] = jnp.concatenate(spare, axis=0).astype(BF16)
        first_ref[piece, 10 * PIECE :] = wo_grad[piece * SLICE : (piece + 1) * SLICE]
    turned = turned_ref[...]
    for slot in range(8):
        low_rows_slot = slots_grad[:, slot * rows : (slot + 1) * rows].astype(F32).T.astype(BF16)
        part = dot(low_rows_slot, turned)
        if slot % 2:
            send_ref[slot // 2] = part.astype(BF16)
        else:
            keep_ref[slot // 2] = part


def attention_backward(
    me, da, came, other, heads, wo, cosine, sine, start, h1, pre, mixed, inverse, turned, extra, experts, q_heads, after=()
):
    rows, width = da.shape
    total = 8 * rows
    columns = pre.shape[0]
    q_columns = q_heads * HEAD
    return kernel_call(
        functools.partial(backward_kernel, experts=experts, q_heads=q_heads),
        "attention_backward",
        12,
        [me, da, *came, other, heads, wo, cosine, sine, start, h1, pre, mixed, inverse, turned, extra],
        [
            ((16, 10 * PIECE + SLICE, 128), BF16),
            ((4, rows, width), F32),
            ((4, rows, width), BF16),
        ],
        smem=1,
        after=after,
        held=(6, 7),
        late=(11, 12, 13, 14, 15),
        scratch=[
            pltpu.VMEM((total, width), BF16),
            pltpu.VMEM((q_columns, total), BF16),
            pltpu.VMEM((HEAD, total), F32),
            pltpu.VMEM((HEAD, total), F32),
            pltpu.VMEM((columns, total), BF16),
            pltpu.VMEM((q_columns, total), BF16),
            pltpu.VMEM((columns + 64, width), F32),
        ],
    )


def deal_kernel(owner_ref, c_ref, down_ref, rows_c, mask_ref, back_ref, c_scratch, sems, *, experts, capacity, wait, store):
    owner = owner_ref[0]
    per_owner, hidden, width = down_ref.shape
    rows = c_ref.shape[1]
    loads = [pltpu.make_async_copy(c_ref.at[i], c_scratch.at[i], sems.at[i]) for i in range(16)]
    for load in loads:
        load.start()
    lanes = lax.broadcasted_iota(jnp.int32, (experts, 128), 1)
    subs = lax.broadcasted_iota(jnp.int32, (experts, 128), 0)
    eye = (lanes == subs).astype(BF16)
    before = earlier(rows)
    mine_of = lax.broadcasted_iota(jnp.int32, (experts, rows), 0) - owner * per_owner
    slot = lax.broadcasted_iota(jnp.int32, (capacity, rows), 0).astype(F32) + 1.0
    for block in range(16):
        loads[block].wait()
        c = c_scratch[block]
        mask = dot(eye, c[:, width:], ((1,), (1,)))
        ranks = dot(mask.astype(BF16), before)
        deals = []
        for k in range(per_owner):
            mine = mine_of == k
            hit = jnp.sum(jnp.where(mine, mask, 0.0), axis=0, keepdims=True)
            rank = jnp.sum(jnp.where(mine, ranks, 0.0), axis=0, keepdims=True)
            deals.append(jnp.where((rank == slot) & (hit > 0.5), 1.0, 0.0))
        taken = dot(jnp.concatenate(deals, axis=0).astype(BF16), c).astype(BF16)
        span = slice(block * capacity, (block + 1) * capacity)
        for k in range(per_owner):
            spot = slice(k * capacity, (k + 1) * capacity)
            rows_c[k, span] = taken[spot, :width]
            mask_ref[k, span] = taken[spot, width:]
    store(0, 1)
    wait(2)
    for k in range(per_owner):
        for tile in range(16 * capacity // TILE):
            span = slice(tile * TILE, (tile + 1) * TILE)
            back_ref[k, span] = dot(rows_c[k, span], down_ref[k], ((1,), (1,)))


def deal_rows(owner, c, down, experts, capacity):
    per_owner, hidden, width = down.shape
    count = 16 * capacity
    return kernel_call(
        functools.partial(deal_kernel, experts=experts, capacity=capacity),
        "deal_rows",
        12.0,
        [owner, c, down],
        [
            ((per_owner, count, width), BF16),
            ((per_owner, count, 128), BF16),
            ((per_owner, count, hidden), F32),
        ],
        smem=1,
        hbm=(1,),
        scratch=[pltpu.VMEM(c.shape, BF16), pltpu.SemaphoreType.DMA((16,))],
        late=(2,),
        stored=(0, 1, 2),
    )


def expert_kernel(
    owner_ref,
    h_hbm,
    gains_ref,
    mask_ref,
    back_hbm,
    gate_hbm,
    up_hbm,
    rows_hbm,
    gate_out,
    up_out,
    active_out,
    weighted_out,
    share_ref,
    h_ref,
    back_in,
    gate_ref,
    up_ref,
    rows_back,
    load_sem,
    store_sem,
    *,
    experts,
    store,
):
    owners, per_owner, capacity, width = h_hbm.shape
    group = 8
    parts = owners // group
    size = group * capacity
    loads = {}
    for k in range(per_owner):
        for part in range(parts):
            blocks = slice(part * group, (part + 1) * group)
            spot = (k * parts + part) * 4
            loads[k, part] = [
                pltpu.make_async_copy(h_hbm.at[blocks, k], h_ref.at[blocks, k], load_sem.at[spot]),
                pltpu.make_async_copy(
                    back_hbm.at[k, part * size : (part + 1) * size],
                    back_in.at[k, part * size : (part + 1) * size],
                    load_sem.at[spot + 1],
                ),
            ]
            if part == 0:
                loads[k, part] += [
                    pltpu.make_async_copy(gate_hbm.at[k], gate_ref.at[k], load_sem.at[spot + 2]),
                    pltpu.make_async_copy(up_hbm.at[k], up_ref.at[k], load_sem.at[spot + 3]),
                ]
            for load in loads[k, part]:
                load.start()
    owner = owner_ref[0]
    router = jnp.concatenate([gains_ref[:experts], jnp.zeros((128 - experts, width), F32)], axis=0)
    router = router.astype(BF16)
    lane = lax.broadcasted_iota(jnp.int32, (size, 128), 1)
    copies = []
    for k in range(per_owner):
        place = owner * per_owner + k
        for part in range(parts):
            blocks = slice(part * group, (part + 1) * group)
            span = slice(part * size, (part + 1) * size)
            for load in loads[k, part]:
                load.wait()
            h = h_ref[blocks, k].reshape(size, width)
            gate = dot(h, gate_ref[k])
            up = dot(h, up_ref[k])
            logits = dot(h, router, ((1,), (1,)))
            chosen = mask_ref[k, span] > 0.5
            top = jnp.max(jnp.where(chosen, logits, -1e30), axis=1, keepdims=True)
            powers = jnp.where(chosen, jnp.exp(logits - top), 0.0)
            total = jnp.sum(powers, axis=1, keepdims=True)
            share = jnp.sum(jnp.where(lane == place, powers, 0.0), axis=1, keepdims=True)
            share = share / jnp.where(total > 0.0, total, 1.0)
            share_ref[k, span] = jnp.broadcast_to(share, (size, 128))
            back = back_in[k, span]
            sig = 1.0 / (1.0 + jnp.exp(-gate))
            silu = gate * sig
            active = silu * up
            active_low = active.astype(BF16)
            route_grad = jnp.sum(active_low.astype(F32) * back, axis=1, keepdims=True)
            grad = back * share
            gate_low = (grad * up * (sig + silu * (1.0 - sig))).astype(BF16)
            up_low = (grad * silu).astype(BF16)
            active_out[k, span] = active_low
            weighted_out[k, span] = (active * share).astype(BF16)
            gate_out[k, span] = gate_low
            up_out[k, span] = up_low
            rows = dot(gate_low, gate_ref[k], ((1,), (1,))) + dot(up_low, up_ref[k], ((1,), (1,)))
            high = route_grad.astype(BF16).astype(F32)
            spread_out = jnp.where(lane == place, high, 0.0)
            spread_out = jnp.where(lane == place + experts, route_grad - high, spread_out)
            whole = jnp.concatenate([rows.astype(BF16), spread_out.astype(BF16)], axis=1)
            rows_back[blocks, k] = whole.reshape(group, capacity, width + 128)
            copies.append(
                pltpu.make_async_copy(
                    rows_back.at[blocks, k], rows_hbm.at[blocks, k], store_sem.at[k * parts + part]
                )
            )
            copies[-1].start()
    store(1, 2, 3, 4, 5)
    for copy in copies:
        copy.wait()


def expert_layer(owner, h, gains, mask, back, gate, up, experts):
    per_owner, width, hidden = gate.shape
    owners, _, capacity, _ = h.shape
    count = owners * capacity
    narrow = ((per_owner, count, hidden), BF16)
    rows_back = ((owners, per_owner, capacity, width + 128), BF16)
    pieces = per_owner * (owners // 8)
    return kernel_call(
        functools.partial(expert_kernel, experts=experts),
        "expert_layer",
        14.0,
        [owner, h, gains, mask, back, gate, up],
        [rows_back] + [narrow] * 4 + [((per_owner, count, 128), F32)],
        smem=1,
        hbm=(1, 4, 5, 6),
        out_hbm=(0,),
        scratch=[pltpu.VMEM(value.shape, value.dtype) for value in (h, back, gate, up)]
        + [pltpu.VMEM(*rows_back), pltpu.SemaphoreType.DMA((4 * pieces,)), pltpu.SemaphoreType.DMA((pieces,))],
        stored=(1, 2, 3, 4, 5),
    )


def weights_kernel(
    h_hbm, rows_c, gate_low, up_low, weighted, out_hbm, tick_ref, h_ref, out_ref, load_sem, store_sem, *, wait
):
    tick_ref[...] = jnp.zeros(tick_ref.shape, F32)
    first = ((0,), (0,))
    owners, per_owner, capacity, width = h_hbm.shape
    hidden = gate_low.shape[2]
    half = width // 2
    loads = [
        pltpu.make_async_copy(h_hbm.at[:, k], h_ref.at[:, k], load_sem.at[k]) for k in range(per_owner)
    ]
    for load in loads:
        load.start()
    stores = []

    def keep(place):
        stores.append(pltpu.make_async_copy(out_ref.at[place], out_hbm.at[place], store_sem.at[place]))
        stores[-1].start()

    wait(2)
    for k in range(per_owner):
        loads[k].wait()
        rows_h = h_ref[:, k].reshape(owners * capacity, width)
        for place, low in ((k, gate_low), (per_owner + k, up_low)):
            if k == 0 and place:
                wait(3)
            total = dot(rows_h, low[k], first).astype(BF16)
            out_ref[place, :, :hidden] = total[:half]
            out_ref[place, :, hidden:] = total[half:]
            keep(place)
        if k == 0:
            wait(4)
            wait(1)
        place = 2 * per_owner + k
        out_ref[place] = dot(weighted[k], rows_c[k], first).astype(BF16)
        keep(place)
    for store in stores:
        store.wait()


def expert_weights(h, rows_c, gate_low, up_low, weighted):
    per_owner, count, width = rows_c.shape
    hidden = gate_low.shape[2]
    out = ((3 * per_owner, hidden, width), BF16)
    return kernel_call(
        weights_kernel,
        "expert_weights",
        0.1,
        [h, rows_c, gate_low, up_low, weighted],
        [out, ((8, 128), F32)],
        hbm=(0,),
        out_hbm=(0,),
        scratch=[
            pltpu.VMEM(h.shape, BF16),
            pltpu.VMEM(*out),
            pltpu.SemaphoreType.DMA((per_owner,)),
            pltpu.SemaphoreType.DMA((3 * per_owner,)),
        ],
        late=(2, 3, 4, 1),
    )


def widen_kernel(low_ref, gate_ref, up_ref, down_ref):
    step = pl.program_id(0)
    hidden = gate_ref.shape[2]
    value = low_ref[0].astype(F32)
    half = value.shape[0]
    for place, ref in ((0, gate_ref), (1, up_ref)):

        @pl.when(step // 2 == place)
        def _():
            ref[0, :half] = value[:, :hidden]
            ref[0, half:] = value[:, hidden:]

    @pl.when(step // 2 == 2)
    def _():
        down_ref[0] = value


def widen(low):
    count, hidden, width = low.shape
    per_owner = count // 3

    def spot(place):
        return lambda i: (jnp.clip(i - place * per_owner, 0, per_owner - 1), 0, 0)

    return pl.pallas_call(
        widen_kernel,
        grid=(count,),
        out_shape=[shape((per_owner, width, hidden), F32)] * 2 + [shape((per_owner, hidden, width), F32)],
        in_specs=[pl.BlockSpec((1, hidden, width), lambda i: (i, 0, 0))],
        out_specs=[
            pl.BlockSpec((1, width, hidden), spot(0)),
            pl.BlockSpec((1, width, hidden), spot(1)),
            pl.BlockSpec((1, hidden, width), spot(2)),
        ],
        compiler_params=pltpu.CompilerParams(vmem_limit_bytes=63 * 1024 * 1024),
        cost_estimate=pl.CostEstimate(flops=0, bytes_accessed=24_000_000, transcendentals=0),
        name="widen",
    )(low)


def outputs_kernel(active, share, down_ref, sent_ref, tick_ref, out_ref, out_sem, *, wait):
    tick_ref[...] = jnp.zeros(tick_ref.shape, F32)
    per_owner, count, hidden = active.shape
    owners, _, capacity, width = sent_ref.shape
    group = 8
    size = group * capacity
    copies = []
    for i in range(3):
        wait(i)
    for k in range(per_owner):
        for part in range(owners // group):
            span = slice(part * size, (part + 1) * size)
            blocks = slice(part * group, (part + 1) * group)
            produced = dot(active[k, span], down_ref[k]).astype(BF16).astype(F32)
            produced = (produced * share[k, span, :1]).astype(BF16)
            out_ref[blocks, k] = produced.reshape(group, capacity, width)
            copies.append(
                pltpu.make_async_copy(
                    out_ref.at[blocks, k], sent_ref.at[blocks, k], out_sem.at[k * (owners // group) + part]
                )
            )
            copies[-1].start()
    for copy in copies:
        copy.wait()


def expert_outputs(active, share, down, owners, after=()):
    per_owner, count, hidden = active.shape
    width = down.shape[2]
    sent = ((owners, per_owner, count // owners, width), BF16)
    return kernel_call(
        outputs_kernel,
        "expert_outputs",
        0.1,
        [active, share, down],
        [sent, ((8, 128), F32)],
        out_hbm=(0,),
        after=after,
        scratch=[pltpu.VMEM(*sent), pltpu.SemaphoreType.DMA((per_owner * (owners // 8),))],
        late=(0, 1, 2),
    )


def combined(rows_hbm, rows_ref, sems, turn_ref, ready):
    owners, per_owner, capacity, wide = rows_hbm.shape
    group = owners // 4
    size = group * per_owner * capacity
    loads = []
    for part in range(4):
        blocks = slice(part * group, (part + 1) * group)
        loads.append(pltpu.make_async_copy(rows_hbm.at[blocks], rows_ref.at[blocks], sems.at[part]))
        loads[-1].start()
    ready()
    total = None
    for part in range(4):
        loads[part].wait()
        rows = rows_ref[part * group : (part + 1) * group].reshape(size, wide)
        one = dot(turn_ref[:, part * size : (part + 1) * size], rows)
        total = one if total is None else total + one
    return total


def output_kernel(rows_hbm, turn_ref, middle_ref, out_ref, tick_ref, rows_ref, sems, *, wait, store):
    tick_ref[...] = jnp.zeros(tick_ref.shape, F32)
    total = combined(rows_hbm, rows_ref, sems, turn_ref, lambda: wait(1))
    wait(2)
    out_ref[...] = (middle_ref[...] + total).astype(BF16)


def layer_output(rows, turn, middle):
    return kernel_call(
        output_kernel,
        "layer_output",
        3,
        [rows, turn, middle],
        [(middle.shape, BF16), ((8, 128), F32)],
        hbm=(0,),
        scratch=[pltpu.VMEM(rows.shape, BF16), pltpu.SemaphoreType.DMA((4,))],
        late=(1, 2),
        stored=(0,),
    )


def router_kernel(
    rows_hbm,
    turn_ref,
    middle_ref,
    probs_ref,
    mask_ref,
    gains_ref,
    c_ref,
    hidden_ref,
    grad_ref,
    send_ref,
    extra_ref,
    rows_ref,
    sems,
    *,
    experts,
    wait,
    store,
):
    rows, width = middle_ref.shape
    returned = combined(rows_hbm, rows_ref, sems, turn_ref, lambda: wait(1))
    for i in (2, 4, 6, 7):
        wait(i)
    tail = returned[:, width:].T
    route_grad = tail[:experts] + tail[experts : 2 * experts]
    mask = mask_ref[...]
    probs = probs_ref[...]
    picked = probs * mask
    picked_sum = jnp.sum(picked, axis=0, keepdims=True)
    share = picked / picked_sum
    picked_grad = (route_grad - jnp.sum(route_grad * share, axis=0, keepdims=True)) / picked_sum
    prob_grad = mask * picked_grad
    logit_grad = probs * (prob_grad - jnp.sum(probs * prob_grad, axis=0, keepdims=True))
    extra_ref[:experts] = dot(logit_grad.astype(BF16), hidden_ref[...])
    logit_rows = jnp.concatenate([logit_grad, jnp.zeros((128 - experts, rows), F32)], axis=0).T
    router = gains_ref[:experts].astype(BF16)
    hidden_grad = returned[:, :width] + dot(logit_rows[:, :experts].astype(BF16), router)
    middle = middle_ref[...]
    scale = lax.rsqrt(jnp.mean(middle * middle, axis=1, keepdims=True) + EPSILON)
    normed = middle * scale
    extra_ref[experts : experts + 8] = jnp.broadcast_to(
        jnp.sum(hidden_grad * normed, axis=0, keepdims=True), (8, width)
    )
    inner = hidden_grad * gains_ref[experts + 1 : experts + 2]
    grad = c_ref[...].astype(F32) + scale * (
        inner - normed * jnp.mean(inner * normed, axis=1, keepdims=True)
    )
    grad_ref[...] = grad
    send_ref[...] = grad.astype(BF16)


def router_backward(rows_back, turn, middle, probs, mask, gains, c, hidden, experts, after=()):
    rows, width = middle.shape
    return kernel_call(
        functools.partial(router_kernel, experts=experts),
        "router_backward",
        5,
        [rows_back, turn, middle, probs, mask, gains, c, hidden],
        [((rows, width), F32), ((rows, width), BF16), ((experts + 8, width), F32)],
        hbm=(0,),
        after=after,
        scratch=[pltpu.VMEM(rows_back.shape, BF16), pltpu.SemaphoreType.DMA((4,))],
        late=(1, 2, 4, 6, 7),
        stored=(0,),
    )


def pair_kernel(keep_ref, other_ref, total_ref, *sends):
    for flip in range(4):
        total = keep_ref[flip] + other_ref[flip].astype(F32)
        if flip:
            sends[flip - 1][...] = total.astype(BF16)
        else:
            total_ref[...] = total


def pair_sum(keep, other):
    rows, width = keep.shape[1:]
    return kernel_call(
        pair_kernel, "pair_sum", 1.2, [keep, other], [((rows, width), F32)] + [((rows, width), BF16)] * 3
    )


def input_kernel(total_ref, *refs, experts, store):
    came = refs[:3]
    x_ref, gains_ref, middle_grad_ref, out_ref = refs[3:]
    total = total_ref[...]
    for piece in came:
        total = total + piece[...].astype(F32)
    x = x_ref[...].astype(F32)
    scale = lax.rsqrt(jnp.mean(x * x, axis=1, keepdims=True) + EPSILON)
    normed = x * scale
    inner = total * gains_ref[experts : experts + 1]
    out_ref[...] = middle_grad_ref[...] + scale * (
        inner - normed * jnp.mean(inner * normed, axis=1, keepdims=True)
    )


def input_grad(total, came, x, gains, middle_grad, experts):
    return kernel_call(
        functools.partial(input_kernel, experts=experts),
        "input_grad",
        2,
        [total, *came, x, gains, middle_grad],
        [(middle_grad.shape, F32)],
        held=(4, 6),
        stored=(0,),
    )[0]


PIECE, SPARE, SLICE = 16, 3, 64


def passed(value, after):
    results = [(value.shape, value.dtype)]
    return move_call(lambda *refs: [refs], "passed", 0.5, [value], results, after, 63)[0]


def shares_kernel(pieces_ref, out_ref, rest_ref):
    total = pieces_ref[0].astype(F32)
    for i in range(1, pieces_ref.shape[0]):
        total = total + pieces_ref[i].astype(F32)
    base = 8 * PIECE
    fill = jnp.zeros((PIECE - SPARE, 128), F32)
    for part in range(8):
        out_ref[part, :PIECE] = total[part * PIECE : (part + 1) * PIECE].astype(BF16)
        spare = total[base + part * SPARE : base + (part + 1) * SPARE]
        out_ref[part, PIECE:] = jnp.concatenate([spare, fill], axis=0).astype(BF16)
    rest_ref[...] = total[base + 2 * PIECE :].astype(BF16)


def shares_sum(pieces, after=()):
    return kernel_call(
        shares_kernel,
        "shares_sum",
        0.1,
        [pieces],
        [((8, 2 * PIECE, 128), BF16), ((SLICE, 128), BF16)],
        after=after,
    )


def whole_kernel(came_ref, rest_ref, out_ref):
    spare = came_ref[0, PIECE:].astype(F32)
    for i in range(1, 8):
        spare = spare + came_ref[i, PIECE:].astype(F32)
    rows = [came_ref[i, :PIECE] for i in range(8)] + [spare.astype(BF16), rest_ref[...]]
    rows = jnp.concatenate(rows, axis=0)
    for i in range(16):
        out_ref[i] = rows


def whole_pieces(came, rest, after=()):
    return kernel_call(
        whole_kernel,
        "whole_pieces",
        0.1,
        [came, rest],
        [((16, 9 * PIECE + SLICE, 128), BF16)],
        after=after,
    )[0]


def final_kernel(pieces_ref, wq_ref, wk_ref, wv_ref, gain_ref, *outs, experts):
    query_ref, key_ref, value_ref, output_ref, one_ref, two_ref, qg_ref, kg_ref, router_ref = outs
    rows = pieces_ref.shape[2]
    q_columns = query_ref.shape[1] // 8
    kv_columns = key_ref.shape[1] // 8
    sums = jnp.zeros((rows, 1), F32)
    base = 8 * PIECE
    for pair in range(4):
        keys, values = [], []
        for source in (2 * pair, 2 * pair + 1):
            block = [pieces_ref[i, source * PIECE : (source + 1) * PIECE] for i in range(16)]
            turned = jnp.concatenate(block, axis=0).astype(F32).T
            span = slice(source * q_columns, (source + 1) * q_columns)
            query = turned[:, :q_columns]
            query_ref[:, span] = query
            sums = sums + jnp.sum(query * wq_ref[:, span].astype(F32), axis=1, keepdims=True)
            keys.append(turned[:, q_columns : q_columns + kv_columns])
            values.append(turned[:, q_columns + kv_columns :])
        span = slice(2 * pair * kv_columns, 2 * (pair + 1) * kv_columns)
        for parts, ref, weight in ((keys, key_ref, wk_ref), (values, value_ref, wv_ref)):
            both = jnp.concatenate(parts, axis=1)
            ref[:, span] = both
            sums = sums + jnp.sum(both * weight[:, span].astype(F32), axis=1, keepdims=True)
    for i in range(16):
        half = i % 2 * SLICE
        output_ref[half : half + SLICE, i // 2 * rows : (i // 2 + 1) * rows] = pieces_ref[
            i, base + PIECE :
        ].astype(F32)
    spare = pieces_ref[:, base : base + PIECE].astype(F32)
    spare = jnp.concatenate([spare[i, :SPARE] for i in range(16)], axis=0)
    one_ref[...] = jnp.broadcast_to(sums, (rows, 128)).T[:1] / gain_ref[...].astype(F32)
    two_ref[...] = spare[experts : experts + 1]
    step = qg_ref.shape[1]
    qg_ref[...] = spare[experts + 1 : experts + 2, :step]
    kg_ref[...] = spare[experts + 2 : experts + 3, :step]
    router_ref[...] = spare[:experts]


def final_grads(pieces, wq, wk, wv, gain, experts):
    rows = pieces.shape[2]
    return kernel_call(
        functools.partial(final_kernel, experts=experts),
        "final_grads",
        0.2,
        [pieces, wq, wk, wv, gain],
        [
            (wq.shape, F32),
            (wk.shape, F32),
            (wv.shape, F32),
            ((rows, 8 * rows), F32),
            ((1, rows), F32),
            ((1, rows), F32),
            ((1, HEAD // 8), F32),
            ((1, HEAD // 8), F32),
            ((experts, rows), F32),
        ],
        held=(1, 2, 3, 4),
    )


def send(values, axis, flip):
    count = lax.axis_size(axis)
    return lax.ppermute(values, axis, [(i, i ^ flip) for i in range(count)])


def along_z(values):
    if not isinstance(values, (list, tuple)):
        values = [values] * 3
    return [send(value, "fsdp", 2 * (i + 1)) for i, value in enumerate(values)]


def gather_fsdp(block, name):
    came = along_z(block)
    return came, send(row([block, *came], name), "fsdp", 1)


def exchange(rows):
    return lax.all_to_all(rows, "expert", 0, 0, tiled=True)


def shards(
    tokens,
    lengths,
    routes,
    first_gain,
    query_weight,
    key_weight,
    value_weight,
    output_weight,
    query_gain,
    key_gain,
    second_gain,
    router_weight,
    gate_weight,
    up_weight,
    down_weight,
    cotangent,
):
    own = tokens[0]
    upstream = cotangent[0]
    rows, width = own.shape
    fsdp = lax.axis_size("fsdp")
    owners = lax.axis_size("expert")
    me = lax.axis_index("fsdp").astype(jnp.int32).reshape(1)
    owner = lax.axis_index("expert").astype(jnp.int32).reshape(1)
    experts = router_weight.shape[1]
    capacity = 3 * rows * routes.shape[2] // (2 * experts)
    kv_columns = key_weight.shape[1] // fsdp
    q_columns = query_weight.shape[1] // fsdp
    columns = q_columns + 2 * kv_columns
    q_heads = q_columns // HEAD

    ends = jnp.cumsum(lengths[0])
    place = jnp.arange(rows * fsdp, dtype=jnp.int32)
    start = jnp.max(jnp.where(ends[:, None] <= place[None, :], ends[:, None], 0), axis=0)
    position = (place - start).astype(F32)
    frequency = ROPE_BASE ** (-jnp.arange(HEAD // 2, dtype=F32) * 2.0 / HEAD)
    angles = frequency[:, None] * position[None, :]
    cosine, sine = jnp.cos(angles), jnp.sin(angles)
    start = start[None, :].astype(jnp.int32)

    packed, x_sends, dressed, mask = pack_weights(
        me,
        own,
        query_weight,
        key_weight,
        value_weight,
        router_weight.T,
        first_gain[None],
        second_gain[None],
        query_gain[None],
        key_gain[None],
        routes[0].T,
        upstream,
    )
    x_came = along_z(x_sends)
    x_other = [send(own, "fsdp", 1), send(packed[1], "fsdp", 1)]
    deal, turn = slot_tables(mask, capacity)
    ready = (*x_other, deal, cosine, sine, start)
    x_other.append(send(relay(x_came, rows * fsdp, after=ready), "fsdp", 1))
    c_all = lax.all_gather(dressed, "expert", axis=0)
    wo_came = along_z(output_weight)

    h1, pre, keep, give, inverse, gains, heads, turned, mixed = attention_forward(
        me, own, packed[0], x_came, x_other, cosine, sine, start, experts, q_heads
    )
    other = send(give, "fsdp", 1)
    mixed_sends, wo_stack = merge(keep, other, output_weight, wo_came)
    mixed_came = along_z(mixed_sends)
    wo_other = send(wo_stack, "fsdp", 1)
    middle, probs, hidden, sent = middle_layer(
        own, keep, other, mixed_came, output_weight, wo_came, wo_other, gains, deal, experts, owners
    )
    h_rows = exchange(sent)
    rows_c, row_mask, back = deal_rows(owner, c_all, down_weight, experts, capacity)
    rows_back, gate_low, up_low, active, weighted, share = expert_layer(
        owner, h_rows, gains, row_mask, back, gate_weight, up_weight, experts
    )
    came_back = exchange(rows_back)
    grads, tick = expert_weights(h_rows, rows_c, gate_low, up_low, weighted)
    grads = lax.psum(grads, "fsdp")
    gate_sum, up_sum, down_sum = widen(grads)
    sent, tick = expert_outputs(active, share, down_weight, owners, after=(tick,))

    middle_grad, middle_low, extra = router_backward(
        came_back, turn, middle, probs, mask, gains, upstream, hidden, experts, after=(tick,)
    )
    da_came, da_other = gather_fsdp(middle_low, "row_middle")
    out_rows = exchange(sent)
    layer_out, _ = layer_output(out_rows, turn, middle)
    first, dh_keep, dh_give = attention_backward(
        me,
        middle_low,
        da_came,
        da_other,
        heads,
        output_weight,
        cosine,
        sine,
        start,
        h1,
        pre,
        mixed,
        inverse,
        turned,
        extra,
        experts,
        q_heads,
    )
    dh_total, *dh_sends = pair_sum(dh_keep, send(dh_give, "fsdp", 1))
    dh_came = along_z(dh_sends)
    tokens_grad = input_grad(dh_total, dh_came, own, gains, middle_grad, experts)
    first = passed(first, after=(out_rows, grads))
    parted, rest = shares_sum(exchange(first), after=tuple(dh_came))
    parted = lax.all_to_all(parted, "fsdp", 0, 0, tiled=True)
    pieces = exchange(whole_pieces(parted, rest, after=(layer_out, tokens_grad)))
    query_sum, key_sum, value_sum, output_sum, one_sum, two_sum, *gain_sums, router_sum = final_grads(
        pieces, query_weight, key_weight, value_weight, first_gain[None], experts
    )
    return (
        layer_out[None],
        tokens_grad[None],
        one_sum[0],
        query_sum,
        key_sum,
        value_sum,
        output_sum,
        gain_sums[0][0],
        gain_sums[1][0],
        two_sum[0],
        router_sum.T,
        gate_sum,
        up_sum,
        down_sum,
    )


def solution(mesh):
    whole = P("expert", "fsdp", None)
    rows = P("fsdp", None)
    vector = P("fsdp")
    owned = P("expert", None, None)
    return jax.shard_map(
        shards,
        mesh=mesh,
        in_specs=(
            whole,
            P("expert", None),
            whole,
            vector,
            rows,
            rows,
            rows,
            rows,
            vector,
            vector,
            vector,
            rows,
            owned,
            owned,
            owned,
            whole,
        ),
        out_specs=(
            whole,
            whole,
            vector,
            rows,
            rows,
            rows,
            rows,
            vector,
            vector,
            vector,
            rows,
            owned,
            owned,
            owned,
        ),
        check_vma=False,
    )
```

```python
import functools

import jax
import jax.numpy as jnp
from jax import lax
from jax.experimental import pallas as pl
from jax.experimental.pallas import tpu as pltpu
from jax.sharding import PartitionSpec as P

EPSILON = 1e-06
ROPE_BASE = 10000.0
HEAD = 64
TILE = 256
F32 = jnp.float32
BF16 = jnp.bfloat16
VMEM = pl.BlockSpec(memory_space=pltpu.VMEM)
SMEM = pl.BlockSpec(memory_space=pltpu.SMEM)
ANY = pl.BlockSpec(memory_space=pl.ANY)
HBM = pl.BlockSpec(memory_space=pltpu.HBM)


def dot(left, right, dims=((1,), (0,))):
    return lax.dot_general(left, right, (dims, ((), ())), preferred_element_type=F32)


def shape(extent, dtype):
    return jax.ShapeDtypeStruct(extent, dtype)


def kernel_call(
    body, name, micros, operands, results, smem=0, hbm=(), out_hbm=(), after=(), scratch=(), held=(), late=(), stored=(), mib=63
):
    held = tuple(held) + tuple(late)
    n, a, r, s = len(operands), len(after), len(results), len(scratch)
    specs = [SMEM if i < smem else HBM if i in held or i in hbm else VMEM for i in range(n)]
    out_specs = [HBM if i in stored or i in out_hbm else VMEM for i in range(r)]
    staged = [pltpu.VMEM(operands[i].shape, operands[i].dtype) for i in held]
    staged += [pltpu.VMEM(*results[i]) for i in stored]
    sems = [pltpu.SemaphoreType.DMA((max(len(held), 1),)), pltpu.SemaphoreType.DMA((max(len(stored), 1),))]

    def wrapped(*refs):
        ins, outs = list(refs[:n]), list(refs[n + a : n + a + r])
        own = refs[n + a + r : n + a + r + s]
        stages, (load_sem, store_sem) = refs[n + a + r + s : -2], refs[-2:]
        loads, stores, begun = {}, {}, []
        for k, i in enumerate(held):
            loads[i] = pltpu.make_async_copy(ins[i], stages[k], load_sem.at[k])
            loads[i].start()
            ins[i] = stages[k]
        for k, i in enumerate(stored):
            stores[i] = pltpu.make_async_copy(stages[len(held) + k], outs[i], store_sem.at[k])
            outs[i] = stages[len(held) + k]
        for i in held:
            if i not in late:
                loads[i].wait()

        def store(*which):
            for i in which:
                stores[i].start()
                begun.append(i)

        extra = {}
        if late:
            extra["wait"] = lambda i: loads[i].wait()
        if stored:
            extra["store"] = store
        body(*ins, *outs, *own, **extra)
        store(*[i for i in stored if i not in begun])
        for i in stored:
            stores[i].wait()

    return pl.pallas_call(
        wrapped,
        out_shape=[shape(*result) for result in results],
        in_specs=specs + [ANY] * a,
        out_specs=out_specs,
        scratch_shapes=list(scratch) + staged + sems,
        compiler_params=pltpu.CompilerParams(vmem_limit_bytes=mib * 1024 * 1024),
        cost_estimate=pl.CostEstimate(flops=0, bytes_accessed=int(micros * 3.6e6), transcendentals=0),
        name=name,
    )(*operands, *after)


def move_call(moves, name, micros, operands, results, after=(), mib=10):
    def body(*refs):
        for source, target in moves(*refs):
            target[...] = source[...]

    return kernel_call(body, name, micros, operands, results, after=after, mib=mib)


def lane_blocks(value):
    return jnp.concatenate([value[:, i : i + 128] for i in range(0, value.shape[1], 128)], axis=0)


def joined_lanes(value, count):
    rows = value.shape[0] // count
    return jnp.concatenate([value[i * rows : (i + 1) * rows] for i in range(count)], axis=1)


def softmax_rows(logits):
    powers = jnp.exp(logits - jnp.max(logits, axis=0, keepdims=True))
    return powers / jnp.sum(powers, axis=0, keepdims=True)


def head_forward(pre, gain, cosine, sine):
    scale = lax.rsqrt(jnp.mean(pre * pre, axis=0, keepdims=True) + EPSILON)
    normed = pre * scale
    scaled = normed * gain
    a, b = scaled[: HEAD // 2], scaled[HEAD // 2 :]
    turned = jnp.concatenate([a * cosine - b * sine, b * cosine + a * sine], axis=0)
    return turned, normed, scale


def head_backward(grad, normed, scale, gain, cosine, sine):
    a, b = grad[: HEAD // 2], grad[HEAD // 2 :]
    unturned = jnp.concatenate([a * cosine + b * sine, b * cosine - a * sine], axis=0)
    gain_grad = jnp.sum(unturned * normed, axis=1, keepdims=True)
    inner = unturned * gain
    pre_grad = scale * (inner - normed * jnp.mean(inner * normed, axis=0, keepdims=True))
    return pre_grad, gain_grad


def slots_kernel(mask_ref, deal_ref, turn_ref, whole_ref, *, capacity, store):
    experts, rows = mask_ref.shape
    mask = mask_ref[...]
    ranks = dot(mask.astype(BF16), earlier(rows))
    slot = lax.broadcasted_iota(jnp.int32, (capacity, rows), 0).astype(F32) + 1.0
    for expert in range(experts):
        one = slice(expert, expert + 1)
        whole_ref[expert * capacity : (expert + 1) * capacity] = jnp.where(
            (ranks[one] == slot) & (mask[one] > 0.5), 1.0, 0.0
        )
    deal_ref[...] = whole_ref[...].astype(BF16)
    store(0)
    for part in range(0, experts * capacity, 128):
        turn_ref[:, part : part + 128] = whole_ref[part : part + 128].T.astype(BF16)


def slot_tables(mask, capacity):
    experts, rows = mask.shape
    slots = experts * capacity
    return kernel_call(
        functools.partial(slots_kernel, capacity=capacity),
        "slot_tables",
        2.0,
        [mask],
        [((slots, rows), BF16), ((rows, slots), BF16)],
        scratch=[pltpu.VMEM((slots, rows), F32)],
        stored=(0, 1),
    )


def earlier(rows):
    return (
        lax.broadcasted_iota(jnp.int32, (rows, rows), 0)
        <= lax.broadcasted_iota(jnp.int32, (rows, rows), 1)
    ).astype(BF16)


def pack_kernel(
    me_ref, x_ref, wq_ref, wk_ref, wv_ref, router_ref, one_ref, two_ref, qg_ref, kg_ref, routes_ref, c_ref, *outs, wait, store
):
    own_ref, sends, dressed_ref, mask_ref, other_ref, parts_ref = outs[0], outs[1:4], *outs[4:]
    experts, rows = router_ref.shape
    wide = wq_ref.shape[1] // 8
    narrow = wk_ref.shape[1] // 8
    count = qg_ref.shape[1]
    heads = jnp.concatenate([qg_ref[...], kg_ref[...]], axis=0).astype(F32)
    heads = jnp.concatenate([heads, jnp.zeros((2, 128 - count), F32)], axis=1)
    heads = jnp.concatenate([heads, jnp.zeros((126, 128), F32)], axis=0).T[:count]
    small = jnp.concatenate(
        [
            router_ref[...].astype(F32),
            one_ref[...].astype(F32),
            two_ref[...].astype(F32),
            jnp.zeros((6, 128), F32),
            heads,
        ],
        axis=0,
    ).astype(BF16)
    for part in range(8):
        parts_ref[part, :wide] = wq_ref[:, part * wide : (part + 1) * wide].astype(F32).T.astype(BF16)
        parts_ref[part, wide + 2 * narrow :] = small
    for pair in range(4):
        span = slice(pair * 128, (pair + 1) * 128)
        for ref, place in ((wk_ref, wide), (wv_ref, wide + narrow)):
            turned = ref[:, span].astype(F32).T.astype(BF16)
            parts_ref[2 * pair, place : place + narrow] = turned[:narrow]
            parts_ref[2 * pair + 1, place : place + narrow] = turned[narrow:]
    me = me_ref[0]
    tall = parts_ref.shape[1]
    blocks = lane_blocks(x_ref[...])
    base = blocks.shape[0]
    own_ref[...] = parts_ref[me]
    other_ref[...] = parts_ref[me ^ 1]
    for flip in range(1, 4):
        sends[flip - 1][:base] = blocks
        sends[flip - 1][base : base + tall] = parts_ref[me ^ (2 * flip)]
        sends[flip - 1][base + tall :] = parts_ref[me ^ (2 * flip + 1)]
    store(1, 2, 3, 6, 0)
    wait(10)
    wait(11)
    width = c_ref.shape[1]
    subs = lax.broadcasted_iota(jnp.int32, (128, rows), 0)
    routed = jnp.zeros((128, rows), F32)
    for route in range(routes_ref.shape[0]):
        routed = routed + jnp.where(routes_ref[route : route + 1] == subs, 1.0, 0.0)
    dressed_ref[:, :width] = c_ref[...]
    dressed_ref[:, width:] = routed.T.astype(BF16)
    mask_ref[...] = routed[:experts]


def pack_weights(me, x, wq, wk, wv, router, one, two, qg, kg, routes, c):
    experts = router.shape[0]
    tall = (wq.shape[1] + wk.shape[1] + wv.shape[1]) // 8 + experts + 16
    rows, width = x.shape
    base = rows * 8
    own, first, second, third, dressed, mask, other = kernel_call(
        pack_kernel,
        "pack_weights",
        2.5,
        [me, x, wq, wk, wv, router, one, two, qg, kg, routes, c],
        [((tall, 128), BF16)]
        + [((base + 2 * tall, 128), BF16)] * 3
        + [((rows, width + 128), BF16), ((experts, rows), F32), ((tall, 128), BF16)],
        smem=1,
        scratch=[pltpu.VMEM((8, tall, 128), BF16)],
        held=range(1, 10),
        late=(10, 11),
        stored=(0, 1, 2, 3, 4, 5, 6),
    )
    return (own, other), [first, second, third], dressed, mask


def relay(came, base, after):
    tall = (came[0].shape[0] - base) // 2

    def moves(*refs):
        pairs = []
        for flip, ref in enumerate(refs[:3]):
            pairs.append((ref.at[:base], refs[3].at[flip, :base]))
            pairs.append((ref.at[base + tall :], refs[3].at[flip, base:]))
        return pairs

    return move_call(moves, "relay", 1.5, came, [((3, base + tall, 128), BF16)], after)[0]


def forward_kernel(me_ref, x_ref, own_ref, *refs, experts, q_heads, store):
    came, other_x, other_w, other_ref = refs[:3], refs[3], refs[4], refs[5]
    cos_ref, sin_ref, start_ref = refs[6:9]
    h1_ref, pre_ref, keep_ref, give_ref, inverse_ref, gains_ref, heads_ref, turned_ref, out_ref = refs[-9:]
    rows, width = x_ref.shape
    q_columns = q_heads * HEAD
    columns = q_columns + 2 * HEAD
    total = rows * 8
    tall = own_ref.shape[0]
    base = 8 * rows
    me = me_ref[0]
    for slot in range(8):
        flip = slot // 2
        if slot % 2:
            piece = other_ref[flip - 1, base:] if flip else other_w[...]
        elif flip:
            piece = came[flip - 1][base : base + tall]
        else:
            piece = own_ref[...]
        span = pl.ds(pl.multiple_of((me ^ slot) * rows, rows), rows)
        turned_ref[:, span] = piece[:columns]
        small = piece[columns:].astype(F32)
        gains_ref[:, span] = small[: experts + 8]
        heads_ref[pl.ds(pl.multiple_of((me ^ slot) * 8, 8), 8)] = small[experts + 8 :]
    gain_one = gains_ref[experts : experts + 1]
    for slot in range(8):
        flip = slot // 2
        if slot % 2:
            x = joined_lanes(other_ref[flip - 1, :base], 8) if flip else other_x[...]
        elif flip:
            x = joined_lanes(came[flip - 1][:base], 8)
        else:
            x = x_ref[...]
        x = x.astype(F32)
        scale = lax.rsqrt(jnp.mean(x * x, axis=1, keepdims=True) + EPSILON)
        h1_ref[slot] = (x * scale * gain_one).astype(BF16)
    store(0, 6, 7)
    for slot in range(8):
        block = dot(turned_ref[...], h1_ref[slot], ((1,), (1,)))
        place = pl.multiple_of((me ^ slot) * rows, rows)
        pre_ref[:, pl.ds(place, rows)] = block
    store(1)
    cosine, sine = cos_ref[...], sin_ref[...]
    gain_query, gain_key = heads_ref[:, :1], heads_ref[:, 1:2]
    key = head_forward(pre_ref[q_columns : q_columns + HEAD], gain_key, cosine, sine)[0]
    key = key.T.astype(BF16)
    value = pre_ref[q_columns + HEAD :].astype(BF16)
    inverse_ref[...] = jnp.zeros(inverse_ref.shape, F32)
    for head in range(q_heads):
        query = head_forward(pre_ref[head * HEAD : (head + 1) * HEAD], gain_query, cosine, sine)[0]
        query = query.astype(BF16) * jnp.array(HEAD ** (-0.5), BF16)
        for tile in range(total // TILE):
            low, high = tile * TILE, (tile + 1) * TILE
            scores = dot(key[:high], query[:, low:high])
            u = lax.broadcasted_iota(jnp.int32, (high, TILE), 0)
            t = lax.broadcasted_iota(jnp.int32, (high, TILE), 1) + low
            allowed = (u >= start_ref[:, low:high]) & (u <= t)
            powers = jnp.where(allowed, jnp.exp(scores), 0.0)
            inverse = 1.0 / jnp.sum(powers, axis=0, keepdims=True)
            probs = (powers * inverse).astype(BF16)
            mixed = dot(value[:, :high], probs).astype(BF16)
            inverse_ref[head : head + 1, low:high] = inverse
            for part in range(TILE // rows):
                out_ref[low // rows + part, head * HEAD : (head + 1) * HEAD] = mixed[
                    :, part * rows : (part + 1) * rows
                ]
    for slot in range(8):
        (give_ref if slot % 2 else keep_ref)[slot // 2] = out_ref[me ^ slot]


def attention_forward(me, x, own, came, other, cosine, sine, start, experts, q_heads, after=()):
    rows, width = x.shape
    total = 8 * rows
    columns = (q_heads + 2) * HEAD
    q_columns = q_heads * HEAD
    return kernel_call(
        functools.partial(forward_kernel, experts=experts, q_heads=q_heads),
        "attention_forward",
        7.0,
        [me, x, own, *came, *other, cosine, sine, start],
        [
            ((8, rows, width), BF16),
            ((columns, total), F32),
            ((4, q_columns, rows), BF16),
            ((4, q_columns, rows), BF16),
            ((8, total), F32),
            ((experts + 8, width), F32),
            ((HEAD, 128), F32),
            ((columns, width), BF16),
            ((8, q_columns, rows), BF16),
        ],
        smem=1,
        after=after,
        held=(1,),
        stored=(0, 1, 4, 6, 7, 8),
    )


def merge(keep, came, wo, wo_came):
    def moves(keep_ref, came_ref, *refs):
        weights, outs, stacked = refs[:4], refs[4:7], refs[7]
        pairs = [(weight, stacked.at[i]) for i, weight in enumerate(weights)]
        for flip in range(1, 4):
            pairs.append((keep_ref.at[flip], outs[flip - 1].at[0]))
            pairs.append((came_ref.at[flip], outs[flip - 1].at[1]))
        return pairs

    extent = ((2,) + keep.shape[1:], BF16)
    results = [extent] * 3 + [((4,) + wo.shape, BF16)]
    *sends, stacked = move_call(moves, "merge", 1.0, [keep, came, wo, *wo_came], results)
    return sends, stacked


def middle_kernel(x_ref, keep_ref, other_ref, *refs, experts, wait, store):
    came, wo_ref, wo_came, wo_other_ref, gains_ref, deal_ref = refs[:3], refs[3], refs[4:7], refs[7], refs[8], refs[9]
    middle_ref, probs_ref, hidden_ref, sent_ref, mixed_ref, whole_ref, out_ref, out_sem = refs[10:]
    rows, width = x_ref.shape
    for slot in range(8):
        flip, core = slot // 2, slot % 2
        if flip:
            piece = came[flip - 1][core]
        else:
            piece = (other_ref if core else keep_ref)[0]
        span = slice(slot * 128, (slot + 1) * 128)
        mixed_ref[:, span] = piece.astype(F32).T.astype(BF16)
    for i in (6, 7, 8, 9, 10):
        wait(i)
    for slot in range(8):
        flip = slot // 2
        span = slice(slot * 128, (slot + 1) * 128)
        if slot % 2:
            whole_ref[span] = wo_other_ref[flip]
        else:
            whole_ref[span] = (wo_came[flip - 1] if flip else wo_ref)[...]
    wait(0)
    middle = x_ref[...].astype(F32) + dot(mixed_ref[...], whole_ref[...])
    middle_ref[...] = middle
    scale = lax.rsqrt(jnp.mean(middle * middle, axis=1, keepdims=True) + EPSILON)
    hidden = (middle * scale * gains_ref[experts + 1 : experts + 2]).astype(BF16)
    hidden_ref[...] = hidden
    probs_ref[...] = softmax_rows(dot(gains_ref[:experts].astype(BF16), hidden, ((1,), (1,))))
    store(0, 2)
    owners, per_owner, capacity, _ = sent_ref.shape
    group = owners // 4
    size = group * per_owner * capacity
    copies = []
    wait(12)
    for part in range(4):
        taken = dot(deal_ref[part * size : (part + 1) * size], hidden).astype(BF16)
        blocks = slice(group * part, group * (part + 1))
        out_ref[blocks] = taken.reshape(group, per_owner, capacity, width)
        copies.append(pltpu.make_async_copy(out_ref.at[blocks], sent_ref.at[blocks], out_sem.at[part]))
        copies[-1].start()
    for copy in copies:
        copy.wait()


def middle_layer(x, keep, other, came, wo, wo_came, wo_other, gains, deal, experts, owners):
    rows, width = x.shape
    per_owner = experts // owners
    capacity = deal.shape[0] // experts
    sent = ((owners, per_owner, capacity, width), BF16)
    return kernel_call(
        functools.partial(middle_kernel, experts=experts),
        "middle_layer",
        3.0,
        [x, keep, other, *came, wo, *wo_came, wo_other, gains, deal],
        [((rows, width), F32), ((experts, rows), F32), ((rows, width), BF16), sent],
        out_hbm=(3,),
        scratch=[
            pltpu.VMEM((rows, width), BF16),
            pltpu.VMEM((width, width), BF16),
            pltpu.VMEM(*sent),
            pltpu.SemaphoreType.DMA((4,)),
        ],
        late=(6, 7, 8, 9, 10, 0, 12),
        stored=(0, 2),
    )


def row(pieces, name):
    def moves(*refs):
        return [(ref, refs[-1].at[i]) for i, ref in enumerate(refs[:-1])]

    return move_call(moves, name, 1.0, pieces, [((len(pieces),) + pieces[0].shape, BF16)])[0]


def backward_kernel(me_ref, own_da_ref, *refs, experts, q_heads, wait):
    came, other_ref = refs[:3], refs[3]
    heads_ref, wo_ref, cos_ref, sin_ref, start_ref = refs[4:9]
    h1_ref, pre_ref, mixed_ref, inverse_ref, turned_ref, extra_ref = refs[9:15]
    first_ref, keep_ref, send_ref = refs[-10:-7]
    da_ref, mixed_grad_ref, dkey_ref, dvalue_ref, low_ref, out_slots_ref, grad_ref = refs[-7:]
    rows, width = own_da_ref.shape
    q_columns = q_heads * HEAD
    columns = q_columns + 2 * HEAD
    total = rows * 8
    me = me_ref[0]
    for slot in range(8):
        flip, core = slot // 2, slot % 2
        if core:
            piece = other_ref[flip]
        else:
            piece = (came[flip - 1] if flip else own_da_ref)[...]
        span = slice(slot * rows, (slot + 1) * rows)
        da_ref[span] = piece
        place = pl.multiple_of((me ^ slot) * rows, rows)
        mixed_grad_ref[:, pl.ds(place, rows)] = dot(wo_ref[...], piece, ((1,), (1,))).astype(BF16)
    wait(13)
    for slot in range(8):
        out_slots_ref[:, slot * rows : (slot + 1) * rows] = mixed_ref[me ^ slot]
    wo_grad = dot(out_slots_ref[...], da_ref[...]).astype(BF16)
    wo_grad = lane_blocks(wo_grad)
    wait(12)
    wait(14)
    gain_query, gain_key = heads_ref[:, :1], heads_ref[:, 1:2]
    cosine, sine = cos_ref[...], sin_ref[...]
    key_turned, key_normed, key_scale = head_forward(
        pre_ref[q_columns : q_columns + HEAD], gain_key, cosine, sine
    )
    key_low = key_turned.astype(BF16)
    key = key_turned.T.astype(BF16)
    value = pre_ref[q_columns + HEAD :].T.astype(BF16)
    dkey_ref[...] = jnp.zeros(dkey_ref.shape, F32)
    dvalue_ref[...] = jnp.zeros(dvalue_ref.shape, F32)
    gain_query_grad = jnp.zeros((HEAD, 1), F32)
    pieces = []
    for head in range(q_heads):
        span = slice(head * HEAD, (head + 1) * HEAD)
        turned, normed, scale = head_forward(pre_ref[span], gain_query, cosine, sine)
        query = turned.astype(BF16) * jnp.array(HEAD ** (-0.5), BF16)
        grads = []
        for tile in range(total // TILE):
            low, high = tile * TILE, (tile + 1) * TILE
            part = query[:, low:high]
            mixed_grad = mixed_grad_ref[span, low:high]
            scores = dot(key[:high], part)
            u = lax.broadcasted_iota(jnp.int32, (high, TILE), 0)
            t = lax.broadcasted_iota(jnp.int32, (high, TILE), 1) + low
            allowed = (u >= start_ref[:, low:high]) & (u <= t)
            probs = jnp.where(allowed, jnp.exp(scores) * inverse_ref[head : head + 1, low:high], 0.0)
            attend = dot(value[:high], mixed_grad)
            delta = jnp.sum(probs * attend, axis=0, keepdims=True)
            score_low = (probs * (attend - delta)).astype(BF16)
            grads.append(dot(key_low[:, :high], score_low))
            dkey_ref[:, :high] += dot(part, score_low, ((1,), (1,)))
            dvalue_ref[:, :high] += dot(mixed_grad, probs.astype(BF16), ((1,), (1,)))
        query_grad = jnp.concatenate(grads, axis=1) * HEAD ** (-0.5)
        pre_grad, gain_grad = head_backward(query_grad, normed, scale, gain_query, cosine, sine)
        gain_query_grad += gain_grad
        pieces.append(pre_grad)
    pre_grad, gain_key_grad = head_backward(
        dkey_ref[...], key_normed, key_scale, gain_key, cosine, sine
    )
    pieces += [pre_grad, dvalue_ref[...]]
    pre_grad = jnp.concatenate(pieces, axis=0)
    low_ref[...] = pre_grad.astype(BF16)
    slots_grad = []
    for slot in range(8):
        place = pl.multiple_of((me ^ slot) * rows, rows)
        slots_grad.append(low_ref[:, pl.ds(place, rows)])
    slots_grad = jnp.concatenate(slots_grad, axis=1)
    wait(11)
    wait(15)
    grad_ref[:columns] = dot(slots_grad, h1_ref[...].reshape(total, width))
    extra = extra_ref[...]
    lane = lax.broadcasted_iota(jnp.int32, (HEAD, 128), 1)
    gains = jnp.where(lane == 0, gain_query_grad, jnp.where(lane == 1, gain_key_grad, 0.0))
    gains = gains.T[:2]
    step = HEAD // 8
    grad_ref[columns:] = jnp.zeros((64, width), F32)
    grad_ref[columns : columns + experts + 1] = extra[: experts + 1]
    for part in range(8):
        grad_ref[columns + experts + 1 : columns + experts + 3, part * rows : part * rows + step] = gains[
            :, part * step : (part + 1) * step
        ]
    for piece in range(16):
        spare = []
        place = columns + piece * SPARE
        for part in range(8):
            span = slice(part * rows, (part + 1) * rows)
            block = grad_ref[piece * PIECE : (piece + 1) * PIECE, span]
            first_ref[piece, part * PIECE : (part + 1) * PIECE] = block.astype(BF16)
            spare.append(grad_ref[place : place + SPARE, span])
        spare.append(jnp.zeros((2 * PIECE - 8 * SPARE, 128), F32))
        first_ref[piece, 8 * PIECE : 10 * PIECE] = jnp.concatenate(spare, axis=0).astype(BF16)
        first_ref[piece, 10 * PIECE :] = wo_grad[piece * SLICE : (piece + 1) * SLICE]
    turned = turned_ref[...]
    for slot in range(8):
        low_rows_slot = slots_grad[:, slot * rows : (slot + 1) * rows].astype(F32).T.astype(BF16)
        part = dot(low_rows_slot, turned)
        if slot % 2:
            send_ref[slot // 2] = part.astype(BF16)
        else:
            keep_ref[slot // 2] = part


def attention_backward(
    me, da, came, other, heads, wo, cosine, sine, start, h1, pre, mixed, inverse, turned, extra, experts, q_heads, after=()
):
    rows, width = da.shape
    total = 8 * rows
    columns = pre.shape[0]
    q_columns = q_heads * HEAD
    return kernel_call(
        functools.partial(backward_kernel, experts=experts, q_heads=q_heads),
        "attention_backward",
        12,
        [me, da, *came, other, heads, wo, cosine, sine, start, h1, pre, mixed, inverse, turned, extra],
        [
            ((16, 10 * PIECE + SLICE, 128), BF16),
            ((4, rows, width), F32),
            ((4, rows, width), BF16),
        ],
        smem=1,
        after=after,
        held=(6, 7),
        late=(11, 12, 13, 14, 15),
        scratch=[
            pltpu.VMEM((total, width), BF16),
            pltpu.VMEM((q_columns, total), BF16),
            pltpu.VMEM((HEAD, total), F32),
            pltpu.VMEM((HEAD, total), F32),
            pltpu.VMEM((columns, total), BF16),
            pltpu.VMEM((q_columns, total), BF16),
            pltpu.VMEM((columns + 64, width), F32),
        ],
    )


def deal_kernel(owner_ref, c_ref, down_ref, rows_c, mask_ref, back_ref, c_scratch, sems, *, experts, capacity, wait, store):
    owner = owner_ref[0]
    per_owner, hidden, width = down_ref.shape
    rows = c_ref.shape[1]
    loads = [pltpu.make_async_copy(c_ref.at[i], c_scratch.at[i], sems.at[i]) for i in range(16)]
    for load in loads:
        load.start()
    lanes = lax.broadcasted_iota(jnp.int32, (experts, 128), 1)
    subs = lax.broadcasted_iota(jnp.int32, (experts, 128), 0)
    eye = (lanes == subs).astype(BF16)
    before = earlier(rows)
    mine_of = lax.broadcasted_iota(jnp.int32, (experts, rows), 0) - owner * per_owner
    slot = lax.broadcasted_iota(jnp.int32, (capacity, rows), 0).astype(F32) + 1.0
    for block in range(16):
        loads[block].wait()
        c = c_scratch[block]
        mask = dot(eye, c[:, width:], ((1,), (1,)))
        ranks = dot(mask.astype(BF16), before)
        deals = []
        for k in range(per_owner):
            mine = mine_of == k
            hit = jnp.sum(jnp.where(mine, mask, 0.0), axis=0, keepdims=True)
            rank = jnp.sum(jnp.where(mine, ranks, 0.0), axis=0, keepdims=True)
            deals.append(jnp.where((rank == slot) & (hit > 0.5), 1.0, 0.0))
        taken = dot(jnp.concatenate(deals, axis=0).astype(BF16), c).astype(BF16)
        span = slice(block * capacity, (block + 1) * capacity)
        for k in range(per_owner):
            spot = slice(k * capacity, (k + 1) * capacity)
            rows_c[k, span] = taken[spot, :width]
            mask_ref[k, span] = taken[spot, width:]
    store(0, 1)
    wait(2)
    for k in range(per_owner):
        for tile in range(16 * capacity // TILE):
            span = slice(tile * TILE, (tile + 1) * TILE)
            back_ref[k, span] = dot(rows_c[k, span], down_ref[k], ((1,), (1,)))


def deal_rows(owner, c, down, experts, capacity):
    per_owner, hidden, width = down.shape
    count = 16 * capacity
    return kernel_call(
        functools.partial(deal_kernel, experts=experts, capacity=capacity),
        "deal_rows",
        12.0,
        [owner, c, down],
        [
            ((per_owner, count, width), BF16),
            ((per_owner, count, 128), BF16),
            ((per_owner, count, hidden), F32),
        ],
        smem=1,
        hbm=(1,),
        scratch=[pltpu.VMEM(c.shape, BF16), pltpu.SemaphoreType.DMA((16,))],
        late=(2,),
        stored=(0, 1, 2),
    )


def expert_kernel(
    owner_ref,
    h_hbm,
    gains_ref,
    mask_ref,
    back_hbm,
    gate_hbm,
    up_hbm,
    rows_hbm,
    gate_out,
    up_out,
    active_out,
    weighted_out,
    share_ref,
    h_ref,
    back_in,
    gate_ref,
    up_ref,
    rows_back,
    load_sem,
    store_sem,
    *,
    experts,
    store,
):
    owners, per_owner, capacity, width = h_hbm.shape
    group = 8
    parts = owners // group
    size = group * capacity
    loads = {}
    for k in range(per_owner):
        for part in range(parts):
            blocks = slice(part * group, (part + 1) * group)
            spot = (k * parts + part) * 4
            loads[k, part] = [
                pltpu.make_async_copy(h_hbm.at[blocks, k], h_ref.at[blocks, k], load_sem.at[spot]),
                pltpu.make_async_copy(
                    back_hbm.at[k, part * size : (part + 1) * size],
                    back_in.at[k, part * size : (part + 1) * size],
                    load_sem.at[spot + 1],
                ),
            ]
            if part == 0:
                loads[k, part] += [
                    pltpu.make_async_copy(gate_hbm.at[k], gate_ref.at[k], load_sem.at[spot + 2]),
                    pltpu.make_async_copy(up_hbm.at[k], up_ref.at[k], load_sem.at[spot + 3]),
                ]
            for load in loads[k, part]:
                load.start()
    owner = owner_ref[0]
    router = jnp.concatenate([gains_ref[:experts], jnp.zeros((128 - experts, width), F32)], axis=0)
    router = router.astype(BF16)
    lane = lax.broadcasted_iota(jnp.int32, (size, 128), 1)
    copies = []
    for k in range(per_owner):
        place = owner * per_owner + k
        for part in range(parts):
            blocks = slice(part * group, (part + 1) * group)
            span = slice(part * size, (part + 1) * size)
            for load in loads[k, part]:
                load.wait()
            h = h_ref[blocks, k].reshape(size, width)
            gate = dot(h, gate_ref[k])
            up = dot(h, up_ref[k])
            logits = dot(h, router, ((1,), (1,)))
            chosen = mask_ref[k, span] > 0.5
            top = jnp.max(jnp.where(chosen, logits, -1e30), axis=1, keepdims=True)
            powers = jnp.where(chosen, jnp.exp(logits - top), 0.0)
            total = jnp.sum(powers, axis=1, keepdims=True)
            share = jnp.sum(jnp.where(lane == place, powers, 0.0), axis=1, keepdims=True)
            share = share / jnp.where(total > 0.0, total, 1.0)
            share_ref[k, span] = jnp.broadcast_to(share, (size, 128))
            back = back_in[k, span]
            sig = 1.0 / (1.0 + jnp.exp(-gate))
            silu = gate * sig
            active = silu * up
            active_low = active.astype(BF16)
            route_grad = jnp.sum(active_low.astype(F32) * back, axis=1, keepdims=True)
            grad = back * share
            gate_low = (grad * up * (sig + silu * (1.0 - sig))).astype(BF16)
            up_low = (grad * silu).astype(BF16)
            active_out[k, span] = active_low
            weighted_out[k, span] = (active * share).astype(BF16)
            gate_out[k, span] = gate_low
            up_out[k, span] = up_low
            rows = dot(gate_low, gate_ref[k], ((1,), (1,))) + dot(up_low, up_ref[k], ((1,), (1,)))
            high = route_grad.astype(BF16).astype(F32)
            spread_out = jnp.where(lane == place, high, 0.0)
            spread_out = jnp.where(lane == place + experts, route_grad - high, spread_out)
            whole = jnp.concatenate([rows.astype(BF16), spread_out.astype(BF16)], axis=1)
            rows_back[blocks, k] = whole.reshape(group, capacity, width + 128)
            copies.append(
                pltpu.make_async_copy(
                    rows_back.at[blocks, k], rows_hbm.at[blocks, k], store_sem.at[k * parts + part]
                )
            )
            copies[-1].start()
    store(1, 2, 3, 4, 5)
    for copy in copies:
        copy.wait()


def expert_layer(owner, h, gains, mask, back, gate, up, experts):
    per_owner, width, hidden = gate.shape
    owners, _, capacity, _ = h.shape
    count = owners * capacity
    narrow = ((per_owner, count, hidden), BF16)
    rows_back = ((owners, per_owner, capacity, width + 128), BF16)
    pieces = per_owner * (owners // 8)
    return kernel_call(
        functools.partial(expert_kernel, experts=experts),
        "expert_layer",
        14.0,
        [owner, h, gains, mask, back, gate, up],
        [rows_back] + [narrow] * 4 + [((per_owner, count, 128), F32)],
        smem=1,
        hbm=(1, 4, 5, 6),
        out_hbm=(0,),
        scratch=[pltpu.VMEM(value.shape, value.dtype) for value in (h, back, gate, up)]
        + [pltpu.VMEM(*rows_back), pltpu.SemaphoreType.DMA((4 * pieces,)), pltpu.SemaphoreType.DMA((pieces,))],
        stored=(1, 2, 3, 4, 5),
    )


def weights_kernel(
    h_hbm, rows_c, gate_low, up_low, weighted, out_hbm, tick_ref, h_ref, out_ref, load_sem, store_sem, *, wait
):
    tick_ref[...] = jnp.zeros(tick_ref.shape, F32)
    first = ((0,), (0,))
    owners, per_owner, capacity, width = h_hbm.shape
    hidden = gate_low.shape[2]
    half = width // 2
    loads = [
        pltpu.make_async_copy(h_hbm.at[:, k], h_ref.at[:, k], load_sem.at[k]) for k in range(per_owner)
    ]
    for load in loads:
        load.start()
    stores = []

    def keep(place):
        stores.append(pltpu.make_async_copy(out_ref.at[place], out_hbm.at[place], store_sem.at[place]))
        stores[-1].start()

    wait(2)
    for k in range(per_owner):
        loads[k].wait()
        rows_h = h_ref[:, k].reshape(owners * capacity, width)
        for place, low in ((k, gate_low), (per_owner + k, up_low)):
            if k == 0 and place:
                wait(3)
            total = dot(rows_h, low[k], first).astype(BF16)
            out_ref[place, :, :hidden] = total[:half]
            out_ref[place, :, hidden:] = total[half:]
            keep(place)
        if k == 0:
            wait(4)
            wait(1)
        place = 2 * per_owner + k
        out_ref[place] = dot(weighted[k], rows_c[k], first).astype(BF16)
        keep(place)
    for store in stores:
        store.wait()


def expert_weights(h, rows_c, gate_low, up_low, weighted):
    per_owner, count, width = rows_c.shape
    hidden = gate_low.shape[2]
    out = ((3 * per_owner, hidden, width), BF16)
    return kernel_call(
        weights_kernel,
        "expert_weights",
        0.1,
        [h, rows_c, gate_low, up_low, weighted],
        [out, ((8, 128), F32)],
        hbm=(0,),
        out_hbm=(0,),
        scratch=[
            pltpu.VMEM(h.shape, BF16),
            pltpu.VMEM(*out),
            pltpu.SemaphoreType.DMA((per_owner,)),
            pltpu.SemaphoreType.DMA((3 * per_owner,)),
        ],
        late=(2, 3, 4, 1),
    )


def widen_kernel(low_ref, gate_ref, up_ref, down_ref):
    step = pl.program_id(0)
    hidden = gate_ref.shape[2]
    value = low_ref[0].astype(F32)
    half = value.shape[0]
    for place, ref in ((0, gate_ref), (1, up_ref)):

        @pl.when(step // 2 == place)
        def _():
            ref[0, :half] = value[:, :hidden]
            ref[0, half:] = value[:, hidden:]

    @pl.when(step // 2 == 2)
    def _():
        down_ref[0] = value


def widen(low):
    count, hidden, width = low.shape
    per_owner = count // 3

    def spot(place):
        return lambda i: (jnp.clip(i - place * per_owner, 0, per_owner - 1), 0, 0)

    return pl.pallas_call(
        widen_kernel,
        grid=(count,),
        out_shape=[shape((per_owner, width, hidden), F32)] * 2 + [shape((per_owner, hidden, width), F32)],
        in_specs=[pl.BlockSpec((1, hidden, width), lambda i: (i, 0, 0))],
        out_specs=[
            pl.BlockSpec((1, width, hidden), spot(0)),
            pl.BlockSpec((1, width, hidden), spot(1)),
            pl.BlockSpec((1, hidden, width), spot(2)),
        ],
        compiler_params=pltpu.CompilerParams(vmem_limit_bytes=63 * 1024 * 1024),
        cost_estimate=pl.CostEstimate(flops=0, bytes_accessed=24_000_000, transcendentals=0),
        name="widen",
    )(low)


def outputs_kernel(active, share, down_ref, sent_ref, tick_ref, out_ref, out_sem, *, wait):
    tick_ref[...] = jnp.zeros(tick_ref.shape, F32)
    per_owner, count, hidden = active.shape
    owners, _, capacity, width = sent_ref.shape
    group = 8
    size = group * capacity
    copies = []
    for i in range(3):
        wait(i)
    for k in range(per_owner):
        for part in range(owners // group):
            span = slice(part * size, (part + 1) * size)
            blocks = slice(part * group, (part + 1) * group)
            produced = dot(active[k, span], down_ref[k]).astype(BF16).astype(F32)
            produced = (produced * share[k, span, :1]).astype(BF16)
            out_ref[blocks, k] = produced.reshape(group, capacity, width)
            copies.append(
                pltpu.make_async_copy(
                    out_ref.at[blocks, k], sent_ref.at[blocks, k], out_sem.at[k * (owners // group) + part]
                )
            )
            copies[-1].start()
    for copy in copies:
        copy.wait()


def expert_outputs(active, share, down, owners, after=()):
    per_owner, count, hidden = active.shape
    width = down.shape[2]
    sent = ((owners, per_owner, count // owners, width), BF16)
    return kernel_call(
        outputs_kernel,
        "expert_outputs",
        0.1,
        [active, share, down],
        [sent, ((8, 128), F32)],
        out_hbm=(0,),
        after=after,
        scratch=[pltpu.VMEM(*sent), pltpu.SemaphoreType.DMA((per_owner * (owners // 8),))],
        late=(0, 1, 2),
    )


def combined(rows_hbm, rows_ref, sems, turn_ref, ready):
    owners, per_owner, capacity, wide = rows_hbm.shape
    group = owners // 4
    size = group * per_owner * capacity
    loads = []
    for part in range(4):
        blocks = slice(part * group, (part + 1) * group)
        loads.append(pltpu.make_async_copy(rows_hbm.at[blocks], rows_ref.at[blocks], sems.at[part]))
        loads[-1].start()
    ready()
    total = None
    for part in range(4):
        loads[part].wait()
        rows = rows_ref[part * group : (part + 1) * group].reshape(size, wide)
        one = dot(turn_ref[:, part * size : (part + 1) * size], rows)
        total = one if total is None else total + one
    return total


def output_kernel(rows_hbm, turn_ref, middle_ref, out_ref, tick_ref, rows_ref, sems, *, wait, store):
    tick_ref[...] = jnp.zeros(tick_ref.shape, F32)
    total = combined(rows_hbm, rows_ref, sems, turn_ref, lambda: wait(1))
    wait(2)
    out_ref[...] = (middle_ref[...] + total).astype(BF16)


def layer_output(rows, turn, middle):
    return kernel_call(
        output_kernel,
        "layer_output",
        3,
        [rows, turn, middle],
        [(middle.shape, BF16), ((8, 128), F32)],
        hbm=(0,),
        scratch=[pltpu.VMEM(rows.shape, BF16), pltpu.SemaphoreType.DMA((4,))],
        late=(1, 2),
        stored=(0,),
    )


def router_kernel(
    rows_hbm,
    turn_ref,
    middle_ref,
    probs_ref,
    mask_ref,
    gains_ref,
    c_ref,
    hidden_ref,
    grad_ref,
    send_ref,
    extra_ref,
    rows_ref,
    sems,
    *,
    experts,
    wait,
    store,
):
    rows, width = middle_ref.shape
    returned = combined(rows_hbm, rows_ref, sems, turn_ref, lambda: wait(1))
    for i in (2, 4, 6, 7):
        wait(i)
    tail = returned[:, width:].T
    route_grad = tail[:experts] + tail[experts : 2 * experts]
    mask = mask_ref[...]
    probs = probs_ref[...]
    picked = probs * mask
    picked_sum = jnp.sum(picked, axis=0, keepdims=True)
    share = picked / picked_sum
    picked_grad = (route_grad - jnp.sum(route_grad * share, axis=0, keepdims=True)) / picked_sum
    prob_grad = mask * picked_grad
    logit_grad = probs * (prob_grad - jnp.sum(probs * prob_grad, axis=0, keepdims=True))
    extra_ref[:experts] = dot(logit_grad.astype(BF16), hidden_ref[...])
    logit_rows = jnp.concatenate([logit_grad, jnp.zeros((128 - experts, rows), F32)], axis=0).T
    router = gains_ref[:experts].astype(BF16)
    hidden_grad = returned[:, :width] + dot(logit_rows[:, :experts].astype(BF16), router)
    middle = middle_ref[...]
    scale = lax.rsqrt(jnp.mean(middle * middle, axis=1, keepdims=True) + EPSILON)
    normed = middle * scale
    extra_ref[experts : experts + 8] = jnp.broadcast_to(
        jnp.sum(hidden_grad * normed, axis=0, keepdims=True), (8, width)
    )
    inner = hidden_grad * gains_ref[experts + 1 : experts + 2]
    grad = c_ref[...].astype(F32) + scale * (
        inner - normed * jnp.mean(inner * normed, axis=1, keepdims=True)
    )
    grad_ref[...] = grad
    send_ref[...] = grad.astype(BF16)


def router_backward(rows_back, turn, middle, probs, mask, gains, c, hidden, experts, after=()):
    rows, width = middle.shape
    return kernel_call(
        functools.partial(router_kernel, experts=experts),
        "router_backward",
        5,
        [rows_back, turn, middle, probs, mask, gains, c, hidden],
        [((rows, width), F32), ((rows, width), BF16), ((experts + 8, width), F32)],
        hbm=(0,),
        after=after,
        scratch=[pltpu.VMEM(rows_back.shape, BF16), pltpu.SemaphoreType.DMA((4,))],
        late=(1, 2, 4, 6, 7),
        stored=(0,),
    )


def pair_kernel(keep_ref, other_ref, total_ref, *sends):
    for flip in range(4):
        total = keep_ref[flip] + other_ref[flip].astype(F32)
        if flip:
            sends[flip - 1][...] = total.astype(BF16)
        else:
            total_ref[...] = total


def pair_sum(keep, other):
    rows, width = keep.shape[1:]
    return kernel_call(
        pair_kernel, "pair_sum", 1.2, [keep, other], [((rows, width), F32)] + [((rows, width), BF16)] * 3
    )


def input_kernel(total_ref, *refs, experts, store):
    came = refs[:3]
    x_ref, gains_ref, middle_grad_ref, out_ref = refs[3:]
    total = total_ref[...]
    for piece in came:
        total = total + piece[...].astype(F32)
    x = x_ref[...].astype(F32)
    scale = lax.rsqrt(jnp.mean(x * x, axis=1, keepdims=True) + EPSILON)
    normed = x * scale
    inner = total * gains_ref[experts : experts + 1]
    out_ref[...] = middle_grad_ref[...] + scale * (
        inner - normed * jnp.mean(inner * normed, axis=1, keepdims=True)
    )


def input_grad(total, came, x, gains, middle_grad, experts):
    return kernel_call(
        functools.partial(input_kernel, experts=experts),
        "input_grad",
        2,
        [total, *came, x, gains, middle_grad],
        [(middle_grad.shape, F32)],
        held=(4, 6),
        stored=(0,),
    )[0]


PIECE, SPARE, SLICE = 16, 3, 64


def passed(value, after):
    results = [(value.shape, value.dtype)]
    return move_call(lambda *refs: [refs], "passed", 0.5, [value], results, after, 63)[0]


def shares_kernel(pieces_ref, out_ref, rest_ref):
    total = pieces_ref[0].astype(F32)
    for i in range(1, pieces_ref.shape[0]):
        total = total + pieces_ref[i].astype(F32)
    base = 8 * PIECE
    fill = jnp.zeros((PIECE - SPARE, 128), F32)
    for part in range(8):
        out_ref[part, :PIECE] = total[part * PIECE : (part + 1) * PIECE].astype(BF16)
        spare = total[base + part * SPARE : base + (part + 1) * SPARE]
        out_ref[part, PIECE:] = jnp.concatenate([spare, fill], axis=0).astype(BF16)
    rest_ref[...] = total[base + 2 * PIECE :].astype(BF16)


def shares_sum(pieces, after=()):
    return kernel_call(
        shares_kernel,
        "shares_sum",
        0.1,
        [pieces],
        [((8, 2 * PIECE, 128), BF16), ((SLICE, 128), BF16)],
        after=after,
    )


def whole_kernel(came_ref, rest_ref, out_ref):
    spare = came_ref[0, PIECE:].astype(F32)
    for i in range(1, 8):
        spare = spare + came_ref[i, PIECE:].astype(F32)
    rows = [came_ref[i, :PIECE] for i in range(8)] + [spare.astype(BF16), rest_ref[...]]
    rows = jnp.concatenate(rows, axis=0)
    for i in range(16):
        out_ref[i] = rows


def whole_pieces(came, rest, after=()):
    return kernel_call(
        whole_kernel,
        "whole_pieces",
        0.1,
        [came, rest],
        [((16, 9 * PIECE + SLICE, 128), BF16)],
        after=after,
    )[0]


def final_kernel(pieces_ref, wq_ref, wk_ref, wv_ref, gain_ref, *outs, experts):
    query_ref, key_ref, value_ref, output_ref, one_ref, two_ref, qg_ref, kg_ref, router_ref = outs
    rows = pieces_ref.shape[2]
    q_columns = query_ref.shape[1] // 8
    kv_columns = key_ref.shape[1] // 8
    sums = jnp.zeros((rows, 1), F32)
    base = 8 * PIECE
    for pair in range(4):
        keys, values = [], []
        for source in (2 * pair, 2 * pair + 1):
            block = [pieces_ref[i, source * PIECE : (source + 1) * PIECE] for i in range(16)]
            turned = jnp.concatenate(block, axis=0).astype(F32).T
            span = slice(source * q_columns, (source + 1) * q_columns)
            query = turned[:, :q_columns]
            query_ref[:, span] = query
            sums = sums + jnp.sum(query * wq_ref[:, span].astype(F32), axis=1, keepdims=True)
            keys.append(turned[:, q_columns : q_columns + kv_columns])
            values.append(turned[:, q_columns + kv_columns :])
        span = slice(2 * pair * kv_columns, 2 * (pair + 1) * kv_columns)
        for parts, ref, weight in ((keys, key_ref, wk_ref), (values, value_ref, wv_ref)):
            both = jnp.concatenate(parts, axis=1)
            ref[:, span] = both
            sums = sums + jnp.sum(both * weight[:, span].astype(F32), axis=1, keepdims=True)
    for i in range(16):
        half = i % 2 * SLICE
        output_ref[half : half + SLICE, i // 2 * rows : (i // 2 + 1) * rows] = pieces_ref[
            i, base + PIECE :
        ].astype(F32)
    spare = pieces_ref[:, base : base + PIECE].astype(F32)
    spare = jnp.concatenate([spare[i, :SPARE] for i in range(16)], axis=0)
    one_ref[...] = jnp.broadcast_to(sums, (rows, 128)).T[:1] / gain_ref[...].astype(F32)
    two_ref[...] = spare[experts : experts + 1]
    step = qg_ref.shape[1]
    qg_ref[...] = spare[experts + 1 : experts + 2, :step]
    kg_ref[...] = spare[experts + 2 : experts + 3, :step]
    router_ref[...] = spare[:experts]


def final_grads(pieces, wq, wk, wv, gain, experts):
    rows = pieces.shape[2]
    return kernel_call(
        functools.partial(final_kernel, experts=experts),
        "final_grads",
        0.2,
        [pieces, wq, wk, wv, gain],
        [
            (wq.shape, F32),
            (wk.shape, F32),
            (wv.shape, F32),
            ((rows, 8 * rows), F32),
            ((1, rows), F32),
            ((1, rows), F32),
            ((1, HEAD // 8), F32),
            ((1, HEAD // 8), F32),
            ((experts, rows), F32),
        ],
        held=(1, 2, 3, 4),
    )


def send(values, axis, flip):
    count = lax.axis_size(axis)
    return lax.ppermute(values, axis, [(i, i ^ flip) for i in range(count)])


def along_z(values):
    if not isinstance(values, (list, tuple)):
        values = [values] * 3
    return [send(value, "fsdp", 2 * (i + 1)) for i, value in enumerate(values)]


def gather_fsdp(block, name):
    came = along_z(block)
    return came, send(row([block, *came], name), "fsdp", 1)


def exchange(rows):
    return lax.all_to_all(rows, "expert", 0, 0, tiled=True)


def shards(
    tokens,
    lengths,
    routes,
    first_gain,
    query_weight,
    key_weight,
    value_weight,
    output_weight,
    query_gain,
    key_gain,
    second_gain,
    router_weight,
    gate_weight,
    up_weight,
    down_weight,
    cotangent,
):
    own = tokens[0]
    upstream = cotangent[0]
    rows, width = own.shape
    fsdp = lax.axis_size("fsdp")
    owners = lax.axis_size("expert")
    me = lax.axis_index("fsdp").astype(jnp.int32).reshape(1)
    owner = lax.axis_index("expert").astype(jnp.int32).reshape(1)
    experts = router_weight.shape[1]
    capacity = 3 * rows * routes.shape[2] // (2 * experts)
    kv_columns = key_weight.shape[1] // fsdp
    q_columns = query_weight.shape[1] // fsdp
    columns = q_columns + 2 * kv_columns
    q_heads = q_columns // HEAD

    ends = jnp.cumsum(lengths[0])
    place = jnp.arange(rows * fsdp, dtype=jnp.int32)
    start = jnp.max(jnp.where(ends[:, None] <= place[None, :], ends[:, None], 0), axis=0)
    position = (place - start).astype(F32)
    frequency = ROPE_BASE ** (-jnp.arange(HEAD // 2, dtype=F32) * 2.0 / HEAD)
    angles = frequency[:, None] * position[None, :]
    cosine, sine = jnp.cos(angles), jnp.sin(angles)
    start = start[None, :].astype(jnp.int32)

    packed, x_sends, dressed, mask = pack_weights(
        me,
        own,
        query_weight,
        key_weight,
        value_weight,
        router_weight.T,
        first_gain[None],
        second_gain[None],
        query_gain[None],
        key_gain[None],
        routes[0].T,
        upstream,
    )
    x_came = along_z(x_sends)
    x_other = [send(own, "fsdp", 1), send(packed[1], "fsdp", 1)]
    deal, turn = slot_tables(mask, capacity)
    ready = (*x_other, deal, cosine, sine, start)
    x_other.append(send(relay(x_came, rows * fsdp, after=ready), "fsdp", 1))
    c_all = lax.all_gather(dressed, "expert", axis=0)
    wo_came = along_z(output_weight)

    h1, pre, keep, give, inverse, gains, heads, turned, mixed = attention_forward(
        me, own, packed[0], x_came, x_other, cosine, sine, start, experts, q_heads
    )
    other = send(give, "fsdp", 1)
    mixed_sends, wo_stack = merge(keep, other, output_weight, wo_came)
    mixed_came = along_z(mixed_sends)
    wo_other = send(wo_stack, "fsdp", 1)
    middle, probs, hidden, sent = middle_layer(
        own, keep, other, mixed_came, output_weight, wo_came, wo_other, gains, deal, experts, owners
    )
    h_rows = exchange(sent)
    rows_c, row_mask, back = deal_rows(owner, c_all, down_weight, experts, capacity)
    rows_back, gate_low, up_low, active, weighted, share = expert_layer(
        owner, h_rows, gains, row_mask, back, gate_weight, up_weight, experts
    )
    came_back = exchange(rows_back)
    grads, tick = expert_weights(h_rows, rows_c, gate_low, up_low, weighted)
    grads = lax.psum(grads, "fsdp")
    gate_sum, up_sum, down_sum = widen(grads)
    sent, tick = expert_outputs(active, share, down_weight, owners, after=(tick,))

    middle_grad, middle_low, extra = router_backward(
        came_back, turn, middle, probs, mask, gains, upstream, hidden, experts, after=(tick,)
    )
    da_came, da_other = gather_fsdp(middle_low, "row_middle")
    out_rows = exchange(sent)
    layer_out, _ = layer_output(out_rows, turn, middle)
    first, dh_keep, dh_give = attention_backward(
        me,
        middle_low,
        da_came,
        da_other,
        heads,
        output_weight,
        cosine,
        sine,
        start,
        h1,
        pre,
        mixed,
        inverse,
        turned,
        extra,
        experts,
        q_heads,
    )
    dh_total, *dh_sends = pair_sum(dh_keep, send(dh_give, "fsdp", 1))
    dh_came = along_z(dh_sends)
    tokens_grad = input_grad(dh_total, dh_came, own, gains, middle_grad, experts)
    first = passed(first, after=(out_rows, grads, dh_total))
    parted, rest = shares_sum(exchange(first), after=tuple(dh_came))
    parted = lax.all_to_all(parted, "fsdp", 0, 0, tiled=True)
    pieces = exchange(whole_pieces(parted, rest, after=(layer_out, tokens_grad)))
    query_sum, key_sum, value_sum, output_sum, one_sum, two_sum, *gain_sums, router_sum = final_grads(
        pieces, query_weight, key_weight, value_weight, first_gain[None], experts
    )
    return (
        layer_out[None],
        tokens_grad[None],
        one_sum[0],
        query_sum,
        key_sum,
        value_sum,
        output_sum,
        gain_sums[0][0],
        gain_sums[1][0],
        two_sum[0],
        router_sum.T,
        gate_sum,
        up_sum,
        down_sum,
    )


def solution(mesh):
    whole = P("expert", "fsdp", None)
    rows = P("fsdp", None)
    vector = P("fsdp")
    owned = P("expert", None, None)
    return jax.shard_map(
        shards,
        mesh=mesh,
        in_specs=(
            whole,
            P("expert", None),
            whole,
            vector,
            rows,
            rows,
            rows,
            rows,
            vector,
            vector,
            vector,
            rows,
            owned,
            owned,
            owned,
            whole,
        ),
        out_specs=(
            whole,
            whole,
            vector,
            rows,
            rows,
            rows,
            rows,
            vector,
            vector,
            vector,
            rows,
            owned,
            owned,
            owned,
        ),
        check_vma=False,
    )
```

```python
import functools

import jax
import jax.numpy as jnp
from jax import lax
from jax.experimental import pallas as pl
from jax.experimental.pallas import tpu as pltpu
from jax.sharding import PartitionSpec as P

EPSILON = 1e-06
ROPE_BASE = 10000.0
HEAD = 64
TILE = 256
F32 = jnp.float32
BF16 = jnp.bfloat16
VMEM = pl.BlockSpec(memory_space=pltpu.VMEM)
SMEM = pl.BlockSpec(memory_space=pltpu.SMEM)
ANY = pl.BlockSpec(memory_space=pl.ANY)
HBM = pl.BlockSpec(memory_space=pltpu.HBM)


def dot(left, right, dims=((1,), (0,))):
    return lax.dot_general(left, right, (dims, ((), ())), preferred_element_type=F32)


def shape(extent, dtype):
    return jax.ShapeDtypeStruct(extent, dtype)


def kernel_call(
    body, name, micros, operands, results, smem=0, hbm=(), out_hbm=(), after=(), scratch=(), held=(), late=(), stored=(), mib=63
):
    held = tuple(held) + tuple(late)
    n, a, r, s = len(operands), len(after), len(results), len(scratch)
    specs = [SMEM if i < smem else HBM if i in held or i in hbm else VMEM for i in range(n)]
    out_specs = [HBM if i in stored or i in out_hbm else VMEM for i in range(r)]
    staged = [pltpu.VMEM(operands[i].shape, operands[i].dtype) for i in held]
    staged += [pltpu.VMEM(*results[i]) for i in stored]
    sems = [pltpu.SemaphoreType.DMA((max(len(held), 1),)), pltpu.SemaphoreType.DMA((max(len(stored), 1),))]

    def wrapped(*refs):
        ins, outs = list(refs[:n]), list(refs[n + a : n + a + r])
        own = refs[n + a + r : n + a + r + s]
        stages, (load_sem, store_sem) = refs[n + a + r + s : -2], refs[-2:]
        loads, stores, begun = {}, {}, []
        for k, i in enumerate(held):
            loads[i] = pltpu.make_async_copy(ins[i], stages[k], load_sem.at[k])
            loads[i].start()
            ins[i] = stages[k]
        for k, i in enumerate(stored):
            stores[i] = pltpu.make_async_copy(stages[len(held) + k], outs[i], store_sem.at[k])
            outs[i] = stages[len(held) + k]
        for i in held:
            if i not in late:
                loads[i].wait()

        def store(*which):
            for i in which:
                stores[i].start()
                begun.append(i)

        extra = {}
        if late:
            extra["wait"] = lambda i: loads[i].wait()
        if stored:
            extra["store"] = store
        body(*ins, *outs, *own, **extra)
        store(*[i for i in stored if i not in begun])
        for i in stored:
            stores[i].wait()

    return pl.pallas_call(
        wrapped,
        out_shape=[shape(*result) for result in results],
        in_specs=specs + [ANY] * a,
        out_specs=out_specs,
        scratch_shapes=list(scratch) + staged + sems,
        compiler_params=pltpu.CompilerParams(vmem_limit_bytes=mib * 1024 * 1024),
        cost_estimate=pl.CostEstimate(flops=0, bytes_accessed=int(micros * 3.6e6), transcendentals=0),
        name=name,
    )(*operands, *after)


def move_call(moves, name, micros, operands, results, after=(), mib=10):
    def body(*refs):
        for source, target in moves(*refs):
            target[...] = source[...]

    return kernel_call(body, name, micros, operands, results, after=after, mib=mib)


def lane_blocks(value):
    return jnp.concatenate([value[:, i : i + 128] for i in range(0, value.shape[1], 128)], axis=0)


def joined_lanes(value, count):
    rows = value.shape[0] // count
    return jnp.concatenate([value[i * rows : (i + 1) * rows] for i in range(count)], axis=1)


def softmax_rows(logits):
    powers = jnp.exp(logits - jnp.max(logits, axis=0, keepdims=True))
    return powers / jnp.sum(powers, axis=0, keepdims=True)


def head_forward(pre, gain, cosine, sine):
    scale = lax.rsqrt(jnp.mean(pre * pre, axis=0, keepdims=True) + EPSILON)
    normed = pre * scale
    scaled = normed * gain
    a, b = scaled[: HEAD // 2], scaled[HEAD // 2 :]
    turned = jnp.concatenate([a * cosine - b * sine, b * cosine + a * sine], axis=0)
    return turned, normed, scale


def head_backward(grad, normed, scale, gain, cosine, sine):
    a, b = grad[: HEAD // 2], grad[HEAD // 2 :]
    unturned = jnp.concatenate([a * cosine + b * sine, b * cosine - a * sine], axis=0)
    gain_grad = jnp.sum(unturned * normed, axis=1, keepdims=True)
    inner = unturned * gain
    pre_grad = scale * (inner - normed * jnp.mean(inner * normed, axis=0, keepdims=True))
    return pre_grad, gain_grad


def slots_kernel(mask_ref, deal_ref, turn_ref, whole_ref, *, capacity, store):
    experts, rows = mask_ref.shape
    mask = mask_ref[...]
    ranks = dot(mask.astype(BF16), earlier(rows))
    slot = lax.broadcasted_iota(jnp.int32, (capacity, rows), 0).astype(F32) + 1.0
    for expert in range(experts):
        one = slice(expert, expert + 1)
        whole_ref[expert * capacity : (expert + 1) * capacity] = jnp.where(
            (ranks[one] == slot) & (mask[one] > 0.5), 1.0, 0.0
        )
    deal_ref[...] = whole_ref[...].astype(BF16)
    store(0)
    for part in range(0, experts * capacity, 128):
        turn_ref[:, part : part + 128] = whole_ref[part : part + 128].T.astype(BF16)


def slot_tables(mask, capacity):
    experts, rows = mask.shape
    slots = experts * capacity
    return kernel_call(
        functools.partial(slots_kernel, capacity=capacity),
        "slot_tables",
        2.0,
        [mask],
        [((slots, rows), BF16), ((rows, slots), BF16)],
        scratch=[pltpu.VMEM((slots, rows), F32)],
        stored=(0, 1),
    )


def earlier(rows):
    return (
        lax.broadcasted_iota(jnp.int32, (rows, rows), 0)
        <= lax.broadcasted_iota(jnp.int32, (rows, rows), 1)
    ).astype(BF16)


def pack_kernel(
    me_ref, x_ref, wq_ref, wk_ref, wv_ref, router_ref, one_ref, two_ref, qg_ref, kg_ref, routes_ref, c_ref, *outs, wait, store
):
    own_ref, sends, dressed_ref, mask_ref, other_ref, parts_ref = outs[0], outs[1:4], *outs[4:]
    experts, rows = router_ref.shape
    wide = wq_ref.shape[1] // 8
    narrow = wk_ref.shape[1] // 8
    count = qg_ref.shape[1]
    heads = jnp.concatenate([qg_ref[...], kg_ref[...]], axis=0).astype(F32)
    heads = jnp.concatenate([heads, jnp.zeros((2, 128 - count), F32)], axis=1)
    heads = jnp.concatenate([heads, jnp.zeros((126, 128), F32)], axis=0).T[:count]
    small = jnp.concatenate(
        [
            router_ref[...].astype(F32),
            one_ref[...].astype(F32),
            two_ref[...].astype(F32),
            jnp.zeros((6, 128), F32),
            heads,
        ],
        axis=0,
    ).astype(BF16)
    for part in range(8):
        parts_ref[part, :wide] = wq_ref[:, part * wide : (part + 1) * wide].astype(F32).T.astype(BF16)
        parts_ref[part, wide + 2 * narrow :] = small
    for pair in range(4):
        span = slice(pair * 128, (pair + 1) * 128)
        for ref, place in ((wk_ref, wide), (wv_ref, wide + narrow)):
            turned = ref[:, span].astype(F32).T.astype(BF16)
            parts_ref[2 * pair, place : place + narrow] = turned[:narrow]
            parts_ref[2 * pair + 1, place : place + narrow] = turned[narrow:]
    me = me_ref[0]
    tall = parts_ref.shape[1]
    blocks = lane_blocks(x_ref[...])
    base = blocks.shape[0]
    own_ref[...] = parts_ref[me]
    other_ref[...] = parts_ref[me ^ 1]
    for flip in range(1, 4):
        sends[flip - 1][:base] = blocks
        sends[flip - 1][base : base + tall] = parts_ref[me ^ (2 * flip)]
        sends[flip - 1][base + tall :] = parts_ref[me ^ (2 * flip + 1)]
    store(1, 2, 3, 6, 0)
    wait(10)
    wait(11)
    width = c_ref.shape[1]
    subs = lax.broadcasted_iota(jnp.int32, (128, rows), 0)
    routed = jnp.zeros((128, rows), F32)
    for route in range(routes_ref.shape[0]):
        routed = routed + jnp.where(routes_ref[route : route + 1] == subs, 1.0, 0.0)
    dressed_ref[:, :width] = c_ref[...]
    dressed_ref[:, width:] = routed.T.astype(BF16)
    mask_ref[...] = routed[:experts]


def pack_weights(me, x, wq, wk, wv, router, one, two, qg, kg, routes, c):
    experts = router.shape[0]
    tall = (wq.shape[1] + wk.shape[1] + wv.shape[1]) // 8 + experts + 16
    rows, width = x.shape
    base = rows * 8
    own, first, second, third, dressed, mask, other = kernel_call(
        pack_kernel,
        "pack_weights",
        2.5,
        [me, x, wq, wk, wv, router, one, two, qg, kg, routes, c],
        [((tall, 128), BF16)]
        + [((base + 2 * tall, 128), BF16)] * 3
        + [((rows, width + 128), BF16), ((experts, rows), F32), ((tall, 128), BF16)],
        smem=1,
        scratch=[pltpu.VMEM((8, tall, 128), BF16)],
        held=range(1, 10),
        late=(10, 11),
        stored=(0, 1, 2, 3, 4, 5, 6),
    )
    return (own, other), [first, second, third], dressed, mask


def relay(came, base, after):
    tall = (came[0].shape[0] - base) // 2

    def moves(*refs):
        pairs = []
        for flip, ref in enumerate(refs[:3]):
            pairs.append((ref.at[:base], refs[3].at[flip, :base]))
            pairs.append((ref.at[base + tall :], refs[3].at[flip, base:]))
        return pairs

    return move_call(moves, "relay", 1.5, came, [((3, base + tall, 128), BF16)], after)[0]


def forward_kernel(me_ref, x_ref, own_ref, *refs, experts, q_heads, store):
    came, other_x, other_w, other_ref = refs[:3], refs[3], refs[4], refs[5]
    cos_ref, sin_ref, start_ref = refs[6:9]
    h1_ref, pre_ref, keep_ref, give_ref, inverse_ref, gains_ref, heads_ref, turned_ref, out_ref = refs[-9:]
    rows, width = x_ref.shape
    q_columns = q_heads * HEAD
    columns = q_columns + 2 * HEAD
    total = rows * 8
    tall = own_ref.shape[0]
    base = 8 * rows
    me = me_ref[0]
    for slot in range(8):
        flip = slot // 2
        if slot % 2:
            piece = other_ref[flip - 1, base:] if flip else other_w[...]
        elif flip:
            piece = came[flip - 1][base : base + tall]
        else:
            piece = own_ref[...]
        span = pl.ds(pl.multiple_of((me ^ slot) * rows, rows), rows)
        turned_ref[:, span] = piece[:columns]
        small = piece[columns:].astype(F32)
        gains_ref[:, span] = small[: experts + 8]
        heads_ref[pl.ds(pl.multiple_of((me ^ slot) * 8, 8), 8)] = small[experts + 8 :]
    gain_one = gains_ref[experts : experts + 1]
    for slot in range(8):
        flip = slot // 2
        if slot % 2:
            x = joined_lanes(other_ref[flip - 1, :base], 8) if flip else other_x[...]
        elif flip:
            x = joined_lanes(came[flip - 1][:base], 8)
        else:
            x = x_ref[...]
        x = x.astype(F32)
        scale = lax.rsqrt(jnp.mean(x * x, axis=1, keepdims=True) + EPSILON)
        h1_ref[slot] = (x * scale * gain_one).astype(BF16)
    store(0, 6, 7)
    for slot in range(8):
        block = dot(turned_ref[...], h1_ref[slot], ((1,), (1,)))
        place = pl.multiple_of((me ^ slot) * rows, rows)
        pre_ref[:, pl.ds(place, rows)] = block
    store(1)
    cosine, sine = cos_ref[...], sin_ref[...]
    gain_query, gain_key = heads_ref[:, :1], heads_ref[:, 1:2]
    key = head_forward(pre_ref[q_columns : q_columns + HEAD], gain_key, cosine, sine)[0]
    key = key.T.astype(BF16)
    value = pre_ref[q_columns + HEAD :].astype(BF16)
    inverse_ref[...] = jnp.zeros(inverse_ref.shape, F32)
    for head in range(q_heads):
        query = head_forward(pre_ref[head * HEAD : (head + 1) * HEAD], gain_query, cosine, sine)[0]
        query = query.astype(BF16) * jnp.array(HEAD ** (-0.5), BF16)
        for tile in range(total // TILE):
            low, high = tile * TILE, (tile + 1) * TILE
            scores = dot(key[:high], query[:, low:high])
            u = lax.broadcasted_iota(jnp.int32, (high, TILE), 0)
            t = lax.broadcasted_iota(jnp.int32, (high, TILE), 1) + low
            allowed = (u >= start_ref[:, low:high]) & (u <= t)
            powers = jnp.where(allowed, jnp.exp(scores), 0.0)
            inverse = 1.0 / jnp.sum(powers, axis=0, keepdims=True)
            probs = (powers * inverse).astype(BF16)
            mixed = dot(value[:, :high], probs).astype(BF16)
            inverse_ref[head : head + 1, low:high] = inverse
            for part in range(TILE // rows):
                out_ref[low // rows + part, head * HEAD : (head + 1) * HEAD] = mixed[
                    :, part * rows : (part + 1) * rows
                ]
    for slot in range(8):
        (give_ref if slot % 2 else keep_ref)[slot // 2] = out_ref[me ^ slot]


def attention_forward(me, x, own, came, other, cosine, sine, start, experts, q_heads, after=()):
    rows, width = x.shape
    total = 8 * rows
    columns = (q_heads + 2) * HEAD
    q_columns = q_heads * HEAD
    return kernel_call(
        functools.partial(forward_kernel, experts=experts, q_heads=q_heads),
        "attention_forward",
        7.0,
        [me, x, own, *came, *other, cosine, sine, start],
        [
            ((8, rows, width), BF16),
            ((columns, total), F32),
            ((4, q_columns, rows), BF16),
            ((4, q_columns, rows), BF16),
            ((8, total), F32),
            ((experts + 8, width), F32),
            ((HEAD, 128), F32),
            ((columns, width), BF16),
            ((8, q_columns, rows), BF16),
        ],
        smem=1,
        after=after,
        held=(1,),
        stored=(0, 1, 4, 6, 7, 8),
    )


def merge(keep, came, wo, wo_came):
    def moves(keep_ref, came_ref, *refs):
        weights, outs, stacked = refs[:4], refs[4:7], refs[7]
        pairs = [(weight, stacked.at[i]) for i, weight in enumerate(weights)]
        for flip in range(1, 4):
            pairs.append((keep_ref.at[flip], outs[flip - 1].at[0]))
            pairs.append((came_ref.at[flip], outs[flip - 1].at[1]))
        return pairs

    extent = ((2,) + keep.shape[1:], BF16)
    results = [extent] * 3 + [((4,) + wo.shape, BF16)]
    *sends, stacked = move_call(moves, "merge", 1.0, [keep, came, wo, *wo_came], results)
    return sends, stacked


def middle_kernel(x_ref, keep_ref, other_ref, *refs, experts, wait, store):
    came, wo_ref, wo_came, wo_other_ref, gains_ref, deal_ref = refs[:3], refs[3], refs[4:7], refs[7], refs[8], refs[9]
    middle_ref, probs_ref, hidden_ref, sent_ref, mixed_ref, whole_ref, out_ref, out_sem = refs[10:]
    rows, width = x_ref.shape
    for slot in range(8):
        flip, core = slot // 2, slot % 2
        if flip:
            piece = came[flip - 1][core]
        else:
            piece = (other_ref if core else keep_ref)[0]
        span = slice(slot * 128, (slot + 1) * 128)
        mixed_ref[:, span] = piece.astype(F32).T.astype(BF16)
    for i in (6, 7, 8, 9, 10):
        wait(i)
    for slot in range(8):
        flip = slot // 2
        span = slice(slot * 128, (slot + 1) * 128)
        if slot % 2:
            whole_ref[span] = wo_other_ref[flip]
        else:
            whole_ref[span] = (wo_came[flip - 1] if flip else wo_ref)[...]
    wait(0)
    middle = x_ref[...].astype(F32) + dot(mixed_ref[...], whole_ref[...])
    middle_ref[...] = middle
    scale = lax.rsqrt(jnp.mean(middle * middle, axis=1, keepdims=True) + EPSILON)
    hidden = (middle * scale * gains_ref[experts + 1 : experts + 2]).astype(BF16)
    hidden_ref[...] = hidden
    probs_ref[...] = softmax_rows(dot(gains_ref[:experts].astype(BF16), hidden, ((1,), (1,))))
    store(0, 2)
    owners, per_owner, capacity, _ = sent_ref.shape
    group = owners // 4
    size = group * per_owner * capacity
    copies = []
    wait(12)
    for part in range(4):
        taken = dot(deal_ref[part * size : (part + 1) * size], hidden).astype(BF16)
        blocks = slice(group * part, group * (part + 1))
        out_ref[blocks] = taken.reshape(group, per_owner, capacity, width)
        copies.append(pltpu.make_async_copy(out_ref.at[blocks], sent_ref.at[blocks], out_sem.at[part]))
        copies[-1].start()
    for copy in copies:
        copy.wait()


def middle_layer(x, keep, other, came, wo, wo_came, wo_other, gains, deal, experts, owners):
    rows, width = x.shape
    per_owner = experts // owners
    capacity = deal.shape[0] // experts
    sent = ((owners, per_owner, capacity, width), BF16)
    return kernel_call(
        functools.partial(middle_kernel, experts=experts),
        "middle_layer",
        3.0,
        [x, keep, other, *came, wo, *wo_came, wo_other, gains, deal],
        [((rows, width), F32), ((experts, rows), F32), ((rows, width), BF16), sent],
        out_hbm=(3,),
        scratch=[
            pltpu.VMEM((rows, width), BF16),
            pltpu.VMEM((width, width), BF16),
            pltpu.VMEM(*sent),
            pltpu.SemaphoreType.DMA((4,)),
        ],
        late=(6, 7, 8, 9, 10, 0, 12),
        stored=(0, 2),
    )


def row(pieces, name):
    def moves(*refs):
        return [(ref, refs[-1].at[i]) for i, ref in enumerate(refs[:-1])]

    return move_call(moves, name, 1.0, pieces, [((len(pieces),) + pieces[0].shape, BF16)])[0]


def backward_kernel(me_ref, own_da_ref, *refs, experts, q_heads, wait):
    came, other_ref = refs[:3], refs[3]
    heads_ref, wo_ref, cos_ref, sin_ref, start_ref = refs[4:9]
    h1_ref, pre_ref, mixed_ref, inverse_ref, turned_ref, extra_ref = refs[9:15]
    first_ref, keep_ref, send_ref = refs[-10:-7]
    da_ref, mixed_grad_ref, dkey_ref, dvalue_ref, low_ref, out_slots_ref, grad_ref = refs[-7:]
    rows, width = own_da_ref.shape
    q_columns = q_heads * HEAD
    columns = q_columns + 2 * HEAD
    total = rows * 8
    me = me_ref[0]
    for slot in range(8):
        flip, core = slot // 2, slot % 2
        if core:
            piece = other_ref[flip]
        else:
            piece = (came[flip - 1] if flip else own_da_ref)[...]
        span = slice(slot * rows, (slot + 1) * rows)
        da_ref[span] = piece
        place = pl.multiple_of((me ^ slot) * rows, rows)
        mixed_grad_ref[:, pl.ds(place, rows)] = dot(wo_ref[...], piece, ((1,), (1,))).astype(BF16)
    wait(13)
    for slot in range(8):
        out_slots_ref[:, slot * rows : (slot + 1) * rows] = mixed_ref[me ^ slot]
    wo_grad = dot(out_slots_ref[...], da_ref[...]).astype(BF16)
    wo_grad = lane_blocks(wo_grad)
    wait(12)
    wait(14)
    gain_query, gain_key = heads_ref[:, :1], heads_ref[:, 1:2]
    cosine, sine = cos_ref[...], sin_ref[...]
    key_turned, key_normed, key_scale = head_forward(
        pre_ref[q_columns : q_columns + HEAD], gain_key, cosine, sine
    )
    key_low = key_turned.astype(BF16)
    key = key_turned.T.astype(BF16)
    value = pre_ref[q_columns + HEAD :].T.astype(BF16)
    dkey_ref[...] = jnp.zeros(dkey_ref.shape, F32)
    dvalue_ref[...] = jnp.zeros(dvalue_ref.shape, F32)
    gain_query_grad = jnp.zeros((HEAD, 1), F32)
    pieces = []
    for head in range(q_heads):
        span = slice(head * HEAD, (head + 1) * HEAD)
        turned, normed, scale = head_forward(pre_ref[span], gain_query, cosine, sine)
        query = turned.astype(BF16) * jnp.array(HEAD ** (-0.5), BF16)
        grads = []
        for tile in range(total // TILE):
            low, high = tile * TILE, (tile + 1) * TILE
            part = query[:, low:high]
            mixed_grad = mixed_grad_ref[span, low:high]
            scores = dot(key[:high], part)
            u = lax.broadcasted_iota(jnp.int32, (high, TILE), 0)
            t = lax.broadcasted_iota(jnp.int32, (high, TILE), 1) + low
            allowed = (u >= start_ref[:, low:high]) & (u <= t)
            probs = jnp.where(allowed, jnp.exp(scores) * inverse_ref[head : head + 1, low:high], 0.0)
            attend = dot(value[:high], mixed_grad)
            delta = jnp.sum(probs * attend, axis=0, keepdims=True)
            score_low = (probs * (attend - delta)).astype(BF16)
            grads.append(dot(key_low[:, :high], score_low))
            dkey_ref[:, :high] += dot(part, score_low, ((1,), (1,)))
            dvalue_ref[:, :high] += dot(mixed_grad, probs.astype(BF16), ((1,), (1,)))
        query_grad = jnp.concatenate(grads, axis=1) * HEAD ** (-0.5)
        pre_grad, gain_grad = head_backward(query_grad, normed, scale, gain_query, cosine, sine)
        gain_query_grad += gain_grad
        pieces.append(pre_grad)
    pre_grad, gain_key_grad = head_backward(
        dkey_ref[...], key_normed, key_scale, gain_key, cosine, sine
    )
    pieces += [pre_grad, dvalue_ref[...]]
    pre_grad = jnp.concatenate(pieces, axis=0)
    low_ref[...] = pre_grad.astype(BF16)
    slots_grad = []
    for slot in range(8):
        place = pl.multiple_of((me ^ slot) * rows, rows)
        slots_grad.append(low_ref[:, pl.ds(place, rows)])
    slots_grad = jnp.concatenate(slots_grad, axis=1)
    wait(11)
    wait(15)
    grad_ref[:columns] = dot(slots_grad, h1_ref[...].reshape(total, width))
    extra = extra_ref[...]
    lane = lax.broadcasted_iota(jnp.int32, (HEAD, 128), 1)
    gains = jnp.where(lane == 0, gain_query_grad, jnp.where(lane == 1, gain_key_grad, 0.0))
    gains = gains.T[:2]
    step = HEAD // 8
    grad_ref[columns:] = jnp.zeros((64, width), F32)
    grad_ref[columns : columns + experts + 1] = extra[: experts + 1]
    for part in range(8):
        grad_ref[columns + experts + 1 : columns + experts + 3, part * rows : part * rows + step] = gains[
            :, part * step : (part + 1) * step
        ]
    for piece in range(16):
        spare = []
        place = columns + piece * SPARE
        for part in range(8):
            span = slice(part * rows, (part + 1) * rows)
            block = grad_ref[piece * PIECE : (piece + 1) * PIECE, span]
            first_ref[piece, part * PIECE : (part + 1) * PIECE] = block.astype(BF16)
            spare.append(grad_ref[place : place + SPARE, span])
        spare.append(jnp.zeros((2 * PIECE - 8 * SPARE, 128), F32))
        first_ref[piece, 8 * PIECE : 10 * PIECE] = jnp.concatenate(spare, axis=0).astype(BF16)
        first_ref[piece, 10 * PIECE :] = wo_grad[piece * SLICE : (piece + 1) * SLICE]
    turned = turned_ref[...]
    for slot in range(8):
        low_rows_slot = slots_grad[:, slot * rows : (slot + 1) * rows].astype(F32).T.astype(BF16)
        part = dot(low_rows_slot, turned)
        if slot % 2:
            send_ref[slot // 2] = part.astype(BF16)
        else:
            keep_ref[slot // 2] = part


def attention_backward(
    me, da, came, other, heads, wo, cosine, sine, start, h1, pre, mixed, inverse, turned, extra, experts, q_heads, after=()
):
    rows, width = da.shape
    total = 8 * rows
    columns = pre.shape[0]
    q_columns = q_heads * HEAD
    return kernel_call(
        functools.partial(backward_kernel, experts=experts, q_heads=q_heads),
        "attention_backward",
        12,
        [me, da, *came, other, heads, wo, cosine, sine, start, h1, pre, mixed, inverse, turned, extra],
        [
            ((16, 10 * PIECE + SLICE, 128), BF16),
            ((4, rows, width), F32),
            ((4, rows, width), BF16),
        ],
        smem=1,
        after=after,
        held=(6, 7),
        late=(11, 12, 13, 14, 15),
        scratch=[
            pltpu.VMEM((total, width), BF16),
            pltpu.VMEM((q_columns, total), BF16),
            pltpu.VMEM((HEAD, total), F32),
            pltpu.VMEM((HEAD, total), F32),
            pltpu.VMEM((columns, total), BF16),
            pltpu.VMEM((q_columns, total), BF16),
            pltpu.VMEM((columns + 64, width), F32),
        ],
    )


def deal_kernel(owner_ref, c_ref, down_ref, rows_c, mask_ref, back_ref, c_scratch, sems, *, experts, capacity, wait, store):
    owner = owner_ref[0]
    per_owner, hidden, width = down_ref.shape
    rows = c_ref.shape[1]
    loads = [pltpu.make_async_copy(c_ref.at[i], c_scratch.at[i], sems.at[i]) for i in range(16)]
    for load in loads:
        load.start()
    lanes = lax.broadcasted_iota(jnp.int32, (experts, 128), 1)
    subs = lax.broadcasted_iota(jnp.int32, (experts, 128), 0)
    eye = (lanes == subs).astype(BF16)
    before = earlier(rows)
    mine_of = lax.broadcasted_iota(jnp.int32, (experts, rows), 0) - owner * per_owner
    slot = lax.broadcasted_iota(jnp.int32, (capacity, rows), 0).astype(F32) + 1.0
    for block in range(16):
        loads[block].wait()
        c = c_scratch[block]
        mask = dot(eye, c[:, width:], ((1,), (1,)))
        ranks = dot(mask.astype(BF16), before)
        deals = []
        for k in range(per_owner):
            mine = mine_of == k
            hit = jnp.sum(jnp.where(mine, mask, 0.0), axis=0, keepdims=True)
            rank = jnp.sum(jnp.where(mine, ranks, 0.0), axis=0, keepdims=True)
            deals.append(jnp.where((rank == slot) & (hit > 0.5), 1.0, 0.0))
        taken = dot(jnp.concatenate(deals, axis=0).astype(BF16), c).astype(BF16)
        span = slice(block * capacity, (block + 1) * capacity)
        for k in range(per_owner):
            spot = slice(k * capacity, (k + 1) * capacity)
            rows_c[k, span] = taken[spot, :width]
            mask_ref[k, span] = taken[spot, width:]
    store(0, 1)
    wait(2)
    for k in range(per_owner):
        for tile in range(16 * capacity // TILE):
            span = slice(tile * TILE, (tile + 1) * TILE)
            back_ref[k, span] = dot(rows_c[k, span], down_ref[k], ((1,), (1,)))


def deal_rows(owner, c, down, experts, capacity):
    per_owner, hidden, width = down.shape
    count = 16 * capacity
    return kernel_call(
        functools.partial(deal_kernel, experts=experts, capacity=capacity),
        "deal_rows",
        12.0,
        [owner, c, down],
        [
            ((per_owner, count, width), BF16),
            ((per_owner, count, 128), BF16),
            ((per_owner, count, hidden), F32),
        ],
        smem=1,
        hbm=(1,),
        scratch=[pltpu.VMEM(c.shape, BF16), pltpu.SemaphoreType.DMA((16,))],
        late=(2,),
        stored=(0, 1, 2),
    )


def expert_kernel(
    owner_ref,
    h_hbm,
    gains_ref,
    mask_ref,
    back_hbm,
    gate_hbm,
    up_hbm,
    rows_hbm,
    gate_out,
    up_out,
    active_out,
    weighted_out,
    share_ref,
    h_ref,
    back_in,
    gate_ref,
    up_ref,
    rows_back,
    load_sem,
    store_sem,
    *,
    experts,
    store,
):
    owners, per_owner, capacity, width = h_hbm.shape
    group = 8
    parts = owners // group
    size = group * capacity
    loads = {}
    for k in range(per_owner):
        for part in range(parts):
            blocks = slice(part * group, (part + 1) * group)
            spot = (k * parts + part) * 4
            loads[k, part] = [
                pltpu.make_async_copy(h_hbm.at[blocks, k], h_ref.at[blocks, k], load_sem.at[spot]),
                pltpu.make_async_copy(
                    back_hbm.at[k, part * size : (part + 1) * size],
                    back_in.at[k, part * size : (part + 1) * size],
                    load_sem.at[spot + 1],
                ),
            ]
            if part == 0:
                loads[k, part] += [
                    pltpu.make_async_copy(gate_hbm.at[k], gate_ref.at[k], load_sem.at[spot + 2]),
                    pltpu.make_async_copy(up_hbm.at[k], up_ref.at[k], load_sem.at[spot + 3]),
                ]
            for load in loads[k, part]:
                load.start()
    owner = owner_ref[0]
    router = jnp.concatenate([gains_ref[:experts], jnp.zeros((128 - experts, width), F32)], axis=0)
    router = router.astype(BF16)
    lane = lax.broadcasted_iota(jnp.int32, (size, 128), 1)
    copies = []
    for k in range(per_owner):
        place = owner * per_owner + k
        for part in range(parts):
            blocks = slice(part * group, (part + 1) * group)
            span = slice(part * size, (part + 1) * size)
            for load in loads[k, part]:
                load.wait()
            h = h_ref[blocks, k].reshape(size, width)
            gate = dot(h, gate_ref[k])
            up = dot(h, up_ref[k])
            logits = dot(h, router, ((1,), (1,)))
            chosen = mask_ref[k, span] > 0.5
            top = jnp.max(jnp.where(chosen, logits, -1e30), axis=1, keepdims=True)
            powers = jnp.where(chosen, jnp.exp(logits - top), 0.0)
            total = jnp.sum(powers, axis=1, keepdims=True)
            share = jnp.sum(jnp.where(lane == place, powers, 0.0), axis=1, keepdims=True)
            share = share / jnp.where(total > 0.0, total, 1.0)
            share_ref[k, span] = jnp.broadcast_to(share, (size, 128))
            back = back_in[k, span]
            sig = 1.0 / (1.0 + jnp.exp(-gate))
            silu = gate * sig
            active = silu * up
            active_low = active.astype(BF16)
            route_grad = jnp.sum(active_low.astype(F32) * back, axis=1, keepdims=True)
            grad = back * share
            gate_low = (grad * up * (sig + silu * (1.0 - sig))).astype(BF16)
            up_low = (grad * silu).astype(BF16)
            active_out[k, span] = active_low
            weighted_out[k, span] = (active * share).astype(BF16)
            gate_out[k, span] = gate_low
            up_out[k, span] = up_low
            rows = dot(gate_low, gate_ref[k], ((1,), (1,))) + dot(up_low, up_ref[k], ((1,), (1,)))
            high = route_grad.astype(BF16).astype(F32)
            spread_out = jnp.where(lane == place, high, 0.0)
            spread_out = jnp.where(lane == place + experts, route_grad - high, spread_out)
            whole = jnp.concatenate([rows.astype(BF16), spread_out.astype(BF16)], axis=1)
            rows_back[blocks, k] = whole.reshape(group, capacity, width + 128)
            copies.append(
                pltpu.make_async_copy(
                    rows_back.at[blocks, k], rows_hbm.at[blocks, k], store_sem.at[k * parts + part]
                )
            )
            copies[-1].start()
    store(1, 2, 3, 4, 5)
    for copy in copies:
        copy.wait()


def expert_layer(owner, h, gains, mask, back, gate, up, experts):
    per_owner, width, hidden = gate.shape
    owners, _, capacity, _ = h.shape
    count = owners * capacity
    narrow = ((per_owner, count, hidden), BF16)
    rows_back = ((owners, per_owner, capacity, width + 128), BF16)
    pieces = per_owner * (owners // 8)
    return kernel_call(
        functools.partial(expert_kernel, experts=experts),
        "expert_layer",
        14.0,
        [owner, h, gains, mask, back, gate, up],
        [rows_back] + [narrow] * 4 + [((per_owner, count, 128), F32)],
        smem=1,
        hbm=(1, 4, 5, 6),
        out_hbm=(0,),
        scratch=[pltpu.VMEM(value.shape, value.dtype) for value in (h, back, gate, up)]
        + [pltpu.VMEM(*rows_back), pltpu.SemaphoreType.DMA((4 * pieces,)), pltpu.SemaphoreType.DMA((pieces,))],
        stored=(1, 2, 3, 4, 5),
    )


def weights_kernel(
    h_hbm, rows_c, gate_low, up_low, weighted, out_hbm, tick_ref, h_ref, out_ref, load_sem, store_sem, *, wait
):
    tick_ref[...] = jnp.zeros(tick_ref.shape, F32)
    first = ((0,), (0,))
    owners, per_owner, capacity, width = h_hbm.shape
    hidden = gate_low.shape[2]
    half = width // 2
    loads = [
        pltpu.make_async_copy(h_hbm.at[:, k], h_ref.at[:, k], load_sem.at[k]) for k in range(per_owner)
    ]
    for load in loads:
        load.start()
    stores = []

    def keep(place):
        stores.append(pltpu.make_async_copy(out_ref.at[place], out_hbm.at[place], store_sem.at[place]))
        stores[-1].start()

    wait(2)
    for k in range(per_owner):
        loads[k].wait()
        rows_h = h_ref[:, k].reshape(owners * capacity, width)
        for place, low in ((k, gate_low), (per_owner + k, up_low)):
            if k == 0 and place:
                wait(3)
            total = dot(rows_h, low[k], first).astype(BF16)
            out_ref[place, :, :hidden] = total[:half]
            out_ref[place, :, hidden:] = total[half:]
            keep(place)
        if k == 0:
            wait(4)
            wait(1)
        place = 2 * per_owner + k
        out_ref[place] = dot(weighted[k], rows_c[k], first).astype(BF16)
        keep(place)
    for store in stores:
        store.wait()


def expert_weights(h, rows_c, gate_low, up_low, weighted):
    per_owner, count, width = rows_c.shape
    hidden = gate_low.shape[2]
    out = ((3 * per_owner, hidden, width), BF16)
    return kernel_call(
        weights_kernel,
        "expert_weights",
        0.1,
        [h, rows_c, gate_low, up_low, weighted],
        [out, ((8, 128), F32)],
        hbm=(0,),
        out_hbm=(0,),
        scratch=[
            pltpu.VMEM(h.shape, BF16),
            pltpu.VMEM(*out),
            pltpu.SemaphoreType.DMA((per_owner,)),
            pltpu.SemaphoreType.DMA((3 * per_owner,)),
        ],
        late=(2, 3, 4, 1),
    )


def widen_kernel(low_ref, gate_ref, up_ref, down_ref):
    step = pl.program_id(0)
    hidden = gate_ref.shape[2]
    value = low_ref[0].astype(F32)
    half = value.shape[0]
    for place, ref in ((0, gate_ref), (1, up_ref)):

        @pl.when(step // 2 == place)
        def _():
            ref[0, :half] = value[:, :hidden]
            ref[0, half:] = value[:, hidden:]

    @pl.when(step // 2 == 2)
    def _():
        down_ref[0] = value


def widen(low):
    count, hidden, width = low.shape
    per_owner = count // 3

    def spot(place):
        return lambda i: (jnp.clip(i - place * per_owner, 0, per_owner - 1), 0, 0)

    return pl.pallas_call(
        widen_kernel,
        grid=(count,),
        out_shape=[shape((per_owner, width, hidden), F32)] * 2 + [shape((per_owner, hidden, width), F32)],
        in_specs=[pl.BlockSpec((1, hidden, width), lambda i: (i, 0, 0))],
        out_specs=[
            pl.BlockSpec((1, width, hidden), spot(0)),
            pl.BlockSpec((1, width, hidden), spot(1)),
            pl.BlockSpec((1, hidden, width), spot(2)),
        ],
        compiler_params=pltpu.CompilerParams(vmem_limit_bytes=63 * 1024 * 1024),
        cost_estimate=pl.CostEstimate(flops=0, bytes_accessed=24_000_000, transcendentals=0),
        name="widen",
    )(low)


def outputs_kernel(active, share, down_ref, sent_ref, tick_ref, out_ref, out_sem, *, wait):
    tick_ref[...] = jnp.zeros(tick_ref.shape, F32)
    per_owner, count, hidden = active.shape
    owners, _, capacity, width = sent_ref.shape
    group = 8
    size = group * capacity
    copies = []
    for i in range(3):
        wait(i)
    for k in range(per_owner):
        for part in range(owners // group):
            span = slice(part * size, (part + 1) * size)
            blocks = slice(part * group, (part + 1) * group)
            produced = dot(active[k, span], down_ref[k]).astype(BF16).astype(F32)
            produced = (produced * share[k, span, :1]).astype(BF16)
            out_ref[blocks, k] = produced.reshape(group, capacity, width)
            copies.append(
                pltpu.make_async_copy(
                    out_ref.at[blocks, k], sent_ref.at[blocks, k], out_sem.at[k * (owners // group) + part]
                )
            )
            copies[-1].start()
    for copy in copies:
        copy.wait()


def expert_outputs(active, share, down, owners, after=()):
    per_owner, count, hidden = active.shape
    width = down.shape[2]
    sent = ((owners, per_owner, count // owners, width), BF16)
    return kernel_call(
        outputs_kernel,
        "expert_outputs",
        0.1,
        [active, share, down],
        [sent, ((8, 128), F32)],
        out_hbm=(0,),
        after=after,
        scratch=[pltpu.VMEM(*sent), pltpu.SemaphoreType.DMA((per_owner * (owners // 8),))],
        late=(0, 1, 2),
    )


def combined(rows_hbm, rows_ref, sems, turn_ref, ready):
    owners, per_owner, capacity, wide = rows_hbm.shape
    group = owners // 4
    size = group * per_owner * capacity
    loads = []
    for part in range(4):
        blocks = slice(part * group, (part + 1) * group)
        loads.append(pltpu.make_async_copy(rows_hbm.at[blocks], rows_ref.at[blocks], sems.at[part]))
        loads[-1].start()
    ready()
    total = None
    for part in range(4):
        loads[part].wait()
        rows = rows_ref[part * group : (part + 1) * group].reshape(size, wide)
        one = dot(turn_ref[:, part * size : (part + 1) * size], rows)
        total = one if total is None else total + one
    return total


def output_kernel(rows_hbm, turn_ref, middle_ref, out_ref, tick_ref, rows_ref, sems, *, wait, store):
    tick_ref[...] = jnp.zeros(tick_ref.shape, F32)
    total = combined(rows_hbm, rows_ref, sems, turn_ref, lambda: wait(1))
    wait(2)
    out_ref[...] = (middle_ref[...] + total).astype(BF16)


def layer_output(rows, turn, middle):
    return kernel_call(
        output_kernel,
        "layer_output",
        3,
        [rows, turn, middle],
        [(middle.shape, BF16), ((8, 128), F32)],
        hbm=(0,),
        scratch=[pltpu.VMEM(rows.shape, BF16), pltpu.SemaphoreType.DMA((4,))],
        late=(1, 2),
        stored=(0,),
    )


def router_kernel(
    rows_hbm,
    turn_ref,
    middle_ref,
    probs_ref,
    mask_ref,
    gains_ref,
    c_ref,
    hidden_ref,
    grad_ref,
    send_ref,
    extra_ref,
    rows_ref,
    sems,
    *,
    experts,
    wait,
    store,
):
    rows, width = middle_ref.shape
    returned = combined(rows_hbm, rows_ref, sems, turn_ref, lambda: wait(1))
    for i in (2, 4, 6, 7):
        wait(i)
    tail = returned[:, width:].T
    route_grad = tail[:experts] + tail[experts : 2 * experts]
    mask = mask_ref[...]
    probs = probs_ref[...]
    picked = probs * mask
    picked_sum = jnp.sum(picked, axis=0, keepdims=True)
    share = picked / picked_sum
    picked_grad = (route_grad - jnp.sum(route_grad * share, axis=0, keepdims=True)) / picked_sum
    prob_grad = mask * picked_grad
    logit_grad = probs * (prob_grad - jnp.sum(probs * prob_grad, axis=0, keepdims=True))
    extra_ref[:experts] = dot(logit_grad.astype(BF16), hidden_ref[...])
    logit_rows = jnp.concatenate([logit_grad, jnp.zeros((128 - experts, rows), F32)], axis=0).T
    router = gains_ref[:experts].astype(BF16)
    hidden_grad = returned[:, :width] + dot(logit_rows[:, :experts].astype(BF16), router)
    middle = middle_ref[...]
    scale = lax.rsqrt(jnp.mean(middle * middle, axis=1, keepdims=True) + EPSILON)
    normed = middle * scale
    extra_ref[experts : experts + 8] = jnp.broadcast_to(
        jnp.sum(hidden_grad * normed, axis=0, keepdims=True), (8, width)
    )
    inner = hidden_grad * gains_ref[experts + 1 : experts + 2]
    grad = c_ref[...].astype(F32) + scale * (
        inner - normed * jnp.mean(inner * normed, axis=1, keepdims=True)
    )
    grad_ref[...] = grad
    send_ref[...] = grad.astype(BF16)


def router_backward(rows_back, turn, middle, probs, mask, gains, c, hidden, experts, after=()):
    rows, width = middle.shape
    return kernel_call(
        functools.partial(router_kernel, experts=experts),
        "router_backward",
        5,
        [rows_back, turn, middle, probs, mask, gains, c, hidden],
        [((rows, width), F32), ((rows, width), BF16), ((experts + 8, width), F32)],
        hbm=(0,),
        after=after,
        scratch=[pltpu.VMEM(rows_back.shape, BF16), pltpu.SemaphoreType.DMA((4,))],
        late=(1, 2, 4, 6, 7),
        stored=(0,),
    )


def pair_kernel(keep_ref, other_ref, total_ref, *sends):
    for flip in range(4):
        total = keep_ref[flip] + other_ref[flip].astype(F32)
        if flip:
            sends[flip - 1][...] = total.astype(BF16)
        else:
            total_ref[...] = total


def pair_sum(keep, other):
    rows, width = keep.shape[1:]
    return kernel_call(
        pair_kernel, "pair_sum", 1.2, [keep, other], [((rows, width), F32)] + [((rows, width), BF16)] * 3
    )


def input_kernel(total_ref, *refs, experts, store):
    came = refs[:3]
    x_ref, gains_ref, middle_grad_ref, out_ref, tick_ref = refs[3:]
    tick_ref[...] = jnp.zeros(tick_ref.shape, F32)
    total = total_ref[...]
    for piece in came:
        total = total + piece[...].astype(F32)
    x = x_ref[...].astype(F32)
    scale = lax.rsqrt(jnp.mean(x * x, axis=1, keepdims=True) + EPSILON)
    normed = x * scale
    inner = total * gains_ref[experts : experts + 1]
    out_ref[...] = middle_grad_ref[...] + scale * (
        inner - normed * jnp.mean(inner * normed, axis=1, keepdims=True)
    )


def input_grad(total, came, x, gains, middle_grad, experts):
    return kernel_call(
        functools.partial(input_kernel, experts=experts),
        "input_grad",
        2,
        [total, *came, x, gains, middle_grad],
        [(middle_grad.shape, F32), ((8, 128), F32)],
        held=(4, 6),
        stored=(0,),
    )


PIECE, SPARE, SLICE = 16, 3, 64


def passed(value, after):
    results = [(value.shape, value.dtype)]
    return move_call(lambda *refs: [refs], "passed", 0.5, [value], results, after, 63)[0]


def shares_kernel(pieces_ref, out_ref, rest_ref):
    total = pieces_ref[0].astype(F32)
    for i in range(1, pieces_ref.shape[0]):
        total = total + pieces_ref[i].astype(F32)
    base = 8 * PIECE
    fill = jnp.zeros((PIECE - SPARE, 128), F32)
    for part in range(8):
        out_ref[part, :PIECE] = total[part * PIECE : (part + 1) * PIECE].astype(BF16)
        spare = total[base + part * SPARE : base + (part + 1) * SPARE]
        out_ref[part, PIECE:] = jnp.concatenate([spare, fill], axis=0).astype(BF16)
    rest_ref[...] = total[base + 2 * PIECE :].astype(BF16)


def shares_sum(pieces, after=()):
    return kernel_call(
        shares_kernel,
        "shares_sum",
        0.1,
        [pieces],
        [((8, 2 * PIECE, 128), BF16), ((SLICE, 128), BF16)],
        after=after,
        mib=12,
    )


def whole_kernel(came_ref, rest_ref, out_ref):
    spare = came_ref[0, PIECE:].astype(F32)
    for i in range(1, 8):
        spare = spare + came_ref[i, PIECE:].astype(F32)
    rows = [came_ref[i, :PIECE] for i in range(8)] + [spare.astype(BF16), rest_ref[...]]
    rows = jnp.concatenate(rows, axis=0)
    for i in range(16):
        out_ref[i] = rows


def whole_pieces(came, rest, after=()):
    return kernel_call(
        whole_kernel,
        "whole_pieces",
        0.1,
        [came, rest],
        [((16, 9 * PIECE + SLICE, 128), BF16)],
        after=after,
        mib=12,
    )[0]


def final_kernel(pieces_ref, wq_ref, wk_ref, wv_ref, gain_ref, *outs, experts):
    query_ref, key_ref, value_ref, output_ref, one_ref, two_ref, qg_ref, kg_ref, router_ref = outs
    rows = pieces_ref.shape[2]
    q_columns = query_ref.shape[1] // 8
    kv_columns = key_ref.shape[1] // 8
    sums = jnp.zeros((rows, 1), F32)
    base = 8 * PIECE
    for pair in range(4):
        keys, values = [], []
        for source in (2 * pair, 2 * pair + 1):
            block = [pieces_ref[i, source * PIECE : (source + 1) * PIECE] for i in range(16)]
            turned = jnp.concatenate(block, axis=0).astype(F32).T
            span = slice(source * q_columns, (source + 1) * q_columns)
            query = turned[:, :q_columns]
            query_ref[:, span] = query
            sums = sums + jnp.sum(query * wq_ref[:, span].astype(F32), axis=1, keepdims=True)
            keys.append(turned[:, q_columns : q_columns + kv_columns])
            values.append(turned[:, q_columns + kv_columns :])
        span = slice(2 * pair * kv_columns, 2 * (pair + 1) * kv_columns)
        for parts, ref, weight in ((keys, key_ref, wk_ref), (values, value_ref, wv_ref)):
            both = jnp.concatenate(parts, axis=1)
            ref[:, span] = both
            sums = sums + jnp.sum(both * weight[:, span].astype(F32), axis=1, keepdims=True)
    for i in range(16):
        half = i % 2 * SLICE
        output_ref[half : half + SLICE, i // 2 * rows : (i // 2 + 1) * rows] = pieces_ref[
            i, base + PIECE :
        ].astype(F32)
    spare = pieces_ref[:, base : base + PIECE].astype(F32)
    spare = jnp.concatenate([spare[i, :SPARE] for i in range(16)], axis=0)
    one_ref[...] = jnp.broadcast_to(sums, (rows, 128)).T[:1] / gain_ref[...].astype(F32)
    two_ref[...] = spare[experts : experts + 1]
    step = qg_ref.shape[1]
    qg_ref[...] = spare[experts + 1 : experts + 2, :step]
    kg_ref[...] = spare[experts + 2 : experts + 3, :step]
    router_ref[...] = spare[:experts]


def final_grads(pieces, wq, wk, wv, gain, experts):
    rows = pieces.shape[2]
    return kernel_call(
        functools.partial(final_kernel, experts=experts),
        "final_grads",
        0.2,
        [pieces, wq, wk, wv, gain],
        [
            (wq.shape, F32),
            (wk.shape, F32),
            (wv.shape, F32),
            ((rows, 8 * rows), F32),
            ((1, rows), F32),
            ((1, rows), F32),
            ((1, HEAD // 8), F32),
            ((1, HEAD // 8), F32),
            ((experts, rows), F32),
        ],
        held=(1, 2, 3, 4),
    )


def send(values, axis, flip):
    count = lax.axis_size(axis)
    return lax.ppermute(values, axis, [(i, i ^ flip) for i in range(count)])


def along_z(values):
    if not isinstance(values, (list, tuple)):
        values = [values] * 3
    return [send(value, "fsdp", 2 * (i + 1)) for i, value in enumerate(values)]


def gather_fsdp(block, name):
    came = along_z(block)
    return came, send(row([block, *came], name), "fsdp", 1)


def exchange(rows):
    return lax.all_to_all(rows, "expert", 0, 0, tiled=True)


def shards(
    tokens,
    lengths,
    routes,
    first_gain,
    query_weight,
    key_weight,
    value_weight,
    output_weight,
    query_gain,
    key_gain,
    second_gain,
    router_weight,
    gate_weight,
    up_weight,
    down_weight,
    cotangent,
):
    own = tokens[0]
    upstream = cotangent[0]
    rows, width = own.shape
    fsdp = lax.axis_size("fsdp")
    owners = lax.axis_size("expert")
    me = lax.axis_index("fsdp").astype(jnp.int32).reshape(1)
    owner = lax.axis_index("expert").astype(jnp.int32).reshape(1)
    experts = router_weight.shape[1]
    capacity = 3 * rows * routes.shape[2] // (2 * experts)
    kv_columns = key_weight.shape[1] // fsdp
    q_columns = query_weight.shape[1] // fsdp
    columns = q_columns + 2 * kv_columns
    q_heads = q_columns // HEAD

    ends = jnp.cumsum(lengths[0])
    place = jnp.arange(rows * fsdp, dtype=jnp.int32)
    start = jnp.max(jnp.where(ends[:, None] <= place[None, :], ends[:, None], 0), axis=0)
    position = (place - start).astype(F32)
    frequency = ROPE_BASE ** (-jnp.arange(HEAD // 2, dtype=F32) * 2.0 / HEAD)
    angles = frequency[:, None] * position[None, :]
    cosine, sine = jnp.cos(angles), jnp.sin(angles)
    start = start[None, :].astype(jnp.int32)

    packed, x_sends, dressed, mask = pack_weights(
        me,
        own,
        query_weight,
        key_weight,
        value_weight,
        router_weight.T,
        first_gain[None],
        second_gain[None],
        query_gain[None],
        key_gain[None],
        routes[0].T,
        upstream,
    )
    x_came = along_z(x_sends)
    x_other = [send(own, "fsdp", 1), send(packed[1], "fsdp", 1)]
    deal, turn = slot_tables(mask, capacity)
    ready = (*x_other, deal, cosine, sine, start)
    x_other.append(send(relay(x_came, rows * fsdp, after=ready), "fsdp", 1))
    c_all = lax.all_gather(dressed, "expert", axis=0)
    wo_came = along_z(output_weight)

    h1, pre, keep, give, inverse, gains, heads, turned, mixed = attention_forward(
        me, own, packed[0], x_came, x_other, cosine, sine, start, experts, q_heads
    )
    other = send(give, "fsdp", 1)
    mixed_sends, wo_stack = merge(keep, other, output_weight, wo_came)
    mixed_came = along_z(mixed_sends)
    wo_other = send(wo_stack, "fsdp", 1)
    middle, probs, hidden, sent = middle_layer(
        own, keep, other, mixed_came, output_weight, wo_came, wo_other, gains, deal, experts, owners
    )
    h_rows = exchange(sent)
    rows_c, row_mask, back = deal_rows(owner, c_all, down_weight, experts, capacity)
    rows_back, gate_low, up_low, active, weighted, share = expert_layer(
        owner, h_rows, gains, row_mask, back, gate_weight, up_weight, experts
    )
    came_back = exchange(rows_back)
    grads, tick = expert_weights(h_rows, rows_c, gate_low, up_low, weighted)
    grads = lax.psum(grads, "fsdp")
    gate_sum, up_sum, down_sum = widen(grads)
    sent, tick = expert_outputs(active, share, down_weight, owners, after=(tick,))

    middle_grad, middle_low, extra = router_backward(
        came_back, turn, middle, probs, mask, gains, upstream, hidden, experts, after=(tick,)
    )
    da_came, da_other = gather_fsdp(middle_low, "row_middle")
    out_rows = exchange(sent)
    layer_out, _ = layer_output(out_rows, turn, middle)
    first, dh_keep, dh_give = attention_backward(
        me,
        middle_low,
        da_came,
        da_other,
        heads,
        output_weight,
        cosine,
        sine,
        start,
        h1,
        pre,
        mixed,
        inverse,
        turned,
        extra,
        experts,
        q_heads,
    )
    dh_total, *dh_sends = pair_sum(dh_keep, send(dh_give, "fsdp", 1))
    dh_came = along_z(dh_sends)
    tokens_grad, tick = input_grad(dh_total, dh_came, own, gains, middle_grad, experts)
    first = passed(first, after=(out_rows, grads, dh_total))
    parted, rest = shares_sum(exchange(first), after=tuple(dh_came))
    parted = lax.all_to_all(parted, "fsdp", 0, 0, tiled=True)
    pieces = exchange(whole_pieces(parted, rest, after=(tick,)))
    query_sum, key_sum, value_sum, output_sum, one_sum, two_sum, *gain_sums, router_sum = final_grads(
        pieces, query_weight, key_weight, value_weight, first_gain[None], experts
    )
    return (
        layer_out[None],
        tokens_grad[None],
        one_sum[0],
        query_sum,
        key_sum,
        value_sum,
        output_sum,
        gain_sums[0][0],
        gain_sums[1][0],
        two_sum[0],
        router_sum.T,
        gate_sum,
        up_sum,
        down_sum,
    )


def solution(mesh):
    whole = P("expert", "fsdp", None)
    rows = P("fsdp", None)
    vector = P("fsdp")
    owned = P("expert", None, None)
    return jax.shard_map(
        shards,
        mesh=mesh,
        in_specs=(
            whole,
            P("expert", None),
            whole,
            vector,
            rows,
            rows,
            rows,
            rows,
            vector,
            vector,
            vector,
            rows,
            owned,
            owned,
            owned,
            whole,
        ),
        out_specs=(
            whole,
            whole,
            vector,
            rows,
            rows,
            rows,
            rows,
            vector,
            vector,
            vector,
            rows,
            owned,
            owned,
            owned,
        ),
        check_vma=False,
    )
```

```python
import functools

import jax
import jax.numpy as jnp
from jax import lax
from jax.experimental import pallas as pl
from jax.experimental.pallas import tpu as pltpu
from jax.sharding import PartitionSpec as P

EPSILON = 1e-06
ROPE_BASE = 10000.0
HEAD = 64
TILE = 256
F32 = jnp.float32
BF16 = jnp.bfloat16
VMEM = pl.BlockSpec(memory_space=pltpu.VMEM)
SMEM = pl.BlockSpec(memory_space=pltpu.SMEM)
ANY = pl.BlockSpec(memory_space=pl.ANY)
HBM = pl.BlockSpec(memory_space=pltpu.HBM)


def dot(left, right, dims=((1,), (0,))):
    return lax.dot_general(left, right, (dims, ((), ())), preferred_element_type=F32)


def shape(extent, dtype):
    return jax.ShapeDtypeStruct(extent, dtype)


def kernel_call(
    body, name, micros, operands, results, smem=0, hbm=(), out_hbm=(), after=(), scratch=(), held=(), late=(), stored=(), mib=63
):
    held = tuple(held) + tuple(late)
    n, a, r, s = len(operands), len(after), len(results), len(scratch)
    specs = [SMEM if i < smem else HBM if i in held or i in hbm else VMEM for i in range(n)]
    out_specs = [HBM if i in stored or i in out_hbm else VMEM for i in range(r)]
    staged = [pltpu.VMEM(operands[i].shape, operands[i].dtype) for i in held]
    staged += [pltpu.VMEM(*results[i]) for i in stored]
    sems = [pltpu.SemaphoreType.DMA((max(len(held), 1),)), pltpu.SemaphoreType.DMA((max(len(stored), 1),))]

    def wrapped(*refs):
        ins, outs = list(refs[:n]), list(refs[n + a : n + a + r])
        own = refs[n + a + r : n + a + r + s]
        stages, (load_sem, store_sem) = refs[n + a + r + s : -2], refs[-2:]
        loads, stores, begun = {}, {}, []
        for k, i in enumerate(held):
            loads[i] = pltpu.make_async_copy(ins[i], stages[k], load_sem.at[k])
            loads[i].start()
            ins[i] = stages[k]
        for k, i in enumerate(stored):
            stores[i] = pltpu.make_async_copy(stages[len(held) + k], outs[i], store_sem.at[k])
            outs[i] = stages[len(held) + k]
        for i in held:
            if i not in late:
                loads[i].wait()

        def store(*which):
            for i in which:
                stores[i].start()
                begun.append(i)

        extra = {}
        if late:
            extra["wait"] = lambda i: loads[i].wait()
        if stored:
            extra["store"] = store
        body(*ins, *outs, *own, **extra)
        store(*[i for i in stored if i not in begun])
        for i in stored:
            stores[i].wait()

    return pl.pallas_call(
        wrapped,
        out_shape=[shape(*result) for result in results],
        in_specs=specs + [ANY] * a,
        out_specs=out_specs,
        scratch_shapes=list(scratch) + staged + sems,
        compiler_params=pltpu.CompilerParams(vmem_limit_bytes=mib * 1024 * 1024),
        cost_estimate=pl.CostEstimate(flops=0, bytes_accessed=int(micros * 3.6e6), transcendentals=0),
        name=name,
    )(*operands, *after)


def move_call(moves, name, micros, operands, results, after=(), mib=10):
    def body(*refs):
        for source, target in moves(*refs):
            target[...] = source[...]

    return kernel_call(body, name, micros, operands, results, after=after, mib=mib)


def lane_blocks(value):
    return jnp.concatenate([value[:, i : i + 128] for i in range(0, value.shape[1], 128)], axis=0)


def joined_lanes(value, count):
    rows = value.shape[0] // count
    return jnp.concatenate([value[i * rows : (i + 1) * rows] for i in range(count)], axis=1)


def softmax_rows(logits):
    powers = jnp.exp(logits - jnp.max(logits, axis=0, keepdims=True))
    return powers / jnp.sum(powers, axis=0, keepdims=True)


def head_forward(pre, gain, cosine, sine):
    scale = lax.rsqrt(jnp.mean(pre * pre, axis=0, keepdims=True) + EPSILON)
    normed = pre * scale
    scaled = normed * gain
    a, b = scaled[: HEAD // 2], scaled[HEAD // 2 :]
    turned = jnp.concatenate([a * cosine - b * sine, b * cosine + a * sine], axis=0)
    return turned, normed, scale


def head_backward(grad, normed, scale, gain, cosine, sine):
    a, b = grad[: HEAD // 2], grad[HEAD // 2 :]
    unturned = jnp.concatenate([a * cosine + b * sine, b * cosine - a * sine], axis=0)
    gain_grad = jnp.sum(unturned * normed, axis=1, keepdims=True)
    inner = unturned * gain
    pre_grad = scale * (inner - normed * jnp.mean(inner * normed, axis=0, keepdims=True))
    return pre_grad, gain_grad


def slots_kernel(mask_ref, deal_ref, turn_ref, whole_ref, *, capacity, store):
    experts, rows = mask_ref.shape
    mask = mask_ref[...]
    ranks = dot(mask.astype(BF16), earlier(rows))
    slot = lax.broadcasted_iota(jnp.int32, (capacity, rows), 0).astype(F32) + 1.0
    for expert in range(experts):
        one = slice(expert, expert + 1)
        whole_ref[expert * capacity : (expert + 1) * capacity] = jnp.where(
            (ranks[one] == slot) & (mask[one] > 0.5), 1.0, 0.0
        )
    deal_ref[...] = whole_ref[...].astype(BF16)
    store(0)
    for part in range(0, experts * capacity, 128):
        turn_ref[:, part : part + 128] = whole_ref[part : part + 128].T.astype(BF16)


def slot_tables(mask, capacity):
    experts, rows = mask.shape
    slots = experts * capacity
    return kernel_call(
        functools.partial(slots_kernel, capacity=capacity),
        "slot_tables",
        2.0,
        [mask],
        [((slots, rows), BF16), ((rows, slots), BF16)],
        scratch=[pltpu.VMEM((slots, rows), F32)],
        stored=(0, 1),
    )


def earlier(rows):
    return (
        lax.broadcasted_iota(jnp.int32, (rows, rows), 0)
        <= lax.broadcasted_iota(jnp.int32, (rows, rows), 1)
    ).astype(BF16)


def pack_kernel(
    me_ref, x_ref, wq_ref, wk_ref, wv_ref, router_ref, one_ref, two_ref, qg_ref, kg_ref, routes_ref, c_ref, *outs, wait, store
):
    own_ref, sends, dressed_ref, mask_ref, other_ref, parts_ref = outs[0], outs[1:4], *outs[4:]
    experts, rows = router_ref.shape
    wide = wq_ref.shape[1] // 8
    narrow = wk_ref.shape[1] // 8
    count = qg_ref.shape[1]
    heads = jnp.concatenate([qg_ref[...], kg_ref[...]], axis=0).astype(F32)
    heads = jnp.concatenate([heads, jnp.zeros((2, 128 - count), F32)], axis=1)
    heads = jnp.concatenate([heads, jnp.zeros((126, 128), F32)], axis=0).T[:count]
    small = jnp.concatenate(
        [
            router_ref[...].astype(F32),
            one_ref[...].astype(F32),
            two_ref[...].astype(F32),
            jnp.zeros((6, 128), F32),
            heads,
        ],
        axis=0,
    ).astype(BF16)
    for part in range(8):
        parts_ref[part, :wide] = wq_ref[:, part * wide : (part + 1) * wide].astype(F32).T.astype(BF16)
        parts_ref[part, wide + 2 * narrow :] = small
    for pair in range(4):
        span = slice(pair * 128, (pair + 1) * 128)
        for ref, place in ((wk_ref, wide), (wv_ref, wide + narrow)):
            turned = ref[:, span].astype(F32).T.astype(BF16)
            parts_ref[2 * pair, place : place + narrow] = turned[:narrow]
            parts_ref[2 * pair + 1, place : place + narrow] = turned[narrow:]
    me = me_ref[0]
    tall = parts_ref.shape[1]
    blocks = lane_blocks(x_ref[...])
    base = blocks.shape[0]
    own_ref[...] = parts_ref[me]
    other_ref[...] = parts_ref[me ^ 1]
    for flip in range(1, 4):
        sends[flip - 1][:base] = blocks
        sends[flip - 1][base : base + tall] = parts_ref[me ^ (2 * flip)]
        sends[flip - 1][base + tall :] = parts_ref[me ^ (2 * flip + 1)]
    store(1, 2, 3, 6, 0)
    wait(10)
    wait(11)
    width = c_ref.shape[1]
    subs = lax.broadcasted_iota(jnp.int32, (128, rows), 0)
    routed = jnp.zeros((128, rows), F32)
    for route in range(routes_ref.shape[0]):
        routed = routed + jnp.where(routes_ref[route : route + 1] == subs, 1.0, 0.0)
    dressed_ref[:, :width] = c_ref[...]
    dressed_ref[:, width:] = routed.T.astype(BF16)
    mask_ref[...] = routed[:experts]


def pack_weights(me, x, wq, wk, wv, router, one, two, qg, kg, routes, c):
    experts = router.shape[0]
    tall = (wq.shape[1] + wk.shape[1] + wv.shape[1]) // 8 + experts + 16
    rows, width = x.shape
    base = rows * 8
    own, first, second, third, dressed, mask, other = kernel_call(
        pack_kernel,
        "pack_weights",
        2.5,
        [me, x, wq, wk, wv, router, one, two, qg, kg, routes, c],
        [((tall, 128), BF16)]
        + [((base + 2 * tall, 128), BF16)] * 3
        + [((rows, width + 128), BF16), ((experts, rows), F32), ((tall, 128), BF16)],
        smem=1,
        scratch=[pltpu.VMEM((8, tall, 128), BF16)],
        held=range(1, 10),
        late=(10, 11),
        stored=(0, 1, 2, 3, 4, 5, 6),
    )
    return (own, other), [first, second, third], dressed, mask


def relay(came, base, after):
    tall = (came[0].shape[0] - base) // 2

    def moves(*refs):
        pairs = []
        for flip, ref in enumerate(refs[:3]):
            pairs.append((ref.at[:base], refs[3].at[flip, :base]))
            pairs.append((ref.at[base + tall :], refs[3].at[flip, base:]))
        return pairs

    return move_call(moves, "relay", 1.5, came, [((3, base + tall, 128), BF16)], after)[0]


def forward_kernel(me_ref, x_ref, own_ref, *refs, experts, q_heads, store):
    came, other_x, other_w, other_ref = refs[:3], refs[3], refs[4], refs[5]
    cos_ref, sin_ref, start_ref = refs[6:9]
    h1_ref, pre_ref, keep_ref, give_ref, inverse_ref, gains_ref, heads_ref, turned_ref, out_ref = refs[-9:]
    rows, width = x_ref.shape
    q_columns = q_heads * HEAD
    columns = q_columns + 2 * HEAD
    total = rows * 8
    tall = own_ref.shape[0]
    base = 8 * rows
    me = me_ref[0]
    for slot in range(8):
        flip = slot // 2
        if slot % 2:
            piece = other_ref[flip - 1, base:] if flip else other_w[...]
        elif flip:
            piece = came[flip - 1][base : base + tall]
        else:
            piece = own_ref[...]
        span = pl.ds(pl.multiple_of((me ^ slot) * rows, rows), rows)
        turned_ref[:, span] = piece[:columns]
        small = piece[columns:].astype(F32)
        gains_ref[:, span] = small[: experts + 8]
        heads_ref[pl.ds(pl.multiple_of((me ^ slot) * 8, 8), 8)] = small[experts + 8 :]
    gain_one = gains_ref[experts : experts + 1]
    for slot in range(8):
        flip = slot // 2
        if slot % 2:
            x = joined_lanes(other_ref[flip - 1, :base], 8) if flip else other_x[...]
        elif flip:
            x = joined_lanes(came[flip - 1][:base], 8)
        else:
            x = x_ref[...]
        x = x.astype(F32)
        scale = lax.rsqrt(jnp.mean(x * x, axis=1, keepdims=True) + EPSILON)
        h1_ref[slot] = (x * scale * gain_one).astype(BF16)
    store(0, 6, 7)
    for slot in range(8):
        block = dot(turned_ref[...], h1_ref[slot], ((1,), (1,)))
        place = pl.multiple_of((me ^ slot) * rows, rows)
        pre_ref[:, pl.ds(place, rows)] = block
    store(1)
    cosine, sine = cos_ref[...], sin_ref[...]
    gain_query, gain_key = heads_ref[:, :1], heads_ref[:, 1:2]
    key = head_forward(pre_ref[q_columns : q_columns + HEAD], gain_key, cosine, sine)[0]
    key = key.T.astype(BF16)
    value = pre_ref[q_columns + HEAD :].astype(BF16)
    inverse_ref[...] = jnp.zeros(inverse_ref.shape, F32)
    for head in range(q_heads):
        query = head_forward(pre_ref[head * HEAD : (head + 1) * HEAD], gain_query, cosine, sine)[0]
        query = query.astype(BF16) * jnp.array(HEAD ** (-0.5), BF16)
        for tile in range(total // TILE):
            low, high = tile * TILE, (tile + 1) * TILE
            scores = dot(key[:high], query[:, low:high])
            u = lax.broadcasted_iota(jnp.int32, (high, TILE), 0)
            t = lax.broadcasted_iota(jnp.int32, (high, TILE), 1) + low
            allowed = (u >= start_ref[:, low:high]) & (u <= t)
            powers = jnp.where(allowed, jnp.exp(scores), 0.0)
            inverse = 1.0 / jnp.sum(powers, axis=0, keepdims=True)
            probs = (powers * inverse).astype(BF16)
            mixed = dot(value[:, :high], probs).astype(BF16)
            inverse_ref[head : head + 1, low:high] = inverse
            for part in range(TILE // rows):
                out_ref[low // rows + part, head * HEAD : (head + 1) * HEAD] = mixed[
                    :, part * rows : (part + 1) * rows
                ]
    for slot in range(8):
        (give_ref if slot % 2 else keep_ref)[slot // 2] = out_ref[me ^ slot]


def attention_forward(me, x, own, came, other, cosine, sine, start, experts, q_heads, after=()):
    rows, width = x.shape
    total = 8 * rows
    columns = (q_heads + 2) * HEAD
    q_columns = q_heads * HEAD
    return kernel_call(
        functools.partial(forward_kernel, experts=experts, q_heads=q_heads),
        "attention_forward",
        7.0,
        [me, x, own, *came, *other, cosine, sine, start],
        [
            ((8, rows, width), BF16),
            ((columns, total), F32),
            ((4, q_columns, rows), BF16),
            ((4, q_columns, rows), BF16),
            ((8, total), F32),
            ((experts + 8, width), F32),
            ((HEAD, 128), F32),
            ((columns, width), BF16),
            ((8, q_columns, rows), BF16),
        ],
        smem=1,
        after=after,
        held=(1,),
        stored=(0, 1, 4, 6, 7, 8),
    )


def merge(keep, came, wo, wo_came):
    def moves(keep_ref, came_ref, *refs):
        weights, outs, stacked = refs[:4], refs[4:7], refs[7]
        pairs = [(weight, stacked.at[i]) for i, weight in enumerate(weights)]
        for flip in range(1, 4):
            pairs.append((keep_ref.at[flip], outs[flip - 1].at[0]))
            pairs.append((came_ref.at[flip], outs[flip - 1].at[1]))
        return pairs

    extent = ((2,) + keep.shape[1:], BF16)
    results = [extent] * 3 + [((4,) + wo.shape, BF16)]
    *sends, stacked = move_call(moves, "merge", 1.0, [keep, came, wo, *wo_came], results)
    return sends, stacked


def middle_kernel(x_ref, keep_ref, other_ref, *refs, experts, wait, store):
    came, wo_ref, wo_came, wo_other_ref, gains_ref, deal_ref = refs[:3], refs[3], refs[4:7], refs[7], refs[8], refs[9]
    middle_ref, probs_ref, hidden_ref, sent_ref, mixed_ref, whole_ref, out_ref, out_sem = refs[10:]
    rows, width = x_ref.shape
    for slot in range(8):
        flip, core = slot // 2, slot % 2
        if flip:
            piece = came[flip - 1][core]
        else:
            piece = (other_ref if core else keep_ref)[0]
        span = slice(slot * 128, (slot + 1) * 128)
        mixed_ref[:, span] = piece.astype(F32).T.astype(BF16)
    for i in (6, 7, 8, 9, 10):
        wait(i)
    for slot in range(8):
        flip = slot // 2
        span = slice(slot * 128, (slot + 1) * 128)
        if slot % 2:
            whole_ref[span] = wo_other_ref[flip]
        else:
            whole_ref[span] = (wo_came[flip - 1] if flip else wo_ref)[...]
    wait(0)
    middle = x_ref[...].astype(F32) + dot(mixed_ref[...], whole_ref[...])
    middle_ref[...] = middle
    scale = lax.rsqrt(jnp.mean(middle * middle, axis=1, keepdims=True) + EPSILON)
    hidden = (middle * scale * gains_ref[experts + 1 : experts + 2]).astype(BF16)
    hidden_ref[...] = hidden
    probs_ref[...] = softmax_rows(dot(gains_ref[:experts].astype(BF16), hidden, ((1,), (1,))))
    store(0, 2)
    owners, per_owner, capacity, _ = sent_ref.shape
    group = owners // 4
    size = group * per_owner * capacity
    copies = []
    wait(12)
    for part in range(4):
        taken = dot(deal_ref[part * size : (part + 1) * size], hidden).astype(BF16)
        blocks = slice(group * part, group * (part + 1))
        out_ref[blocks] = taken.reshape(group, per_owner, capacity, width)
        copies.append(pltpu.make_async_copy(out_ref.at[blocks], sent_ref.at[blocks], out_sem.at[part]))
        copies[-1].start()
    for copy in copies:
        copy.wait()


def middle_layer(x, keep, other, came, wo, wo_came, wo_other, gains, deal, experts, owners):
    rows, width = x.shape
    per_owner = experts // owners
    capacity = deal.shape[0] // experts
    sent = ((owners, per_owner, capacity, width), BF16)
    return kernel_call(
        functools.partial(middle_kernel, experts=experts),
        "middle_layer",
        3.0,
        [x, keep, other, *came, wo, *wo_came, wo_other, gains, deal],
        [((rows, width), F32), ((experts, rows), F32), ((rows, width), BF16), sent],
        out_hbm=(3,),
        scratch=[
            pltpu.VMEM((rows, width), BF16),
            pltpu.VMEM((width, width), BF16),
            pltpu.VMEM(*sent),
            pltpu.SemaphoreType.DMA((4,)),
        ],
        late=(6, 7, 8, 9, 10, 0, 12),
        stored=(0, 2),
    )


def row(pieces, name):
    def moves(*refs):
        return [(ref, refs[-1].at[i]) for i, ref in enumerate(refs[:-1])]

    return move_call(moves, name, 1.0, pieces, [((len(pieces),) + pieces[0].shape, BF16)])[0]


def backward_kernel(me_ref, own_da_ref, *refs, experts, q_heads, wait):
    came, other_ref = refs[:3], refs[3]
    heads_ref, wo_ref, cos_ref, sin_ref, start_ref = refs[4:9]
    h1_ref, pre_ref, mixed_ref, inverse_ref, turned_ref, extra_ref = refs[9:15]
    first_ref, keep_ref, send_ref = refs[-10:-7]
    da_ref, mixed_grad_ref, dkey_ref, dvalue_ref, low_ref, out_slots_ref, grad_ref = refs[-7:]
    rows, width = own_da_ref.shape
    q_columns = q_heads * HEAD
    columns = q_columns + 2 * HEAD
    total = rows * 8
    me = me_ref[0]
    for slot in range(8):
        flip, core = slot // 2, slot % 2
        if core:
            piece = other_ref[flip]
        else:
            piece = (came[flip - 1] if flip else own_da_ref)[...]
        span = slice(slot * rows, (slot + 1) * rows)
        da_ref[span] = piece
        place = pl.multiple_of((me ^ slot) * rows, rows)
        mixed_grad_ref[:, pl.ds(place, rows)] = dot(wo_ref[...], piece, ((1,), (1,))).astype(BF16)
    wait(13)
    for slot in range(8):
        out_slots_ref[:, slot * rows : (slot + 1) * rows] = mixed_ref[me ^ slot]
    wo_grad = dot(out_slots_ref[...], da_ref[...]).astype(BF16)
    wo_grad = lane_blocks(wo_grad)
    wait(12)
    wait(14)
    gain_query, gain_key = heads_ref[:, :1], heads_ref[:, 1:2]
    cosine, sine = cos_ref[...], sin_ref[...]
    key_turned, key_normed, key_scale = head_forward(
        pre_ref[q_columns : q_columns + HEAD], gain_key, cosine, sine
    )
    key_low = key_turned.astype(BF16)
    key = key_turned.T.astype(BF16)
    value = pre_ref[q_columns + HEAD :].T.astype(BF16)
    dkey_ref[...] = jnp.zeros(dkey_ref.shape, F32)
    dvalue_ref[...] = jnp.zeros(dvalue_ref.shape, F32)
    gain_query_grad = jnp.zeros((HEAD, 1), F32)
    pieces = []
    for head in range(q_heads):
        span = slice(head * HEAD, (head + 1) * HEAD)
        turned, normed, scale = head_forward(pre_ref[span], gain_query, cosine, sine)
        query = turned.astype(BF16) * jnp.array(HEAD ** (-0.5), BF16)
        grads = []
        for tile in range(total // TILE):
            low, high = tile * TILE, (tile + 1) * TILE
            part = query[:, low:high]
            mixed_grad = mixed_grad_ref[span, low:high]
            scores = dot(key[:high], part)
            u = lax.broadcasted_iota(jnp.int32, (high, TILE), 0)
            t = lax.broadcasted_iota(jnp.int32, (high, TILE), 1) + low
            allowed = (u >= start_ref[:, low:high]) & (u <= t)
            probs = jnp.where(allowed, jnp.exp(scores) * inverse_ref[head : head + 1, low:high], 0.0)
            attend = dot(value[:high], mixed_grad)
            delta = jnp.sum(probs * attend, axis=0, keepdims=True)
            score_low = (probs * (attend - delta)).astype(BF16)
            grads.append(dot(key_low[:, :high], score_low))
            dkey_ref[:, :high] += dot(part, score_low, ((1,), (1,)))
            dvalue_ref[:, :high] += dot(mixed_grad, probs.astype(BF16), ((1,), (1,)))
        query_grad = jnp.concatenate(grads, axis=1) * HEAD ** (-0.5)
        pre_grad, gain_grad = head_backward(query_grad, normed, scale, gain_query, cosine, sine)
        gain_query_grad += gain_grad
        pieces.append(pre_grad)
    pre_grad, gain_key_grad = head_backward(
        dkey_ref[...], key_normed, key_scale, gain_key, cosine, sine
    )
    pieces += [pre_grad, dvalue_ref[...]]
    pre_grad = jnp.concatenate(pieces, axis=0)
    low_ref[...] = pre_grad.astype(BF16)
    slots_grad = []
    for slot in range(8):
        place = pl.multiple_of((me ^ slot) * rows, rows)
        slots_grad.append(low_ref[:, pl.ds(place, rows)])
    slots_grad = jnp.concatenate(slots_grad, axis=1)
    wait(11)
    wait(15)
    grad_ref[:columns] = dot(slots_grad, h1_ref[...].reshape(total, width))
    extra = extra_ref[...]
    lane = lax.broadcasted_iota(jnp.int32, (HEAD, 128), 1)
    gains = jnp.where(lane == 0, gain_query_grad, jnp.where(lane == 1, gain_key_grad, 0.0))
    gains = gains.T[:2]
    step = HEAD // 8
    grad_ref[columns:] = jnp.zeros((64, width), F32)
    grad_ref[columns : columns + experts + 1] = extra[: experts + 1]
    for part in range(8):
        grad_ref[columns + experts + 1 : columns + experts + 3, part * rows : part * rows + step] = gains[
            :, part * step : (part + 1) * step
        ]
    for piece in range(16):
        spare = []
        place = columns + piece * SPARE
        for part in range(8):
            span = slice(part * rows, (part + 1) * rows)
            block = grad_ref[piece * PIECE : (piece + 1) * PIECE, span]
            first_ref[piece, part * PIECE : (part + 1) * PIECE] = block.astype(BF16)
            spare.append(grad_ref[place : place + SPARE, span])
        spare.append(jnp.zeros((2 * PIECE - 8 * SPARE, 128), F32))
        first_ref[piece, 8 * PIECE : 10 * PIECE] = jnp.concatenate(spare, axis=0).astype(BF16)
        first_ref[piece, 10 * PIECE :] = wo_grad[piece * SLICE : (piece + 1) * SLICE]
    turned = turned_ref[...]
    for slot in range(8):
        low_rows_slot = slots_grad[:, slot * rows : (slot + 1) * rows].astype(F32).T.astype(BF16)
        part = dot(low_rows_slot, turned)
        if slot % 2:
            send_ref[slot // 2] = part.astype(BF16)
        else:
            keep_ref[slot // 2] = part


def attention_backward(
    me, da, came, other, heads, wo, cosine, sine, start, h1, pre, mixed, inverse, turned, extra, experts, q_heads, after=()
):
    rows, width = da.shape
    total = 8 * rows
    columns = pre.shape[0]
    q_columns = q_heads * HEAD
    return kernel_call(
        functools.partial(backward_kernel, experts=experts, q_heads=q_heads),
        "attention_backward",
        12,
        [me, da, *came, other, heads, wo, cosine, sine, start, h1, pre, mixed, inverse, turned, extra],
        [
            ((16, 10 * PIECE + SLICE, 128), BF16),
            ((4, rows, width), F32),
            ((4, rows, width), BF16),
        ],
        smem=1,
        after=after,
        held=(6, 7),
        late=(11, 12, 13, 14, 15),
        scratch=[
            pltpu.VMEM((total, width), BF16),
            pltpu.VMEM((q_columns, total), BF16),
            pltpu.VMEM((HEAD, total), F32),
            pltpu.VMEM((HEAD, total), F32),
            pltpu.VMEM((columns, total), BF16),
            pltpu.VMEM((q_columns, total), BF16),
            pltpu.VMEM((columns + 64, width), F32),
        ],
    )


def deal_kernel(owner_ref, c_ref, down_ref, rows_c, mask_ref, back_ref, c_scratch, sems, *, experts, capacity, wait, store):
    owner = owner_ref[0]
    per_owner, hidden, width = down_ref.shape
    rows = c_ref.shape[1]
    loads = [pltpu.make_async_copy(c_ref.at[i], c_scratch.at[i], sems.at[i]) for i in range(16)]
    for load in loads:
        load.start()
    lanes = lax.broadcasted_iota(jnp.int32, (experts, 128), 1)
    subs = lax.broadcasted_iota(jnp.int32, (experts, 128), 0)
    eye = (lanes == subs).astype(BF16)
    before = earlier(rows)
    mine_of = lax.broadcasted_iota(jnp.int32, (experts, rows), 0) - owner * per_owner
    slot = lax.broadcasted_iota(jnp.int32, (capacity, rows), 0).astype(F32) + 1.0
    for block in range(16):
        loads[block].wait()
        c = c_scratch[block]
        mask = dot(eye, c[:, width:], ((1,), (1,)))
        ranks = dot(mask.astype(BF16), before)
        deals = []
        for k in range(per_owner):
            mine = mine_of == k
            hit = jnp.sum(jnp.where(mine, mask, 0.0), axis=0, keepdims=True)
            rank = jnp.sum(jnp.where(mine, ranks, 0.0), axis=0, keepdims=True)
            deals.append(jnp.where((rank == slot) & (hit > 0.5), 1.0, 0.0))
        taken = dot(jnp.concatenate(deals, axis=0).astype(BF16), c).astype(BF16)
        span = slice(block * capacity, (block + 1) * capacity)
        for k in range(per_owner):
            spot = slice(k * capacity, (k + 1) * capacity)
            rows_c[k, span] = taken[spot, :width]
            mask_ref[k, span] = taken[spot, width:]
    store(0, 1)
    wait(2)
    for k in range(per_owner):
        for tile in range(16 * capacity // TILE):
            span = slice(tile * TILE, (tile + 1) * TILE)
            back_ref[k, span] = dot(rows_c[k, span], down_ref[k], ((1,), (1,)))


def deal_rows(owner, c, down, experts, capacity):
    per_owner, hidden, width = down.shape
    count = 16 * capacity
    return kernel_call(
        functools.partial(deal_kernel, experts=experts, capacity=capacity),
        "deal_rows",
        12.0,
        [owner, c, down],
        [
            ((per_owner, count, width), BF16),
            ((per_owner, count, 128), BF16),
            ((per_owner, count, hidden), F32),
        ],
        smem=1,
        hbm=(1,),
        scratch=[pltpu.VMEM(c.shape, BF16), pltpu.SemaphoreType.DMA((16,))],
        late=(2,),
        stored=(0, 1, 2),
    )


def expert_kernel(
    owner_ref,
    h_hbm,
    gains_ref,
    mask_ref,
    back_hbm,
    gate_hbm,
    up_hbm,
    rows_hbm,
    gate_out,
    up_out,
    active_out,
    weighted_out,
    share_ref,
    h_ref,
    back_in,
    gate_ref,
    up_ref,
    rows_back,
    gate_sum,
    up_sum,
    logit_sum,
    spread_ref,
    load_sem,
    store_sem,
    *,
    experts,
    store,
):
    owners, per_owner, capacity, width = h_hbm.shape
    group = 8
    parts = owners // group
    size = group * capacity
    loads = {}
    for k in range(per_owner):
        for part in range(parts):
            blocks = slice(part * group, (part + 1) * group)
            spot = (k * parts + part) * 4
            loads[k, part] = [
                pltpu.make_async_copy(h_hbm.at[blocks, k], h_ref.at[blocks, k], load_sem.at[spot]),
                pltpu.make_async_copy(
                    back_hbm.at[k, part * size : (part + 1) * size],
                    back_in.at[k, part * size : (part + 1) * size],
                    load_sem.at[spot + 1],
                ),
            ]
            if part == 0:
                loads[k, part] += [
                    pltpu.make_async_copy(gate_hbm.at[k], gate_ref.at[k], load_sem.at[spot + 2]),
                    pltpu.make_async_copy(up_hbm.at[k], up_ref.at[k], load_sem.at[spot + 3]),
                ]
            for load in loads[k, part]:
                load.start()
    owner = owner_ref[0]
    router = jnp.concatenate([gains_ref[:experts], jnp.zeros((128 - experts, width), F32)], axis=0)
    router = router.astype(BF16)
    lane = lax.broadcasted_iota(jnp.int32, (size, 128), 1)
    copies = []
    chunk = capacity
    lane = lane[:chunk]
    order = [(k, part) for k in range(per_owner) for part in range(parts)]

    def begin(i):
        k, part = order[i]
        blocks = slice(part * group, (part + 1) * group)
        for load in loads[k, part]:
            load.wait()
        h = h_ref[blocks, k].reshape(size, width)
        gate_sum[i % 2] = dot(h, gate_ref[k])
        up_sum[i % 2] = dot(h, up_ref[k])
        logit_sum[i % 2] = dot(h, router, ((1,), (1,)))

    begin(0)
    for i, (k, part) in enumerate(order):
        if i + 1 < len(order):
            begin(i + 1)
        place = owner * per_owner + k
        blocks = slice(part * group, (part + 1) * group)
        span = slice(part * size, (part + 1) * size)
        for spot in range(0, size, chunk):
            here = slice(part * size + spot, part * size + spot + chunk)
            near = slice(spot, spot + chunk)
            logits = logit_sum[i % 2, near]
            chosen = mask_ref[k, here] > 0.5
            top = jnp.max(jnp.where(chosen, logits, -1e30), axis=1, keepdims=True)
            powers = jnp.where(chosen, jnp.exp(logits - top), 0.0)
            total = jnp.sum(powers, axis=1, keepdims=True)
            share = jnp.sum(jnp.where(lane == place, powers, 0.0), axis=1, keepdims=True)
            share = share / jnp.where(total > 0.0, total, 1.0)
            share_ref[k, here] = jnp.broadcast_to(share, (chunk, 128))
            gate, up, back = gate_sum[i % 2, near], up_sum[i % 2, near], back_in[k, here]
            sig = 1.0 / (1.0 + jnp.exp(-gate))
            silu = gate * sig
            active = silu * up
            active_low = active.astype(BF16)
            route_grad = jnp.sum(active_low.astype(F32) * back, axis=1, keepdims=True)
            grad = back * share
            gate_out[k, here] = (grad * up * (sig + silu * (1.0 - sig))).astype(BF16)
            up_out[k, here] = (grad * silu).astype(BF16)
            active_out[k, here] = active_low
            weighted_out[k, here] = (active * share).astype(BF16)
            high = route_grad.astype(BF16).astype(F32)
            spread_out = jnp.where(lane == place, high, 0.0)
            spread_out = jnp.where(lane == place + experts, route_grad - high, spread_out)
            spread_ref[near] = spread_out.astype(BF16)
        rows = dot(gate_out[k, span], gate_ref[k], ((1,), (1,))) + dot(up_out[k, span], up_ref[k], ((1,), (1,)))
        rows_back[blocks, k, :, :width] = rows.astype(BF16).reshape(group, capacity, width)
        rows_back[blocks, k, :, width:] = spread_ref[...].reshape(group, capacity, 128)
        copies.append(
            pltpu.make_async_copy(rows_back.at[blocks, k], rows_hbm.at[blocks, k], store_sem.at[k * parts + part])
        )
        copies[-1].start()
    store(1, 2, 3, 4, 5)
    for copy in copies:
        copy.wait()


def expert_layer(owner, h, gains, mask, back, gate, up, experts):
    per_owner, width, hidden = gate.shape
    owners, _, capacity, _ = h.shape
    count = owners * capacity
    narrow = ((per_owner, count, hidden), BF16)
    rows_back = ((owners, per_owner, capacity, width + 128), BF16)
    pieces = per_owner * (owners // 8)
    return kernel_call(
        functools.partial(expert_kernel, experts=experts),
        "expert_layer",
        14.0,
        [owner, h, gains, mask, back, gate, up],
        [rows_back] + [narrow] * 4 + [((per_owner, count, 128), F32)],
        smem=1,
        hbm=(1, 4, 5, 6),
        out_hbm=(0,),
        scratch=[pltpu.VMEM(value.shape, value.dtype) for value in (h, back, gate, up)]
        + [pltpu.VMEM(*rows_back)]
        + [pltpu.VMEM((2, 8 * capacity, n), F32) for n in (hidden, hidden, 128)]
        + [pltpu.VMEM((8 * capacity, 128), BF16)]
        + [pltpu.SemaphoreType.DMA((4 * pieces,)), pltpu.SemaphoreType.DMA((pieces,))],
        stored=(1, 2, 3, 4, 5),
    )


def weights_kernel(
    h_hbm, rows_c, gate_low, up_low, weighted, out_hbm, tick_ref, h_ref, out_ref, load_sem, store_sem, *, wait
):
    tick_ref[...] = jnp.zeros(tick_ref.shape, F32)
    first = ((0,), (0,))
    owners, per_owner, capacity, width = h_hbm.shape
    hidden = gate_low.shape[2]
    half = width // 2
    loads = [
        pltpu.make_async_copy(h_hbm.at[:, k], h_ref.at[:, k], load_sem.at[k]) for k in range(per_owner)
    ]
    for load in loads:
        load.start()
    stores = []

    def keep(place):
        stores.append(pltpu.make_async_copy(out_ref.at[place], out_hbm.at[place], store_sem.at[place]))
        stores[-1].start()

    wait(2)
    for k in range(per_owner):
        loads[k].wait()
        rows_h = h_ref[:, k].reshape(owners * capacity, width)
        for place, low in ((k, gate_low), (per_owner + k, up_low)):
            if k == 0 and place:
                wait(3)
            total = dot(rows_h, low[k], first).astype(BF16)
            out_ref[place, :, :hidden] = total[:half]
            out_ref[place, :, hidden:] = total[half:]
            keep(place)
        if k == 0:
            wait(4)
            wait(1)
        place = 2 * per_owner + k
        out_ref[place] = dot(weighted[k], rows_c[k], first).astype(BF16)
        keep(place)
    for store in stores:
        store.wait()


def expert_weights(h, rows_c, gate_low, up_low, weighted):
    per_owner, count, width = rows_c.shape
    hidden = gate_low.shape[2]
    out = ((3 * per_owner, hidden, width), BF16)
    return kernel_call(
        weights_kernel,
        "expert_weights",
        0.1,
        [h, rows_c, gate_low, up_low, weighted],
        [out, ((8, 128), F32)],
        hbm=(0,),
        out_hbm=(0,),
        scratch=[
            pltpu.VMEM(h.shape, BF16),
            pltpu.VMEM(*out),
            pltpu.SemaphoreType.DMA((per_owner,)),
            pltpu.SemaphoreType.DMA((3 * per_owner,)),
        ],
        late=(2, 3, 4, 1),
    )


def widen_kernel(low_ref, gate_ref, up_ref, down_ref):
    step = pl.program_id(0)
    hidden = gate_ref.shape[2]
    value = low_ref[0].astype(F32)
    half = value.shape[0]
    for place, ref in ((0, gate_ref), (1, up_ref)):

        @pl.when(step // 2 == place)
        def _():
            ref[0, :half] = value[:, :hidden]
            ref[0, half:] = value[:, hidden:]

    @pl.when(step // 2 == 2)
    def _():
        down_ref[0] = value


def widen(low):
    count, hidden, width = low.shape
    per_owner = count // 3

    def spot(place):
        return lambda i: (jnp.clip(i - place * per_owner, 0, per_owner - 1), 0, 0)

    return pl.pallas_call(
        widen_kernel,
        grid=(count,),
        out_shape=[shape((per_owner, width, hidden), F32)] * 2 + [shape((per_owner, hidden, width), F32)],
        in_specs=[pl.BlockSpec((1, hidden, width), lambda i: (i, 0, 0))],
        out_specs=[
            pl.BlockSpec((1, width, hidden), spot(0)),
            pl.BlockSpec((1, width, hidden), spot(1)),
            pl.BlockSpec((1, hidden, width), spot(2)),
        ],
        compiler_params=pltpu.CompilerParams(vmem_limit_bytes=63 * 1024 * 1024),
        cost_estimate=pl.CostEstimate(flops=0, bytes_accessed=24_000_000, transcendentals=0),
        name="widen",
    )(low)


def outputs_kernel(active, share, down_ref, sent_ref, tick_ref, out_ref, out_sem, *, wait):
    tick_ref[...] = jnp.zeros(tick_ref.shape, F32)
    per_owner, count, hidden = active.shape
    owners, _, capacity, width = sent_ref.shape
    group = 8
    size = group * capacity
    copies = []
    for i in range(3):
        wait(i)
    for k in range(per_owner):
        for part in range(owners // group):
            span = slice(part * size, (part + 1) * size)
            blocks = slice(part * group, (part + 1) * group)
            produced = dot(active[k, span], down_ref[k]).astype(BF16).astype(F32)
            produced = (produced * share[k, span, :1]).astype(BF16)
            out_ref[blocks, k] = produced.reshape(group, capacity, width)
            copies.append(
                pltpu.make_async_copy(
                    out_ref.at[blocks, k], sent_ref.at[blocks, k], out_sem.at[k * (owners // group) + part]
                )
            )
            copies[-1].start()
    for copy in copies:
        copy.wait()


def expert_outputs(active, share, down, owners, after=()):
    per_owner, count, hidden = active.shape
    width = down.shape[2]
    sent = ((owners, per_owner, count // owners, width), BF16)
    return kernel_call(
        outputs_kernel,
        "expert_outputs",
        0.1,
        [active, share, down],
        [sent, ((8, 128), F32)],
        out_hbm=(0,),
        after=after,
        scratch=[pltpu.VMEM(*sent), pltpu.SemaphoreType.DMA((per_owner * (owners // 8),))],
        late=(0, 1, 2),
    )


def combined(rows_hbm, rows_ref, sems, turn_ref, ready):
    owners, per_owner, capacity, wide = rows_hbm.shape
    group = owners // 4
    size = group * per_owner * capacity
    loads = []
    for part in range(4):
        blocks = slice(part * group, (part + 1) * group)
        loads.append(pltpu.make_async_copy(rows_hbm.at[blocks], rows_ref.at[blocks], sems.at[part]))
        loads[-1].start()
    ready()
    total = None
    for part in range(4):
        loads[part].wait()
        rows = rows_ref[part * group : (part + 1) * group].reshape(size, wide)
        one = dot(turn_ref[:, part * size : (part + 1) * size], rows)
        total = one if total is None else total + one
    return total


def output_kernel(rows_hbm, turn_ref, middle_ref, out_ref, tick_ref, rows_ref, sems, *, wait, store):
    tick_ref[...] = jnp.zeros(tick_ref.shape, F32)
    total = combined(rows_hbm, rows_ref, sems, turn_ref, lambda: wait(1))
    wait(2)
    out_ref[...] = (middle_ref[...] + total).astype(BF16)


def layer_output(rows, turn, middle):
    return kernel_call(
        output_kernel,
        "layer_output",
        3,
        [rows, turn, middle],
        [(middle.shape, BF16), ((8, 128), F32)],
        hbm=(0,),
        scratch=[pltpu.VMEM(rows.shape, BF16), pltpu.SemaphoreType.DMA((4,))],
        late=(1, 2),
        stored=(0,),
    )


def router_kernel(
    rows_hbm,
    turn_ref,
    middle_ref,
    probs_ref,
    mask_ref,
    gains_ref,
    c_ref,
    hidden_ref,
    grad_ref,
    send_ref,
    extra_ref,
    rows_ref,
    sems,
    *,
    experts,
    wait,
    store,
):
    rows, width = middle_ref.shape
    returned = combined(rows_hbm, rows_ref, sems, turn_ref, lambda: wait(1))
    for i in (2, 4, 6, 7):
        wait(i)
    tail = returned[:, width:].T
    route_grad = tail[:experts] + tail[experts : 2 * experts]
    mask = mask_ref[...]
    probs = probs_ref[...]
    picked = probs * mask
    picked_sum = jnp.sum(picked, axis=0, keepdims=True)
    share = picked / picked_sum
    picked_grad = (route_grad - jnp.sum(route_grad * share, axis=0, keepdims=True)) / picked_sum
    prob_grad = mask * picked_grad
    logit_grad = probs * (prob_grad - jnp.sum(probs * prob_grad, axis=0, keepdims=True))
    extra_ref[:experts] = dot(logit_grad.astype(BF16), hidden_ref[...])
    logit_rows = jnp.concatenate([logit_grad, jnp.zeros((128 - experts, rows), F32)], axis=0).T
    router = gains_ref[:experts].astype(BF16)
    hidden_grad = returned[:, :width] + dot(logit_rows[:, :experts].astype(BF16), router)
    middle = middle_ref[...]
    scale = lax.rsqrt(jnp.mean(middle * middle, axis=1, keepdims=True) + EPSILON)
    normed = middle * scale
    extra_ref[experts : experts + 8] = jnp.broadcast_to(
        jnp.sum(hidden_grad * normed, axis=0, keepdims=True), (8, width)
    )
    inner = hidden_grad * gains_ref[experts + 1 : experts + 2]
    grad = c_ref[...].astype(F32) + scale * (
        inner - normed * jnp.mean(inner * normed, axis=1, keepdims=True)
    )
    grad_ref[...] = grad
    send_ref[...] = grad.astype(BF16)


def router_backward(rows_back, turn, middle, probs, mask, gains, c, hidden, experts, after=()):
    rows, width = middle.shape
    return kernel_call(
        functools.partial(router_kernel, experts=experts),
        "router_backward",
        5,
        [rows_back, turn, middle, probs, mask, gains, c, hidden],
        [((rows, width), F32), ((rows, width), BF16), ((experts + 8, width), F32)],
        hbm=(0,),
        after=after,
        scratch=[pltpu.VMEM(rows_back.shape, BF16), pltpu.SemaphoreType.DMA((4,))],
        late=(1, 2, 4, 6, 7),
        stored=(0,),
    )


def pair_kernel(keep_ref, other_ref, total_ref, *sends):
    for flip in range(4):
        total = keep_ref[flip] + other_ref[flip].astype(F32)
        if flip:
            sends[flip - 1][...] = total.astype(BF16)
        else:
            total_ref[...] = total


def pair_sum(keep, other):
    rows, width = keep.shape[1:]
    return kernel_call(
        pair_kernel, "pair_sum", 1.2, [keep, other], [((rows, width), F32)] + [((rows, width), BF16)] * 3
    )


def input_kernel(total_ref, *refs, experts, store):
    came = refs[:3]
    x_ref, gains_ref, middle_grad_ref, out_ref, tick_ref = refs[3:]
    tick_ref[...] = jnp.zeros(tick_ref.shape, F32)
    total = total_ref[...]
    for piece in came:
        total = total + piece[...].astype(F32)
    x = x_ref[...].astype(F32)
    scale = lax.rsqrt(jnp.mean(x * x, axis=1, keepdims=True) + EPSILON)
    normed = x * scale
    inner = total * gains_ref[experts : experts + 1]
    out_ref[...] = middle_grad_ref[...] + scale * (
        inner - normed * jnp.mean(inner * normed, axis=1, keepdims=True)
    )


def input_grad(total, came, x, gains, middle_grad, experts):
    return kernel_call(
        functools.partial(input_kernel, experts=experts),
        "input_grad",
        2,
        [total, *came, x, gains, middle_grad],
        [(middle_grad.shape, F32), ((8, 128), F32)],
        held=(4, 6),
        stored=(0,),
    )


PIECE, SPARE, SLICE = 16, 3, 64


def passed(value, after):
    results = [(value.shape, value.dtype)]
    return move_call(lambda *refs: [refs], "passed", 0.5, [value], results, after, 63)[0]


def shares_kernel(pieces_ref, out_ref, rest_ref):
    total = pieces_ref[0].astype(F32)
    for i in range(1, pieces_ref.shape[0]):
        total = total + pieces_ref[i].astype(F32)
    base = 8 * PIECE
    fill = jnp.zeros((PIECE - SPARE, 128), F32)
    for part in range(8):
        out_ref[part, :PIECE] = total[part * PIECE : (part + 1) * PIECE].astype(BF16)
        spare = total[base + part * SPARE : base + (part + 1) * SPARE]
        out_ref[part, PIECE:] = jnp.concatenate([spare, fill], axis=0).astype(BF16)
    rest_ref[...] = total[base + 2 * PIECE :].astype(BF16)


def shares_sum(pieces, after=()):
    return kernel_call(
        shares_kernel,
        "shares_sum",
        0.1,
        [pieces],
        [((8, 2 * PIECE, 128), BF16), ((SLICE, 128), BF16)],
        after=after,
        mib=12,
    )


def whole_kernel(came_ref, rest_ref, out_ref):
    spare = came_ref[0, PIECE:].astype(F32)
    for i in range(1, 8):
        spare = spare + came_ref[i, PIECE:].astype(F32)
    rows = [came_ref[i, :PIECE] for i in range(8)] + [spare.astype(BF16), rest_ref[...]]
    rows = jnp.concatenate(rows, axis=0)
    for i in range(16):
        out_ref[i] = rows


def whole_pieces(came, rest, after=()):
    return kernel_call(
        whole_kernel,
        "whole_pieces",
        0.1,
        [came, rest],
        [((16, 9 * PIECE + SLICE, 128), BF16)],
        after=after,
        mib=12,
    )[0]


def final_kernel(pieces_ref, wq_ref, wk_ref, wv_ref, gain_ref, *outs, experts, wait, store):
    query_ref, key_ref, value_ref, output_ref, one_ref, two_ref, qg_ref, kg_ref, router_ref = outs
    rows = pieces_ref.shape[2]
    q_columns = query_ref.shape[1] // 8
    kv_columns = key_ref.shape[1] // 8
    sums = jnp.zeros((rows, 1), F32)
    base = 8 * PIECE
    for i in range(16):
        half = i % 2 * SLICE
        output_ref[half : half + SLICE, i // 2 * rows : (i // 2 + 1) * rows] = pieces_ref[
            i, base + PIECE :
        ].astype(F32)
    store(3)
    for i in (1, 2, 3, 4):
        wait(i)
    for pair in range(4):
        keys, values = [], []
        for source in (2 * pair, 2 * pair + 1):
            block = [pieces_ref[i, source * PIECE : (source + 1) * PIECE] for i in range(16)]
            turned = jnp.concatenate(block, axis=0).astype(F32).T
            span = slice(source * q_columns, (source + 1) * q_columns)
            query = turned[:, :q_columns]
            query_ref[:, span] = query
            sums = sums + jnp.sum(query * wq_ref[:, span].astype(F32), axis=1, keepdims=True)
            keys.append(turned[:, q_columns : q_columns + kv_columns])
            values.append(turned[:, q_columns + kv_columns :])
        span = slice(2 * pair * kv_columns, 2 * (pair + 1) * kv_columns)
        for parts, ref, weight in ((keys, key_ref, wk_ref), (values, value_ref, wv_ref)):
            both = jnp.concatenate(parts, axis=1)
            ref[:, span] = both
            sums = sums + jnp.sum(both * weight[:, span].astype(F32), axis=1, keepdims=True)
    store(0, 1, 2)
    spare = pieces_ref[:, base : base + PIECE].astype(F32)
    spare = jnp.concatenate([spare[i, :SPARE] for i in range(16)], axis=0)
    one_ref[...] = jnp.broadcast_to(sums, (rows, 128)).T[:1] / gain_ref[...].astype(F32)
    two_ref[...] = spare[experts : experts + 1]
    step = qg_ref.shape[1]
    qg_ref[...] = spare[experts + 1 : experts + 2, :step]
    kg_ref[...] = spare[experts + 2 : experts + 3, :step]
    router_ref[...] = spare[:experts]


def final_grads(pieces, wq, wk, wv, gain, experts):
    rows = pieces.shape[2]
    return kernel_call(
        functools.partial(final_kernel, experts=experts),
        "final_grads",
        0.2,
        [pieces, wq, wk, wv, gain],
        [
            (wq.shape, F32),
            (wk.shape, F32),
            (wv.shape, F32),
            ((rows, 8 * rows), F32),
            ((1, rows), F32),
            ((1, rows), F32),
            ((1, HEAD // 8), F32),
            ((1, HEAD // 8), F32),
            ((experts, rows), F32),
        ],
        late=(1, 2, 3, 4),
        stored=(0, 1, 2, 3),
    )


def send(values, axis, flip):
    count = lax.axis_size(axis)
    return lax.ppermute(values, axis, [(i, i ^ flip) for i in range(count)])


def along_z(values):
    if not isinstance(values, (list, tuple)):
        values = [values] * 3
    return [send(value, "fsdp", 2 * (i + 1)) for i, value in enumerate(values)]


def gather_fsdp(block, name):
    came = along_z(block)
    return came, send(row([block, *came], name), "fsdp", 1)


def exchange(rows):
    return lax.all_to_all(rows, "expert", 0, 0, tiled=True)


def shards(
    tokens,
    lengths,
    routes,
    first_gain,
    query_weight,
    key_weight,
    value_weight,
    output_weight,
    query_gain,
    key_gain,
    second_gain,
    router_weight,
    gate_weight,
    up_weight,
    down_weight,
    cotangent,
):
    own = tokens[0]
    upstream = cotangent[0]
    rows, width = own.shape
    fsdp = lax.axis_size("fsdp")
    owners = lax.axis_size("expert")
    me = lax.axis_index("fsdp").astype(jnp.int32).reshape(1)
    owner = lax.axis_index("expert").astype(jnp.int32).reshape(1)
    experts = router_weight.shape[1]
    capacity = 3 * rows * routes.shape[2] // (2 * experts)
    kv_columns = key_weight.shape[1] // fsdp
    q_columns = query_weight.shape[1] // fsdp
    columns = q_columns + 2 * kv_columns
    q_heads = q_columns // HEAD

    ends = jnp.cumsum(lengths[0])
    place = jnp.arange(rows * fsdp, dtype=jnp.int32)
    start = jnp.max(jnp.where(ends[:, None] <= place[None, :], ends[:, None], 0), axis=0)
    position = (place - start).astype(F32)
    frequency = ROPE_BASE ** (-jnp.arange(HEAD // 2, dtype=F32) * 2.0 / HEAD)
    angles = frequency[:, None] * position[None, :]
    cosine, sine = jnp.cos(angles), jnp.sin(angles)
    start = start[None, :].astype(jnp.int32)

    packed, x_sends, dressed, mask = pack_weights(
        me,
        own,
        query_weight,
        key_weight,
        value_weight,
        router_weight.T,
        first_gain[None],
        second_gain[None],
        query_gain[None],
        key_gain[None],
        routes[0].T,
        upstream,
    )
    x_came = along_z(x_sends)
    x_other = [send(own, "fsdp", 1), send(packed[1], "fsdp", 1)]
    deal, turn = slot_tables(mask, capacity)
    ready = (*x_other, deal, cosine, sine, start)
    x_other.append(send(relay(x_came, rows * fsdp, after=ready), "fsdp", 1))
    c_all = lax.all_gather(dressed, "expert", axis=0)
    wo_came = along_z(output_weight)

    h1, pre, keep, give, inverse, gains, heads, turned, mixed = attention_forward(
        me, own, packed[0], x_came, x_other, cosine, sine, start, experts, q_heads
    )
    other = send(give, "fsdp", 1)
    mixed_sends, wo_stack = merge(keep, other, output_weight, wo_came)
    mixed_came = along_z(mixed_sends)
    wo_other = send(wo_stack, "fsdp", 1)
    middle, probs, hidden, sent = middle_layer(
        own, keep, other, mixed_came, output_weight, wo_came, wo_other, gains, deal, experts, owners
    )
    h_rows = exchange(sent)
    rows_c, row_mask, back = deal_rows(owner, c_all, down_weight, experts, capacity)
    rows_back, gate_low, up_low, active, weighted, share = expert_layer(
        owner, h_rows, gains, row_mask, back, gate_weight, up_weight, experts
    )
    came_back = exchange(rows_back)
    grads, tick = expert_weights(h_rows, rows_c, gate_low, up_low, weighted)
    grads = lax.psum(grads, "fsdp")
    gate_sum, up_sum, down_sum = widen(grads)
    sent, tick = expert_outputs(active, share, down_weight, owners, after=(tick,))

    middle_grad, middle_low, extra = router_backward(
        came_back, turn, middle, probs, mask, gains, upstream, hidden, experts, after=(tick,)
    )
    da_came, da_other = gather_fsdp(middle_low, "row_middle")
    out_rows = exchange(sent)
    layer_out, _ = layer_output(out_rows, turn, middle)
    first, dh_keep, dh_give = attention_backward(
        me,
        middle_low,
        da_came,
        da_other,
        heads,
        output_weight,
        cosine,
        sine,
        start,
        h1,
        pre,
        mixed,
        inverse,
        turned,
        extra,
        experts,
        q_heads,
    )
    dh_total, *dh_sends = pair_sum(dh_keep, send(dh_give, "fsdp", 1))
    dh_came = along_z(dh_sends)
    tokens_grad, tick = input_grad(dh_total, dh_came, own, gains, middle_grad, experts)
    first = passed(first, after=(out_rows, grads, dh_total))
    parted, rest = shares_sum(exchange(first), after=tuple(dh_came))
    parted = lax.all_to_all(parted, "fsdp", 0, 0, tiled=True)
    pieces = exchange(whole_pieces(parted, rest, after=(tick,)))
    query_sum, key_sum, value_sum, output_sum, one_sum, two_sum, *gain_sums, router_sum = final_grads(
        pieces, query_weight, key_weight, value_weight, first_gain[None], experts
    )
    return (
        layer_out[None],
        tokens_grad[None],
        one_sum[0],
        query_sum,
        key_sum,
        value_sum,
        output_sum,
        gain_sums[0][0],
        gain_sums[1][0],
        two_sum[0],
        router_sum.T,
        gate_sum,
        up_sum,
        down_sum,
    )


def solution(mesh):
    whole = P("expert", "fsdp", None)
    rows = P("fsdp", None)
    vector = P("fsdp")
    owned = P("expert", None, None)
    return jax.shard_map(
        shards,
        mesh=mesh,
        in_specs=(
            whole,
            P("expert", None),
            whole,
            vector,
            rows,
            rows,
            rows,
            rows,
            vector,
            vector,
            vector,
            rows,
            owned,
            owned,
            owned,
            whole,
        ),
        out_specs=(
            whole,
            whole,
            vector,
            rows,
            rows,
            rows,
            rows,
            vector,
            vector,
            vector,
            rows,
            owned,
            owned,
            owned,
        ),
        check_vma=False,
    )
```

```python
import functools

import jax
import jax.numpy as jnp
from jax import lax
from jax.experimental import pallas as pl
from jax.experimental.pallas import tpu as pltpu
from jax.sharding import PartitionSpec as P

EPSILON = 1e-06
ROPE_BASE = 10000.0
HEAD = 64
TILE = 256
F32 = jnp.float32
BF16 = jnp.bfloat16
VMEM = pl.BlockSpec(memory_space=pltpu.VMEM)
SMEM = pl.BlockSpec(memory_space=pltpu.SMEM)
ANY = pl.BlockSpec(memory_space=pl.ANY)
HBM = pl.BlockSpec(memory_space=pltpu.HBM)


def dot(left, right, dims=((1,), (0,))):
    return lax.dot_general(left, right, (dims, ((), ())), preferred_element_type=F32)


def shape(extent, dtype):
    return jax.ShapeDtypeStruct(extent, dtype)


def kernel_call(
    body, name, micros, operands, results, smem=0, hbm=(), out_hbm=(), after=(), scratch=(), held=(), late=(), stored=(), mib=63
):
    held = tuple(held) + tuple(late)
    n, a, r, s = len(operands), len(after), len(results), len(scratch)
    specs = [SMEM if i < smem else HBM if i in held or i in hbm else VMEM for i in range(n)]
    out_specs = [HBM if i in stored or i in out_hbm else VMEM for i in range(r)]
    staged = [pltpu.VMEM(operands[i].shape, operands[i].dtype) for i in held]
    staged += [pltpu.VMEM(*results[i]) for i in stored]
    sems = [pltpu.SemaphoreType.DMA((max(len(held), 1),)), pltpu.SemaphoreType.DMA((max(len(stored), 1),))]

    def wrapped(*refs):
        ins, outs = list(refs[:n]), list(refs[n + a : n + a + r])
        own = refs[n + a + r : n + a + r + s]
        stages, (load_sem, store_sem) = refs[n + a + r + s : -2], refs[-2:]
        loads, stores, begun = {}, {}, []
        for k, i in enumerate(held):
            loads[i] = pltpu.make_async_copy(ins[i], stages[k], load_sem.at[k])
            loads[i].start()
            ins[i] = stages[k]
        for k, i in enumerate(stored):
            stores[i] = pltpu.make_async_copy(stages[len(held) + k], outs[i], store_sem.at[k])
            outs[i] = stages[len(held) + k]
        for i in held:
            if i not in late:
                loads[i].wait()

        def store(*which):
            for i in which:
                stores[i].start()
                begun.append(i)

        extra = {}
        if late:
            extra["wait"] = lambda i: loads[i].wait()
        if stored:
            extra["store"] = store
        body(*ins, *outs, *own, **extra)
        store(*[i for i in stored if i not in begun])
        for i in stored:
            stores[i].wait()

    return pl.pallas_call(
        wrapped,
        out_shape=[shape(*result) for result in results],
        in_specs=specs + [ANY] * a,
        out_specs=out_specs,
        scratch_shapes=list(scratch) + staged + sems,
        compiler_params=pltpu.CompilerParams(vmem_limit_bytes=mib * 1024 * 1024),
        cost_estimate=pl.CostEstimate(flops=0, bytes_accessed=int(micros * 3.6e6), transcendentals=0),
        name=name,
    )(*operands, *after)


def move_call(moves, name, micros, operands, results, after=(), mib=10):
    def body(*refs):
        for source, target in moves(*refs):
            target[...] = source[...]

    return kernel_call(body, name, micros, operands, results, after=after, mib=mib)


def lane_blocks(value):
    return jnp.concatenate([value[:, i : i + 128] for i in range(0, value.shape[1], 128)], axis=0)


def joined_lanes(value, count):
    rows = value.shape[0] // count
    return jnp.concatenate([value[i * rows : (i + 1) * rows] for i in range(count)], axis=1)


def softmax_rows(logits):
    powers = jnp.exp(logits - jnp.max(logits, axis=0, keepdims=True))
    return powers / jnp.sum(powers, axis=0, keepdims=True)


def head_forward(pre, gain, cosine, sine):
    scale = lax.rsqrt(jnp.mean(pre * pre, axis=0, keepdims=True) + EPSILON)
    normed = pre * scale
    scaled = normed * gain
    a, b = scaled[: HEAD // 2], scaled[HEAD // 2 :]
    turned = jnp.concatenate([a * cosine - b * sine, b * cosine + a * sine], axis=0)
    return turned, normed, scale


def head_backward(grad, normed, scale, gain, cosine, sine):
    a, b = grad[: HEAD // 2], grad[HEAD // 2 :]
    unturned = jnp.concatenate([a * cosine + b * sine, b * cosine - a * sine], axis=0)
    gain_grad = jnp.sum(unturned * normed, axis=1, keepdims=True)
    inner = unturned * gain
    pre_grad = scale * (inner - normed * jnp.mean(inner * normed, axis=0, keepdims=True))
    return pre_grad, gain_grad


def slots_kernel(mask_ref, deal_ref, turn_ref, whole_ref, *, capacity, store):
    experts, rows = mask_ref.shape
    mask = mask_ref[...]
    ranks = dot(mask.astype(BF16), earlier(rows))
    slot = lax.broadcasted_iota(jnp.int32, (capacity, rows), 0).astype(F32) + 1.0
    for expert in range(experts):
        one = slice(expert, expert + 1)
        whole_ref[expert * capacity : (expert + 1) * capacity] = jnp.where(
            (ranks[one] == slot) & (mask[one] > 0.5), 1.0, 0.0
        )
    deal_ref[...] = whole_ref[...].astype(BF16)
    store(0)
    for part in range(0, experts * capacity, 128):
        turn_ref[:, part : part + 128] = whole_ref[part : part + 128].T.astype(BF16)


def slot_tables(mask, capacity):
    experts, rows = mask.shape
    slots = experts * capacity
    return kernel_call(
        functools.partial(slots_kernel, capacity=capacity),
        "slot_tables",
        2.0,
        [mask],
        [((slots, rows), BF16), ((rows, slots), BF16)],
        scratch=[pltpu.VMEM((slots, rows), F32)],
        stored=(0, 1),
    )


def earlier(rows):
    return (
        lax.broadcasted_iota(jnp.int32, (rows, rows), 0)
        <= lax.broadcasted_iota(jnp.int32, (rows, rows), 1)
    ).astype(BF16)


def pack_kernel(
    me_ref, x_ref, wq_ref, wk_ref, wv_ref, router_ref, one_ref, two_ref, qg_ref, kg_ref, routes_ref, c_ref, *outs, wait, store
):
    own_ref, sends, dressed_ref, mask_ref, other_ref, parts_ref = outs[0], outs[1:4], *outs[4:]
    experts, rows = router_ref.shape
    wide = wq_ref.shape[1] // 8
    narrow = wk_ref.shape[1] // 8
    count = qg_ref.shape[1]
    heads = jnp.concatenate([qg_ref[...], kg_ref[...]], axis=0).astype(F32)
    heads = jnp.concatenate([heads, jnp.zeros((2, 128 - count), F32)], axis=1)
    heads = jnp.concatenate([heads, jnp.zeros((126, 128), F32)], axis=0).T[:count]
    small = jnp.concatenate(
        [
            router_ref[...].astype(F32),
            one_ref[...].astype(F32),
            two_ref[...].astype(F32),
            jnp.zeros((6, 128), F32),
            heads,
        ],
        axis=0,
    ).astype(BF16)
    for part in range(8):
        parts_ref[part, :wide] = wq_ref[:, part * wide : (part + 1) * wide].astype(F32).T.astype(BF16)
        parts_ref[part, wide + 2 * narrow :] = small
    for pair in range(4):
        span = slice(pair * 128, (pair + 1) * 128)
        for ref, place in ((wk_ref, wide), (wv_ref, wide + narrow)):
            turned = ref[:, span].astype(F32).T.astype(BF16)
            parts_ref[2 * pair, place : place + narrow] = turned[:narrow]
            parts_ref[2 * pair + 1, place : place + narrow] = turned[narrow:]
    me = me_ref[0]
    tall = parts_ref.shape[1]
    blocks = lane_blocks(x_ref[...])
    base = blocks.shape[0]
    own_ref[...] = parts_ref[me]
    other_ref[...] = parts_ref[me ^ 1]
    for flip in range(1, 4):
        sends[flip - 1][:base] = blocks
        sends[flip - 1][base : base + tall] = parts_ref[me ^ (2 * flip)]
        sends[flip - 1][base + tall :] = parts_ref[me ^ (2 * flip + 1)]
    store(1, 2, 3, 6, 0)
    wait(10)
    wait(11)
    width = c_ref.shape[1]
    subs = lax.broadcasted_iota(jnp.int32, (128, rows), 0)
    routed = jnp.zeros((128, rows), F32)
    for route in range(routes_ref.shape[0]):
        routed = routed + jnp.where(routes_ref[route : route + 1] == subs, 1.0, 0.0)
    dressed_ref[:, :width] = c_ref[...]
    dressed_ref[:, width:] = routed.T.astype(BF16)
    mask_ref[...] = routed[:experts]


def pack_weights(me, x, wq, wk, wv, router, one, two, qg, kg, routes, c):
    experts = router.shape[0]
    tall = (wq.shape[1] + wk.shape[1] + wv.shape[1]) // 8 + experts + 16
    rows, width = x.shape
    base = rows * 8
    own, first, second, third, dressed, mask, other = kernel_call(
        pack_kernel,
        "pack_weights",
        2.5,
        [me, x, wq, wk, wv, router, one, two, qg, kg, routes, c],
        [((tall, 128), BF16)]
        + [((base + 2 * tall, 128), BF16)] * 3
        + [((rows, width + 128), BF16), ((experts, rows), F32), ((tall, 128), BF16)],
        smem=1,
        scratch=[pltpu.VMEM((8, tall, 128), BF16)],
        held=range(1, 10),
        late=(10, 11),
        stored=(0, 1, 2, 3, 4, 5, 6),
    )
    return (own, other), [first, second, third], dressed, mask


def relay(came, base, after):
    tall = (came[0].shape[0] - base) // 2

    def moves(*refs):
        pairs = []
        for flip, ref in enumerate(refs[:3]):
            pairs.append((ref.at[:base], refs[3].at[flip, :base]))
            pairs.append((ref.at[base + tall :], refs[3].at[flip, base:]))
        return pairs

    return move_call(moves, "relay", 1.5, came, [((3, base + tall, 128), BF16)], after)[0]


def forward_kernel(me_ref, x_ref, own_ref, *refs, experts, q_heads, store):
    came, other_x, other_w, other_ref = refs[:3], refs[3], refs[4], refs[5]
    cos_ref, sin_ref, start_ref = refs[6:9]
    h1_ref, pre_ref, keep_ref, give_ref, inverse_ref, gains_ref, heads_ref, turned_ref, out_ref = refs[-9:]
    rows, width = x_ref.shape
    q_columns = q_heads * HEAD
    columns = q_columns + 2 * HEAD
    total = rows * 8
    tall = own_ref.shape[0]
    base = 8 * rows
    me = me_ref[0]
    for slot in range(8):
        flip = slot // 2
        if slot % 2:
            piece = other_ref[flip - 1, base:] if flip else other_w[...]
        elif flip:
            piece = came[flip - 1][base : base + tall]
        else:
            piece = own_ref[...]
        span = pl.ds(pl.multiple_of((me ^ slot) * rows, rows), rows)
        turned_ref[:, span] = piece[:columns]
        small = piece[columns:].astype(F32)
        gains_ref[:, span] = small[: experts + 8]
        heads_ref[pl.ds(pl.multiple_of((me ^ slot) * 8, 8), 8)] = small[experts + 8 :]
    gain_one = gains_ref[experts : experts + 1]
    for slot in range(8):
        flip = slot // 2
        if slot % 2:
            x = joined_lanes(other_ref[flip - 1, :base], 8) if flip else other_x[...]
        elif flip:
            x = joined_lanes(came[flip - 1][:base], 8)
        else:
            x = x_ref[...]
        x = x.astype(F32)
        scale = lax.rsqrt(jnp.mean(x * x, axis=1, keepdims=True) + EPSILON)
        h1_ref[slot] = (x * scale * gain_one).astype(BF16)
    store(0, 6, 7)
    for slot in range(8):
        block = dot(turned_ref[...], h1_ref[slot], ((1,), (1,)))
        place = pl.multiple_of((me ^ slot) * rows, rows)
        pre_ref[:, pl.ds(place, rows)] = block
    store(1)
    cosine, sine = cos_ref[...], sin_ref[...]
    gain_query, gain_key = heads_ref[:, :1], heads_ref[:, 1:2]
    key = head_forward(pre_ref[q_columns : q_columns + HEAD], gain_key, cosine, sine)[0]
    key = key.T.astype(BF16)
    value = pre_ref[q_columns + HEAD :].astype(BF16)
    inverse_ref[...] = jnp.zeros(inverse_ref.shape, F32)
    for head in range(q_heads):
        query = head_forward(pre_ref[head * HEAD : (head + 1) * HEAD], gain_query, cosine, sine)[0]
        query = query.astype(BF16) * jnp.array(HEAD ** (-0.5), BF16)
        for tile in range(total // TILE):
            low, high = tile * TILE, (tile + 1) * TILE
            scores = dot(key[:high], query[:, low:high])
            u = lax.broadcasted_iota(jnp.int32, (high, TILE), 0)
            t = lax.broadcasted_iota(jnp.int32, (high, TILE), 1) + low
            allowed = (u >= start_ref[:, low:high]) & (u <= t)
            powers = jnp.where(allowed, jnp.exp(scores), 0.0)
            inverse = 1.0 / jnp.sum(powers, axis=0, keepdims=True)
            probs = (powers * inverse).astype(BF16)
            mixed = dot(value[:, :high], probs).astype(BF16)
            inverse_ref[head : head + 1, low:high] = inverse
            for part in range(TILE // rows):
                out_ref[low // rows + part, head * HEAD : (head + 1) * HEAD] = mixed[
                    :, part * rows : (part + 1) * rows
                ]
    for slot in range(8):
        (give_ref if slot % 2 else keep_ref)[slot // 2] = out_ref[me ^ slot]


def attention_forward(me, x, own, came, other, cosine, sine, start, experts, q_heads, after=()):
    rows, width = x.shape
    total = 8 * rows
    columns = (q_heads + 2) * HEAD
    q_columns = q_heads * HEAD
    return kernel_call(
        functools.partial(forward_kernel, experts=experts, q_heads=q_heads),
        "attention_forward",
        7.0,
        [me, x, own, *came, *other, cosine, sine, start],
        [
            ((8, rows, width), BF16),
            ((columns, total), F32),
            ((4, q_columns, rows), BF16),
            ((4, q_columns, rows), BF16),
            ((8, total), F32),
            ((experts + 8, width), F32),
            ((HEAD, 128), F32),
            ((columns, width), BF16),
            ((8, q_columns, rows), BF16),
        ],
        smem=1,
        after=after,
        held=(1,),
        stored=(0, 1, 4, 6, 7, 8),
    )


def merge(keep, came, wo, wo_came):
    def moves(keep_ref, came_ref, *refs):
        weights, outs, stacked = refs[:4], refs[4:7], refs[7]
        pairs = [(weight, stacked.at[i]) for i, weight in enumerate(weights)]
        for flip in range(1, 4):
            pairs.append((keep_ref.at[flip], outs[flip - 1].at[0]))
            pairs.append((came_ref.at[flip], outs[flip - 1].at[1]))
        return pairs

    extent = ((2,) + keep.shape[1:], BF16)
    results = [extent] * 3 + [((4,) + wo.shape, BF16)]
    *sends, stacked = move_call(moves, "merge", 1.0, [keep, came, wo, *wo_came], results)
    return sends, stacked


def middle_kernel(x_ref, keep_ref, other_ref, *refs, experts, wait, store):
    came, wo_ref, wo_came, wo_other_ref, gains_ref, deal_ref = refs[:3], refs[3], refs[4:7], refs[7], refs[8], refs[9]
    middle_ref, probs_ref, hidden_ref, sent_ref, mixed_ref, whole_ref, out_ref, out_sem = refs[10:]
    rows, width = x_ref.shape
    for slot in range(8):
        flip, core = slot // 2, slot % 2
        if flip:
            piece = came[flip - 1][core]
        else:
            piece = (other_ref if core else keep_ref)[0]
        span = slice(slot * 128, (slot + 1) * 128)
        mixed_ref[:, span] = piece.astype(F32).T.astype(BF16)
    for i in (6, 7, 8, 9, 10):
        wait(i)
    for slot in range(8):
        flip = slot // 2
        span = slice(slot * 128, (slot + 1) * 128)
        if slot % 2:
            whole_ref[span] = wo_other_ref[flip]
        else:
            whole_ref[span] = (wo_came[flip - 1] if flip else wo_ref)[...]
    wait(0)
    middle = x_ref[...].astype(F32) + dot(mixed_ref[...], whole_ref[...])
    middle_ref[...] = middle
    scale = lax.rsqrt(jnp.mean(middle * middle, axis=1, keepdims=True) + EPSILON)
    hidden = (middle * scale * gains_ref[experts + 1 : experts + 2]).astype(BF16)
    hidden_ref[...] = hidden
    probs_ref[...] = softmax_rows(dot(gains_ref[:experts].astype(BF16), hidden, ((1,), (1,))))
    store(0, 2)
    owners, per_owner, capacity, _ = sent_ref.shape
    group = owners // 4
    size = group * per_owner * capacity
    copies = []
    wait(12)
    for part in range(4):
        taken = dot(deal_ref[part * size : (part + 1) * size], hidden).astype(BF16)
        blocks = slice(group * part, group * (part + 1))
        out_ref[blocks] = taken.reshape(group, per_owner, capacity, width)
        copies.append(pltpu.make_async_copy(out_ref.at[blocks], sent_ref.at[blocks], out_sem.at[part]))
        copies[-1].start()
    for copy in copies:
        copy.wait()


def middle_layer(x, keep, other, came, wo, wo_came, wo_other, gains, deal, experts, owners):
    rows, width = x.shape
    per_owner = experts // owners
    capacity = deal.shape[0] // experts
    sent = ((owners, per_owner, capacity, width), BF16)
    return kernel_call(
        functools.partial(middle_kernel, experts=experts),
        "middle_layer",
        3.0,
        [x, keep, other, *came, wo, *wo_came, wo_other, gains, deal],
        [((rows, width), F32), ((experts, rows), F32), ((rows, width), BF16), sent],
        out_hbm=(3,),
        scratch=[
            pltpu.VMEM((rows, width), BF16),
            pltpu.VMEM((width, width), BF16),
            pltpu.VMEM(*sent),
            pltpu.SemaphoreType.DMA((4,)),
        ],
        late=(6, 7, 8, 9, 10, 0, 12),
        stored=(0, 2),
    )


def row(pieces, name):
    def moves(*refs):
        return [(ref, refs[-1].at[i]) for i, ref in enumerate(refs[:-1])]

    return move_call(moves, name, 1.0, pieces, [((len(pieces),) + pieces[0].shape, BF16)])[0]


def backward_kernel(me_ref, own_da_ref, *refs, experts, q_heads, wait):
    came, others = refs[:3], refs[3:7]
    heads_ref, wo_ref, cos_ref, sin_ref, start_ref = refs[7:12]
    h1_ref, pre_ref, mixed_ref, inverse_ref, turned_ref, extra_ref = refs[12:18]
    first_ref, keep_ref, send_ref = refs[-10:-7]
    da_ref, mixed_grad_ref, dkey_ref, dvalue_ref, low_ref, out_slots_ref, grad_ref = refs[-7:]
    rows, width = own_da_ref.shape
    q_columns = q_heads * HEAD
    columns = q_columns + 2 * HEAD
    total = rows * 8
    me = me_ref[0]
    for slot in range(8):
        flip, core = slot // 2, slot % 2
        if core:
            piece = others[flip][...]
        else:
            piece = (came[flip - 1] if flip else own_da_ref)[...]
        span = slice(slot * rows, (slot + 1) * rows)
        da_ref[span] = piece
        place = pl.multiple_of((me ^ slot) * rows, rows)
        mixed_grad_ref[:, pl.ds(place, rows)] = dot(wo_ref[...], piece, ((1,), (1,))).astype(BF16)
    wait(16)
    for slot in range(8):
        out_slots_ref[:, slot * rows : (slot + 1) * rows] = mixed_ref[me ^ slot]
    wo_grad = dot(out_slots_ref[...], da_ref[...]).astype(BF16)
    wo_grad = lane_blocks(wo_grad)
    wait(15)
    wait(17)
    gain_query, gain_key = heads_ref[:, :1], heads_ref[:, 1:2]
    cosine, sine = cos_ref[...], sin_ref[...]
    key_turned, key_normed, key_scale = head_forward(
        pre_ref[q_columns : q_columns + HEAD], gain_key, cosine, sine
    )
    key_low = key_turned.astype(BF16)
    key = key_turned.T.astype(BF16)
    value = pre_ref[q_columns + HEAD :].T.astype(BF16)
    dkey_ref[...] = jnp.zeros(dkey_ref.shape, F32)
    dvalue_ref[...] = jnp.zeros(dvalue_ref.shape, F32)
    gain_query_grad = jnp.zeros((HEAD, 1), F32)
    pieces = []
    for head in range(q_heads):
        span = slice(head * HEAD, (head + 1) * HEAD)
        turned, normed, scale = head_forward(pre_ref[span], gain_query, cosine, sine)
        query = turned.astype(BF16) * jnp.array(HEAD ** (-0.5), BF16)
        grads = []
        for tile in range(total // TILE):
            low, high = tile * TILE, (tile + 1) * TILE
            part = query[:, low:high]
            mixed_grad = mixed_grad_ref[span, low:high]
            scores = dot(key[:high], part)
            u = lax.broadcasted_iota(jnp.int32, (high, TILE), 0)
            t = lax.broadcasted_iota(jnp.int32, (high, TILE), 1) + low
            allowed = (u >= start_ref[:, low:high]) & (u <= t)
            probs = jnp.where(allowed, jnp.exp(scores) * inverse_ref[head : head + 1, low:high], 0.0)
            attend = dot(value[:high], mixed_grad)
            delta = jnp.sum(probs * attend, axis=0, keepdims=True)
            score_low = (probs * (attend - delta)).astype(BF16)
            grads.append(dot(key_low[:, :high], score_low))
            dkey_ref[:, :high] += dot(part, score_low, ((1,), (1,)))
            dvalue_ref[:, :high] += dot(mixed_grad, probs.astype(BF16), ((1,), (1,)))
        query_grad = jnp.concatenate(grads, axis=1) * HEAD ** (-0.5)
        pre_grad, gain_grad = head_backward(query_grad, normed, scale, gain_query, cosine, sine)
        gain_query_grad += gain_grad
        pieces.append(pre_grad)
    pre_grad, gain_key_grad = head_backward(
        dkey_ref[...], key_normed, key_scale, gain_key, cosine, sine
    )
    pieces += [pre_grad, dvalue_ref[...]]
    pre_grad = jnp.concatenate(pieces, axis=0)
    low_ref[...] = pre_grad.astype(BF16)
    slots_grad = []
    for slot in range(8):
        place = pl.multiple_of((me ^ slot) * rows, rows)
        slots_grad.append(low_ref[:, pl.ds(place, rows)])
    slots_grad = jnp.concatenate(slots_grad, axis=1)
    wait(14)
    wait(18)
    grad_ref[:columns] = dot(slots_grad, h1_ref[...].reshape(total, width))
    extra = extra_ref[...]
    lane = lax.broadcasted_iota(jnp.int32, (HEAD, 128), 1)
    gains = jnp.where(lane == 0, gain_query_grad, jnp.where(lane == 1, gain_key_grad, 0.0))
    gains = gains.T[:2]
    step = HEAD // 8
    grad_ref[columns:] = jnp.zeros((64, width), F32)
    grad_ref[columns : columns + experts + 1] = extra[: experts + 1]
    for part in range(8):
        grad_ref[columns + experts + 1 : columns + experts + 3, part * rows : part * rows + step] = gains[
            :, part * step : (part + 1) * step
        ]
    for piece in range(16):
        spare = []
        place = columns + piece * SPARE
        for part in range(8):
            span = slice(part * rows, (part + 1) * rows)
            block = grad_ref[piece * PIECE : (piece + 1) * PIECE, span]
            first_ref[piece, part * PIECE : (part + 1) * PIECE] = block.astype(BF16)
            spare.append(grad_ref[place : place + SPARE, span])
        spare.append(jnp.zeros((2 * PIECE - 8 * SPARE, 128), F32))
        first_ref[piece, 8 * PIECE : 10 * PIECE] = jnp.concatenate(spare, axis=0).astype(BF16)
        first_ref[piece, 10 * PIECE :] = wo_grad[piece * SLICE : (piece + 1) * SLICE]
    turned = turned_ref[...]
    for slot in range(8):
        low_rows_slot = slots_grad[:, slot * rows : (slot + 1) * rows].astype(F32).T.astype(BF16)
        part = dot(low_rows_slot, turned)
        if slot % 2:
            send_ref[slot // 2] = part.astype(BF16)
        else:
            keep_ref[slot // 2] = part


def attention_backward(
    me, da, came, other, heads, wo, cosine, sine, start, h1, pre, mixed, inverse, turned, extra, experts, q_heads, after=()
):
    rows, width = da.shape
    total = 8 * rows
    columns = pre.shape[0]
    q_columns = q_heads * HEAD
    return kernel_call(
        functools.partial(backward_kernel, experts=experts, q_heads=q_heads),
        "attention_backward",
        12,
        [me, da, *came, *other, heads, wo, cosine, sine, start, h1, pre, mixed, inverse, turned, extra],
        [
            ((16, 10 * PIECE + SLICE, 128), BF16),
            ((4, rows, width), F32),
            ((4, rows, width), BF16),
        ],
        smem=1,
        after=after,
        held=(9, 10),
        late=(14, 15, 16, 17, 18),
        scratch=[
            pltpu.VMEM((total, width), BF16),
            pltpu.VMEM((q_columns, total), BF16),
            pltpu.VMEM((HEAD, total), F32),
            pltpu.VMEM((HEAD, total), F32),
            pltpu.VMEM((columns, total), BF16),
            pltpu.VMEM((q_columns, total), BF16),
            pltpu.VMEM((columns + 64, width), F32),
        ],
    )


def deal_kernel(owner_ref, c_ref, down_ref, rows_c, mask_ref, back_ref, c_scratch, sems, *, experts, capacity, wait, store):
    owner = owner_ref[0]
    per_owner, hidden, width = down_ref.shape
    rows = c_ref.shape[1]
    loads = [pltpu.make_async_copy(c_ref.at[i], c_scratch.at[i], sems.at[i]) for i in range(16)]
    for load in loads:
        load.start()
    lanes = lax.broadcasted_iota(jnp.int32, (experts, 128), 1)
    subs = lax.broadcasted_iota(jnp.int32, (experts, 128), 0)
    eye = (lanes == subs).astype(BF16)
    before = earlier(rows)
    mine_of = lax.broadcasted_iota(jnp.int32, (experts, rows), 0) - owner * per_owner
    slot = lax.broadcasted_iota(jnp.int32, (capacity, rows), 0).astype(F32) + 1.0
    for block in range(16):
        loads[block].wait()
        c = c_scratch[block]
        mask = dot(eye, c[:, width:], ((1,), (1,)))
        ranks = dot(mask.astype(BF16), before)
        deals = []
        for k in range(per_owner):
            mine = mine_of == k
            hit = jnp.sum(jnp.where(mine, mask, 0.0), axis=0, keepdims=True)
            rank = jnp.sum(jnp.where(mine, ranks, 0.0), axis=0, keepdims=True)
            deals.append(jnp.where((rank == slot) & (hit > 0.5), 1.0, 0.0))
        taken = dot(jnp.concatenate(deals, axis=0).astype(BF16), c).astype(BF16)
        span = slice(block * capacity, (block + 1) * capacity)
        for k in range(per_owner):
            spot = slice(k * capacity, (k + 1) * capacity)
            rows_c[k, span] = taken[spot, :width]
            mask_ref[k, span] = taken[spot, width:]
    store(0, 1)
    wait(2)
    for k in range(per_owner):
        for tile in range(16 * capacity // TILE):
            span = slice(tile * TILE, (tile + 1) * TILE)
            back_ref[k, span] = dot(rows_c[k, span], down_ref[k], ((1,), (1,)))


def deal_rows(owner, c, down, experts, capacity):
    per_owner, hidden, width = down.shape
    count = 16 * capacity
    return kernel_call(
        functools.partial(deal_kernel, experts=experts, capacity=capacity),
        "deal_rows",
        12.0,
        [owner, c, down],
        [
            ((per_owner, count, width), BF16),
            ((per_owner, count, 128), BF16),
            ((per_owner, count, hidden), F32),
        ],
        smem=1,
        hbm=(1,),
        scratch=[pltpu.VMEM(c.shape, BF16), pltpu.SemaphoreType.DMA((16,))],
        late=(2,),
        stored=(0, 1, 2),
    )


def expert_kernel(
    owner_ref,
    h_hbm,
    gains_ref,
    mask_ref,
    back_hbm,
    gate_hbm,
    up_hbm,
    rows_hbm,
    gate_out,
    up_out,
    active_out,
    weighted_out,
    share_ref,
    h_ref,
    back_in,
    gate_ref,
    up_ref,
    rows_back,
    gate_sum,
    up_sum,
    logit_sum,
    spread_ref,
    load_sem,
    store_sem,
    *,
    experts,
    store,
):
    owners, per_owner, capacity, width = h_hbm.shape
    group = 8
    parts = owners // group
    size = group * capacity
    loads = {}
    for k in range(per_owner):
        for part in range(parts):
            blocks = slice(part * group, (part + 1) * group)
            spot = (k * parts + part) * 4
            loads[k, part] = [
                pltpu.make_async_copy(h_hbm.at[blocks, k], h_ref.at[blocks, k], load_sem.at[spot]),
                pltpu.make_async_copy(
                    back_hbm.at[k, part * size : (part + 1) * size],
                    back_in.at[k, part * size : (part + 1) * size],
                    load_sem.at[spot + 1],
                ),
            ]
            if part == 0:
                loads[k, part] += [
                    pltpu.make_async_copy(gate_hbm.at[k], gate_ref.at[k], load_sem.at[spot + 2]),
                    pltpu.make_async_copy(up_hbm.at[k], up_ref.at[k], load_sem.at[spot + 3]),
                ]
            for load in loads[k, part]:
                load.start()
    owner = owner_ref[0]
    router = jnp.concatenate([gains_ref[:experts], jnp.zeros((128 - experts, width), F32)], axis=0)
    router = router.astype(BF16)
    lane = lax.broadcasted_iota(jnp.int32, (size, 128), 1)
    copies = []
    chunk = capacity
    lane = lane[:chunk]
    order = [(k, part) for k in range(per_owner) for part in range(parts)]

    def begin(i):
        k, part = order[i]
        blocks = slice(part * group, (part + 1) * group)
        for load in loads[k, part]:
            load.wait()
        h = h_ref[blocks, k].reshape(size, width)
        gate_sum[i % 2] = dot(h, gate_ref[k])
        up_sum[i % 2] = dot(h, up_ref[k])
        logit_sum[i % 2] = dot(h, router, ((1,), (1,)))

    begin(0)
    for i, (k, part) in enumerate(order):
        if i + 1 < len(order):
            begin(i + 1)
        place = owner * per_owner + k
        blocks = slice(part * group, (part + 1) * group)
        span = slice(part * size, (part + 1) * size)
        for spot in range(0, size, chunk):
            here = slice(part * size + spot, part * size + spot + chunk)
            near = slice(spot, spot + chunk)
            logits = logit_sum[i % 2, near]
            chosen = mask_ref[k, here] > 0.5
            top = jnp.max(jnp.where(chosen, logits, -1e30), axis=1, keepdims=True)
            powers = jnp.where(chosen, jnp.exp(logits - top), 0.0)
            total = jnp.sum(powers, axis=1, keepdims=True)
            share = jnp.sum(jnp.where(lane == place, powers, 0.0), axis=1, keepdims=True)
            share = share / jnp.where(total > 0.0, total, 1.0)
            share_ref[k, here] = jnp.broadcast_to(share, (chunk, 128))
            gate, up, back = gate_sum[i % 2, near], up_sum[i % 2, near], back_in[k, here]
            sig = 1.0 / (1.0 + jnp.exp(-gate))
            silu = gate * sig
            active = silu * up
            active_low = active.astype(BF16)
            route_grad = jnp.sum(active_low.astype(F32) * back, axis=1, keepdims=True)
            grad = back * share
            gate_out[k, here] = (grad * up * (sig + silu * (1.0 - sig))).astype(BF16)
            up_out[k, here] = (grad * silu).astype(BF16)
            active_out[k, here] = active_low
            weighted_out[k, here] = (active * share).astype(BF16)
            high = route_grad.astype(BF16).astype(F32)
            spread_out = jnp.where(lane == place, high, 0.0)
            spread_out = jnp.where(lane == place + experts, route_grad - high, spread_out)
            spread_ref[near] = spread_out.astype(BF16)
        rows = dot(gate_out[k, span], gate_ref[k], ((1,), (1,))) + dot(up_out[k, span], up_ref[k], ((1,), (1,)))
        rows_back[blocks, k, :, :width] = rows.astype(BF16).reshape(group, capacity, width)
        rows_back[blocks, k, :, width:] = spread_ref[...].reshape(group, capacity, 128)
        copies.append(
            pltpu.make_async_copy(rows_back.at[blocks, k], rows_hbm.at[blocks, k], store_sem.at[k * parts + part])
        )
        copies[-1].start()
    store(1, 2, 3, 4, 5)
    for copy in copies:
        copy.wait()


def expert_layer(owner, h, gains, mask, back, gate, up, experts):
    per_owner, width, hidden = gate.shape
    owners, _, capacity, _ = h.shape
    count = owners * capacity
    narrow = ((per_owner, count, hidden), BF16)
    rows_back = ((owners, per_owner, capacity, width + 128), BF16)
    pieces = per_owner * (owners // 8)
    return kernel_call(
        functools.partial(expert_kernel, experts=experts),
        "expert_layer",
        14.0,
        [owner, h, gains, mask, back, gate, up],
        [rows_back] + [narrow] * 4 + [((per_owner, count, 128), F32)],
        smem=1,
        hbm=(1, 4, 5, 6),
        out_hbm=(0,),
        scratch=[pltpu.VMEM(value.shape, value.dtype) for value in (h, back, gate, up)]
        + [pltpu.VMEM(*rows_back)]
        + [pltpu.VMEM((2, 8 * capacity, n), F32) for n in (hidden, hidden, 128)]
        + [pltpu.VMEM((8 * capacity, 128), BF16)]
        + [pltpu.SemaphoreType.DMA((4 * pieces,)), pltpu.SemaphoreType.DMA((pieces,))],
        stored=(1, 2, 3, 4, 5),
    )


def weights_kernel(
    h_hbm, rows_c, gate_low, up_low, weighted, out_hbm, tick_ref, h_ref, out_ref, load_sem, store_sem, *, wait
):
    tick_ref[...] = jnp.zeros(tick_ref.shape, F32)
    first = ((0,), (0,))
    owners, per_owner, capacity, width = h_hbm.shape
    hidden = gate_low.shape[2]
    half = width // 2
    loads = [
        pltpu.make_async_copy(h_hbm.at[:, k], h_ref.at[:, k], load_sem.at[k]) for k in range(per_owner)
    ]
    for load in loads:
        load.start()
    stores = []

    def keep(place):
        stores.append(pltpu.make_async_copy(out_ref.at[place], out_hbm.at[place], store_sem.at[place]))
        stores[-1].start()

    wait(2)
    for k in range(per_owner):
        loads[k].wait()
        rows_h = h_ref[:, k].reshape(owners * capacity, width)
        for place, low in ((k, gate_low), (per_owner + k, up_low)):
            if k == 0 and place:
                wait(3)
            total = dot(rows_h, low[k], first).astype(BF16)
            out_ref[place, :, :hidden] = total[:half]
            out_ref[place, :, hidden:] = total[half:]
            keep(place)
        if k == 0:
            wait(4)
            wait(1)
        place = 2 * per_owner + k
        out_ref[place] = dot(weighted[k], rows_c[k], first).astype(BF16)
        keep(place)
    for store in stores:
        store.wait()


def expert_weights(h, rows_c, gate_low, up_low, weighted):
    per_owner, count, width = rows_c.shape
    hidden = gate_low.shape[2]
    out = ((3 * per_owner, hidden, width), BF16)
    return kernel_call(
        weights_kernel,
        "expert_weights",
        0.1,
        [h, rows_c, gate_low, up_low, weighted],
        [out, ((8, 128), F32)],
        hbm=(0,),
        out_hbm=(0,),
        scratch=[
            pltpu.VMEM(h.shape, BF16),
            pltpu.VMEM(*out),
            pltpu.SemaphoreType.DMA((per_owner,)),
            pltpu.SemaphoreType.DMA((3 * per_owner,)),
        ],
        late=(2, 3, 4, 1),
    )


def widen_kernel(low_ref, gate_ref, up_ref, down_ref):
    step = pl.program_id(0)
    hidden = gate_ref.shape[2]
    value = low_ref[0].astype(F32)
    half = value.shape[0]
    for place, ref in ((0, gate_ref), (1, up_ref)):

        @pl.when(step // 2 == place)
        def _():
            ref[0, :half] = value[:, :hidden]
            ref[0, half:] = value[:, hidden:]

    @pl.when(step // 2 == 2)
    def _():
        down_ref[0] = value


def widen(low):
    count, hidden, width = low.shape
    per_owner = count // 3

    def spot(place):
        return lambda i: (jnp.clip(i - place * per_owner, 0, per_owner - 1), 0, 0)

    return pl.pallas_call(
        widen_kernel,
        grid=(count,),
        out_shape=[shape((per_owner, width, hidden), F32)] * 2 + [shape((per_owner, hidden, width), F32)],
        in_specs=[pl.BlockSpec((1, hidden, width), lambda i: (i, 0, 0))],
        out_specs=[
            pl.BlockSpec((1, width, hidden), spot(0)),
            pl.BlockSpec((1, width, hidden), spot(1)),
            pl.BlockSpec((1, hidden, width), spot(2)),
        ],
        compiler_params=pltpu.CompilerParams(vmem_limit_bytes=63 * 1024 * 1024),
        cost_estimate=pl.CostEstimate(flops=0, bytes_accessed=24_000_000, transcendentals=0),
        name="widen",
    )(low)


def outputs_kernel(active, share, down_ref, sent_ref, tick_ref, out_ref, out_sem, *, wait):
    tick_ref[...] = jnp.zeros(tick_ref.shape, F32)
    per_owner, count, hidden = active.shape
    owners, _, capacity, width = sent_ref.shape
    group = 8
    size = group * capacity
    copies = []
    for i in range(3):
        wait(i)
    for k in range(per_owner):
        for part in range(owners // group):
            span = slice(part * size, (part + 1) * size)
            blocks = slice(part * group, (part + 1) * group)
            produced = dot(active[k, span], down_ref[k]).astype(BF16).astype(F32)
            produced = (produced * share[k, span, :1]).astype(BF16)
            out_ref[blocks, k] = produced.reshape(group, capacity, width)
            copies.append(
                pltpu.make_async_copy(
                    out_ref.at[blocks, k], sent_ref.at[blocks, k], out_sem.at[k * (owners // group) + part]
                )
            )
            copies[-1].start()
    for copy in copies:
        copy.wait()


def expert_outputs(active, share, down, owners, after=()):
    per_owner, count, hidden = active.shape
    width = down.shape[2]
    sent = ((owners, per_owner, count // owners, width), BF16)
    return kernel_call(
        outputs_kernel,
        "expert_outputs",
        0.1,
        [active, share, down],
        [sent, ((8, 128), F32)],
        out_hbm=(0,),
        after=after,
        scratch=[pltpu.VMEM(*sent), pltpu.SemaphoreType.DMA((per_owner * (owners // 8),))],
        late=(0, 1, 2),
    )


def combined(rows_hbm, rows_ref, sems, turn_ref, ready):
    owners, per_owner, capacity, wide = rows_hbm.shape
    group = owners // 4
    size = group * per_owner * capacity
    loads = []
    for part in range(4):
        blocks = slice(part * group, (part + 1) * group)
        loads.append(pltpu.make_async_copy(rows_hbm.at[blocks], rows_ref.at[blocks], sems.at[part]))
        loads[-1].start()
    ready()
    total = None
    for part in range(4):
        loads[part].wait()
        rows = rows_ref[part * group : (part + 1) * group].reshape(size, wide)
        one = dot(turn_ref[:, part * size : (part + 1) * size], rows)
        total = one if total is None else total + one
    return total


def output_kernel(rows_hbm, turn_ref, middle_ref, out_ref, tick_ref, rows_ref, sems, *, wait, store):
    tick_ref[...] = jnp.zeros(tick_ref.shape, F32)
    total = combined(rows_hbm, rows_ref, sems, turn_ref, lambda: wait(1))
    wait(2)
    out_ref[...] = (middle_ref[...] + total).astype(BF16)


def layer_output(rows, turn, middle):
    return kernel_call(
        output_kernel,
        "layer_output",
        3,
        [rows, turn, middle],
        [(middle.shape, BF16), ((8, 128), F32)],
        hbm=(0,),
        scratch=[pltpu.VMEM(rows.shape, BF16), pltpu.SemaphoreType.DMA((4,))],
        late=(1, 2),
        stored=(0,),
    )


def router_kernel(
    rows_hbm,
    turn_ref,
    middle_ref,
    probs_ref,
    mask_ref,
    gains_ref,
    c_ref,
    hidden_ref,
    grad_ref,
    send_ref,
    extra_ref,
    rows_ref,
    sems,
    *,
    experts,
    wait,
    store,
):
    rows, width = middle_ref.shape
    returned = combined(rows_hbm, rows_ref, sems, turn_ref, lambda: wait(1))
    for i in (2, 4, 6, 7):
        wait(i)
    tail = returned[:, width:].T
    route_grad = tail[:experts] + tail[experts : 2 * experts]
    mask = mask_ref[...]
    probs = probs_ref[...]
    picked = probs * mask
    picked_sum = jnp.sum(picked, axis=0, keepdims=True)
    share = picked / picked_sum
    picked_grad = (route_grad - jnp.sum(route_grad * share, axis=0, keepdims=True)) / picked_sum
    prob_grad = mask * picked_grad
    logit_grad = probs * (prob_grad - jnp.sum(probs * prob_grad, axis=0, keepdims=True))
    extra_ref[:experts] = dot(logit_grad.astype(BF16), hidden_ref[...])
    logit_rows = jnp.concatenate([logit_grad, jnp.zeros((128 - experts, rows), F32)], axis=0).T
    router = gains_ref[:experts].astype(BF16)
    hidden_grad = returned[:, :width] + dot(logit_rows[:, :experts].astype(BF16), router)
    middle = middle_ref[...]
    scale = lax.rsqrt(jnp.mean(middle * middle, axis=1, keepdims=True) + EPSILON)
    normed = middle * scale
    extra_ref[experts : experts + 8] = jnp.broadcast_to(
        jnp.sum(hidden_grad * normed, axis=0, keepdims=True), (8, width)
    )
    inner = hidden_grad * gains_ref[experts + 1 : experts + 2]
    grad = c_ref[...].astype(F32) + scale * (
        inner - normed * jnp.mean(inner * normed, axis=1, keepdims=True)
    )
    grad_ref[...] = grad
    send_ref[...] = grad.astype(BF16)


def router_backward(rows_back, turn, middle, probs, mask, gains, c, hidden, experts, after=()):
    rows, width = middle.shape
    return kernel_call(
        functools.partial(router_kernel, experts=experts),
        "router_backward",
        5,
        [rows_back, turn, middle, probs, mask, gains, c, hidden],
        [((rows, width), F32), ((rows, width), BF16), ((experts + 8, width), F32)],
        hbm=(0,),
        after=after,
        scratch=[pltpu.VMEM(rows_back.shape, BF16), pltpu.SemaphoreType.DMA((4,))],
        late=(1, 2, 4, 6, 7),
        stored=(0,),
    )


def pair_kernel(keep_ref, other_ref, total_ref, *sends):
    for flip in range(4):
        total = keep_ref[flip] + other_ref[flip].astype(F32)
        if flip:
            sends[flip - 1][...] = total.astype(BF16)
        else:
            total_ref[...] = total


def pair_sum(keep, other):
    rows, width = keep.shape[1:]
    return kernel_call(
        pair_kernel, "pair_sum", 1.2, [keep, other], [((rows, width), F32)] + [((rows, width), BF16)] * 3
    )


def input_kernel(total_ref, *refs, experts, store):
    came = refs[:3]
    x_ref, gains_ref, middle_grad_ref, out_ref, tick_ref = refs[3:]
    tick_ref[...] = jnp.zeros(tick_ref.shape, F32)
    total = total_ref[...]
    for piece in came:
        total = total + piece[...].astype(F32)
    x = x_ref[...].astype(F32)
    scale = lax.rsqrt(jnp.mean(x * x, axis=1, keepdims=True) + EPSILON)
    normed = x * scale
    inner = total * gains_ref[experts : experts + 1]
    out_ref[...] = middle_grad_ref[...] + scale * (
        inner - normed * jnp.mean(inner * normed, axis=1, keepdims=True)
    )


def input_grad(total, came, x, gains, middle_grad, experts):
    return kernel_call(
        functools.partial(input_kernel, experts=experts),
        "input_grad",
        2,
        [total, *came, x, gains, middle_grad],
        [(middle_grad.shape, F32), ((8, 128), F32)],
        held=(4, 6),
        stored=(0,),
    )


PIECE, SPARE, SLICE = 16, 3, 64


def passed(value, after):
    results = [(value.shape, value.dtype)]
    return move_call(lambda *refs: [refs], "passed", 0.5, [value], results, after, 63)[0]


def shares_kernel(pieces_ref, out_ref, rest_ref):
    total = pieces_ref[0].astype(F32)
    for i in range(1, pieces_ref.shape[0]):
        total = total + pieces_ref[i].astype(F32)
    base = 8 * PIECE
    fill = jnp.zeros((PIECE - SPARE, 128), F32)
    for part in range(8):
        out_ref[part, :PIECE] = total[part * PIECE : (part + 1) * PIECE].astype(BF16)
        spare = total[base + part * SPARE : base + (part + 1) * SPARE]
        out_ref[part, PIECE:] = jnp.concatenate([spare, fill], axis=0).astype(BF16)
    rest_ref[...] = total[base + 2 * PIECE :].astype(BF16)


def shares_sum(pieces, after=()):
    return kernel_call(
        shares_kernel,
        "shares_sum",
        0.1,
        [pieces],
        [((8, 2 * PIECE, 128), BF16), ((SLICE, 128), BF16)],
        after=after,
        mib=12,
    )


def whole_kernel(came_ref, rest_ref, out_ref):
    spare = came_ref[0, PIECE:].astype(F32)
    for i in range(1, 8):
        spare = spare + came_ref[i, PIECE:].astype(F32)
    rows = [came_ref[i, :PIECE] for i in range(8)] + [spare.astype(BF16), rest_ref[...]]
    rows = jnp.concatenate(rows, axis=0)
    for i in range(16):
        out_ref[i] = rows


def whole_pieces(came, rest, after=()):
    return kernel_call(
        whole_kernel,
        "whole_pieces",
        0.1,
        [came, rest],
        [((16, 9 * PIECE + SLICE, 128), BF16)],
        after=after,
        mib=12,
    )[0]


def final_kernel(pieces_ref, wq_ref, wk_ref, wv_ref, gain_ref, *outs, experts, wait, store):
    query_ref, key_ref, value_ref, output_ref, one_ref, two_ref, qg_ref, kg_ref, router_ref = outs
    rows = pieces_ref.shape[2]
    q_columns = query_ref.shape[1] // 8
    kv_columns = key_ref.shape[1] // 8
    sums = jnp.zeros((rows, 1), F32)
    base = 8 * PIECE
    for i in range(16):
        half = i % 2 * SLICE
        output_ref[half : half + SLICE, i // 2 * rows : (i // 2 + 1) * rows] = pieces_ref[
            i, base + PIECE :
        ].astype(F32)
    store(3)
    for i in (1, 2, 3, 4):
        wait(i)
    for pair in range(4):
        keys, values = [], []
        for source in (2 * pair, 2 * pair + 1):
            block = [pieces_ref[i, source * PIECE : (source + 1) * PIECE] for i in range(16)]
            turned = jnp.concatenate(block, axis=0).astype(F32).T
            span = slice(source * q_columns, (source + 1) * q_columns)
            query = turned[:, :q_columns]
            query_ref[:, span] = query
            sums = sums + jnp.sum(query * wq_ref[:, span].astype(F32), axis=1, keepdims=True)
            keys.append(turned[:, q_columns : q_columns + kv_columns])
            values.append(turned[:, q_columns + kv_columns :])
        span = slice(2 * pair * kv_columns, 2 * (pair + 1) * kv_columns)
        for parts, ref, weight in ((keys, key_ref, wk_ref), (values, value_ref, wv_ref)):
            both = jnp.concatenate(parts, axis=1)
            ref[:, span] = both
            sums = sums + jnp.sum(both * weight[:, span].astype(F32), axis=1, keepdims=True)
    store(0, 1, 2)
    spare = pieces_ref[:, base : base + PIECE].astype(F32)
    spare = jnp.concatenate([spare[i, :SPARE] for i in range(16)], axis=0)
    one_ref[...] = jnp.broadcast_to(sums, (rows, 128)).T[:1] / gain_ref[...].astype(F32)
    two_ref[...] = spare[experts : experts + 1]
    step = qg_ref.shape[1]
    qg_ref[...] = spare[experts + 1 : experts + 2, :step]
    kg_ref[...] = spare[experts + 2 : experts + 3, :step]
    router_ref[...] = spare[:experts]


def final_grads(pieces, wq, wk, wv, gain, experts):
    rows = pieces.shape[2]
    return kernel_call(
        functools.partial(final_kernel, experts=experts),
        "final_grads",
        0.2,
        [pieces, wq, wk, wv, gain],
        [
            (wq.shape, F32),
            (wk.shape, F32),
            (wv.shape, F32),
            ((rows, 8 * rows), F32),
            ((1, rows), F32),
            ((1, rows), F32),
            ((1, HEAD // 8), F32),
            ((1, HEAD // 8), F32),
            ((experts, rows), F32),
        ],
        late=(1, 2, 3, 4),
        stored=(0, 1, 2, 3),
    )


def send(values, axis, flip):
    count = lax.axis_size(axis)
    return lax.ppermute(values, axis, [(i, i ^ flip) for i in range(count)])


def along_z(values):
    if not isinstance(values, (list, tuple)):
        values = [values] * 3
    return [send(value, "fsdp", 2 * (i + 1)) for i, value in enumerate(values)]


def gather_fsdp(block):
    came = along_z(block)
    return came, [send(value, "fsdp", 1) for value in (block, *came)]


def exchange(rows):
    return lax.all_to_all(rows, "expert", 0, 0, tiled=True)


def shards(
    tokens,
    lengths,
    routes,
    first_gain,
    query_weight,
    key_weight,
    value_weight,
    output_weight,
    query_gain,
    key_gain,
    second_gain,
    router_weight,
    gate_weight,
    up_weight,
    down_weight,
    cotangent,
):
    own = tokens[0]
    upstream = cotangent[0]
    rows, width = own.shape
    fsdp = lax.axis_size("fsdp")
    owners = lax.axis_size("expert")
    me = lax.axis_index("fsdp").astype(jnp.int32).reshape(1)
    owner = lax.axis_index("expert").astype(jnp.int32).reshape(1)
    experts = router_weight.shape[1]
    capacity = 3 * rows * routes.shape[2] // (2 * experts)
    kv_columns = key_weight.shape[1] // fsdp
    q_columns = query_weight.shape[1] // fsdp
    columns = q_columns + 2 * kv_columns
    q_heads = q_columns // HEAD

    ends = jnp.cumsum(lengths[0])
    place = jnp.arange(rows * fsdp, dtype=jnp.int32)
    start = jnp.max(jnp.where(ends[:, None] <= place[None, :], ends[:, None], 0), axis=0)
    position = (place - start).astype(F32)
    frequency = ROPE_BASE ** (-jnp.arange(HEAD // 2, dtype=F32) * 2.0 / HEAD)
    angles = frequency[:, None] * position[None, :]
    cosine, sine = jnp.cos(angles), jnp.sin(angles)
    start = start[None, :].astype(jnp.int32)

    packed, x_sends, dressed, mask = pack_weights(
        me,
        own,
        query_weight,
        key_weight,
        value_weight,
        router_weight.T,
        first_gain[None],
        second_gain[None],
        query_gain[None],
        key_gain[None],
        routes[0].T,
        upstream,
    )
    x_came = along_z(x_sends)
    x_other = [send(own, "fsdp", 1), send(packed[1], "fsdp", 1)]
    deal, turn = slot_tables(mask, capacity)
    ready = (*x_other, deal, cosine, sine, start)
    x_other.append(send(relay(x_came, rows * fsdp, after=ready), "fsdp", 1))
    c_all = lax.all_gather(dressed, "expert", axis=0)
    wo_came = along_z(output_weight)

    h1, pre, keep, give, inverse, gains, heads, turned, mixed = attention_forward(
        me, own, packed[0], x_came, x_other, cosine, sine, start, experts, q_heads
    )
    other = send(give, "fsdp", 1)
    mixed_sends, wo_stack = merge(keep, other, output_weight, wo_came)
    mixed_came = along_z(mixed_sends)
    wo_other = send(wo_stack, "fsdp", 1)
    middle, probs, hidden, sent = middle_layer(
        own, keep, other, mixed_came, output_weight, wo_came, wo_other, gains, deal, experts, owners
    )
    h_rows = exchange(sent)
    rows_c, row_mask, back = deal_rows(owner, c_all, down_weight, experts, capacity)
    rows_back, gate_low, up_low, active, weighted, share = expert_layer(
        owner, h_rows, gains, row_mask, back, gate_weight, up_weight, experts
    )
    came_back = exchange(rows_back)
    grads, tick = expert_weights(h_rows, rows_c, gate_low, up_low, weighted)
    grads = lax.psum(grads, "fsdp")
    gate_sum, up_sum, down_sum = widen(grads)
    sent, tick = expert_outputs(active, share, down_weight, owners, after=(tick,))

    middle_grad, middle_low, extra = router_backward(
        came_back, turn, middle, probs, mask, gains, upstream, hidden, experts, after=(tick,)
    )
    da_came, da_other = gather_fsdp(middle_low)
    out_rows = exchange(sent)
    layer_out, _ = layer_output(out_rows, turn, middle)
    first, dh_keep, dh_give = attention_backward(
        me,
        middle_low,
        da_came,
        da_other,
        heads,
        output_weight,
        cosine,
        sine,
        start,
        h1,
        pre,
        mixed,
        inverse,
        turned,
        extra,
        experts,
        q_heads,
    )
    dh_total, *dh_sends = pair_sum(dh_keep, send(dh_give, "fsdp", 1))
    dh_came = along_z(dh_sends)
    tokens_grad, tick = input_grad(dh_total, dh_came, own, gains, middle_grad, experts)
    first = passed(first, after=(out_rows, grads, dh_total))
    parted, rest = shares_sum(exchange(first), after=tuple(dh_came))
    parted = lax.all_to_all(parted, "fsdp", 0, 0, tiled=True)
    pieces = exchange(whole_pieces(parted, rest, after=(tick,)))
    query_sum, key_sum, value_sum, output_sum, one_sum, two_sum, *gain_sums, router_sum = final_grads(
        pieces, query_weight, key_weight, value_weight, first_gain[None], experts
    )
    return (
        layer_out[None],
        tokens_grad[None],
        one_sum[0],
        query_sum,
        key_sum,
        value_sum,
        output_sum,
        gain_sums[0][0],
        gain_sums[1][0],
        two_sum[0],
        router_sum.T,
        gate_sum,
        up_sum,
        down_sum,
    )


def solution(mesh):
    whole = P("expert", "fsdp", None)
    rows = P("fsdp", None)
    vector = P("fsdp")
    owned = P("expert", None, None)
    return jax.shard_map(
        shards,
        mesh=mesh,
        in_specs=(
            whole,
            P("expert", None),
            whole,
            vector,
            rows,
            rows,
            rows,
            rows,
            vector,
            vector,
            vector,
            rows,
            owned,
            owned,
            owned,
            whole,
        ),
        out_specs=(
            whole,
            whole,
            vector,
            rows,
            rows,
            rows,
            rows,
            vector,
            vector,
            vector,
            rows,
            owned,
            owned,
            owned,
        ),
        check_vma=False,
    )
```
